32 devices in a mesh: expert: 16 (over z, y, x), tensor: 2 (over core).
Axes of the slice: x: 2, y: 2, z: 4, core: 2. Of those that a mesh axis runs over, the one named last changes fastest.
Arguments:
- inputs: bfloat16 [4096, 2048], P('expert'), may hold values from -6 to 6
- attn_gain: bfloat16 [2048], P('expert'), may hold values from 0.5 to 1.5
- w_query: bfloat16 [2048, 3072], P('expert', 'tensor'), may hold values from -0.125 to 0.125
- w_latent: bfloat16 [2048, 576], P('expert'), may hold values from -0.125 to 0.125
- latent_gain: bfloat16 [512], P('expert'), may hold values from 0.5 to 1.5
- w_kv: bfloat16 [512, 4096], P('expert', 'tensor'), may hold values from -0.25 to 0.25
- w_out: bfloat16 [2048, 2048], P('tensor', 'expert'), may hold values from -0.75 to 0.75
- ffn_gain: bfloat16 [2048], P('expert'), may hold values from 0.5 to 1.5
- w_router: bfloat16 [2048, 16], P('expert'), may hold values from -0.0625 to 0.0625
- shared_gate_up: bfloat16 [2, 2048, 2816], P(None, 'expert', 'tensor'), may hold values from -0.125 to 0.125
- shared_down: bfloat16 [2816, 2048], P('tensor', 'expert'), may hold values from -0.109375 to 0.109375
- expert_gate_up: bfloat16 [16, 2, 2048, 1408], P('expert', None, None, 'tensor'), may hold values from -0.125 to 0.125
- expert_down: bfloat16 [16, 1408, 2048], P('expert', 'tensor'), may hold values from -0.15625 to 0.15625
- lengths: int32 [16, 4], P('expert'), may hold values from 1 to 128, 256 in all within a row
- routes: int32 [4096, 6], P('expert'), may hold values from 0 to 15, all different within a row; in each aligned block of 256 rows (0 to 255, 256 to 511, ...) at most 128 rows name the same one
- cotangent: bfloat16 [4096, 2048], P('expert'), may hold values from -6 to 6
Outputs:
- mixed: bfloat16 [4096, 2048], P('expert')
- input_grad: float32 [4096, 2048], P('expert')
- attn_gain_grad: float32 [2048], P('expert')
- w_query_grad: float32 [2048, 3072], P('expert', 'tensor')
- w_latent_grad: float32 [2048, 576], P('expert')
- latent_gain_grad: float32 [512], P('expert')
- w_kv_grad: float32 [512, 4096], P('expert', 'tensor')
- w_out_grad: float32 [2048, 2048], P('tensor', 'expert')
- ffn_gain_grad: float32 [2048], P('expert')
- w_router_grad: float32 [2048, 16], P('expert')
- shared_gate_up_grad: float32 [2, 2048, 2816], P(None, 'expert', 'tensor')
- shared_down_grad: float32 [2816, 2048], P('tensor', 'expert')
- expert_gate_up_grad: float32 [16, 2, 2048, 1408], P('expert', None, None, 'tensor')
- expert_down_grad: float32 [16, 1408, 2048], P('expert', 'tensor')
The draws below stay inside these ranges and needn't reach their ends.
Inputs may be any that keep to these rules, and one draw needn't show every extreme that they name: Each row holds 4 document lengths that sum to 256; the longest of each row has 128 tokens. `routes`: each token names 6 different experts; within the rows of one group no expert is named more than 128 times.
All inputs are finite; a program needn't handle non-finite values.
Results may differ from the reference program's by a relative error of at most 0.018.
Values may be sent and summed in bfloat16 or wider, within the bound.
No kernel may reach another device: no remote copies, remote signals or barrier semaphores. Data moves between devices by JAX's collectives and lax.ppermute only.
A program may use at most 256 MiB of HBM per device.

```python
import math
import jax
import jax.numpy as jnp
import numpy as np
from jax import lax

D = 2048
H = 16
DN = 128
DR = 64
DV = 128
R = 512
FE = 1408
TOP = 6
DOCS = 4
TOK_DEV = 256
EXPERTS = 16
GROUPS = 16
TOKENS = 4096
FS = 2816
CAP = 128
N_TENSOR = 2


def levels(key, dims, split, low, high):
    loudness = 1.0
    for dim, shards_of in split:
        steps = jax.random.uniform(jax.random.fold_in(jax.random.fold_in(key, 6), dim), (shards_of,), jnp.float32, low / len(split), high / len(split))
        loudness = loudness * jnp.repeat(jnp.exp(steps), dims[dim] // shards_of).reshape((-1,) + (1,) * (len(dims) - 1 - dim))
    return loudness


def split_up(count, total, limit, skew):
    portions = [(1 << 20) // math.isqrt(rank ** skew) + 1 for rank in range(2, count + 1)]
    surplus, holding = total - limit - (count - 1), [1] * (count - 1)
    while surplus > 0:
        movable = [i for i in range(count - 1) if holding[i] < limit]
        whole, left = sum([portions[i] for i in movable]), surplus
        for i in movable:
            extra = min(limit - holding[i], max(1, left * portions[i] // whole), surplus)
            holding[i] = holding[i] + extra
            surplus = surplus - extra
    return np.array([limit] + holding)


def uneven_parts(rng, amount, total, most, skew):
    if amount == 2:
        one = jax.random.randint(rng, (), max(1, total - most), min(most, total - 1) + 1)
        return jnp.stack([one, total - one])
    sizes = jnp.asarray(split_up(amount, total, most, skew), jnp.int32)
    pairs = (amount - 1) // 2
    source_of, sink = sizes[1:1 + 2 * pairs:2], sizes[2:2 + 2 * pairs:2]
    margin = jnp.minimum(source_of - 1, most - sink)
    passed = jax.random.randint(jax.random.fold_in(rng, 1), (pairs,), 0, 1 << 20) % (margin + 1)
    sizes = sizes.at[1:1 + 2 * pairs:2].set(source_of - passed).at[2:2 + 2 * pairs:2].set(sink + passed)
    return sizes[jax.random.permutation(jax.random.fold_in(rng, 2), amount)]


def deal_out(own_key, own, number, rows, count, top, limit, skew):
    order = jax.random.permutation(own_key, count)
    heavy_load, common = portions_of(count, rows * top, limit, skew, True), portions_of(count, rows * top, limit, skew, False)
    places = jnp.arange(count)

    def named(tallies, rotation):
        used = int((tallies > 0).sum())
        fixed = max(1, used // 4)
        moved = fixed + (places - fixed + rotation * (used - fixed)) % max(1, count - fixed)
        return jnp.zeros((count,), jnp.int32).at[order[jnp.where(places < fixed, places, moved)]].set(jnp.asarray(tallies, jnp.int32))

    tallies = jnp.where(number % 4 == 0, named(heavy_load, number // 4), named(common, number - number // 4 - 1))
    mixed = jax.random.permutation(jax.random.fold_in(own, 3), count)
    donor, sink = mixed[0:count // 2 * 2:2], mixed[1:count // 2 * 2:2]
    margin = jnp.minimum(tallies[donor] - 1, limit - tallies[sink]) // 2
    margin = jnp.where((donor == order[0]) | (sink == order[0]) | (tallies[sink] == 0), 0, jnp.maximum(margin, 0))
    moved = jax.random.randint(jax.random.fold_in(own, 4), (count // 2,), 0, 1 << 20) % (margin + 1)
    tallies = tallies.at[donor].add(-moved).at[sink].add(moved)
    items = jnp.searchsorted(jnp.cumsum(tallies), jnp.arange(rows * top), side="right").astype(jnp.int32)
    table = items.reshape(top, rows).T
    table = table[jax.random.permutation(jax.random.fold_in(own, 1), rows)]
    rotation = jax.random.randint(jax.random.fold_in(own, 2), (rows, 1), 0, top)
    return jnp.take_along_axis(table, (jnp.arange(top)[None, :] + rotation) % top, axis=1)


def portions_of(number_of, total, most, lean, full):
    portions = [(1 << 20) // math.isqrt(standing ** lean) + 1 for standing in range(1, number_of + 1)]
    largest = most if full else min(most, max(-(-total // number_of), total * portions[0] // sum(portions)))
    least = 1 if total - largest >= number_of - 1 else 0
    counts, spare = [largest] + [least] * (number_of - 1), total - largest - least * (number_of - 1)
    while spare > 0:
        free = [i for i in range(1, number_of) if counts[i] < largest] or [i for i in range(1, number_of) if counts[i] < most]
        mass, remaining = sum([portions[i] for i in free]), spare
        for i in free:
            extra = min(most - counts[i], max(1, remaining * portions[i] // mass), spare)
            counts[i] = counts[i] + extra
            spare = spare - extra
    return np.array(counts)


def normal_values(own_key, extent, deviation, most, pieces=(), held_as=jnp.bfloat16):
    array = jax.random.normal(own_key, extent, jnp.float32) * deviation
    if len(pieces) > 0:
        array = levels(own_key, extent, pieces, -0.22, 0.18) * array
    return jnp.clip(array, min=-most, max=most).astype(held_as)


def setup_inputs(seed: int = 0) -> dict:
    arg_keys = jax.random.split(jax.random.key(seed), 17)
    inputs = normal_values(arg_keys[0], (TOKENS, D), 1.0, 6.0, ((0, 16),))
    attn_gain = jnp.clip(1.0 + 0.1 * jax.random.normal(arg_keys[1], (D,), jnp.float32), 0.5, 1.5).astype(jnp.bfloat16)
    w_query = normal_values(arg_keys[2], (D, H * (DN + DR)), D ** -0.5, 0.125, ((0, 16), (1, 2)))
    w_latent = normal_values(arg_keys[3], (D, R + DR), D ** -0.5, 0.125, ((0, 16),))
    latent_gain = jnp.clip(1.0 + 0.1 * jax.random.normal(arg_keys[4], (R,), jnp.float32), 0.5, 1.5).astype(jnp.bfloat16)
    w_kv = normal_values(arg_keys[5], (R, H * (DN + DV)), R ** -0.5, 0.25, ((0, 16), (1, 2)))
    w_out = normal_values(arg_keys[6], (H * DV, D), (H * DV // 32) ** -0.5, 0.75, ((0, 2), (1, 16)))
    ffn_gain = jnp.clip(1.0 + 0.1 * jax.random.normal(arg_keys[7], (D,), jnp.float32), 0.5, 1.5).astype(jnp.bfloat16)
    w_router = normal_values(arg_keys[8], (D, EXPERTS), (4 * D) ** -0.5, 0.0625, ((0, 16),))
    shared_gate_up = normal_values(arg_keys[9], (2, D, FS), D ** -0.5, 0.125, ((1, 16), (2, 2)))
    shared_down = normal_values(arg_keys[10], (FS, D), FS ** -0.5, 0.109375, ((0, 2), (1, 16)))
    expert_gate_up = normal_values(arg_keys[11], (EXPERTS, 2, D, FE), D ** -0.5, 0.125, ((0, 16), (3, 2)))
    expert_down = normal_values(arg_keys[12], (EXPERTS, FE, D), FE ** -0.5, 0.15625, ((0, 16), (1, 2)))
    lengths = jax.vmap(lambda own: uneven_parts(own, DOCS, TOK_DEV, TOK_DEV // 2, 2))(jax.random.split(arg_keys[13], GROUPS)).reshape((GROUPS, DOCS)).astype(jnp.int32)
    routes_keys = jax.random.split(jax.random.fold_in(arg_keys[14], 1), TOKENS // TOK_DEV)
    routes_turns = jax.random.permutation(jax.random.fold_in(arg_keys[14], 3), TOKENS // TOK_DEV)
    routes = jax.vmap(lambda own, number: deal_out(jax.random.fold_in(arg_keys[14], 2), own, number, TOK_DEV, EXPERTS, TOP, CAP, 1))(routes_keys, routes_turns).reshape((TOKENS, TOP))
    cotangent = normal_values(arg_keys[15], (TOKENS, D), 1.0, 6.0, ((0, 16),))
    return {"inputs": inputs, "attn_gain": attn_gain, "w_query": w_query, "w_latent": w_latent, "latent_gain": latent_gain, "w_kv": w_kv, "w_out": w_out, "ffn_gain": ffn_gain, "w_router": w_router, "shared_gate_up": shared_gate_up, "shared_down": shared_down, "expert_gate_up": expert_gate_up, "expert_down": expert_down, "lengths": lengths, "routes": routes, "cotangent": cotangent}


EPSILON = 1e-06
ROUTE_SCALE = 2.446
ROPE_BASE = 50000.0
NEGATIVE = -1e+30
HIGHEST = lax.Precision.HIGHEST

@jax.custom_vjp
def low(v):
    return lax.optimization_barrier(v.astype(jnp.bfloat16)).astype(jnp.float32)

@jax.custom_vjp
def low_back(v):
    return v

def low_keep(v):
    return (low(v), None)

def low_pass(kept, grad):
    return (grad,)

def back_keep(v):
    return (v, None)

def back_low(kept, grad):
    return (low(grad),)
low.defvjp(low_keep, low_pass)
low_back.defvjp(back_keep, back_low)

def rounded(tensor_in):
    return low(low_back(tensor_in))

def product(left_arr, right_arr):
    return jnp.dot(left_arr, right_arr, precision=HIGHEST, preferred_element_type=jnp.float32)

def rms_norm(rows_in, gain_vec):
    return rows_in * lax.rsqrt(lax.optimization_barrier(jnp.mean(rows_in * rows_in, axis=-1, keepdims=True)) + EPSILON) * gain_vec

def doc_layout(doc_lengths, row_count):
    ends_at = jnp.cumsum(doc_lengths).astype(jnp.int32)
    starts_at = ends_at - doc_lengths.astype(jnp.int32)
    position = jnp.arange(row_count, dtype=jnp.int32)
    doc_ids = lax.optimization_barrier(jnp.sum((position[:, None] >= ends_at[None, :]).astype(jnp.int32), axis=1))
    hitting = doc_ids[:, None] == jnp.arange(doc_lengths.shape[0], dtype=jnp.int32)[None, :]
    start_of = lax.optimization_barrier(jnp.sum(jnp.where(hitting, starts_at[None, :], 0), axis=1)).astype(jnp.int32)
    relative = position - start_of
    visible = (doc_ids[:, None] == doc_ids[None, :]) & (position[:, None] >= position[None, :])
    return (relative, visible)

def rope_tables(relative, rot_width):
    counter = jnp.arange(rot_width // 2, dtype=jnp.float32)
    frequency = ROPE_BASE ** (-2.0 * counter / rot_width)
    angles = relative.astype(jnp.float32)[:, None] * frequency[None, :]
    return (jnp.cos(angles), jnp.sin(angles))

def rotate(tensor_in, cosine, sine_tab):
    half_width = tensor_in.shape[-1] // 2
    leading = tensor_in[..., :half_width]
    trailing = tensor_in[..., half_width:]
    return jnp.concatenate([leading * cosine - trailing * sine_tab, trailing * cosine + leading * sine_tab], axis=-1)

def slot_tables(route_rows, expert_count, capacity):
    flat_routes = route_rows.reshape(-1).astype(jnp.int32)
    one_hot = (flat_routes[:, None] == jnp.arange(expert_count, dtype=jnp.int32)[None, :]).astype(jnp.int32)
    ranking = lax.optimization_barrier(jnp.sum((jnp.cumsum(one_hot, axis=0).astype(jnp.int32) - one_hot) * one_hot, axis=1)).astype(jnp.int32)
    slot_ids = flat_routes * capacity + ranking
    row_total = flat_routes.shape[0]
    source = jnp.zeros((expert_count * capacity,), jnp.int32).at[slot_ids].set(jnp.arange(row_total, dtype=jnp.int32))
    filled = jnp.zeros((expert_count * capacity,), jnp.int32).at[slot_ids].set(1)
    return (slot_ids, source, filled)

def reference(inputs, attn_gain, w_query, w_latent, latent_gain, w_kv, w_out, ffn_gain, w_router, shared_gate_up, shared_down, expert_gate_up, expert_down, lengths, routes, cotangent):
    slot_ids, source, filled = jax.vmap(lambda route_grp: slot_tables(route_grp, EXPERTS, CAP))(routes.reshape(GROUPS, TOK_DEV, TOP))

    def forward(block_in, gain_one, query_w, latent_w, latent_g, kv_w, out_w, gain_two, router_w, sgate_up, sdown_w, egate_up, edown_w):
        normed = low(rms_norm(block_in, gain_one))

        def attend(group_in):
            rows_in, doc_lengths = group_in
            relative, visible = doc_layout(doc_lengths, TOK_DEV)
            cosine, sine_tab = rope_tables(relative, DR)
            queries = low_back(product(rows_in, query_w)).reshape(TOK_DEV, H, DN + DR)
            q_rot = rotate(queries[..., DN:], cosine[:, None, :], sine_tab[:, None, :])
            q_all = low(jnp.concatenate([queries[..., :DN], q_rot], axis=-1))
            latent = low_back(product(rows_in, latent_w))
            compressed = low(rms_norm(latent[:, :R], latent_g))
            k_rope = low(rotate(latent[:, R:], cosine, sine_tab))
            kv_all = low_back(product(compressed, kv_w)).reshape(TOK_DEV, H, DN + DV)
            k_nope = low(kv_all[..., :DN])
            values = low(kv_all[..., DN:])
            key_all = jnp.concatenate([k_nope, jnp.broadcast_to(k_rope[:, None, :], (TOK_DEV, H, DR))], axis=-1)
            scores = low_back(jnp.einsum('qhd,khd->hqk', q_all, key_all, precision=HIGHEST) * (DN + DR) ** (-0.5))
            scores = jnp.where(visible[None], scores, NEGATIVE)
            weights = low(jax.nn.softmax(scores, axis=-1))
            attended = rounded(jnp.einsum('hqk,khd->qhd', weights, values, precision=HIGHEST))
            return product(attended.reshape(TOK_DEV, H * DV), out_w)
        attn = lax.map(jax.checkpoint(attend), (normed.reshape(GROUPS, TOK_DEV, D), lengths))
        attn = low_back(attn.reshape(TOKENS, D))
        hidden = block_in + attn
        hnormed = low(rms_norm(hidden, gain_two))
        logits = low_back(product(hnormed, router_w))
        sigmoid_vals = jax.nn.sigmoid(logits)
        chosen = jnp.take_along_axis(sigmoid_vals, routes, axis=1)
        gate_vals = ROUTE_SCALE * chosen / lax.optimization_barrier(jnp.sum(chosen, axis=1, keepdims=True))
        shared_gu = low_back(jnp.einsum('td,gdf->gtf', hnormed, sgate_up, precision=HIGHEST))
        shared_act = low(jax.nn.silu(shared_gu[0]) * shared_gu[1])
        shared_out = product(shared_act, sdown_w)
        grouped = hnormed.reshape(GROUPS, TOK_DEV, D)
        picked_rows = jax.vmap(lambda rows_grp, index_grp: rows_grp[index_grp])(grouped, source // TOP)
        sent_rows = jnp.where(filled[..., None] == 1, picked_rows, 0.0)
        sent_rows = sent_rows.reshape(GROUPS, EXPERTS, CAP, D).transpose(1, 0, 2, 3).reshape(EXPERTS, GROUPS * CAP, D)

        def run_expert(packed):
            rows_in, gate_up_joined, down_mat = packed
            half_cols = FE // N_TENSOR
            summed = jnp.zeros((rows_in.shape[0], D), jnp.float32)
            for shard_idx in range(N_TENSOR):
                lower_col = shard_idx * half_cols
                taken_rows = low_back(rows_in)
                gate_part = low_back(product(taken_rows, gate_up_joined[0, :, lower_col:lower_col + half_cols]))
                up_part = low_back(product(taken_rows, gate_up_joined[1, :, lower_col:lower_col + half_cols]))
                active = low(jax.nn.silu(gate_part) * up_part)
                summed = summed + rounded(product(active, down_mat[lower_col:lower_col + half_cols]))
            return summed
        expert_res = lax.map(jax.checkpoint(run_expert), (sent_rows, egate_up, edown_w))
        returned_all = expert_res.reshape(EXPERTS, GROUPS, CAP, D).transpose(1, 0, 2, 3).reshape(GROUPS, EXPERTS * CAP, D)
        returned = jax.vmap(lambda rows_grp, index_grp: rows_grp[index_grp])(returned_all, slot_ids).reshape(TOKENS, TOP, D)
        routed = jnp.einsum('tk,tkd->td', gate_vals, returned, precision=HIGHEST)
        return hidden + shared_out + routed
    floats = tuple((array_in.astype(jnp.float32) for array_in in (inputs, attn_gain, w_query, w_latent, latent_gain, w_kv, w_out, ffn_gain, w_router, shared_gate_up, shared_down, expert_gate_up, expert_down)))
    output, pullback = jax.vjp(forward, *floats)
    grads = pullback(cotangent.astype(jnp.float32))
    return (output.astype(jnp.bfloat16), grads[0], grads[1], grads[2], grads[3], grads[4], grads[5], grads[6], grads[7], grads[8], grads[9], grads[10], grads[11], grads[12])
```

```python
import jax
import jax.numpy as jnp
from jax import lax
from jax.sharding import PartitionSpec as P

DN = 128
DR = 64
DV = 128


EPSILON = 1e-06
ROUTE_SCALE = 2.446
ROPE_BASE = 50000.0
NEGATIVE = -1e30


def cut_along(value, dim, length):
    before, after = (value.shape[:dim], value.shape[dim + 1 :])
    return jnp.moveaxis(value.reshape(*before, length, -1, *after), dim, 0)


def summed_on_arrival(value, axis, dim):
    length = lax.axis_size(axis)
    tiles = lax.all_to_all(cut_along(value, dim, length), axis, 0, 0, tiled=True)
    return jnp.sum(tiles.astype(jnp.float32), axis=0)


def sent_together(arrays, axis, dim, along):
    columns = [a.reshape(*a.shape[:along], -1) for a in arrays]
    both = jnp.concatenate(columns, axis=along)
    whole, at, outs = (summed_on_arrival(both, axis, dim), 0, [])
    for a, column in zip(arrays, columns):
        slab = whole[..., at : at + column.shape[along]]
        outs.append(slab.reshape(*slab.shape[:along], *a.shape[along:]))
        at += column.shape[along]
    return tuple(outs)


def contract_rows(left_arr, right_arr):
    return lax.dot_general(
        left_arr, right_arr, (((0,), (0,)), ((), ())), preferred_element_type=jnp.float32
    )


def contract_cols(left_arr, right_arr):
    return lax.dot_general(
        left_arr, right_arr, (((1,), (1,)), ((), ())), preferred_element_type=jnp.float32
    )


def rms_forward(rows_in, gain_vec):
    inverse = lax.rsqrt(jnp.mean(rows_in * rows_in, axis=-1, keepdims=True) + EPSILON)
    return (rows_in * inverse * gain_vec, inverse)


def rms_backward(rows_in, inverse, gain_vec, grad_out):
    gain_grad = jnp.sum(grad_out * rows_in * inverse, axis=0)
    weighted = grad_out * gain_vec
    inner_mean = jnp.mean(weighted * rows_in, axis=-1, keepdims=True)
    return (inverse * weighted - rows_in * inverse * inverse * inverse * inner_mean, gain_grad)


def doc_layout(doc_lengths, row_count):
    ends_at = jnp.cumsum(doc_lengths)
    starts_at = ends_at - doc_lengths
    position = jnp.arange(row_count, dtype=jnp.int32)
    doc_ids = jnp.sum((position[:, None] >= ends_at[None, :]).astype(jnp.int32), axis=1)
    hitting = doc_ids[:, None] == jnp.arange(doc_lengths.shape[0], dtype=jnp.int32)[None, :]
    start_of = jnp.sum(jnp.where(hitting, starts_at[None, :], 0), axis=1)
    relative = position - start_of
    visible = (doc_ids[:, None] == doc_ids[None, :]) & (position[:, None] >= position[None, :])
    return (relative, visible)


def rope_tables(relative, rot_width):
    counter = jnp.arange(rot_width // 2, dtype=jnp.float32)
    frequency = ROPE_BASE ** (-2.0 * counter / rot_width)
    angles = relative.astype(jnp.float32)[:, None] * frequency[None, :]
    return (jnp.cos(angles), jnp.sin(angles))


def rotate(tensor_in, cosine, sine_tab):
    half_width = tensor_in.shape[-1] // 2
    leading = tensor_in[..., :half_width]
    trailing = tensor_in[..., half_width:]
    return jnp.concatenate(
        [leading * cosine - trailing * sine_tab, trailing * cosine + leading * sine_tab], axis=-1
    )


def unrotate(grad_in, cosine, sine_tab):
    half_width = grad_in.shape[-1] // 2
    leading = grad_in[..., :half_width]
    trailing = grad_in[..., half_width:]
    return jnp.concatenate(
        [leading * cosine + trailing * sine_tab, trailing * cosine - leading * sine_tab], axis=-1
    )


def gated_linear_backward(gate_in, up_in, grad_act):
    sigmoid_g = jax.nn.sigmoid(gate_in)
    grad_gate = grad_act * up_in * sigmoid_g * (1.0 + gate_in * (1.0 - sigmoid_g))
    return (grad_gate, grad_act * gate_in * sigmoid_g)


def slot_tables(route_rows, expert_count, capacity):
    flat_routes = route_rows.reshape(-1)
    one_hot = (flat_routes[:, None] == jnp.arange(expert_count, dtype=jnp.int32)[None, :]).astype(
        jnp.int32
    )
    ranking = jnp.sum((jnp.cumsum(one_hot, axis=0) - one_hot) * one_hot, axis=1)
    slot_ids = flat_routes * capacity + ranking
    row_total = flat_routes.shape[0]
    source = (
        jnp.zeros((expert_count * capacity,), jnp.int32)
        .at[slot_ids]
        .set(jnp.arange(row_total, dtype=jnp.int32))
    )
    filled = jnp.zeros((expert_count * capacity,), jnp.int32).at[slot_ids].set(1)
    return (slot_ids, source, filled)


def to_owner(rows_in):
    arrived = lax.all_to_all(rows_in, "expert", split_axis=0, concat_axis=1, tiled=True)
    return arrived


def weight_plan(
    inputs,
    attn_gain,
    w_query,
    w_latent,
    latent_gain,
    w_kv,
    w_out,
    ffn_gain,
    w_router,
    shared_gate_up,
    shared_down,
    expert_gate_up,
    expert_down,
    lengths,
    routes,
    cotangent,
):
    tok_rows = inputs.shape[0]
    model_width = inputs.shape[1]
    expert_count = w_router.shape[1]
    route_count = routes.shape[1]
    capacity = tok_rows * route_count * 4 // (3 * expert_count)
    brain_float16 = jnp.bfloat16
    f32 = jnp.float32
    gathered = (
        lax.all_gather(attn_gain, "expert", axis=0, tiled=True),
        lax.all_gather(w_query, "expert", axis=0, tiled=True),
        lax.all_gather(w_latent, "expert", axis=0, tiled=True),
        lax.all_gather(latent_gain, "expert", axis=0, tiled=True),
        lax.all_gather(w_kv, "expert", axis=0, tiled=True),
        lax.all_gather(w_out, "expert", axis=1, tiled=True),
        lax.all_gather(ffn_gain, "expert", axis=0, tiled=True),
        lax.all_gather(w_router, "expert", axis=0, tiled=True),
        lax.all_gather(shared_gate_up, "expert", axis=1, tiled=True),
        lax.all_gather(shared_down, "expert", axis=1, tiled=True),
    )
    gain_one, query_w, latent_w, latent_g, kv_w, out_w, gain_two, router_w, sgate_up, sdown_w = (
        gathered
    )
    local_heads = query_w.shape[1] // (DN + DR)
    rank_width = latent_g.shape[0]
    x_float = inputs.astype(f32)
    relative, visible = doc_layout(lengths[0], tok_rows)
    cosine, sine_tab = rope_tables(relative, DR)
    q_scale = (DN + DR) ** (-0.5)
    normed, scale_one = rms_forward(x_float, gain_one.astype(f32))
    normed_b = normed.astype(brain_float16)
    queries = jnp.dot(normed_b, query_w, preferred_element_type=f32).reshape(
        tok_rows, local_heads, DN + DR
    )
    q_rot = rotate(queries[..., DN:], cosine[:, None, :], sine_tab[:, None, :])
    q_all = jnp.concatenate([queries[..., :DN], q_rot], axis=-1).astype(brain_float16)
    latent = jnp.dot(normed_b, latent_w, preferred_element_type=f32)
    compressed, scale_kv = rms_forward(latent[:, :rank_width], latent_g.astype(f32))
    compressed_b = compressed.astype(brain_float16)
    k_rope = rotate(latent[:, rank_width:], cosine, sine_tab).astype(brain_float16)
    kv_all = jnp.dot(compressed_b, kv_w, preferred_element_type=f32).reshape(
        tok_rows, local_heads, DN + DV
    )
    k_nope = kv_all[..., :DN].astype(brain_float16)
    values = kv_all[..., DN:].astype(brain_float16)
    key_all = jnp.concatenate(
        [k_nope, jnp.broadcast_to(k_rope[:, None, :], (tok_rows, local_heads, DR))], axis=-1
    )

    def score_block():
        raw_scores = (
            jnp.einsum("qhd,khd->hqk", q_all, key_all, preferred_element_type=f32) * q_scale
        )
        return jnp.where(visible[None], raw_scores, NEGATIVE)

    scores = score_block()
    top_score = jnp.max(scores, axis=-1, keepdims=True)
    log_total = top_score + jnp.log(jnp.sum(jnp.exp(scores - top_score), axis=-1, keepdims=True))
    probs_b = jnp.exp(scores - log_total).astype(brain_float16)
    attended = jnp.einsum("hqk,khd->qhd", probs_b, values, preferred_element_type=f32)
    attended_b = attended.reshape(tok_rows, local_heads * DV).astype(brain_float16)
    attn = lax.psum(jnp.dot(attended_b, out_w, preferred_element_type=f32), "tensor")
    hidden = x_float + attn
    hnormed, scale_two = rms_forward(hidden, gain_two.astype(f32))
    hnormed_b = hnormed.astype(brain_float16)
    logits = jnp.dot(hnormed_b, router_w, preferred_element_type=f32)
    sigmoid_vals = jax.nn.sigmoid(logits)
    route_hot = routes[:, :, None] == jnp.arange(expert_count, dtype=jnp.int32)[None, None, :]
    chosen = jnp.sum(jnp.where(route_hot, sigmoid_vals[:, None, :], 0.0), axis=2)
    chosen_sum = jnp.sum(chosen, axis=1, keepdims=True)
    gate_vals = ROUTE_SCALE * chosen / chosen_sum
    slot_ids, source, filled = slot_tables(routes, expert_count, capacity)
    is_filled = filled[:, None] == 1
    sent_rows = jnp.where(is_filled, hnormed_b[source // route_count], 0).reshape(
        expert_count, capacity, model_width
    )
    received = to_owner(sent_rows)
    gate_up_joined = jnp.einsum(
        "erd,egdf->egrf", received, expert_gate_up, preferred_element_type=f32
    )
    expert_act = (jax.nn.silu(gate_up_joined[:, 0]) * gate_up_joined[:, 1]).astype(brain_float16)
    expert_res = jnp.einsum(
        "erf,efd->erd", expert_act, expert_down, preferred_element_type=f32
    ).astype(brain_float16)
    returned_all = lax.all_to_all(expert_res, "expert", split_axis=1, concat_axis=0, tiled=True)
    returned = returned_all.reshape(expert_count * capacity, model_width)[slot_ids].reshape(
        tok_rows, route_count, model_width
    )
    shared_gu = jnp.einsum("td,gdf->gtf", hnormed_b, sgate_up, preferred_element_type=f32)
    shared_act = (jax.nn.silu(shared_gu[0]) * shared_gu[1]).astype(brain_float16)
    branch_sum = jnp.dot(shared_act, sdown_w, preferred_element_type=f32)
    for route_idx in range(route_count):
        branch_sum = branch_sum + gate_vals[:, route_idx : route_idx + 1] * returned[
            :, route_idx
        ].astype(f32)
    moe_out = lax.psum(branch_sum.astype(jnp.bfloat16), "tensor").astype(jnp.float32)
    mixed = (hidden + moe_out).astype(brain_float16)
    grad_y = cotangent.astype(f32)
    sdown_grad = contract_rows(shared_act, cotangent)
    grad_sact = contract_cols(cotangent, sdown_w)
    grad_sgate, grad_sup = gated_linear_backward(shared_gu[0], shared_gu[1], grad_sact)
    grad_sgu = jnp.stack([grad_sgate, grad_sup], axis=0).astype(brain_float16)
    sgu_grad = jnp.einsum("td,gtf->gdf", hnormed_b, grad_sgu, preferred_element_type=f32)
    grad_hn_part = jnp.einsum("gtf,gdf->td", grad_sgu, sgate_up, preferred_element_type=f32)
    gate_columns = []
    for route_idx in range(route_count):
        gate_columns.append(jnp.sum(grad_y * returned[:, route_idx].astype(f32), axis=1))
    gate_part = jnp.stack(gate_columns, axis=1)
    slot_grads = (
        (gate_vals[:, :, None] * grad_y[:, None, :])
        .reshape(tok_rows * route_count, model_width)
        .astype(brain_float16)
    )
    grad_sent = jnp.where(is_filled, slot_grads[source], 0).reshape(
        expert_count, capacity, model_width
    )
    grad_received = to_owner(grad_sent)
    edown_grad = jnp.einsum("erf,erd->efd", expert_act, grad_received, preferred_element_type=f32)
    expert_activation_gradient = jnp.einsum(
        "erd,efd->erf", grad_received, expert_down, preferred_element_type=f32
    )
    expert_gate_gradient, expert_up_gradient = gated_linear_backward(
        gate_up_joined[:, 0], gate_up_joined[:, 1], expert_activation_gradient
    )
    expert_gate_up_gradient = jnp.stack([expert_gate_gradient, expert_up_gradient], axis=1).astype(
        brain_float16
    )
    egu_grad = jnp.einsum(
        "erd,egrf->egdf", received, expert_gate_up_gradient, preferred_element_type=f32
    )
    grad_rows = jnp.einsum(
        "egrf,egdf->erd", expert_gate_up_gradient, expert_gate_up, preferred_element_type=f32
    ).astype(brain_float16)
    grad_back = lax.all_to_all(grad_rows, "expert", split_axis=1, concat_axis=0, tiled=True)
    grad_routes = grad_back.reshape(expert_count * capacity, model_width)[slot_ids].reshape(
        tok_rows, route_count, model_width
    )
    for route_idx in range(route_count):
        grad_hn_part = grad_hn_part + grad_routes[:, route_idx].astype(f32)
    gate_grads = lax.psum(gate_part, "tensor")
    grad_chosen = ROUTE_SCALE * (
        gate_grads / chosen_sum
        - jnp.sum(gate_grads * chosen, axis=1, keepdims=True) / (chosen_sum * chosen_sum)
    )
    grad_sig = jnp.sum(jnp.where(route_hot, grad_chosen[:, :, None], 0.0), axis=1)
    grad_logits = (grad_sig * sigmoid_vals * (1.0 - sigmoid_vals)).astype(brain_float16)
    router_grad = contract_rows(hnormed_b, grad_logits)
    grad_hn = lax.psum(grad_hn_part, "tensor") + contract_cols(grad_logits, router_w)
    grad_hidden_norm, gain_two_grad = rms_backward(hidden, scale_two, gain_two.astype(f32), grad_hn)
    grad_hidden = grad_y + grad_hidden_norm
    grad_hidden_b = grad_hidden.astype(brain_float16)
    out_grad = contract_rows(attended_b, grad_hidden_b)
    grad_att = (
        contract_cols(grad_hidden_b, out_w).reshape(tok_rows, local_heads, DV).astype(brain_float16)
    )
    probs = jnp.exp(score_block() - log_total)
    probs_again = probs.astype(brain_float16)
    grad_probs = jnp.einsum("qhd,khd->hqk", grad_att, values, preferred_element_type=f32)
    grad_vals = jnp.einsum("hqk,qhd->khd", probs_again, grad_att, preferred_element_type=f32)
    row_delta = jnp.sum(probs * grad_probs, axis=-1, keepdims=True)
    grad_scores = (probs * (grad_probs - row_delta)).astype(brain_float16)
    grad_q = jnp.einsum("hqk,khd->qhd", grad_scores, key_all, preferred_element_type=f32) * q_scale
    grad_keys = jnp.einsum("hqk,qhd->khd", grad_scores, q_all, preferred_element_type=f32) * q_scale
    grad_kv = (
        jnp.concatenate([grad_keys[..., :DN], grad_vals], axis=-1)
        .reshape(tok_rows, local_heads * (DN + DV))
        .astype(brain_float16)
    )
    kv_grad = contract_rows(compressed_b, grad_kv)
    grad_comp_part = contract_cols(grad_kv, kv_w)
    grad_krope_part = jnp.sum(grad_keys[..., DN:], axis=1)
    grad_comp, grad_krope = (
        lax.psum(grad_comp_part.astype(jnp.bfloat16), "tensor").astype(jnp.float32),
        lax.psum(grad_krope_part.astype(jnp.bfloat16), "tensor").astype(jnp.float32),
    )
    grad_c, latent_gain_grad = rms_backward(
        latent[:, :rank_width], scale_kv, latent_g.astype(f32), grad_comp
    )
    grad_latent = jnp.concatenate([grad_c, unrotate(grad_krope, cosine, sine_tab)], axis=-1).astype(
        brain_float16
    )
    grad_qrot = unrotate(grad_q[..., DN:], cosine[:, None, :], sine_tab[:, None, :])
    grad_queries = (
        jnp.concatenate([grad_q[..., :DN], grad_qrot], axis=-1)
        .reshape(tok_rows, local_heads * (DN + DR))
        .astype(brain_float16)
    )
    query_grad = contract_rows(normed_b, grad_queries)
    latent_grad = contract_rows(normed_b, grad_latent)
    grad_normed = lax.psum(
        contract_cols(grad_queries, query_w).astype(jnp.bfloat16), "tensor"
    ).astype(jnp.float32) + contract_cols(grad_latent, latent_w)
    grad_x_norm, gain_one_grad = rms_backward(x_float, scale_one, gain_one.astype(f32), grad_normed)
    input_grad = grad_hidden + grad_x_norm
    first_owned = (
        *sent_together(
            (
                gain_one_grad.astype(jnp.bfloat16),
                query_grad.astype(jnp.bfloat16),
                latent_grad.astype(jnp.bfloat16),
            ),
            "expert",
            0,
            1,
        ),
        *sent_together(
            (latent_gain_grad.astype(jnp.bfloat16), kv_grad.astype(jnp.bfloat16)), "expert", 0, 1
        ),
    )
    second_owned = (
        lax.psum_scatter(out_grad, "expert", scatter_dimension=1, tiled=True),
        lax.psum_scatter(gain_two_grad, "expert", scatter_dimension=0, tiled=True),
        lax.psum_scatter(router_grad, "expert", scatter_dimension=0, tiled=True),
        lax.psum_scatter(sgu_grad, "expert", scatter_dimension=1, tiled=True),
        lax.psum_scatter(sdown_grad, "expert", scatter_dimension=1, tiled=True),
    )
    return (
        mixed,
        input_grad,
        first_owned[0],
        first_owned[1],
        first_owned[2],
        first_owned[3],
        first_owned[4],
        second_owned[0],
        second_owned[1],
        second_owned[2],
        second_owned[3],
        second_owned[4],
        egu_grad,
        edown_grad,
    )


def swap_cores(value):
    return lax.ppermute(value, "tensor", [(0, 1), (1, 0)])


def take_rows(value, start, count):
    return lax.dynamic_slice_in_dim(value, start, count, axis=0)


def in_order(core, own, other):
    return jnp.where(
        core == 0, jnp.concatenate([own, other], axis=0), jnp.concatenate([other, own], axis=0)
    )


def all_groups(value):
    return lax.all_gather(value, "expert", axis=0, tiled=False)


def sum_groups(value):
    return lax.psum_scatter(value, "expert", scatter_dimension=0, tiled=False)


def token_plan(
    inputs,
    attn_gain,
    w_query,
    w_latent,
    latent_gain,
    w_kv,
    w_out,
    ffn_gain,
    w_router,
    shared_gate_up,
    shared_down,
    expert_gate_up,
    expert_down,
    lengths,
    routes,
    cotangent,
):
    f32, bf16 = jnp.float32, jnp.bfloat16
    core, me = lax.axis_index("tensor"), lax.axis_index("expert")
    groups = lax.axis_size("expert")
    tok_rows, width = inputs.shape
    half = tok_rows // 2
    own_at, other_at = core * half, (1 - core) * half
    expert_count = w_router.shape[1]
    route_count = routes.shape[1]
    capacity = tok_rows * route_count * 4 // (3 * expert_count)
    shared_cols = shared_gate_up.shape[2] // groups

    query_w = lax.all_gather(w_query, "expert", axis=0, tiled=True)
    small = jnp.concatenate(
        [w_latent, w_router, attn_gain[:, None], ffn_gain[:, None]], axis=1
    )
    small_w = lax.all_gather(small, "expert", axis=0, tiled=True)
    latent_cols = w_latent.shape[1]
    latent_w = small_w[:, :latent_cols]
    router_w = small_w[:, latent_cols : latent_cols + expert_count]
    gain_one = small_w[:, latent_cols + expert_count]
    gain_two = small_w[:, latent_cols + expert_count + 1]
    kv_small = jnp.concatenate([w_kv, latent_gain[:, None]], axis=1)
    kv_all_w = lax.all_gather(kv_small, "expert", axis=0, tiled=True)
    kv_w, latent_g = kv_all_w[:, :-1], kv_all_w[:, -1]
    out_wt = lax.all_gather(w_out.T, "expert", axis=0, tiled=True)
    all_routes = all_groups(routes)
    sgu_w = lax.all_to_all(shared_gate_up, "expert", split_axis=2, concat_axis=1, tiled=True)
    sdown_w = lax.all_to_all(shared_down, "expert", split_axis=0, concat_axis=1, tiled=True)
    dy_own_rows = take_rows(cotangent, own_at, half)
    dy_own = all_groups(dy_own_rows)
    dy_other = swap_cores(dy_own)

    local_heads = query_w.shape[1] // (DN + DR)
    rank_width = latent_g.shape[0]
    x_float = inputs.astype(f32)
    relative, visible = doc_layout(lengths[0], tok_rows)
    cosine, sine_tab = rope_tables(relative, DR)
    q_scale = (DN + DR) ** (-0.5)
    normed, scale_one = rms_forward(x_float, gain_one.astype(f32))
    normed_b = normed.astype(bf16)
    queries = jnp.dot(normed_b, query_w, preferred_element_type=f32).reshape(
        tok_rows, local_heads, DN + DR
    )
    q_rot = rotate(queries[..., DN:], cosine[:, None, :], sine_tab[:, None, :])
    q_all = jnp.concatenate([queries[..., :DN], q_rot], axis=-1).astype(bf16)
    latent = jnp.dot(normed_b, latent_w, preferred_element_type=f32)
    compressed, scale_kv = rms_forward(latent[:, :rank_width], latent_g.astype(f32))
    compressed_b = compressed.astype(bf16)
    k_rope = rotate(latent[:, rank_width:], cosine, sine_tab).astype(bf16)
    kv_all = jnp.dot(compressed_b, kv_w, preferred_element_type=f32).reshape(
        tok_rows, local_heads, DN + DV
    )
    k_nope = kv_all[..., :DN].astype(bf16)
    values = kv_all[..., DN:].astype(bf16)
    key_all = jnp.concatenate(
        [k_nope, jnp.broadcast_to(k_rope[:, None, :], (tok_rows, local_heads, DR))], axis=-1
    )

    def score_block():
        raw_scores = (
            jnp.einsum("qhd,khd->hqk", q_all, key_all, preferred_element_type=f32) * q_scale
        )
        return jnp.where(visible[None], raw_scores, NEGATIVE)

    scores = score_block()
    top_score = jnp.max(scores, axis=-1, keepdims=True)
    log_total = top_score + jnp.log(jnp.sum(jnp.exp(scores - top_score), axis=-1, keepdims=True))
    probs_b = jnp.exp(scores - log_total).astype(bf16)
    attended = jnp.einsum("hqk,khd->qhd", probs_b, values, preferred_element_type=f32)
    attended_b = attended.reshape(tok_rows, local_heads * DV).astype(bf16)
    attn_part = contract_cols(attended_b, out_wt)
    attn_own = take_rows(attn_part, own_at, half) + swap_cores(take_rows(attn_part, other_at, half))
    hidden = take_rows(x_float, own_at, half) + attn_own
    hnormed, scale_two = rms_forward(hidden, gain_two.astype(f32))
    hnormed_b = hnormed.astype(bf16)

    hn_own = all_groups(hnormed_b)
    hn_other = swap_cores(hn_own)

    member = jnp.any(all_routes == me, axis=-1)
    hot = jnp.any(
        all_routes[..., None] == jnp.arange(expert_count, dtype=jnp.int32), axis=2
    )

    def halves(value):
        return (
            lax.dynamic_slice_in_dim(value, own_at, half, axis=1),
            lax.dynamic_slice_in_dim(value, other_at, half, axis=1),
        )

    member_own, member_other = halves(member)
    hot_own, hot_other = halves(hot)
    lower = (
        jnp.arange(half, dtype=jnp.int32)[:, None] <= jnp.arange(half, dtype=jnp.int32)[None, :]
    ).astype(bf16)

    def running(mask):
        counts = jnp.dot(mask.astype(bf16), lower, preferred_element_type=f32)
        return counts.astype(jnp.int32)

    count_own, count_other = running(member_own), running(member_other)
    place_own = jnp.where(member_own, count_own - 1, -1)
    place_other = jnp.where(member_other, count_own[:, -1:] + count_other - 1, -1)
    slot_index = jnp.arange(capacity, dtype=jnp.int32)

    def dispatch(place):
        return (place[:, None, :] == slot_index[None, :, None]).astype(bf16)

    pick_own, pick_other = dispatch(place_own), dispatch(place_other)

    def to_slots(own, other):
        def part(pick, rows):
            return jnp.einsum("gst,gtd->gsd", pick, rows, preferred_element_type=bf16)

        return (part(pick_own, own) + part(pick_other, other)).reshape(groups * capacity, width)

    first_w = jnp.concatenate([sgu_w[0], sgu_w[1], router_w], axis=1)
    shared_w = first_w[:, : 2 * shared_cols]

    def shared_forward(rows, hot_rows, member_rows):
        flat = rows.reshape(groups * half, width)
        products = jnp.dot(flat, first_w, preferred_element_type=f32)
        gate, up = products[:, :shared_cols], products[:, shared_cols : 2 * shared_cols]
        act = (jax.nn.silu(gate) * up).astype(bf16)
        sig = jax.nn.sigmoid(products[:, 2 * shared_cols :]).reshape(groups, half, expert_count)
        total = jnp.sum(jnp.where(hot_rows, sig, 0.0), axis=-1)
        mine = jnp.sum(jnp.where(jnp.arange(expert_count) == me, sig, 0.0), axis=-1)
        gates = jnp.where(member_rows, ROUTE_SCALE * mine / total, 0.0)
        return gate, up, act, gates

    gate_own, up_own, act_own, gates_own = shared_forward(hn_own, hot_own, member_own)
    gate_other, up_other, act_other, gates_other = shared_forward(hn_other, hot_other, member_other)

    slot_rows = to_slots(hn_own, hn_other)
    slot_dy = to_slots(dy_own, dy_other)
    slot_gate = (
        jnp.sum(pick_own.astype(f32) * gates_own[:, None, :], axis=-1)
        + jnp.sum(pick_other.astype(f32) * gates_other[:, None, :], axis=-1)
    ).reshape(groups * capacity, 1)
    gate_w, up_w, down_w = expert_gate_up[0, 0], expert_gate_up[0, 1], expert_down[0]
    slot_g = jnp.dot(slot_rows, gate_w, preferred_element_type=f32)
    slot_u = jnp.dot(slot_rows, up_w, preferred_element_type=f32)
    slot_act = (jax.nn.silu(slot_g) * slot_u).astype(bf16)
    slot_out = jnp.dot(slot_act, down_w, preferred_element_type=f32)
    dy_float = slot_dy.astype(f32)
    slot_dgate = jnp.sum(slot_out * dy_float, axis=-1).reshape(groups, capacity)
    slot_scaled = (slot_gate * slot_out).astype(bf16).reshape(groups, capacity, width)
    slot_grad = (slot_gate * dy_float).astype(bf16)
    edown_grad = contract_rows(slot_act, slot_grad)
    d_act = contract_cols(slot_grad, down_w)
    d_gate, d_up = gated_linear_backward(slot_g, slot_u, d_act)
    d_gate, d_up = d_gate.astype(bf16), d_up.astype(bf16)
    egu_grad = jnp.stack([contract_rows(slot_rows, d_gate), contract_rows(slot_rows, d_up)])
    slot_drows = (contract_cols(d_gate, gate_w) + contract_cols(d_up, up_w)).astype(bf16)
    slot_drows = slot_drows.reshape(groups, capacity, width)

    def from_slots(pick, rows, left, right):
        routed = jnp.einsum("gst,gsd->gtd", pick, rows, preferred_element_type=f32)
        shared = jnp.dot(left, right, preferred_element_type=f32)
        return (routed + shared.reshape(groups, half, width)).astype(bf16)

    def shared_backward(rows_dy, gate, up):
        d_sact = contract_cols(rows_dy.reshape(groups * half, width), sdown_w)
        d_sgate, d_sup = gated_linear_backward(gate, up, d_sact)
        return jnp.concatenate([d_sgate, d_sup], axis=1).astype(bf16)

    d_shared_own = shared_backward(dy_own, gate_own, up_own)
    d_shared_other = shared_backward(dy_other, gate_other, up_other)
    shared_wt = shared_w.T
    d_rows_own = from_slots(pick_own, slot_drows, d_shared_own, shared_wt)
    d_rows_other = from_slots(pick_other, slot_drows, d_shared_other, shared_wt)
    d_rows = (d_rows_own.astype(f32) + swap_cores(d_rows_other).astype(f32)).astype(bf16)
    d_hn = sum_groups(d_rows).astype(f32)

    out_own = from_slots(pick_own, slot_scaled, act_own, sdown_w)
    out_other = from_slots(pick_other, slot_scaled, act_other, sdown_w)
    out_rows = (out_own.astype(f32) + swap_cores(out_other).astype(f32)).astype(bf16)
    moe_own = sum_groups(out_rows).astype(f32)
    mixed_own = (hidden + moe_own).astype(bf16)
    mixed = in_order(core, mixed_own, swap_cores(mixed_own))

    def flat_rows(value):
        return value.reshape(groups * half, -1)

    sgu_grad = contract_rows(flat_rows(hn_own), d_shared_own) + contract_rows(
        flat_rows(hn_other), d_shared_other
    )
    sdown_grad = contract_rows(act_own, flat_rows(dy_own)) + contract_rows(
        act_other, flat_rows(dy_other)
    )
    sgu_grad = jnp.stack([sgu_grad[:, :shared_cols], sgu_grad[:, shared_cols:]])
    sgu_out = lax.all_to_all(
        sgu_grad.astype(bf16), "expert", split_axis=1, concat_axis=2, tiled=True
    ).astype(f32)
    sdown_out = lax.all_to_all(
        sdown_grad.astype(bf16), "expert", split_axis=1, concat_axis=0, tiled=True
    ).astype(f32)

    def to_tokens(pick):
        return jnp.sum(pick.astype(f32) * slot_dgate[:, :, None], axis=1)

    dgate_sent = to_tokens(pick_own) + swap_cores(to_tokens(pick_other))
    dgate = lax.all_to_all(dgate_sent, "expert", split_axis=0, concat_axis=0, tiled=True).T
    hot_mine = take_rows(
        jnp.any(routes[..., None] == jnp.arange(expert_count, dtype=jnp.int32), axis=1), own_at, half
    )
    sig = jax.nn.sigmoid(jnp.dot(hnormed_b, router_w, preferred_element_type=f32))
    chosen = jnp.where(hot_mine, sig, 0.0)
    chosen_sum = jnp.sum(chosen, axis=1, keepdims=True)
    dgate = jnp.where(hot_mine, dgate, 0.0)
    inner = jnp.sum(dgate * chosen, axis=1, keepdims=True)
    d_chosen = ROUTE_SCALE * (dgate / chosen_sum - inner / (chosen_sum * chosen_sum))
    d_logits = (jnp.where(hot_mine, d_chosen, 0.0) * sig * (1.0 - sig)).astype(bf16)
    router_grad = contract_rows(hnormed_b, d_logits)
    d_hn = d_hn + contract_cols(d_logits, router_w)
    d_hidden_norm, gain_two_grad = rms_backward(hidden, scale_two, gain_two.astype(f32), d_hn)
    d_hidden = dy_own_rows.astype(f32) + d_hidden_norm
    d_hidden_half = d_hidden.astype(bf16)
    d_hidden_b = in_order(core, d_hidden_half, swap_cores(d_hidden_half))

    out_grad = contract_rows(d_hidden_b, attended_b)
    grad_att = (
        jnp.dot(d_hidden_b, out_wt, preferred_element_type=f32)
        .reshape(tok_rows, local_heads, DV)
        .astype(bf16)
    )
    probs = jnp.exp(score_block() - log_total)
    probs_again = probs.astype(bf16)
    grad_probs = jnp.einsum("qhd,khd->hqk", grad_att, values, preferred_element_type=f32)
    grad_vals = jnp.einsum("hqk,qhd->khd", probs_again, grad_att, preferred_element_type=f32)
    row_delta = jnp.sum(probs * grad_probs, axis=-1, keepdims=True)
    grad_scores = (probs * (grad_probs - row_delta)).astype(bf16)
    grad_q = jnp.einsum("hqk,khd->qhd", grad_scores, key_all, preferred_element_type=f32) * q_scale
    grad_keys = jnp.einsum("hqk,qhd->khd", grad_scores, q_all, preferred_element_type=f32) * q_scale
    grad_kv = (
        jnp.concatenate([grad_keys[..., :DN], grad_vals], axis=-1)
        .reshape(tok_rows, local_heads * (DN + DV))
        .astype(bf16)
    )
    kv_grad = contract_rows(compressed_b, grad_kv)
    grad_latent_part = jnp.concatenate(
        [contract_cols(grad_kv, kv_w), jnp.sum(grad_keys[..., DN:], axis=1)], axis=1
    ).astype(bf16)
    grad_both = grad_latent_part.astype(f32) + swap_cores(grad_latent_part).astype(f32)
    grad_c, latent_gain_grad = rms_backward(
        latent[:, :rank_width], scale_kv, latent_g.astype(f32), grad_both[:, :rank_width]
    )
    grad_latent = jnp.concatenate(
        [grad_c, unrotate(grad_both[:, rank_width:], cosine, sine_tab)], axis=-1
    ).astype(bf16)
    grad_qrot = unrotate(grad_q[..., DN:], cosine[:, None, :], sine_tab[:, None, :])
    grad_queries = (
        jnp.concatenate([grad_q[..., :DN], grad_qrot], axis=-1)
        .reshape(tok_rows, local_heads * (DN + DR))
        .astype(bf16)
    )
    query_grad = contract_rows(normed_b, grad_queries)
    latent_half = latent_cols // 2
    latent_grad = contract_rows(
        normed_b, lax.dynamic_slice_in_dim(grad_latent, core * latent_half, latent_half, axis=1)
    )
    normed_part = contract_cols(grad_queries, query_w)
    sent_part = take_rows(normed_part, other_at, half).astype(bf16)
    grad_normed = (
        take_rows(normed_part, own_at, half)
        + swap_cores(sent_part).astype(f32)
        + contract_cols(take_rows(grad_latent, own_at, half), latent_w)
    )
    x_own, scale_own = take_rows(x_float, own_at, half), take_rows(scale_one, own_at, half)
    grad_x_norm, gain_one_grad = rms_backward(x_own, scale_own, gain_one.astype(f32), grad_normed)
    input_own = d_hidden + grad_x_norm
    input_grad = in_order(core, input_own, swap_cores(input_own))

    def own_block(*columns):
        joined = jnp.concatenate([a.astype(bf16) for a in columns], axis=1)
        return lax.psum_scatter(joined, "expert", scatter_dimension=0, tiled=True).astype(f32)

    w_out_grad = own_block(out_grad).T
    first = own_block(
        query_grad, latent_grad, router_grad, gain_one_grad[:, None], gain_two_grad[:, None]
    )
    kv_first = own_block(kv_grad, latent_gain_grad[:, None])
    query_cols = query_grad.shape[1]
    half_sums = first[:, query_cols + latent_half :]
    half_sums = half_sums + swap_cores(half_sums)
    latent_mine = first[:, query_cols : query_cols + latent_half]
    latent_theirs = swap_cores(latent_mine)
    latent_out = jnp.where(
        core == 0,
        jnp.concatenate([latent_mine, latent_theirs], axis=1),
        jnp.concatenate([latent_theirs, latent_mine], axis=1),
    )
    return (
        mixed,
        input_grad,
        half_sums[:, expert_count],
        first[:, :query_cols],
        latent_out,
        kv_first[:, -1],
        kv_first[:, :-1],
        w_out_grad,
        half_sums[:, expert_count + 1],
        half_sums[:, :expert_count],
        sgu_out,
        sdown_out,
        egu_grad[None],
        edown_grad[None],
    )


def solution(mesh):
    groups = mesh.shape["expert"]
    plan = token_plan if groups <= 16 else weight_plan
    return jax.shard_map(
        plan,
        mesh=mesh,
        in_specs=(
            P("expert", None),
            P("expert"),
            P("expert", "tensor"),
            P("expert", None),
            P("expert"),
            P("expert", "tensor"),
            P("tensor", "expert"),
            P("expert"),
            P("expert", None),
            P(None, "expert", "tensor"),
            P("tensor", "expert"),
            P("expert", None, None, "tensor"),
            P("expert", "tensor", None),
            P("expert", None),
            P("expert", None),
            P("expert", None),
        ),
        out_specs=(
            P("expert", None),
            P("expert", None),
            P("expert"),
            P("expert", "tensor"),
            P("expert", None),
            P("expert"),
            P("expert", "tensor"),
            P("tensor", "expert"),
            P("expert"),
            P("expert", None),
            P(None, "expert", "tensor"),
            P("tensor", "expert"),
            P("expert", None, None, "tensor"),
            P("expert", "tensor", None),
        ),
        check_vma=False,
    )
```

```python
import jax
import jax.numpy as jnp
from jax import lax
from jax.sharding import PartitionSpec as P

DN = 128
DR = 64
DV = 128


EPSILON = 1e-06
ROUTE_SCALE = 2.446
ROPE_BASE = 50000.0
NEGATIVE = -1e30


def cut_along(value, dim, length):
    before, after = (value.shape[:dim], value.shape[dim + 1 :])
    return jnp.moveaxis(value.reshape(*before, length, -1, *after), dim, 0)


def summed_on_arrival(value, axis, dim):
    length = lax.axis_size(axis)
    tiles = lax.all_to_all(cut_along(value, dim, length), axis, 0, 0, tiled=True)
    return jnp.sum(tiles.astype(jnp.float32), axis=0)


def sent_together(arrays, axis, dim, along):
    columns = [a.reshape(*a.shape[:along], -1) for a in arrays]
    both = jnp.concatenate(columns, axis=along)
    whole, at, outs = (summed_on_arrival(both, axis, dim), 0, [])
    for a, column in zip(arrays, columns):
        slab = whole[..., at : at + column.shape[along]]
        outs.append(slab.reshape(*slab.shape[:along], *a.shape[along:]))
        at += column.shape[along]
    return tuple(outs)


def contract_rows(left_arr, right_arr):
    return lax.dot_general(
        left_arr, right_arr, (((0,), (0,)), ((), ())), preferred_element_type=jnp.float32
    )


def contract_cols(left_arr, right_arr):
    return lax.dot_general(
        left_arr, right_arr, (((1,), (1,)), ((), ())), preferred_element_type=jnp.float32
    )


def rms_forward(rows_in, gain_vec):
    inverse = lax.rsqrt(jnp.mean(rows_in * rows_in, axis=-1, keepdims=True) + EPSILON)
    return (rows_in * inverse * gain_vec, inverse)


def rms_backward(rows_in, inverse, gain_vec, grad_out):
    gain_grad = jnp.sum(grad_out * rows_in * inverse, axis=0)
    weighted = grad_out * gain_vec
    inner_mean = jnp.mean(weighted * rows_in, axis=-1, keepdims=True)
    return (inverse * weighted - rows_in * inverse * inverse * inverse * inner_mean, gain_grad)


def doc_layout(doc_lengths, row_count):
    ends_at = jnp.cumsum(doc_lengths)
    starts_at = ends_at - doc_lengths
    position = jnp.arange(row_count, dtype=jnp.int32)
    doc_ids = jnp.sum((position[:, None] >= ends_at[None, :]).astype(jnp.int32), axis=1)
    hitting = doc_ids[:, None] == jnp.arange(doc_lengths.shape[0], dtype=jnp.int32)[None, :]
    start_of = jnp.sum(jnp.where(hitting, starts_at[None, :], 0), axis=1)
    relative = position - start_of
    visible = (doc_ids[:, None] == doc_ids[None, :]) & (position[:, None] >= position[None, :])
    return (relative, visible)


def rope_tables(relative, rot_width):
    counter = jnp.arange(rot_width // 2, dtype=jnp.float32)
    frequency = ROPE_BASE ** (-2.0 * counter / rot_width)
    angles = relative.astype(jnp.float32)[:, None] * frequency[None, :]
    return (jnp.cos(angles), jnp.sin(angles))


def rotate(tensor_in, cosine, sine_tab):
    half_width = tensor_in.shape[-1] // 2
    leading = tensor_in[..., :half_width]
    trailing = tensor_in[..., half_width:]
    return jnp.concatenate(
        [leading * cosine - trailing * sine_tab, trailing * cosine + leading * sine_tab], axis=-1
    )


def unrotate(grad_in, cosine, sine_tab):
    half_width = grad_in.shape[-1] // 2
    leading = grad_in[..., :half_width]
    trailing = grad_in[..., half_width:]
    return jnp.concatenate(
        [leading * cosine + trailing * sine_tab, trailing * cosine - leading * sine_tab], axis=-1
    )


def gated_linear_backward(gate_in, up_in, grad_act):
    sigmoid_g = jax.nn.sigmoid(gate_in)
    grad_gate = grad_act * up_in * sigmoid_g * (1.0 + gate_in * (1.0 - sigmoid_g))
    return (grad_gate, grad_act * gate_in * sigmoid_g)


def slot_tables(route_rows, expert_count, capacity):
    flat_routes = route_rows.reshape(-1)
    one_hot = (flat_routes[:, None] == jnp.arange(expert_count, dtype=jnp.int32)[None, :]).astype(
        jnp.int32
    )
    ranking = jnp.sum((jnp.cumsum(one_hot, axis=0) - one_hot) * one_hot, axis=1)
    slot_ids = flat_routes * capacity + ranking
    row_total = flat_routes.shape[0]
    source = (
        jnp.zeros((expert_count * capacity,), jnp.int32)
        .at[slot_ids]
        .set(jnp.arange(row_total, dtype=jnp.int32))
    )
    filled = jnp.zeros((expert_count * capacity,), jnp.int32).at[slot_ids].set(1)
    return (slot_ids, source, filled)


def to_owner(rows_in):
    arrived = lax.all_to_all(rows_in, "expert", split_axis=0, concat_axis=1, tiled=True)
    return arrived


def weight_plan(
    inputs,
    attn_gain,
    w_query,
    w_latent,
    latent_gain,
    w_kv,
    w_out,
    ffn_gain,
    w_router,
    shared_gate_up,
    shared_down,
    expert_gate_up,
    expert_down,
    lengths,
    routes,
    cotangent,
):
    tok_rows = inputs.shape[0]
    model_width = inputs.shape[1]
    expert_count = w_router.shape[1]
    route_count = routes.shape[1]
    capacity = tok_rows * route_count * 4 // (3 * expert_count)
    brain_float16 = jnp.bfloat16
    f32 = jnp.float32
    gathered = (
        lax.all_gather(attn_gain, "expert", axis=0, tiled=True),
        lax.all_gather(w_query, "expert", axis=0, tiled=True),
        lax.all_gather(w_latent, "expert", axis=0, tiled=True),
        lax.all_gather(latent_gain, "expert", axis=0, tiled=True),
        lax.all_gather(w_kv, "expert", axis=0, tiled=True),
        lax.all_gather(w_out, "expert", axis=1, tiled=True),
        lax.all_gather(ffn_gain, "expert", axis=0, tiled=True),
        lax.all_gather(w_router, "expert", axis=0, tiled=True),
        lax.all_gather(shared_gate_up, "expert", axis=1, tiled=True),
        lax.all_gather(shared_down, "expert", axis=1, tiled=True),
    )
    gain_one, query_w, latent_w, latent_g, kv_w, out_w, gain_two, router_w, sgate_up, sdown_w = (
        gathered
    )
    local_heads = query_w.shape[1] // (DN + DR)
    rank_width = latent_g.shape[0]
    x_float = inputs.astype(f32)
    relative, visible = doc_layout(lengths[0], tok_rows)
    cosine, sine_tab = rope_tables(relative, DR)
    q_scale = (DN + DR) ** (-0.5)
    normed, scale_one = rms_forward(x_float, gain_one.astype(f32))
    normed_b = normed.astype(brain_float16)
    queries = jnp.dot(normed_b, query_w, preferred_element_type=f32).reshape(
        tok_rows, local_heads, DN + DR
    )
    q_rot = rotate(queries[..., DN:], cosine[:, None, :], sine_tab[:, None, :])
    q_all = jnp.concatenate([queries[..., :DN], q_rot], axis=-1).astype(brain_float16)
    latent = jnp.dot(normed_b, latent_w, preferred_element_type=f32)
    compressed, scale_kv = rms_forward(latent[:, :rank_width], latent_g.astype(f32))
    compressed_b = compressed.astype(brain_float16)
    k_rope = rotate(latent[:, rank_width:], cosine, sine_tab).astype(brain_float16)
    kv_all = jnp.dot(compressed_b, kv_w, preferred_element_type=f32).reshape(
        tok_rows, local_heads, DN + DV
    )
    k_nope = kv_all[..., :DN].astype(brain_float16)
    values = kv_all[..., DN:].astype(brain_float16)
    key_all = jnp.concatenate(
        [k_nope, jnp.broadcast_to(k_rope[:, None, :], (tok_rows, local_heads, DR))], axis=-1
    )

    def score_block():
        raw_scores = (
            jnp.einsum("qhd,khd->hqk", q_all, key_all, preferred_element_type=f32) * q_scale
        )
        return jnp.where(visible[None], raw_scores, NEGATIVE)

    scores = score_block()
    top_score = jnp.max(scores, axis=-1, keepdims=True)
    log_total = top_score + jnp.log(jnp.sum(jnp.exp(scores - top_score), axis=-1, keepdims=True))
    probs_b = jnp.exp(scores - log_total).astype(brain_float16)
    attended = jnp.einsum("hqk,khd->qhd", probs_b, values, preferred_element_type=f32)
    attended_b = attended.reshape(tok_rows, local_heads * DV).astype(brain_float16)
    attn = lax.psum(jnp.dot(attended_b, out_w, preferred_element_type=f32), "tensor")
    hidden = x_float + attn
    hnormed, scale_two = rms_forward(hidden, gain_two.astype(f32))
    hnormed_b = hnormed.astype(brain_float16)
    logits = jnp.dot(hnormed_b, router_w, preferred_element_type=f32)
    sigmoid_vals = jax.nn.sigmoid(logits)
    route_hot = routes[:, :, None] == jnp.arange(expert_count, dtype=jnp.int32)[None, None, :]
    chosen = jnp.sum(jnp.where(route_hot, sigmoid_vals[:, None, :], 0.0), axis=2)
    chosen_sum = jnp.sum(chosen, axis=1, keepdims=True)
    gate_vals = ROUTE_SCALE * chosen / chosen_sum
    slot_ids, source, filled = slot_tables(routes, expert_count, capacity)
    is_filled = filled[:, None] == 1
    sent_rows = jnp.where(is_filled, hnormed_b[source // route_count], 0).reshape(
        expert_count, capacity, model_width
    )
    received = to_owner(sent_rows)
    gate_up_joined = jnp.einsum(
        "erd,egdf->egrf", received, expert_gate_up, preferred_element_type=f32
    )
    expert_act = (jax.nn.silu(gate_up_joined[:, 0]) * gate_up_joined[:, 1]).astype(brain_float16)
    expert_res = jnp.einsum(
        "erf,efd->erd", expert_act, expert_down, preferred_element_type=f32
    ).astype(brain_float16)
    returned_all = lax.all_to_all(expert_res, "expert", split_axis=1, concat_axis=0, tiled=True)
    returned = returned_all.reshape(expert_count * capacity, model_width)[slot_ids].reshape(
        tok_rows, route_count, model_width
    )
    shared_gu = jnp.einsum("td,gdf->gtf", hnormed_b, sgate_up, preferred_element_type=f32)
    shared_act = (jax.nn.silu(shared_gu[0]) * shared_gu[1]).astype(brain_float16)
    branch_sum = jnp.dot(shared_act, sdown_w, preferred_element_type=f32)
    for route_idx in range(route_count):
        branch_sum = branch_sum + gate_vals[:, route_idx : route_idx + 1] * returned[
            :, route_idx
        ].astype(f32)
    moe_out = lax.psum(branch_sum.astype(jnp.bfloat16), "tensor").astype(jnp.float32)
    mixed = (hidden + moe_out).astype(brain_float16)
    grad_y = cotangent.astype(f32)
    sdown_grad = contract_rows(shared_act, cotangent)
    grad_sact = contract_cols(cotangent, sdown_w)
    grad_sgate, grad_sup = gated_linear_backward(shared_gu[0], shared_gu[1], grad_sact)
    grad_sgu = jnp.stack([grad_sgate, grad_sup], axis=0).astype(brain_float16)
    sgu_grad = jnp.einsum("td,gtf->gdf", hnormed_b, grad_sgu, preferred_element_type=f32)
    grad_hn_part = jnp.einsum("gtf,gdf->td", grad_sgu, sgate_up, preferred_element_type=f32)
    gate_columns = []
    for route_idx in range(route_count):
        gate_columns.append(jnp.sum(grad_y * returned[:, route_idx].astype(f32), axis=1))
    gate_part = jnp.stack(gate_columns, axis=1)
    slot_grads = (
        (gate_vals[:, :, None] * grad_y[:, None, :])
        .reshape(tok_rows * route_count, model_width)
        .astype(brain_float16)
    )
    grad_sent = jnp.where(is_filled, slot_grads[source], 0).reshape(
        expert_count, capacity, model_width
    )
    grad_received = to_owner(grad_sent)
    edown_grad = jnp.einsum("erf,erd->efd", expert_act, grad_received, preferred_element_type=f32)
    expert_activation_gradient = jnp.einsum(
        "erd,efd->erf", grad_received, expert_down, preferred_element_type=f32
    )
    expert_gate_gradient, expert_up_gradient = gated_linear_backward(
        gate_up_joined[:, 0], gate_up_joined[:, 1], expert_activation_gradient
    )
    expert_gate_up_gradient = jnp.stack([expert_gate_gradient, expert_up_gradient], axis=1).astype(
        brain_float16
    )
    egu_grad = jnp.einsum(
        "erd,egrf->egdf", received, expert_gate_up_gradient, preferred_element_type=f32
    )
    grad_rows = jnp.einsum(
        "egrf,egdf->erd", expert_gate_up_gradient, expert_gate_up, preferred_element_type=f32
    ).astype(brain_float16)
    grad_back = lax.all_to_all(grad_rows, "expert", split_axis=1, concat_axis=0, tiled=True)
    grad_routes = grad_back.reshape(expert_count * capacity, model_width)[slot_ids].reshape(
        tok_rows, route_count, model_width
    )
    for route_idx in range(route_count):
        grad_hn_part = grad_hn_part + grad_routes[:, route_idx].astype(f32)
    gate_grads = lax.psum(gate_part, "tensor")
    grad_chosen = ROUTE_SCALE * (
        gate_grads / chosen_sum
        - jnp.sum(gate_grads * chosen, axis=1, keepdims=True) / (chosen_sum * chosen_sum)
    )
    grad_sig = jnp.sum(jnp.where(route_hot, grad_chosen[:, :, None], 0.0), axis=1)
    grad_logits = (grad_sig * sigmoid_vals * (1.0 - sigmoid_vals)).astype(brain_float16)
    router_grad = contract_rows(hnormed_b, grad_logits)
    grad_hn = lax.psum(grad_hn_part, "tensor") + contract_cols(grad_logits, router_w)
    grad_hidden_norm, gain_two_grad = rms_backward(hidden, scale_two, gain_two.astype(f32), grad_hn)
    grad_hidden = grad_y + grad_hidden_norm
    grad_hidden_b = grad_hidden.astype(brain_float16)
    out_grad = contract_rows(attended_b, grad_hidden_b)
    grad_att = (
        contract_cols(grad_hidden_b, out_w).reshape(tok_rows, local_heads, DV).astype(brain_float16)
    )
    probs = jnp.exp(score_block() - log_total)
    probs_again = probs.astype(brain_float16)
    grad_probs = jnp.einsum("qhd,khd->hqk", grad_att, values, preferred_element_type=f32)
    grad_vals = jnp.einsum("hqk,qhd->khd", probs_again, grad_att, preferred_element_type=f32)
    row_delta = jnp.sum(probs * grad_probs, axis=-1, keepdims=True)
    grad_scores = (probs * (grad_probs - row_delta)).astype(brain_float16)
    grad_q = jnp.einsum("hqk,khd->qhd", grad_scores, key_all, preferred_element_type=f32) * q_scale
    grad_keys = jnp.einsum("hqk,qhd->khd", grad_scores, q_all, preferred_element_type=f32) * q_scale
    grad_kv = (
        jnp.concatenate([grad_keys[..., :DN], grad_vals], axis=-1)
        .reshape(tok_rows, local_heads * (DN + DV))
        .astype(brain_float16)
    )
    kv_grad = contract_rows(compressed_b, grad_kv)
    grad_comp_part = contract_cols(grad_kv, kv_w)
    grad_krope_part = jnp.sum(grad_keys[..., DN:], axis=1)
    grad_comp, grad_krope = (
        lax.psum(grad_comp_part.astype(jnp.bfloat16), "tensor").astype(jnp.float32),
        lax.psum(grad_krope_part.astype(jnp.bfloat16), "tensor").astype(jnp.float32),
    )
    grad_c, latent_gain_grad = rms_backward(
        latent[:, :rank_width], scale_kv, latent_g.astype(f32), grad_comp
    )
    grad_latent = jnp.concatenate([grad_c, unrotate(grad_krope, cosine, sine_tab)], axis=-1).astype(
        brain_float16
    )
    grad_qrot = unrotate(grad_q[..., DN:], cosine[:, None, :], sine_tab[:, None, :])
    grad_queries = (
        jnp.concatenate([grad_q[..., :DN], grad_qrot], axis=-1)
        .reshape(tok_rows, local_heads * (DN + DR))
        .astype(brain_float16)
    )
    query_grad = contract_rows(normed_b, grad_queries)
    latent_grad = contract_rows(normed_b, grad_latent)
    grad_normed = lax.psum(
        contract_cols(grad_queries, query_w).astype(jnp.bfloat16), "tensor"
    ).astype(jnp.float32) + contract_cols(grad_latent, latent_w)
    grad_x_norm, gain_one_grad = rms_backward(x_float, scale_one, gain_one.astype(f32), grad_normed)
    input_grad = grad_hidden + grad_x_norm
    first_owned = (
        *sent_together(
            (
                gain_one_grad.astype(jnp.bfloat16),
                query_grad.astype(jnp.bfloat16),
                latent_grad.astype(jnp.bfloat16),
            ),
            "expert",
            0,
            1,
        ),
        *sent_together(
            (latent_gain_grad.astype(jnp.bfloat16), kv_grad.astype(jnp.bfloat16)), "expert", 0, 1
        ),
    )
    second_owned = (
        lax.psum_scatter(out_grad, "expert", scatter_dimension=1, tiled=True),
        lax.psum_scatter(gain_two_grad, "expert", scatter_dimension=0, tiled=True),
        lax.psum_scatter(router_grad, "expert", scatter_dimension=0, tiled=True),
        lax.psum_scatter(sgu_grad, "expert", scatter_dimension=1, tiled=True),
        lax.psum_scatter(sdown_grad, "expert", scatter_dimension=1, tiled=True),
    )
    return (
        mixed,
        input_grad,
        first_owned[0],
        first_owned[1],
        first_owned[2],
        first_owned[3],
        first_owned[4],
        second_owned[0],
        second_owned[1],
        second_owned[2],
        second_owned[3],
        second_owned[4],
        egu_grad,
        edown_grad,
    )


def swap_cores(value):
    return lax.ppermute(value, "tensor", [(0, 1), (1, 0)])


def take_rows(value, start, count):
    return lax.dynamic_slice_in_dim(value, start, count, axis=0)


def in_order(core, own, other):
    return jnp.where(
        core == 0, jnp.concatenate([own, other], axis=0), jnp.concatenate([other, own], axis=0)
    )


def all_groups(value):
    return lax.all_gather(value, "expert", axis=0, tiled=False)


def flip_pairs(groups, stride):
    return [(g, g ^ stride) for g in range(groups)]


def shift_pairs(groups, step):
    deep = groups // 4
    return [(g, (g // 4 + step) % deep * 4 + g % 4) for g in range(groups)]


def add_wide(*parts):
    total = parts[0].astype(jnp.float32)
    for part in parts[1:]:
        total = total + part.astype(jnp.float32)
    return total


def at_index(value, axis, index):
    return lax.dynamic_index_in_dim(value, index, axis, keepdims=False)


def sum_groups(value):
    groups, rows = value.shape[:2]
    me = lax.axis_index("expert")
    z, y, x = me // 4, me // 2 % 2, me % 2
    deep = groups // 4
    blocks = value.reshape(deep, 2, 2, *value.shape[1:])
    cut = rows // 2

    def along(held, axis, mine, stride):
        sent = lax.ppermute(at_index(held, axis, 1 - mine), "expert", flip_pairs(groups, stride))
        return add_wide(at_index(held, axis, mine), sent).astype(value.dtype)

    first = along(blocks[:, :, :, :cut], 1, y, 2)
    second = along(blocks[:, :, :, cut:], 2, x, 1)
    first = along(first, 1, x, 1)
    second = along(second, 1, y, 2)

    def deep_sum(held):
        parts = [at_index(held, 0, z)]
        for step in range(1, deep):
            sent = at_index(held, 0, (z + step) % deep)
            parts.append(lax.ppermute(sent, "expert", shift_pairs(groups, step)))
        return add_wide(*parts)

    return jnp.concatenate([deep_sum(first), deep_sum(second)], axis=0)


def token_plan(
    inputs,
    attn_gain,
    w_query,
    w_latent,
    latent_gain,
    w_kv,
    w_out,
    ffn_gain,
    w_router,
    shared_gate_up,
    shared_down,
    expert_gate_up,
    expert_down,
    lengths,
    routes,
    cotangent,
):
    f32, bf16 = jnp.float32, jnp.bfloat16
    core, me = lax.axis_index("tensor"), lax.axis_index("expert")
    groups = lax.axis_size("expert")
    tok_rows, width = inputs.shape
    half = tok_rows // 2
    own_at, other_at = core * half, (1 - core) * half
    expert_count = w_router.shape[1]
    route_count = routes.shape[1]
    capacity = tok_rows * route_count * 4 // (3 * expert_count)
    shared_cols = shared_gate_up.shape[2] // groups

    latent_cols, out_rows_here = w_latent.shape[1], w_out.shape[0]
    block_rows, query_cols = w_query.shape
    kv_rows, kv_cols = w_kv.shape
    kv_parts = block_rows // kv_rows
    kv_piece = kv_cols // kv_parts
    kv_sent = jnp.concatenate(
        [w_kv[:, p * kv_piece : (p + 1) * kv_piece] for p in range(kv_parts)], axis=0
    )
    gain_sent = jnp.pad(latent_gain, (0, block_rows - kv_rows))
    used = latent_cols + expert_count + 3
    small = jnp.concatenate(
        [
            w_latent,
            w_router,
            attn_gain[:, None],
            ffn_gain[:, None],
            gain_sent[:, None],
            jnp.zeros((block_rows, -used % 128), bf16),
        ],
        axis=1,
    )
    sent_w = jnp.concatenate([w_query, w_out.T, kv_sent, small], axis=1)
    all_w = all_groups(sent_w)
    flat_w = all_w.reshape(groups * block_rows, -1)
    at = query_cols
    query_w = flat_w[:, :at]
    out_wt = flat_w[:, at : at + out_rows_here]
    at += out_rows_here
    kv_w = jnp.concatenate(
        [
            all_w[:, p * kv_rows : (p + 1) * kv_rows, at : at + kv_piece].reshape(-1, kv_piece)
            for p in range(kv_parts)
        ],
        axis=1,
    )
    at += kv_piece
    latent_w = flat_w[:, at : at + latent_cols]
    at += latent_cols
    router_w = flat_w[:, at : at + expert_count]
    at += expert_count
    gain_one, gain_two = flat_w[:, at], flat_w[:, at + 1]
    latent_g = all_w[:, :kv_rows, at + 2].reshape(-1)
    sgu_w = lax.all_to_all(shared_gate_up, "expert", split_axis=2, concat_axis=1, tiled=True)
    sdown_w = lax.all_to_all(shared_down, "expert", split_axis=0, concat_axis=1, tiled=True)
    dy_own_rows = take_rows(cotangent, own_at, half)
    route_sent = jnp.pad(take_rows(routes, own_at, half).astype(bf16), ((0, 0), (0, -route_count % 128)))
    dy_own_sent = all_groups(jnp.concatenate([dy_own_rows, route_sent], axis=1))
    dy_other_sent = swap_cores(dy_own_sent)
    dy_own, dy_other = dy_own_sent[..., :width], dy_other_sent[..., :width]
    routes_own = dy_own_sent[..., width : width + route_count].astype(jnp.int32)
    routes_other = dy_other_sent[..., width : width + route_count].astype(jnp.int32)

    local_heads = query_w.shape[1] // (DN + DR)
    rank_width = latent_g.shape[0]
    x_float = inputs.astype(f32)
    relative, visible = doc_layout(lengths[0], tok_rows)
    cosine, sine_tab = rope_tables(relative, DR)
    q_scale = (DN + DR) ** (-0.5)
    normed, scale_one = rms_forward(x_float, gain_one.astype(f32))
    normed_b = normed.astype(bf16)
    queries = jnp.dot(normed_b, query_w, preferred_element_type=f32).reshape(
        tok_rows, local_heads, DN + DR
    )
    q_rot = rotate(queries[..., DN:], cosine[:, None, :], sine_tab[:, None, :])
    q_all = jnp.concatenate([queries[..., :DN], q_rot], axis=-1).astype(bf16)
    latent = jnp.dot(normed_b, latent_w, preferred_element_type=f32)
    compressed, scale_kv = rms_forward(latent[:, :rank_width], latent_g.astype(f32))
    compressed_b = compressed.astype(bf16)
    k_rope = rotate(latent[:, rank_width:], cosine, sine_tab).astype(bf16)
    kv_all = jnp.dot(compressed_b, kv_w, preferred_element_type=f32).reshape(
        tok_rows, local_heads, DN + DV
    )
    k_nope = kv_all[..., :DN].astype(bf16)
    values = kv_all[..., DN:].astype(bf16)
    key_all = jnp.concatenate(
        [k_nope, jnp.broadcast_to(k_rope[:, None, :], (tok_rows, local_heads, DR))], axis=-1
    )

    def score_block():
        raw_scores = (
            jnp.einsum("qhd,khd->hqk", q_all, key_all, preferred_element_type=f32) * q_scale
        )
        return jnp.where(visible[None], raw_scores, NEGATIVE)

    scores = score_block()
    top_score = jnp.max(scores, axis=-1, keepdims=True)
    log_total = top_score + jnp.log(jnp.sum(jnp.exp(scores - top_score), axis=-1, keepdims=True))
    probs_b = jnp.exp(scores - log_total).astype(bf16)
    attended = jnp.einsum("hqk,khd->qhd", probs_b, values, preferred_element_type=f32)
    attended_b = attended.reshape(tok_rows, local_heads * DV).astype(bf16)
    attn_part = contract_cols(attended_b, out_wt)
    attn_own = take_rows(attn_part, own_at, half) + swap_cores(take_rows(attn_part, other_at, half))
    hidden = take_rows(x_float, own_at, half) + attn_own
    hnormed, scale_two = rms_forward(hidden, gain_two.astype(f32))
    hnormed_b = hnormed.astype(bf16)

    hn_own = all_groups(hnormed_b)
    hn_other = swap_cores(hn_own)

    def membership(named):
        one_hot = named[..., None] == jnp.arange(expert_count, dtype=jnp.int32)
        return jnp.any(named == me, axis=-1), jnp.any(one_hot, axis=2)

    member_own, hot_own = membership(routes_own)
    member_other, hot_other = membership(routes_other)
    lower = (
        jnp.arange(half, dtype=jnp.int32)[:, None] <= jnp.arange(half, dtype=jnp.int32)[None, :]
    ).astype(bf16)

    def running(mask):
        counts = jnp.dot(mask.astype(bf16), lower, preferred_element_type=f32)
        return counts.astype(jnp.int32)

    count_own, count_other = running(member_own), running(member_other)
    place_own = jnp.where(member_own, count_own - 1, -1)
    place_other = jnp.where(member_other, count_own[:, -1:] + count_other - 1, -1)
    slot_index = jnp.arange(capacity, dtype=jnp.int32)

    def dispatch(place):
        return (place[:, None, :] == slot_index[None, :, None]).astype(bf16)

    pick_own, pick_other = dispatch(place_own), dispatch(place_other)

    def to_slots(own, other):
        def part(pick, rows):
            return jnp.einsum("gst,gtd->gsd", pick, rows, preferred_element_type=bf16)

        return (part(pick_own, own) + part(pick_other, other)).reshape(groups * capacity, width)

    first_w = jnp.concatenate([sgu_w[0], sgu_w[1], router_w], axis=1)
    shared_w = first_w[:, : 2 * shared_cols]

    def shared_forward(rows, hot_rows, member_rows):
        flat = rows.reshape(groups * half, width)
        products = jnp.dot(flat, first_w, preferred_element_type=f32)
        gate, up = products[:, :shared_cols], products[:, shared_cols : 2 * shared_cols]
        act = (jax.nn.silu(gate) * up).astype(bf16)
        sig = jax.nn.sigmoid(products[:, 2 * shared_cols :]).reshape(groups, half, expert_count)
        total = jnp.sum(jnp.where(hot_rows, sig, 0.0), axis=-1)
        mine = jnp.sum(jnp.where(jnp.arange(expert_count) == me, sig, 0.0), axis=-1)
        gates = jnp.where(member_rows, ROUTE_SCALE * mine / total, 0.0)
        return gate, up, act, gates

    gate_own, up_own, act_own, gates_own = shared_forward(hn_own, hot_own, member_own)
    gate_other, up_other, act_other, gates_other = shared_forward(hn_other, hot_other, member_other)

    slot_rows = to_slots(hn_own, hn_other)
    slot_dy = to_slots(dy_own, dy_other)
    slot_gate = (
        jnp.sum(pick_own.astype(f32) * gates_own[:, None, :], axis=-1)
        + jnp.sum(pick_other.astype(f32) * gates_other[:, None, :], axis=-1)
    ).reshape(groups * capacity, 1)
    gate_w, up_w, down_w = expert_gate_up[0, 0], expert_gate_up[0, 1], expert_down[0]
    slot_g = jnp.dot(slot_rows, gate_w, preferred_element_type=f32)
    slot_u = jnp.dot(slot_rows, up_w, preferred_element_type=f32)
    slot_act = (jax.nn.silu(slot_g) * slot_u).astype(bf16)
    slot_out = jnp.dot(slot_act, down_w, preferred_element_type=f32)
    dy_float = slot_dy.astype(f32)
    slot_dgate = jnp.sum(slot_out * dy_float, axis=-1).reshape(groups, capacity)
    slot_scaled = (slot_gate * slot_out).astype(bf16).reshape(groups, capacity, width)
    slot_grad = (slot_gate * dy_float).astype(bf16)
    edown_grad = contract_rows(slot_act, slot_grad)
    d_act = contract_cols(slot_grad, down_w)
    d_gate, d_up = gated_linear_backward(slot_g, slot_u, d_act)
    d_gate, d_up = d_gate.astype(bf16), d_up.astype(bf16)
    egu_grad = jnp.stack([contract_rows(slot_rows, d_gate), contract_rows(slot_rows, d_up)])
    slot_drows = (contract_cols(d_gate, gate_w) + contract_cols(d_up, up_w)).astype(bf16)
    slot_drows = slot_drows.reshape(groups, capacity, width)

    def from_slots(pick, rows, left, right):
        routed = jnp.einsum("gst,gsd->gtd", pick, rows, preferred_element_type=f32)
        shared = jnp.dot(left, right, preferred_element_type=f32)
        return (routed + shared.reshape(groups, half, width)).astype(bf16)

    def shared_backward(rows_dy, gate, up):
        d_sact = contract_cols(rows_dy.reshape(groups * half, width), sdown_w)
        d_sgate, d_sup = gated_linear_backward(gate, up, d_sact)
        return jnp.concatenate([d_sgate, d_sup], axis=1).astype(bf16)

    d_shared_own = shared_backward(dy_own, gate_own, up_own)
    d_shared_other = shared_backward(dy_other, gate_other, up_other)
    shared_wt = shared_w.T
    d_rows_own = from_slots(pick_own, slot_drows, d_shared_own, shared_wt)
    d_rows_other = from_slots(pick_other, slot_drows, d_shared_other, shared_wt)
    d_rows = (d_rows_own.astype(f32) + swap_cores(d_rows_other).astype(f32)).astype(bf16)
    d_hn = sum_groups(d_rows)

    out_own = from_slots(pick_own, slot_scaled, act_own, sdown_w)
    out_other = from_slots(pick_other, slot_scaled, act_other, sdown_w)
    out_rows = (out_own.astype(f32) + swap_cores(out_other).astype(f32)).astype(bf16)
    out_rows, d_hn = lax.optimization_barrier((out_rows, d_hn))
    moe_own = sum_groups(out_rows)
    mixed_own = (hidden + moe_own).astype(bf16)
    mixed = in_order(core, mixed_own, swap_cores(mixed_own))

    def flat_rows(value):
        return value.reshape(groups * half, -1)

    sgu_grad = contract_rows(flat_rows(hn_own), d_shared_own) + contract_rows(
        flat_rows(hn_other), d_shared_other
    )
    sdown_grad = contract_rows(act_own, flat_rows(dy_own)) + contract_rows(
        act_other, flat_rows(dy_other)
    )
    sgu_grad = jnp.stack([sgu_grad[:, :shared_cols], sgu_grad[:, shared_cols:]])
    sgu_out = lax.all_to_all(
        sgu_grad.astype(bf16), "expert", split_axis=1, concat_axis=2, tiled=True
    ).astype(f32)
    sdown_out = lax.all_to_all(
        sdown_grad.astype(bf16), "expert", split_axis=1, concat_axis=0, tiled=True
    ).astype(f32)

    def to_tokens(pick):
        return jnp.sum(pick.astype(f32) * slot_dgate[:, :, None], axis=1)

    dgate_sent = to_tokens(pick_own) + swap_cores(to_tokens(pick_other))
    dgate = lax.all_to_all(dgate_sent, "expert", split_axis=0, concat_axis=0, tiled=True).T
    hot_mine = take_rows(
        jnp.any(routes[..., None] == jnp.arange(expert_count, dtype=jnp.int32), axis=1), own_at, half
    )
    sig = jax.nn.sigmoid(jnp.dot(hnormed_b, router_w, preferred_element_type=f32))
    chosen = jnp.where(hot_mine, sig, 0.0)
    chosen_sum = jnp.sum(chosen, axis=1, keepdims=True)
    dgate = jnp.where(hot_mine, dgate, 0.0)
    inner = jnp.sum(dgate * chosen, axis=1, keepdims=True)
    d_chosen = ROUTE_SCALE * (dgate / chosen_sum - inner / (chosen_sum * chosen_sum))
    d_logits = (jnp.where(hot_mine, d_chosen, 0.0) * sig * (1.0 - sig)).astype(bf16)
    router_grad = contract_rows(d_logits, hnormed_b)
    d_hn = d_hn + contract_cols(d_logits, router_w)
    d_hidden_norm, gain_two_grad = rms_backward(hidden, scale_two, gain_two.astype(f32), d_hn)
    d_hidden = dy_own_rows.astype(f32) + d_hidden_norm
    d_hidden_half = d_hidden.astype(bf16)
    d_hidden_b = in_order(core, d_hidden_half, swap_cores(d_hidden_half))

    grad_att = (
        jnp.dot(d_hidden_b, out_wt, preferred_element_type=f32)
        .reshape(tok_rows, local_heads, DV)
        .astype(bf16)
    )
    probs = jnp.exp(score_block() - log_total)
    probs_again = probs.astype(bf16)
    grad_probs = jnp.einsum("qhd,khd->hqk", grad_att, values, preferred_element_type=f32)
    grad_vals = jnp.einsum("hqk,qhd->khd", probs_again, grad_att, preferred_element_type=f32)
    row_delta = jnp.sum(probs * grad_probs, axis=-1, keepdims=True)
    grad_scores = (probs * (grad_probs - row_delta)).astype(bf16)
    grad_q = jnp.einsum("hqk,khd->qhd", grad_scores, key_all, preferred_element_type=f32) * q_scale
    grad_keys = jnp.einsum("hqk,qhd->khd", grad_scores, q_all, preferred_element_type=f32) * q_scale
    grad_kv = (
        jnp.concatenate([grad_keys[..., :DN], grad_vals], axis=-1)
        .reshape(tok_rows, local_heads * (DN + DV))
        .astype(bf16)
    )
    kv_grad = contract_rows(compressed_b, grad_kv)
    grad_latent_part = jnp.concatenate(
        [contract_cols(grad_kv, kv_w), jnp.sum(grad_keys[..., DN:], axis=1)], axis=1
    ).astype(bf16)
    grad_both = grad_latent_part.astype(f32) + swap_cores(grad_latent_part).astype(f32)
    grad_c, latent_gain_grad = rms_backward(
        latent[:, :rank_width], scale_kv, latent_g.astype(f32), grad_both[:, :rank_width]
    )
    grad_latent = jnp.concatenate(
        [grad_c, unrotate(grad_both[:, rank_width:], cosine, sine_tab)], axis=-1
    ).astype(bf16)
    grad_qrot = unrotate(grad_q[..., DN:], cosine[:, None, :], sine_tab[:, None, :])
    grad_queries = (
        jnp.concatenate([grad_q[..., :DN], grad_qrot], axis=-1)
        .reshape(tok_rows, local_heads * (DN + DR))
        .astype(bf16)
    )
    latent_half = latent_cols // 2
    latent_sent = lax.dynamic_slice_in_dim(grad_latent, core * latent_half, latent_half, axis=1)
    first_grad = contract_rows(normed_b, jnp.concatenate([grad_queries, latent_sent], axis=1))
    normed_part = contract_cols(grad_queries, query_w)
    sent_part = take_rows(normed_part, other_at, half).astype(bf16)
    grad_normed = (
        take_rows(normed_part, own_at, half)
        + swap_cores(sent_part).astype(f32)
        + contract_cols(take_rows(grad_latent, own_at, half), latent_w)
    )
    x_own, scale_own = take_rows(x_float, own_at, half), take_rows(scale_one, own_at, half)
    grad_x_norm, gain_one_grad = rms_backward(x_own, scale_own, gain_one.astype(f32), grad_normed)
    input_own = d_hidden + grad_x_norm
    input_grad = in_order(core, input_own, swap_cores(input_own))

    out_grad = contract_rows(d_hidden_b, attended_b)

    def own_block(value):
        return sum_groups(value.astype(bf16).reshape(groups, -1, value.shape[1]))

    w_out_grad = own_block(out_grad).T
    first = own_block(first_grad)
    kv_first = own_block(kv_grad)
    gain_lanes = jnp.pad(
        latent_gain_grad.reshape(groups, kv_rows), ((0, 0), (0, block_rows - kv_rows))
    )
    vectors = jnp.concatenate(
        [
            router_grad,
            gain_one_grad[None],
            gain_two_grad[None],
            0.5 * gain_lanes.reshape(1, -1),
        ],
        axis=0,
    ).reshape(-1, groups, block_rows)
    arrived = lax.all_to_all(vectors, "expert", split_axis=1, concat_axis=1, tiled=True)
    sums = jnp.sum(arrived, axis=1)
    sums = sums + swap_cores(sums)
    latent_mine = first[:, query_cols:]
    latent_theirs = swap_cores(latent_mine)
    latent_out = jnp.where(
        core == 0,
        jnp.concatenate([latent_mine, latent_theirs], axis=1),
        jnp.concatenate([latent_theirs, latent_mine], axis=1),
    )
    return (
        mixed,
        input_grad,
        sums[expert_count],
        first[:, :query_cols],
        latent_out,
        sums[expert_count + 2, :kv_rows],
        kv_first,
        w_out_grad,
        sums[expert_count + 1],
        sums[:expert_count].T,
        sgu_out,
        sdown_out,
        egu_grad[None],
        edown_grad[None],
    )


def solution(mesh):
    groups = mesh.shape["expert"]
    plan = token_plan if groups <= 16 else weight_plan
    return jax.shard_map(
        plan,
        mesh=mesh,
        in_specs=(
            P("expert", None),
            P("expert"),
            P("expert", "tensor"),
            P("expert", None),
            P("expert"),
            P("expert", "tensor"),
            P("tensor", "expert"),
            P("expert"),
            P("expert", None),
            P(None, "expert", "tensor"),
            P("tensor", "expert"),
            P("expert", None, None, "tensor"),
            P("expert", "tensor", None),
            P("expert", None),
            P("expert", None),
            P("expert", None),
        ),
        out_specs=(
            P("expert", None),
            P("expert", None),
            P("expert"),
            P("expert", "tensor"),
            P("expert", None),
            P("expert"),
            P("expert", "tensor"),
            P("tensor", "expert"),
            P("expert"),
            P("expert", None),
            P(None, "expert", "tensor"),
            P("tensor", "expert"),
            P("expert", None, None, "tensor"),
            P("expert", "tensor", None),
        ),
        check_vma=False,
    )
```

```python
import jax
import jax.numpy as jnp
from jax import lax
from jax.sharding import PartitionSpec as P

DN = 128
DR = 64
DV = 128


EPSILON = 1e-06
ROUTE_SCALE = 2.446
ROPE_BASE = 50000.0
NEGATIVE = -1e30


def cut_along(value, dim, length):
    before, after = (value.shape[:dim], value.shape[dim + 1 :])
    return jnp.moveaxis(value.reshape(*before, length, -1, *after), dim, 0)


def summed_on_arrival(value, axis, dim):
    length = lax.axis_size(axis)
    tiles = lax.all_to_all(cut_along(value, dim, length), axis, 0, 0, tiled=True)
    return jnp.sum(tiles.astype(jnp.float32), axis=0)


def sent_together(arrays, axis, dim, along):
    columns = [a.reshape(*a.shape[:along], -1) for a in arrays]
    both = jnp.concatenate(columns, axis=along)
    whole, at, outs = (summed_on_arrival(both, axis, dim), 0, [])
    for a, column in zip(arrays, columns):
        slab = whole[..., at : at + column.shape[along]]
        outs.append(slab.reshape(*slab.shape[:along], *a.shape[along:]))
        at += column.shape[along]
    return tuple(outs)


def contract_rows(left_arr, right_arr):
    return lax.dot_general(
        left_arr, right_arr, (((0,), (0,)), ((), ())), preferred_element_type=jnp.float32
    )


def contract_cols(left_arr, right_arr):
    return lax.dot_general(
        left_arr, right_arr, (((1,), (1,)), ((), ())), preferred_element_type=jnp.float32
    )


def rms_forward(rows_in, gain_vec):
    inverse = lax.rsqrt(jnp.mean(rows_in * rows_in, axis=-1, keepdims=True) + EPSILON)
    return (rows_in * inverse * gain_vec, inverse)


def rms_backward(rows_in, inverse, gain_vec, grad_out):
    gain_grad = jnp.sum(grad_out * rows_in * inverse, axis=0)
    weighted = grad_out * gain_vec
    inner_mean = jnp.mean(weighted * rows_in, axis=-1, keepdims=True)
    return (inverse * weighted - rows_in * inverse * inverse * inverse * inner_mean, gain_grad)


def doc_layout(doc_lengths, row_count):
    ends_at = jnp.cumsum(doc_lengths)
    starts_at = ends_at - doc_lengths
    position = jnp.arange(row_count, dtype=jnp.int32)
    doc_ids = jnp.sum((position[:, None] >= ends_at[None, :]).astype(jnp.int32), axis=1)
    hitting = doc_ids[:, None] == jnp.arange(doc_lengths.shape[0], dtype=jnp.int32)[None, :]
    start_of = jnp.sum(jnp.where(hitting, starts_at[None, :], 0), axis=1)
    relative = position - start_of
    visible = (doc_ids[:, None] == doc_ids[None, :]) & (position[:, None] >= position[None, :])
    return (relative, visible)


def rope_tables(relative, rot_width):
    counter = jnp.arange(rot_width // 2, dtype=jnp.float32)
    frequency = ROPE_BASE ** (-2.0 * counter / rot_width)
    angles = relative.astype(jnp.float32)[:, None] * frequency[None, :]
    return (jnp.cos(angles), jnp.sin(angles))


def rotate(tensor_in, cosine, sine_tab):
    half_width = tensor_in.shape[-1] // 2
    leading = tensor_in[..., :half_width]
    trailing = tensor_in[..., half_width:]
    return jnp.concatenate(
        [leading * cosine - trailing * sine_tab, trailing * cosine + leading * sine_tab], axis=-1
    )


def unrotate(grad_in, cosine, sine_tab):
    half_width = grad_in.shape[-1] // 2
    leading = grad_in[..., :half_width]
    trailing = grad_in[..., half_width:]
    return jnp.concatenate(
        [leading * cosine + trailing * sine_tab, trailing * cosine - leading * sine_tab], axis=-1
    )


def gated_linear_backward(gate_in, up_in, grad_act):
    sigmoid_g = jax.nn.sigmoid(gate_in)
    grad_gate = grad_act * up_in * sigmoid_g * (1.0 + gate_in * (1.0 - sigmoid_g))
    return (grad_gate, grad_act * gate_in * sigmoid_g)


def slot_tables(route_rows, expert_count, capacity):
    flat_routes = route_rows.reshape(-1)
    one_hot = (flat_routes[:, None] == jnp.arange(expert_count, dtype=jnp.int32)[None, :]).astype(
        jnp.int32
    )
    ranking = jnp.sum((jnp.cumsum(one_hot, axis=0) - one_hot) * one_hot, axis=1)
    slot_ids = flat_routes * capacity + ranking
    row_total = flat_routes.shape[0]
    source = (
        jnp.zeros((expert_count * capacity,), jnp.int32)
        .at[slot_ids]
        .set(jnp.arange(row_total, dtype=jnp.int32))
    )
    filled = jnp.zeros((expert_count * capacity,), jnp.int32).at[slot_ids].set(1)
    return (slot_ids, source, filled)


def to_owner(rows_in):
    arrived = lax.all_to_all(rows_in, "expert", split_axis=0, concat_axis=1, tiled=True)
    return arrived


def weight_plan(
    inputs,
    attn_gain,
    w_query,
    w_latent,
    latent_gain,
    w_kv,
    w_out,
    ffn_gain,
    w_router,
    shared_gate_up,
    shared_down,
    expert_gate_up,
    expert_down,
    lengths,
    routes,
    cotangent,
):
    tok_rows = inputs.shape[0]
    model_width = inputs.shape[1]
    expert_count = w_router.shape[1]
    route_count = routes.shape[1]
    capacity = tok_rows * route_count * 4 // (3 * expert_count)
    brain_float16 = jnp.bfloat16
    f32 = jnp.float32
    gathered = (
        lax.all_gather(attn_gain, "expert", axis=0, tiled=True),
        lax.all_gather(w_query, "expert", axis=0, tiled=True),
        lax.all_gather(w_latent, "expert", axis=0, tiled=True),
        lax.all_gather(latent_gain, "expert", axis=0, tiled=True),
        lax.all_gather(w_kv, "expert", axis=0, tiled=True),
        lax.all_gather(w_out, "expert", axis=1, tiled=True),
        lax.all_gather(ffn_gain, "expert", axis=0, tiled=True),
        lax.all_gather(w_router, "expert", axis=0, tiled=True),
        lax.all_gather(shared_gate_up, "expert", axis=1, tiled=True),
        lax.all_gather(shared_down, "expert", axis=1, tiled=True),
    )
    gain_one, query_w, latent_w, latent_g, kv_w, out_w, gain_two, router_w, sgate_up, sdown_w = (
        gathered
    )
    local_heads = query_w.shape[1] // (DN + DR)
    rank_width = latent_g.shape[0]
    x_float = inputs.astype(f32)
    relative, visible = doc_layout(lengths[0], tok_rows)
    cosine, sine_tab = rope_tables(relative, DR)
    q_scale = (DN + DR) ** (-0.5)
    normed, scale_one = rms_forward(x_float, gain_one.astype(f32))
    normed_b = normed.astype(brain_float16)
    queries = jnp.dot(normed_b, query_w, preferred_element_type=f32).reshape(
        tok_rows, local_heads, DN + DR
    )
    q_rot = rotate(queries[..., DN:], cosine[:, None, :], sine_tab[:, None, :])
    q_all = jnp.concatenate([queries[..., :DN], q_rot], axis=-1).astype(brain_float16)
    latent = jnp.dot(normed_b, latent_w, preferred_element_type=f32)
    compressed, scale_kv = rms_forward(latent[:, :rank_width], latent_g.astype(f32))
    compressed_b = compressed.astype(brain_float16)
    k_rope = rotate(latent[:, rank_width:], cosine, sine_tab).astype(brain_float16)
    kv_all = jnp.dot(compressed_b, kv_w, preferred_element_type=f32).reshape(
        tok_rows, local_heads, DN + DV
    )
    k_nope = kv_all[..., :DN].astype(brain_float16)
    values = kv_all[..., DN:].astype(brain_float16)
    key_all = jnp.concatenate(
        [k_nope, jnp.broadcast_to(k_rope[:, None, :], (tok_rows, local_heads, DR))], axis=-1
    )

    def score_block():
        raw_scores = (
            jnp.einsum("qhd,khd->hqk", q_all, key_all, preferred_element_type=f32) * q_scale
        )
        return jnp.where(visible[None], raw_scores, NEGATIVE)

    scores = score_block()
    top_score = jnp.max(scores, axis=-1, keepdims=True)
    log_total = top_score + jnp.log(jnp.sum(jnp.exp(scores - top_score), axis=-1, keepdims=True))
    probs_b = jnp.exp(scores - log_total).astype(brain_float16)
    attended = jnp.einsum("hqk,khd->qhd", probs_b, values, preferred_element_type=f32)
    attended_b = attended.reshape(tok_rows, local_heads * DV).astype(brain_float16)
    attn = lax.psum(jnp.dot(attended_b, out_w, preferred_element_type=f32), "tensor")
    hidden = x_float + attn
    hnormed, scale_two = rms_forward(hidden, gain_two.astype(f32))
    hnormed_b = hnormed.astype(brain_float16)
    logits = jnp.dot(hnormed_b, router_w, preferred_element_type=f32)
    sigmoid_vals = jax.nn.sigmoid(logits)
    route_hot = routes[:, :, None] == jnp.arange(expert_count, dtype=jnp.int32)[None, None, :]
    chosen = jnp.sum(jnp.where(route_hot, sigmoid_vals[:, None, :], 0.0), axis=2)
    chosen_sum = jnp.sum(chosen, axis=1, keepdims=True)
    gate_vals = ROUTE_SCALE * chosen / chosen_sum
    slot_ids, source, filled = slot_tables(routes, expert_count, capacity)
    is_filled = filled[:, None] == 1
    sent_rows = jnp.where(is_filled, hnormed_b[source // route_count], 0).reshape(
        expert_count, capacity, model_width
    )
    received = to_owner(sent_rows)
    gate_up_joined = jnp.einsum(
        "erd,egdf->egrf", received, expert_gate_up, preferred_element_type=f32
    )
    expert_act = (jax.nn.silu(gate_up_joined[:, 0]) * gate_up_joined[:, 1]).astype(brain_float16)
    expert_res = jnp.einsum(
        "erf,efd->erd", expert_act, expert_down, preferred_element_type=f32
    ).astype(brain_float16)
    returned_all = lax.all_to_all(expert_res, "expert", split_axis=1, concat_axis=0, tiled=True)
    returned = returned_all.reshape(expert_count * capacity, model_width)[slot_ids].reshape(
        tok_rows, route_count, model_width
    )
    shared_gu = jnp.einsum("td,gdf->gtf", hnormed_b, sgate_up, preferred_element_type=f32)
    shared_act = (jax.nn.silu(shared_gu[0]) * shared_gu[1]).astype(brain_float16)
    branch_sum = jnp.dot(shared_act, sdown_w, preferred_element_type=f32)
    for route_idx in range(route_count):
        branch_sum = branch_sum + gate_vals[:, route_idx : route_idx + 1] * returned[
            :, route_idx
        ].astype(f32)
    moe_out = lax.psum(branch_sum.astype(jnp.bfloat16), "tensor").astype(jnp.float32)
    mixed = (hidden + moe_out).astype(brain_float16)
    grad_y = cotangent.astype(f32)
    sdown_grad = contract_rows(shared_act, cotangent)
    grad_sact = contract_cols(cotangent, sdown_w)
    grad_sgate, grad_sup = gated_linear_backward(shared_gu[0], shared_gu[1], grad_sact)
    grad_sgu = jnp.stack([grad_sgate, grad_sup], axis=0).astype(brain_float16)
    sgu_grad = jnp.einsum("td,gtf->gdf", hnormed_b, grad_sgu, preferred_element_type=f32)
    grad_hn_part = jnp.einsum("gtf,gdf->td", grad_sgu, sgate_up, preferred_element_type=f32)
    gate_columns = []
    for route_idx in range(route_count):
        gate_columns.append(jnp.sum(grad_y * returned[:, route_idx].astype(f32), axis=1))
    gate_part = jnp.stack(gate_columns, axis=1)
    slot_grads = (
        (gate_vals[:, :, None] * grad_y[:, None, :])
        .reshape(tok_rows * route_count, model_width)
        .astype(brain_float16)
    )
    grad_sent = jnp.where(is_filled, slot_grads[source], 0).reshape(
        expert_count, capacity, model_width
    )
    grad_received = to_owner(grad_sent)
    edown_grad = jnp.einsum("erf,erd->efd", expert_act, grad_received, preferred_element_type=f32)
    expert_activation_gradient = jnp.einsum(
        "erd,efd->erf", grad_received, expert_down, preferred_element_type=f32
    )
    expert_gate_gradient, expert_up_gradient = gated_linear_backward(
        gate_up_joined[:, 0], gate_up_joined[:, 1], expert_activation_gradient
    )
    expert_gate_up_gradient = jnp.stack([expert_gate_gradient, expert_up_gradient], axis=1).astype(
        brain_float16
    )
    egu_grad = jnp.einsum(
        "erd,egrf->egdf", received, expert_gate_up_gradient, preferred_element_type=f32
    )
    grad_rows = jnp.einsum(
        "egrf,egdf->erd", expert_gate_up_gradient, expert_gate_up, preferred_element_type=f32
    ).astype(brain_float16)
    grad_back = lax.all_to_all(grad_rows, "expert", split_axis=1, concat_axis=0, tiled=True)
    grad_routes = grad_back.reshape(expert_count * capacity, model_width)[slot_ids].reshape(
        tok_rows, route_count, model_width
    )
    for route_idx in range(route_count):
        grad_hn_part = grad_hn_part + grad_routes[:, route_idx].astype(f32)
    gate_grads = lax.psum(gate_part, "tensor")
    grad_chosen = ROUTE_SCALE * (
        gate_grads / chosen_sum
        - jnp.sum(gate_grads * chosen, axis=1, keepdims=True) / (chosen_sum * chosen_sum)
    )
    grad_sig = jnp.sum(jnp.where(route_hot, grad_chosen[:, :, None], 0.0), axis=1)
    grad_logits = (grad_sig * sigmoid_vals * (1.0 - sigmoid_vals)).astype(brain_float16)
    router_grad = contract_rows(hnormed_b, grad_logits)
    grad_hn = lax.psum(grad_hn_part, "tensor") + contract_cols(grad_logits, router_w)
    grad_hidden_norm, gain_two_grad = rms_backward(hidden, scale_two, gain_two.astype(f32), grad_hn)
    grad_hidden = grad_y + grad_hidden_norm
    grad_hidden_b = grad_hidden.astype(brain_float16)
    out_grad = contract_rows(attended_b, grad_hidden_b)
    grad_att = (
        contract_cols(grad_hidden_b, out_w).reshape(tok_rows, local_heads, DV).astype(brain_float16)
    )
    probs = jnp.exp(score_block() - log_total)
    probs_again = probs.astype(brain_float16)
    grad_probs = jnp.einsum("qhd,khd->hqk", grad_att, values, preferred_element_type=f32)
    grad_vals = jnp.einsum("hqk,qhd->khd", probs_again, grad_att, preferred_element_type=f32)
    row_delta = jnp.sum(probs * grad_probs, axis=-1, keepdims=True)
    grad_scores = (probs * (grad_probs - row_delta)).astype(brain_float16)
    grad_q = jnp.einsum("hqk,khd->qhd", grad_scores, key_all, preferred_element_type=f32) * q_scale
    grad_keys = jnp.einsum("hqk,qhd->khd", grad_scores, q_all, preferred_element_type=f32) * q_scale
    grad_kv = (
        jnp.concatenate([grad_keys[..., :DN], grad_vals], axis=-1)
        .reshape(tok_rows, local_heads * (DN + DV))
        .astype(brain_float16)
    )
    kv_grad = contract_rows(compressed_b, grad_kv)
    grad_comp_part = contract_cols(grad_kv, kv_w)
    grad_krope_part = jnp.sum(grad_keys[..., DN:], axis=1)
    grad_comp, grad_krope = (
        lax.psum(grad_comp_part.astype(jnp.bfloat16), "tensor").astype(jnp.float32),
        lax.psum(grad_krope_part.astype(jnp.bfloat16), "tensor").astype(jnp.float32),
    )
    grad_c, latent_gain_grad = rms_backward(
        latent[:, :rank_width], scale_kv, latent_g.astype(f32), grad_comp
    )
    grad_latent = jnp.concatenate([grad_c, unrotate(grad_krope, cosine, sine_tab)], axis=-1).astype(
        brain_float16
    )
    grad_qrot = unrotate(grad_q[..., DN:], cosine[:, None, :], sine_tab[:, None, :])
    grad_queries = (
        jnp.concatenate([grad_q[..., :DN], grad_qrot], axis=-1)
        .reshape(tok_rows, local_heads * (DN + DR))
        .astype(brain_float16)
    )
    query_grad = contract_rows(normed_b, grad_queries)
    latent_grad = contract_rows(normed_b, grad_latent)
    grad_normed = lax.psum(
        contract_cols(grad_queries, query_w).astype(jnp.bfloat16), "tensor"
    ).astype(jnp.float32) + contract_cols(grad_latent, latent_w)
    grad_x_norm, gain_one_grad = rms_backward(x_float, scale_one, gain_one.astype(f32), grad_normed)
    input_grad = grad_hidden + grad_x_norm
    first_owned = (
        *sent_together(
            (
                gain_one_grad.astype(jnp.bfloat16),
                query_grad.astype(jnp.bfloat16),
                latent_grad.astype(jnp.bfloat16),
            ),
            "expert",
            0,
            1,
        ),
        *sent_together(
            (latent_gain_grad.astype(jnp.bfloat16), kv_grad.astype(jnp.bfloat16)), "expert", 0, 1
        ),
    )
    second_owned = (
        lax.psum_scatter(out_grad, "expert", scatter_dimension=1, tiled=True),
        lax.psum_scatter(gain_two_grad, "expert", scatter_dimension=0, tiled=True),
        lax.psum_scatter(router_grad, "expert", scatter_dimension=0, tiled=True),
        lax.psum_scatter(sgu_grad, "expert", scatter_dimension=1, tiled=True),
        lax.psum_scatter(sdown_grad, "expert", scatter_dimension=1, tiled=True),
    )
    return (
        mixed,
        input_grad,
        first_owned[0],
        first_owned[1],
        first_owned[2],
        first_owned[3],
        first_owned[4],
        second_owned[0],
        second_owned[1],
        second_owned[2],
        second_owned[3],
        second_owned[4],
        egu_grad,
        edown_grad,
    )


def swap_cores(value):
    return lax.ppermute(value, "tensor", [(0, 1), (1, 0)])


def take_rows(value, start, count, axis=0):
    return lax.dynamic_slice_in_dim(value, start, count, axis=axis)


def in_order(core, own, other, axis=0):
    return jnp.where(
        core == 0,
        jnp.concatenate([own, other], axis=axis),
        jnp.concatenate([other, own], axis=axis),
    )


def add_wide(*parts):
    total = parts[0].astype(jnp.float32)
    for part in parts[1:]:
        total = total + part.astype(jnp.float32)
    return total


PLANE = 4


def to_partner(value, flips):
    groups = lax.axis_size("expert")
    return lax.ppermute(value, "expert", [(g, g ^ flips) for g in range(groups)])


def to_deeper(value, step):
    groups = lax.axis_size("expert")
    pairs = [(g, (g + step * PLANE) % groups) for g in range(groups)]
    return lax.ppermute(value, "expert", pairs)


def plane_gather(value):
    return [value] + [to_partner(value, r) for r in range(1, PLANE)]


def plane_scatter(parts):
    return add_wide(parts[0], *[to_partner(parts[r], r) for r in range(1, PLANE)])


def by_place(parts, place):
    odd, high = place % 2 == 1, place // 2 == 1
    parts = [jnp.where(odd, parts[i ^ 1], parts[i]) for i in range(PLANE)]
    return [jnp.where(high, parts[i ^ 2], parts[i]) for i in range(PLANE)]


def deep_gather(value, z):
    deep = lax.axis_size("expert") // PLANE
    whole = jnp.zeros((deep, *value.shape), value.dtype)
    whole = lax.dynamic_update_index_in_dim(whole, value, z, 0)
    for step in range(1, deep):
        came = to_deeper(value, step)
        whole = lax.dynamic_update_index_in_dim(whole, came, (z - step) % deep, 0)
    return whole


def deep_scatter(blocks, z):
    deep = blocks.shape[0]

    def block(index):
        return lax.dynamic_index_in_dim(blocks, index, 0, keepdims=False)

    return add_wide(
        block(z), *[to_deeper(block((z + step) % deep), step) for step in range(1, deep)]
    )


def gather_columns(weight, place, z):
    quarter = weight.shape[1] // PLANE
    parts = [take_rows(weight, place * quarter, quarter, axis=1)]
    for r in range(1, PLANE):
        parts.append(to_partner(take_rows(weight, (place ^ r) * quarter, quarter, axis=1), r))
    rows = jnp.concatenate(by_place(parts, place), axis=0)
    return deep_gather(rows, z).reshape(-1, quarter)


def scatter_columns(grad, place, z):
    deep = lax.axis_size("expert") // PLANE
    quarter = grad.shape[1]
    rows = deep_scatter(grad.astype(jnp.bfloat16).reshape(deep, -1, quarter), z)
    rows = rows.astype(jnp.bfloat16).reshape(PLANE, -1, quarter)

    def block(index):
        return lax.dynamic_index_in_dim(rows, index, 0, keepdims=False)

    parts = [block(place)] + [to_partner(block(place ^ r), r) for r in range(1, PLANE)]
    return jnp.concatenate(by_place(parts, place), axis=1).astype(jnp.float32)


def gather_tokens(value):
    deep = lax.axis_size("expert") // PLANE
    cut = value.shape[0] // 2

    def half(own, near, far):
        line = [own] + [to_deeper(own, step) for step in range(1, deep)]
        beside = [to_partner(piece, near) for piece in line]
        across = [to_partner(piece, far) for piece in line]
        corner = [to_partner(piece, far) for piece in beside]
        found = {0: line, near: beside, far: across, near | far: corner}
        return jnp.stack([piece for r in range(PLANE) for piece in found[r]])

    return jnp.concatenate([half(value[:cut], 1, 2), half(value[cut:], 2, 1)], axis=1)


def scatter_tokens(value):
    deep = lax.axis_size("expert") // PLANE
    cut = value.shape[1] // 2
    blocks = value.reshape(PLANE, deep, *value.shape[1:])

    def half(held, near, far):
        beside = add_wide(held[near], to_partner(held[near | far], far)).astype(value.dtype)
        line = add_wide(held[0], to_partner(held[far], far)).astype(value.dtype)
        line = add_wide(line, to_partner(beside, near)).astype(value.dtype)
        return add_wide(line[0], *[to_deeper(line[step], -step) for step in range(1, deep)])

    return jnp.concatenate([half(blocks[:, :, :cut], 1, 2), half(blocks[:, :, cut:], 2, 1)], axis=0)


def token_plan(
    inputs,
    attn_gain,
    w_query,
    w_latent,
    latent_gain,
    w_kv,
    w_out,
    ffn_gain,
    w_router,
    shared_gate_up,
    shared_down,
    expert_gate_up,
    expert_down,
    lengths,
    routes,
    cotangent,
):
    f32, bf16 = jnp.float32, jnp.bfloat16
    core, me = lax.axis_index("tensor"), lax.axis_index("expert")
    groups = lax.axis_size("expert")
    deep, place, z = groups // PLANE, me % PLANE, me // PLANE
    tok_rows, width = inputs.shape
    half = tok_rows // 2
    own_at, other_at = core * half, (1 - core) * half
    expert_count = w_router.shape[1]
    route_count = routes.shape[1]
    capacity = tok_rows * route_count * 4 // (3 * expert_count)
    shared_cols = shared_gate_up.shape[2] // groups
    latent_cols, rank_width = w_latent.shape[1], latent_gain.shape[0] * groups
    block_rows = w_query.shape[0]
    kv_rows = w_kv.shape[0]

    lengths_near = jnp.stack(plane_gather(lengths[0]))
    x_near_own = jnp.stack(plane_gather(take_rows(inputs, own_at, half)))
    x_near = in_order(core, x_near_own, swap_cores(x_near_own), axis=1)
    query_cols = w_query.shape[1] // PLANE
    out_cols = w_out.shape[0] // PLANE
    used = latent_cols + expert_count + 3
    small = jnp.concatenate(
        [
            w_latent,
            w_router,
            attn_gain[:, None],
            ffn_gain[:, None],
            jnp.pad(latent_gain, (0, block_rows - kv_rows))[:, None],
            jnp.zeros((block_rows, -used % 128), bf16),
        ],
        axis=1,
    )
    small_half = take_rows(small, core * (block_rows // 2), block_rows // 2)
    small_plane = jnp.stack(by_place(plane_gather(small_half), place))
    small_own = deep_gather(small_plane, z)
    small_all = in_order(core, small_own, swap_cores(small_own), axis=2)
    small_all = small_all.reshape(groups, block_rows, -1)
    flat_small = small_all.reshape(groups * block_rows, -1)
    latent_w = flat_small[:, :latent_cols]
    at = latent_cols
    router_w = flat_small[:, at : at + expert_count]
    at += expert_count
    gain_one, gain_two = flat_small[:, at], flat_small[:, at + 1]
    latent_g = small_all[:, :kv_rows, at + 2].reshape(-1)
    query_w = gather_columns(w_query, place, z)
    kv_w = gather_columns(w_kv, place, z)
    out_wt = gather_columns(w_out.T, place, z)
    route_sent = jnp.broadcast_to(
        routes.astype(bf16).reshape(1, -1), (groups, tok_rows * route_count)
    )
    route_came = lax.all_to_all(route_sent, "expert", split_axis=0, concat_axis=0, tiled=True)
    block_index = jnp.arange(groups)
    block_chip = (z - block_index % deep) % deep * PLANE + (place ^ (block_index // deep))
    in_blocks = (block_chip[:, None] == block_index[None, :]).astype(bf16)
    route_all = jnp.dot(in_blocks, route_came, preferred_element_type=f32)
    route_all = route_all.astype(jnp.int32).reshape(groups, tok_rows, route_count)
    sgu_w = lax.all_to_all(shared_gate_up, "expert", split_axis=2, concat_axis=1, tiled=True)
    sdown_w = lax.all_to_all(shared_down, "expert", split_axis=0, concat_axis=1, tiled=True)

    near_rows = PLANE * tok_rows
    local_heads = query_cols // (DN + DR)
    x_float = x_near.astype(f32)
    relative, visible = jax.vmap(lambda one: doc_layout(one, tok_rows))(lengths_near)
    cosine, sine_tab = rope_tables(relative.reshape(-1), DR)
    q_scale = (DN + DR) ** (-0.5)
    normed, _ = rms_forward(x_float, gain_one.astype(f32))
    normed_b = normed.astype(bf16).reshape(near_rows, width)
    queries = jnp.dot(normed_b, query_w, preferred_element_type=f32).reshape(
        near_rows, local_heads, DN + DR
    )
    q_rot = rotate(queries[..., DN:], cosine[:, None, :], sine_tab[:, None, :])
    q_all = jnp.concatenate([queries[..., :DN], q_rot], axis=-1).astype(bf16)
    q_all = q_all.reshape(PLANE, tok_rows, local_heads, DN + DR)
    latent = jnp.dot(normed_b, latent_w, preferred_element_type=f32)
    compressed, _ = rms_forward(latent[:, :rank_width], latent_g.astype(f32))
    compressed_b = compressed.astype(bf16)
    k_rope = rotate(latent[:, rank_width:], cosine, sine_tab).astype(bf16)
    kv_all = jnp.dot(compressed_b, kv_w, preferred_element_type=f32).reshape(
        PLANE, tok_rows, local_heads, DN + DV
    )
    k_nope = kv_all[..., :DN].astype(bf16)
    values = kv_all[..., DN:].astype(bf16)
    k_rope = k_rope.reshape(PLANE, tok_rows, 1, DR)
    key_all = jnp.concatenate(
        [k_nope, jnp.broadcast_to(k_rope, (PLANE, tok_rows, local_heads, DR))], axis=-1
    )

    def score_block():
        raw_scores = (
            jnp.einsum("gqhd,gkhd->ghqk", q_all, key_all, preferred_element_type=f32) * q_scale
        )
        return jnp.where(visible[:, None], raw_scores, NEGATIVE)

    scores = score_block()
    top_score = jnp.max(scores, axis=-1, keepdims=True)
    log_total = top_score + jnp.log(jnp.sum(jnp.exp(scores - top_score), axis=-1, keepdims=True))
    probs_b = jnp.exp(scores - log_total).astype(bf16)
    attended = jnp.einsum("ghqk,gkhd->gqhd", probs_b, values, preferred_element_type=f32)
    attended_b = attended.reshape(near_rows, local_heads * DV).astype(bf16)

    def sum_heads(part):
        part = part.astype(bf16).reshape(PLANE, tok_rows, -1)
        came = swap_cores(take_rows(part, other_at, half, axis=1))
        both = add_wide(take_rows(part, own_at, half, axis=1), came).astype(bf16)
        return plane_scatter([both[r] for r in range(PLANE)])

    attn_own = sum_heads(contract_cols(attended_b, out_wt))
    x_own = take_rows(inputs, own_at, half).astype(f32)
    hidden = x_own + attn_own
    hnormed, scale_two = rms_forward(hidden, gain_two.astype(f32))
    hnormed_b = hnormed.astype(bf16)
    dy_own_rows = take_rows(cotangent, own_at, half)
    dy_sent, _ = lax.optimization_barrier((dy_own_rows, out_wt))
    dy_own = gather_tokens(dy_sent)
    dy_other = swap_cores(dy_own)

    hn_own = gather_tokens(hnormed_b)
    hn_other = swap_cores(hn_own)

    def membership(named):
        one_hot = named[..., None] == jnp.arange(expert_count, dtype=jnp.int32)
        return jnp.any(named == me, axis=-1), jnp.any(one_hot, axis=2)

    member_own, hot_own = membership(take_rows(route_all, own_at, half, axis=1))
    member_other, hot_other = membership(take_rows(route_all, other_at, half, axis=1))
    lower = (
        jnp.arange(half, dtype=jnp.int32)[:, None] <= jnp.arange(half, dtype=jnp.int32)[None, :]
    ).astype(bf16)

    def running(mask):
        counts = jnp.dot(mask.astype(bf16), lower, preferred_element_type=f32)
        return counts.astype(jnp.int32)

    count_own, count_other = running(member_own), running(member_other)
    place_own = jnp.where(member_own, count_own - 1, -1)
    place_other = jnp.where(member_other, count_own[:, -1:] + count_other - 1, -1)
    slot_index = jnp.arange(capacity, dtype=jnp.int32)

    def dispatch(place):
        return (place[:, None, :] == slot_index[None, :, None]).astype(bf16)

    pick_own, pick_other = dispatch(place_own), dispatch(place_other)

    def to_slots(own, other):
        def part(pick, rows):
            return jnp.einsum("gst,gtd->gsd", pick, rows, preferred_element_type=bf16)

        return (part(pick_own, own) + part(pick_other, other)).reshape(groups * capacity, width)

    first_w = jnp.concatenate([sgu_w[0], sgu_w[1], router_w], axis=1)
    shared_w = first_w[:, : 2 * shared_cols]

    def shared_forward(rows, hot_rows, member_rows):
        flat = rows.reshape(groups * half, width)
        products = jnp.dot(flat, first_w, preferred_element_type=f32)
        gate, up = products[:, :shared_cols], products[:, shared_cols : 2 * shared_cols]
        act = (jax.nn.silu(gate) * up).astype(bf16)
        sig = jax.nn.sigmoid(products[:, 2 * shared_cols :]).reshape(groups, half, expert_count)
        total = jnp.sum(jnp.where(hot_rows, sig, 0.0), axis=-1)
        mine = jnp.sum(jnp.where(jnp.arange(expert_count) == me, sig, 0.0), axis=-1)
        gates = jnp.where(member_rows, ROUTE_SCALE * mine / total, 0.0)
        return gate, up, act, gates

    gate_own, up_own, act_own, gates_own = shared_forward(hn_own, hot_own, member_own)
    gate_other, up_other, act_other, gates_other = shared_forward(hn_other, hot_other, member_other)

    slot_rows = to_slots(hn_own, hn_other)
    slot_dy = to_slots(dy_own, dy_other)
    slot_gate = (
        jnp.sum(pick_own.astype(f32) * gates_own[:, None, :], axis=-1)
        + jnp.sum(pick_other.astype(f32) * gates_other[:, None, :], axis=-1)
    ).reshape(groups * capacity, 1)
    gate_w, up_w, down_w = expert_gate_up[0, 0], expert_gate_up[0, 1], expert_down[0]
    slot_g = jnp.dot(slot_rows, gate_w, preferred_element_type=f32)
    slot_u = jnp.dot(slot_rows, up_w, preferred_element_type=f32)
    slot_act = (jax.nn.silu(slot_g) * slot_u).astype(bf16)
    slot_out = jnp.dot(slot_act, down_w, preferred_element_type=f32)
    dy_float = slot_dy.astype(f32)
    slot_dgate = jnp.sum(slot_out * dy_float, axis=-1).reshape(groups, capacity)
    slot_scaled = (slot_gate * slot_out).astype(bf16).reshape(groups, capacity, width)
    slot_grad = (slot_gate * dy_float).astype(bf16)
    edown_grad = contract_rows(slot_act, slot_grad)
    d_act = contract_cols(slot_grad, down_w)
    d_gate, d_up = gated_linear_backward(slot_g, slot_u, d_act)
    d_gate, d_up = d_gate.astype(bf16), d_up.astype(bf16)
    egu_grad = jnp.stack([contract_rows(slot_rows, d_gate), contract_rows(slot_rows, d_up)])
    slot_drows = (contract_cols(d_gate, gate_w) + contract_cols(d_up, up_w)).astype(bf16)
    slot_drows = slot_drows.reshape(groups, capacity, width)

    def from_slots(pick, rows, left, right):
        routed = jnp.einsum("gst,gsd->gtd", pick, rows, preferred_element_type=f32)
        shared = jnp.dot(left, right, preferred_element_type=f32)
        return (routed + shared.reshape(groups, half, width)).astype(bf16)

    def shared_backward(rows_dy, gate, up):
        d_sact = contract_cols(rows_dy.reshape(groups * half, width), sdown_w)
        d_sgate, d_sup = gated_linear_backward(gate, up, d_sact)
        return jnp.concatenate([d_sgate, d_sup], axis=1).astype(bf16)

    d_shared_own = shared_backward(dy_own, gate_own, up_own)
    d_shared_other = shared_backward(dy_other, gate_other, up_other)
    shared_wt = shared_w.T
    d_rows_own = from_slots(pick_own, slot_drows, d_shared_own, shared_wt)
    d_rows_other = from_slots(pick_other, slot_drows, d_shared_other, shared_wt)
    d_rows = (d_rows_own.astype(f32) + swap_cores(d_rows_other).astype(f32)).astype(bf16)
    d_hn = scatter_tokens(d_rows)

    out_own = from_slots(pick_own, slot_scaled, act_own, sdown_w)
    out_other = from_slots(pick_other, slot_scaled, act_other, sdown_w)
    out_rows = (out_own.astype(f32) + swap_cores(out_other).astype(f32)).astype(bf16)
    out_rows, d_hn = lax.optimization_barrier((out_rows, d_hn))
    moe_own = scatter_tokens(out_rows)
    mixed_own = (hidden + moe_own).astype(bf16)
    mixed = in_order(core, mixed_own, swap_cores(mixed_own))

    def flat_rows(value):
        return value.reshape(groups * half, -1)

    sgu_grad = contract_rows(flat_rows(hn_own), d_shared_own) + contract_rows(
        flat_rows(hn_other), d_shared_other
    )
    sdown_grad = contract_rows(act_own, flat_rows(dy_own)) + contract_rows(
        act_other, flat_rows(dy_other)
    )
    sgu_grad = jnp.stack([sgu_grad[:, :shared_cols], sgu_grad[:, shared_cols:]])
    sgu_out = lax.all_to_all(
        sgu_grad.astype(bf16), "expert", split_axis=1, concat_axis=2, tiled=True
    ).astype(f32)
    sdown_out = lax.all_to_all(
        sdown_grad.astype(bf16), "expert", split_axis=1, concat_axis=0, tiled=True
    ).astype(f32)

    def to_tokens(pick):
        return jnp.sum(pick.astype(f32) * slot_dgate[:, :, None], axis=1)

    dgate_sent = to_tokens(pick_own) + swap_cores(to_tokens(pick_other))
    to_chip = (block_chip[None, :] == block_index[:, None]).astype(f32)
    dgate_sent = jnp.dot(to_chip, dgate_sent, precision=lax.Precision.HIGHEST)
    dgate = lax.all_to_all(dgate_sent, "expert", split_axis=0, concat_axis=0, tiled=True).T
    hot_mine = take_rows(
        jnp.any(routes[..., None] == jnp.arange(expert_count, dtype=jnp.int32), axis=1), own_at, half
    )
    sig = jax.nn.sigmoid(jnp.dot(hnormed_b, router_w, preferred_element_type=f32))
    chosen = jnp.where(hot_mine, sig, 0.0)
    chosen_sum = jnp.sum(chosen, axis=1, keepdims=True)
    dgate = jnp.where(hot_mine, dgate, 0.0)
    inner = jnp.sum(dgate * chosen, axis=1, keepdims=True)
    d_chosen = ROUTE_SCALE * (dgate / chosen_sum - inner / (chosen_sum * chosen_sum))
    d_logits = (jnp.where(hot_mine, d_chosen, 0.0) * sig * (1.0 - sig)).astype(bf16)
    router_grad = contract_rows(d_logits, hnormed_b)
    d_hn = d_hn + contract_cols(d_logits, router_w)
    d_hidden_norm, gain_two_grad = rms_backward(hidden, scale_two, gain_two.astype(f32), d_hn)
    d_hidden = dy_own_rows.astype(f32) + d_hidden_norm
    d_near_own = jnp.stack(plane_gather(d_hidden.astype(bf16)))
    d_near = in_order(core, d_near_own, swap_cores(d_near_own), axis=1).reshape(near_rows, width)

    grad_att = (
        jnp.dot(d_near, out_wt, preferred_element_type=f32)
        .reshape(PLANE, tok_rows, local_heads, DV)
        .astype(bf16)
    )
    w_out_grad = scatter_columns(contract_rows(d_near, attended_b), place, z).T
    probs = jnp.exp(score_block() - log_total)
    probs_again = probs.astype(bf16)
    grad_probs = jnp.einsum("gqhd,gkhd->ghqk", grad_att, values, preferred_element_type=f32)
    grad_vals = jnp.einsum("ghqk,gqhd->gkhd", probs_again, grad_att, preferred_element_type=f32)
    row_delta = jnp.sum(probs * grad_probs, axis=-1, keepdims=True)
    grad_scores = (probs * (grad_probs - row_delta)).astype(bf16)
    grad_q = (
        jnp.einsum("ghqk,gkhd->gqhd", grad_scores, key_all, preferred_element_type=f32) * q_scale
    ).reshape(near_rows, local_heads, DN + DR)
    grad_keys = (
        jnp.einsum("ghqk,gqhd->gkhd", grad_scores, q_all, preferred_element_type=f32) * q_scale
    )
    grad_kv = (
        jnp.concatenate([grad_keys[..., :DN], grad_vals], axis=-1)
        .reshape(near_rows, local_heads * (DN + DV))
        .astype(bf16)
    )
    grad_latent_part = jnp.concatenate(
        [
            contract_cols(grad_kv, kv_w),
            jnp.sum(grad_keys[..., DN:], axis=2).reshape(near_rows, DR),
        ],
        axis=1,
    )
    grad_both = sum_heads(grad_latent_part)
    latent_own = take_rows(latent[:tok_rows], own_at, half)
    cosine_own = take_rows(cosine[:tok_rows], own_at, half)
    sine_own = take_rows(sine_tab[:tok_rows], own_at, half)
    _, scale_kv = rms_forward(latent_own[:, :rank_width], latent_g.astype(f32))
    grad_c, latent_gain_grad = rms_backward(
        latent_own[:, :rank_width], scale_kv, latent_g.astype(f32), grad_both[:, :rank_width]
    )
    grad_latent = jnp.concatenate(
        [grad_c, unrotate(grad_both[:, rank_width:], cosine_own, sine_own)], axis=-1
    ).astype(bf16)
    grad_qrot = unrotate(grad_q[..., DN:], cosine[:, None, :], sine_tab[:, None, :])
    grad_queries = (
        jnp.concatenate([grad_q[..., :DN], grad_qrot], axis=-1)
        .reshape(near_rows, local_heads * (DN + DR))
        .astype(bf16)
    )
    w_query_grad = scatter_columns(contract_rows(normed_b, grad_queries), place, z)
    w_kv_grad = scatter_columns(contract_rows(compressed_b, grad_kv), place, z)
    grad_normed = sum_heads(contract_cols(grad_queries, query_w))
    grad_normed = grad_normed + contract_cols(grad_latent, latent_w)
    _, scale_own = rms_forward(x_own, gain_one.astype(f32))
    grad_x_norm, gain_one_grad = rms_backward(x_own, scale_own, gain_one.astype(f32), grad_normed)
    input_own = d_hidden + grad_x_norm
    input_grad = in_order(core, input_own, swap_cores(input_own))

    latent_near_own = jnp.stack(plane_gather(grad_latent))
    latent_near = in_order(core, latent_near_own, swap_cores(latent_near_own), axis=1)
    rows_at = place * block_rows + core * (block_rows // 2)
    normed_cols = normed_b.reshape(near_rows, deep, PLANE * block_rows)
    normed_cols = take_rows(normed_cols, rows_at, block_rows // 2, axis=2)
    latent_blocks = contract_rows(
        normed_cols.reshape(near_rows, -1), latent_near.reshape(near_rows, latent_cols)
    )
    latent_half = deep_scatter(latent_blocks.astype(bf16).reshape(deep, -1, latent_cols), z)
    w_latent_grad = in_order(core, latent_half, swap_cores(latent_half))

    gain_lanes = jnp.pad(
        latent_gain_grad.reshape(groups, kv_rows), ((0, 0), (0, block_rows - kv_rows))
    )
    vectors = jnp.concatenate(
        [
            router_grad,
            gain_one_grad[None],
            gain_two_grad[None],
            gain_lanes.reshape(1, -1),
        ],
        axis=0,
    ).reshape(-1, groups, block_rows)
    arrived = lax.all_to_all(vectors, "expert", split_axis=1, concat_axis=1, tiled=True)
    sums = jnp.sum(arrived, axis=1)
    sums = sums + swap_cores(sums)
    return (
        mixed,
        input_grad,
        sums[expert_count],
        w_query_grad,
        w_latent_grad,
        sums[expert_count + 2, :kv_rows],
        w_kv_grad,
        w_out_grad,
        sums[expert_count + 1],
        sums[:expert_count].T,
        sgu_out,
        sdown_out,
        egu_grad[None],
        edown_grad[None],
    )


def solution(mesh):
    groups = mesh.shape["expert"]
    plan = token_plan if groups <= 16 else weight_plan
    return jax.shard_map(
        plan,
        mesh=mesh,
        in_specs=(
            P("expert", None),
            P("expert"),
            P("expert", "tensor"),
            P("expert", None),
            P("expert"),
            P("expert", "tensor"),
            P("tensor", "expert"),
            P("expert"),
            P("expert", None),
            P(None, "expert", "tensor"),
            P("tensor", "expert"),
            P("expert", None, None, "tensor"),
            P("expert", "tensor", None),
            P("expert", None),
            P("expert", None),
            P("expert", None),
        ),
        out_specs=(
            P("expert", None),
            P("expert", None),
            P("expert"),
            P("expert", "tensor"),
            P("expert", None),
            P("expert"),
            P("expert", "tensor"),
            P("tensor", "expert"),
            P("expert"),
            P("expert", None),
            P(None, "expert", "tensor"),
            P("tensor", "expert"),
            P("expert", None, None, "tensor"),
            P("expert", "tensor", None),
        ),
        check_vma=False,
    )
```

```python
import jax
import jax.numpy as jnp
from jax import lax
from jax.sharding import PartitionSpec as P

DN = 128
DR = 64
DV = 128


EPSILON = 1e-06
ROUTE_SCALE = 2.446
ROPE_BASE = 50000.0
NEGATIVE = -1e30


def cut_along(value, dim, length):
    before, after = (value.shape[:dim], value.shape[dim + 1 :])
    return jnp.moveaxis(value.reshape(*before, length, -1, *after), dim, 0)


def summed_on_arrival(value, axis, dim):
    length = lax.axis_size(axis)
    tiles = lax.all_to_all(cut_along(value, dim, length), axis, 0, 0, tiled=True)
    return jnp.sum(tiles.astype(jnp.float32), axis=0)


def sent_together(arrays, axis, dim, along):
    columns = [a.reshape(*a.shape[:along], -1) for a in arrays]
    both = jnp.concatenate(columns, axis=along)
    whole, at, outs = (summed_on_arrival(both, axis, dim), 0, [])
    for a, column in zip(arrays, columns):
        slab = whole[..., at : at + column.shape[along]]
        outs.append(slab.reshape(*slab.shape[:along], *a.shape[along:]))
        at += column.shape[along]
    return tuple(outs)


def contract_rows(left_arr, right_arr):
    return lax.dot_general(
        left_arr, right_arr, (((0,), (0,)), ((), ())), preferred_element_type=jnp.float32
    )


def contract_cols(left_arr, right_arr):
    return lax.dot_general(
        left_arr, right_arr, (((1,), (1,)), ((), ())), preferred_element_type=jnp.float32
    )


def rms_forward(rows_in, gain_vec):
    inverse = lax.rsqrt(jnp.mean(rows_in * rows_in, axis=-1, keepdims=True) + EPSILON)
    return (rows_in * inverse * gain_vec, inverse)


def rms_backward(rows_in, inverse, gain_vec, grad_out):
    gain_grad = jnp.sum(grad_out * rows_in * inverse, axis=0)
    weighted = grad_out * gain_vec
    inner_mean = jnp.mean(weighted * rows_in, axis=-1, keepdims=True)
    return (inverse * weighted - rows_in * inverse * inverse * inverse * inner_mean, gain_grad)


def doc_layout(doc_lengths, row_count):
    ends_at = jnp.cumsum(doc_lengths)
    starts_at = ends_at - doc_lengths
    position = jnp.arange(row_count, dtype=jnp.int32)
    doc_ids = jnp.sum((position[:, None] >= ends_at[None, :]).astype(jnp.int32), axis=1)
    hitting = doc_ids[:, None] == jnp.arange(doc_lengths.shape[0], dtype=jnp.int32)[None, :]
    start_of = jnp.sum(jnp.where(hitting, starts_at[None, :], 0), axis=1)
    relative = position - start_of
    visible = (doc_ids[:, None] == doc_ids[None, :]) & (position[:, None] >= position[None, :])
    return (relative, visible)


def rope_tables(relative, rot_width):
    counter = jnp.arange(rot_width // 2, dtype=jnp.float32)
    frequency = ROPE_BASE ** (-2.0 * counter / rot_width)
    angles = relative.astype(jnp.float32)[:, None] * frequency[None, :]
    return (jnp.cos(angles), jnp.sin(angles))


def rotate(tensor_in, cosine, sine_tab):
    half_width = tensor_in.shape[-1] // 2
    leading = tensor_in[..., :half_width]
    trailing = tensor_in[..., half_width:]
    return jnp.concatenate(
        [leading * cosine - trailing * sine_tab, trailing * cosine + leading * sine_tab], axis=-1
    )


def unrotate(grad_in, cosine, sine_tab):
    half_width = grad_in.shape[-1] // 2
    leading = grad_in[..., :half_width]
    trailing = grad_in[..., half_width:]
    return jnp.concatenate(
        [leading * cosine + trailing * sine_tab, trailing * cosine - leading * sine_tab], axis=-1
    )


def gated_linear_backward(gate_in, up_in, grad_act):
    sigmoid_g = jax.nn.sigmoid(gate_in)
    grad_gate = grad_act * up_in * sigmoid_g * (1.0 + gate_in * (1.0 - sigmoid_g))
    return (grad_gate, grad_act * gate_in * sigmoid_g)


def slot_tables(route_rows, expert_count, capacity):
    flat_routes = route_rows.reshape(-1)
    one_hot = (flat_routes[:, None] == jnp.arange(expert_count, dtype=jnp.int32)[None, :]).astype(
        jnp.int32
    )
    ranking = jnp.sum((jnp.cumsum(one_hot, axis=0) - one_hot) * one_hot, axis=1)
    slot_ids = flat_routes * capacity + ranking
    row_total = flat_routes.shape[0]
    source = (
        jnp.zeros((expert_count * capacity,), jnp.int32)
        .at[slot_ids]
        .set(jnp.arange(row_total, dtype=jnp.int32))
    )
    filled = jnp.zeros((expert_count * capacity,), jnp.int32).at[slot_ids].set(1)
    return (slot_ids, source, filled)


def to_owner(rows_in):
    arrived = lax.all_to_all(rows_in, "expert", split_axis=0, concat_axis=1, tiled=True)
    return arrived


def weight_plan(
    inputs,
    attn_gain,
    w_query,
    w_latent,
    latent_gain,
    w_kv,
    w_out,
    ffn_gain,
    w_router,
    shared_gate_up,
    shared_down,
    expert_gate_up,
    expert_down,
    lengths,
    routes,
    cotangent,
):
    tok_rows = inputs.shape[0]
    model_width = inputs.shape[1]
    expert_count = w_router.shape[1]
    route_count = routes.shape[1]
    capacity = tok_rows * route_count * 4 // (3 * expert_count)
    brain_float16 = jnp.bfloat16
    f32 = jnp.float32
    gathered = (
        lax.all_gather(attn_gain, "expert", axis=0, tiled=True),
        lax.all_gather(w_query, "expert", axis=0, tiled=True),
        lax.all_gather(w_latent, "expert", axis=0, tiled=True),
        lax.all_gather(latent_gain, "expert", axis=0, tiled=True),
        lax.all_gather(w_kv, "expert", axis=0, tiled=True),
        lax.all_gather(w_out, "expert", axis=1, tiled=True),
        lax.all_gather(ffn_gain, "expert", axis=0, tiled=True),
        lax.all_gather(w_router, "expert", axis=0, tiled=True),
        lax.all_gather(shared_gate_up, "expert", axis=1, tiled=True),
        lax.all_gather(shared_down, "expert", axis=1, tiled=True),
    )
    gain_one, query_w, latent_w, latent_g, kv_w, out_w, gain_two, router_w, sgate_up, sdown_w = (
        gathered
    )
    local_heads = query_w.shape[1] // (DN + DR)
    rank_width = latent_g.shape[0]
    x_float = inputs.astype(f32)
    relative, visible = doc_layout(lengths[0], tok_rows)
    cosine, sine_tab = rope_tables(relative, DR)
    q_scale = (DN + DR) ** (-0.5)
    normed, scale_one = rms_forward(x_float, gain_one.astype(f32))
    normed_b = normed.astype(brain_float16)
    queries = jnp.dot(normed_b, query_w, preferred_element_type=f32).reshape(
        tok_rows, local_heads, DN + DR
    )
    q_rot = rotate(queries[..., DN:], cosine[:, None, :], sine_tab[:, None, :])
    q_all = jnp.concatenate([queries[..., :DN], q_rot], axis=-1).astype(brain_float16)
    latent = jnp.dot(normed_b, latent_w, preferred_element_type=f32)
    compressed, scale_kv = rms_forward(latent[:, :rank_width], latent_g.astype(f32))
    compressed_b = compressed.astype(brain_float16)
    k_rope = rotate(latent[:, rank_width:], cosine, sine_tab).astype(brain_float16)
    kv_all = jnp.dot(compressed_b, kv_w, preferred_element_type=f32).reshape(
        tok_rows, local_heads, DN + DV
    )
    k_nope = kv_all[..., :DN].astype(brain_float16)
    values = kv_all[..., DN:].astype(brain_float16)
    key_all = jnp.concatenate(
        [k_nope, jnp.broadcast_to(k_rope[:, None, :], (tok_rows, local_heads, DR))], axis=-1
    )

    def score_block():
        raw_scores = (
            jnp.einsum("qhd,khd->hqk", q_all, key_all, preferred_element_type=f32) * q_scale
        )
        return jnp.where(visible[None], raw_scores, NEGATIVE)

    scores = score_block()
    top_score = jnp.max(scores, axis=-1, keepdims=True)
    log_total = top_score + jnp.log(jnp.sum(jnp.exp(scores - top_score), axis=-1, keepdims=True))
    probs_b = jnp.exp(scores - log_total).astype(brain_float16)
    attended = jnp.einsum("hqk,khd->qhd", probs_b, values, preferred_element_type=f32)
    attended_b = attended.reshape(tok_rows, local_heads * DV).astype(brain_float16)
    attn = lax.psum(jnp.dot(attended_b, out_w, preferred_element_type=f32), "tensor")
    hidden = x_float + attn
    hnormed, scale_two = rms_forward(hidden, gain_two.astype(f32))
    hnormed_b = hnormed.astype(brain_float16)
    logits = jnp.dot(hnormed_b, router_w, preferred_element_type=f32)
    sigmoid_vals = jax.nn.sigmoid(logits)
    route_hot = routes[:, :, None] == jnp.arange(expert_count, dtype=jnp.int32)[None, None, :]
    chosen = jnp.sum(jnp.where(route_hot, sigmoid_vals[:, None, :], 0.0), axis=2)
    chosen_sum = jnp.sum(chosen, axis=1, keepdims=True)
    gate_vals = ROUTE_SCALE * chosen / chosen_sum
    slot_ids, source, filled = slot_tables(routes, expert_count, capacity)
    is_filled = filled[:, None] == 1
    sent_rows = jnp.where(is_filled, hnormed_b[source // route_count], 0).reshape(
        expert_count, capacity, model_width
    )
    received = to_owner(sent_rows)
    gate_up_joined = jnp.einsum(
        "erd,egdf->egrf", received, expert_gate_up, preferred_element_type=f32
    )
    expert_act = (jax.nn.silu(gate_up_joined[:, 0]) * gate_up_joined[:, 1]).astype(brain_float16)
    expert_res = jnp.einsum(
        "erf,efd->erd", expert_act, expert_down, preferred_element_type=f32
    ).astype(brain_float16)
    returned_all = lax.all_to_all(expert_res, "expert", split_axis=1, concat_axis=0, tiled=True)
    returned = returned_all.reshape(expert_count * capacity, model_width)[slot_ids].reshape(
        tok_rows, route_count, model_width
    )
    shared_gu = jnp.einsum("td,gdf->gtf", hnormed_b, sgate_up, preferred_element_type=f32)
    shared_act = (jax.nn.silu(shared_gu[0]) * shared_gu[1]).astype(brain_float16)
    branch_sum = jnp.dot(shared_act, sdown_w, preferred_element_type=f32)
    for route_idx in range(route_count):
        branch_sum = branch_sum + gate_vals[:, route_idx : route_idx + 1] * returned[
            :, route_idx
        ].astype(f32)
    moe_out = lax.psum(branch_sum.astype(jnp.bfloat16), "tensor").astype(jnp.float32)
    mixed = (hidden + moe_out).astype(brain_float16)
    grad_y = cotangent.astype(f32)
    sdown_grad = contract_rows(shared_act, cotangent)
    grad_sact = contract_cols(cotangent, sdown_w)
    grad_sgate, grad_sup = gated_linear_backward(shared_gu[0], shared_gu[1], grad_sact)
    grad_sgu = jnp.stack([grad_sgate, grad_sup], axis=0).astype(brain_float16)
    sgu_grad = jnp.einsum("td,gtf->gdf", hnormed_b, grad_sgu, preferred_element_type=f32)
    grad_hn_part = jnp.einsum("gtf,gdf->td", grad_sgu, sgate_up, preferred_element_type=f32)
    gate_columns = []
    for route_idx in range(route_count):
        gate_columns.append(jnp.sum(grad_y * returned[:, route_idx].astype(f32), axis=1))
    gate_part = jnp.stack(gate_columns, axis=1)
    slot_grads = (
        (gate_vals[:, :, None] * grad_y[:, None, :])
        .reshape(tok_rows * route_count, model_width)
        .astype(brain_float16)
    )
    grad_sent = jnp.where(is_filled, slot_grads[source], 0).reshape(
        expert_count, capacity, model_width
    )
    grad_received = to_owner(grad_sent)
    edown_grad = jnp.einsum("erf,erd->efd", expert_act, grad_received, preferred_element_type=f32)
    expert_activation_gradient = jnp.einsum(
        "erd,efd->erf", grad_received, expert_down, preferred_element_type=f32
    )
    expert_gate_gradient, expert_up_gradient = gated_linear_backward(
        gate_up_joined[:, 0], gate_up_joined[:, 1], expert_activation_gradient
    )
    expert_gate_up_gradient = jnp.stack([expert_gate_gradient, expert_up_gradient], axis=1).astype(
        brain_float16
    )
    egu_grad = jnp.einsum(
        "erd,egrf->egdf", received, expert_gate_up_gradient, preferred_element_type=f32
    )
    grad_rows = jnp.einsum(
        "egrf,egdf->erd", expert_gate_up_gradient, expert_gate_up, preferred_element_type=f32
    ).astype(brain_float16)
    grad_back = lax.all_to_all(grad_rows, "expert", split_axis=1, concat_axis=0, tiled=True)
    grad_routes = grad_back.reshape(expert_count * capacity, model_width)[slot_ids].reshape(
        tok_rows, route_count, model_width
    )
    for route_idx in range(route_count):
        grad_hn_part = grad_hn_part + grad_routes[:, route_idx].astype(f32)
    gate_grads = lax.psum(gate_part, "tensor")
    grad_chosen = ROUTE_SCALE * (
        gate_grads / chosen_sum
        - jnp.sum(gate_grads * chosen, axis=1, keepdims=True) / (chosen_sum * chosen_sum)
    )
    grad_sig = jnp.sum(jnp.where(route_hot, grad_chosen[:, :, None], 0.0), axis=1)
    grad_logits = (grad_sig * sigmoid_vals * (1.0 - sigmoid_vals)).astype(brain_float16)
    router_grad = contract_rows(hnormed_b, grad_logits)
    grad_hn = lax.psum(grad_hn_part, "tensor") + contract_cols(grad_logits, router_w)
    grad_hidden_norm, gain_two_grad = rms_backward(hidden, scale_two, gain_two.astype(f32), grad_hn)
    grad_hidden = grad_y + grad_hidden_norm
    grad_hidden_b = grad_hidden.astype(brain_float16)
    out_grad = contract_rows(attended_b, grad_hidden_b)
    grad_att = (
        contract_cols(grad_hidden_b, out_w).reshape(tok_rows, local_heads, DV).astype(brain_float16)
    )
    probs = jnp.exp(score_block() - log_total)
    probs_again = probs.astype(brain_float16)
    grad_probs = jnp.einsum("qhd,khd->hqk", grad_att, values, preferred_element_type=f32)
    grad_vals = jnp.einsum("hqk,qhd->khd", probs_again, grad_att, preferred_element_type=f32)
    row_delta = jnp.sum(probs * grad_probs, axis=-1, keepdims=True)
    grad_scores = (probs * (grad_probs - row_delta)).astype(brain_float16)
    grad_q = jnp.einsum("hqk,khd->qhd", grad_scores, key_all, preferred_element_type=f32) * q_scale
    grad_keys = jnp.einsum("hqk,qhd->khd", grad_scores, q_all, preferred_element_type=f32) * q_scale
    grad_kv = (
        jnp.concatenate([grad_keys[..., :DN], grad_vals], axis=-1)
        .reshape(tok_rows, local_heads * (DN + DV))
        .astype(brain_float16)
    )
    kv_grad = contract_rows(compressed_b, grad_kv)
    grad_comp_part = contract_cols(grad_kv, kv_w)
    grad_krope_part = jnp.sum(grad_keys[..., DN:], axis=1)
    grad_comp, grad_krope = (
        lax.psum(grad_comp_part.astype(jnp.bfloat16), "tensor").astype(jnp.float32),
        lax.psum(grad_krope_part.astype(jnp.bfloat16), "tensor").astype(jnp.float32),
    )
    grad_c, latent_gain_grad = rms_backward(
        latent[:, :rank_width], scale_kv, latent_g.astype(f32), grad_comp
    )
    grad_latent = jnp.concatenate([grad_c, unrotate(grad_krope, cosine, sine_tab)], axis=-1).astype(
        brain_float16
    )
    grad_qrot = unrotate(grad_q[..., DN:], cosine[:, None, :], sine_tab[:, None, :])
    grad_queries = (
        jnp.concatenate([grad_q[..., :DN], grad_qrot], axis=-1)
        .reshape(tok_rows, local_heads * (DN + DR))
        .astype(brain_float16)
    )
    query_grad = contract_rows(normed_b, grad_queries)
    latent_grad = contract_rows(normed_b, grad_latent)
    grad_normed = lax.psum(
        contract_cols(grad_queries, query_w).astype(jnp.bfloat16), "tensor"
    ).astype(jnp.float32) + contract_cols(grad_latent, latent_w)
    grad_x_norm, gain_one_grad = rms_backward(x_float, scale_one, gain_one.astype(f32), grad_normed)
    input_grad = grad_hidden + grad_x_norm
    first_owned = (
        *sent_together(
            (
                gain_one_grad.astype(jnp.bfloat16),
                query_grad.astype(jnp.bfloat16),
                latent_grad.astype(jnp.bfloat16),
            ),
            "expert",
            0,
            1,
        ),
        *sent_together(
            (latent_gain_grad.astype(jnp.bfloat16), kv_grad.astype(jnp.bfloat16)), "expert", 0, 1
        ),
    )
    second_owned = (
        lax.psum_scatter(out_grad, "expert", scatter_dimension=1, tiled=True),
        lax.psum_scatter(gain_two_grad, "expert", scatter_dimension=0, tiled=True),
        lax.psum_scatter(router_grad, "expert", scatter_dimension=0, tiled=True),
        lax.psum_scatter(sgu_grad, "expert", scatter_dimension=1, tiled=True),
        lax.psum_scatter(sdown_grad, "expert", scatter_dimension=1, tiled=True),
    )
    return (
        mixed,
        input_grad,
        first_owned[0],
        first_owned[1],
        first_owned[2],
        first_owned[3],
        first_owned[4],
        second_owned[0],
        second_owned[1],
        second_owned[2],
        second_owned[3],
        second_owned[4],
        egu_grad,
        edown_grad,
    )


def swap_cores(value):
    return lax.ppermute(value, "tensor", [(0, 1), (1, 0)])


def take_rows(value, start, count, axis=0):
    return lax.dynamic_slice_in_dim(value, start, count, axis=axis)


def in_order(core, own, other, axis=0):
    return jnp.where(
        core == 0,
        jnp.concatenate([own, other], axis=axis),
        jnp.concatenate([other, own], axis=axis),
    )


def add_wide(*parts):
    total = parts[0].astype(jnp.float32)
    for part in parts[1:]:
        total = total + part.astype(jnp.float32)
    return total


PLANE = 4


def to_partner(value, flips):
    groups = lax.axis_size("expert")
    return lax.ppermute(value, "expert", [(g, g ^ flips) for g in range(groups)])


def to_deeper(value, step):
    groups = lax.axis_size("expert")
    pairs = [(g, (g + step * PLANE) % groups) for g in range(groups)]
    return lax.ppermute(value, "expert", pairs)


def plane_gather(value):
    return [value] + [to_partner(value, r) for r in range(1, PLANE)]


def plane_scatter(parts):
    return add_wide(parts[0], *[to_partner(parts[r], r) for r in range(1, PLANE)])


def by_place(parts, place):
    odd, high = place % 2 == 1, place // 2 == 1
    parts = [jnp.where(odd, parts[i ^ 1], parts[i]) for i in range(PLANE)]
    return [jnp.where(high, parts[i ^ 2], parts[i]) for i in range(PLANE)]


def deep_gather(value, z):
    deep = lax.axis_size("expert") // PLANE
    whole = jnp.zeros((deep, *value.shape), value.dtype)
    whole = lax.dynamic_update_index_in_dim(whole, value, z, 0)
    for step in range(1, deep):
        came = to_deeper(value, step)
        whole = lax.dynamic_update_index_in_dim(whole, came, (z - step) % deep, 0)
    return whole


def deep_scatter(blocks, z):
    deep = blocks.shape[0]

    def block(index):
        return lax.dynamic_index_in_dim(blocks, index, 0, keepdims=False)

    return add_wide(
        block(z), *[to_deeper(block((z + step) % deep), step) for step in range(1, deep)]
    )


def gather_columns(weight, place, z):
    quarter = weight.shape[1] // PLANE
    parts = [take_rows(weight, place * quarter, quarter, axis=1)]
    for r in range(1, PLANE):
        parts.append(to_partner(take_rows(weight, (place ^ r) * quarter, quarter, axis=1), r))
    rows = jnp.concatenate(by_place(parts, place), axis=0)
    return deep_gather(rows, z).reshape(-1, quarter)


def scatter_columns(grad, place, z):
    deep = lax.axis_size("expert") // PLANE
    quarter = grad.shape[1]
    rows = deep_scatter(grad.astype(jnp.bfloat16).reshape(deep, -1, quarter), z)
    rows = rows.astype(jnp.bfloat16).reshape(PLANE, -1, quarter)

    def block(index):
        return lax.dynamic_index_in_dim(rows, index, 0, keepdims=False)

    parts = [block(place)] + [to_partner(block(place ^ r), r) for r in range(1, PLANE)]
    return jnp.concatenate(by_place(parts, place), axis=1).astype(jnp.float32)


def all_groups(value):
    return lax.all_gather(value, "expert", axis=0, tiled=False)


def at_index(value, axis, index):
    return lax.dynamic_index_in_dim(value, index, axis, keepdims=False)


def scatter_tokens(value):
    groups, rows = value.shape[:2]
    me = lax.axis_index("expert")
    z, y, x = me // PLANE, me // 2 % 2, me % 2
    deep = groups // PLANE
    blocks = value.reshape(deep, 2, 2, *value.shape[1:])
    cut = rows // 2

    def along(held, axis, mine, flips):
        sent = to_partner(at_index(held, axis, 1 - mine), flips)
        return add_wide(at_index(held, axis, mine), sent).astype(value.dtype)

    first = along(blocks[:, :, :, :cut], 1, y, 2)
    second = along(blocks[:, :, :, cut:], 2, x, 1)
    first = along(first, 1, x, 1)
    second = along(second, 1, y, 2)
    line = jnp.concatenate([first, second], axis=1)
    return deep_scatter(line, z)


def token_plan(
    inputs,
    attn_gain,
    w_query,
    w_latent,
    latent_gain,
    w_kv,
    w_out,
    ffn_gain,
    w_router,
    shared_gate_up,
    shared_down,
    expert_gate_up,
    expert_down,
    lengths,
    routes,
    cotangent,
):
    f32, bf16 = jnp.float32, jnp.bfloat16
    core, me = lax.axis_index("tensor"), lax.axis_index("expert")
    groups = lax.axis_size("expert")
    deep, place, z = groups // PLANE, me % PLANE, me // PLANE
    tok_rows, width = inputs.shape
    half = tok_rows // 2
    own_at, other_at = core * half, (1 - core) * half
    expert_count = w_router.shape[1]
    route_count = routes.shape[1]
    capacity = tok_rows * route_count * 4 // (3 * expert_count)
    shared_cols = shared_gate_up.shape[2] // groups
    latent_cols, rank_width = w_latent.shape[1], latent_gain.shape[0] * groups
    block_rows = w_query.shape[0]
    kv_rows = w_kv.shape[0]

    lengths_near = jnp.stack(plane_gather(lengths[0]))
    x_near_own = jnp.stack(plane_gather(take_rows(inputs, own_at, half)))
    x_near = in_order(core, x_near_own, swap_cores(x_near_own), axis=1)
    query_cols = w_query.shape[1] // PLANE
    out_cols = w_out.shape[0] // PLANE
    used = latent_cols + expert_count + 3
    small = jnp.concatenate(
        [
            w_latent,
            w_router,
            attn_gain[:, None],
            ffn_gain[:, None],
            jnp.pad(latent_gain, (0, block_rows - kv_rows))[:, None],
            jnp.zeros((block_rows, -used % 128), bf16),
        ],
        axis=1,
    )
    small_half = take_rows(small, core * (block_rows // 2), block_rows // 2)
    small_own = all_groups(small_half)
    small_all = in_order(core, small_own, swap_cores(small_own), axis=1)
    flat_small = small_all.reshape(groups * block_rows, -1)
    latent_w = flat_small[:, :latent_cols]
    at = latent_cols
    router_w = flat_small[:, at : at + expert_count]
    at += expert_count
    gain_one, gain_two = flat_small[:, at], flat_small[:, at + 1]
    latent_g = small_all[:, :kv_rows, at + 2].reshape(-1)
    kv_cols = w_kv.shape[1] // PLANE
    kv_parts = block_rows // kv_rows
    kv_piece = kv_cols // kv_parts
    w_out_t = w_out.T

    def quarter(index):
        kv_here = take_rows(w_kv, index * kv_cols, kv_cols, axis=1)
        kv_here = [kv_here[:, p * kv_piece : (p + 1) * kv_piece] for p in range(kv_parts)]
        return jnp.concatenate(
            [
                take_rows(w_query, index * query_cols, query_cols, axis=1),
                take_rows(w_out_t, index * out_cols, out_cols, axis=1),
                jnp.concatenate(kv_here, axis=0),
            ],
            axis=1,
        )

    near_w = [quarter(place)] + [to_partner(quarter(place ^ r), r) for r in range(1, PLANE)]
    head_w = deep_gather(jnp.stack(by_place(near_w, place)), z)
    head_w = head_w.reshape(groups, block_rows, -1)
    flat_head = head_w.reshape(groups * block_rows, -1)
    query_w = flat_head[:, :query_cols]
    out_wt = flat_head[:, query_cols : query_cols + out_cols]
    kv_w = head_w[:, :, query_cols + out_cols :].reshape(groups, kv_parts, kv_rows, kv_piece)
    kv_w = kv_w.transpose(0, 2, 1, 3).reshape(groups * kv_rows, kv_cols)
    route_sent = jnp.broadcast_to(
        routes.astype(bf16).reshape(1, -1), (groups, tok_rows * route_count)
    )
    route_all = lax.all_to_all(route_sent, "expert", split_axis=0, concat_axis=0, tiled=True)
    route_all = route_all.astype(jnp.int32).reshape(groups, tok_rows, route_count)
    sgu_w = lax.all_to_all(shared_gate_up, "expert", split_axis=2, concat_axis=1, tiled=True)
    sdown_w = lax.all_to_all(shared_down, "expert", split_axis=0, concat_axis=1, tiled=True)
    dy_own_rows = take_rows(cotangent, own_at, half)
    dy_sent, _ = lax.optimization_barrier((dy_own_rows, small_own))
    dy_own = all_groups(dy_sent)
    dy_other = swap_cores(dy_own)

    near_rows = PLANE * tok_rows
    local_heads = query_cols // (DN + DR)
    x_float = x_near.astype(f32)
    relative, visible = jax.vmap(lambda one: doc_layout(one, tok_rows))(lengths_near)
    cosine, sine_tab = rope_tables(relative.reshape(-1), DR)
    q_scale = (DN + DR) ** (-0.5)
    normed, _ = rms_forward(x_float, gain_one.astype(f32))
    normed_b = normed.astype(bf16).reshape(near_rows, width)
    queries = jnp.dot(normed_b, query_w, preferred_element_type=f32).reshape(
        near_rows, local_heads, DN + DR
    )
    q_rot = rotate(queries[..., DN:], cosine[:, None, :], sine_tab[:, None, :])
    q_all = jnp.concatenate([queries[..., :DN], q_rot], axis=-1).astype(bf16)
    q_all = q_all.reshape(PLANE, tok_rows, local_heads, DN + DR)
    latent = jnp.dot(normed_b, latent_w, preferred_element_type=f32)
    compressed, _ = rms_forward(latent[:, :rank_width], latent_g.astype(f32))
    compressed_b = compressed.astype(bf16)
    k_rope = rotate(latent[:, rank_width:], cosine, sine_tab).astype(bf16)
    kv_all = jnp.dot(compressed_b, kv_w, preferred_element_type=f32).reshape(
        PLANE, tok_rows, local_heads, DN + DV
    )
    k_nope = kv_all[..., :DN].astype(bf16)
    values = kv_all[..., DN:].astype(bf16)
    k_rope = k_rope.reshape(PLANE, tok_rows, 1, DR)
    key_all = jnp.concatenate(
        [k_nope, jnp.broadcast_to(k_rope, (PLANE, tok_rows, local_heads, DR))], axis=-1
    )

    def score_block():
        raw_scores = (
            jnp.einsum("gqhd,gkhd->ghqk", q_all, key_all, preferred_element_type=f32) * q_scale
        )
        return jnp.where(visible[:, None], raw_scores, NEGATIVE)

    scores = score_block()
    top_score = jnp.max(scores, axis=-1, keepdims=True)
    log_total = top_score + jnp.log(jnp.sum(jnp.exp(scores - top_score), axis=-1, keepdims=True))
    probs_b = jnp.exp(scores - log_total).astype(bf16)
    attended = jnp.einsum("ghqk,gkhd->gqhd", probs_b, values, preferred_element_type=f32)
    attended_b = attended.reshape(near_rows, local_heads * DV).astype(bf16)

    def sum_heads(part):
        part = part.astype(bf16).reshape(PLANE, tok_rows, -1)
        came = swap_cores(take_rows(part, other_at, half, axis=1))
        both = add_wide(take_rows(part, own_at, half, axis=1), came).astype(bf16)
        return plane_scatter([both[r] for r in range(PLANE)])

    attn_own = sum_heads(contract_cols(attended_b, out_wt))
    x_own = take_rows(inputs, own_at, half).astype(f32)
    hidden = x_own + attn_own
    hnormed, scale_two = rms_forward(hidden, gain_two.astype(f32))
    hnormed_b = hnormed.astype(bf16)
    hnormed_b, sgu_w, sdown_w, route_all = lax.optimization_barrier(
        (hnormed_b, sgu_w, sdown_w, route_all)
    )

    hn_own = all_groups(hnormed_b)
    hn_other = swap_cores(hn_own)

    def membership(named):
        one_hot = named[..., None] == jnp.arange(expert_count, dtype=jnp.int32)
        return jnp.any(named == me, axis=-1), jnp.any(one_hot, axis=2)

    member_own, hot_own = membership(take_rows(route_all, own_at, half, axis=1))
    member_other, hot_other = membership(take_rows(route_all, other_at, half, axis=1))
    lower = (
        jnp.arange(half, dtype=jnp.int32)[:, None] <= jnp.arange(half, dtype=jnp.int32)[None, :]
    ).astype(bf16)

    def running(mask):
        counts = jnp.dot(mask.astype(bf16), lower, preferred_element_type=f32)
        return counts.astype(jnp.int32)

    count_own, count_other = running(member_own), running(member_other)
    place_own = jnp.where(member_own, count_own - 1, -1)
    place_other = jnp.where(member_other, count_own[:, -1:] + count_other - 1, -1)
    slot_index = jnp.arange(capacity, dtype=jnp.int32)

    def dispatch(place):
        return (place[:, None, :] == slot_index[None, :, None]).astype(bf16)

    pick_own, pick_other = dispatch(place_own), dispatch(place_other)

    def to_slots(own, other):
        def part(pick, rows):
            return jnp.einsum("gst,gtd->gsd", pick, rows, preferred_element_type=bf16)

        return (part(pick_own, own) + part(pick_other, other)).reshape(groups * capacity, width)

    first_w = jnp.concatenate([sgu_w[0], sgu_w[1], router_w], axis=1)
    shared_w = first_w[:, : 2 * shared_cols]

    def shared_forward(rows, hot_rows, member_rows):
        flat = rows.reshape(groups * half, width)
        products = jnp.dot(flat, first_w, preferred_element_type=f32)
        gate, up = products[:, :shared_cols], products[:, shared_cols : 2 * shared_cols]
        act = (jax.nn.silu(gate) * up).astype(bf16)
        sig = jax.nn.sigmoid(products[:, 2 * shared_cols :]).reshape(groups, half, expert_count)
        total = jnp.sum(jnp.where(hot_rows, sig, 0.0), axis=-1)
        mine = jnp.sum(jnp.where(jnp.arange(expert_count) == me, sig, 0.0), axis=-1)
        gates = jnp.where(member_rows, ROUTE_SCALE * mine / total, 0.0)
        return gate, up, act, gates

    gate_own, up_own, act_own, gates_own = shared_forward(hn_own, hot_own, member_own)
    gate_other, up_other, act_other, gates_other = shared_forward(hn_other, hot_other, member_other)

    slot_rows = to_slots(hn_own, hn_other)
    slot_dy = to_slots(dy_own, dy_other)
    slot_gate = (
        jnp.sum(pick_own.astype(f32) * gates_own[:, None, :], axis=-1)
        + jnp.sum(pick_other.astype(f32) * gates_other[:, None, :], axis=-1)
    ).reshape(groups * capacity, 1)
    gate_w, up_w, down_w = expert_gate_up[0, 0], expert_gate_up[0, 1], expert_down[0]
    slot_g = jnp.dot(slot_rows, gate_w, preferred_element_type=f32)
    slot_u = jnp.dot(slot_rows, up_w, preferred_element_type=f32)
    slot_act = (jax.nn.silu(slot_g) * slot_u).astype(bf16)
    dy_float = slot_dy.astype(f32)
    slot_grad = (slot_gate * dy_float).astype(bf16)
    d_act = contract_cols(slot_grad, down_w)
    d_gate, d_up = gated_linear_backward(slot_g, slot_u, d_act)
    d_gate, d_up = d_gate.astype(bf16), d_up.astype(bf16)
    slot_drows = (contract_cols(d_gate, gate_w) + contract_cols(d_up, up_w)).astype(bf16)
    slot_drows = slot_drows.reshape(groups, capacity, width)

    def from_slots(pick, rows, left, right):
        routed = jnp.einsum("gst,gsd->gtd", pick, rows, preferred_element_type=f32)
        shared = jnp.dot(left, right, preferred_element_type=f32)
        return (routed + shared.reshape(groups, half, width)).astype(bf16)

    def shared_backward(rows_dy, gate, up):
        d_sact = contract_cols(rows_dy.reshape(groups * half, width), sdown_w)
        d_sgate, d_sup = gated_linear_backward(gate, up, d_sact)
        return jnp.concatenate([d_sgate, d_sup], axis=1).astype(bf16)

    d_shared_own = shared_backward(dy_own, gate_own, up_own)
    d_shared_other = shared_backward(dy_other, gate_other, up_other)
    shared_wt = shared_w.T
    d_rows_own = from_slots(pick_own, slot_drows, d_shared_own, shared_wt)
    d_rows_other = from_slots(pick_other, slot_drows, d_shared_other, shared_wt)
    d_rows = (d_rows_own.astype(f32) + swap_cores(d_rows_other).astype(f32)).astype(bf16)
    (d_rows, slot_act, slot_rows, slot_grad, d_gate, d_up, d_shared_own, d_shared_other) = (
        lax.optimization_barrier(
            (d_rows, slot_act, slot_rows, slot_grad, d_gate, d_up, d_shared_own, d_shared_other)
        )
    )
    d_hn = scatter_tokens(d_rows)
    slot_out = jnp.dot(slot_act, down_w, preferred_element_type=f32)
    slot_dgate = jnp.sum(slot_out * slot_dy.astype(f32), axis=-1).reshape(groups, capacity)
    slot_scaled = (slot_gate * slot_out).astype(bf16).reshape(groups, capacity, width)
    out_own = from_slots(pick_own, slot_scaled, act_own, sdown_w)
    out_other = from_slots(pick_other, slot_scaled, act_other, sdown_w)
    out_rows = (out_own.astype(f32) + swap_cores(out_other).astype(f32)).astype(bf16)
    moe_own = lax.psum_scatter(out_rows, "expert", scatter_dimension=0, tiled=False).astype(f32)
    edown_grad = contract_rows(slot_act, slot_grad)
    egu_grad = jnp.stack([contract_rows(slot_rows, d_gate), contract_rows(slot_rows, d_up)])
    mixed_own = (hidden + moe_own).astype(bf16)
    mixed = in_order(core, mixed_own, swap_cores(mixed_own))

    def flat_rows(value):
        return value.reshape(groups * half, -1)

    sgu_grad = contract_rows(flat_rows(hn_own), d_shared_own) + contract_rows(
        flat_rows(hn_other), d_shared_other
    )
    sdown_grad = contract_rows(act_own, flat_rows(dy_own)) + contract_rows(
        act_other, flat_rows(dy_other)
    )
    sgu_grad = jnp.stack([sgu_grad[:, :shared_cols], sgu_grad[:, shared_cols:]])
    sgu_out = lax.all_to_all(
        sgu_grad.astype(bf16), "expert", split_axis=1, concat_axis=2, tiled=True
    ).astype(f32)
    sdown_out = lax.all_to_all(
        sdown_grad.astype(bf16), "expert", split_axis=1, concat_axis=0, tiled=True
    ).astype(f32)

    def to_tokens(pick):
        return jnp.sum(pick.astype(f32) * slot_dgate[:, :, None], axis=1)

    dgate_sent = to_tokens(pick_own) + swap_cores(to_tokens(pick_other))
    dgate = lax.all_to_all(dgate_sent, "expert", split_axis=0, concat_axis=0, tiled=True).T
    hot_mine = take_rows(
        jnp.any(routes[..., None] == jnp.arange(expert_count, dtype=jnp.int32), axis=1), own_at, half
    )
    sig = jax.nn.sigmoid(jnp.dot(hnormed_b, router_w, preferred_element_type=f32))
    chosen = jnp.where(hot_mine, sig, 0.0)
    chosen_sum = jnp.sum(chosen, axis=1, keepdims=True)
    dgate = jnp.where(hot_mine, dgate, 0.0)
    inner = jnp.sum(dgate * chosen, axis=1, keepdims=True)
    d_chosen = ROUTE_SCALE * (dgate / chosen_sum - inner / (chosen_sum * chosen_sum))
    d_logits = (jnp.where(hot_mine, d_chosen, 0.0) * sig * (1.0 - sig)).astype(bf16)
    router_grad = contract_rows(d_logits, hnormed_b)
    d_hn = d_hn + contract_cols(d_logits, router_w)
    d_hidden_norm, gain_two_grad = rms_backward(hidden, scale_two, gain_two.astype(f32), d_hn)
    d_hidden = dy_own_rows.astype(f32) + d_hidden_norm
    d_near_own = jnp.stack(plane_gather(d_hidden.astype(bf16)))
    d_near = in_order(core, d_near_own, swap_cores(d_near_own), axis=1).reshape(near_rows, width)

    grad_att = (
        jnp.dot(d_near, out_wt, preferred_element_type=f32)
        .reshape(PLANE, tok_rows, local_heads, DV)
        .astype(bf16)
    )
    w_out_grad = scatter_columns(contract_rows(d_near, attended_b), place, z).T
    probs = jnp.exp(score_block() - log_total)
    probs_again = probs.astype(bf16)
    grad_probs = jnp.einsum("gqhd,gkhd->ghqk", grad_att, values, preferred_element_type=f32)
    grad_vals = jnp.einsum("ghqk,gqhd->gkhd", probs_again, grad_att, preferred_element_type=f32)
    row_delta = jnp.sum(probs * grad_probs, axis=-1, keepdims=True)
    grad_scores = (probs * (grad_probs - row_delta)).astype(bf16)
    grad_q = (
        jnp.einsum("ghqk,gkhd->gqhd", grad_scores, key_all, preferred_element_type=f32) * q_scale
    ).reshape(near_rows, local_heads, DN + DR)
    grad_keys = (
        jnp.einsum("ghqk,gqhd->gkhd", grad_scores, q_all, preferred_element_type=f32) * q_scale
    )
    grad_kv = (
        jnp.concatenate([grad_keys[..., :DN], grad_vals], axis=-1)
        .reshape(near_rows, local_heads * (DN + DV))
        .astype(bf16)
    )
    grad_latent_part = jnp.concatenate(
        [
            contract_cols(grad_kv, kv_w),
            jnp.sum(grad_keys[..., DN:], axis=2).reshape(near_rows, DR),
        ],
        axis=1,
    )
    grad_both = sum_heads(grad_latent_part)
    latent_own = take_rows(latent[:tok_rows], own_at, half)
    cosine_own = take_rows(cosine[:tok_rows], own_at, half)
    sine_own = take_rows(sine_tab[:tok_rows], own_at, half)
    _, scale_kv = rms_forward(latent_own[:, :rank_width], latent_g.astype(f32))
    grad_c, latent_gain_grad = rms_backward(
        latent_own[:, :rank_width], scale_kv, latent_g.astype(f32), grad_both[:, :rank_width]
    )
    grad_latent = jnp.concatenate(
        [grad_c, unrotate(grad_both[:, rank_width:], cosine_own, sine_own)], axis=-1
    ).astype(bf16)
    grad_qrot = unrotate(grad_q[..., DN:], cosine[:, None, :], sine_tab[:, None, :])
    grad_queries = (
        jnp.concatenate([grad_q[..., :DN], grad_qrot], axis=-1)
        .reshape(near_rows, local_heads * (DN + DR))
        .astype(bf16)
    )
    w_query_grad = scatter_columns(contract_rows(normed_b, grad_queries), place, z)
    w_kv_grad = scatter_columns(contract_rows(compressed_b, grad_kv), place, z)
    grad_normed = sum_heads(contract_cols(grad_queries, query_w))
    grad_normed = grad_normed + contract_cols(grad_latent, latent_w)
    _, scale_own = rms_forward(x_own, gain_one.astype(f32))
    grad_x_norm, gain_one_grad = rms_backward(x_own, scale_own, gain_one.astype(f32), grad_normed)
    input_own = d_hidden + grad_x_norm
    input_grad = in_order(core, input_own, swap_cores(input_own))

    latent_near_own = jnp.stack(plane_gather(grad_latent))
    latent_near = in_order(core, latent_near_own, swap_cores(latent_near_own), axis=1)
    rows_at = place * block_rows + core * (block_rows // 2)
    normed_cols = normed_b.reshape(near_rows, deep, PLANE * block_rows)
    normed_cols = take_rows(normed_cols, rows_at, block_rows // 2, axis=2)
    latent_blocks = contract_rows(
        normed_cols.reshape(near_rows, -1), latent_near.reshape(near_rows, latent_cols)
    )
    latent_half = deep_scatter(latent_blocks.astype(bf16).reshape(deep, -1, latent_cols), z)
    w_latent_grad = in_order(core, latent_half, swap_cores(latent_half))

    gain_lanes = jnp.pad(
        latent_gain_grad.reshape(groups, kv_rows), ((0, 0), (0, block_rows - kv_rows))
    )
    vectors = jnp.concatenate(
        [
            router_grad,
            gain_one_grad[None],
            gain_two_grad[None],
            gain_lanes.reshape(1, -1),
        ],
        axis=0,
    ).reshape(-1, groups, block_rows)
    arrived = lax.all_to_all(vectors, "expert", split_axis=1, concat_axis=1, tiled=True)
    sums = jnp.sum(arrived, axis=1)
    sums = sums + swap_cores(sums)
    return (
        mixed,
        input_grad,
        sums[expert_count],
        w_query_grad,
        w_latent_grad,
        sums[expert_count + 2, :kv_rows],
        w_kv_grad,
        w_out_grad,
        sums[expert_count + 1],
        sums[:expert_count].T,
        sgu_out,
        sdown_out,
        egu_grad[None],
        edown_grad[None],
    )


def solution(mesh):
    groups = mesh.shape["expert"]
    plan = token_plan if groups <= 16 else weight_plan
    return jax.shard_map(
        plan,
        mesh=mesh,
        in_specs=(
            P("expert", None),
            P("expert"),
            P("expert", "tensor"),
            P("expert", None),
            P("expert"),
            P("expert", "tensor"),
            P("tensor", "expert"),
            P("expert"),
            P("expert", None),
            P(None, "expert", "tensor"),
            P("tensor", "expert"),
            P("expert", None, None, "tensor"),
            P("expert", "tensor", None),
            P("expert", None),
            P("expert", None),
            P("expert", None),
        ),
        out_specs=(
            P("expert", None),
            P("expert", None),
            P("expert"),
            P("expert", "tensor"),
            P("expert", None),
            P("expert"),
            P("expert", "tensor"),
            P("tensor", "expert"),
            P("expert"),
            P("expert", None),
            P(None, "expert", "tensor"),
            P("tensor", "expert"),
            P("expert", None, None, "tensor"),
            P("expert", "tensor", None),
        ),
        check_vma=False,
    )
```

```python
import jax
import jax.numpy as jnp
from jax import lax
from jax.sharding import PartitionSpec as P

DN = 128
DR = 64
DV = 128


EPSILON = 1e-06
ROUTE_SCALE = 2.446
ROPE_BASE = 50000.0
NEGATIVE = -1e30


def cut_along(value, dim, length):
    before, after = (value.shape[:dim], value.shape[dim + 1 :])
    return jnp.moveaxis(value.reshape(*before, length, -1, *after), dim, 0)


def summed_on_arrival(value, axis, dim):
    length = lax.axis_size(axis)
    tiles = lax.all_to_all(cut_along(value, dim, length), axis, 0, 0, tiled=True)
    return jnp.sum(tiles.astype(jnp.float32), axis=0)


def sent_together(arrays, axis, dim, along):
    columns = [a.reshape(*a.shape[:along], -1) for a in arrays]
    both = jnp.concatenate(columns, axis=along)
    whole, at, outs = (summed_on_arrival(both, axis, dim), 0, [])
    for a, column in zip(arrays, columns):
        slab = whole[..., at : at + column.shape[along]]
        outs.append(slab.reshape(*slab.shape[:along], *a.shape[along:]))
        at += column.shape[along]
    return tuple(outs)


def contract_rows(left_arr, right_arr):
    return lax.dot_general(
        left_arr, right_arr, (((0,), (0,)), ((), ())), preferred_element_type=jnp.float32
    )


def contract_cols(left_arr, right_arr):
    return lax.dot_general(
        left_arr, right_arr, (((1,), (1,)), ((), ())), preferred_element_type=jnp.float32
    )


def rms_forward(rows_in, gain_vec):
    inverse = lax.rsqrt(jnp.mean(rows_in * rows_in, axis=-1, keepdims=True) + EPSILON)
    return (rows_in * inverse * gain_vec, inverse)


def rms_backward(rows_in, inverse, gain_vec, grad_out):
    gain_grad = jnp.sum(grad_out * rows_in * inverse, axis=0)
    weighted = grad_out * gain_vec
    inner_mean = jnp.mean(weighted * rows_in, axis=-1, keepdims=True)
    return (inverse * weighted - rows_in * inverse * inverse * inverse * inner_mean, gain_grad)


def doc_layout(doc_lengths, row_count):
    ends_at = jnp.cumsum(doc_lengths)
    starts_at = ends_at - doc_lengths
    position = jnp.arange(row_count, dtype=jnp.int32)
    doc_ids = jnp.sum((position[:, None] >= ends_at[None, :]).astype(jnp.int32), axis=1)
    hitting = doc_ids[:, None] == jnp.arange(doc_lengths.shape[0], dtype=jnp.int32)[None, :]
    start_of = jnp.sum(jnp.where(hitting, starts_at[None, :], 0), axis=1)
    relative = position - start_of
    visible = (doc_ids[:, None] == doc_ids[None, :]) & (position[:, None] >= position[None, :])
    return (relative, visible)


def rope_tables(relative, rot_width):
    counter = jnp.arange(rot_width // 2, dtype=jnp.float32)
    frequency = ROPE_BASE ** (-2.0 * counter / rot_width)
    angles = relative.astype(jnp.float32)[:, None] * frequency[None, :]
    return (jnp.cos(angles), jnp.sin(angles))


def rotate(tensor_in, cosine, sine_tab):
    half_width = tensor_in.shape[-1] // 2
    leading = tensor_in[..., :half_width]
    trailing = tensor_in[..., half_width:]
    return jnp.concatenate(
        [leading * cosine - trailing * sine_tab, trailing * cosine + leading * sine_tab], axis=-1
    )


def unrotate(grad_in, cosine, sine_tab):
    half_width = grad_in.shape[-1] // 2
    leading = grad_in[..., :half_width]
    trailing = grad_in[..., half_width:]
    return jnp.concatenate(
        [leading * cosine + trailing * sine_tab, trailing * cosine - leading * sine_tab], axis=-1
    )


def gated_linear_backward(gate_in, up_in, grad_act):
    sigmoid_g = jax.nn.sigmoid(gate_in)
    grad_gate = grad_act * up_in * sigmoid_g * (1.0 + gate_in * (1.0 - sigmoid_g))
    return (grad_gate, grad_act * gate_in * sigmoid_g)


def slot_tables(route_rows, expert_count, capacity):
    flat_routes = route_rows.reshape(-1)
    one_hot = (flat_routes[:, None] == jnp.arange(expert_count, dtype=jnp.int32)[None, :]).astype(
        jnp.int32
    )
    ranking = jnp.sum((jnp.cumsum(one_hot, axis=0) - one_hot) * one_hot, axis=1)
    slot_ids = flat_routes * capacity + ranking
    row_total = flat_routes.shape[0]
    source = (
        jnp.zeros((expert_count * capacity,), jnp.int32)
        .at[slot_ids]
        .set(jnp.arange(row_total, dtype=jnp.int32))
    )
    filled = jnp.zeros((expert_count * capacity,), jnp.int32).at[slot_ids].set(1)
    return (slot_ids, source, filled)


def to_owner(rows_in):
    arrived = lax.all_to_all(rows_in, "expert", split_axis=0, concat_axis=1, tiled=True)
    return arrived


def weight_plan(
    inputs,
    attn_gain,
    w_query,
    w_latent,
    latent_gain,
    w_kv,
    w_out,
    ffn_gain,
    w_router,
    shared_gate_up,
    shared_down,
    expert_gate_up,
    expert_down,
    lengths,
    routes,
    cotangent,
):
    tok_rows = inputs.shape[0]
    model_width = inputs.shape[1]
    expert_count = w_router.shape[1]
    route_count = routes.shape[1]
    capacity = tok_rows * route_count * 4 // (3 * expert_count)
    brain_float16 = jnp.bfloat16
    f32 = jnp.float32
    gathered = (
        lax.all_gather(attn_gain, "expert", axis=0, tiled=True),
        lax.all_gather(w_query, "expert", axis=0, tiled=True),
        lax.all_gather(w_latent, "expert", axis=0, tiled=True),
        lax.all_gather(latent_gain, "expert", axis=0, tiled=True),
        lax.all_gather(w_kv, "expert", axis=0, tiled=True),
        lax.all_gather(w_out, "expert", axis=1, tiled=True),
        lax.all_gather(ffn_gain, "expert", axis=0, tiled=True),
        lax.all_gather(w_router, "expert", axis=0, tiled=True),
        lax.all_gather(shared_gate_up, "expert", axis=1, tiled=True),
        lax.all_gather(shared_down, "expert", axis=1, tiled=True),
    )
    gain_one, query_w, latent_w, latent_g, kv_w, out_w, gain_two, router_w, sgate_up, sdown_w = (
        gathered
    )
    local_heads = query_w.shape[1] // (DN + DR)
    rank_width = latent_g.shape[0]
    x_float = inputs.astype(f32)
    relative, visible = doc_layout(lengths[0], tok_rows)
    cosine, sine_tab = rope_tables(relative, DR)
    q_scale = (DN + DR) ** (-0.5)
    normed, scale_one = rms_forward(x_float, gain_one.astype(f32))
    normed_b = normed.astype(brain_float16)
    queries = jnp.dot(normed_b, query_w, preferred_element_type=f32).reshape(
        tok_rows, local_heads, DN + DR
    )
    q_rot = rotate(queries[..., DN:], cosine[:, None, :], sine_tab[:, None, :])
    q_all = jnp.concatenate([queries[..., :DN], q_rot], axis=-1).astype(brain_float16)
    latent = jnp.dot(normed_b, latent_w, preferred_element_type=f32)
    compressed, scale_kv = rms_forward(latent[:, :rank_width], latent_g.astype(f32))
    compressed_b = compressed.astype(brain_float16)
    k_rope = rotate(latent[:, rank_width:], cosine, sine_tab).astype(brain_float16)
    kv_all = jnp.dot(compressed_b, kv_w, preferred_element_type=f32).reshape(
        tok_rows, local_heads, DN + DV
    )
    k_nope = kv_all[..., :DN].astype(brain_float16)
    values = kv_all[..., DN:].astype(brain_float16)
    key_all = jnp.concatenate(
        [k_nope, jnp.broadcast_to(k_rope[:, None, :], (tok_rows, local_heads, DR))], axis=-1
    )

    def score_block():
        raw_scores = (
            jnp.einsum("qhd,khd->hqk", q_all, key_all, preferred_element_type=f32) * q_scale
        )
        return jnp.where(visible[None], raw_scores, NEGATIVE)

    scores = score_block()
    top_score = jnp.max(scores, axis=-1, keepdims=True)
    log_total = top_score + jnp.log(jnp.sum(jnp.exp(scores - top_score), axis=-1, keepdims=True))
    probs_b = jnp.exp(scores - log_total).astype(brain_float16)
    attended = jnp.einsum("hqk,khd->qhd", probs_b, values, preferred_element_type=f32)
    attended_b = attended.reshape(tok_rows, local_heads * DV).astype(brain_float16)
    attn = lax.psum(jnp.dot(attended_b, out_w, preferred_element_type=f32), "tensor")
    hidden = x_float + attn
    hnormed, scale_two = rms_forward(hidden, gain_two.astype(f32))
    hnormed_b = hnormed.astype(brain_float16)
    logits = jnp.dot(hnormed_b, router_w, preferred_element_type=f32)
    sigmoid_vals = jax.nn.sigmoid(logits)
    route_hot = routes[:, :, None] == jnp.arange(expert_count, dtype=jnp.int32)[None, None, :]
    chosen = jnp.sum(jnp.where(route_hot, sigmoid_vals[:, None, :], 0.0), axis=2)
    chosen_sum = jnp.sum(chosen, axis=1, keepdims=True)
    gate_vals = ROUTE_SCALE * chosen / chosen_sum
    slot_ids, source, filled = slot_tables(routes, expert_count, capacity)
    is_filled = filled[:, None] == 1
    sent_rows = jnp.where(is_filled, hnormed_b[source // route_count], 0).reshape(
        expert_count, capacity, model_width
    )
    received = to_owner(sent_rows)
    gate_up_joined = jnp.einsum(
        "erd,egdf->egrf", received, expert_gate_up, preferred_element_type=f32
    )
    expert_act = (jax.nn.silu(gate_up_joined[:, 0]) * gate_up_joined[:, 1]).astype(brain_float16)
    expert_res = jnp.einsum(
        "erf,efd->erd", expert_act, expert_down, preferred_element_type=f32
    ).astype(brain_float16)
    returned_all = lax.all_to_all(expert_res, "expert", split_axis=1, concat_axis=0, tiled=True)
    returned = returned_all.reshape(expert_count * capacity, model_width)[slot_ids].reshape(
        tok_rows, route_count, model_width
    )
    shared_gu = jnp.einsum("td,gdf->gtf", hnormed_b, sgate_up, preferred_element_type=f32)
    shared_act = (jax.nn.silu(shared_gu[0]) * shared_gu[1]).astype(brain_float16)
    branch_sum = jnp.dot(shared_act, sdown_w, preferred_element_type=f32)
    for route_idx in range(route_count):
        branch_sum = branch_sum + gate_vals[:, route_idx : route_idx + 1] * returned[
            :, route_idx
        ].astype(f32)
    moe_out = lax.psum(branch_sum.astype(jnp.bfloat16), "tensor").astype(jnp.float32)
    mixed = (hidden + moe_out).astype(brain_float16)
    grad_y = cotangent.astype(f32)
    sdown_grad = contract_rows(shared_act, cotangent)
    grad_sact = contract_cols(cotangent, sdown_w)
    grad_sgate, grad_sup = gated_linear_backward(shared_gu[0], shared_gu[1], grad_sact)
    grad_sgu = jnp.stack([grad_sgate, grad_sup], axis=0).astype(brain_float16)
    sgu_grad = jnp.einsum("td,gtf->gdf", hnormed_b, grad_sgu, preferred_element_type=f32)
    grad_hn_part = jnp.einsum("gtf,gdf->td", grad_sgu, sgate_up, preferred_element_type=f32)
    gate_columns = []
    for route_idx in range(route_count):
        gate_columns.append(jnp.sum(grad_y * returned[:, route_idx].astype(f32), axis=1))
    gate_part = jnp.stack(gate_columns, axis=1)
    slot_grads = (
        (gate_vals[:, :, None] * grad_y[:, None, :])
        .reshape(tok_rows * route_count, model_width)
        .astype(brain_float16)
    )
    grad_sent = jnp.where(is_filled, slot_grads[source], 0).reshape(
        expert_count, capacity, model_width
    )
    grad_received = to_owner(grad_sent)
    edown_grad = jnp.einsum("erf,erd->efd", expert_act, grad_received, preferred_element_type=f32)
    expert_activation_gradient = jnp.einsum(
        "erd,efd->erf", grad_received, expert_down, preferred_element_type=f32
    )
    expert_gate_gradient, expert_up_gradient = gated_linear_backward(
        gate_up_joined[:, 0], gate_up_joined[:, 1], expert_activation_gradient
    )
    expert_gate_up_gradient = jnp.stack([expert_gate_gradient, expert_up_gradient], axis=1).astype(
        brain_float16
    )
    egu_grad = jnp.einsum(
        "erd,egrf->egdf", received, expert_gate_up_gradient, preferred_element_type=f32
    )
    grad_rows = jnp.einsum(
        "egrf,egdf->erd", expert_gate_up_gradient, expert_gate_up, preferred_element_type=f32
    ).astype(brain_float16)
    grad_back = lax.all_to_all(grad_rows, "expert", split_axis=1, concat_axis=0, tiled=True)
    grad_routes = grad_back.reshape(expert_count * capacity, model_width)[slot_ids].reshape(
        tok_rows, route_count, model_width
    )
    for route_idx in range(route_count):
        grad_hn_part = grad_hn_part + grad_routes[:, route_idx].astype(f32)
    gate_grads = lax.psum(gate_part, "tensor")
    grad_chosen = ROUTE_SCALE * (
        gate_grads / chosen_sum
        - jnp.sum(gate_grads * chosen, axis=1, keepdims=True) / (chosen_sum * chosen_sum)
    )
    grad_sig = jnp.sum(jnp.where(route_hot, grad_chosen[:, :, None], 0.0), axis=1)
    grad_logits = (grad_sig * sigmoid_vals * (1.0 - sigmoid_vals)).astype(brain_float16)
    router_grad = contract_rows(hnormed_b, grad_logits)
    grad_hn = lax.psum(grad_hn_part, "tensor") + contract_cols(grad_logits, router_w)
    grad_hidden_norm, gain_two_grad = rms_backward(hidden, scale_two, gain_two.astype(f32), grad_hn)
    grad_hidden = grad_y + grad_hidden_norm
    grad_hidden_b = grad_hidden.astype(brain_float16)
    out_grad = contract_rows(attended_b, grad_hidden_b)
    grad_att = (
        contract_cols(grad_hidden_b, out_w).reshape(tok_rows, local_heads, DV).astype(brain_float16)
    )
    probs = jnp.exp(score_block() - log_total)
    probs_again = probs.astype(brain_float16)
    grad_probs = jnp.einsum("qhd,khd->hqk", grad_att, values, preferred_element_type=f32)
    grad_vals = jnp.einsum("hqk,qhd->khd", probs_again, grad_att, preferred_element_type=f32)
    row_delta = jnp.sum(probs * grad_probs, axis=-1, keepdims=True)
    grad_scores = (probs * (grad_probs - row_delta)).astype(brain_float16)
    grad_q = jnp.einsum("hqk,khd->qhd", grad_scores, key_all, preferred_element_type=f32) * q_scale
    grad_keys = jnp.einsum("hqk,qhd->khd", grad_scores, q_all, preferred_element_type=f32) * q_scale
    grad_kv = (
        jnp.concatenate([grad_keys[..., :DN], grad_vals], axis=-1)
        .reshape(tok_rows, local_heads * (DN + DV))
        .astype(brain_float16)
    )
    kv_grad = contract_rows(compressed_b, grad_kv)
    grad_comp_part = contract_cols(grad_kv, kv_w)
    grad_krope_part = jnp.sum(grad_keys[..., DN:], axis=1)
    grad_comp, grad_krope = (
        lax.psum(grad_comp_part.astype(jnp.bfloat16), "tensor").astype(jnp.float32),
        lax.psum(grad_krope_part.astype(jnp.bfloat16), "tensor").astype(jnp.float32),
    )
    grad_c, latent_gain_grad = rms_backward(
        latent[:, :rank_width], scale_kv, latent_g.astype(f32), grad_comp
    )
    grad_latent = jnp.concatenate([grad_c, unrotate(grad_krope, cosine, sine_tab)], axis=-1).astype(
        brain_float16
    )
    grad_qrot = unrotate(grad_q[..., DN:], cosine[:, None, :], sine_tab[:, None, :])
    grad_queries = (
        jnp.concatenate([grad_q[..., :DN], grad_qrot], axis=-1)
        .reshape(tok_rows, local_heads * (DN + DR))
        .astype(brain_float16)
    )
    query_grad = contract_rows(normed_b, grad_queries)
    latent_grad = contract_rows(normed_b, grad_latent)
    grad_normed = lax.psum(
        contract_cols(grad_queries, query_w).astype(jnp.bfloat16), "tensor"
    ).astype(jnp.float32) + contract_cols(grad_latent, latent_w)
    grad_x_norm, gain_one_grad = rms_backward(x_float, scale_one, gain_one.astype(f32), grad_normed)
    input_grad = grad_hidden + grad_x_norm
    first_owned = (
        *sent_together(
            (
                gain_one_grad.astype(jnp.bfloat16),
                query_grad.astype(jnp.bfloat16),
                latent_grad.astype(jnp.bfloat16),
            ),
            "expert",
            0,
            1,
        ),
        *sent_together(
            (latent_gain_grad.astype(jnp.bfloat16), kv_grad.astype(jnp.bfloat16)), "expert", 0, 1
        ),
    )
    second_owned = (
        lax.psum_scatter(out_grad, "expert", scatter_dimension=1, tiled=True),
        lax.psum_scatter(gain_two_grad, "expert", scatter_dimension=0, tiled=True),
        lax.psum_scatter(router_grad, "expert", scatter_dimension=0, tiled=True),
        lax.psum_scatter(sgu_grad, "expert", scatter_dimension=1, tiled=True),
        lax.psum_scatter(sdown_grad, "expert", scatter_dimension=1, tiled=True),
    )
    return (
        mixed,
        input_grad,
        first_owned[0],
        first_owned[1],
        first_owned[2],
        first_owned[3],
        first_owned[4],
        second_owned[0],
        second_owned[1],
        second_owned[2],
        second_owned[3],
        second_owned[4],
        egu_grad,
        edown_grad,
    )


def swap_cores(value):
    return lax.ppermute(value, "tensor", [(0, 1), (1, 0)])


def take_rows(value, start, count, axis=0):
    return lax.dynamic_slice_in_dim(value, start, count, axis=axis)


def in_order(core, own, other, axis=0):
    return jnp.where(
        core == 0,
        jnp.concatenate([own, other], axis=axis),
        jnp.concatenate([other, own], axis=axis),
    )


def add_wide(*parts):
    total = parts[0].astype(jnp.float32)
    for part in parts[1:]:
        total = total + part.astype(jnp.float32)
    return total


PLANE = 4


def to_partner(value, flips):
    groups = lax.axis_size("expert")
    return lax.ppermute(value, "expert", [(g, g ^ flips) for g in range(groups)])


def to_deeper(value, step):
    groups = lax.axis_size("expert")
    pairs = [(g, (g + step * PLANE) % groups) for g in range(groups)]
    return lax.ppermute(value, "expert", pairs)


def plane_gather(value):
    return [value] + [to_partner(value, r) for r in range(1, PLANE)]


def plane_scatter(parts):
    return add_wide(parts[0], *[to_partner(parts[r], r) for r in range(1, PLANE)])


def by_place(parts, place):
    odd, high = place % 2 == 1, place // 2 == 1
    parts = [jnp.where(odd, parts[i ^ 1], parts[i]) for i in range(PLANE)]
    return [jnp.where(high, parts[i ^ 2], parts[i]) for i in range(PLANE)]


def deep_gather(value, z):
    deep = lax.axis_size("expert") // PLANE
    whole = jnp.zeros((deep, *value.shape), value.dtype)
    whole = lax.dynamic_update_index_in_dim(whole, value, z, 0)
    for step in range(1, deep):
        came = to_deeper(value, step)
        whole = lax.dynamic_update_index_in_dim(whole, came, (z - step) % deep, 0)
    return whole


def deep_scatter(blocks, z):
    deep = blocks.shape[0]

    def block(index):
        return lax.dynamic_index_in_dim(blocks, index, 0, keepdims=False)

    return add_wide(
        block(z), *[to_deeper(block((z + step) % deep), step) for step in range(1, deep)]
    )


def sum_planes(grad, z):
    deep = lax.axis_size("expert") // PLANE
    rows = deep_scatter(grad.astype(jnp.bfloat16).reshape(deep, -1, grad.shape[1]), z)
    return rows.astype(jnp.bfloat16).reshape(PLANE, -1, grad.shape[1])


def share_columns(rows, place):
    parts = [at_index(rows, 0, place)]
    for r in range(1, PLANE):
        parts.append(to_partner(at_index(rows, 0, place ^ r), r))
    return by_place(parts, place)


def all_groups(value):
    return lax.all_gather(value, "expert", axis=0, tiled=False)


def at_index(value, axis, index):
    return lax.dynamic_index_in_dim(value, index, axis, keepdims=False)


def scatter_tokens(value):
    groups, rows = value.shape[:2]
    me = lax.axis_index("expert")
    z, y, x = me // PLANE, me // 2 % 2, me % 2
    deep = groups // PLANE
    blocks = value.reshape(deep, 2, 2, *value.shape[1:])
    cut = rows // 2

    def along(held, axis, mine, flips):
        sent = to_partner(at_index(held, axis, 1 - mine), flips)
        return add_wide(at_index(held, axis, mine), sent).astype(value.dtype)

    first = along(blocks[:, :, :, :cut], 1, y, 2)
    second = along(blocks[:, :, :, cut:], 2, x, 1)
    first = along(first, 1, x, 1)
    second = along(second, 1, y, 2)
    line = jnp.concatenate([first, second], axis=1)
    return deep_scatter(line, z)


def token_plan(
    inputs,
    attn_gain,
    w_query,
    w_latent,
    latent_gain,
    w_kv,
    w_out,
    ffn_gain,
    w_router,
    shared_gate_up,
    shared_down,
    expert_gate_up,
    expert_down,
    lengths,
    routes,
    cotangent,
):
    f32, bf16 = jnp.float32, jnp.bfloat16
    core, me = lax.axis_index("tensor"), lax.axis_index("expert")
    groups = lax.axis_size("expert")
    deep, place, z = groups // PLANE, me % PLANE, me // PLANE
    tok_rows, width = inputs.shape
    half = tok_rows // 2
    own_at, other_at = core * half, (1 - core) * half
    expert_count = w_router.shape[1]
    route_count = routes.shape[1]
    capacity = tok_rows * route_count * 4 // (3 * expert_count)
    shared_cols = shared_gate_up.shape[2] // groups
    latent_cols, rank_width = w_latent.shape[1], latent_gain.shape[0] * groups
    block_rows = w_query.shape[0]
    kv_rows = w_kv.shape[0]

    query_cols = w_query.shape[1] // PLANE
    out_cols = w_out.shape[0] // PLANE
    used = latent_cols + expert_count + 3
    small = jnp.concatenate(
        [
            w_latent,
            w_router,
            attn_gain[:, None],
            ffn_gain[:, None],
            jnp.pad(latent_gain, (0, block_rows - kv_rows))[:, None],
            jnp.zeros((block_rows, -used % 128), bf16),
        ],
        axis=1,
    )
    route_half = take_rows(routes, own_at, half).astype(bf16).reshape(block_rows // 2, -1)
    small_half = jnp.concatenate(
        [
            take_rows(small, core * (block_rows // 2), block_rows // 2),
            jnp.pad(route_half, ((0, 0), (0, -route_half.shape[1] % 128))),
        ],
        axis=1,
    )
    small_own = all_groups(small_half)
    small_other = swap_cores(small_own)
    small_cols = small.shape[1]
    small_all = in_order(core, small_own, small_other, axis=1)

    def routes_of(came):
        came = came[:, :, small_cols : small_cols + route_half.shape[1]]
        return came.astype(jnp.int32).reshape(groups, half, route_count)

    routes_own, routes_other = routes_of(small_own), routes_of(small_other)
    flat_small = small_all.reshape(groups * block_rows, -1)
    latent_w = flat_small[:, :latent_cols]
    at = latent_cols
    router_w = flat_small[:, at : at + expert_count]
    at += expert_count
    gain_one, gain_two = flat_small[:, at], flat_small[:, at + 1]
    latent_g = small_all[:, :kv_rows, at + 2].reshape(-1)
    kv_cols = w_kv.shape[1] // PLANE
    kv_parts = block_rows // kv_rows
    kv_piece = kv_cols // kv_parts
    w_out_t = w_out.T

    def quarter(index):
        kv_here = take_rows(w_kv, index * kv_cols, kv_cols, axis=1)
        kv_here = [kv_here[:, p * kv_piece : (p + 1) * kv_piece] for p in range(kv_parts)]
        return jnp.concatenate(
            [
                take_rows(w_query, index * query_cols, query_cols, axis=1),
                take_rows(w_out_t, index * out_cols, out_cols, axis=1),
                jnp.concatenate(kv_here, axis=0),
            ],
            axis=1,
        )

    near_w = [quarter(place)] + [to_partner(quarter(place ^ r), r) for r in range(1, PLANE)]
    x_half, lengths_here, near_w = lax.optimization_barrier(
        (take_rows(inputs, own_at, half), lengths[0], near_w)
    )
    lengths_near = jnp.stack(plane_gather(lengths_here))
    x_near_own = jnp.stack(plane_gather(x_half))
    x_near = in_order(core, x_near_own, swap_cores(x_near_own), axis=1)
    x_near = lax.optimization_barrier(x_near.reshape(PLANE * tok_rows, width))
    head_w = deep_gather(jnp.stack(by_place(near_w, place)), z)
    head_w = head_w.reshape(groups, block_rows, -1)
    flat_head = head_w.reshape(groups * block_rows, -1)
    query_w = flat_head[:, :query_cols]
    out_wt = flat_head[:, query_cols : query_cols + out_cols]
    kv_w = head_w[:, :, query_cols + out_cols :].reshape(groups, kv_parts, kv_rows, kv_piece)
    kv_w = kv_w.transpose(0, 2, 1, 3).reshape(groups * kv_rows, kv_cols)
    sgu_w = lax.all_to_all(shared_gate_up, "expert", split_axis=2, concat_axis=1, tiled=True)
    sdown_w = lax.all_to_all(shared_down, "expert", split_axis=0, concat_axis=1, tiled=True)
    dy_own_rows = take_rows(cotangent, own_at, half)
    dy_sent, small_own = lax.optimization_barrier((dy_own_rows, small_own))
    dy_own = all_groups(dy_sent)
    dy_other = swap_cores(dy_own)

    near_rows = PLANE * tok_rows
    local_heads = query_cols // (DN + DR)
    x_float = x_near.astype(f32)
    relative, visible = jax.vmap(lambda one: doc_layout(one, tok_rows))(lengths_near)
    cosine, sine_tab = rope_tables(relative.reshape(-1), DR)
    q_scale = (DN + DR) ** (-0.5)
    scale_one = lax.rsqrt(jnp.mean(x_float * x_float, axis=-1, keepdims=True) + EPSILON)
    scale_one = lax.optimization_barrier(scale_one)
    normed_b = (x_near.astype(f32) * scale_one * gain_one.astype(f32)).astype(bf16)
    normed_b = lax.optimization_barrier(normed_b)
    queries = jnp.dot(normed_b, query_w, preferred_element_type=f32).reshape(
        near_rows, local_heads, DN + DR
    )
    q_rot = rotate(queries[..., DN:], cosine[:, None, :], sine_tab[:, None, :])
    q_all = jnp.concatenate([queries[..., :DN], q_rot], axis=-1).astype(bf16)
    q_all = q_all.reshape(PLANE, tok_rows, local_heads, DN + DR)
    latent = jnp.dot(normed_b, latent_w, preferred_element_type=f32)
    compressed, _ = rms_forward(latent[:, :rank_width], latent_g.astype(f32))
    compressed_b = compressed.astype(bf16)
    k_rope = rotate(latent[:, rank_width:], cosine, sine_tab).astype(bf16)
    kv_all = jnp.dot(compressed_b, kv_w, preferred_element_type=f32).reshape(
        PLANE, tok_rows, local_heads, DN + DV
    )
    k_nope = kv_all[..., :DN].astype(bf16)
    values = kv_all[..., DN:].astype(bf16)
    k_rope = k_rope.reshape(PLANE, tok_rows, 1, DR)
    key_all = jnp.concatenate(
        [k_nope, jnp.broadcast_to(k_rope, (PLANE, tok_rows, local_heads, DR))], axis=-1
    )

    def score_block():
        raw_scores = (
            jnp.einsum("gqhd,gkhd->ghqk", q_all, key_all, preferred_element_type=f32) * q_scale
        )
        return jnp.where(visible[:, None], raw_scores, NEGATIVE)

    scores = score_block()
    top_score = jnp.max(scores, axis=-1, keepdims=True)
    log_total = top_score + jnp.log(jnp.sum(jnp.exp(scores - top_score), axis=-1, keepdims=True))
    probs_b = jnp.exp(scores - log_total).astype(bf16)
    attended = jnp.einsum("ghqk,gkhd->gqhd", probs_b, values, preferred_element_type=f32)
    attended_b = attended.reshape(near_rows, local_heads * DV).astype(bf16)
    attended_b, sgu_w, sdown_w = lax.optimization_barrier((attended_b, sgu_w, sdown_w))

    def sum_heads(part):
        part = part.astype(bf16).reshape(PLANE, tok_rows, -1)
        came = swap_cores(take_rows(part, other_at, half, axis=1))
        both = add_wide(take_rows(part, own_at, half, axis=1), came).astype(bf16)
        return plane_scatter([both[r] for r in range(PLANE)])

    attn_own = sum_heads(contract_cols(attended_b, out_wt))
    x_own = take_rows(inputs, own_at, half).astype(f32)
    hidden = x_own + attn_own
    hnormed, scale_two = rms_forward(hidden, gain_two.astype(f32))
    hnormed_b = hnormed.astype(bf16)
    hnormed_b, dy_own, dy_other = lax.optimization_barrier((hnormed_b, dy_own, dy_other))

    hn_own = all_groups(hnormed_b)
    hn_other = swap_cores(hn_own)

    def membership(named):
        one_hot = named[..., None] == jnp.arange(expert_count, dtype=jnp.int32)
        return jnp.any(named == me, axis=-1), jnp.any(one_hot, axis=2)

    member_own, hot_own = membership(routes_own)
    member_other, hot_other = membership(routes_other)
    lower = (
        jnp.arange(half, dtype=jnp.int32)[:, None] <= jnp.arange(half, dtype=jnp.int32)[None, :]
    ).astype(bf16)

    def running(mask):
        counts = jnp.dot(mask.astype(bf16), lower, preferred_element_type=f32)
        return counts.astype(jnp.int32)

    count_own, count_other = running(member_own), running(member_other)
    place_own = jnp.where(member_own, count_own - 1, -1)
    place_other = jnp.where(member_other, count_own[:, -1:] + count_other - 1, -1)
    slot_index = jnp.arange(capacity, dtype=jnp.int32)

    def dispatch(place):
        return (place[:, None, :] == slot_index[None, :, None]).astype(bf16)

    pick_own, pick_other = dispatch(place_own), dispatch(place_other)

    def to_slots(own, other):
        def part(pick, rows):
            return jnp.einsum("gst,gtd->gsd", pick, rows, preferred_element_type=bf16)

        return (part(pick_own, own) + part(pick_other, other)).reshape(groups * capacity, width)

    first_w = jnp.concatenate([sgu_w[0], sgu_w[1], router_w], axis=1)
    shared_w = first_w[:, : 2 * shared_cols]

    def shared_forward(rows, hot_rows, member_rows):
        flat = rows.reshape(groups * half, width)
        products = jnp.dot(flat, first_w, preferred_element_type=f32)
        gate, up = products[:, :shared_cols], products[:, shared_cols : 2 * shared_cols]
        act = (jax.nn.silu(gate) * up).astype(bf16)
        sig = jax.nn.sigmoid(products[:, 2 * shared_cols :]).reshape(groups, half, expert_count)
        total = jnp.sum(jnp.where(hot_rows, sig, 0.0), axis=-1)
        mine = jnp.sum(jnp.where(jnp.arange(expert_count) == me, sig, 0.0), axis=-1)
        gates = jnp.where(member_rows, ROUTE_SCALE * mine / total, 0.0)
        return gate, up, act, gates

    gate_own, up_own, act_own, gates_own = shared_forward(hn_own, hot_own, member_own)
    gate_other, up_other, act_other, gates_other = shared_forward(hn_other, hot_other, member_other)

    slot_rows = to_slots(hn_own, hn_other)
    slot_dy = to_slots(dy_own, dy_other)
    slot_gate = (
        jnp.sum(pick_own.astype(f32) * gates_own[:, None, :], axis=-1)
        + jnp.sum(pick_other.astype(f32) * gates_other[:, None, :], axis=-1)
    ).reshape(groups * capacity, 1)
    gate_w, up_w, down_w = expert_gate_up[0, 0], expert_gate_up[0, 1], expert_down[0]
    slot_g = jnp.dot(slot_rows, gate_w, preferred_element_type=f32)
    slot_u = jnp.dot(slot_rows, up_w, preferred_element_type=f32)
    slot_act = (jax.nn.silu(slot_g) * slot_u).astype(bf16)
    dy_float = slot_dy.astype(f32)
    slot_grad = (slot_gate * dy_float).astype(bf16)
    d_act = contract_cols(slot_grad, down_w)
    d_gate, d_up = gated_linear_backward(slot_g, slot_u, d_act)
    d_gate, d_up = d_gate.astype(bf16), d_up.astype(bf16)
    slot_drows = (contract_cols(d_gate, gate_w) + contract_cols(d_up, up_w)).astype(bf16)
    slot_drows = slot_drows.reshape(groups, capacity, width)

    def from_slots(pick, rows, left, right):
        routed = jnp.einsum("gst,gsd->gtd", pick, rows, preferred_element_type=f32)
        shared = jnp.dot(left, right, preferred_element_type=f32)
        return (routed + shared.reshape(groups, half, width)).astype(bf16)

    def shared_backward(rows_dy, gate, up):
        d_sact = contract_cols(rows_dy.reshape(groups * half, width), sdown_w)
        d_sgate, d_sup = gated_linear_backward(gate, up, d_sact)
        return jnp.concatenate([d_sgate, d_sup], axis=1).astype(bf16)

    d_shared_own = shared_backward(dy_own, gate_own, up_own)
    d_shared_other = shared_backward(dy_other, gate_other, up_other)
    shared_wt = shared_w.T
    d_rows_own = from_slots(pick_own, slot_drows, d_shared_own, shared_wt)
    d_rows_other = from_slots(pick_other, slot_drows, d_shared_other, shared_wt)
    d_rows = (d_rows_own.astype(f32) + swap_cores(d_rows_other).astype(f32)).astype(bf16)
    (d_rows, slot_act, slot_rows, slot_grad, d_gate, d_up, d_shared_own, d_shared_other) = (
        lax.optimization_barrier(
            (d_rows, slot_act, slot_rows, slot_grad, d_gate, d_up, d_shared_own, d_shared_other)
        )
    )
    d_hn = scatter_tokens(d_rows)
    slot_out = jnp.dot(slot_act, down_w, preferred_element_type=f32)
    slot_dgate = jnp.sum(slot_out * slot_dy.astype(f32), axis=-1).reshape(groups, capacity)
    slot_scaled = (slot_gate * slot_out).astype(bf16).reshape(groups, capacity, width)
    out_own = from_slots(pick_own, slot_scaled, act_own, sdown_w)
    out_other = from_slots(pick_other, slot_scaled, act_other, sdown_w)
    out_rows = (out_own.astype(f32) + swap_cores(out_other).astype(f32)).astype(bf16)
    moe_own = lax.psum_scatter(out_rows, "expert", scatter_dimension=0, tiled=False).astype(f32)
    edown_grad = contract_rows(slot_act, slot_grad)
    egu_grad = jnp.stack([contract_rows(slot_rows, d_gate), contract_rows(slot_rows, d_up)])
    mixed_own = (hidden + moe_own).astype(bf16)
    mixed = in_order(core, mixed_own, swap_cores(mixed_own))

    def flat_rows(value):
        return value.reshape(groups * half, -1)

    sgu_grad = contract_rows(flat_rows(hn_own), d_shared_own) + contract_rows(
        flat_rows(hn_other), d_shared_other
    )
    sdown_grad = contract_rows(act_own, flat_rows(dy_own)) + contract_rows(
        act_other, flat_rows(dy_other)
    )
    sgu_grad = jnp.stack([sgu_grad[:, :shared_cols], sgu_grad[:, shared_cols:]])
    sgu_out = lax.all_to_all(
        sgu_grad.astype(bf16), "expert", split_axis=1, concat_axis=2, tiled=True
    ).astype(f32)
    sdown_out = lax.all_to_all(
        sdown_grad.astype(bf16), "expert", split_axis=1, concat_axis=0, tiled=True
    ).astype(f32)

    def to_tokens(pick):
        return jnp.sum(pick.astype(f32) * slot_dgate[:, :, None], axis=1)

    dgate_sent = to_tokens(pick_own) + swap_cores(to_tokens(pick_other))
    dgate = lax.all_to_all(dgate_sent, "expert", split_axis=0, concat_axis=0, tiled=True).T
    hot_mine = take_rows(
        jnp.any(routes[..., None] == jnp.arange(expert_count, dtype=jnp.int32), axis=1), own_at, half
    )
    sig = jax.nn.sigmoid(jnp.dot(hnormed_b, router_w, preferred_element_type=f32))
    chosen = jnp.where(hot_mine, sig, 0.0)
    chosen_sum = jnp.sum(chosen, axis=1, keepdims=True)
    dgate = jnp.where(hot_mine, dgate, 0.0)
    inner = jnp.sum(dgate * chosen, axis=1, keepdims=True)
    d_chosen = ROUTE_SCALE * (dgate / chosen_sum - inner / (chosen_sum * chosen_sum))
    d_logits = (jnp.where(hot_mine, d_chosen, 0.0) * sig * (1.0 - sig)).astype(bf16)
    router_grad = contract_rows(d_logits, hnormed_b)
    d_hn = d_hn + contract_cols(d_logits, router_w)
    d_hidden_norm, gain_two_grad = rms_backward(hidden, scale_two, gain_two.astype(f32), d_hn)
    d_hidden = dy_own_rows.astype(f32) + d_hidden_norm
    d_near_own = jnp.stack(plane_gather(d_hidden.astype(bf16)))
    d_near = in_order(core, d_near_own, swap_cores(d_near_own), axis=1).reshape(near_rows, width)

    grad_att = (
        jnp.dot(d_near, out_wt, preferred_element_type=f32)
        .reshape(PLANE, tok_rows, local_heads, DV)
        .astype(bf16)
    )
    out_sums = sum_planes(contract_rows(d_near, attended_b), z)
    probs = jnp.exp(score_block() - log_total)
    probs_again = probs.astype(bf16)
    grad_probs = jnp.einsum("gqhd,gkhd->ghqk", grad_att, values, preferred_element_type=f32)
    grad_vals = jnp.einsum("ghqk,gqhd->gkhd", probs_again, grad_att, preferred_element_type=f32)
    row_delta = jnp.sum(probs * grad_probs, axis=-1, keepdims=True)
    grad_scores = (probs * (grad_probs - row_delta)).astype(bf16)
    grad_q = (
        jnp.einsum("ghqk,gkhd->gqhd", grad_scores, key_all, preferred_element_type=f32) * q_scale
    ).reshape(near_rows, local_heads, DN + DR)
    grad_keys = (
        jnp.einsum("ghqk,gqhd->gkhd", grad_scores, q_all, preferred_element_type=f32) * q_scale
    )
    grad_kv = (
        jnp.concatenate([grad_keys[..., :DN], grad_vals], axis=-1)
        .reshape(near_rows, local_heads * (DN + DV))
        .astype(bf16)
    )
    grad_latent_part = jnp.concatenate(
        [
            contract_cols(grad_kv, kv_w),
            jnp.sum(grad_keys[..., DN:], axis=2).reshape(near_rows, DR),
        ],
        axis=1,
    )
    grad_both = sum_heads(grad_latent_part)
    latent_own = take_rows(latent[:tok_rows], own_at, half)
    cosine_own = take_rows(cosine[:tok_rows], own_at, half)
    sine_own = take_rows(sine_tab[:tok_rows], own_at, half)
    _, scale_kv = rms_forward(latent_own[:, :rank_width], latent_g.astype(f32))
    grad_c, latent_gain_grad = rms_backward(
        latent_own[:, :rank_width], scale_kv, latent_g.astype(f32), grad_both[:, :rank_width]
    )
    grad_latent = jnp.concatenate(
        [grad_c, unrotate(grad_both[:, rank_width:], cosine_own, sine_own)], axis=-1
    ).astype(bf16)
    grad_qrot = unrotate(grad_q[..., DN:], cosine[:, None, :], sine_tab[:, None, :])
    grad_queries = (
        jnp.concatenate([grad_q[..., :DN], grad_qrot], axis=-1)
        .reshape(near_rows, local_heads * (DN + DR))
        .astype(bf16)
    )
    kv_grad = contract_rows(compressed_b, grad_kv).astype(bf16)
    kv_grad = kv_grad.reshape(groups, kv_rows, kv_parts, kv_piece).transpose(0, 2, 1, 3)
    query_grad = contract_rows(normed_b, grad_queries).astype(bf16)
    first_sums = sum_planes(
        jnp.concatenate([query_grad, kv_grad.reshape(-1, kv_piece)], axis=1), z
    )
    shared_out = share_columns(jnp.concatenate([first_sums, out_sums], axis=2), place)
    at_kv, at_out = query_cols, query_cols + kv_piece
    w_query_grad = jnp.concatenate([p[:, :at_kv] for p in shared_out], axis=1).astype(f32)
    w_kv_grad = jnp.concatenate(
        [
            p[q * kv_rows : (q + 1) * kv_rows, at_kv:at_out]
            for p in shared_out
            for q in range(kv_parts)
        ],
        axis=1,
    ).astype(f32)
    w_out_grad = jnp.concatenate([p[:, at_out:] for p in shared_out], axis=1).astype(f32).T
    grad_normed = sum_heads(contract_cols(grad_queries, query_w))
    grad_normed = grad_normed + contract_cols(grad_latent, latent_w)
    _, scale_own = rms_forward(x_own, gain_one.astype(f32))
    grad_x_norm, gain_one_grad = rms_backward(x_own, scale_own, gain_one.astype(f32), grad_normed)
    input_own = d_hidden + grad_x_norm
    input_grad = in_order(core, input_own, swap_cores(input_own))

    latent_near_own = jnp.stack(plane_gather(grad_latent))
    latent_near = in_order(core, latent_near_own, swap_cores(latent_near_own), axis=1)
    rows_at = place * block_rows + core * (block_rows // 2)
    normed_cols = normed_b.reshape(near_rows, deep, PLANE * block_rows)
    normed_cols = take_rows(normed_cols, rows_at, block_rows // 2, axis=2)
    latent_blocks = contract_rows(
        normed_cols.reshape(near_rows, -1), latent_near.reshape(near_rows, latent_cols)
    )
    latent_half = deep_scatter(latent_blocks.astype(bf16).reshape(deep, -1, latent_cols), z)
    w_latent_grad = in_order(core, latent_half, swap_cores(latent_half))

    gain_lanes = jnp.pad(
        latent_gain_grad.reshape(groups, kv_rows), ((0, 0), (0, block_rows - kv_rows))
    )
    vectors = jnp.concatenate(
        [
            router_grad,
            gain_one_grad[None],
            gain_two_grad[None],
            gain_lanes.reshape(1, -1),
        ],
        axis=0,
    ).reshape(-1, groups, block_rows)
    arrived = lax.all_to_all(vectors, "expert", split_axis=1, concat_axis=1, tiled=True)
    sums = jnp.sum(arrived, axis=1)
    sums = sums + swap_cores(sums)
    return (
        mixed,
        input_grad,
        sums[expert_count],
        w_query_grad,
        w_latent_grad,
        sums[expert_count + 2, :kv_rows],
        w_kv_grad,
        w_out_grad,
        sums[expert_count + 1],
        sums[:expert_count].T,
        sgu_out,
        sdown_out,
        egu_grad[None],
        edown_grad[None],
    )


def solution(mesh):
    groups = mesh.shape["expert"]
    plan = token_plan if groups <= 16 else weight_plan
    return jax.shard_map(
        plan,
        mesh=mesh,
        in_specs=(
            P("expert", None),
            P("expert"),
            P("expert", "tensor"),
            P("expert", None),
            P("expert"),
            P("expert", "tensor"),
            P("tensor", "expert"),
            P("expert"),
            P("expert", None),
            P(None, "expert", "tensor"),
            P("tensor", "expert"),
            P("expert", None, None, "tensor"),
            P("expert", "tensor", None),
            P("expert", None),
            P("expert", None),
            P("expert", None),
        ),
        out_specs=(
            P("expert", None),
            P("expert", None),
            P("expert"),
            P("expert", "tensor"),
            P("expert", None),
            P("expert"),
            P("expert", "tensor"),
            P("tensor", "expert"),
            P("expert"),
            P("expert", None),
            P(None, "expert", "tensor"),
            P("tensor", "expert"),
            P("expert", None, None, "tensor"),
            P("expert", "tensor", None),
        ),
        check_vma=False,
    )
```

```python
import functools

import jax
import jax.numpy as jnp
from jax import lax
from jax.experimental import pallas as pl
from jax.experimental.pallas import tpu as pltpu
from jax.sharding import PartitionSpec as P

DN = 128
DR = 64
DV = 128
LANES = 128


EPSILON = 1e-06
ROUTE_SCALE = 2.446
ROPE_BASE = 50000.0
NEGATIVE = -1e30


def cut_along(value, dim, length):
    before, after = (value.shape[:dim], value.shape[dim + 1 :])
    return jnp.moveaxis(value.reshape(*before, length, -1, *after), dim, 0)


def summed_on_arrival(value, axis, dim):
    length = lax.axis_size(axis)
    tiles = lax.all_to_all(cut_along(value, dim, length), axis, 0, 0, tiled=True)
    return jnp.sum(tiles.astype(jnp.float32), axis=0)


def sent_together(arrays, axis, dim, along):
    columns = [a.reshape(*a.shape[:along], -1) for a in arrays]
    both = jnp.concatenate(columns, axis=along)
    whole, at, outs = (summed_on_arrival(both, axis, dim), 0, [])
    for a, column in zip(arrays, columns):
        slab = whole[..., at : at + column.shape[along]]
        outs.append(slab.reshape(*slab.shape[:along], *a.shape[along:]))
        at += column.shape[along]
    return tuple(outs)


def contract_rows(left_arr, right_arr):
    return lax.dot_general(
        left_arr, right_arr, (((0,), (0,)), ((), ())), preferred_element_type=jnp.float32
    )


def contract_cols(left_arr, right_arr):
    return lax.dot_general(
        left_arr, right_arr, (((1,), (1,)), ((), ())), preferred_element_type=jnp.float32
    )


def rms_forward(rows_in, gain_vec):
    inverse = lax.rsqrt(jnp.mean(rows_in * rows_in, axis=-1, keepdims=True) + EPSILON)
    return (rows_in * inverse * gain_vec, inverse)


def rms_backward(rows_in, inverse, gain_vec, grad_out):
    gain_grad = jnp.sum(grad_out * rows_in * inverse, axis=0)
    weighted = grad_out * gain_vec
    inner_mean = jnp.mean(weighted * rows_in, axis=-1, keepdims=True)
    return (inverse * weighted - rows_in * inverse * inverse * inverse * inner_mean, gain_grad)


def doc_layout(doc_lengths, row_count):
    ends_at = jnp.cumsum(doc_lengths)
    starts_at = ends_at - doc_lengths
    position = jnp.arange(row_count, dtype=jnp.int32)
    doc_ids = jnp.sum((position[:, None] >= ends_at[None, :]).astype(jnp.int32), axis=1)
    hitting = doc_ids[:, None] == jnp.arange(doc_lengths.shape[0], dtype=jnp.int32)[None, :]
    start_of = jnp.sum(jnp.where(hitting, starts_at[None, :], 0), axis=1)
    relative = position - start_of
    visible = (doc_ids[:, None] == doc_ids[None, :]) & (position[:, None] >= position[None, :])
    return (relative, visible)


def rope_tables(relative, rot_width):
    counter = jnp.arange(rot_width // 2, dtype=jnp.float32)
    frequency = ROPE_BASE ** (-2.0 * counter / rot_width)
    angles = relative.astype(jnp.float32)[:, None] * frequency[None, :]
    return (jnp.cos(angles), jnp.sin(angles))


def rotate(tensor_in, cosine, sine_tab):
    half_width = tensor_in.shape[-1] // 2
    leading = tensor_in[..., :half_width]
    trailing = tensor_in[..., half_width:]
    return jnp.concatenate(
        [leading * cosine - trailing * sine_tab, trailing * cosine + leading * sine_tab], axis=-1
    )


def unrotate(grad_in, cosine, sine_tab):
    half_width = grad_in.shape[-1] // 2
    leading = grad_in[..., :half_width]
    trailing = grad_in[..., half_width:]
    return jnp.concatenate(
        [leading * cosine + trailing * sine_tab, trailing * cosine - leading * sine_tab], axis=-1
    )


def gated_linear_backward(gate_in, up_in, grad_act):
    sigmoid_g = jax.nn.sigmoid(gate_in)
    grad_gate = grad_act * up_in * sigmoid_g * (1.0 + gate_in * (1.0 - sigmoid_g))
    return (grad_gate, grad_act * gate_in * sigmoid_g)


def slot_tables(route_rows, expert_count, capacity):
    flat_routes = route_rows.reshape(-1)
    one_hot = (flat_routes[:, None] == jnp.arange(expert_count, dtype=jnp.int32)[None, :]).astype(
        jnp.int32
    )
    ranking = jnp.sum((jnp.cumsum(one_hot, axis=0) - one_hot) * one_hot, axis=1)
    slot_ids = flat_routes * capacity + ranking
    row_total = flat_routes.shape[0]
    source = (
        jnp.zeros((expert_count * capacity,), jnp.int32)
        .at[slot_ids]
        .set(jnp.arange(row_total, dtype=jnp.int32))
    )
    filled = jnp.zeros((expert_count * capacity,), jnp.int32).at[slot_ids].set(1)
    return (slot_ids, source, filled)


def to_owner(rows_in):
    arrived = lax.all_to_all(rows_in, "expert", split_axis=0, concat_axis=1, tiled=True)
    return arrived


def weight_plan(
    inputs,
    attn_gain,
    w_query,
    w_latent,
    latent_gain,
    w_kv,
    w_out,
    ffn_gain,
    w_router,
    shared_gate_up,
    shared_down,
    expert_gate_up,
    expert_down,
    lengths,
    routes,
    cotangent,
):
    tok_rows = inputs.shape[0]
    model_width = inputs.shape[1]
    expert_count = w_router.shape[1]
    route_count = routes.shape[1]
    capacity = tok_rows * route_count * 4 // (3 * expert_count)
    brain_float16 = jnp.bfloat16
    f32 = jnp.float32
    gathered = (
        lax.all_gather(attn_gain, "expert", axis=0, tiled=True),
        lax.all_gather(w_query, "expert", axis=0, tiled=True),
        lax.all_gather(w_latent, "expert", axis=0, tiled=True),
        lax.all_gather(latent_gain, "expert", axis=0, tiled=True),
        lax.all_gather(w_kv, "expert", axis=0, tiled=True),
        lax.all_gather(w_out, "expert", axis=1, tiled=True),
        lax.all_gather(ffn_gain, "expert", axis=0, tiled=True),
        lax.all_gather(w_router, "expert", axis=0, tiled=True),
        lax.all_gather(shared_gate_up, "expert", axis=1, tiled=True),
        lax.all_gather(shared_down, "expert", axis=1, tiled=True),
    )
    gain_one, query_w, latent_w, latent_g, kv_w, out_w, gain_two, router_w, sgate_up, sdown_w = (
        gathered
    )
    local_heads = query_w.shape[1] // (DN + DR)
    rank_width = latent_g.shape[0]
    x_float = inputs.astype(f32)
    relative, visible = doc_layout(lengths[0], tok_rows)
    cosine, sine_tab = rope_tables(relative, DR)
    q_scale = (DN + DR) ** (-0.5)
    normed, scale_one = rms_forward(x_float, gain_one.astype(f32))
    normed_b = normed.astype(brain_float16)
    queries = jnp.dot(normed_b, query_w, preferred_element_type=f32).reshape(
        tok_rows, local_heads, DN + DR
    )
    q_rot = rotate(queries[..., DN:], cosine[:, None, :], sine_tab[:, None, :])
    q_all = jnp.concatenate([queries[..., :DN], q_rot], axis=-1).astype(brain_float16)
    latent = jnp.dot(normed_b, latent_w, preferred_element_type=f32)
    compressed, scale_kv = rms_forward(latent[:, :rank_width], latent_g.astype(f32))
    compressed_b = compressed.astype(brain_float16)
    k_rope = rotate(latent[:, rank_width:], cosine, sine_tab).astype(brain_float16)
    kv_all = jnp.dot(compressed_b, kv_w, preferred_element_type=f32).reshape(
        tok_rows, local_heads, DN + DV
    )
    k_nope = kv_all[..., :DN].astype(brain_float16)
    values = kv_all[..., DN:].astype(brain_float16)
    key_all = jnp.concatenate(
        [k_nope, jnp.broadcast_to(k_rope[:, None, :], (tok_rows, local_heads, DR))], axis=-1
    )

    def score_block():
        raw_scores = (
            jnp.einsum("qhd,khd->hqk", q_all, key_all, preferred_element_type=f32) * q_scale
        )
        return jnp.where(visible[None], raw_scores, NEGATIVE)

    scores = score_block()
    top_score = jnp.max(scores, axis=-1, keepdims=True)
    log_total = top_score + jnp.log(jnp.sum(jnp.exp(scores - top_score), axis=-1, keepdims=True))
    probs_b = jnp.exp(scores - log_total).astype(brain_float16)
    attended = jnp.einsum("hqk,khd->qhd", probs_b, values, preferred_element_type=f32)
    attended_b = attended.reshape(tok_rows, local_heads * DV).astype(brain_float16)
    attn = lax.psum(jnp.dot(attended_b, out_w, preferred_element_type=f32), "tensor")
    hidden = x_float + attn
    hnormed, scale_two = rms_forward(hidden, gain_two.astype(f32))
    hnormed_b = hnormed.astype(brain_float16)
    logits = jnp.dot(hnormed_b, router_w, preferred_element_type=f32)
    sigmoid_vals = jax.nn.sigmoid(logits)
    route_hot = routes[:, :, None] == jnp.arange(expert_count, dtype=jnp.int32)[None, None, :]
    chosen = jnp.sum(jnp.where(route_hot, sigmoid_vals[:, None, :], 0.0), axis=2)
    chosen_sum = jnp.sum(chosen, axis=1, keepdims=True)
    gate_vals = ROUTE_SCALE * chosen / chosen_sum
    slot_ids, source, filled = slot_tables(routes, expert_count, capacity)
    is_filled = filled[:, None] == 1
    sent_rows = jnp.where(is_filled, hnormed_b[source // route_count], 0).reshape(
        expert_count, capacity, model_width
    )
    received = to_owner(sent_rows)
    gate_up_joined = jnp.einsum(
        "erd,egdf->egrf", received, expert_gate_up, preferred_element_type=f32
    )
    expert_act = (jax.nn.silu(gate_up_joined[:, 0]) * gate_up_joined[:, 1]).astype(brain_float16)
    expert_res = jnp.einsum(
        "erf,efd->erd", expert_act, expert_down, preferred_element_type=f32
    ).astype(brain_float16)
    returned_all = lax.all_to_all(expert_res, "expert", split_axis=1, concat_axis=0, tiled=True)
    returned = returned_all.reshape(expert_count * capacity, model_width)[slot_ids].reshape(
        tok_rows, route_count, model_width
    )
    shared_gu = jnp.einsum("td,gdf->gtf", hnormed_b, sgate_up, preferred_element_type=f32)
    shared_act = (jax.nn.silu(shared_gu[0]) * shared_gu[1]).astype(brain_float16)
    branch_sum = jnp.dot(shared_act, sdown_w, preferred_element_type=f32)
    for route_idx in range(route_count):
        branch_sum = branch_sum + gate_vals[:, route_idx : route_idx + 1] * returned[
            :, route_idx
        ].astype(f32)
    moe_out = lax.psum(branch_sum.astype(jnp.bfloat16), "tensor").astype(jnp.float32)
    mixed = (hidden + moe_out).astype(brain_float16)
    grad_y = cotangent.astype(f32)
    sdown_grad = contract_rows(shared_act, cotangent)
    grad_sact = contract_cols(cotangent, sdown_w)
    grad_sgate, grad_sup = gated_linear_backward(shared_gu[0], shared_gu[1], grad_sact)
    grad_sgu = jnp.stack([grad_sgate, grad_sup], axis=0).astype(brain_float16)
    sgu_grad = jnp.einsum("td,gtf->gdf", hnormed_b, grad_sgu, preferred_element_type=f32)
    grad_hn_part = jnp.einsum("gtf,gdf->td", grad_sgu, sgate_up, preferred_element_type=f32)
    gate_columns = []
    for route_idx in range(route_count):
        gate_columns.append(jnp.sum(grad_y * returned[:, route_idx].astype(f32), axis=1))
    gate_part = jnp.stack(gate_columns, axis=1)
    slot_grads = (
        (gate_vals[:, :, None] * grad_y[:, None, :])
        .reshape(tok_rows * route_count, model_width)
        .astype(brain_float16)
    )
    grad_sent = jnp.where(is_filled, slot_grads[source], 0).reshape(
        expert_count, capacity, model_width
    )
    grad_received = to_owner(grad_sent)
    edown_grad = jnp.einsum("erf,erd->efd", expert_act, grad_received, preferred_element_type=f32)
    expert_activation_gradient = jnp.einsum(
        "erd,efd->erf", grad_received, expert_down, preferred_element_type=f32
    )
    expert_gate_gradient, expert_up_gradient = gated_linear_backward(
        gate_up_joined[:, 0], gate_up_joined[:, 1], expert_activation_gradient
    )
    expert_gate_up_gradient = jnp.stack([expert_gate_gradient, expert_up_gradient], axis=1).astype(
        brain_float16
    )
    egu_grad = jnp.einsum(
        "erd,egrf->egdf", received, expert_gate_up_gradient, preferred_element_type=f32
    )
    grad_rows = jnp.einsum(
        "egrf,egdf->erd", expert_gate_up_gradient, expert_gate_up, preferred_element_type=f32
    ).astype(brain_float16)
    grad_back = lax.all_to_all(grad_rows, "expert", split_axis=1, concat_axis=0, tiled=True)
    grad_routes = grad_back.reshape(expert_count * capacity, model_width)[slot_ids].reshape(
        tok_rows, route_count, model_width
    )
    for route_idx in range(route_count):
        grad_hn_part = grad_hn_part + grad_routes[:, route_idx].astype(f32)
    gate_grads = lax.psum(gate_part, "tensor")
    grad_chosen = ROUTE_SCALE * (
        gate_grads / chosen_sum
        - jnp.sum(gate_grads * chosen, axis=1, keepdims=True) / (chosen_sum * chosen_sum)
    )
    grad_sig = jnp.sum(jnp.where(route_hot, grad_chosen[:, :, None], 0.0), axis=1)
    grad_logits = (grad_sig * sigmoid_vals * (1.0 - sigmoid_vals)).astype(brain_float16)
    router_grad = contract_rows(hnormed_b, grad_logits)
    grad_hn = lax.psum(grad_hn_part, "tensor") + contract_cols(grad_logits, router_w)
    grad_hidden_norm, gain_two_grad = rms_backward(hidden, scale_two, gain_two.astype(f32), grad_hn)
    grad_hidden = grad_y + grad_hidden_norm
    grad_hidden_b = grad_hidden.astype(brain_float16)
    out_grad = contract_rows(attended_b, grad_hidden_b)
    grad_att = (
        contract_cols(grad_hidden_b, out_w).reshape(tok_rows, local_heads, DV).astype(brain_float16)
    )
    probs = jnp.exp(score_block() - log_total)
    probs_again = probs.astype(brain_float16)
    grad_probs = jnp.einsum("qhd,khd->hqk", grad_att, values, preferred_element_type=f32)
    grad_vals = jnp.einsum("hqk,qhd->khd", probs_again, grad_att, preferred_element_type=f32)
    row_delta = jnp.sum(probs * grad_probs, axis=-1, keepdims=True)
    grad_scores = (probs * (grad_probs - row_delta)).astype(brain_float16)
    grad_q = jnp.einsum("hqk,khd->qhd", grad_scores, key_all, preferred_element_type=f32) * q_scale
    grad_keys = jnp.einsum("hqk,qhd->khd", grad_scores, q_all, preferred_element_type=f32) * q_scale
    grad_kv = (
        jnp.concatenate([grad_keys[..., :DN], grad_vals], axis=-1)
        .reshape(tok_rows, local_heads * (DN + DV))
        .astype(brain_float16)
    )
    kv_grad = contract_rows(compressed_b, grad_kv)
    grad_comp_part = contract_cols(grad_kv, kv_w)
    grad_krope_part = jnp.sum(grad_keys[..., DN:], axis=1)
    grad_comp, grad_krope = (
        lax.psum(grad_comp_part.astype(jnp.bfloat16), "tensor").astype(jnp.float32),
        lax.psum(grad_krope_part.astype(jnp.bfloat16), "tensor").astype(jnp.float32),
    )
    grad_c, latent_gain_grad = rms_backward(
        latent[:, :rank_width], scale_kv, latent_g.astype(f32), grad_comp
    )
    grad_latent = jnp.concatenate([grad_c, unrotate(grad_krope, cosine, sine_tab)], axis=-1).astype(
        brain_float16
    )
    grad_qrot = unrotate(grad_q[..., DN:], cosine[:, None, :], sine_tab[:, None, :])
    grad_queries = (
        jnp.concatenate([grad_q[..., :DN], grad_qrot], axis=-1)
        .reshape(tok_rows, local_heads * (DN + DR))
        .astype(brain_float16)
    )
    query_grad = contract_rows(normed_b, grad_queries)
    latent_grad = contract_rows(normed_b, grad_latent)
    grad_normed = lax.psum(
        contract_cols(grad_queries, query_w).astype(jnp.bfloat16), "tensor"
    ).astype(jnp.float32) + contract_cols(grad_latent, latent_w)
    grad_x_norm, gain_one_grad = rms_backward(x_float, scale_one, gain_one.astype(f32), grad_normed)
    input_grad = grad_hidden + grad_x_norm
    first_owned = (
        *sent_together(
            (
                gain_one_grad.astype(jnp.bfloat16),
                query_grad.astype(jnp.bfloat16),
                latent_grad.astype(jnp.bfloat16),
            ),
            "expert",
            0,
            1,
        ),
        *sent_together(
            (latent_gain_grad.astype(jnp.bfloat16), kv_grad.astype(jnp.bfloat16)), "expert", 0, 1
        ),
    )
    second_owned = (
        lax.psum_scatter(out_grad, "expert", scatter_dimension=1, tiled=True),
        lax.psum_scatter(gain_two_grad, "expert", scatter_dimension=0, tiled=True),
        lax.psum_scatter(router_grad, "expert", scatter_dimension=0, tiled=True),
        lax.psum_scatter(sgu_grad, "expert", scatter_dimension=1, tiled=True),
        lax.psum_scatter(sdown_grad, "expert", scatter_dimension=1, tiled=True),
    )
    return (
        mixed,
        input_grad,
        first_owned[0],
        first_owned[1],
        first_owned[2],
        first_owned[3],
        first_owned[4],
        second_owned[0],
        second_owned[1],
        second_owned[2],
        second_owned[3],
        second_owned[4],
        egu_grad,
        edown_grad,
    )


def swap_cores(value):
    return lax.ppermute(value, "tensor", [(0, 1), (1, 0)])


def take_rows(value, start, count, axis=0):
    return lax.dynamic_slice_in_dim(value, start, count, axis=axis)


def in_order(core, own, other, axis=0):
    return jnp.where(
        core == 0,
        jnp.concatenate([own, other], axis=axis),
        jnp.concatenate([other, own], axis=axis),
    )


def add_wide(*parts):
    total = parts[0].astype(jnp.float32)
    for part in parts[1:]:
        total = total + part.astype(jnp.float32)
    return total


PLANE = 4


def to_partner(value, flips):
    groups = lax.axis_size("expert")
    return lax.ppermute(value, "expert", [(g, g ^ flips) for g in range(groups)])


def to_deeper(value, step):
    groups = lax.axis_size("expert")
    pairs = [(g, (g + step * PLANE) % groups) for g in range(groups)]
    return lax.ppermute(value, "expert", pairs)


def plane_gather(value):
    return [value] + [to_partner(value, r) for r in range(1, PLANE)]


def plane_scatter(parts):
    return add_wide(parts[0], *[to_partner(parts[r], r) for r in range(1, PLANE)])


def by_place(parts, place):
    odd, high = place % 2 == 1, place // 2 == 1
    parts = [jnp.where(odd, parts[i ^ 1], parts[i]) for i in range(PLANE)]
    return [jnp.where(high, parts[i ^ 2], parts[i]) for i in range(PLANE)]


def deep_gather(value, z):
    deep = lax.axis_size("expert") // PLANE
    whole = jnp.zeros((deep, *value.shape), value.dtype)
    whole = lax.dynamic_update_index_in_dim(whole, value, z, 0)
    for step in range(1, deep):
        came = to_deeper(value, step)
        whole = lax.dynamic_update_index_in_dim(whole, came, (z - step) % deep, 0)
    return whole


def deep_scatter(blocks, z):
    deep = blocks.shape[0]

    def block(index):
        return lax.dynamic_index_in_dim(blocks, index, 0, keepdims=False)

    return add_wide(
        block(z), *[to_deeper(block((z + step) % deep), step) for step in range(1, deep)]
    )


def sum_planes(grad, z):
    deep = lax.axis_size("expert") // PLANE
    rows = deep_scatter(grad.astype(jnp.bfloat16).reshape(deep, -1, grad.shape[1]), z)
    return rows.astype(jnp.bfloat16).reshape(PLANE, -1, grad.shape[1])


def share_columns(rows, place):
    parts = [at_index(rows, 0, place)]
    for r in range(1, PLANE):
        parts.append(to_partner(at_index(rows, 0, place ^ r), r))
    return by_place(parts, place)


def all_groups(value):
    return lax.all_gather(value, "expert", axis=0, tiled=False)


def at_index(value, axis, index):
    return lax.dynamic_index_in_dim(value, index, axis, keepdims=False)


def scatter_tokens(value):
    groups, rows = value.shape[:2]
    me = lax.axis_index("expert")
    z, y, x = me // PLANE, me // 2 % 2, me % 2
    deep = groups // PLANE
    blocks = value.reshape(deep, 2, 2, *value.shape[1:])
    cut = rows // 2

    def along(held, axis, mine, flips):
        sent = to_partner(at_index(held, axis, 1 - mine), flips)
        return add_wide(at_index(held, axis, mine), sent).astype(value.dtype)

    first = along(blocks[:, :, :, :cut], 1, y, 2)
    second = along(blocks[:, :, :, cut:], 2, x, 1)
    first = along(first, 1, x, 1)
    second = along(second, 1, y, 2)
    line = jnp.concatenate([first, second], axis=1)
    return deep_scatter(line, z)


def dot_nn(left, right):
    return lax.dot_general(left, right, (((1,), (0,)), ((), ())), preferred_element_type=jnp.float32)


def dot_nt(left, right):
    return lax.dot_general(left, right, (((1,), (1,)), ((), ())), preferred_element_type=jnp.float32)


def dot_tn(left, right):
    return lax.dot_general(left, right, (((0,), (0,)), ((), ())), preferred_element_type=jnp.float32)


def two_lanes(column, lane):
    high = column.astype(jnp.bfloat16).astype(jnp.float32)
    spread = jnp.where(lane == 0, high, jnp.where(lane == 1, column - high, 0.0))
    return spread.astype(jnp.bfloat16)


def expert_kernel(
    shared_cols,
    expert_count,
    me_ref,
    hn_own,
    hn_other,
    dy_own,
    dy_other,
    meta_own,
    meta_other,
    gate_up_w,
    down_w,
    first_w,
    sdown_w,
    slots_out,
    slot_dy_out,
    act_out,
    d_gate_up_out,
    rows_own_out,
    rows_other_out,
    sact_own_out,
    sact_other_out,
    dsh_own_out,
    dsh_other_out,
    dgate_own_out,
    dgate_other_out,
):
    f32, bf16 = jnp.float32, jnp.bfloat16
    count, half, _ = hn_own.shape
    tokens = 2 * half
    me = me_ref[0]
    lane = lax.broadcasted_iota(jnp.int32, (tokens, LANES), 1)
    is_router = (lane >= shared_cols) & (lane < shared_cols + expert_count)
    first = first_w[...]
    slots, slot_dys, slot_gates, picks, dshs = [], [], [], [], []
    for i in range(count):
        rows = jnp.concatenate([hn_own[i], hn_other[i]], axis=0)
        rows_dy = jnp.concatenate([dy_own[i], dy_other[i]], axis=0)
        meta = jnp.concatenate([meta_own[i], meta_other[i]], axis=0)
        products = dot_nn(rows, first)
        gate, up = products[:, :LANES], products[:, LANES:]
        sig = jax.nn.sigmoid(gate)
        total = jnp.sum(jnp.where(is_router, sig * meta, 0.0), axis=1, keepdims=True)
        mine = jnp.sum(jnp.where(lane == shared_cols + me, sig, 0.0), axis=1, keepdims=True)
        token_gate = ROUTE_SCALE * mine / total
        sact = (gate * sig * up).astype(bf16)
        sact_own_out[i], sact_other_out[i] = sact[:half], sact[half:]
        d_sact = dot_nt(rows_dy, sdown_w[...])
        d_sgate = d_sact * up * sig * (1.0 + gate * (1.0 - sig))
        dsh = jnp.concatenate([d_sgate, d_sact * gate * sig], axis=1).astype(bf16)
        dsh_own_out[i], dsh_other_out[i] = dsh[:half], dsh[half:]
        dshs.append(dsh)
        pick = (meta[:, :1] == lane.astype(f32)).astype(bf16)
        picks.append(pick)
        slots.append(dot_tn(pick, rows).astype(bf16))
        slot_dys.append(dot_tn(pick, rows_dy).astype(bf16))
        slot_gates.append(
            jnp.sum(dot_tn(pick, two_lanes(token_gate, lane)), axis=1, keepdims=True)
        )
    slot_rows = jnp.concatenate(slots, axis=0)
    slot_dy = jnp.concatenate(slot_dys, axis=0)
    slot_gate = jnp.concatenate(slot_gates, axis=0)
    slots_out[...] = slot_rows
    slot_dy_out[...] = slot_dy
    gate = dot_nn(slot_rows, gate_up_w[0])
    up = dot_nn(slot_rows, gate_up_w[1])
    d_act = dot_nt(slot_dy, down_w[...])
    sig = jax.nn.sigmoid(gate)
    silu = gate * sig
    act = silu * up
    slot_dgate = jnp.sum(act * d_act, axis=1, keepdims=True)
    act_out[...] = (slot_gate * act).astype(bf16)
    d_act = slot_gate * d_act
    d_gate = (d_act * up * sig * (1.0 + gate * (1.0 - sig))).astype(bf16)
    d_up = (d_act * silu).astype(bf16)
    d_gate_up_out[0] = d_gate
    d_gate_up_out[1] = d_up
    d_slots = (dot_nt(d_gate, gate_up_w[0]) + dot_nt(d_up, gate_up_w[1])).astype(bf16)
    slot_lane = lax.broadcasted_iota(jnp.int32, (LANES, LANES), 1)
    for i in range(count):
        here = slice(i * LANES, (i + 1) * LANES)
        d_rows = (dot_nn(picks[i], d_slots[here]) + dot_nt(dshs[i], first)).astype(bf16)
        rows_own_out[i], rows_other_out[i] = d_rows[:half], d_rows[half:]
        dgate = dot_nn(picks[i], two_lanes(slot_dgate[here], slot_lane))
        dgate_own_out[i], dgate_other_out[i] = dgate[:half], dgate[half:]


def block_specs(per_step):
    def lead(*tail):
        return pl.BlockSpec((per_step, *tail), lambda i: (i,) + (0,) * len(tail))

    def flat(cols):
        return pl.BlockSpec((per_step * LANES, cols), lambda i: (i, 0))

    def whole(a):
        return pl.BlockSpec(a.shape, lambda i: (0,) * a.ndim, pipeline_mode=pl.Buffered(1))

    return lead, flat, whole


def slots_cost(width, hidden, products):
    return LANES * width * hidden * products


def experts(
    me,
    hn_own,
    hn_other,
    dy_own,
    dy_other,
    meta_own,
    meta_other,
    gate_up_w,
    down_w,
    first_w,
    sdown_w,
    shared_cols,
    expert_count,
    per_step=2,
):
    groups, half, width = hn_own.shape
    hidden = down_w.shape[0]
    slots = groups * LANES
    f32, bf16 = jnp.float32, jnp.bfloat16
    lead, flat, whole = block_specs(per_step)
    sds = jax.ShapeDtypeStruct
    rows_cost = 2 * groups * (2 * half * width * 4 * LANES + slots_cost(width, hidden, 5))
    return pl.pallas_call(
        functools.partial(expert_kernel, shared_cols, expert_count),
        grid=(groups // per_step,),
        in_specs=[
            pl.BlockSpec(memory_space=pltpu.SMEM),
            *[lead(half, width)] * 4,
            *[lead(half, LANES)] * 2,
            *[whole(a) for a in (gate_up_w, down_w, first_w, sdown_w)],
        ],
        out_specs=[
            flat(width),
            flat(width),
            flat(hidden),
            pl.BlockSpec((2, per_step * LANES, hidden), lambda i: (0, i, 0)),
            *[lead(half, width)] * 2,
            *[lead(half, LANES)] * 2,
            *[lead(half, 2 * LANES)] * 2,
            *[lead(half, LANES)] * 2,
        ],
        out_shape=[
            sds((slots, width), bf16),
            sds((slots, width), bf16),
            sds((slots, hidden), bf16),
            sds((2, slots, hidden), bf16),
            *[sds((groups, half, width), bf16)] * 2,
            *[sds((groups, half, LANES), bf16)] * 2,
            *[sds((groups, half, 2 * LANES), bf16)] * 2,
            *[sds((groups, half, LANES), f32)] * 2,
        ],
        compiler_params=pltpu.CompilerParams(vmem_limit_bytes=58 * 1024 * 1024),
        cost_estimate=pl.CostEstimate(
            flops=rows_cost, bytes_accessed=20 * groups * half * width, transcendentals=0
        ),
    )(
        me,
        hn_own,
        hn_other,
        dy_own,
        dy_other,
        meta_own,
        meta_other,
        gate_up_w,
        down_w,
        first_w,
        sdown_w,
    )


def output_kernel(act, sact_own, sact_other, meta_own, meta_other, down_w, sdown_w, own_out, other_out):
    f32, bf16 = jnp.float32, jnp.bfloat16
    count, half, _ = meta_own.shape
    lane = lax.broadcasted_iota(jnp.int32, (2 * half, LANES), 1).astype(f32)
    out = dot_nn(act[...], down_w[...]).astype(bf16)
    for i in range(count):
        meta = jnp.concatenate([meta_own[i], meta_other[i]], axis=0)
        pick = (meta[:, :1] == lane).astype(bf16)
        sact = jnp.concatenate([sact_own[i], sact_other[i]], axis=0)
        here = slice(i * LANES, (i + 1) * LANES)
        rows = (dot_nn(pick, out[here]) + dot_nn(sact, sdown_w[...])).astype(bf16)
        own_out[i], other_out[i] = rows[:half], rows[half:]


def outputs(act, sact_own, sact_other, meta_own, meta_other, down_w, sdown_w, per_step=4):
    groups, half, _ = meta_own.shape
    hidden, width = down_w.shape
    lead, flat, whole = block_specs(per_step)
    return pl.pallas_call(
        output_kernel,
        grid=(groups // per_step,),
        in_specs=[
            flat(hidden),
            *[lead(half, LANES)] * 4,
            *[whole(a) for a in (down_w, sdown_w)],
        ],
        out_specs=[lead(half, width)] * 2,
        out_shape=[jax.ShapeDtypeStruct((groups, half, width), jnp.bfloat16)] * 2,
        compiler_params=pltpu.CompilerParams(vmem_limit_bytes=58 * 1024 * 1024),
        cost_estimate=pl.CostEstimate(
            flops=2 * groups * (4 * half * LANES * width + slots_cost(width, hidden, 1)),
            bytes_accessed=5 * groups * half * width,
            transcendentals=0,
        ),
    )(act, sact_own, sact_other, meta_own, meta_other, down_w, sdown_w)


def token_plan(
    inputs,
    attn_gain,
    w_query,
    w_latent,
    latent_gain,
    w_kv,
    w_out,
    ffn_gain,
    w_router,
    shared_gate_up,
    shared_down,
    expert_gate_up,
    expert_down,
    lengths,
    routes,
    cotangent,
):
    f32, bf16 = jnp.float32, jnp.bfloat16
    core, me = lax.axis_index("tensor"), lax.axis_index("expert")
    groups = lax.axis_size("expert")
    deep, place, z = groups // PLANE, me % PLANE, me // PLANE
    tok_rows, width = inputs.shape
    half = tok_rows // 2
    own_at, other_at = core * half, (1 - core) * half
    expert_count = w_router.shape[1]
    route_count = routes.shape[1]
    capacity = tok_rows * route_count * 4 // (3 * expert_count)
    shared_cols = shared_gate_up.shape[2] // groups
    latent_cols, rank_width = w_latent.shape[1], latent_gain.shape[0] * groups
    block_rows = w_query.shape[0]
    kv_rows = w_kv.shape[0]

    query_cols = w_query.shape[1] // PLANE
    out_cols = w_out.shape[0] // PLANE
    used = latent_cols + expert_count + 3
    small = jnp.concatenate(
        [
            w_latent,
            w_router,
            attn_gain[:, None],
            ffn_gain[:, None],
            jnp.pad(latent_gain, (0, block_rows - kv_rows))[:, None],
            jnp.zeros((block_rows, -used % 128), bf16),
        ],
        axis=1,
    )
    route_half = take_rows(routes, own_at, half).astype(bf16).reshape(block_rows // 2, -1)
    small_half = jnp.concatenate(
        [
            take_rows(small, core * (block_rows // 2), block_rows // 2),
            jnp.pad(route_half, ((0, 0), (0, -route_half.shape[1] % 128))),
        ],
        axis=1,
    )
    small_own = all_groups(small_half)
    small_other = swap_cores(small_own)
    small_cols = small.shape[1]
    small_all = in_order(core, small_own, small_other, axis=1)

    def routes_of(came):
        came = came[:, :, small_cols : small_cols + route_half.shape[1]]
        return came.astype(jnp.int32).reshape(groups, half, route_count)

    routes_own, routes_other = routes_of(small_own), routes_of(small_other)
    flat_small = small_all.reshape(groups * block_rows, -1)
    latent_w = flat_small[:, :latent_cols]
    at = latent_cols
    router_w = flat_small[:, at : at + expert_count]
    at += expert_count
    gain_one, gain_two = flat_small[:, at], flat_small[:, at + 1]
    latent_g = small_all[:, :kv_rows, at + 2].reshape(-1)
    kv_cols = w_kv.shape[1] // PLANE
    kv_parts = block_rows // kv_rows
    kv_piece = kv_cols // kv_parts
    w_out_t = w_out.T

    def quarter(index):
        kv_here = take_rows(w_kv, index * kv_cols, kv_cols, axis=1)
        kv_here = [kv_here[:, p * kv_piece : (p + 1) * kv_piece] for p in range(kv_parts)]
        return jnp.concatenate(
            [
                take_rows(w_query, index * query_cols, query_cols, axis=1),
                take_rows(w_out_t, index * out_cols, out_cols, axis=1),
                jnp.concatenate(kv_here, axis=0),
            ],
            axis=1,
        )

    near_w = [quarter(place)] + [to_partner(quarter(place ^ r), r) for r in range(1, PLANE)]
    x_half, lengths_here, near_w = lax.optimization_barrier(
        (take_rows(inputs, own_at, half), lengths[0], near_w)
    )
    lengths_near = jnp.stack(plane_gather(lengths_here))
    x_near_own = jnp.stack(plane_gather(x_half))
    x_near = in_order(core, x_near_own, swap_cores(x_near_own), axis=1)
    x_near = lax.optimization_barrier(x_near.reshape(PLANE * tok_rows, width))
    head_w = deep_gather(jnp.stack(by_place(near_w, place)), z)
    dy_own_rows = take_rows(cotangent, own_at, half)
    dy_sent, shared_gate_up, shared_down, head_w = lax.optimization_barrier(
        (dy_own_rows, shared_gate_up, shared_down, head_w)
    )
    sgu_w = lax.all_to_all(shared_gate_up, "expert", split_axis=2, concat_axis=1, tiled=True)
    sdown_w = lax.all_to_all(shared_down, "expert", split_axis=0, concat_axis=1, tiled=True)
    dy_own = all_groups(dy_sent)
    head_w = head_w.reshape(groups, block_rows, -1)
    flat_head = head_w.reshape(groups * block_rows, -1)
    query_w = flat_head[:, :query_cols]
    out_wt = flat_head[:, query_cols : query_cols + out_cols]
    kv_w = head_w[:, :, query_cols + out_cols :].reshape(groups, kv_parts, kv_rows, kv_piece)
    kv_w = kv_w.transpose(0, 2, 1, 3).reshape(groups * kv_rows, kv_cols)
    near_rows = PLANE * tok_rows
    local_heads = query_cols // (DN + DR)
    x_float = x_near.astype(f32)
    relative, visible = jax.vmap(lambda one: doc_layout(one, tok_rows))(lengths_near)
    cosine, sine_tab = rope_tables(relative.reshape(-1), DR)
    q_scale = (DN + DR) ** (-0.5)
    scale_one = lax.rsqrt(jnp.mean(x_float * x_float, axis=-1, keepdims=True) + EPSILON)
    scale_one = lax.optimization_barrier(scale_one)
    normed_b = (x_near.astype(f32) * scale_one * gain_one.astype(f32)).astype(bf16)
    normed_b = lax.optimization_barrier(normed_b)
    queries = jnp.dot(normed_b, query_w, preferred_element_type=f32).reshape(
        near_rows, local_heads, DN + DR
    )
    q_rot = rotate(queries[..., DN:], cosine[:, None, :], sine_tab[:, None, :])
    q_all = jnp.concatenate([queries[..., :DN], q_rot], axis=-1).astype(bf16)
    q_all = q_all.reshape(PLANE, tok_rows, local_heads, DN + DR)
    latent = jnp.dot(normed_b, latent_w, preferred_element_type=f32)
    compressed, _ = rms_forward(latent[:, :rank_width], latent_g.astype(f32))
    compressed_b = compressed.astype(bf16)
    k_rope = rotate(latent[:, rank_width:], cosine, sine_tab).astype(bf16)
    kv_all = jnp.dot(compressed_b, kv_w, preferred_element_type=f32).reshape(
        PLANE, tok_rows, local_heads, DN + DV
    )
    k_nope = kv_all[..., :DN].astype(bf16)
    values = kv_all[..., DN:].astype(bf16)
    k_rope = k_rope.reshape(PLANE, tok_rows, 1, DR)
    key_all = jnp.concatenate(
        [k_nope, jnp.broadcast_to(k_rope, (PLANE, tok_rows, local_heads, DR))], axis=-1
    )

    def score_block():
        raw_scores = (
            jnp.einsum("gqhd,gkhd->ghqk", q_all, key_all, preferred_element_type=f32) * q_scale
        )
        return jnp.where(visible[:, None], raw_scores, NEGATIVE)

    scores = score_block()
    top_score = jnp.max(scores, axis=-1, keepdims=True)
    log_total = top_score + jnp.log(jnp.sum(jnp.exp(scores - top_score), axis=-1, keepdims=True))
    probs_b = jnp.exp(scores - log_total).astype(bf16)
    attended = jnp.einsum("ghqk,gkhd->gqhd", probs_b, values, preferred_element_type=f32)
    attended_b = attended.reshape(near_rows, local_heads * DV).astype(bf16)

    def sum_heads(part):
        part = part.astype(bf16).reshape(PLANE, tok_rows, -1)
        came = swap_cores(take_rows(part, other_at, half, axis=1))
        both = add_wide(take_rows(part, own_at, half, axis=1), came).astype(bf16)
        return plane_scatter([both[r] for r in range(PLANE)])

    attn_own = sum_heads(contract_cols(attended_b, out_wt))
    x_own = take_rows(inputs, own_at, half).astype(f32)
    hidden = x_own + attn_own
    hnormed, scale_two = rms_forward(hidden, gain_two.astype(f32))
    hnormed_b = hnormed.astype(bf16)
    hnormed_b, dy_own, sgu_w, sdown_w = lax.optimization_barrier((hnormed_b, dy_own, sgu_w, sdown_w))
    dy_other = swap_cores(dy_own)

    hn_own = all_groups(hnormed_b)
    hn_other = swap_cores(hn_own)

    def membership(named):
        one_hot = named[..., None] == jnp.arange(expert_count, dtype=jnp.int32)
        return jnp.any(named == me, axis=-1), jnp.any(one_hot, axis=2)

    member_own, hot_own = membership(routes_own)
    member_other, hot_other = membership(routes_other)
    lower = (
        jnp.arange(half, dtype=jnp.int32)[:, None] <= jnp.arange(half, dtype=jnp.int32)[None, :]
    ).astype(bf16)

    def running(mask):
        counts = jnp.dot(mask.astype(bf16), lower, preferred_element_type=f32)
        return counts.astype(jnp.int32)

    count_own, count_other = running(member_own), running(member_other)
    place_own = jnp.where(member_own, count_own - 1, -1)
    place_other = jnp.where(member_other, count_own[:, -1:] + count_other - 1, -1)

    def metadata(slot, hot):
        return jnp.concatenate(
            [
                slot[..., None].astype(f32),
                jnp.zeros((groups, half, shared_cols - 1), f32),
                hot.astype(f32),
                jnp.zeros((groups, half, LANES - shared_cols - expert_count), f32),
            ],
            axis=-1,
        )

    meta_own, meta_other = metadata(place_own, hot_own), metadata(place_other, hot_other)
    first_w = jnp.concatenate(
        [
            jnp.pad(
                jnp.concatenate([sgu_w[0], router_w], axis=1),
                ((0, 0), (0, LANES - shared_cols - expert_count)),
            ),
            jnp.pad(sgu_w[1], ((0, 0), (0, LANES - shared_cols))),
        ],
        axis=1,
    )
    sdown_rows = jnp.pad(sdown_w, ((0, LANES - shared_cols), (0, 0)))
    gate_up_w, down_w = expert_gate_up[0], expert_down[0]
    (
        slot_rows,
        slot_dy,
        slot_act,
        d_gate_up,
        d_rows_own,
        d_rows_other,
        act_own,
        act_other,
        d_shared_own,
        d_shared_other,
        dgate_own,
        dgate_other,
    ) = experts(
        me.reshape(1).astype(jnp.int32),
        hn_own,
        hn_other,
        dy_own,
        dy_other,
        meta_own,
        meta_other,
        gate_up_w,
        down_w,
        first_w,
        sdown_rows,
        shared_cols,
        expert_count,
    )
    d_rows = add_wide(d_rows_own, swap_cores(d_rows_other)).astype(bf16)
    d_rows, slot_act, slot_rows, d_gate_up, d_shared_own, d_shared_other = (
        lax.optimization_barrier(
            (d_rows, slot_act, slot_rows, d_gate_up, d_shared_own, d_shared_other)
        )
    )
    d_hn = scatter_tokens(d_rows)
    out_own, out_other = outputs(
        slot_act, act_own, act_other, meta_own, meta_other, down_w, sdown_rows
    )
    out_rows = (out_own.astype(f32) + swap_cores(out_other).astype(f32)).astype(bf16)
    moe_own = lax.psum_scatter(out_rows, "expert", scatter_dimension=0, tiled=False).astype(f32)
    edown_grad = contract_rows(slot_act, slot_dy)
    egu_grad = jnp.einsum("sd,gsf->gdf", slot_rows, d_gate_up, preferred_element_type=f32)
    mixed_own = (hidden + moe_own).astype(bf16)
    mixed = in_order(core, mixed_own, swap_cores(mixed_own))

    def flat_rows(value):
        return value.reshape(groups * half, -1)

    sgu_grad = contract_rows(flat_rows(hn_own), flat_rows(d_shared_own)) + contract_rows(
        flat_rows(hn_other), flat_rows(d_shared_other)
    )
    sdown_grad = contract_rows(flat_rows(act_own), flat_rows(dy_own)) + contract_rows(
        flat_rows(act_other), flat_rows(dy_other)
    )
    sdown_grad = sdown_grad[:shared_cols]
    sgu_grad = jnp.stack(
        [sgu_grad[:, :shared_cols], sgu_grad[:, LANES : LANES + shared_cols]]
    )
    sgu_out = lax.all_to_all(
        sgu_grad.astype(bf16), "expert", split_axis=1, concat_axis=2, tiled=True
    ).astype(f32)
    sdown_out = lax.all_to_all(
        sdown_grad.astype(bf16), "expert", split_axis=1, concat_axis=0, tiled=True
    ).astype(f32)

    def two_parts(value):
        return value[..., 0] + value[..., 1]

    dgate_sent = two_parts(dgate_own) + swap_cores(two_parts(dgate_other))
    dgate = lax.all_to_all(dgate_sent, "expert", split_axis=0, concat_axis=0, tiled=True).T
    hot_mine = take_rows(
        jnp.any(routes[..., None] == jnp.arange(expert_count, dtype=jnp.int32), axis=1), own_at, half
    )
    sig = jax.nn.sigmoid(jnp.dot(hnormed_b, router_w, preferred_element_type=f32))
    chosen = jnp.where(hot_mine, sig, 0.0)
    chosen_sum = jnp.sum(chosen, axis=1, keepdims=True)
    dgate = jnp.where(hot_mine, dgate, 0.0)
    inner = jnp.sum(dgate * chosen, axis=1, keepdims=True)
    d_chosen = ROUTE_SCALE * (dgate / chosen_sum - inner / (chosen_sum * chosen_sum))
    d_logits = (jnp.where(hot_mine, d_chosen, 0.0) * sig * (1.0 - sig)).astype(bf16)
    router_grad = contract_rows(d_logits, hnormed_b)
    d_hn = d_hn + contract_cols(d_logits, router_w)
    d_hidden_norm, gain_two_grad = rms_backward(hidden, scale_two, gain_two.astype(f32), d_hn)
    d_hidden = dy_own_rows.astype(f32) + d_hidden_norm
    d_near_own = jnp.stack(plane_gather(d_hidden.astype(bf16)))
    d_near = in_order(core, d_near_own, swap_cores(d_near_own), axis=1).reshape(near_rows, width)

    grad_att = (
        jnp.dot(d_near, out_wt, preferred_element_type=f32)
        .reshape(PLANE, tok_rows, local_heads, DV)
        .astype(bf16)
    )
    out_sums = sum_planes(contract_rows(d_near, attended_b), z)
    probs = jnp.exp(score_block() - log_total)
    probs_again = probs.astype(bf16)
    grad_probs = jnp.einsum("gqhd,gkhd->ghqk", grad_att, values, preferred_element_type=f32)
    grad_vals = jnp.einsum("ghqk,gqhd->gkhd", probs_again, grad_att, preferred_element_type=f32)
    row_delta = jnp.sum(probs * grad_probs, axis=-1, keepdims=True)
    grad_scores = (probs * (grad_probs - row_delta)).astype(bf16)
    grad_q = (
        jnp.einsum("ghqk,gkhd->gqhd", grad_scores, key_all, preferred_element_type=f32) * q_scale
    ).reshape(near_rows, local_heads, DN + DR)
    grad_keys = (
        jnp.einsum("ghqk,gqhd->gkhd", grad_scores, q_all, preferred_element_type=f32) * q_scale
    )
    grad_kv = (
        jnp.concatenate([grad_keys[..., :DN], grad_vals], axis=-1)
        .reshape(near_rows, local_heads * (DN + DV))
        .astype(bf16)
    )
    grad_latent_part = jnp.concatenate(
        [
            contract_cols(grad_kv, kv_w),
            jnp.sum(grad_keys[..., DN:], axis=2).reshape(near_rows, DR),
        ],
        axis=1,
    )
    grad_both = sum_heads(grad_latent_part)
    latent_own = take_rows(latent[:tok_rows], own_at, half)
    cosine_own = take_rows(cosine[:tok_rows], own_at, half)
    sine_own = take_rows(sine_tab[:tok_rows], own_at, half)
    _, scale_kv = rms_forward(latent_own[:, :rank_width], latent_g.astype(f32))
    grad_c, latent_gain_grad = rms_backward(
        latent_own[:, :rank_width], scale_kv, latent_g.astype(f32), grad_both[:, :rank_width]
    )
    grad_latent = jnp.concatenate(
        [grad_c, unrotate(grad_both[:, rank_width:], cosine_own, sine_own)], axis=-1
    ).astype(bf16)
    grad_qrot = unrotate(grad_q[..., DN:], cosine[:, None, :], sine_tab[:, None, :])
    grad_queries = (
        jnp.concatenate([grad_q[..., :DN], grad_qrot], axis=-1)
        .reshape(near_rows, local_heads * (DN + DR))
        .astype(bf16)
    )
    kv_grad = contract_rows(compressed_b, grad_kv).astype(bf16)
    kv_grad = kv_grad.reshape(groups, kv_rows, kv_parts, kv_piece).transpose(0, 2, 1, 3)
    query_grad = contract_rows(normed_b, grad_queries).astype(bf16)
    first_sums = sum_planes(
        jnp.concatenate([query_grad, kv_grad.reshape(-1, kv_piece)], axis=1), z
    )
    shared_out = share_columns(jnp.concatenate([first_sums, out_sums], axis=2), place)
    at_kv, at_out = query_cols, query_cols + kv_piece
    w_query_grad = jnp.concatenate([p[:, :at_kv] for p in shared_out], axis=1).astype(f32)
    w_kv_grad = jnp.concatenate(
        [
            p[q * kv_rows : (q + 1) * kv_rows, at_kv:at_out]
            for p in shared_out
            for q in range(kv_parts)
        ],
        axis=1,
    ).astype(f32)
    w_out_grad = jnp.concatenate([p[:, at_out:] for p in shared_out], axis=1).astype(f32).T
    grad_normed = sum_heads(contract_cols(grad_queries, query_w))
    grad_normed = grad_normed + contract_cols(grad_latent, latent_w)
    _, scale_own = rms_forward(x_own, gain_one.astype(f32))
    grad_x_norm, gain_one_grad = rms_backward(x_own, scale_own, gain_one.astype(f32), grad_normed)
    input_own = d_hidden + grad_x_norm
    input_grad = in_order(core, input_own, swap_cores(input_own))

    latent_near_own = jnp.stack(plane_gather(grad_latent))
    latent_near = in_order(core, latent_near_own, swap_cores(latent_near_own), axis=1)
    rows_at = place * block_rows + core * (block_rows // 2)
    normed_cols = normed_b.reshape(near_rows, deep, PLANE * block_rows)
    normed_cols = take_rows(normed_cols, rows_at, block_rows // 2, axis=2)
    latent_blocks = contract_rows(
        normed_cols.reshape(near_rows, -1), latent_near.reshape(near_rows, latent_cols)
    )
    latent_half = deep_scatter(latent_blocks.astype(bf16).reshape(deep, -1, latent_cols), z)
    w_latent_grad = in_order(core, latent_half, swap_cores(latent_half))

    gain_lanes = jnp.pad(
        latent_gain_grad.reshape(groups, kv_rows), ((0, 0), (0, block_rows - kv_rows))
    )
    vectors = jnp.concatenate(
        [
            router_grad,
            gain_one_grad[None],
            gain_two_grad[None],
            gain_lanes.reshape(1, -1),
        ],
        axis=0,
    ).reshape(-1, groups, block_rows)
    arrived = lax.all_to_all(vectors, "expert", split_axis=1, concat_axis=1, tiled=True)
    sums = jnp.sum(arrived, axis=1)
    sums = sums + swap_cores(sums)
    return (
        mixed,
        input_grad,
        sums[expert_count],
        w_query_grad,
        w_latent_grad,
        sums[expert_count + 2, :kv_rows],
        w_kv_grad,
        w_out_grad,
        sums[expert_count + 1],
        sums[:expert_count].T,
        sgu_out,
        sdown_out,
        egu_grad[None],
        edown_grad[None],
    )


def solution(mesh):
    groups = mesh.shape["expert"]
    plan = token_plan if groups <= 16 else weight_plan
    return jax.shard_map(
        plan,
        mesh=mesh,
        in_specs=(
            P("expert", None),
            P("expert"),
            P("expert", "tensor"),
            P("expert", None),
            P("expert"),
            P("expert", "tensor"),
            P("tensor", "expert"),
            P("expert"),
            P("expert", None),
            P(None, "expert", "tensor"),
            P("tensor", "expert"),
            P("expert", None, None, "tensor"),
            P("expert", "tensor", None),
            P("expert", None),
            P("expert", None),
            P("expert", None),
        ),
        out_specs=(
            P("expert", None),
            P("expert", None),
            P("expert"),
            P("expert", "tensor"),
            P("expert", None),
            P("expert"),
            P("expert", "tensor"),
            P("tensor", "expert"),
            P("expert"),
            P("expert", None),
            P(None, "expert", "tensor"),
            P("tensor", "expert"),
            P("expert", None, None, "tensor"),
            P("expert", "tensor", None),
        ),
        check_vma=False,
    )
```

```python
import functools

import jax
import jax.numpy as jnp
from jax import lax
from jax.experimental import pallas as pl
from jax.experimental.pallas import tpu as pltpu
from jax.sharding import PartitionSpec as P

DN = 128
DR = 64
DV = 128
LANES = 128


EPSILON = 1e-06
ROUTE_SCALE = 2.446
ROPE_BASE = 50000.0
NEGATIVE = -1e30


def cut_along(value, dim, length):
    before, after = (value.shape[:dim], value.shape[dim + 1 :])
    return jnp.moveaxis(value.reshape(*before, length, -1, *after), dim, 0)


def summed_on_arrival(value, axis, dim):
    length = lax.axis_size(axis)
    tiles = lax.all_to_all(cut_along(value, dim, length), axis, 0, 0, tiled=True)
    return jnp.sum(tiles.astype(jnp.float32), axis=0)


def sent_together(arrays, axis, dim, along):
    columns = [a.reshape(*a.shape[:along], -1) for a in arrays]
    both = jnp.concatenate(columns, axis=along)
    whole, at, outs = (summed_on_arrival(both, axis, dim), 0, [])
    for a, column in zip(arrays, columns):
        slab = whole[..., at : at + column.shape[along]]
        outs.append(slab.reshape(*slab.shape[:along], *a.shape[along:]))
        at += column.shape[along]
    return tuple(outs)


def contract_rows(left_arr, right_arr):
    return lax.dot_general(
        left_arr, right_arr, (((0,), (0,)), ((), ())), preferred_element_type=jnp.float32
    )


def contract_cols(left_arr, right_arr):
    return lax.dot_general(
        left_arr, right_arr, (((1,), (1,)), ((), ())), preferred_element_type=jnp.float32
    )


def rms_forward(rows_in, gain_vec):
    inverse = lax.rsqrt(jnp.mean(rows_in * rows_in, axis=-1, keepdims=True) + EPSILON)
    return (rows_in * inverse * gain_vec, inverse)


def rms_backward(rows_in, inverse, gain_vec, grad_out):
    gain_grad = jnp.sum(grad_out * rows_in * inverse, axis=0)
    weighted = grad_out * gain_vec
    inner_mean = jnp.mean(weighted * rows_in, axis=-1, keepdims=True)
    return (inverse * weighted - rows_in * inverse * inverse * inverse * inner_mean, gain_grad)


def doc_layout(doc_lengths, row_count):
    ends_at = jnp.cumsum(doc_lengths)
    starts_at = ends_at - doc_lengths
    position = jnp.arange(row_count, dtype=jnp.int32)
    doc_ids = jnp.sum((position[:, None] >= ends_at[None, :]).astype(jnp.int32), axis=1)
    hitting = doc_ids[:, None] == jnp.arange(doc_lengths.shape[0], dtype=jnp.int32)[None, :]
    start_of = jnp.sum(jnp.where(hitting, starts_at[None, :], 0), axis=1)
    relative = position - start_of
    visible = (doc_ids[:, None] == doc_ids[None, :]) & (position[:, None] >= position[None, :])
    return (relative, visible)


def rope_tables(relative, rot_width):
    counter = jnp.arange(rot_width // 2, dtype=jnp.float32)
    frequency = ROPE_BASE ** (-2.0 * counter / rot_width)
    angles = relative.astype(jnp.float32)[:, None] * frequency[None, :]
    return (jnp.cos(angles), jnp.sin(angles))


def rotate(tensor_in, cosine, sine_tab):
    half_width = tensor_in.shape[-1] // 2
    leading = tensor_in[..., :half_width]
    trailing = tensor_in[..., half_width:]
    return jnp.concatenate(
        [leading * cosine - trailing * sine_tab, trailing * cosine + leading * sine_tab], axis=-1
    )


def unrotate(grad_in, cosine, sine_tab):
    half_width = grad_in.shape[-1] // 2
    leading = grad_in[..., :half_width]
    trailing = grad_in[..., half_width:]
    return jnp.concatenate(
        [leading * cosine + trailing * sine_tab, trailing * cosine - leading * sine_tab], axis=-1
    )


def gated_linear_backward(gate_in, up_in, grad_act):
    sigmoid_g = jax.nn.sigmoid(gate_in)
    grad_gate = grad_act * up_in * sigmoid_g * (1.0 + gate_in * (1.0 - sigmoid_g))
    return (grad_gate, grad_act * gate_in * sigmoid_g)


def slot_tables(route_rows, expert_count, capacity):
    flat_routes = route_rows.reshape(-1)
    one_hot = (flat_routes[:, None] == jnp.arange(expert_count, dtype=jnp.int32)[None, :]).astype(
        jnp.int32
    )
    ranking = jnp.sum((jnp.cumsum(one_hot, axis=0) - one_hot) * one_hot, axis=1)
    slot_ids = flat_routes * capacity + ranking
    row_total = flat_routes.shape[0]
    source = (
        jnp.zeros((expert_count * capacity,), jnp.int32)
        .at[slot_ids]
        .set(jnp.arange(row_total, dtype=jnp.int32))
    )
    filled = jnp.zeros((expert_count * capacity,), jnp.int32).at[slot_ids].set(1)
    return (slot_ids, source, filled)


def to_owner(rows_in):
    arrived = lax.all_to_all(rows_in, "expert", split_axis=0, concat_axis=1, tiled=True)
    return arrived


def weight_plan(
    inputs,
    attn_gain,
    w_query,
    w_latent,
    latent_gain,
    w_kv,
    w_out,
    ffn_gain,
    w_router,
    shared_gate_up,
    shared_down,
    expert_gate_up,
    expert_down,
    lengths,
    routes,
    cotangent,
):
    tok_rows = inputs.shape[0]
    model_width = inputs.shape[1]
    expert_count = w_router.shape[1]
    route_count = routes.shape[1]
    capacity = tok_rows * route_count * 4 // (3 * expert_count)
    brain_float16 = jnp.bfloat16
    f32 = jnp.float32
    gathered = (
        lax.all_gather(attn_gain, "expert", axis=0, tiled=True),
        lax.all_gather(w_query, "expert", axis=0, tiled=True),
        lax.all_gather(w_latent, "expert", axis=0, tiled=True),
        lax.all_gather(latent_gain, "expert", axis=0, tiled=True),
        lax.all_gather(w_kv, "expert", axis=0, tiled=True),
        lax.all_gather(w_out, "expert", axis=1, tiled=True),
        lax.all_gather(ffn_gain, "expert", axis=0, tiled=True),
        lax.all_gather(w_router, "expert", axis=0, tiled=True),
        lax.all_gather(shared_gate_up, "expert", axis=1, tiled=True),
        lax.all_gather(shared_down, "expert", axis=1, tiled=True),
    )
    gain_one, query_w, latent_w, latent_g, kv_w, out_w, gain_two, router_w, sgate_up, sdown_w = (
        gathered
    )
    local_heads = query_w.shape[1] // (DN + DR)
    rank_width = latent_g.shape[0]
    x_float = inputs.astype(f32)
    relative, visible = doc_layout(lengths[0], tok_rows)
    cosine, sine_tab = rope_tables(relative, DR)
    q_scale = (DN + DR) ** (-0.5)
    normed, scale_one = rms_forward(x_float, gain_one.astype(f32))
    normed_b = normed.astype(brain_float16)
    queries = jnp.dot(normed_b, query_w, preferred_element_type=f32).reshape(
        tok_rows, local_heads, DN + DR
    )
    q_rot = rotate(queries[..., DN:], cosine[:, None, :], sine_tab[:, None, :])
    q_all = jnp.concatenate([queries[..., :DN], q_rot], axis=-1).astype(brain_float16)
    latent = jnp.dot(normed_b, latent_w, preferred_element_type=f32)
    compressed, scale_kv = rms_forward(latent[:, :rank_width], latent_g.astype(f32))
    compressed_b = compressed.astype(brain_float16)
    k_rope = rotate(latent[:, rank_width:], cosine, sine_tab).astype(brain_float16)
    kv_all = jnp.dot(compressed_b, kv_w, preferred_element_type=f32).reshape(
        tok_rows, local_heads, DN + DV
    )
    k_nope = kv_all[..., :DN].astype(brain_float16)
    values = kv_all[..., DN:].astype(brain_float16)
    key_all = jnp.concatenate(
        [k_nope, jnp.broadcast_to(k_rope[:, None, :], (tok_rows, local_heads, DR))], axis=-1
    )

    def score_block():
        raw_scores = (
            jnp.einsum("qhd,khd->hqk", q_all, key_all, preferred_element_type=f32) * q_scale
        )
        return jnp.where(visible[None], raw_scores, NEGATIVE)

    scores = score_block()
    top_score = jnp.max(scores, axis=-1, keepdims=True)
    log_total = top_score + jnp.log(jnp.sum(jnp.exp(scores - top_score), axis=-1, keepdims=True))
    probs_b = jnp.exp(scores - log_total).astype(brain_float16)
    attended = jnp.einsum("hqk,khd->qhd", probs_b, values, preferred_element_type=f32)
    attended_b = attended.reshape(tok_rows, local_heads * DV).astype(brain_float16)
    attn = lax.psum(jnp.dot(attended_b, out_w, preferred_element_type=f32), "tensor")
    hidden = x_float + attn
    hnormed, scale_two = rms_forward(hidden, gain_two.astype(f32))
    hnormed_b = hnormed.astype(brain_float16)
    logits = jnp.dot(hnormed_b, router_w, preferred_element_type=f32)
    sigmoid_vals = jax.nn.sigmoid(logits)
    route_hot = routes[:, :, None] == jnp.arange(expert_count, dtype=jnp.int32)[None, None, :]
    chosen = jnp.sum(jnp.where(route_hot, sigmoid_vals[:, None, :], 0.0), axis=2)
    chosen_sum = jnp.sum(chosen, axis=1, keepdims=True)
    gate_vals = ROUTE_SCALE * chosen / chosen_sum
    slot_ids, source, filled = slot_tables(routes, expert_count, capacity)
    is_filled = filled[:, None] == 1
    sent_rows = jnp.where(is_filled, hnormed_b[source // route_count], 0).reshape(
        expert_count, capacity, model_width
    )
    received = to_owner(sent_rows)
    gate_up_joined = jnp.einsum(
        "erd,egdf->egrf", received, expert_gate_up, preferred_element_type=f32
    )
    expert_act = (jax.nn.silu(gate_up_joined[:, 0]) * gate_up_joined[:, 1]).astype(brain_float16)
    expert_res = jnp.einsum(
        "erf,efd->erd", expert_act, expert_down, preferred_element_type=f32
    ).astype(brain_float16)
    returned_all = lax.all_to_all(expert_res, "expert", split_axis=1, concat_axis=0, tiled=True)
    returned = returned_all.reshape(expert_count * capacity, model_width)[slot_ids].reshape(
        tok_rows, route_count, model_width
    )
    shared_gu = jnp.einsum("td,gdf->gtf", hnormed_b, sgate_up, preferred_element_type=f32)
    shared_act = (jax.nn.silu(shared_gu[0]) * shared_gu[1]).astype(brain_float16)
    branch_sum = jnp.dot(shared_act, sdown_w, preferred_element_type=f32)
    for route_idx in range(route_count):
        branch_sum = branch_sum + gate_vals[:, route_idx : route_idx + 1] * returned[
            :, route_idx
        ].astype(f32)
    moe_out = lax.psum(branch_sum.astype(jnp.bfloat16), "tensor").astype(jnp.float32)
    mixed = (hidden + moe_out).astype(brain_float16)
    grad_y = cotangent.astype(f32)
    sdown_grad = contract_rows(shared_act, cotangent)
    grad_sact = contract_cols(cotangent, sdown_w)
    grad_sgate, grad_sup = gated_linear_backward(shared_gu[0], shared_gu[1], grad_sact)
    grad_sgu = jnp.stack([grad_sgate, grad_sup], axis=0).astype(brain_float16)
    sgu_grad = jnp.einsum("td,gtf->gdf", hnormed_b, grad_sgu, preferred_element_type=f32)
    grad_hn_part = jnp.einsum("gtf,gdf->td", grad_sgu, sgate_up, preferred_element_type=f32)
    gate_columns = []
    for route_idx in range(route_count):
        gate_columns.append(jnp.sum(grad_y * returned[:, route_idx].astype(f32), axis=1))
    gate_part = jnp.stack(gate_columns, axis=1)
    slot_grads = (
        (gate_vals[:, :, None] * grad_y[:, None, :])
        .reshape(tok_rows * route_count, model_width)
        .astype(brain_float16)
    )
    grad_sent = jnp.where(is_filled, slot_grads[source], 0).reshape(
        expert_count, capacity, model_width
    )
    grad_received = to_owner(grad_sent)
    edown_grad = jnp.einsum("erf,erd->efd", expert_act, grad_received, preferred_element_type=f32)
    expert_activation_gradient = jnp.einsum(
        "erd,efd->erf", grad_received, expert_down, preferred_element_type=f32
    )
    expert_gate_gradient, expert_up_gradient = gated_linear_backward(
        gate_up_joined[:, 0], gate_up_joined[:, 1], expert_activation_gradient
    )
    expert_gate_up_gradient = jnp.stack([expert_gate_gradient, expert_up_gradient], axis=1).astype(
        brain_float16
    )
    egu_grad = jnp.einsum(
        "erd,egrf->egdf", received, expert_gate_up_gradient, preferred_element_type=f32
    )
    grad_rows = jnp.einsum(
        "egrf,egdf->erd", expert_gate_up_gradient, expert_gate_up, preferred_element_type=f32
    ).astype(brain_float16)
    grad_back = lax.all_to_all(grad_rows, "expert", split_axis=1, concat_axis=0, tiled=True)
    grad_routes = grad_back.reshape(expert_count * capacity, model_width)[slot_ids].reshape(
        tok_rows, route_count, model_width
    )
    for route_idx in range(route_count):
        grad_hn_part = grad_hn_part + grad_routes[:, route_idx].astype(f32)
    gate_grads = lax.psum(gate_part, "tensor")
    grad_chosen = ROUTE_SCALE * (
        gate_grads / chosen_sum
        - jnp.sum(gate_grads * chosen, axis=1, keepdims=True) / (chosen_sum * chosen_sum)
    )
    grad_sig = jnp.sum(jnp.where(route_hot, grad_chosen[:, :, None], 0.0), axis=1)
    grad_logits = (grad_sig * sigmoid_vals * (1.0 - sigmoid_vals)).astype(brain_float16)
    router_grad = contract_rows(hnormed_b, grad_logits)
    grad_hn = lax.psum(grad_hn_part, "tensor") + contract_cols(grad_logits, router_w)
    grad_hidden_norm, gain_two_grad = rms_backward(hidden, scale_two, gain_two.astype(f32), grad_hn)
    grad_hidden = grad_y + grad_hidden_norm
    grad_hidden_b = grad_hidden.astype(brain_float16)
    out_grad = contract_rows(attended_b, grad_hidden_b)
    grad_att = (
        contract_cols(grad_hidden_b, out_w).reshape(tok_rows, local_heads, DV).astype(brain_float16)
    )
    probs = jnp.exp(score_block() - log_total)
    probs_again = probs.astype(brain_float16)
    grad_probs = jnp.einsum("qhd,khd->hqk", grad_att, values, preferred_element_type=f32)
    grad_vals = jnp.einsum("hqk,qhd->khd", probs_again, grad_att, preferred_element_type=f32)
    row_delta = jnp.sum(probs * grad_probs, axis=-1, keepdims=True)
    grad_scores = (probs * (grad_probs - row_delta)).astype(brain_float16)
    grad_q = jnp.einsum("hqk,khd->qhd", grad_scores, key_all, preferred_element_type=f32) * q_scale
    grad_keys = jnp.einsum("hqk,qhd->khd", grad_scores, q_all, preferred_element_type=f32) * q_scale
    grad_kv = (
        jnp.concatenate([grad_keys[..., :DN], grad_vals], axis=-1)
        .reshape(tok_rows, local_heads * (DN + DV))
        .astype(brain_float16)
    )
    kv_grad = contract_rows(compressed_b, grad_kv)
    grad_comp_part = contract_cols(grad_kv, kv_w)
    grad_krope_part = jnp.sum(grad_keys[..., DN:], axis=1)
    grad_comp, grad_krope = (
        lax.psum(grad_comp_part.astype(jnp.bfloat16), "tensor").astype(jnp.float32),
        lax.psum(grad_krope_part.astype(jnp.bfloat16), "tensor").astype(jnp.float32),
    )
    grad_c, latent_gain_grad = rms_backward(
        latent[:, :rank_width], scale_kv, latent_g.astype(f32), grad_comp
    )
    grad_latent = jnp.concatenate([grad_c, unrotate(grad_krope, cosine, sine_tab)], axis=-1).astype(
        brain_float16
    )
    grad_qrot = unrotate(grad_q[..., DN:], cosine[:, None, :], sine_tab[:, None, :])
    grad_queries = (
        jnp.concatenate([grad_q[..., :DN], grad_qrot], axis=-1)
        .reshape(tok_rows, local_heads * (DN + DR))
        .astype(brain_float16)
    )
    query_grad = contract_rows(normed_b, grad_queries)
    latent_grad = contract_rows(normed_b, grad_latent)
    grad_normed = lax.psum(
        contract_cols(grad_queries, query_w).astype(jnp.bfloat16), "tensor"
    ).astype(jnp.float32) + contract_cols(grad_latent, latent_w)
    grad_x_norm, gain_one_grad = rms_backward(x_float, scale_one, gain_one.astype(f32), grad_normed)
    input_grad = grad_hidden + grad_x_norm
    first_owned = (
        *sent_together(
            (
                gain_one_grad.astype(jnp.bfloat16),
                query_grad.astype(jnp.bfloat16),
                latent_grad.astype(jnp.bfloat16),
            ),
            "expert",
            0,
            1,
        ),
        *sent_together(
            (latent_gain_grad.astype(jnp.bfloat16), kv_grad.astype(jnp.bfloat16)), "expert", 0, 1
        ),
    )
    second_owned = (
        lax.psum_scatter(out_grad, "expert", scatter_dimension=1, tiled=True),
        lax.psum_scatter(gain_two_grad, "expert", scatter_dimension=0, tiled=True),
        lax.psum_scatter(router_grad, "expert", scatter_dimension=0, tiled=True),
        lax.psum_scatter(sgu_grad, "expert", scatter_dimension=1, tiled=True),
        lax.psum_scatter(sdown_grad, "expert", scatter_dimension=1, tiled=True),
    )
    return (
        mixed,
        input_grad,
        first_owned[0],
        first_owned[1],
        first_owned[2],
        first_owned[3],
        first_owned[4],
        second_owned[0],
        second_owned[1],
        second_owned[2],
        second_owned[3],
        second_owned[4],
        egu_grad,
        edown_grad,
    )


def swap_cores(value):
    return lax.ppermute(value, "tensor", [(0, 1), (1, 0)])


def take_rows(value, start, count, axis=0):
    return lax.dynamic_slice_in_dim(value, start, count, axis=axis)


def in_order(core, own, other, axis=0):
    return jnp.where(
        core == 0,
        jnp.concatenate([own, other], axis=axis),
        jnp.concatenate([other, own], axis=axis),
    )


def add_wide(*parts):
    total = parts[0].astype(jnp.float32)
    for part in parts[1:]:
        total = total + part.astype(jnp.float32)
    return total


PLANE = 4


def to_partner(value, flips):
    groups = lax.axis_size("expert")
    return lax.ppermute(value, "expert", [(g, g ^ flips) for g in range(groups)])


def to_deeper(value, step):
    groups = lax.axis_size("expert")
    pairs = [(g, (g + step * PLANE) % groups) for g in range(groups)]
    return lax.ppermute(value, "expert", pairs)


def plane_gather(value):
    return [value] + [to_partner(value, r) for r in range(1, PLANE)]


def plane_scatter(parts):
    return add_wide(parts[0], *[to_partner(parts[r], r) for r in range(1, PLANE)])


def by_place(parts, place):
    odd, high = place % 2 == 1, place // 2 == 1
    parts = [jnp.where(odd, parts[i ^ 1], parts[i]) for i in range(PLANE)]
    return [jnp.where(high, parts[i ^ 2], parts[i]) for i in range(PLANE)]


def one_plane(value, step):
    groups = lax.axis_size("expert")
    pairs = [(g, g + step * PLANE) for g in range(groups) if 0 <= g + step * PLANE < groups]
    return lax.ppermute(value, "expert", pairs)


def deep_pieces(value):
    deep = lax.axis_size("expert") // PLANE
    after, before, down, up = [], [], value, value
    for _ in range(1, deep):
        down, up = one_plane(down, 1), one_plane(up, -1)
        after.append(down)
        before.append(up)
    return [after[s - 1] + before[deep - s - 1] for s in range(1, deep)]


def deep_join(value, pieces, z):
    deep = lax.axis_size("expert") // PLANE
    whole = jnp.zeros((deep, *value.shape), value.dtype)
    whole = lax.dynamic_update_index_in_dim(whole, value, z, 0)
    for step in range(1, deep):
        whole = lax.dynamic_update_index_in_dim(whole, pieces[step - 1], (z - step) % deep, 0)
    return whole


def deep_scatter(blocks, z):
    deep = blocks.shape[0]

    def block(index):
        return lax.dynamic_index_in_dim(blocks, index, 0, keepdims=False)

    return add_wide(
        block(z), *[to_deeper(block((z + step) % deep), step) for step in range(1, deep)]
    )


def sum_planes(grad, z):
    deep = lax.axis_size("expert") // PLANE
    rows = deep_scatter(grad.astype(jnp.bfloat16).reshape(deep, -1, grad.shape[1]), z)
    return rows.astype(jnp.bfloat16).reshape(PLANE, -1, grad.shape[1])


def share_columns(rows, place):
    parts = [at_index(rows, 0, place)]
    for r in range(1, PLANE):
        parts.append(to_partner(at_index(rows, 0, place ^ r), r))
    return by_place(parts, place)


def all_groups(value):
    return lax.all_gather(value, "expert", axis=0, tiled=False)


def at_index(value, axis, index):
    return lax.dynamic_index_in_dim(value, index, axis, keepdims=False)


def plane_sums(own, came):
    groups, rows = own.shape[:2]
    me = lax.axis_index("expert")
    y, x = me // 2 % 2, me % 2
    cut = rows // 2

    def along(parts, axis, mine, flips):
        gone = add_wide(*[at_index(p, axis, 1 - mine) for p in parts]).astype(own.dtype)
        kept = [at_index(p, axis, mine) for p in parts]
        return add_wide(*kept, to_partner(gone, flips)).astype(own.dtype)

    blocks = [v.reshape(groups // PLANE, 2, 2, *v.shape[1:]) for v in (own, came)]
    first = along([v[:, :, :, :cut] for v in blocks], 1, y, 2)
    second = along([v[:, :, :, cut:] for v in blocks], 2, x, 1)
    first = along([first], 1, x, 1)
    second = along([second], 1, y, 2)
    return jnp.concatenate([first, second], axis=1)


def dot_nn(left, right):
    return lax.dot_general(left, right, (((1,), (0,)), ((), ())), preferred_element_type=jnp.float32)


def dot_nt(left, right):
    return lax.dot_general(left, right, (((1,), (1,)), ((), ())), preferred_element_type=jnp.float32)


def dot_tn(left, right):
    return lax.dot_general(left, right, (((0,), (0,)), ((), ())), preferred_element_type=jnp.float32)


def two_lanes(column, lane):
    high = column.astype(jnp.bfloat16).astype(jnp.float32)
    spread = jnp.where(lane == 0, high, jnp.where(lane == 1, column - high, 0.0))
    return spread.astype(jnp.bfloat16)


def expert_kernel(
    shared_cols,
    expert_count,
    me_ref,
    hn_own,
    hn_other,
    dy_own,
    dy_other,
    meta_own,
    meta_other,
    gate_up_w,
    down_w,
    first_w,
    sdown_w,
    slots_out,
    slot_dy_out,
    act_out,
    d_gate_up_out,
    rows_own_out,
    rows_other_out,
    sact_own_out,
    sact_other_out,
    dsh_own_out,
    dsh_other_out,
    dgate_own_out,
    dgate_other_out,
):
    f32, bf16 = jnp.float32, jnp.bfloat16
    count, half, _ = hn_own.shape
    tokens = 2 * half
    me = me_ref[0]
    lane = lax.broadcasted_iota(jnp.int32, (tokens, LANES), 1)
    is_router = (lane >= shared_cols) & (lane < shared_cols + expert_count)
    first = first_w[...]
    slots, slot_dys, slot_gates, picks, dshs = [], [], [], [], []
    for i in range(count):
        rows = jnp.concatenate([hn_own[i], hn_other[i]], axis=0)
        rows_dy = jnp.concatenate([dy_own[i], dy_other[i]], axis=0)
        meta = jnp.concatenate([meta_own[i], meta_other[i]], axis=0)
        products = dot_nn(rows, first)
        gate, up = products[:, :LANES], products[:, LANES:]
        sig = jax.nn.sigmoid(gate)
        total = jnp.sum(jnp.where(is_router, sig * meta, 0.0), axis=1, keepdims=True)
        mine = jnp.sum(jnp.where(lane == shared_cols + me, sig, 0.0), axis=1, keepdims=True)
        token_gate = ROUTE_SCALE * mine / total
        sact = (gate * sig * up).astype(bf16)
        sact_own_out[i], sact_other_out[i] = sact[:half], sact[half:]
        d_sact = dot_nt(rows_dy, sdown_w[...])
        d_sgate = d_sact * up * sig * (1.0 + gate * (1.0 - sig))
        dsh = jnp.concatenate([d_sgate, d_sact * gate * sig], axis=1).astype(bf16)
        dsh_own_out[i], dsh_other_out[i] = dsh[:half], dsh[half:]
        dshs.append(dsh)
        pick = (meta[:, :1] == lane.astype(f32)).astype(bf16)
        picks.append(pick)
        slots.append(dot_tn(pick, rows).astype(bf16))
        slot_dys.append(dot_tn(pick, rows_dy).astype(bf16))
        slot_gates.append(
            jnp.sum(dot_tn(pick, two_lanes(token_gate, lane)), axis=1, keepdims=True)
        )
    slot_rows = jnp.concatenate(slots, axis=0)
    slot_dy = jnp.concatenate(slot_dys, axis=0)
    slot_gate = jnp.concatenate(slot_gates, axis=0)
    slots_out[...] = slot_rows
    slot_dy_out[...] = slot_dy
    gate = dot_nt(slot_rows, gate_up_w[0])
    up = dot_nt(slot_rows, gate_up_w[1])
    d_act = dot_nt(slot_dy, down_w[...])
    sig = jax.nn.sigmoid(gate)
    silu = gate * sig
    act = silu * up
    slot_dgate = jnp.sum(act * d_act, axis=1, keepdims=True)
    act_out[...] = (slot_gate * act).astype(bf16)
    d_act = slot_gate * d_act
    d_gate = (d_act * up * sig * (1.0 + gate * (1.0 - sig))).astype(bf16)
    d_up = (d_act * silu).astype(bf16)
    d_gate_up_out[0] = d_gate
    d_gate_up_out[1] = d_up
    d_slots = (dot_nn(d_gate, gate_up_w[0]) + dot_nn(d_up, gate_up_w[1])).astype(bf16)
    slot_lane = lax.broadcasted_iota(jnp.int32, (LANES, LANES), 1)
    for i in range(count):
        here = slice(i * LANES, (i + 1) * LANES)
        d_rows = (dot_nn(picks[i], d_slots[here]) + dot_nt(dshs[i], first)).astype(bf16)
        rows_own_out[i], rows_other_out[i] = d_rows[:half], d_rows[half:]
        dgate = dot_nn(picks[i], two_lanes(slot_dgate[here], slot_lane))
        dgate_own_out[i], dgate_other_out[i] = dgate[:half], dgate[half:]


def block_specs(per_step):
    def lead(*tail):
        return pl.BlockSpec((per_step, *tail), lambda i: (i,) + (0,) * len(tail))

    def flat(cols):
        return pl.BlockSpec((per_step * LANES, cols), lambda i: (i, 0))

    def whole(a):
        return pl.BlockSpec(a.shape, lambda i: (0,) * a.ndim, pipeline_mode=pl.Buffered(1))

    return lead, flat, whole


def slots_cost(width, hidden, products):
    return LANES * width * hidden * products


def experts(
    me,
    hn_own,
    hn_other,
    dy_own,
    dy_other,
    meta_own,
    meta_other,
    gate_up_w,
    down_w,
    first_w,
    sdown_w,
    shared_cols,
    expert_count,
    per_step=2,
):
    groups, half, width = hn_own.shape
    hidden = down_w.shape[0]
    slots = groups * LANES
    f32, bf16 = jnp.float32, jnp.bfloat16
    lead, flat, whole = block_specs(per_step)
    sds = jax.ShapeDtypeStruct
    rows_cost = 2 * groups * (2 * half * width * 4 * LANES + slots_cost(width, hidden, 5))
    return pl.pallas_call(
        functools.partial(expert_kernel, shared_cols, expert_count),
        grid=(groups // per_step,),
        in_specs=[
            pl.BlockSpec(memory_space=pltpu.SMEM),
            *[lead(half, width)] * 4,
            *[lead(half, LANES)] * 2,
            *[whole(a) for a in (gate_up_w, down_w, first_w, sdown_w)],
        ],
        out_specs=[
            flat(width),
            flat(width),
            flat(hidden),
            pl.BlockSpec((2, per_step * LANES, hidden), lambda i: (0, i, 0)),
            *[lead(half, width)] * 2,
            *[lead(half, LANES)] * 2,
            *[lead(half, 2 * LANES)] * 2,
            *[lead(half, LANES)] * 2,
        ],
        out_shape=[
            sds((slots, width), bf16),
            sds((slots, width), bf16),
            sds((slots, hidden), bf16),
            sds((2, slots, hidden), bf16),
            *[sds((groups, half, width), bf16)] * 2,
            *[sds((groups, half, LANES), bf16)] * 2,
            *[sds((groups, half, 2 * LANES), bf16)] * 2,
            *[sds((groups, half, LANES), f32)] * 2,
        ],
        compiler_params=pltpu.CompilerParams(vmem_limit_bytes=58 * 1024 * 1024),
        cost_estimate=pl.CostEstimate(
            flops=rows_cost, bytes_accessed=20 * groups * half * width, transcendentals=0
        ),
    )(
        me,
        hn_own,
        hn_other,
        dy_own,
        dy_other,
        meta_own,
        meta_other,
        gate_up_w,
        down_w,
        first_w,
        sdown_w,
    )


def output_kernel(act, sact_own, sact_other, meta_own, meta_other, down_w, sdown_w, own_out, other_out):
    f32, bf16 = jnp.float32, jnp.bfloat16
    count, half, _ = meta_own.shape
    lane = lax.broadcasted_iota(jnp.int32, (2 * half, LANES), 1).astype(f32)
    out = dot_nn(act[...], down_w[...]).astype(bf16)
    for i in range(count):
        meta = jnp.concatenate([meta_own[i], meta_other[i]], axis=0)
        pick = (meta[:, :1] == lane).astype(bf16)
        sact = jnp.concatenate([sact_own[i], sact_other[i]], axis=0)
        here = slice(i * LANES, (i + 1) * LANES)
        rows = (dot_nn(pick, out[here]) + dot_nn(sact, sdown_w[...])).astype(bf16)
        own_out[i], other_out[i] = rows[:half], rows[half:]


def outputs(act, sact_own, sact_other, meta_own, meta_other, down_w, sdown_w, per_step=4):
    groups, half, _ = meta_own.shape
    hidden, width = down_w.shape
    lead, flat, whole = block_specs(per_step)
    return pl.pallas_call(
        output_kernel,
        grid=(groups // per_step,),
        in_specs=[
            flat(hidden),
            *[lead(half, LANES)] * 4,
            *[whole(a) for a in (down_w, sdown_w)],
        ],
        out_specs=[lead(half, width)] * 2,
        out_shape=[jax.ShapeDtypeStruct((groups, half, width), jnp.bfloat16)] * 2,
        compiler_params=pltpu.CompilerParams(vmem_limit_bytes=58 * 1024 * 1024),
        cost_estimate=pl.CostEstimate(
            flops=2 * groups * (4 * half * LANES * width + slots_cost(width, hidden, 1)),
            bytes_accessed=5 * groups * half * width,
            transcendentals=0,
        ),
    )(act, sact_own, sact_other, meta_own, meta_other, down_w, sdown_w)


def token_plan(
    inputs,
    attn_gain,
    w_query,
    w_latent,
    latent_gain,
    w_kv,
    w_out,
    ffn_gain,
    w_router,
    shared_gate_up,
    shared_down,
    expert_gate_up,
    expert_down,
    lengths,
    routes,
    cotangent,
):
    f32, bf16 = jnp.float32, jnp.bfloat16
    core, me = lax.axis_index("tensor"), lax.axis_index("expert")
    groups = lax.axis_size("expert")
    deep, place, z = groups // PLANE, me % PLANE, me // PLANE
    tok_rows, width = inputs.shape
    half = tok_rows // 2
    own_at, other_at = core * half, (1 - core) * half
    expert_count = w_router.shape[1]
    route_count = routes.shape[1]
    capacity = tok_rows * route_count * 4 // (3 * expert_count)
    shared_cols = shared_gate_up.shape[2] // groups
    latent_cols, rank_width = w_latent.shape[1], latent_gain.shape[0] * groups
    block_rows = w_query.shape[0]
    kv_rows = w_kv.shape[0]

    query_cols = w_query.shape[1] // PLANE
    out_cols = w_out.shape[0] // PLANE
    used = latent_cols + expert_count + 3
    small = jnp.concatenate(
        [
            w_latent,
            w_router,
            attn_gain[:, None],
            ffn_gain[:, None],
            jnp.pad(latent_gain, (0, block_rows - kv_rows))[:, None],
            jnp.zeros((block_rows, -used % 128), bf16),
        ],
        axis=1,
    )
    small_cols = small.shape[1]
    route_half = take_rows(routes, own_at, half).astype(bf16).reshape(block_rows // 2, -1)
    small_half = jnp.concatenate(
        [
            take_rows(small, core * (block_rows // 2), block_rows // 2),
            jnp.pad(route_half, ((0, 0), (0, -route_half.shape[1] % 128))),
        ],
        axis=1,
    )
    packed_cols = small_half.shape[1] // 2
    small_packed = jnp.concatenate([small_half[:, :packed_cols], small_half[:, packed_cols:]])
    kv_cols = w_kv.shape[1] // PLANE
    kv_parts = block_rows // kv_rows
    kv_piece = kv_cols // kv_parts
    w_out_t = w_out.T

    def quarter(index):
        kv_here = take_rows(w_kv, index * kv_cols, kv_cols, axis=1)
        kv_here = [kv_here[:, p * kv_piece : (p + 1) * kv_piece] for p in range(kv_parts)]
        return jnp.concatenate(
            [
                take_rows(w_query, index * query_cols, query_cols, axis=1),
                take_rows(w_out_t, index * out_cols, out_cols, axis=1),
                jnp.concatenate(kv_here, axis=0),
                small_packed,
            ],
            axis=1,
        )

    near_w = [quarter(place)] + [to_partner(quarter(place ^ r), r) for r in range(1, PLANE)]
    x_half, lengths_here, near_w = lax.optimization_barrier(
        (take_rows(inputs, own_at, half), lengths[0], near_w)
    )
    plane_w = jnp.stack(by_place(near_w, place))
    lengths_near = jnp.stack(plane_gather(lengths_here))
    deep_w, x_parts = lax.optimization_barrier((deep_pieces(plane_w), plane_gather(x_half)))
    x_near_own = jnp.stack(x_parts)
    x_near = in_order(core, x_near_own, swap_cores(x_near_own), axis=1)
    x_near = lax.optimization_barrier(x_near.reshape(PLANE * tok_rows, width))
    head_w = deep_join(plane_w, deep_w, z)
    dy_own_rows = take_rows(cotangent, own_at, half)
    dy_own = all_groups(dy_own_rows)
    shared_gate_up, shared_down, head_w = lax.optimization_barrier(
        (shared_gate_up, shared_down, head_w)
    )
    sgu_w = lax.all_to_all(shared_gate_up, "expert", split_axis=2, concat_axis=1, tiled=True)
    sdown_w = lax.all_to_all(shared_down, "expert", split_axis=0, concat_axis=1, tiled=True)
    head_w = head_w.reshape(groups, block_rows, -1)
    flat_head = head_w.reshape(groups * block_rows, -1)
    query_w = flat_head[:, :query_cols]
    at = query_cols + out_cols
    out_wt = flat_head[:, query_cols:at]
    kv_w = head_w[:, :, at : at + kv_piece].reshape(groups, kv_parts, kv_rows, kv_piece)
    kv_w = kv_w.transpose(0, 2, 1, 3).reshape(groups * kv_rows, kv_cols)
    small_own = head_w[:, :, at + kv_piece :]
    small_own = jnp.concatenate(
        [small_own[:, : block_rows // 2], small_own[:, block_rows // 2 :]], axis=2
    )
    small_other = swap_cores(small_own)
    small_all = in_order(core, small_own, small_other, axis=1)

    def routes_of(came):
        came = came[:, :, small_cols : small_cols + route_half.shape[1]]
        return came.astype(jnp.int32).reshape(groups, half, route_count)

    routes_own, routes_other = routes_of(small_own), routes_of(small_other)
    flat_small = small_all.reshape(groups * block_rows, -1)
    latent_w = flat_small[:, :latent_cols]
    at = latent_cols
    router_w = flat_small[:, at : at + expert_count]
    at += expert_count
    gain_one, gain_two = flat_small[:, at], flat_small[:, at + 1]
    latent_g = small_all[:, :kv_rows, at + 2].reshape(-1)

    near_rows = PLANE * tok_rows
    local_heads = query_cols // (DN + DR)
    x_float = x_near.astype(f32)
    relative, visible = jax.vmap(lambda one: doc_layout(one, tok_rows))(lengths_near)
    cosine, sine_tab = rope_tables(relative.reshape(-1), DR)
    q_scale = (DN + DR) ** (-0.5)
    scale_one = lax.rsqrt(jnp.mean(x_float * x_float, axis=-1, keepdims=True) + EPSILON)
    scale_one = lax.optimization_barrier(scale_one)
    normed_b = (x_near.astype(f32) * scale_one * gain_one.astype(f32)).astype(bf16)
    normed_b = lax.optimization_barrier(normed_b)
    queries = jnp.dot(normed_b, query_w, preferred_element_type=f32).reshape(
        near_rows, local_heads, DN + DR
    )
    q_rot = rotate(queries[..., DN:], cosine[:, None, :], sine_tab[:, None, :])
    q_all = jnp.concatenate([queries[..., :DN], q_rot], axis=-1).astype(bf16)
    q_all = q_all.reshape(PLANE, tok_rows, local_heads, DN + DR)
    latent = jnp.dot(normed_b, latent_w, preferred_element_type=f32)
    compressed, _ = rms_forward(latent[:, :rank_width], latent_g.astype(f32))
    compressed_b = compressed.astype(bf16)
    k_rope = rotate(latent[:, rank_width:], cosine, sine_tab).astype(bf16)
    kv_all = jnp.dot(compressed_b, kv_w, preferred_element_type=f32).reshape(
        PLANE, tok_rows, local_heads, DN + DV
    )
    k_nope = kv_all[..., :DN].astype(bf16)
    values = kv_all[..., DN:].astype(bf16)
    k_rope = k_rope.reshape(PLANE, tok_rows, 1, DR)
    key_all = jnp.concatenate(
        [k_nope, jnp.broadcast_to(k_rope, (PLANE, tok_rows, local_heads, DR))], axis=-1
    )

    def score_block():
        raw_scores = (
            jnp.einsum("gqhd,gkhd->ghqk", q_all, key_all, preferred_element_type=f32) * q_scale
        )
        return jnp.where(visible[:, None], raw_scores, NEGATIVE)

    scores = score_block()
    top_score = jnp.max(scores, axis=-1, keepdims=True)
    log_total = top_score + jnp.log(jnp.sum(jnp.exp(scores - top_score), axis=-1, keepdims=True))
    probs_b = jnp.exp(scores - log_total).astype(bf16)
    attended = jnp.einsum("ghqk,gkhd->gqhd", probs_b, values, preferred_element_type=f32)
    attended_b = attended.reshape(near_rows, local_heads * DV).astype(bf16)
    attended_b, dy_own = lax.optimization_barrier((attended_b, dy_own))

    def sum_heads(part):
        part = part.astype(bf16).reshape(PLANE, tok_rows, -1)
        came = swap_cores(take_rows(part, other_at, half, axis=1))
        both = add_wide(take_rows(part, own_at, half, axis=1), came).astype(bf16)
        return plane_scatter([both[r] for r in range(PLANE)])

    attn_own = sum_heads(contract_cols(attended_b, out_wt))
    x_own = take_rows(inputs, own_at, half).astype(f32)
    hidden = x_own + attn_own
    hnormed, scale_two = rms_forward(hidden, gain_two.astype(f32))
    hnormed_b = hnormed.astype(bf16)
    hnormed_b, sgu_w, sdown_w = lax.optimization_barrier((hnormed_b, sgu_w, sdown_w))
    dy_other = swap_cores(dy_own)

    hn_own = all_groups(hnormed_b)
    hn_other = swap_cores(hn_own)

    def membership(named):
        one_hot = named[..., None] == jnp.arange(expert_count, dtype=jnp.int32)
        return jnp.any(named == me, axis=-1), jnp.any(one_hot, axis=2)

    member_own, hot_own = membership(routes_own)
    member_other, hot_other = membership(routes_other)
    lower = (
        jnp.arange(half, dtype=jnp.int32)[:, None] <= jnp.arange(half, dtype=jnp.int32)[None, :]
    ).astype(bf16)

    def running(mask):
        counts = jnp.dot(mask.astype(bf16), lower, preferred_element_type=f32)
        return counts.astype(jnp.int32)

    count_own, count_other = running(member_own), running(member_other)
    place_own = jnp.where(member_own, count_own - 1, -1)
    place_other = jnp.where(member_other, count_own[:, -1:] + count_other - 1, -1)

    def metadata(slot, hot):
        return jnp.concatenate(
            [
                slot[..., None].astype(f32),
                jnp.zeros((groups, half, shared_cols - 1), f32),
                hot.astype(f32),
                jnp.zeros((groups, half, LANES - shared_cols - expert_count), f32),
            ],
            axis=-1,
        )

    meta_own, meta_other = metadata(place_own, hot_own), metadata(place_other, hot_other)
    first_w = jnp.concatenate(
        [
            jnp.pad(
                jnp.concatenate([sgu_w[0], router_w], axis=1),
                ((0, 0), (0, LANES - shared_cols - expert_count)),
            ),
            jnp.pad(sgu_w[1], ((0, 0), (0, LANES - shared_cols))),
        ],
        axis=1,
    )
    sdown_rows = jnp.pad(sdown_w, ((0, LANES - shared_cols), (0, 0)))
    gate_up_w, down_w = jnp.swapaxes(expert_gate_up[0], 1, 2), expert_down[0]
    (
        slot_rows,
        slot_dy,
        slot_act,
        d_gate_up,
        d_rows_own,
        d_rows_other,
        act_own,
        act_other,
        d_shared_own,
        d_shared_other,
        dgate_own,
        dgate_other,
    ) = experts(
        me.reshape(1).astype(jnp.int32),
        hn_own,
        hn_other,
        dy_own,
        dy_other,
        meta_own,
        meta_other,
        gate_up_w,
        down_w,
        first_w,
        sdown_rows,
        shared_cols,
        expert_count,
    )
    d_rows_came = swap_cores(d_rows_other)
    d_rows_own, slot_act, slot_rows, d_gate_up, d_shared_own, d_shared_other = (
        lax.optimization_barrier(
            (d_rows_own, slot_act, slot_rows, d_gate_up, d_shared_own, d_shared_other)
        )
    )
    out_own, out_other = outputs(
        slot_act, act_own, act_other, meta_own, meta_other, down_w, sdown_rows
    )
    out_came = swap_cores(out_other)
    d_line = plane_sums(d_rows_own, d_rows_came)
    d_line, out_own, out_came = lax.optimization_barrier((d_line, out_own, out_came))
    d_hn = deep_scatter(d_line, z)
    moe_own = deep_scatter(plane_sums(out_own, out_came), z)
    edown_grad = contract_rows(slot_act, slot_dy)
    egu_grad = jnp.einsum("sd,gsf->gdf", slot_rows, d_gate_up, preferred_element_type=f32)
    mixed_own = (hidden + moe_own).astype(bf16)
    mixed = in_order(core, mixed_own, swap_cores(mixed_own))

    def flat_rows(value):
        return value.reshape(groups * half, -1)

    sgu_grad = contract_rows(flat_rows(hn_own), flat_rows(d_shared_own)) + contract_rows(
        flat_rows(hn_other), flat_rows(d_shared_other)
    )
    sdown_grad = contract_rows(flat_rows(act_own), flat_rows(dy_own)) + contract_rows(
        flat_rows(act_other), flat_rows(dy_other)
    )
    sdown_grad = sdown_grad[:shared_cols]
    sgu_grad = jnp.stack(
        [sgu_grad[:, :shared_cols], sgu_grad[:, LANES : LANES + shared_cols]]
    )
    sgu_out = lax.all_to_all(
        sgu_grad.astype(bf16), "expert", split_axis=1, concat_axis=2, tiled=True
    ).astype(f32)
    sdown_out = lax.all_to_all(
        sdown_grad.astype(bf16), "expert", split_axis=1, concat_axis=0, tiled=True
    ).astype(f32)

    def two_parts(value):
        return value[..., 0] + value[..., 1]

    dgate_sent = two_parts(dgate_own) + swap_cores(two_parts(dgate_other))
    dgate = lax.all_to_all(dgate_sent, "expert", split_axis=0, concat_axis=0, tiled=True).T
    hot_mine = take_rows(
        jnp.any(routes[..., None] == jnp.arange(expert_count, dtype=jnp.int32), axis=1), own_at, half
    )
    sig = jax.nn.sigmoid(jnp.dot(hnormed_b, router_w, preferred_element_type=f32))
    chosen = jnp.where(hot_mine, sig, 0.0)
    chosen_sum = jnp.sum(chosen, axis=1, keepdims=True)
    dgate = jnp.where(hot_mine, dgate, 0.0)
    inner = jnp.sum(dgate * chosen, axis=1, keepdims=True)
    d_chosen = ROUTE_SCALE * (dgate / chosen_sum - inner / (chosen_sum * chosen_sum))
    d_logits = (jnp.where(hot_mine, d_chosen, 0.0) * sig * (1.0 - sig)).astype(bf16)
    router_grad = contract_rows(d_logits, hnormed_b)
    d_hn = d_hn + contract_cols(d_logits, router_w)
    d_hidden_norm, gain_two_grad = rms_backward(hidden, scale_two, gain_two.astype(f32), d_hn)
    d_hidden = dy_own_rows.astype(f32) + d_hidden_norm
    d_near_own = jnp.stack(plane_gather(d_hidden.astype(bf16)))
    d_near = in_order(core, d_near_own, swap_cores(d_near_own), axis=1).reshape(near_rows, width)

    grad_att = (
        jnp.dot(d_near, out_wt, preferred_element_type=f32)
        .reshape(PLANE, tok_rows, local_heads, DV)
        .astype(bf16)
    )
    out_sums = sum_planes(contract_rows(d_near, attended_b), z)
    probs = jnp.exp(score_block() - log_total)
    probs_again = probs.astype(bf16)
    grad_probs = jnp.einsum("gqhd,gkhd->ghqk", grad_att, values, preferred_element_type=f32)
    grad_vals = jnp.einsum("ghqk,gqhd->gkhd", probs_again, grad_att, preferred_element_type=f32)
    row_delta = jnp.sum(probs * grad_probs, axis=-1, keepdims=True)
    grad_scores = (probs * (grad_probs - row_delta)).astype(bf16)
    grad_q = (
        jnp.einsum("ghqk,gkhd->gqhd", grad_scores, key_all, preferred_element_type=f32) * q_scale
    ).reshape(near_rows, local_heads, DN + DR)
    grad_keys = (
        jnp.einsum("ghqk,gqhd->gkhd", grad_scores, q_all, preferred_element_type=f32) * q_scale
    )
    grad_kv = (
        jnp.concatenate([grad_keys[..., :DN], grad_vals], axis=-1)
        .reshape(near_rows, local_heads * (DN + DV))
        .astype(bf16)
    )
    grad_latent_part = jnp.concatenate(
        [
            contract_cols(grad_kv, kv_w),
            jnp.sum(grad_keys[..., DN:], axis=2).reshape(near_rows, DR),
        ],
        axis=1,
    )
    grad_both = sum_heads(grad_latent_part)
    latent_own = take_rows(latent[:tok_rows], own_at, half)
    cosine_own = take_rows(cosine[:tok_rows], own_at, half)
    sine_own = take_rows(sine_tab[:tok_rows], own_at, half)
    _, scale_kv = rms_forward(latent_own[:, :rank_width], latent_g.astype(f32))
    grad_c, latent_gain_grad = rms_backward(
        latent_own[:, :rank_width], scale_kv, latent_g.astype(f32), grad_both[:, :rank_width]
    )
    grad_latent = jnp.concatenate(
        [grad_c, unrotate(grad_both[:, rank_width:], cosine_own, sine_own)], axis=-1
    ).astype(bf16)
    grad_qrot = unrotate(grad_q[..., DN:], cosine[:, None, :], sine_tab[:, None, :])
    grad_queries = (
        jnp.concatenate([grad_q[..., :DN], grad_qrot], axis=-1)
        .reshape(near_rows, local_heads * (DN + DR))
        .astype(bf16)
    )
    kv_grad = contract_rows(compressed_b, grad_kv).astype(bf16)
    kv_grad = kv_grad.reshape(groups, kv_rows, kv_parts, kv_piece).transpose(0, 2, 1, 3)
    query_grad = contract_rows(normed_b, grad_queries).astype(bf16)
    first_sums = sum_planes(
        jnp.concatenate([query_grad, kv_grad.reshape(-1, kv_piece)], axis=1), z
    )
    shared_out = share_columns(jnp.concatenate([first_sums, out_sums], axis=2), place)
    at_kv, at_out = query_cols, query_cols + kv_piece
    w_query_grad = jnp.concatenate([p[:, :at_kv] for p in shared_out], axis=1).astype(f32)
    w_kv_grad = jnp.concatenate(
        [
            p[q * kv_rows : (q + 1) * kv_rows, at_kv:at_out]
            for p in shared_out
            for q in range(kv_parts)
        ],
        axis=1,
    ).astype(f32)
    w_out_grad = jnp.concatenate([p[:, at_out:] for p in shared_out], axis=1).astype(f32).T
    grad_normed = sum_heads(contract_cols(grad_queries, query_w))
    grad_normed = grad_normed + contract_cols(grad_latent, latent_w)
    _, scale_own = rms_forward(x_own, gain_one.astype(f32))
    grad_x_norm, gain_one_grad = rms_backward(x_own, scale_own, gain_one.astype(f32), grad_normed)
    input_own = d_hidden + grad_x_norm
    input_grad = in_order(core, input_own, swap_cores(input_own))

    latent_near_own = jnp.stack(plane_gather(grad_latent))
    latent_near = in_order(core, latent_near_own, swap_cores(latent_near_own), axis=1)
    normed_cols = normed_b.reshape(near_rows, deep, PLANE * block_rows)
    normed_cols = take_rows(normed_cols, place * block_rows, block_rows, axis=2)
    latent_cut = latent_cols // 2
    latent_near = latent_near.reshape(near_rows, latent_cols)
    latent_blocks = contract_rows(
        normed_cols.reshape(near_rows, -1),
        take_rows(latent_near, core * latent_cut, latent_cut, axis=1),
    )
    latent_half = deep_scatter(latent_blocks.astype(bf16).reshape(deep, -1, latent_cut), z)
    w_latent_grad = in_order(core, latent_half, swap_cores(latent_half), axis=1)

    gain_lanes = jnp.pad(
        latent_gain_grad.reshape(groups, kv_rows), ((0, 0), (0, block_rows - kv_rows))
    )
    vectors = jnp.concatenate(
        [
            router_grad,
            gain_one_grad[None],
            gain_two_grad[None],
            gain_lanes.reshape(1, -1),
        ],
        axis=0,
    ).reshape(-1, groups, block_rows)
    arrived = lax.all_to_all(vectors, "expert", split_axis=1, concat_axis=1, tiled=True)
    sums = jnp.sum(arrived, axis=1)
    sums = sums + swap_cores(sums)
    return (
        mixed,
        input_grad,
        sums[expert_count],
        w_query_grad,
        w_latent_grad,
        sums[expert_count + 2, :kv_rows],
        w_kv_grad,
        w_out_grad,
        sums[expert_count + 1],
        sums[:expert_count].T,
        sgu_out,
        sdown_out,
        egu_grad[None],
        edown_grad[None],
    )


def solution(mesh):
    groups = mesh.shape["expert"]
    plan = token_plan if groups <= 16 else weight_plan
    return jax.shard_map(
        plan,
        mesh=mesh,
        in_specs=(
            P("expert", None),
            P("expert"),
            P("expert", "tensor"),
            P("expert", None),
            P("expert"),
            P("expert", "tensor"),
            P("tensor", "expert"),
            P("expert"),
            P("expert", None),
            P(None, "expert", "tensor"),
            P("tensor", "expert"),
            P("expert", None, None, "tensor"),
            P("expert", "tensor", None),
            P("expert", None),
            P("expert", None),
            P("expert", None),
        ),
        out_specs=(
            P("expert", None),
            P("expert", None),
            P("expert"),
            P("expert", "tensor"),
            P("expert", None),
            P("expert"),
            P("expert", "tensor"),
            P("tensor", "expert"),
            P("expert"),
            P("expert", None),
            P(None, "expert", "tensor"),
            P("tensor", "expert"),
            P("expert", None, None, "tensor"),
            P("expert", "tensor", None),
        ),
        check_vma=False,
    )
```

```python
import functools

import jax
import jax.numpy as jnp
from jax import lax
from jax.experimental import pallas as pl
from jax.experimental.pallas import tpu as pltpu
from jax.sharding import PartitionSpec as P

DN = 128
DR = 64
DV = 128
LANES = 128


EPSILON = 1e-06
ROUTE_SCALE = 2.446
ROPE_BASE = 50000.0
NEGATIVE = -1e30


def cut_along(value, dim, length):
    before, after = (value.shape[:dim], value.shape[dim + 1 :])
    return jnp.moveaxis(value.reshape(*before, length, -1, *after), dim, 0)


def summed_on_arrival(value, axis, dim):
    length = lax.axis_size(axis)
    tiles = lax.all_to_all(cut_along(value, dim, length), axis, 0, 0, tiled=True)
    return jnp.sum(tiles.astype(jnp.float32), axis=0)


def sent_together(arrays, axis, dim, along):
    columns = [a.reshape(*a.shape[:along], -1) for a in arrays]
    both = jnp.concatenate(columns, axis=along)
    whole, at, outs = (summed_on_arrival(both, axis, dim), 0, [])
    for a, column in zip(arrays, columns):
        slab = whole[..., at : at + column.shape[along]]
        outs.append(slab.reshape(*slab.shape[:along], *a.shape[along:]))
        at += column.shape[along]
    return tuple(outs)


def contract_rows(left_arr, right_arr):
    return lax.dot_general(
        left_arr, right_arr, (((0,), (0,)), ((), ())), preferred_element_type=jnp.float32
    )


def contract_cols(left_arr, right_arr):
    return lax.dot_general(
        left_arr, right_arr, (((1,), (1,)), ((), ())), preferred_element_type=jnp.float32
    )


def rms_forward(rows_in, gain_vec):
    inverse = lax.rsqrt(jnp.mean(rows_in * rows_in, axis=-1, keepdims=True) + EPSILON)
    return (rows_in * inverse * gain_vec, inverse)


def rms_backward(rows_in, inverse, gain_vec, grad_out):
    gain_grad = jnp.sum(grad_out * rows_in * inverse, axis=0)
    weighted = grad_out * gain_vec
    inner_mean = jnp.mean(weighted * rows_in, axis=-1, keepdims=True)
    return (inverse * weighted - rows_in * inverse * inverse * inverse * inner_mean, gain_grad)


def doc_layout(doc_lengths, row_count):
    ends_at = jnp.cumsum(doc_lengths)
    starts_at = ends_at - doc_lengths
    position = jnp.arange(row_count, dtype=jnp.int32)
    doc_ids = jnp.sum((position[:, None] >= ends_at[None, :]).astype(jnp.int32), axis=1)
    hitting = doc_ids[:, None] == jnp.arange(doc_lengths.shape[0], dtype=jnp.int32)[None, :]
    start_of = jnp.sum(jnp.where(hitting, starts_at[None, :], 0), axis=1)
    relative = position - start_of
    visible = (doc_ids[:, None] == doc_ids[None, :]) & (position[:, None] >= position[None, :])
    return (relative, visible)


def rope_tables(relative, rot_width):
    counter = jnp.arange(rot_width // 2, dtype=jnp.float32)
    frequency = ROPE_BASE ** (-2.0 * counter / rot_width)
    angles = relative.astype(jnp.float32)[:, None] * frequency[None, :]
    return (jnp.cos(angles), jnp.sin(angles))


def rotate(tensor_in, cosine, sine_tab):
    half_width = tensor_in.shape[-1] // 2
    leading = tensor_in[..., :half_width]
    trailing = tensor_in[..., half_width:]
    return jnp.concatenate(
        [leading * cosine - trailing * sine_tab, trailing * cosine + leading * sine_tab], axis=-1
    )


def unrotate(grad_in, cosine, sine_tab):
    half_width = grad_in.shape[-1] // 2
    leading = grad_in[..., :half_width]
    trailing = grad_in[..., half_width:]
    return jnp.concatenate(
        [leading * cosine + trailing * sine_tab, trailing * cosine - leading * sine_tab], axis=-1
    )


def gated_linear_backward(gate_in, up_in, grad_act):
    sigmoid_g = jax.nn.sigmoid(gate_in)
    grad_gate = grad_act * up_in * sigmoid_g * (1.0 + gate_in * (1.0 - sigmoid_g))
    return (grad_gate, grad_act * gate_in * sigmoid_g)


def slot_tables(route_rows, expert_count, capacity):
    flat_routes = route_rows.reshape(-1)
    one_hot = (flat_routes[:, None] == jnp.arange(expert_count, dtype=jnp.int32)[None, :]).astype(
        jnp.int32
    )
    ranking = jnp.sum((jnp.cumsum(one_hot, axis=0) - one_hot) * one_hot, axis=1)
    slot_ids = flat_routes * capacity + ranking
    row_total = flat_routes.shape[0]
    source = (
        jnp.zeros((expert_count * capacity,), jnp.int32)
        .at[slot_ids]
        .set(jnp.arange(row_total, dtype=jnp.int32))
    )
    filled = jnp.zeros((expert_count * capacity,), jnp.int32).at[slot_ids].set(1)
    return (slot_ids, source, filled)


def to_owner(rows_in):
    arrived = lax.all_to_all(rows_in, "expert", split_axis=0, concat_axis=1, tiled=True)
    return arrived


def weight_plan(
    inputs,
    attn_gain,
    w_query,
    w_latent,
    latent_gain,
    w_kv,
    w_out,
    ffn_gain,
    w_router,
    shared_gate_up,
    shared_down,
    expert_gate_up,
    expert_down,
    lengths,
    routes,
    cotangent,
):
    tok_rows = inputs.shape[0]
    model_width = inputs.shape[1]
    expert_count = w_router.shape[1]
    route_count = routes.shape[1]
    capacity = tok_rows * route_count * 4 // (3 * expert_count)
    brain_float16 = jnp.bfloat16
    f32 = jnp.float32
    gathered = (
        lax.all_gather(attn_gain, "expert", axis=0, tiled=True),
        lax.all_gather(w_query, "expert", axis=0, tiled=True),
        lax.all_gather(w_latent, "expert", axis=0, tiled=True),
        lax.all_gather(latent_gain, "expert", axis=0, tiled=True),
        lax.all_gather(w_kv, "expert", axis=0, tiled=True),
        lax.all_gather(w_out, "expert", axis=1, tiled=True),
        lax.all_gather(ffn_gain, "expert", axis=0, tiled=True),
        lax.all_gather(w_router, "expert", axis=0, tiled=True),
        lax.all_gather(shared_gate_up, "expert", axis=1, tiled=True),
        lax.all_gather(shared_down, "expert", axis=1, tiled=True),
    )
    gain_one, query_w, latent_w, latent_g, kv_w, out_w, gain_two, router_w, sgate_up, sdown_w = (
        gathered
    )
    local_heads = query_w.shape[1] // (DN + DR)
    rank_width = latent_g.shape[0]
    x_float = inputs.astype(f32)
    relative, visible = doc_layout(lengths[0], tok_rows)
    cosine, sine_tab = rope_tables(relative, DR)
    q_scale = (DN + DR) ** (-0.5)
    normed, scale_one = rms_forward(x_float, gain_one.astype(f32))
    normed_b = normed.astype(brain_float16)
    queries = jnp.dot(normed_b, query_w, preferred_element_type=f32).reshape(
        tok_rows, local_heads, DN + DR
    )
    q_rot = rotate(queries[..., DN:], cosine[:, None, :], sine_tab[:, None, :])
    q_all = jnp.concatenate([queries[..., :DN], q_rot], axis=-1).astype(brain_float16)
    latent = jnp.dot(normed_b, latent_w, preferred_element_type=f32)
    compressed, scale_kv = rms_forward(latent[:, :rank_width], latent_g.astype(f32))
    compressed_b = compressed.astype(brain_float16)
    k_rope = rotate(latent[:, rank_width:], cosine, sine_tab).astype(brain_float16)
    kv_all = jnp.dot(compressed_b, kv_w, preferred_element_type=f32).reshape(
        tok_rows, local_heads, DN + DV
    )
    k_nope = kv_all[..., :DN].astype(brain_float16)
    values = kv_all[..., DN:].astype(brain_float16)
    key_all = jnp.concatenate(
        [k_nope, jnp.broadcast_to(k_rope[:, None, :], (tok_rows, local_heads, DR))], axis=-1
    )

    def score_block():
        raw_scores = (
            jnp.einsum("qhd,khd->hqk", q_all, key_all, preferred_element_type=f32) * q_scale
        )
        return jnp.where(visible[None], raw_scores, NEGATIVE)

    scores = score_block()
    top_score = jnp.max(scores, axis=-1, keepdims=True)
    log_total = top_score + jnp.log(jnp.sum(jnp.exp(scores - top_score), axis=-1, keepdims=True))
    probs_b = jnp.exp(scores - log_total).astype(brain_float16)
    attended = jnp.einsum("hqk,khd->qhd", probs_b, values, preferred_element_type=f32)
    attended_b = attended.reshape(tok_rows, local_heads * DV).astype(brain_float16)
    attn = lax.psum(jnp.dot(attended_b, out_w, preferred_element_type=f32), "tensor")
    hidden = x_float + attn
    hnormed, scale_two = rms_forward(hidden, gain_two.astype(f32))
    hnormed_b = hnormed.astype(brain_float16)
    logits = jnp.dot(hnormed_b, router_w, preferred_element_type=f32)
    sigmoid_vals = jax.nn.sigmoid(logits)
    route_hot = routes[:, :, None] == jnp.arange(expert_count, dtype=jnp.int32)[None, None, :]
    chosen = jnp.sum(jnp.where(route_hot, sigmoid_vals[:, None, :], 0.0), axis=2)
    chosen_sum = jnp.sum(chosen, axis=1, keepdims=True)
    gate_vals = ROUTE_SCALE * chosen / chosen_sum
    slot_ids, source, filled = slot_tables(routes, expert_count, capacity)
    is_filled = filled[:, None] == 1
    sent_rows = jnp.where(is_filled, hnormed_b[source // route_count], 0).reshape(
        expert_count, capacity, model_width
    )
    received = to_owner(sent_rows)
    gate_up_joined = jnp.einsum(
        "erd,egdf->egrf", received, expert_gate_up, preferred_element_type=f32
    )
    expert_act = (jax.nn.silu(gate_up_joined[:, 0]) * gate_up_joined[:, 1]).astype(brain_float16)
    expert_res = jnp.einsum(
        "erf,efd->erd", expert_act, expert_down, preferred_element_type=f32
    ).astype(brain_float16)
    returned_all = lax.all_to_all(expert_res, "expert", split_axis=1, concat_axis=0, tiled=True)
    returned = returned_all.reshape(expert_count * capacity, model_width)[slot_ids].reshape(
        tok_rows, route_count, model_width
    )
    shared_gu = jnp.einsum("td,gdf->gtf", hnormed_b, sgate_up, preferred_element_type=f32)
    shared_act = (jax.nn.silu(shared_gu[0]) * shared_gu[1]).astype(brain_float16)
    branch_sum = jnp.dot(shared_act, sdown_w, preferred_element_type=f32)
    for route_idx in range(route_count):
        branch_sum = branch_sum + gate_vals[:, route_idx : route_idx + 1] * returned[
            :, route_idx
        ].astype(f32)
    moe_out = lax.psum(branch_sum.astype(jnp.bfloat16), "tensor").astype(jnp.float32)
    mixed = (hidden + moe_out).astype(brain_float16)
    grad_y = cotangent.astype(f32)
    sdown_grad = contract_rows(shared_act, cotangent)
    grad_sact = contract_cols(cotangent, sdown_w)
    grad_sgate, grad_sup = gated_linear_backward(shared_gu[0], shared_gu[1], grad_sact)
    grad_sgu = jnp.stack([grad_sgate, grad_sup], axis=0).astype(brain_float16)
    sgu_grad = jnp.einsum("td,gtf->gdf", hnormed_b, grad_sgu, preferred_element_type=f32)
    grad_hn_part = jnp.einsum("gtf,gdf->td", grad_sgu, sgate_up, preferred_element_type=f32)
    gate_columns = []
    for route_idx in range(route_count):
        gate_columns.append(jnp.sum(grad_y * returned[:, route_idx].astype(f32), axis=1))
    gate_part = jnp.stack(gate_columns, axis=1)
    slot_grads = (
        (gate_vals[:, :, None] * grad_y[:, None, :])
        .reshape(tok_rows * route_count, model_width)
        .astype(brain_float16)
    )
    grad_sent = jnp.where(is_filled, slot_grads[source], 0).reshape(
        expert_count, capacity, model_width
    )
    grad_received = to_owner(grad_sent)
    edown_grad = jnp.einsum("erf,erd->efd", expert_act, grad_received, preferred_element_type=f32)
    expert_activation_gradient = jnp.einsum(
        "erd,efd->erf", grad_received, expert_down, preferred_element_type=f32
    )
    expert_gate_gradient, expert_up_gradient = gated_linear_backward(
        gate_up_joined[:, 0], gate_up_joined[:, 1], expert_activation_gradient
    )
    expert_gate_up_gradient = jnp.stack([expert_gate_gradient, expert_up_gradient], axis=1).astype(
        brain_float16
    )
    egu_grad = jnp.einsum(
        "erd,egrf->egdf", received, expert_gate_up_gradient, preferred_element_type=f32
    )
    grad_rows = jnp.einsum(
        "egrf,egdf->erd", expert_gate_up_gradient, expert_gate_up, preferred_element_type=f32
    ).astype(brain_float16)
    grad_back = lax.all_to_all(grad_rows, "expert", split_axis=1, concat_axis=0, tiled=True)
    grad_routes = grad_back.reshape(expert_count * capacity, model_width)[slot_ids].reshape(
        tok_rows, route_count, model_width
    )
    for route_idx in range(route_count):
        grad_hn_part = grad_hn_part + grad_routes[:, route_idx].astype(f32)
    gate_grads = lax.psum(gate_part, "tensor")
    grad_chosen = ROUTE_SCALE * (
        gate_grads / chosen_sum
        - jnp.sum(gate_grads * chosen, axis=1, keepdims=True) / (chosen_sum * chosen_sum)
    )
    grad_sig = jnp.sum(jnp.where(route_hot, grad_chosen[:, :, None], 0.0), axis=1)
    grad_logits = (grad_sig * sigmoid_vals * (1.0 - sigmoid_vals)).astype(brain_float16)
    router_grad = contract_rows(hnormed_b, grad_logits)
    grad_hn = lax.psum(grad_hn_part, "tensor") + contract_cols(grad_logits, router_w)
    grad_hidden_norm, gain_two_grad = rms_backward(hidden, scale_two, gain_two.astype(f32), grad_hn)
    grad_hidden = grad_y + grad_hidden_norm
    grad_hidden_b = grad_hidden.astype(brain_float16)
    out_grad = contract_rows(attended_b, grad_hidden_b)
    grad_att = (
        contract_cols(grad_hidden_b, out_w).reshape(tok_rows, local_heads, DV).astype(brain_float16)
    )
    probs = jnp.exp(score_block() - log_total)
    probs_again = probs.astype(brain_float16)
    grad_probs = jnp.einsum("qhd,khd->hqk", grad_att, values, preferred_element_type=f32)
    grad_vals = jnp.einsum("hqk,qhd->khd", probs_again, grad_att, preferred_element_type=f32)
    row_delta = jnp.sum(probs * grad_probs, axis=-1, keepdims=True)
    grad_scores = (probs * (grad_probs - row_delta)).astype(brain_float16)
    grad_q = jnp.einsum("hqk,khd->qhd", grad_scores, key_all, preferred_element_type=f32) * q_scale
    grad_keys = jnp.einsum("hqk,qhd->khd", grad_scores, q_all, preferred_element_type=f32) * q_scale
    grad_kv = (
        jnp.concatenate([grad_keys[..., :DN], grad_vals], axis=-1)
        .reshape(tok_rows, local_heads * (DN + DV))
        .astype(brain_float16)
    )
    kv_grad = contract_rows(compressed_b, grad_kv)
    grad_comp_part = contract_cols(grad_kv, kv_w)
    grad_krope_part = jnp.sum(grad_keys[..., DN:], axis=1)
    grad_comp, grad_krope = (
        lax.psum(grad_comp_part.astype(jnp.bfloat16), "tensor").astype(jnp.float32),
        lax.psum(grad_krope_part.astype(jnp.bfloat16), "tensor").astype(jnp.float32),
    )
    grad_c, latent_gain_grad = rms_backward(
        latent[:, :rank_width], scale_kv, latent_g.astype(f32), grad_comp
    )
    grad_latent = jnp.concatenate([grad_c, unrotate(grad_krope, cosine, sine_tab)], axis=-1).astype(
        brain_float16
    )
    grad_qrot = unrotate(grad_q[..., DN:], cosine[:, None, :], sine_tab[:, None, :])
    grad_queries = (
        jnp.concatenate([grad_q[..., :DN], grad_qrot], axis=-1)
        .reshape(tok_rows, local_heads * (DN + DR))
        .astype(brain_float16)
    )
    query_grad = contract_rows(normed_b, grad_queries)
    latent_grad = contract_rows(normed_b, grad_latent)
    grad_normed = lax.psum(
        contract_cols(grad_queries, query_w).astype(jnp.bfloat16), "tensor"
    ).astype(jnp.float32) + contract_cols(grad_latent, latent_w)
    grad_x_norm, gain_one_grad = rms_backward(x_float, scale_one, gain_one.astype(f32), grad_normed)
    input_grad = grad_hidden + grad_x_norm
    first_owned = (
        *sent_together(
            (
                gain_one_grad.astype(jnp.bfloat16),
                query_grad.astype(jnp.bfloat16),
                latent_grad.astype(jnp.bfloat16),
            ),
            "expert",
            0,
            1,
        ),
        *sent_together(
            (latent_gain_grad.astype(jnp.bfloat16), kv_grad.astype(jnp.bfloat16)), "expert", 0, 1
        ),
    )
    second_owned = (
        lax.psum_scatter(out_grad, "expert", scatter_dimension=1, tiled=True),
        lax.psum_scatter(gain_two_grad, "expert", scatter_dimension=0, tiled=True),
        lax.psum_scatter(router_grad, "expert", scatter_dimension=0, tiled=True),
        lax.psum_scatter(sgu_grad, "expert", scatter_dimension=1, tiled=True),
        lax.psum_scatter(sdown_grad, "expert", scatter_dimension=1, tiled=True),
    )
    return (
        mixed,
        input_grad,
        first_owned[0],
        first_owned[1],
        first_owned[2],
        first_owned[3],
        first_owned[4],
        second_owned[0],
        second_owned[1],
        second_owned[2],
        second_owned[3],
        second_owned[4],
        egu_grad,
        edown_grad,
    )


def swap_cores(value):
    return lax.ppermute(value, "tensor", [(0, 1), (1, 0)])


def take_rows(value, start, count, axis=0):
    return lax.dynamic_slice_in_dim(value, start, count, axis=axis)


def in_order(core, own, other, axis=0):
    return jnp.where(
        core == 0,
        jnp.concatenate([own, other], axis=axis),
        jnp.concatenate([other, own], axis=axis),
    )


def add_wide(*parts):
    total = parts[0].astype(jnp.float32)
    for part in parts[1:]:
        total = total + part.astype(jnp.float32)
    return total


PLANE = 4


def to_partner(value, flips):
    groups = lax.axis_size("expert")
    return lax.ppermute(value, "expert", [(g, g ^ flips) for g in range(groups)])


def to_deeper(value, step):
    groups = lax.axis_size("expert")
    pairs = [(g, (g + step * PLANE) % groups) for g in range(groups)]
    return lax.ppermute(value, "expert", pairs)


def plane_gather(value):
    return [value] + [to_partner(value, r) for r in range(1, PLANE)]


def plane_scatter(parts):
    return add_wide(parts[0], *[to_partner(parts[r], r) for r in range(1, PLANE)])


def by_place(parts, place):
    odd, high = place % 2 == 1, place // 2 == 1
    parts = [jnp.where(odd, parts[i ^ 1], parts[i]) for i in range(PLANE)]
    return [jnp.where(high, parts[i ^ 2], parts[i]) for i in range(PLANE)]


def tie(*values):
    return lax.optimization_barrier(values)


def deep_pieces(value):
    deep = lax.axis_size("expert") // PLANE
    return [to_deeper(value, s) for s in range(1, deep)]


def deep_join(value, pieces, z):
    deep = lax.axis_size("expert") // PLANE
    whole = jnp.zeros((deep, *value.shape), value.dtype)
    whole = lax.dynamic_update_index_in_dim(whole, value, z, 0)
    for step in range(1, deep):
        whole = lax.dynamic_update_index_in_dim(whole, pieces[step - 1], (z - step) % deep, 0)
    return whole


def deep_scatter(blocks, z):
    deep = blocks.shape[0]

    def block(index):
        return lax.dynamic_index_in_dim(blocks, index, 0, keepdims=False)

    return add_wide(
        block(z), *[to_deeper(block((z + step) % deep), step) for step in range(1, deep)]
    )


def sum_planes(grad, z):
    deep = lax.axis_size("expert") // PLANE
    rows = deep_scatter(grad.astype(jnp.bfloat16).reshape(deep, -1, grad.shape[1]), z)
    return rows.astype(jnp.bfloat16).reshape(PLANE, -1, grad.shape[1])


def share_columns(rows, place):
    parts = [at_index(rows, 0, place)]
    for r in range(1, PLANE):
        parts.append(to_partner(at_index(rows, 0, place ^ r), r))
    return by_place(parts, place)


def all_groups(value):
    return lax.all_gather(value, "expert", axis=0, tiled=False)


def at_index(value, axis, index):
    return lax.dynamic_index_in_dim(value, index, axis, keepdims=False)


class PlaneSum:
    def __init__(self, *terms):
        groups, rows = terms[0].shape[:2]
        me = lax.axis_index("expert")
        self.type = terms[0].dtype
        near, far = me % 2, me // 2 % 2
        cut = rows // 2
        blocks = [v.reshape(groups // PLANE, 2, 2, *v.shape[1:]) for v in terms]
        self.first = [v[:, :, :, :cut] for v in blocks], far, near, 2, 1
        self.second = [jnp.swapaxes(v[:, :, :, cut:], 1, 2) for v in blocks], near, far, 1, 2

    def sends(self):
        return [self._add(at_index(v, 1, 1 - one) for v in held) for held, one, *_ in self._halves()]

    def _halves(self):
        return self.first, self.second

    def _add(self, parts):
        return add_wide(*parts).astype(self.type)

    def move(self, sends):
        return [to_partner(v, half[3]) for v, half in zip(sends, self._halves())]

    def sends_again(self, came):
        return [
            self._add(
                [at_index(at_index(v, 1, one), 1, 1 - two) for v in held]
                + [at_index(c, 1, 1 - two)]
            )
            for c, (held, one, two, *_) in zip(came, self._halves())
        ]

    def move_again(self, sends):
        return [to_partner(v, half[4]) for v, half in zip(sends, self._halves())]

    def line(self, came, came_again):
        sums = [
            self._add(
                [at_index(at_index(v, 1, one), 1, two) for v in held] + [at_index(c, 1, two), d]
            )
            for c, d, (held, one, two, *_) in zip(came, came_again, self._halves())
        ]
        return jnp.concatenate(sums, axis=1)


def deep_sends(line, z):
    deep = line.shape[0]
    return [at_index(line, 0, (z + step) % deep) for step in range(deep)]


def deep_move(sends):
    return [sends[0]] + [to_deeper(v, step) for step, v in enumerate(sends) if step > 0]


def dot_nn(left, right):
    return lax.dot_general(left, right, (((1,), (0,)), ((), ())), preferred_element_type=jnp.float32)


def dot_nt(left, right):
    return lax.dot_general(left, right, (((1,), (1,)), ((), ())), preferred_element_type=jnp.float32)


def dot_tn(left, right):
    return lax.dot_general(left, right, (((0,), (0,)), ((), ())), preferred_element_type=jnp.float32)


def two_lanes(column, lane):
    high = column.astype(jnp.bfloat16).astype(jnp.float32)
    spread = jnp.where(lane == 0, high, jnp.where(lane == 1, column - high, 0.0))
    return spread.astype(jnp.bfloat16)


def expert_kernel(
    shared_cols,
    expert_count,
    me_ref,
    hn_own,
    hn_other,
    dy_own,
    dy_other,
    meta_own,
    meta_other,
    gate_up_w,
    down_w,
    first_w,
    sdown_w,
    slots_out,
    slot_dy_out,
    act_out,
    d_gate_up_out,
    rows_own_out,
    rows_other_out,
    sact_own_out,
    sact_other_out,
    dsh_own_out,
    dsh_other_out,
    dgate_own_out,
    dgate_other_out,
):
    f32, bf16 = jnp.float32, jnp.bfloat16
    count, half, _ = hn_own.shape
    tokens = 2 * half
    me = me_ref[0]
    lane = lax.broadcasted_iota(jnp.int32, (tokens, LANES), 1)
    is_router = (lane >= shared_cols) & (lane < shared_cols + expert_count)
    first = first_w[...]
    slots, slot_dys, slot_gates, picks, dshs = [], [], [], [], []
    for i in range(count):
        rows = jnp.concatenate([hn_own[i], hn_other[i]], axis=0)
        rows_dy = jnp.concatenate([dy_own[i], dy_other[i]], axis=0)
        meta = jnp.concatenate([meta_own[i], meta_other[i]], axis=0)
        products = dot_nn(rows, first)
        gate, up = products[:, :LANES], products[:, LANES:]
        sig = jax.nn.sigmoid(gate)
        total = jnp.sum(jnp.where(is_router, sig * meta, 0.0), axis=1, keepdims=True)
        mine = jnp.sum(jnp.where(lane == shared_cols + me, sig, 0.0), axis=1, keepdims=True)
        token_gate = ROUTE_SCALE * mine / total
        sact = (gate * sig * up).astype(bf16)
        sact_own_out[i], sact_other_out[i] = sact[:half], sact[half:]
        d_sact = dot_nt(rows_dy, sdown_w[...])
        d_sgate = d_sact * up * sig * (1.0 + gate * (1.0 - sig))
        dsh = jnp.concatenate([d_sgate, d_sact * gate * sig], axis=1).astype(bf16)
        dsh_own_out[i], dsh_other_out[i] = dsh[:half], dsh[half:]
        dshs.append(dsh)
        pick = (meta[:, :1] == lane.astype(f32)).astype(bf16)
        picks.append(pick)
        slots.append(dot_tn(pick, rows).astype(bf16))
        slot_dys.append(dot_tn(pick, rows_dy).astype(bf16))
        slot_gates.append(
            jnp.sum(dot_tn(pick, two_lanes(token_gate, lane)), axis=1, keepdims=True)
        )
    slot_rows = jnp.concatenate(slots, axis=0)
    slot_dy = jnp.concatenate(slot_dys, axis=0)
    slot_gate = jnp.concatenate(slot_gates, axis=0)
    slots_out[...] = slot_rows
    slot_dy_out[...] = slot_dy
    gate = dot_nt(slot_rows, gate_up_w[0])
    up = dot_nt(slot_rows, gate_up_w[1])
    d_act = dot_nt(slot_dy, down_w[...])
    sig = jax.nn.sigmoid(gate)
    silu = gate * sig
    act = silu * up
    slot_dgate = jnp.sum(act * d_act, axis=1, keepdims=True)
    act_out[...] = (slot_gate * act).astype(bf16)
    d_act = slot_gate * d_act
    d_gate = (d_act * up * sig * (1.0 + gate * (1.0 - sig))).astype(bf16)
    d_up = (d_act * silu).astype(bf16)
    d_gate_up_out[0] = d_gate
    d_gate_up_out[1] = d_up
    d_slots = (dot_nn(d_gate, gate_up_w[0]) + dot_nn(d_up, gate_up_w[1])).astype(bf16)
    slot_lane = lax.broadcasted_iota(jnp.int32, (LANES, LANES), 1)
    for i in range(count):
        here = slice(i * LANES, (i + 1) * LANES)
        d_rows = (dot_nn(picks[i], d_slots[here]) + dot_nt(dshs[i], first)).astype(bf16)
        rows_own_out[i], rows_other_out[i] = d_rows[:half], d_rows[half:]
        dgate = dot_nn(picks[i], two_lanes(slot_dgate[here], slot_lane))
        dgate_own_out[i], dgate_other_out[i] = dgate[:half], dgate[half:]


def block_specs(per_step):
    def lead(*tail):
        return pl.BlockSpec((per_step, *tail), lambda i: (i,) + (0,) * len(tail))

    def flat(cols):
        return pl.BlockSpec((per_step * LANES, cols), lambda i: (i, 0))

    def whole(a):
        return pl.BlockSpec(a.shape, lambda i: (0,) * a.ndim, pipeline_mode=pl.Buffered(1))

    return lead, flat, whole


def slots_cost(width, hidden, products):
    return LANES * width * hidden * products


def experts(
    me,
    hn_own,
    hn_other,
    dy_own,
    dy_other,
    meta_own,
    meta_other,
    gate_up_w,
    down_w,
    first_w,
    sdown_w,
    shared_cols,
    expert_count,
    per_step=2,
):
    groups, half, width = hn_own.shape
    hidden = down_w.shape[0]
    slots = groups * LANES
    f32, bf16 = jnp.float32, jnp.bfloat16
    lead, flat, whole = block_specs(per_step)
    sds = jax.ShapeDtypeStruct
    rows_cost = 2 * groups * (2 * half * width * 4 * LANES + slots_cost(width, hidden, 5))
    return pl.pallas_call(
        functools.partial(expert_kernel, shared_cols, expert_count),
        grid=(groups // per_step,),
        in_specs=[
            pl.BlockSpec(memory_space=pltpu.SMEM),
            *[lead(half, width)] * 4,
            *[lead(half, LANES)] * 2,
            *[whole(a) for a in (gate_up_w, down_w, first_w, sdown_w)],
        ],
        out_specs=[
            flat(width),
            flat(width),
            flat(hidden),
            pl.BlockSpec((2, per_step * LANES, hidden), lambda i: (0, i, 0)),
            *[lead(half, width)] * 2,
            *[lead(half, LANES)] * 2,
            *[lead(half, 2 * LANES)] * 2,
            *[lead(half, LANES)] * 2,
        ],
        out_shape=[
            sds((slots, width), bf16),
            sds((slots, width), bf16),
            sds((slots, hidden), bf16),
            sds((2, slots, hidden), bf16),
            *[sds((groups, half, width), bf16)] * 2,
            *[sds((groups, half, LANES), bf16)] * 2,
            *[sds((groups, half, 2 * LANES), bf16)] * 2,
            *[sds((groups, half, LANES), f32)] * 2,
        ],
        compiler_params=pltpu.CompilerParams(vmem_limit_bytes=58 * 1024 * 1024),
        cost_estimate=pl.CostEstimate(
            flops=rows_cost, bytes_accessed=20 * groups * half * width, transcendentals=0
        ),
    )(
        me,
        hn_own,
        hn_other,
        dy_own,
        dy_other,
        meta_own,
        meta_other,
        gate_up_w,
        down_w,
        first_w,
        sdown_w,
    )


def output_kernel(act, sact_own, sact_other, meta_own, meta_other, down_w, sdown_w, own_out, other_out):
    f32, bf16 = jnp.float32, jnp.bfloat16
    count, half, _ = meta_own.shape
    lane = lax.broadcasted_iota(jnp.int32, (2 * half, LANES), 1).astype(f32)
    out = dot_nn(act[...], down_w[...]).astype(bf16)
    for i in range(count):
        meta = jnp.concatenate([meta_own[i], meta_other[i]], axis=0)
        pick = (meta[:, :1] == lane).astype(bf16)
        sact = jnp.concatenate([sact_own[i], sact_other[i]], axis=0)
        here = slice(i * LANES, (i + 1) * LANES)
        rows = (dot_nn(pick, out[here]) + dot_nn(sact, sdown_w[...])).astype(bf16)
        own_out[i], other_out[i] = rows[:half], rows[half:]


def outputs(act, sact_own, sact_other, meta_own, meta_other, down_w, sdown_w, per_step=4):
    groups, half, _ = meta_own.shape
    hidden, width = down_w.shape
    lead, flat, whole = block_specs(per_step)
    return pl.pallas_call(
        output_kernel,
        grid=(groups // per_step,),
        in_specs=[
            flat(hidden),
            *[lead(half, LANES)] * 4,
            *[whole(a) for a in (down_w, sdown_w)],
        ],
        out_specs=[lead(half, width)] * 2,
        out_shape=[jax.ShapeDtypeStruct((groups, half, width), jnp.bfloat16)] * 2,
        compiler_params=pltpu.CompilerParams(vmem_limit_bytes=58 * 1024 * 1024),
        cost_estimate=pl.CostEstimate(
            flops=2 * groups * (4 * half * LANES * width + slots_cost(width, hidden, 1)),
            bytes_accessed=5 * groups * half * width,
            transcendentals=0,
        ),
    )(act, sact_own, sact_other, meta_own, meta_other, down_w, sdown_w)


def token_plan(
    inputs,
    attn_gain,
    w_query,
    w_latent,
    latent_gain,
    w_kv,
    w_out,
    ffn_gain,
    w_router,
    shared_gate_up,
    shared_down,
    expert_gate_up,
    expert_down,
    lengths,
    routes,
    cotangent,
):
    f32, bf16 = jnp.float32, jnp.bfloat16
    core, me = lax.axis_index("tensor"), lax.axis_index("expert")
    groups = lax.axis_size("expert")
    deep, place, z = groups // PLANE, me % PLANE, me // PLANE
    tok_rows, width = inputs.shape
    half = tok_rows // 2
    own_at, other_at = core * half, (1 - core) * half
    expert_count = w_router.shape[1]
    route_count = routes.shape[1]
    capacity = tok_rows * route_count * 4 // (3 * expert_count)
    shared_cols = shared_gate_up.shape[2] // groups
    latent_cols, rank_width = w_latent.shape[1], latent_gain.shape[0] * groups
    block_rows = w_query.shape[0]
    kv_rows = w_kv.shape[0]

    query_cols = w_query.shape[1] // PLANE
    out_cols = w_out.shape[0] // PLANE
    used = latent_cols + expert_count + 3
    small = jnp.concatenate(
        [
            w_latent,
            w_router,
            attn_gain[:, None],
            ffn_gain[:, None],
            jnp.pad(latent_gain, (0, block_rows - kv_rows))[:, None],
            jnp.zeros((block_rows, -used % 128), bf16),
        ],
        axis=1,
    )
    small_cols = small.shape[1]
    route_half = take_rows(routes, own_at, half).astype(bf16).reshape(block_rows // 2, -1)
    small_half = jnp.concatenate(
        [
            take_rows(small, core * (block_rows // 2), block_rows // 2),
            jnp.pad(route_half, ((0, 0), (0, -route_half.shape[1] % 128))),
        ],
        axis=1,
    )
    packed_cols = small_half.shape[1] // 2
    small_packed = jnp.concatenate([small_half[:, :packed_cols], small_half[:, packed_cols:]])
    kv_cols = w_kv.shape[1] // PLANE
    kv_parts = block_rows // kv_rows
    kv_piece = kv_cols // kv_parts
    w_out_t = w_out.T

    def quarter(index):
        kv_here = take_rows(w_kv, index * kv_cols, kv_cols, axis=1)
        kv_here = [kv_here[:, p * kv_piece : (p + 1) * kv_piece] for p in range(kv_parts)]
        return jnp.concatenate(
            [
                take_rows(w_query, index * query_cols, query_cols, axis=1),
                take_rows(w_out_t, index * out_cols, out_cols, axis=1),
                jnp.concatenate(kv_here, axis=0),
            ],
            axis=1,
        )

    near_w = [quarter(place)] + [to_partner(quarter(place ^ r), r) for r in range(1, PLANE)]
    small_line = deep_join(small_packed, deep_pieces(small_packed), z)
    near_w, small_line = tie(near_w, small_line)
    plane_w = jnp.stack(by_place(near_w, place))
    x_half, lengths_here, small_line = tie(
        take_rows(inputs, own_at, half), lengths[0], small_line
    )
    deep_w = deep_pieces(plane_w)
    small_parts = plane_gather(small_line)
    lengths_near = jnp.stack(plane_gather(lengths_here))
    x_near_own = jnp.stack(plane_gather(x_half))
    x_near = in_order(core, x_near_own, swap_cores(x_near_own), axis=1)
    x_near = lax.optimization_barrier(x_near.reshape(PLANE * tok_rows, width))
    small_own = jnp.stack(by_place(small_parts, place), axis=1)
    small_own = small_own.reshape(groups, block_rows, packed_cols)
    small_own = jnp.concatenate(
        [small_own[:, : block_rows // 2], small_own[:, block_rows // 2 :]], axis=2
    )
    small_other = swap_cores(small_own)
    small_all = in_order(core, small_own, small_other, axis=1)
    head_w = deep_join(plane_w, deep_w, z)
    shared_gate_up, shared_down, dy_sent, head_w = tie(
        shared_gate_up, shared_down, take_rows(cotangent, own_at, half), head_w
    )
    dy_own_rows = take_rows(cotangent, own_at, half)
    dy_own = all_groups(dy_sent)
    sgu_w = lax.all_to_all(shared_gate_up, "expert", split_axis=2, concat_axis=1, tiled=True)
    sdown_w = lax.all_to_all(shared_down, "expert", split_axis=0, concat_axis=1, tiled=True)
    head_w = head_w.reshape(groups, block_rows, -1)
    flat_head = head_w.reshape(groups * block_rows, -1)
    query_w = flat_head[:, :query_cols]
    at = query_cols + out_cols
    out_wt = flat_head[:, query_cols:at]
    kv_w = head_w[:, :, at : at + kv_piece].reshape(groups, kv_parts, kv_rows, kv_piece)
    kv_w = kv_w.transpose(0, 2, 1, 3).reshape(groups * kv_rows, kv_cols)

    def routes_of(came):
        came = came[:, :, small_cols : small_cols + route_half.shape[1]]
        return came.astype(jnp.int32).reshape(groups, half, route_count)

    routes_own, routes_other = routes_of(small_own), routes_of(small_other)
    flat_small = small_all.reshape(groups * block_rows, -1)
    latent_w = flat_small[:, :latent_cols]
    at = latent_cols
    router_w = flat_small[:, at : at + expert_count]
    at += expert_count
    gain_one, gain_two = flat_small[:, at], flat_small[:, at + 1]
    latent_g = small_all[:, :kv_rows, at + 2].reshape(-1)

    near_rows = PLANE * tok_rows
    local_heads = query_cols // (DN + DR)
    x_float = x_near.astype(f32)
    relative, visible = jax.vmap(lambda one: doc_layout(one, tok_rows))(lengths_near)
    cosine, sine_tab = rope_tables(relative.reshape(-1), DR)
    q_scale = (DN + DR) ** (-0.5)
    scale_one = lax.rsqrt(jnp.mean(x_float * x_float, axis=-1, keepdims=True) + EPSILON)
    scale_one = lax.optimization_barrier(scale_one)
    normed_b = (x_near.astype(f32) * scale_one * gain_one.astype(f32)).astype(bf16)
    normed_b = lax.optimization_barrier(normed_b)
    queries = jnp.dot(normed_b, query_w, preferred_element_type=f32).reshape(
        near_rows, local_heads, DN + DR
    )
    q_rot = rotate(queries[..., DN:], cosine[:, None, :], sine_tab[:, None, :])
    q_all = jnp.concatenate([queries[..., :DN], q_rot], axis=-1).astype(bf16)
    q_all = q_all.reshape(PLANE, tok_rows, local_heads, DN + DR)
    latent = jnp.dot(normed_b, latent_w, preferred_element_type=f32)
    compressed, _ = rms_forward(latent[:, :rank_width], latent_g.astype(f32))
    compressed_b = compressed.astype(bf16)
    k_rope = rotate(latent[:, rank_width:], cosine, sine_tab).astype(bf16)
    kv_all = jnp.dot(compressed_b, kv_w, preferred_element_type=f32).reshape(
        PLANE, tok_rows, local_heads, DN + DV
    )
    k_nope = kv_all[..., :DN].astype(bf16)
    values = kv_all[..., DN:].astype(bf16)
    k_rope = k_rope.reshape(PLANE, tok_rows, 1, DR)
    key_all = jnp.concatenate(
        [k_nope, jnp.broadcast_to(k_rope, (PLANE, tok_rows, local_heads, DR))], axis=-1
    )

    def score_block():
        raw_scores = (
            jnp.einsum("gqhd,gkhd->ghqk", q_all, key_all, preferred_element_type=f32) * q_scale
        )
        return jnp.where(visible[:, None], raw_scores, NEGATIVE)

    scores = score_block()
    top_score = jnp.max(scores, axis=-1, keepdims=True)
    log_total = top_score + jnp.log(jnp.sum(jnp.exp(scores - top_score), axis=-1, keepdims=True))
    probs_b = jnp.exp(scores - log_total).astype(bf16)
    attended = jnp.einsum("ghqk,gkhd->gqhd", probs_b, values, preferred_element_type=f32)
    attended_b = attended.reshape(near_rows, local_heads * DV).astype(bf16)

    def sum_heads(part):
        part = part.astype(bf16).reshape(PLANE, tok_rows, -1)
        came = swap_cores(take_rows(part, other_at, half, axis=1))
        both = add_wide(take_rows(part, own_at, half, axis=1), came).astype(bf16)
        return plane_scatter([both[r] for r in range(PLANE)])

    attn_own = sum_heads(contract_cols(attended_b, out_wt))
    x_own = take_rows(inputs, own_at, half).astype(f32)
    hidden = x_own + attn_own
    hnormed, scale_two = rms_forward(hidden, gain_two.astype(f32))
    hnormed_b = hnormed.astype(bf16)
    hnormed_b, dy_own, sgu_w, sdown_w = tie(hnormed_b, dy_own, sgu_w, sdown_w)
    dy_other = swap_cores(dy_own)

    hn_own = all_groups(hnormed_b)
    hn_other = swap_cores(hn_own)

    def membership(named):
        one_hot = named[..., None] == jnp.arange(expert_count, dtype=jnp.int32)
        return jnp.any(named == me, axis=-1), jnp.any(one_hot, axis=2)

    member_own, hot_own = membership(routes_own)
    member_other, hot_other = membership(routes_other)
    lower = (
        jnp.arange(half, dtype=jnp.int32)[:, None] <= jnp.arange(half, dtype=jnp.int32)[None, :]
    ).astype(bf16)

    def running(mask):
        counts = jnp.dot(mask.astype(bf16), lower, preferred_element_type=f32)
        return counts.astype(jnp.int32)

    count_own, count_other = running(member_own), running(member_other)
    place_own = jnp.where(member_own, count_own - 1, -1)
    place_other = jnp.where(member_other, count_own[:, -1:] + count_other - 1, -1)

    def metadata(slot, hot):
        return jnp.concatenate(
            [
                slot[..., None].astype(f32),
                jnp.zeros((groups, half, shared_cols - 1), f32),
                hot.astype(f32),
                jnp.zeros((groups, half, LANES - shared_cols - expert_count), f32),
            ],
            axis=-1,
        )

    meta_own, meta_other = metadata(place_own, hot_own), metadata(place_other, hot_other)
    first_w = jnp.concatenate(
        [
            jnp.pad(
                jnp.concatenate([sgu_w[0], router_w], axis=1),
                ((0, 0), (0, LANES - shared_cols - expert_count)),
            ),
            jnp.pad(sgu_w[1], ((0, 0), (0, LANES - shared_cols))),
        ],
        axis=1,
    )
    sdown_rows = jnp.pad(sdown_w, ((0, LANES - shared_cols), (0, 0)))
    gate_up_w, down_w = jnp.swapaxes(expert_gate_up[0], 1, 2), expert_down[0]
    (
        slot_rows,
        slot_dy,
        slot_act,
        d_gate_up,
        d_rows_own,
        d_rows_other,
        act_own,
        act_other,
        d_shared_own,
        d_shared_other,
        dgate_own,
        dgate_other,
    ) = experts(
        me.reshape(1).astype(jnp.int32),
        hn_own,
        hn_other,
        dy_own,
        dy_other,
        meta_own,
        meta_other,
        gate_up_w,
        down_w,
        first_w,
        sdown_rows,
        shared_cols,
        expert_count,
    )
    d_rows_came = swap_cores(d_rows_other)

    def two_parts(value):
        return value[..., 0] + value[..., 1]

    def flat_rows(value):
        return value.reshape(groups * half, -1)

    sgu_grad = contract_rows(flat_rows(hn_own), flat_rows(d_shared_own)) + contract_rows(
        flat_rows(hn_other), flat_rows(d_shared_other)
    )
    sdown_grad = contract_rows(flat_rows(act_own), flat_rows(dy_own)) + contract_rows(
        flat_rows(act_other), flat_rows(dy_other)
    )
    sdown_sent = sdown_grad[:shared_cols].astype(bf16)
    sgu_sent = jnp.stack(
        [sgu_grad[:, :shared_cols], sgu_grad[:, LANES : LANES + shared_cols]]
    ).astype(bf16)
    dgate_sent = two_parts(dgate_own) + swap_cores(two_parts(dgate_other))
    d_rows_came, sgu_sent, sdown_sent, dgate_sent = tie(
        d_rows_came, sgu_sent, sdown_sent, dgate_sent
    )
    d_sum = PlaneSum(d_rows_own, d_rows_came)
    sends, sgu_sent, sdown_sent, dgate_sent, slot_act = tie(
        d_sum.sends(), sgu_sent, sdown_sent, dgate_sent, slot_act
    )
    came = d_sum.move(sends)
    dgate = lax.all_to_all(dgate_sent, "expert", split_axis=0, concat_axis=0, tiled=True).T
    sgu_out = lax.all_to_all(sgu_sent, "expert", split_axis=1, concat_axis=2, tiled=True)
    sdown_out = lax.all_to_all(sdown_sent, "expert", split_axis=1, concat_axis=0, tiled=True)
    out_own, out_other = outputs(
        slot_act, act_own, act_other, meta_own, meta_other, down_w, sdown_rows
    )
    out_came = swap_cores(out_other)
    edown_grad = contract_rows(slot_act, slot_dy)
    came, out_came, edown_grad = tie(came, out_came, edown_grad)
    sends, slot_rows, out_came = tie(d_sum.sends_again(came), slot_rows, out_came)
    came_again = d_sum.move_again(sends)
    egu_grad = jnp.einsum("sd,gsf->gdf", slot_rows, d_gate_up, preferred_element_type=f32)
    out_sum = PlaneSum(out_own, out_came)
    out_sends = out_sum.sends()
    came_again, egu_grad, out_sends = tie(came_again, egu_grad, out_sends)
    z_sends, out_sends, dgate = tie(
        deep_sends(d_sum.line(came, came_again), z), out_sends, dgate
    )
    z_came = deep_move(z_sends)
    out_first = out_sum.move(out_sends)
    hot_mine = take_rows(
        jnp.any(routes[..., None] == jnp.arange(expert_count, dtype=jnp.int32), axis=1), own_at, half
    )
    sig = jax.nn.sigmoid(jnp.dot(hnormed_b, router_w, preferred_element_type=f32))
    chosen = jnp.where(hot_mine, sig, 0.0)
    chosen_sum = jnp.sum(chosen, axis=1, keepdims=True)
    dgate = jnp.where(hot_mine, dgate, 0.0)
    inner = jnp.sum(dgate * chosen, axis=1, keepdims=True)
    d_chosen = ROUTE_SCALE * (dgate / chosen_sum - inner / (chosen_sum * chosen_sum))
    d_logits = (jnp.where(hot_mine, d_chosen, 0.0) * sig * (1.0 - sig)).astype(bf16)
    router_grad = contract_rows(d_logits, hnormed_b)
    z_came, d_logits, router_grad = tie(z_came, d_logits, router_grad)
    d_hn = add_wide(*z_came)
    d_hn = d_hn + contract_cols(d_logits, router_w)
    d_hidden_norm, gain_two_grad = rms_backward(hidden, scale_two, gain_two.astype(f32), d_hn)
    d_hidden = dy_own_rows.astype(f32) + d_hidden_norm
    d_parts, out_first = tie(plane_gather(d_hidden.astype(bf16)), out_first)
    d_near_own = jnp.stack(d_parts)
    d_near = in_order(core, d_near_own, swap_cores(d_near_own), axis=1).reshape(near_rows, width)

    out_sends, d_near = tie(out_sum.sends_again(out_first), d_near)
    out_second = out_sum.move_again(out_sends)

    grad_att = (
        jnp.dot(d_near, out_wt, preferred_element_type=f32)
        .reshape(PLANE, tok_rows, local_heads, DV)
        .astype(bf16)
    )
    out_grad = contract_rows(d_near, attended_b).astype(bf16)
    out_grad, grad_att = tie(out_grad, grad_att)
    out_sums = sum_planes(out_grad, z)
    probs = jnp.exp(score_block() - log_total)
    probs_again = probs.astype(bf16)
    grad_probs = jnp.einsum("gqhd,gkhd->ghqk", grad_att, values, preferred_element_type=f32)
    grad_vals = jnp.einsum("ghqk,gqhd->gkhd", probs_again, grad_att, preferred_element_type=f32)
    row_delta = jnp.sum(probs * grad_probs, axis=-1, keepdims=True)
    grad_scores = (probs * (grad_probs - row_delta)).astype(bf16)
    grad_q = (
        jnp.einsum("ghqk,gkhd->gqhd", grad_scores, key_all, preferred_element_type=f32) * q_scale
    ).reshape(near_rows, local_heads, DN + DR)
    grad_keys = (
        jnp.einsum("ghqk,gqhd->gkhd", grad_scores, q_all, preferred_element_type=f32) * q_scale
    )
    grad_kv = (
        jnp.concatenate([grad_keys[..., :DN], grad_vals], axis=-1)
        .reshape(near_rows, local_heads * (DN + DV))
        .astype(bf16)
    )
    grad_latent_part = jnp.concatenate(
        [
            contract_cols(grad_kv, kv_w),
            jnp.sum(grad_keys[..., DN:], axis=2).reshape(near_rows, DR),
        ],
        axis=1,
    )
    grad_both = sum_heads(grad_latent_part)
    latent_own = take_rows(latent[:tok_rows], own_at, half)
    cosine_own = take_rows(cosine[:tok_rows], own_at, half)
    sine_own = take_rows(sine_tab[:tok_rows], own_at, half)
    _, scale_kv = rms_forward(latent_own[:, :rank_width], latent_g.astype(f32))
    grad_c, latent_gain_grad = rms_backward(
        latent_own[:, :rank_width], scale_kv, latent_g.astype(f32), grad_both[:, :rank_width]
    )
    grad_latent = jnp.concatenate(
        [grad_c, unrotate(grad_both[:, rank_width:], cosine_own, sine_own)], axis=-1
    ).astype(bf16)
    grad_qrot = unrotate(grad_q[..., DN:], cosine[:, None, :], sine_tab[:, None, :])
    grad_queries = (
        jnp.concatenate([grad_q[..., :DN], grad_qrot], axis=-1)
        .reshape(near_rows, local_heads * (DN + DR))
        .astype(bf16)
    )
    out_second, grad_kv, grad_queries = tie(out_second, grad_kv, grad_queries)
    out_z, grad_kv, grad_queries = tie(
        deep_sends(out_sum.line(out_first, out_second), z), grad_kv, grad_queries
    )
    out_z = deep_move(out_z)
    kv_grad = contract_rows(compressed_b, grad_kv).astype(bf16)
    kv_grad = kv_grad.reshape(groups, kv_rows, kv_parts, kv_piece).transpose(0, 2, 1, 3)
    query_grad = contract_rows(normed_b, grad_queries).astype(bf16)
    first_sums = sum_planes(
        jnp.concatenate([query_grad, kv_grad.reshape(-1, kv_piece)], axis=1), z
    )
    shared_out = share_columns(jnp.concatenate([first_sums, out_sums], axis=2), place)
    at_kv, at_out = query_cols, query_cols + kv_piece
    w_query_grad = jnp.concatenate([p[:, :at_kv] for p in shared_out], axis=1).astype(f32)
    w_kv_grad = jnp.concatenate(
        [
            p[q * kv_rows : (q + 1) * kv_rows, at_kv:at_out]
            for p in shared_out
            for q in range(kv_parts)
        ],
        axis=1,
    ).astype(f32)
    w_out_grad = jnp.concatenate([p[:, at_out:] for p in shared_out], axis=1).astype(f32).T
    grad_normed = sum_heads(contract_cols(grad_queries, query_w))
    grad_normed = grad_normed + contract_cols(grad_latent, latent_w)
    moe_own = add_wide(*out_z)
    mixed_own = (hidden + moe_own).astype(bf16)
    mixed = in_order(core, mixed_own, swap_cores(mixed_own))

    _, scale_own = rms_forward(x_own, gain_one.astype(f32))
    grad_x_norm, gain_one_grad = rms_backward(x_own, scale_own, gain_one.astype(f32), grad_normed)
    input_own = d_hidden + grad_x_norm
    input_grad = in_order(core, input_own, swap_cores(input_own))

    latent_near_own = jnp.stack(plane_gather(grad_latent))
    latent_near = in_order(core, latent_near_own, swap_cores(latent_near_own), axis=1)
    normed_cols = normed_b.reshape(near_rows, deep, PLANE * block_rows)
    normed_cols = take_rows(normed_cols, place * block_rows, block_rows, axis=2)
    latent_cut = latent_cols // 2
    latent_near = latent_near.reshape(near_rows, latent_cols)
    latent_blocks = contract_rows(
        normed_cols.reshape(near_rows, -1),
        take_rows(latent_near, core * latent_cut, latent_cut, axis=1),
    )
    latent_half = deep_scatter(latent_blocks.astype(bf16).reshape(deep, -1, latent_cut), z)
    w_latent_grad = in_order(core, latent_half, swap_cores(latent_half), axis=1)

    gain_lanes = jnp.pad(
        latent_gain_grad.reshape(groups, kv_rows), ((0, 0), (0, block_rows - kv_rows))
    )
    vectors = jnp.concatenate(
        [
            router_grad,
            gain_one_grad[None],
            gain_two_grad[None],
            gain_lanes.reshape(1, -1),
        ],
        axis=0,
    ).reshape(-1, groups, block_rows)
    arrived = lax.all_to_all(vectors, "expert", split_axis=1, concat_axis=1, tiled=True)
    sums = jnp.sum(arrived, axis=1)
    sums = sums + swap_cores(sums)
    return (
        mixed,
        input_grad,
        sums[expert_count],
        w_query_grad,
        w_latent_grad,
        sums[expert_count + 2, :kv_rows],
        w_kv_grad,
        w_out_grad,
        sums[expert_count + 1],
        sums[:expert_count].T,
        sgu_out.astype(f32),
        sdown_out.astype(f32),
        egu_grad[None],
        edown_grad[None],
    )


def solution(mesh):
    groups = mesh.shape["expert"]
    plan = token_plan if groups <= 16 else weight_plan
    return jax.shard_map(
        plan,
        mesh=mesh,
        in_specs=(
            P("expert", None),
            P("expert"),
            P("expert", "tensor"),
            P("expert", None),
            P("expert"),
            P("expert", "tensor"),
            P("tensor", "expert"),
            P("expert"),
            P("expert", None),
            P(None, "expert", "tensor"),
            P("tensor", "expert"),
            P("expert", None, None, "tensor"),
            P("expert", "tensor", None),
            P("expert", None),
            P("expert", None),
            P("expert", None),
        ),
        out_specs=(
            P("expert", None),
            P("expert", None),
            P("expert"),
            P("expert", "tensor"),
            P("expert", None),
            P("expert"),
            P("expert", "tensor"),
            P("tensor", "expert"),
            P("expert"),
            P("expert", None),
            P(None, "expert", "tensor"),
            P("tensor", "expert"),
            P("expert", None, None, "tensor"),
            P("expert", "tensor", None),
        ),
        check_vma=False,
    )
```

```python
import functools

import jax
import jax.numpy as jnp
from jax import lax
from jax.experimental import pallas as pl
from jax.experimental.pallas import tpu as pltpu
from jax.sharding import PartitionSpec as P

DN = 128
DR = 64
DV = 128
LANES = 128


EPSILON = 1e-06
ROUTE_SCALE = 2.446
ROPE_BASE = 50000.0
NEGATIVE = -1e30


def cut_along(value, dim, length):
    before, after = (value.shape[:dim], value.shape[dim + 1 :])
    return jnp.moveaxis(value.reshape(*before, length, -1, *after), dim, 0)


def summed_on_arrival(value, axis, dim):
    length = lax.axis_size(axis)
    tiles = lax.all_to_all(cut_along(value, dim, length), axis, 0, 0, tiled=True)
    return jnp.sum(tiles.astype(jnp.float32), axis=0)


def sent_together(arrays, axis, dim, along):
    columns = [a.reshape(*a.shape[:along], -1) for a in arrays]
    both = jnp.concatenate(columns, axis=along)
    whole, at, outs = (summed_on_arrival(both, axis, dim), 0, [])
    for a, column in zip(arrays, columns):
        slab = whole[..., at : at + column.shape[along]]
        outs.append(slab.reshape(*slab.shape[:along], *a.shape[along:]))
        at += column.shape[along]
    return tuple(outs)


def contract_rows(left_arr, right_arr):
    return lax.dot_general(
        left_arr, right_arr, (((0,), (0,)), ((), ())), preferred_element_type=jnp.float32
    )


def contract_cols(left_arr, right_arr):
    return lax.dot_general(
        left_arr, right_arr, (((1,), (1,)), ((), ())), preferred_element_type=jnp.float32
    )


def rms_forward(rows_in, gain_vec):
    inverse = lax.rsqrt(jnp.mean(rows_in * rows_in, axis=-1, keepdims=True) + EPSILON)
    return (rows_in * inverse * gain_vec, inverse)


def rms_backward(rows_in, inverse, gain_vec, grad_out):
    gain_grad = jnp.sum(grad_out * rows_in * inverse, axis=0)
    weighted = grad_out * gain_vec
    inner_mean = jnp.mean(weighted * rows_in, axis=-1, keepdims=True)
    return (inverse * weighted - rows_in * inverse * inverse * inverse * inner_mean, gain_grad)


def doc_layout(doc_lengths, row_count):
    ends_at = jnp.cumsum(doc_lengths)
    starts_at = ends_at - doc_lengths
    position = jnp.arange(row_count, dtype=jnp.int32)
    doc_ids = jnp.sum((position[:, None] >= ends_at[None, :]).astype(jnp.int32), axis=1)
    hitting = doc_ids[:, None] == jnp.arange(doc_lengths.shape[0], dtype=jnp.int32)[None, :]
    start_of = jnp.sum(jnp.where(hitting, starts_at[None, :], 0), axis=1)
    relative = position - start_of
    visible = (doc_ids[:, None] == doc_ids[None, :]) & (position[:, None] >= position[None, :])
    return (relative, visible)


def rope_tables(relative, rot_width):
    counter = jnp.arange(rot_width // 2, dtype=jnp.float32)
    frequency = ROPE_BASE ** (-2.0 * counter / rot_width)
    angles = relative.astype(jnp.float32)[:, None] * frequency[None, :]
    return (jnp.cos(angles), jnp.sin(angles))


def rotate(tensor_in, cosine, sine_tab):
    half_width = tensor_in.shape[-1] // 2
    leading = tensor_in[..., :half_width]
    trailing = tensor_in[..., half_width:]
    return jnp.concatenate(
        [leading * cosine - trailing * sine_tab, trailing * cosine + leading * sine_tab], axis=-1
    )


def unrotate(grad_in, cosine, sine_tab):
    half_width = grad_in.shape[-1] // 2
    leading = grad_in[..., :half_width]
    trailing = grad_in[..., half_width:]
    return jnp.concatenate(
        [leading * cosine + trailing * sine_tab, trailing * cosine - leading * sine_tab], axis=-1
    )


def gated_linear_backward(gate_in, up_in, grad_act):
    sigmoid_g = jax.nn.sigmoid(gate_in)
    grad_gate = grad_act * up_in * sigmoid_g * (1.0 + gate_in * (1.0 - sigmoid_g))
    return (grad_gate, grad_act * gate_in * sigmoid_g)


def slot_tables(route_rows, expert_count, capacity):
    flat_routes = route_rows.reshape(-1)
    one_hot = (flat_routes[:, None] == jnp.arange(expert_count, dtype=jnp.int32)[None, :]).astype(
        jnp.int32
    )
    ranking = jnp.sum((jnp.cumsum(one_hot, axis=0) - one_hot) * one_hot, axis=1)
    slot_ids = flat_routes * capacity + ranking
    row_total = flat_routes.shape[0]
    source = (
        jnp.zeros((expert_count * capacity,), jnp.int32)
        .at[slot_ids]
        .set(jnp.arange(row_total, dtype=jnp.int32))
    )
    filled = jnp.zeros((expert_count * capacity,), jnp.int32).at[slot_ids].set(1)
    return (slot_ids, source, filled)


def to_owner(rows_in):
    arrived = lax.all_to_all(rows_in, "expert", split_axis=0, concat_axis=1, tiled=True)
    return arrived


def weight_plan(
    inputs,
    attn_gain,
    w_query,
    w_latent,
    latent_gain,
    w_kv,
    w_out,
    ffn_gain,
    w_router,
    shared_gate_up,
    shared_down,
    expert_gate_up,
    expert_down,
    lengths,
    routes,
    cotangent,
):
    tok_rows = inputs.shape[0]
    model_width = inputs.shape[1]
    expert_count = w_router.shape[1]
    route_count = routes.shape[1]
    capacity = tok_rows * route_count * 4 // (3 * expert_count)
    brain_float16 = jnp.bfloat16
    f32 = jnp.float32
    gathered = (
        lax.all_gather(attn_gain, "expert", axis=0, tiled=True),
        lax.all_gather(w_query, "expert", axis=0, tiled=True),
        lax.all_gather(w_latent, "expert", axis=0, tiled=True),
        lax.all_gather(latent_gain, "expert", axis=0, tiled=True),
        lax.all_gather(w_kv, "expert", axis=0, tiled=True),
        lax.all_gather(w_out, "expert", axis=1, tiled=True),
        lax.all_gather(ffn_gain, "expert", axis=0, tiled=True),
        lax.all_gather(w_router, "expert", axis=0, tiled=True),
        lax.all_gather(shared_gate_up, "expert", axis=1, tiled=True),
        lax.all_gather(shared_down, "expert", axis=1, tiled=True),
    )
    gain_one, query_w, latent_w, latent_g, kv_w, out_w, gain_two, router_w, sgate_up, sdown_w = (
        gathered
    )
    local_heads = query_w.shape[1] // (DN + DR)
    rank_width = latent_g.shape[0]
    x_float = inputs.astype(f32)
    relative, visible = doc_layout(lengths[0], tok_rows)
    cosine, sine_tab = rope_tables(relative, DR)
    q_scale = (DN + DR) ** (-0.5)
    normed, scale_one = rms_forward(x_float, gain_one.astype(f32))
    normed_b = normed.astype(brain_float16)
    queries = jnp.dot(normed_b, query_w, preferred_element_type=f32).reshape(
        tok_rows, local_heads, DN + DR
    )
    q_rot = rotate(queries[..., DN:], cosine[:, None, :], sine_tab[:, None, :])
    q_all = jnp.concatenate([queries[..., :DN], q_rot], axis=-1).astype(brain_float16)
    latent = jnp.dot(normed_b, latent_w, preferred_element_type=f32)
    compressed, scale_kv = rms_forward(latent[:, :rank_width], latent_g.astype(f32))
    compressed_b = compressed.astype(brain_float16)
    k_rope = rotate(latent[:, rank_width:], cosine, sine_tab).astype(brain_float16)
    kv_all = jnp.dot(compressed_b, kv_w, preferred_element_type=f32).reshape(
        tok_rows, local_heads, DN + DV
    )
    k_nope = kv_all[..., :DN].astype(brain_float16)
    values = kv_all[..., DN:].astype(brain_float16)
    key_all = jnp.concatenate(
        [k_nope, jnp.broadcast_to(k_rope[:, None, :], (tok_rows, local_heads, DR))], axis=-1
    )

    def score_block():
        raw_scores = (
            jnp.einsum("qhd,khd->hqk", q_all, key_all, preferred_element_type=f32) * q_scale
        )
        return jnp.where(visible[None], raw_scores, NEGATIVE)

    scores = score_block()
    top_score = jnp.max(scores, axis=-1, keepdims=True)
    log_total = top_score + jnp.log(jnp.sum(jnp.exp(scores - top_score), axis=-1, keepdims=True))
    probs_b = jnp.exp(scores - log_total).astype(brain_float16)
    attended = jnp.einsum("hqk,khd->qhd", probs_b, values, preferred_element_type=f32)
    attended_b = attended.reshape(tok_rows, local_heads * DV).astype(brain_float16)
    attn = lax.psum(jnp.dot(attended_b, out_w, preferred_element_type=f32), "tensor")
    hidden = x_float + attn
    hnormed, scale_two = rms_forward(hidden, gain_two.astype(f32))
    hnormed_b = hnormed.astype(brain_float16)
    logits = jnp.dot(hnormed_b, router_w, preferred_element_type=f32)
    sigmoid_vals = jax.nn.sigmoid(logits)
    route_hot = routes[:, :, None] == jnp.arange(expert_count, dtype=jnp.int32)[None, None, :]
    chosen = jnp.sum(jnp.where(route_hot, sigmoid_vals[:, None, :], 0.0), axis=2)
    chosen_sum = jnp.sum(chosen, axis=1, keepdims=True)
    gate_vals = ROUTE_SCALE * chosen / chosen_sum
    slot_ids, source, filled = slot_tables(routes, expert_count, capacity)
    is_filled = filled[:, None] == 1
    sent_rows = jnp.where(is_filled, hnormed_b[source // route_count], 0).reshape(
        expert_count, capacity, model_width
    )
    received = to_owner(sent_rows)
    gate_up_joined = jnp.einsum(
        "erd,egdf->egrf", received, expert_gate_up, preferred_element_type=f32
    )
    expert_act = (jax.nn.silu(gate_up_joined[:, 0]) * gate_up_joined[:, 1]).astype(brain_float16)
    expert_res = jnp.einsum(
        "erf,efd->erd", expert_act, expert_down, preferred_element_type=f32
    ).astype(brain_float16)
    returned_all = lax.all_to_all(expert_res, "expert", split_axis=1, concat_axis=0, tiled=True)
    returned = returned_all.reshape(expert_count * capacity, model_width)[slot_ids].reshape(
        tok_rows, route_count, model_width
    )
    shared_gu = jnp.einsum("td,gdf->gtf", hnormed_b, sgate_up, preferred_element_type=f32)
    shared_act = (jax.nn.silu(shared_gu[0]) * shared_gu[1]).astype(brain_float16)
    branch_sum = jnp.dot(shared_act, sdown_w, preferred_element_type=f32)
    for route_idx in range(route_count):
        branch_sum = branch_sum + gate_vals[:, route_idx : route_idx + 1] * returned[
            :, route_idx
        ].astype(f32)
    moe_out = lax.psum(branch_sum.astype(jnp.bfloat16), "tensor").astype(jnp.float32)
    mixed = (hidden + moe_out).astype(brain_float16)
    grad_y = cotangent.astype(f32)
    sdown_grad = contract_rows(shared_act, cotangent)
    grad_sact = contract_cols(cotangent, sdown_w)
    grad_sgate, grad_sup = gated_linear_backward(shared_gu[0], shared_gu[1], grad_sact)
    grad_sgu = jnp.stack([grad_sgate, grad_sup], axis=0).astype(brain_float16)
    sgu_grad = jnp.einsum("td,gtf->gdf", hnormed_b, grad_sgu, preferred_element_type=f32)
    grad_hn_part = jnp.einsum("gtf,gdf->td", grad_sgu, sgate_up, preferred_element_type=f32)
    gate_columns = []
    for route_idx in range(route_count):
        gate_columns.append(jnp.sum(grad_y * returned[:, route_idx].astype(f32), axis=1))
    gate_part = jnp.stack(gate_columns, axis=1)
    slot_grads = (
        (gate_vals[:, :, None] * grad_y[:, None, :])
        .reshape(tok_rows * route_count, model_width)
        .astype(brain_float16)
    )
    grad_sent = jnp.where(is_filled, slot_grads[source], 0).reshape(
        expert_count, capacity, model_width
    )
    grad_received = to_owner(grad_sent)
    edown_grad = jnp.einsum("erf,erd->efd", expert_act, grad_received, preferred_element_type=f32)
    expert_activation_gradient = jnp.einsum(
        "erd,efd->erf", grad_received, expert_down, preferred_element_type=f32
    )
    expert_gate_gradient, expert_up_gradient = gated_linear_backward(
        gate_up_joined[:, 0], gate_up_joined[:, 1], expert_activation_gradient
    )
    expert_gate_up_gradient = jnp.stack([expert_gate_gradient, expert_up_gradient], axis=1).astype(
        brain_float16
    )
    egu_grad = jnp.einsum(
        "erd,egrf->egdf", received, expert_gate_up_gradient, preferred_element_type=f32
    )
    grad_rows = jnp.einsum(
        "egrf,egdf->erd", expert_gate_up_gradient, expert_gate_up, preferred_element_type=f32
    ).astype(brain_float16)
    grad_back = lax.all_to_all(grad_rows, "expert", split_axis=1, concat_axis=0, tiled=True)
    grad_routes = grad_back.reshape(expert_count * capacity, model_width)[slot_ids].reshape(
        tok_rows, route_count, model_width
    )
    for route_idx in range(route_count):
        grad_hn_part = grad_hn_part + grad_routes[:, route_idx].astype(f32)
    gate_grads = lax.psum(gate_part, "tensor")
    grad_chosen = ROUTE_SCALE * (
        gate_grads / chosen_sum
        - jnp.sum(gate_grads * chosen, axis=1, keepdims=True) / (chosen_sum * chosen_sum)
    )
    grad_sig = jnp.sum(jnp.where(route_hot, grad_chosen[:, :, None], 0.0), axis=1)
    grad_logits = (grad_sig * sigmoid_vals * (1.0 - sigmoid_vals)).astype(brain_float16)
    router_grad = contract_rows(hnormed_b, grad_logits)
    grad_hn = lax.psum(grad_hn_part, "tensor") + contract_cols(grad_logits, router_w)
    grad_hidden_norm, gain_two_grad = rms_backward(hidden, scale_two, gain_two.astype(f32), grad_hn)
    grad_hidden = grad_y + grad_hidden_norm
    grad_hidden_b = grad_hidden.astype(brain_float16)
    out_grad = contract_rows(attended_b, grad_hidden_b)
    grad_att = (
        contract_cols(grad_hidden_b, out_w).reshape(tok_rows, local_heads, DV).astype(brain_float16)
    )
    probs = jnp.exp(score_block() - log_total)
    probs_again = probs.astype(brain_float16)
    grad_probs = jnp.einsum("qhd,khd->hqk", grad_att, values, preferred_element_type=f32)
    grad_vals = jnp.einsum("hqk,qhd->khd", probs_again, grad_att, preferred_element_type=f32)
    row_delta = jnp.sum(probs * grad_probs, axis=-1, keepdims=True)
    grad_scores = (probs * (grad_probs - row_delta)).astype(brain_float16)
    grad_q = jnp.einsum("hqk,khd->qhd", grad_scores, key_all, preferred_element_type=f32) * q_scale
    grad_keys = jnp.einsum("hqk,qhd->khd", grad_scores, q_all, preferred_element_type=f32) * q_scale
    grad_kv = (
        jnp.concatenate([grad_keys[..., :DN], grad_vals], axis=-1)
        .reshape(tok_rows, local_heads * (DN + DV))
        .astype(brain_float16)
    )
    kv_grad = contract_rows(compressed_b, grad_kv)
    grad_comp_part = contract_cols(grad_kv, kv_w)
    grad_krope_part = jnp.sum(grad_keys[..., DN:], axis=1)
    grad_comp, grad_krope = (
        lax.psum(grad_comp_part.astype(jnp.bfloat16), "tensor").astype(jnp.float32),
        lax.psum(grad_krope_part.astype(jnp.bfloat16), "tensor").astype(jnp.float32),
    )
    grad_c, latent_gain_grad = rms_backward(
        latent[:, :rank_width], scale_kv, latent_g.astype(f32), grad_comp
    )
    grad_latent = jnp.concatenate([grad_c, unrotate(grad_krope, cosine, sine_tab)], axis=-1).astype(
        brain_float16
    )
    grad_qrot = unrotate(grad_q[..., DN:], cosine[:, None, :], sine_tab[:, None, :])
    grad_queries = (
        jnp.concatenate([grad_q[..., :DN], grad_qrot], axis=-1)
        .reshape(tok_rows, local_heads * (DN + DR))
        .astype(brain_float16)
    )
    query_grad = contract_rows(normed_b, grad_queries)
    latent_grad = contract_rows(normed_b, grad_latent)
    grad_normed = lax.psum(
        contract_cols(grad_queries, query_w).astype(jnp.bfloat16), "tensor"
    ).astype(jnp.float32) + contract_cols(grad_latent, latent_w)
    grad_x_norm, gain_one_grad = rms_backward(x_float, scale_one, gain_one.astype(f32), grad_normed)
    input_grad = grad_hidden + grad_x_norm
    first_owned = (
        *sent_together(
            (
                gain_one_grad.astype(jnp.bfloat16),
                query_grad.astype(jnp.bfloat16),
                latent_grad.astype(jnp.bfloat16),
            ),
            "expert",
            0,
            1,
        ),
        *sent_together(
            (latent_gain_grad.astype(jnp.bfloat16), kv_grad.astype(jnp.bfloat16)), "expert", 0, 1
        ),
    )
    second_owned = (
        lax.psum_scatter(out_grad, "expert", scatter_dimension=1, tiled=True),
        lax.psum_scatter(gain_two_grad, "expert", scatter_dimension=0, tiled=True),
        lax.psum_scatter(router_grad, "expert", scatter_dimension=0, tiled=True),
        lax.psum_scatter(sgu_grad, "expert", scatter_dimension=1, tiled=True),
        lax.psum_scatter(sdown_grad, "expert", scatter_dimension=1, tiled=True),
    )
    return (
        mixed,
        input_grad,
        first_owned[0],
        first_owned[1],
        first_owned[2],
        first_owned[3],
        first_owned[4],
        second_owned[0],
        second_owned[1],
        second_owned[2],
        second_owned[3],
        second_owned[4],
        egu_grad,
        edown_grad,
    )


def swap_cores(value):
    return lax.ppermute(value, "tensor", [(0, 1), (1, 0)])


def take_rows(value, start, count, axis=0):
    return lax.dynamic_slice_in_dim(value, start, count, axis=axis)


def in_order(core, own, other, axis=0):
    return jnp.where(
        core == 0,
        jnp.concatenate([own, other], axis=axis),
        jnp.concatenate([other, own], axis=axis),
    )


def add_wide(*parts):
    total = parts[0].astype(jnp.float32)
    for part in parts[1:]:
        total = total + part.astype(jnp.float32)
    return total


PLANE = 4


def to_partner(value, flips):
    groups = lax.axis_size("expert")
    return lax.ppermute(value, "expert", [(g, g ^ flips) for g in range(groups)])


def to_deeper(value, step):
    groups = lax.axis_size("expert")
    pairs = [(g, (g + step * PLANE) % groups) for g in range(groups)]
    return lax.ppermute(value, "expert", pairs)


def plane_gather(value):
    return [value] + [to_partner(value, r) for r in range(1, PLANE)]


def plane_scatter(parts):
    return add_wide(parts[0], *[to_partner(parts[r], r) for r in range(1, PLANE)])


def by_place(parts, place):
    odd, high = place % 2 == 1, place // 2 == 1
    parts = [jnp.where(odd, parts[i ^ 1], parts[i]) for i in range(PLANE)]
    return [jnp.where(high, parts[i ^ 2], parts[i]) for i in range(PLANE)]


def tie(*values):
    return lax.optimization_barrier(values)


def deep_pieces(value):
    deep = lax.axis_size("expert") // PLANE
    return [to_deeper(value, s) for s in range(1, deep)]


def deep_join(value, pieces, z):
    deep = lax.axis_size("expert") // PLANE
    whole = jnp.zeros((deep, *value.shape), value.dtype)
    whole = lax.dynamic_update_index_in_dim(whole, value, z, 0)
    for step in range(1, deep):
        whole = lax.dynamic_update_index_in_dim(whole, pieces[step - 1], (z - step) % deep, 0)
    return whole


def deep_scatter(blocks, z):
    deep = blocks.shape[0]

    def block(index):
        return lax.dynamic_index_in_dim(blocks, index, 0, keepdims=False)

    return add_wide(
        block(z), *[to_deeper(block((z + step) % deep), step) for step in range(1, deep)]
    )


def sum_planes(grad, z):
    deep = lax.axis_size("expert") // PLANE
    rows = deep_scatter(grad.astype(jnp.bfloat16).reshape(deep, -1, grad.shape[1]), z)
    return rows.astype(jnp.bfloat16).reshape(PLANE, -1, grad.shape[1])


def share_columns(rows, place):
    parts = [at_index(rows, 0, place)]
    for r in range(1, PLANE):
        parts.append(to_partner(at_index(rows, 0, place ^ r), r))
    return by_place(parts, place)


def all_groups(value):
    return lax.all_gather(value, "expert", axis=0, tiled=False)


def at_index(value, axis, index):
    return lax.dynamic_index_in_dim(value, index, axis, keepdims=False)


class PlaneSum:
    def __init__(self, *terms):
        groups, rows = terms[0].shape[:2]
        me = lax.axis_index("expert")
        self.type = terms[0].dtype
        near, far = me % 2, me // 2 % 2
        cut = rows // 2
        blocks = [v.reshape(groups // PLANE, 2, 2, *v.shape[1:]) for v in terms]
        self.first = [v[:, :, :, :cut] for v in blocks], far, near, 2, 1
        self.second = [jnp.swapaxes(v[:, :, :, cut:], 1, 2) for v in blocks], near, far, 1, 2

    def sends(self):
        return [self._add(at_index(v, 1, 1 - one) for v in held) for held, one, *_ in self._halves()]

    def _halves(self):
        return self.first, self.second

    def _add(self, parts):
        return add_wide(*parts).astype(self.type)

    def move(self, sends):
        return [to_partner(v, half[3]) for v, half in zip(sends, self._halves())]

    def sends_again(self, came):
        return [
            self._add(
                [at_index(at_index(v, 1, one), 1, 1 - two) for v in held]
                + [at_index(c, 1, 1 - two)]
            )
            for c, (held, one, two, *_) in zip(came, self._halves())
        ]

    def move_again(self, sends):
        return [to_partner(v, half[4]) for v, half in zip(sends, self._halves())]

    def line(self, came, came_again):
        sums = [
            self._add(
                [at_index(at_index(v, 1, one), 1, two) for v in held] + [at_index(c, 1, two), d]
            )
            for c, d, (held, one, two, *_) in zip(came, came_again, self._halves())
        ]
        return jnp.concatenate(sums, axis=1)


def deep_sends(line, z):
    deep = line.shape[0]
    return [at_index(line, 0, (z + step) % deep) for step in range(deep)]


def deep_move(sends):
    return [sends[0]] + [to_deeper(v, step) for step, v in enumerate(sends) if step > 0]


def dot_nn(left, right):
    return lax.dot_general(left, right, (((1,), (0,)), ((), ())), preferred_element_type=jnp.float32)


def dot_nt(left, right):
    return lax.dot_general(left, right, (((1,), (1,)), ((), ())), preferred_element_type=jnp.float32)


def dot_tn(left, right):
    return lax.dot_general(left, right, (((0,), (0,)), ((), ())), preferred_element_type=jnp.float32)


def two_lanes(column, lane):
    high = column.astype(jnp.bfloat16).astype(jnp.float32)
    spread = jnp.where(lane == 0, high, jnp.where(lane == 1, column - high, 0.0))
    return spread.astype(jnp.bfloat16)


def expert_kernel(
    shared_cols,
    expert_count,
    me_ref,
    hn_own,
    hn_other,
    dy_own,
    dy_other,
    meta_own,
    meta_other,
    gate_up_w,
    down_w,
    first_w,
    sdown_w,
    slots_out,
    slot_dy_out,
    act_out,
    d_gate_up_out,
    rows_own_out,
    rows_other_out,
    sact_own_out,
    sact_other_out,
    dsh_own_out,
    dsh_other_out,
    dgate_own_out,
    dgate_other_out,
):
    f32, bf16 = jnp.float32, jnp.bfloat16
    count, half, _ = hn_own.shape
    tokens = 2 * half
    me = me_ref[0]
    lane = lax.broadcasted_iota(jnp.int32, (tokens, LANES), 1)
    is_router = (lane >= shared_cols) & (lane < shared_cols + expert_count)
    first = first_w[...]
    slots, slot_dys, slot_gates, picks, dshs = [], [], [], [], []
    for i in range(count):
        rows = jnp.concatenate([hn_own[i], hn_other[i]], axis=0)
        rows_dy = jnp.concatenate([dy_own[i], dy_other[i]], axis=0)
        meta = jnp.concatenate([meta_own[i], meta_other[i]], axis=0)
        products = dot_nt(rows, first)
        gate, up = products[:, :LANES], products[:, LANES:]
        sig = jax.nn.sigmoid(gate)
        total = jnp.sum(jnp.where(is_router, sig * meta, 0.0), axis=1, keepdims=True)
        mine = jnp.sum(jnp.where(lane == shared_cols + me, sig, 0.0), axis=1, keepdims=True)
        token_gate = ROUTE_SCALE * mine / total
        sact = (gate * sig * up).astype(bf16)
        sact_own_out[i], sact_other_out[i] = sact[:half], sact[half:]
        d_sact = dot_nt(rows_dy, sdown_w[...])
        d_sgate = d_sact * up * sig * (1.0 + gate * (1.0 - sig))
        dsh = jnp.concatenate([d_sgate, d_sact * gate * sig], axis=1).astype(bf16)
        dsh_own_out[i], dsh_other_out[i] = dsh[:half], dsh[half:]
        dshs.append(dsh)
        pick = (meta[:, :1] == lane.astype(f32)).astype(bf16)
        picks.append(pick)
        slots.append(dot_tn(pick, rows).astype(bf16))
        slot_dys.append(dot_tn(pick, rows_dy).astype(bf16))
        slot_gates.append(
            jnp.sum(dot_tn(pick, two_lanes(token_gate, lane)), axis=1, keepdims=True)
        )
    slot_rows = jnp.concatenate(slots, axis=0)
    slot_dy = jnp.concatenate(slot_dys, axis=0)
    slot_gate = jnp.concatenate(slot_gates, axis=0)
    slots_out[...] = slot_rows
    slot_dy_out[...] = slot_dy
    gate = dot_nt(slot_rows, gate_up_w[0])
    up = dot_nt(slot_rows, gate_up_w[1])
    d_act = dot_nt(slot_dy, down_w[...])
    sig = jax.nn.sigmoid(gate)
    silu = gate * sig
    act = silu * up
    slot_dgate = jnp.sum(act * d_act, axis=1, keepdims=True)
    act_out[...] = (slot_gate * act).astype(bf16)
    d_act = slot_gate * d_act
    d_gate = (d_act * up * sig * (1.0 + gate * (1.0 - sig))).astype(bf16)
    d_up = (d_act * silu).astype(bf16)
    d_gate_up_out[0] = d_gate
    d_gate_up_out[1] = d_up
    d_slots = (dot_nn(d_gate, gate_up_w[0]) + dot_nn(d_up, gate_up_w[1])).astype(bf16)
    slot_lane = lax.broadcasted_iota(jnp.int32, (LANES, LANES), 1)
    for i in range(count):
        here = slice(i * LANES, (i + 1) * LANES)
        d_rows = (dot_nn(picks[i], d_slots[here]) + dot_nn(dshs[i], first)).astype(bf16)
        rows_own_out[i], rows_other_out[i] = d_rows[:half], d_rows[half:]
        dgate = dot_nn(picks[i], two_lanes(slot_dgate[here], slot_lane))
        dgate_own_out[i], dgate_other_out[i] = dgate[:half], dgate[half:]


def block_specs(per_step):
    def lead(*tail):
        return pl.BlockSpec((per_step, *tail), lambda i: (i,) + (0,) * len(tail))

    def flat(cols):
        return pl.BlockSpec((per_step * LANES, cols), lambda i: (i, 0))

    def whole(a):
        return pl.BlockSpec(a.shape, lambda i: (0,) * a.ndim, pipeline_mode=pl.Buffered(1))

    return lead, flat, whole


def slots_cost(width, hidden, products):
    return LANES * width * hidden * products


def experts(
    me,
    hn_own,
    hn_other,
    dy_own,
    dy_other,
    meta_own,
    meta_other,
    gate_up_w,
    down_w,
    first_w,
    sdown_w,
    shared_cols,
    expert_count,
    per_step=2,
):
    groups, half, width = hn_own.shape
    hidden = down_w.shape[0]
    slots = groups * LANES
    f32, bf16 = jnp.float32, jnp.bfloat16
    lead, flat, whole = block_specs(per_step)
    sds = jax.ShapeDtypeStruct
    rows_cost = 2 * groups * (2 * half * width * 4 * LANES + slots_cost(width, hidden, 5))
    return pl.pallas_call(
        functools.partial(expert_kernel, shared_cols, expert_count),
        grid=(groups // per_step,),
        in_specs=[
            pl.BlockSpec(memory_space=pltpu.SMEM),
            *[lead(half, width)] * 4,
            *[lead(half, LANES)] * 2,
            *[whole(a) for a in (gate_up_w, down_w, first_w, sdown_w)],
        ],
        out_specs=[
            flat(width),
            flat(width),
            flat(hidden),
            pl.BlockSpec((2, per_step * LANES, hidden), lambda i: (0, i, 0)),
            *[lead(half, width)] * 2,
            *[lead(half, LANES)] * 2,
            *[lead(half, 2 * LANES)] * 2,
            *[lead(half, LANES)] * 2,
        ],
        out_shape=[
            sds((slots, width), bf16),
            sds((slots, width), bf16),
            sds((slots, hidden), bf16),
            sds((2, slots, hidden), bf16),
            *[sds((groups, half, width), bf16)] * 2,
            *[sds((groups, half, LANES), bf16)] * 2,
            *[sds((groups, half, 2 * LANES), bf16)] * 2,
            *[sds((groups, half, LANES), f32)] * 2,
        ],
        compiler_params=pltpu.CompilerParams(vmem_limit_bytes=58 * 1024 * 1024),
        cost_estimate=pl.CostEstimate(
            flops=rows_cost, bytes_accessed=20 * groups * half * width, transcendentals=0
        ),
    )(
        me,
        hn_own,
        hn_other,
        dy_own,
        dy_other,
        meta_own,
        meta_other,
        gate_up_w,
        down_w,
        first_w,
        sdown_w,
    )


def output_kernel(act, sact_own, sact_other, meta_own, meta_other, down_w, sdown_w, own_out, other_out):
    f32, bf16 = jnp.float32, jnp.bfloat16
    count, half, _ = meta_own.shape
    lane = lax.broadcasted_iota(jnp.int32, (2 * half, LANES), 1).astype(f32)
    out = dot_nn(act[...], down_w[...]).astype(bf16)
    for i in range(count):
        meta = jnp.concatenate([meta_own[i], meta_other[i]], axis=0)
        pick = (meta[:, :1] == lane).astype(bf16)
        sact = jnp.concatenate([sact_own[i], sact_other[i]], axis=0)
        here = slice(i * LANES, (i + 1) * LANES)
        rows = (dot_nn(pick, out[here]) + dot_nn(sact, sdown_w[...])).astype(bf16)
        own_out[i], other_out[i] = rows[:half], rows[half:]


def outputs(act, sact_own, sact_other, meta_own, meta_other, down_w, sdown_w, per_step=4):
    groups, half, _ = meta_own.shape
    hidden, width = down_w.shape
    lead, flat, whole = block_specs(per_step)
    return pl.pallas_call(
        output_kernel,
        grid=(groups // per_step,),
        in_specs=[
            flat(hidden),
            *[lead(half, LANES)] * 4,
            *[whole(a) for a in (down_w, sdown_w)],
        ],
        out_specs=[lead(half, width)] * 2,
        out_shape=[jax.ShapeDtypeStruct((groups, half, width), jnp.bfloat16)] * 2,
        compiler_params=pltpu.CompilerParams(vmem_limit_bytes=58 * 1024 * 1024),
        cost_estimate=pl.CostEstimate(
            flops=groups * half * LANES * width,
            bytes_accessed=groups * half * width,
            transcendentals=0,
        ),
    )(act, sact_own, sact_other, meta_own, meta_other, down_w, sdown_w)


def token_plan(
    inputs,
    attn_gain,
    w_query,
    w_latent,
    latent_gain,
    w_kv,
    w_out,
    ffn_gain,
    w_router,
    shared_gate_up,
    shared_down,
    expert_gate_up,
    expert_down,
    lengths,
    routes,
    cotangent,
):
    f32, bf16 = jnp.float32, jnp.bfloat16
    core, me = lax.axis_index("tensor"), lax.axis_index("expert")
    groups = lax.axis_size("expert")
    deep, place, z = groups // PLANE, me % PLANE, me // PLANE
    tok_rows, width = inputs.shape
    half = tok_rows // 2
    own_at, other_at = core * half, (1 - core) * half
    expert_count = w_router.shape[1]
    route_count = routes.shape[1]
    capacity = tok_rows * route_count * 4 // (3 * expert_count)
    shared_cols = shared_gate_up.shape[2] // groups
    latent_cols, rank_width = w_latent.shape[1], latent_gain.shape[0] * groups
    block_rows = w_query.shape[0]
    kv_rows = w_kv.shape[0]

    query_cols = w_query.shape[1] // PLANE
    out_cols = w_out.shape[0] // PLANE
    used = latent_cols + expert_count + 3
    small = jnp.concatenate(
        [
            w_latent,
            w_router,
            attn_gain[:, None],
            ffn_gain[:, None],
            jnp.pad(latent_gain, (0, block_rows - kv_rows))[:, None],
            jnp.zeros((block_rows, -used % 128), bf16),
        ],
        axis=1,
    )
    small_cols = small.shape[1]
    route_half = take_rows(routes, own_at, half).astype(bf16).reshape(block_rows // 2, -1)
    length_col = jnp.pad(lengths[0].astype(bf16), (0, block_rows // 2 - lengths.shape[1]))[:, None]
    route_cols = route_half.shape[1] + 1
    small_half = jnp.concatenate(
        [
            take_rows(small, core * (block_rows // 2), block_rows // 2),
            jnp.pad(jnp.concatenate([route_half, length_col], axis=1), ((0, 0), (0, -route_cols % 128))),
        ],
        axis=1,
    )
    packed_cols = small_half.shape[1] // 2
    small_packed = jnp.concatenate([small_half[:, :packed_cols], small_half[:, packed_cols:]])
    kv_cols = w_kv.shape[1] // PLANE
    kv_parts = block_rows // kv_rows
    kv_piece = kv_cols // kv_parts
    w_out_t = w_out.T

    def quarter(index):
        kv_here = take_rows(w_kv, index * kv_cols, kv_cols, axis=1)
        kv_here = [kv_here[:, p * kv_piece : (p + 1) * kv_piece] for p in range(kv_parts)]
        return jnp.concatenate(
            [
                take_rows(w_query, index * query_cols, query_cols, axis=1),
                take_rows(w_out_t, index * out_cols, out_cols, axis=1),
                jnp.concatenate(kv_here, axis=0),
            ],
            axis=1,
        )

    near_w = [quarter(place)] + [to_partner(quarter(place ^ r), r) for r in range(1, PLANE)]
    small_line = deep_join(small_packed, deep_pieces(small_packed), z)
    near_w, small_line = tie(near_w, small_line)
    plane_w = jnp.stack(by_place(near_w, place))
    x_half, small_line, plane_w = tie(take_rows(inputs, own_at, half), small_line, plane_w)
    small_parts, x_parts, deep_w = tie(
        plane_gather(small_line), plane_gather(x_half), deep_pieces(plane_w)
    )
    x_near_own = jnp.stack(x_parts)
    x_near = in_order(core, x_near_own, swap_cores(x_near_own), axis=1)
    x_near = lax.optimization_barrier(x_near.reshape(PLANE * tok_rows, width))
    small_own = jnp.stack(by_place(small_parts, place), axis=1)
    small_own = small_own.reshape(groups, block_rows, packed_cols)
    small_own = jnp.concatenate(
        [small_own[:, : block_rows // 2], small_own[:, block_rows // 2 :]], axis=2
    )
    small_other = swap_cores(small_own)
    small_all = in_order(core, small_own, small_other, axis=1)
    head_w = deep_join(plane_w, deep_w, z)
    length_at = small_cols + route_cols - 1
    lengths_near = take_rows(small_own, z * PLANE, PLANE)[:, : lengths.shape[1], length_at]
    lengths_near = lengths_near.astype(jnp.int32)
    lengths_near = jnp.stack(by_place([lengths_near[r] for r in range(PLANE)], place))
    shared_rows = jnp.concatenate(
        [shared_gate_up[0].T, shared_gate_up[1].T, shared_down], axis=0
    ).reshape(3, groups, shared_cols, block_rows)
    shared_rows = shared_rows.swapaxes(0, 1).reshape(groups, 3 * shared_cols, block_rows)
    shared_rows, dy_sent, head_w = tie(shared_rows, take_rows(cotangent, own_at, half), head_w)
    dy_own_rows = take_rows(cotangent, own_at, half)
    dy_own = all_groups(dy_sent)
    shared_w = lax.all_to_all(shared_rows, "expert", split_axis=0, concat_axis=0, tiled=True)
    head_w = head_w.reshape(groups, block_rows, -1)
    flat_head = head_w.reshape(groups * block_rows, -1)
    query_w = flat_head[:, :query_cols]
    at = query_cols + out_cols
    out_wt = flat_head[:, query_cols:at]
    kv_w = head_w[:, :, at : at + kv_piece].reshape(groups, kv_parts, kv_rows, kv_piece)
    kv_w = kv_w.transpose(0, 2, 1, 3).reshape(groups * kv_rows, kv_cols)

    def routes_of(came):
        came = came[:, :, small_cols : small_cols + route_half.shape[1]]
        return came.astype(jnp.int32).reshape(groups, half, route_count)

    routes_own, routes_other = routes_of(small_own), routes_of(small_other)
    flat_small = small_all.reshape(groups * block_rows, -1)
    latent_w = flat_small[:, :latent_cols]
    at = latent_cols
    router_w = flat_small[:, at : at + expert_count]
    at += expert_count
    gain_one, gain_two = flat_small[:, at], flat_small[:, at + 1]
    latent_g = small_all[:, :kv_rows, at + 2].reshape(-1)

    near_rows = PLANE * tok_rows
    local_heads = query_cols // (DN + DR)
    x_float = x_near.astype(f32)
    relative, visible = jax.vmap(lambda one: doc_layout(one, tok_rows))(lengths_near)
    cosine, sine_tab = rope_tables(relative.reshape(-1), DR)
    q_scale = (DN + DR) ** (-0.5)
    scale_one = lax.rsqrt(jnp.mean(x_float * x_float, axis=-1, keepdims=True) + EPSILON)
    scale_one = lax.optimization_barrier(scale_one)
    normed_b = (x_near.astype(f32) * scale_one * gain_one.astype(f32)).astype(bf16)
    normed_b = lax.optimization_barrier(normed_b)
    queries = jnp.dot(normed_b, query_w, preferred_element_type=f32).reshape(
        near_rows, local_heads, DN + DR
    )
    q_rot = rotate(queries[..., DN:], cosine[:, None, :], sine_tab[:, None, :])
    q_all = jnp.concatenate([queries[..., :DN], q_rot], axis=-1).astype(bf16)
    q_all = q_all.reshape(PLANE, tok_rows, local_heads, DN + DR)
    latent = jnp.dot(normed_b, latent_w, preferred_element_type=f32)
    compressed, _ = rms_forward(latent[:, :rank_width], latent_g.astype(f32))
    compressed_b = compressed.astype(bf16)
    k_rope = rotate(latent[:, rank_width:], cosine, sine_tab).astype(bf16)
    kv_all = jnp.dot(compressed_b, kv_w, preferred_element_type=f32).reshape(
        PLANE, tok_rows, local_heads, DN + DV
    )
    k_nope = kv_all[..., :DN].astype(bf16)
    values = kv_all[..., DN:].astype(bf16)
    k_rope = k_rope.reshape(PLANE, tok_rows, 1, DR)
    key_all = jnp.concatenate(
        [k_nope, jnp.broadcast_to(k_rope, (PLANE, tok_rows, local_heads, DR))], axis=-1
    )

    def score_block():
        raw_scores = (
            jnp.einsum("gqhd,gkhd->ghqk", q_all, key_all, preferred_element_type=f32) * q_scale
        )
        return jnp.where(visible[:, None], raw_scores, NEGATIVE)

    scores = score_block()
    top_score = jnp.max(scores, axis=-1, keepdims=True)
    log_total = top_score + jnp.log(jnp.sum(jnp.exp(scores - top_score), axis=-1, keepdims=True))
    probs_b = jnp.exp(scores - log_total).astype(bf16)
    attended = jnp.einsum("ghqk,gkhd->gqhd", probs_b, values, preferred_element_type=f32)
    attended_b = attended.reshape(near_rows, local_heads * DV).astype(bf16)
    attended_b, shared_w = tie(attended_b, shared_w)
    shared_w = shared_w.swapaxes(0, 1).reshape(3 * shared_cols, groups * block_rows)

    def sum_heads(part):
        part = part.astype(bf16).reshape(PLANE, tok_rows, -1)
        came = swap_cores(take_rows(part, other_at, half, axis=1))
        both = add_wide(take_rows(part, own_at, half, axis=1), came).astype(bf16)
        return plane_scatter([both[r] for r in range(PLANE)])

    attn_own = sum_heads(contract_cols(attended_b, out_wt))
    x_own = take_rows(inputs, own_at, half).astype(f32)
    hidden = x_own + attn_own
    hnormed, scale_two = rms_forward(hidden, gain_two.astype(f32))
    hnormed_b = hnormed.astype(bf16)
    normed_cols = jnp.concatenate(
        [
            take_rows(normed_b, (k * PLANE + place) * block_rows, block_rows, axis=1)
            for k in range(deep)
        ],
        axis=1,
    )
    hnormed_b, dy_own, normed_cols = tie(hnormed_b, dy_own, normed_cols)
    dy_other = swap_cores(dy_own)

    hn_own = all_groups(hnormed_b)

    def membership(named):
        one_hot = named[..., None] == jnp.arange(expert_count, dtype=jnp.int32)
        return jnp.any(named == me, axis=-1), jnp.any(one_hot, axis=2)

    member_own, hot_own = membership(routes_own)
    member_other, hot_other = membership(routes_other)
    lower = (
        jnp.arange(half, dtype=jnp.int32)[:, None] <= jnp.arange(half, dtype=jnp.int32)[None, :]
    ).astype(bf16)

    def running(mask):
        counts = jnp.dot(mask.astype(bf16), lower, preferred_element_type=f32)
        return counts.astype(jnp.int32)

    count_own, count_other = running(member_own), running(member_other)
    place_own = jnp.where(member_own, count_own - 1, -1)
    place_other = jnp.where(member_other, count_own[:, -1:] + count_other - 1, -1)

    def metadata(slot, hot):
        return jnp.concatenate(
            [
                slot[..., None].astype(f32),
                jnp.zeros((groups, half, shared_cols - 1), f32),
                hot.astype(f32),
                jnp.zeros((groups, half, LANES - shared_cols - expert_count), f32),
            ],
            axis=-1,
        )

    meta_own, meta_other = metadata(place_own, hot_own), metadata(place_other, hot_other)
    first_w = jnp.concatenate(
        [
            shared_w[:shared_cols],
            router_w.T,
            jnp.zeros((LANES - shared_cols - expert_count, width), bf16),
            shared_w[shared_cols : 2 * shared_cols],
            jnp.zeros((LANES - shared_cols, width), bf16),
        ],
        axis=0,
    )
    sdown_rows = jnp.pad(shared_w[2 * shared_cols :], ((0, LANES - shared_cols), (0, 0)))
    hn_own, meta_own, meta_other, first_w, sdown_rows, dy_other = tie(
        hn_own, meta_own, meta_other, first_w, sdown_rows, dy_other
    )
    hn_other = swap_cores(hn_own)
    gate_up_w, down_w = jnp.swapaxes(expert_gate_up[0], 1, 2), expert_down[0]
    (
        slot_rows,
        slot_dy,
        slot_act,
        d_gate_up,
        d_rows_own,
        d_rows_other,
        act_own,
        act_other,
        d_shared_own,
        d_shared_other,
        dgate_own,
        dgate_other,
    ) = experts(
        me.reshape(1).astype(jnp.int32),
        hn_own,
        hn_other,
        dy_own,
        dy_other,
        meta_own,
        meta_other,
        gate_up_w,
        down_w,
        first_w,
        sdown_rows,
        shared_cols,
        expert_count,
    )
    d_rows_came = swap_cores(d_rows_other)

    def two_parts(value):
        return value[..., 0] + value[..., 1]

    def flat_rows(value):
        return value.reshape(groups * half, -1)

    first_grad = contract_rows(flat_rows(d_shared_own), flat_rows(hn_own)) + contract_rows(
        flat_rows(d_shared_other), flat_rows(hn_other)
    )
    sdown_grad = contract_rows(flat_rows(act_own), flat_rows(dy_own)) + contract_rows(
        flat_rows(act_other), flat_rows(dy_other)
    )
    dgate_sent = two_parts(dgate_own) + swap_cores(two_parts(dgate_other))
    dgate_high = dgate_sent.astype(bf16)
    dgate_low = (dgate_sent - dgate_high.astype(f32)).astype(bf16)
    grads_sent = jnp.concatenate(
        [
            first_grad[:shared_cols].astype(bf16),
            first_grad[LANES : LANES + shared_cols].astype(bf16),
            sdown_grad[:shared_cols].astype(bf16),
            dgate_high.reshape(1, -1),
            dgate_low.reshape(1, -1),
        ],
        axis=0,
    ).reshape(-1, groups, block_rows)
    d_rows_came, grads_sent = tie(d_rows_came, grads_sent)
    d_sum = PlaneSum(d_rows_own, d_rows_came)
    sends, grads_sent, slot_act = tie(d_sum.sends(), grads_sent, slot_act)
    came = d_sum.move(sends)
    grads_came = lax.all_to_all(grads_sent, "expert", split_axis=1, concat_axis=1, tiled=True)
    out_own, out_other = outputs(
        slot_act, act_own, act_other, meta_own, meta_other, down_w, sdown_rows
    )
    out_came = swap_cores(out_other)
    edown_grad = contract_rows(slot_act, slot_dy)
    came, out_came, edown_grad, grads_came = tie(came, out_came, edown_grad, grads_came)
    sgu_out, sdown_out, dgate = (
        grads_came[: 2 * shared_cols],
        grads_came[2 * shared_cols : 3 * shared_cols],
        add_wide(grads_came[3 * shared_cols], grads_came[3 * shared_cols + 1]).T,
    )
    sgu_out = sgu_out.astype(f32).reshape(2, shared_cols, groups, block_rows)
    sgu_out = sgu_out.transpose(0, 3, 2, 1).reshape(2, block_rows, -1)
    sdown_out = sdown_out.astype(f32).swapaxes(0, 1).reshape(-1, block_rows)
    sends, slot_rows, out_came = tie(d_sum.sends_again(came), slot_rows, out_came)
    came_again = d_sum.move_again(sends)
    egu_grad = jnp.einsum("sd,gsf->gdf", slot_rows, d_gate_up, preferred_element_type=f32)
    out_sum = PlaneSum(out_own, out_came)
    out_sends = out_sum.sends()
    came_again, egu_grad, out_sends = tie(came_again, egu_grad, out_sends)
    z_sends, out_sends, dgate = tie(
        deep_sends(d_sum.line(came, came_again), z), out_sends, dgate
    )
    z_came = deep_move(z_sends)
    out_first = out_sum.move(out_sends)
    hot_mine = take_rows(
        jnp.any(routes[..., None] == jnp.arange(expert_count, dtype=jnp.int32), axis=1), own_at, half
    )
    sig = jax.nn.sigmoid(jnp.dot(hnormed_b, router_w, preferred_element_type=f32))
    chosen = jnp.where(hot_mine, sig, 0.0)
    chosen_sum = jnp.sum(chosen, axis=1, keepdims=True)
    dgate = jnp.where(hot_mine, dgate, 0.0)
    inner = jnp.sum(dgate * chosen, axis=1, keepdims=True)
    d_chosen = ROUTE_SCALE * (dgate / chosen_sum - inner / (chosen_sum * chosen_sum))
    d_logits = (jnp.where(hot_mine, d_chosen, 0.0) * sig * (1.0 - sig)).astype(bf16)
    router_grad = contract_rows(d_logits, hnormed_b)
    z_came, d_logits, router_grad = tie(z_came, d_logits, router_grad)
    d_hn = add_wide(*z_came)
    d_hn = d_hn + contract_cols(d_logits, router_w)
    d_hidden_norm, gain_two_grad = rms_backward(hidden, scale_two, gain_two.astype(f32), d_hn)
    d_hidden = dy_own_rows.astype(f32) + d_hidden_norm
    d_parts, out_first = tie(plane_gather(d_hidden.astype(bf16)), out_first)
    d_near_own = jnp.stack(d_parts)
    d_near = in_order(core, d_near_own, swap_cores(d_near_own), axis=1).reshape(near_rows, width)

    out_sends, d_near = tie(out_sum.sends_again(out_first), d_near)
    out_second = out_sum.move_again(out_sends)

    grad_att = (
        jnp.dot(d_near, out_wt, preferred_element_type=f32)
        .reshape(PLANE, tok_rows, local_heads, DV)
        .astype(bf16)
    )
    out_grad = contract_rows(d_near, attended_b).astype(bf16)
    out_grad, grad_att = tie(out_grad, grad_att)
    out_sums = sum_planes(out_grad, z)
    probs = jnp.exp(score_block() - log_total)
    probs_again = probs.astype(bf16)
    grad_probs = jnp.einsum("gqhd,gkhd->ghqk", grad_att, values, preferred_element_type=f32)
    grad_vals = jnp.einsum("ghqk,gqhd->gkhd", probs_again, grad_att, preferred_element_type=f32)
    row_delta = jnp.sum(probs * grad_probs, axis=-1, keepdims=True)
    grad_scores = (probs * (grad_probs - row_delta)).astype(bf16)
    grad_q = (
        jnp.einsum("ghqk,gkhd->gqhd", grad_scores, key_all, preferred_element_type=f32) * q_scale
    ).reshape(near_rows, local_heads, DN + DR)
    grad_keys = (
        jnp.einsum("ghqk,gqhd->gkhd", grad_scores, q_all, preferred_element_type=f32) * q_scale
    )
    grad_kv = (
        jnp.concatenate([grad_keys[..., :DN], grad_vals], axis=-1)
        .reshape(near_rows, local_heads * (DN + DV))
        .astype(bf16)
    )
    grad_latent_part = jnp.concatenate(
        [
            contract_cols(grad_kv, kv_w),
            jnp.sum(grad_keys[..., DN:], axis=2).reshape(near_rows, DR),
        ],
        axis=1,
    )
    grad_both = sum_heads(grad_latent_part)
    latent_own = take_rows(latent[:tok_rows], own_at, half)
    cosine_own = take_rows(cosine[:tok_rows], own_at, half)
    sine_own = take_rows(sine_tab[:tok_rows], own_at, half)
    _, scale_kv = rms_forward(latent_own[:, :rank_width], latent_g.astype(f32))
    grad_c, latent_gain_grad = rms_backward(
        latent_own[:, :rank_width], scale_kv, latent_g.astype(f32), grad_both[:, :rank_width]
    )
    grad_latent = jnp.concatenate(
        [grad_c, unrotate(grad_both[:, rank_width:], cosine_own, sine_own)], axis=-1
    ).astype(bf16)
    grad_qrot = unrotate(grad_q[..., DN:], cosine[:, None, :], sine_tab[:, None, :])
    grad_queries = (
        jnp.concatenate([grad_q[..., :DN], grad_qrot], axis=-1)
        .reshape(near_rows, local_heads * (DN + DR))
        .astype(bf16)
    )
    out_second, grad_kv, grad_queries = tie(out_second, grad_kv, grad_queries)
    out_z, grad_kv, grad_queries = tie(
        deep_sends(out_sum.line(out_first, out_second), z), grad_kv, grad_queries
    )
    out_z = deep_move(out_z)
    kv_grad = contract_rows(compressed_b, grad_kv).astype(bf16)
    kv_grad = kv_grad.reshape(groups, kv_rows, kv_parts, kv_piece).transpose(0, 2, 1, 3)
    query_grad = contract_rows(normed_b, grad_queries).astype(bf16)
    first_sums = sum_planes(
        jnp.concatenate([query_grad, kv_grad.reshape(-1, kv_piece)], axis=1), z
    )
    shared_out = share_columns(jnp.concatenate([first_sums, out_sums], axis=2), place)
    at_kv, at_out = query_cols, query_cols + kv_piece
    w_query_grad = jnp.concatenate([p[:, :at_kv] for p in shared_out], axis=1).astype(f32)
    w_kv_grad = jnp.concatenate(
        [
            p[q * kv_rows : (q + 1) * kv_rows, at_kv:at_out]
            for p in shared_out
            for q in range(kv_parts)
        ],
        axis=1,
    ).astype(f32)
    w_out_grad = jnp.concatenate([p[:, at_out:] for p in shared_out], axis=1).astype(f32).T
    grad_normed = sum_heads(contract_cols(grad_queries, query_w))
    grad_normed = grad_normed + contract_cols(grad_latent, latent_w)
    moe_own = add_wide(*out_z)
    mixed_own = (hidden + moe_own).astype(bf16)
    mixed = in_order(core, mixed_own, swap_cores(mixed_own))

    _, scale_own = rms_forward(x_own, gain_one.astype(f32))
    grad_x_norm, gain_one_grad = rms_backward(x_own, scale_own, gain_one.astype(f32), grad_normed)
    input_own = d_hidden + grad_x_norm
    input_grad = in_order(core, input_own, swap_cores(input_own))

    latent_near_own = jnp.stack(plane_gather(grad_latent))
    latent_near = in_order(core, latent_near_own, swap_cores(latent_near_own), axis=1)
    latent_cut = latent_cols // 2
    latent_near = latent_near.reshape(near_rows, latent_cols)
    latent_blocks = contract_rows(
        normed_cols,
        take_rows(latent_near, core * latent_cut, latent_cut, axis=1),
    )
    latent_half = deep_scatter(latent_blocks.astype(bf16).reshape(deep, -1, latent_cut), z)
    w_latent_grad = in_order(core, latent_half, swap_cores(latent_half), axis=1)

    gain_lanes = jnp.pad(
        latent_gain_grad.reshape(groups, kv_rows), ((0, 0), (0, block_rows - kv_rows))
    )
    vectors = jnp.concatenate(
        [
            router_grad,
            gain_one_grad[None],
            gain_two_grad[None],
            gain_lanes.reshape(1, -1),
        ],
        axis=0,
    ).reshape(-1, groups, block_rows)
    arrived = lax.all_to_all(vectors, "expert", split_axis=1, concat_axis=1, tiled=True)
    sums = jnp.sum(arrived, axis=1)
    sums = sums + swap_cores(sums)
    return (
        mixed,
        input_grad,
        sums[expert_count],
        w_query_grad,
        w_latent_grad,
        sums[expert_count + 2, :kv_rows],
        w_kv_grad,
        w_out_grad,
        sums[expert_count + 1],
        sums[:expert_count].T,
        sgu_out,
        sdown_out,
        egu_grad[None],
        edown_grad[None],
    )


def solution(mesh):
    groups = mesh.shape["expert"]
    plan = token_plan if groups <= 16 else weight_plan
    return jax.shard_map(
        plan,
        mesh=mesh,
        in_specs=(
            P("expert", None),
            P("expert"),
            P("expert", "tensor"),
            P("expert", None),
            P("expert"),
            P("expert", "tensor"),
            P("tensor", "expert"),
            P("expert"),
            P("expert", None),
            P(None, "expert", "tensor"),
            P("tensor", "expert"),
            P("expert", None, None, "tensor"),
            P("expert", "tensor", None),
            P("expert", None),
            P("expert", None),
            P("expert", None),
        ),
        out_specs=(
            P("expert", None),
            P("expert", None),
            P("expert"),
            P("expert", "tensor"),
            P("expert", None),
            P("expert"),
            P("expert", "tensor"),
            P("tensor", "expert"),
            P("expert"),
            P("expert", None),
            P(None, "expert", "tensor"),
            P("tensor", "expert"),
            P("expert", None, None, "tensor"),
            P("expert", "tensor", None),
        ),
        check_vma=False,
    )
```

```python
import functools

import jax
import jax.numpy as jnp
from jax import lax
from jax.experimental import pallas as pl
from jax.experimental.pallas import tpu as pltpu
from jax.sharding import PartitionSpec as P

DN = 128
DR = 64
DV = 128
LANES = 128


EPSILON = 1e-06
ROUTE_SCALE = 2.446
ROPE_BASE = 50000.0
NEGATIVE = -1e30


def cut_along(value, dim, length):
    before, after = (value.shape[:dim], value.shape[dim + 1 :])
    return jnp.moveaxis(value.reshape(*before, length, -1, *after), dim, 0)


def summed_on_arrival(value, axis, dim):
    length = lax.axis_size(axis)
    tiles = lax.all_to_all(cut_along(value, dim, length), axis, 0, 0, tiled=True)
    return jnp.sum(tiles.astype(jnp.float32), axis=0)


def sent_together(arrays, axis, dim, along):
    columns = [a.reshape(*a.shape[:along], -1) for a in arrays]
    both = jnp.concatenate(columns, axis=along)
    whole, at, outs = (summed_on_arrival(both, axis, dim), 0, [])
    for a, column in zip(arrays, columns):
        slab = whole[..., at : at + column.shape[along]]
        outs.append(slab.reshape(*slab.shape[:along], *a.shape[along:]))
        at += column.shape[along]
    return tuple(outs)


def contract_rows(left_arr, right_arr):
    return lax.dot_general(
        left_arr, right_arr, (((0,), (0,)), ((), ())), preferred_element_type=jnp.float32
    )


def contract_cols(left_arr, right_arr):
    return lax.dot_general(
        left_arr, right_arr, (((1,), (1,)), ((), ())), preferred_element_type=jnp.float32
    )


def rms_forward(rows_in, gain_vec):
    inverse = lax.rsqrt(jnp.mean(rows_in * rows_in, axis=-1, keepdims=True) + EPSILON)
    return (rows_in * inverse * gain_vec, inverse)


def rms_backward(rows_in, inverse, gain_vec, grad_out):
    gain_grad = jnp.sum(grad_out * rows_in * inverse, axis=0)
    weighted = grad_out * gain_vec
    inner_mean = jnp.mean(weighted * rows_in, axis=-1, keepdims=True)
    return (inverse * weighted - rows_in * inverse * inverse * inverse * inner_mean, gain_grad)


def doc_layout(doc_lengths, row_count):
    ends_at = jnp.cumsum(doc_lengths)
    starts_at = ends_at - doc_lengths
    position = jnp.arange(row_count, dtype=jnp.int32)
    doc_ids = jnp.sum((position[:, None] >= ends_at[None, :]).astype(jnp.int32), axis=1)
    hitting = doc_ids[:, None] == jnp.arange(doc_lengths.shape[0], dtype=jnp.int32)[None, :]
    start_of = jnp.sum(jnp.where(hitting, starts_at[None, :], 0), axis=1)
    relative = position - start_of
    visible = (doc_ids[:, None] == doc_ids[None, :]) & (position[:, None] >= position[None, :])
    return (relative, visible)


def rope_tables(relative, rot_width):
    counter = jnp.arange(rot_width // 2, dtype=jnp.float32)
    frequency = ROPE_BASE ** (-2.0 * counter / rot_width)
    angles = relative.astype(jnp.float32)[:, None] * frequency[None, :]
    return (jnp.cos(angles), jnp.sin(angles))


def rotate(tensor_in, cosine, sine_tab):
    half_width = tensor_in.shape[-1] // 2
    leading = tensor_in[..., :half_width]
    trailing = tensor_in[..., half_width:]
    return jnp.concatenate(
        [leading * cosine - trailing * sine_tab, trailing * cosine + leading * sine_tab], axis=-1
    )


def unrotate(grad_in, cosine, sine_tab):
    half_width = grad_in.shape[-1] // 2
    leading = grad_in[..., :half_width]
    trailing = grad_in[..., half_width:]
    return jnp.concatenate(
        [leading * cosine + trailing * sine_tab, trailing * cosine - leading * sine_tab], axis=-1
    )


def gated_linear_backward(gate_in, up_in, grad_act):
    sigmoid_g = jax.nn.sigmoid(gate_in)
    grad_gate = grad_act * up_in * sigmoid_g * (1.0 + gate_in * (1.0 - sigmoid_g))
    return (grad_gate, grad_act * gate_in * sigmoid_g)


def slot_tables(route_rows, expert_count, capacity):
    flat_routes = route_rows.reshape(-1)
    one_hot = (flat_routes[:, None] == jnp.arange(expert_count, dtype=jnp.int32)[None, :]).astype(
        jnp.int32
    )
    ranking = jnp.sum((jnp.cumsum(one_hot, axis=0) - one_hot) * one_hot, axis=1)
    slot_ids = flat_routes * capacity + ranking
    row_total = flat_routes.shape[0]
    source = (
        jnp.zeros((expert_count * capacity,), jnp.int32)
        .at[slot_ids]
        .set(jnp.arange(row_total, dtype=jnp.int32))
    )
    filled = jnp.zeros((expert_count * capacity,), jnp.int32).at[slot_ids].set(1)
    return (slot_ids, source, filled)


def to_owner(rows_in):
    arrived = lax.all_to_all(rows_in, "expert", split_axis=0, concat_axis=1, tiled=True)
    return arrived


def weight_plan(
    inputs,
    attn_gain,
    w_query,
    w_latent,
    latent_gain,
    w_kv,
    w_out,
    ffn_gain,
    w_router,
    shared_gate_up,
    shared_down,
    expert_gate_up,
    expert_down,
    lengths,
    routes,
    cotangent,
):
    tok_rows = inputs.shape[0]
    model_width = inputs.shape[1]
    expert_count = w_router.shape[1]
    route_count = routes.shape[1]
    capacity = tok_rows * route_count * 4 // (3 * expert_count)
    brain_float16 = jnp.bfloat16
    f32 = jnp.float32
    gathered = (
        lax.all_gather(attn_gain, "expert", axis=0, tiled=True),
        lax.all_gather(w_query, "expert", axis=0, tiled=True),
        lax.all_gather(w_latent, "expert", axis=0, tiled=True),
        lax.all_gather(latent_gain, "expert", axis=0, tiled=True),
        lax.all_gather(w_kv, "expert", axis=0, tiled=True),
        lax.all_gather(w_out, "expert", axis=1, tiled=True),
        lax.all_gather(ffn_gain, "expert", axis=0, tiled=True),
        lax.all_gather(w_router, "expert", axis=0, tiled=True),
        lax.all_gather(shared_gate_up, "expert", axis=1, tiled=True),
        lax.all_gather(shared_down, "expert", axis=1, tiled=True),
    )
    gain_one, query_w, latent_w, latent_g, kv_w, out_w, gain_two, router_w, sgate_up, sdown_w = (
        gathered
    )
    local_heads = query_w.shape[1] // (DN + DR)
    rank_width = latent_g.shape[0]
    x_float = inputs.astype(f32)
    relative, visible = doc_layout(lengths[0], tok_rows)
    cosine, sine_tab = rope_tables(relative, DR)
    q_scale = (DN + DR) ** (-0.5)
    normed, scale_one = rms_forward(x_float, gain_one.astype(f32))
    normed_b = normed.astype(brain_float16)
    queries = jnp.dot(normed_b, query_w, preferred_element_type=f32).reshape(
        tok_rows, local_heads, DN + DR
    )
    q_rot = rotate(queries[..., DN:], cosine[:, None, :], sine_tab[:, None, :])
    q_all = jnp.concatenate([queries[..., :DN], q_rot], axis=-1).astype(brain_float16)
    latent = jnp.dot(normed_b, latent_w, preferred_element_type=f32)
    compressed, scale_kv = rms_forward(latent[:, :rank_width], latent_g.astype(f32))
    compressed_b = compressed.astype(brain_float16)
    k_rope = rotate(latent[:, rank_width:], cosine, sine_tab).astype(brain_float16)
    kv_all = jnp.dot(compressed_b, kv_w, preferred_element_type=f32).reshape(
        tok_rows, local_heads, DN + DV
    )
    k_nope = kv_all[..., :DN].astype(brain_float16)
    values = kv_all[..., DN:].astype(brain_float16)
    key_all = jnp.concatenate(
        [k_nope, jnp.broadcast_to(k_rope[:, None, :], (tok_rows, local_heads, DR))], axis=-1
    )

    def score_block():
        raw_scores = (
            jnp.einsum("qhd,khd->hqk", q_all, key_all, preferred_element_type=f32) * q_scale
        )
        return jnp.where(visible[None], raw_scores, NEGATIVE)

    scores = score_block()
    top_score = jnp.max(scores, axis=-1, keepdims=True)
    log_total = top_score + jnp.log(jnp.sum(jnp.exp(scores - top_score), axis=-1, keepdims=True))
    probs_b = jnp.exp(scores - log_total).astype(brain_float16)
    attended = jnp.einsum("hqk,khd->qhd", probs_b, values, preferred_element_type=f32)
    attended_b = attended.reshape(tok_rows, local_heads * DV).astype(brain_float16)
    attn = lax.psum(jnp.dot(attended_b, out_w, preferred_element_type=f32), "tensor")
    hidden = x_float + attn
    hnormed, scale_two = rms_forward(hidden, gain_two.astype(f32))
    hnormed_b = hnormed.astype(brain_float16)
    logits = jnp.dot(hnormed_b, router_w, preferred_element_type=f32)
    sigmoid_vals = jax.nn.sigmoid(logits)
    route_hot = routes[:, :, None] == jnp.arange(expert_count, dtype=jnp.int32)[None, None, :]
    chosen = jnp.sum(jnp.where(route_hot, sigmoid_vals[:, None, :], 0.0), axis=2)
    chosen_sum = jnp.sum(chosen, axis=1, keepdims=True)
    gate_vals = ROUTE_SCALE * chosen / chosen_sum
    slot_ids, source, filled = slot_tables(routes, expert_count, capacity)
    is_filled = filled[:, None] == 1
    sent_rows = jnp.where(is_filled, hnormed_b[source // route_count], 0).reshape(
        expert_count, capacity, model_width
    )
    received = to_owner(sent_rows)
    gate_up_joined = jnp.einsum(
        "erd,egdf->egrf", received, expert_gate_up, preferred_element_type=f32
    )
    expert_act = (jax.nn.silu(gate_up_joined[:, 0]) * gate_up_joined[:, 1]).astype(brain_float16)
    expert_res = jnp.einsum(
        "erf,efd->erd", expert_act, expert_down, preferred_element_type=f32
    ).astype(brain_float16)
    returned_all = lax.all_to_all(expert_res, "expert", split_axis=1, concat_axis=0, tiled=True)
    returned = returned_all.reshape(expert_count * capacity, model_width)[slot_ids].reshape(
        tok_rows, route_count, model_width
    )
    shared_gu = jnp.einsum("td,gdf->gtf", hnormed_b, sgate_up, preferred_element_type=f32)
    shared_act = (jax.nn.silu(shared_gu[0]) * shared_gu[1]).astype(brain_float16)
    branch_sum = jnp.dot(shared_act, sdown_w, preferred_element_type=f32)
    for route_idx in range(route_count):
        branch_sum = branch_sum + gate_vals[:, route_idx : route_idx + 1] * returned[
            :, route_idx
        ].astype(f32)
    moe_out = lax.psum(branch_sum.astype(jnp.bfloat16), "tensor").astype(jnp.float32)
    mixed = (hidden + moe_out).astype(brain_float16)
    grad_y = cotangent.astype(f32)
    sdown_grad = contract_rows(shared_act, cotangent)
    grad_sact = contract_cols(cotangent, sdown_w)
    grad_sgate, grad_sup = gated_linear_backward(shared_gu[0], shared_gu[1], grad_sact)
    grad_sgu = jnp.stack([grad_sgate, grad_sup], axis=0).astype(brain_float16)
    sgu_grad = jnp.einsum("td,gtf->gdf", hnormed_b, grad_sgu, preferred_element_type=f32)
    grad_hn_part = jnp.einsum("gtf,gdf->td", grad_sgu, sgate_up, preferred_element_type=f32)
    gate_columns = []
    for route_idx in range(route_count):
        gate_columns.append(jnp.sum(grad_y * returned[:, route_idx].astype(f32), axis=1))
    gate_part = jnp.stack(gate_columns, axis=1)
    slot_grads = (
        (gate_vals[:, :, None] * grad_y[:, None, :])
        .reshape(tok_rows * route_count, model_width)
        .astype(brain_float16)
    )
    grad_sent = jnp.where(is_filled, slot_grads[source], 0).reshape(
        expert_count, capacity, model_width
    )
    grad_received = to_owner(grad_sent)
    edown_grad = jnp.einsum("erf,erd->efd", expert_act, grad_received, preferred_element_type=f32)
    expert_activation_gradient = jnp.einsum(
        "erd,efd->erf", grad_received, expert_down, preferred_element_type=f32
    )
    expert_gate_gradient, expert_up_gradient = gated_linear_backward(
        gate_up_joined[:, 0], gate_up_joined[:, 1], expert_activation_gradient
    )
    expert_gate_up_gradient = jnp.stack([expert_gate_gradient, expert_up_gradient], axis=1).astype(
        brain_float16
    )
    egu_grad = jnp.einsum(
        "erd,egrf->egdf", received, expert_gate_up_gradient, preferred_element_type=f32
    )
    grad_rows = jnp.einsum(
        "egrf,egdf->erd", expert_gate_up_gradient, expert_gate_up, preferred_element_type=f32
    ).astype(brain_float16)
    grad_back = lax.all_to_all(grad_rows, "expert", split_axis=1, concat_axis=0, tiled=True)
    grad_routes = grad_back.reshape(expert_count * capacity, model_width)[slot_ids].reshape(
        tok_rows, route_count, model_width
    )
    for route_idx in range(route_count):
        grad_hn_part = grad_hn_part + grad_routes[:, route_idx].astype(f32)
    gate_grads = lax.psum(gate_part, "tensor")
    grad_chosen = ROUTE_SCALE * (
        gate_grads / chosen_sum
        - jnp.sum(gate_grads * chosen, axis=1, keepdims=True) / (chosen_sum * chosen_sum)
    )
    grad_sig = jnp.sum(jnp.where(route_hot, grad_chosen[:, :, None], 0.0), axis=1)
    grad_logits = (grad_sig * sigmoid_vals * (1.0 - sigmoid_vals)).astype(brain_float16)
    router_grad = contract_rows(hnormed_b, grad_logits)
    grad_hn = lax.psum(grad_hn_part, "tensor") + contract_cols(grad_logits, router_w)
    grad_hidden_norm, gain_two_grad = rms_backward(hidden, scale_two, gain_two.astype(f32), grad_hn)
    grad_hidden = grad_y + grad_hidden_norm
    grad_hidden_b = grad_hidden.astype(brain_float16)
    out_grad = contract_rows(attended_b, grad_hidden_b)
    grad_att = (
        contract_cols(grad_hidden_b, out_w).reshape(tok_rows, local_heads, DV).astype(brain_float16)
    )
    probs = jnp.exp(score_block() - log_total)
    probs_again = probs.astype(brain_float16)
    grad_probs = jnp.einsum("qhd,khd->hqk", grad_att, values, preferred_element_type=f32)
    grad_vals = jnp.einsum("hqk,qhd->khd", probs_again, grad_att, preferred_element_type=f32)
    row_delta = jnp.sum(probs * grad_probs, axis=-1, keepdims=True)
    grad_scores = (probs * (grad_probs - row_delta)).astype(brain_float16)
    grad_q = jnp.einsum("hqk,khd->qhd", grad_scores, key_all, preferred_element_type=f32) * q_scale
    grad_keys = jnp.einsum("hqk,qhd->khd", grad_scores, q_all, preferred_element_type=f32) * q_scale
    grad_kv = (
        jnp.concatenate([grad_keys[..., :DN], grad_vals], axis=-1)
        .reshape(tok_rows, local_heads * (DN + DV))
        .astype(brain_float16)
    )
    kv_grad = contract_rows(compressed_b, grad_kv)
    grad_comp_part = contract_cols(grad_kv, kv_w)
    grad_krope_part = jnp.sum(grad_keys[..., DN:], axis=1)
    grad_comp, grad_krope = (
        lax.psum(grad_comp_part.astype(jnp.bfloat16), "tensor").astype(jnp.float32),
        lax.psum(grad_krope_part.astype(jnp.bfloat16), "tensor").astype(jnp.float32),
    )
    grad_c, latent_gain_grad = rms_backward(
        latent[:, :rank_width], scale_kv, latent_g.astype(f32), grad_comp
    )
    grad_latent = jnp.concatenate([grad_c, unrotate(grad_krope, cosine, sine_tab)], axis=-1).astype(
        brain_float16
    )
    grad_qrot = unrotate(grad_q[..., DN:], cosine[:, None, :], sine_tab[:, None, :])
    grad_queries = (
        jnp.concatenate([grad_q[..., :DN], grad_qrot], axis=-1)
        .reshape(tok_rows, local_heads * (DN + DR))
        .astype(brain_float16)
    )
    query_grad = contract_rows(normed_b, grad_queries)
    latent_grad = contract_rows(normed_b, grad_latent)
    grad_normed = lax.psum(
        contract_cols(grad_queries, query_w).astype(jnp.bfloat16), "tensor"
    ).astype(jnp.float32) + contract_cols(grad_latent, latent_w)
    grad_x_norm, gain_one_grad = rms_backward(x_float, scale_one, gain_one.astype(f32), grad_normed)
    input_grad = grad_hidden + grad_x_norm
    first_owned = (
        *sent_together(
            (
                gain_one_grad.astype(jnp.bfloat16),
                query_grad.astype(jnp.bfloat16),
                latent_grad.astype(jnp.bfloat16),
            ),
            "expert",
            0,
            1,
        ),
        *sent_together(
            (latent_gain_grad.astype(jnp.bfloat16), kv_grad.astype(jnp.bfloat16)), "expert", 0, 1
        ),
    )
    second_owned = (
        lax.psum_scatter(out_grad, "expert", scatter_dimension=1, tiled=True),
        lax.psum_scatter(gain_two_grad, "expert", scatter_dimension=0, tiled=True),
        lax.psum_scatter(router_grad, "expert", scatter_dimension=0, tiled=True),
        lax.psum_scatter(sgu_grad, "expert", scatter_dimension=1, tiled=True),
        lax.psum_scatter(sdown_grad, "expert", scatter_dimension=1, tiled=True),
    )
    return (
        mixed,
        input_grad,
        first_owned[0],
        first_owned[1],
        first_owned[2],
        first_owned[3],
        first_owned[4],
        second_owned[0],
        second_owned[1],
        second_owned[2],
        second_owned[3],
        second_owned[4],
        egu_grad,
        edown_grad,
    )


def swap_cores(value):
    return lax.ppermute(value, "tensor", [(0, 1), (1, 0)])


def take_rows(value, start, count, axis=0):
    return lax.dynamic_slice_in_dim(value, start, count, axis=axis)


def in_order(core, own, other, axis=0):
    return jnp.where(
        core == 0,
        jnp.concatenate([own, other], axis=axis),
        jnp.concatenate([other, own], axis=axis),
    )


def add_wide(*parts):
    total = parts[0].astype(jnp.float32)
    for part in parts[1:]:
        total = total + part.astype(jnp.float32)
    return total


PLANE = 4


def to_partner(value, flips):
    groups = lax.axis_size("expert")
    return lax.ppermute(value, "expert", [(g, g ^ flips) for g in range(groups)])


def to_deeper(value, step):
    groups = lax.axis_size("expert")
    pairs = [(g, (g + step * PLANE) % groups) for g in range(groups)]
    return lax.ppermute(value, "expert", pairs)


def plane_gather(value):
    return [value] + [to_partner(value, r) for r in range(1, PLANE)]


def plane_scatter(parts):
    return add_wide(parts[0], *[to_partner(parts[r], r) for r in range(1, PLANE)])


def by_place(parts, place):
    odd, high = place % 2 == 1, place // 2 == 1
    parts = [jnp.where(odd, parts[i ^ 1], parts[i]) for i in range(PLANE)]
    return [jnp.where(high, parts[i ^ 2], parts[i]) for i in range(PLANE)]


def tie(*values):
    return lax.optimization_barrier(values)


def deep_pieces(value):
    deep = lax.axis_size("expert") // PLANE
    return [to_deeper(value, s) for s in range(1, deep)]


def deep_join(value, pieces, z):
    deep = lax.axis_size("expert") // PLANE
    whole = jnp.zeros((deep, *value.shape), value.dtype)
    whole = lax.dynamic_update_index_in_dim(whole, value, z, 0)
    for step in range(1, deep):
        whole = lax.dynamic_update_index_in_dim(whole, pieces[step - 1], (z - step) % deep, 0)
    return whole


def deep_scatter(blocks, z):
    deep = blocks.shape[0]

    def block(index):
        return lax.dynamic_index_in_dim(blocks, index, 0, keepdims=False)

    return add_wide(
        block(z), *[to_deeper(block((z + step) % deep), step) for step in range(1, deep)]
    )


def sum_planes(grad, z):
    deep = lax.axis_size("expert") // PLANE
    rows = deep_scatter(grad.astype(jnp.bfloat16).reshape(deep, -1, grad.shape[1]), z)
    return rows.astype(jnp.bfloat16).reshape(PLANE, -1, grad.shape[1])


def share_columns(rows, place):
    parts = [at_index(rows, 0, place)]
    for r in range(1, PLANE):
        parts.append(to_partner(at_index(rows, 0, place ^ r), r))
    return by_place(parts, place)


def all_groups(value):
    return lax.all_gather(value, "expert", axis=0, tiled=False)


def at_index(value, axis, index):
    return lax.dynamic_index_in_dim(value, index, axis, keepdims=False)


class RowGather:
    def __init__(self, value):
        self.cut = value.shape[0] // 2
        self.value = value

    def along(self):
        return [self.value] + deep_pieces(self.value)

    def lines(self, came):
        return [jnp.stack([v[: self.cut] for v in came]), jnp.stack([v[self.cut :] for v in came])]

    def over(self, lines):
        first, second = lines
        beside, behind = to_partner(first, 1), to_partner(second, 2)
        return [
            [first, beside, to_partner(first, 2), to_partner(beside, 2)],
            [second, to_partner(second, 1), behind, to_partner(behind, 1)],
        ]

    def whole(self, halves):
        return jnp.concatenate([jnp.concatenate(half, axis=0) for half in halves], axis=1)


class RowSum:
    def __init__(self, *terms):
        groups, rows = terms[0].shape[:2]
        self.type = terms[0].dtype
        cut = rows // 2
        blocks = [v.reshape(PLANE, groups // PLANE, *v.shape[1:]) for v in terms]
        self.halves = (
            ([v[:, :, :cut] for v in blocks], 2, 1),
            ([v[:, :, cut:] for v in blocks], 1, 2),
        )

    def _add(self, parts):
        return add_wide(*parts).astype(self.type)

    def sends(self):
        return [
            jnp.stack([self._add([v[far] for v in held]), self._add([v[far | near] for v in held])])
            for held, far, near in self.halves
        ]

    def move(self, sends):
        return [to_partner(v, far) for v, (_, far, _) in zip(sends, self.halves)]

    def sends_again(self, came):
        return [
            self._add([v[near] for v in held] + [c[1]])
            for c, (held, _, near) in zip(came, self.halves)
        ]

    def move_again(self, sends):
        return [to_partner(v, near) for v, (_, _, near) in zip(sends, self.halves)]

    def line(self, came, came_again):
        sums = [
            self._add([v[0] for v in held] + [c[0], d])
            for c, d, (held, *_) in zip(came, came_again, self.halves)
        ]
        return jnp.concatenate(sums, axis=1)


def line_sends(line):
    return [line[step] for step in range(line.shape[0])]


def line_move(sends):
    return [sends[0]] + [to_deeper(v, -step) for step, v in enumerate(sends) if step > 0]


def dot_nn(left, right):
    return lax.dot_general(left, right, (((1,), (0,)), ((), ())), preferred_element_type=jnp.float32)


def dot_nt(left, right):
    return lax.dot_general(left, right, (((1,), (1,)), ((), ())), preferred_element_type=jnp.float32)


def dot_tn(left, right):
    return lax.dot_general(left, right, (((0,), (0,)), ((), ())), preferred_element_type=jnp.float32)


def two_lanes(column, lane):
    high = column.astype(jnp.bfloat16).astype(jnp.float32)
    spread = jnp.where(lane == 0, high, jnp.where(lane == 1, column - high, 0.0))
    return spread.astype(jnp.bfloat16)


def expert_kernel(
    shared_cols,
    expert_count,
    me_ref,
    hn_own,
    hn_other,
    dy_own,
    dy_other,
    meta_own,
    meta_other,
    gate_up_w,
    down_w,
    first_w,
    sdown_w,
    slots_out,
    slot_dy_out,
    act_out,
    d_gate_up_out,
    rows_own_out,
    rows_other_out,
    sact_own_out,
    sact_other_out,
    dsh_own_out,
    dsh_other_out,
    dgate_own_out,
    dgate_other_out,
):
    f32, bf16 = jnp.float32, jnp.bfloat16
    count, half, _ = hn_own.shape
    tokens = 2 * half
    me = me_ref[0]
    lane = lax.broadcasted_iota(jnp.int32, (tokens, LANES), 1)
    is_router = (lane >= shared_cols) & (lane < shared_cols + expert_count)
    first = first_w[...]
    slots, slot_dys, slot_gates, picks, dshs = [], [], [], [], []
    for i in range(count):
        rows = jnp.concatenate([hn_own[i], hn_other[i]], axis=0)
        rows_dy = jnp.concatenate([dy_own[i], dy_other[i]], axis=0)
        meta = jnp.concatenate([meta_own[i], meta_other[i]], axis=0)
        products = dot_nt(rows, first)
        gate, up = products[:, :LANES], products[:, LANES:]
        sig = jax.nn.sigmoid(gate)
        total = jnp.sum(jnp.where(is_router, sig * meta, 0.0), axis=1, keepdims=True)
        mine = jnp.sum(jnp.where(lane == shared_cols + me, sig, 0.0), axis=1, keepdims=True)
        token_gate = ROUTE_SCALE * mine / total
        sact = (gate * sig * up).astype(bf16)
        sact_own_out[i], sact_other_out[i] = sact[:half], sact[half:]
        d_sact = dot_nt(rows_dy, sdown_w[...])
        d_sgate = d_sact * up * sig * (1.0 + gate * (1.0 - sig))
        dsh = jnp.concatenate([d_sgate, d_sact * gate * sig], axis=1).astype(bf16)
        dsh_own_out[i], dsh_other_out[i] = dsh[:half], dsh[half:]
        dshs.append(dsh)
        pick = (meta[:, :1] == lane.astype(f32)).astype(bf16)
        picks.append(pick)
        slots.append(dot_tn(pick, rows).astype(bf16))
        slot_dys.append(dot_tn(pick, rows_dy).astype(bf16))
        slot_gates.append(
            jnp.sum(dot_tn(pick, two_lanes(token_gate, lane)), axis=1, keepdims=True)
        )
    slot_rows = jnp.concatenate(slots, axis=0)
    slot_dy = jnp.concatenate(slot_dys, axis=0)
    slot_gate = jnp.concatenate(slot_gates, axis=0)
    slots_out[...] = slot_rows
    slot_dy_out[...] = slot_dy
    gate = dot_nt(slot_rows, gate_up_w[0])
    up = dot_nt(slot_rows, gate_up_w[1])
    d_act = dot_nt(slot_dy, down_w[...])
    sig = jax.nn.sigmoid(gate)
    silu = gate * sig
    act = silu * up
    slot_dgate = jnp.sum(act * d_act, axis=1, keepdims=True)
    act_out[...] = (slot_gate * act).astype(bf16)
    d_act = slot_gate * d_act
    d_gate = (d_act * up * sig * (1.0 + gate * (1.0 - sig))).astype(bf16)
    d_up = (d_act * silu).astype(bf16)
    d_gate_up_out[0] = d_gate
    d_gate_up_out[1] = d_up
    d_slots = (dot_nn(d_gate, gate_up_w[0]) + dot_nn(d_up, gate_up_w[1])).astype(bf16)
    slot_lane = lax.broadcasted_iota(jnp.int32, (LANES, LANES), 1)
    for i in range(count):
        here = slice(i * LANES, (i + 1) * LANES)
        d_rows = (dot_nn(picks[i], d_slots[here]) + dot_nn(dshs[i], first)).astype(bf16)
        rows_own_out[i], rows_other_out[i] = d_rows[:half], d_rows[half:]
        dgate = dot_nn(picks[i], two_lanes(slot_dgate[here], slot_lane))
        dgate_own_out[i], dgate_other_out[i] = dgate[:half], dgate[half:]


def block_specs(per_step):
    def lead(*tail):
        return pl.BlockSpec((per_step, *tail), lambda i: (i,) + (0,) * len(tail))

    def flat(cols):
        return pl.BlockSpec((per_step * LANES, cols), lambda i: (i, 0))

    def whole(a):
        return pl.BlockSpec(a.shape, lambda i: (0,) * a.ndim, pipeline_mode=pl.Buffered(1))

    return lead, flat, whole


def slots_cost(width, hidden, products):
    return LANES * width * hidden * products


def experts(
    me,
    hn_own,
    hn_other,
    dy_own,
    dy_other,
    meta_own,
    meta_other,
    gate_up_w,
    down_w,
    first_w,
    sdown_w,
    shared_cols,
    expert_count,
    per_step=2,
):
    groups, half, width = hn_own.shape
    hidden = down_w.shape[0]
    slots = groups * LANES
    f32, bf16 = jnp.float32, jnp.bfloat16
    lead, flat, whole = block_specs(per_step)
    sds = jax.ShapeDtypeStruct
    rows_cost = 2 * groups * (2 * half * width * 4 * LANES + slots_cost(width, hidden, 5))
    return pl.pallas_call(
        functools.partial(expert_kernel, shared_cols, expert_count),
        grid=(groups // per_step,),
        in_specs=[
            pl.BlockSpec(memory_space=pltpu.SMEM),
            *[lead(half, width)] * 4,
            *[lead(half, LANES)] * 2,
            *[whole(a) for a in (gate_up_w, down_w, first_w, sdown_w)],
        ],
        out_specs=[
            flat(width),
            flat(width),
            flat(hidden),
            pl.BlockSpec((2, per_step * LANES, hidden), lambda i: (0, i, 0)),
            *[lead(half, width)] * 2,
            *[lead(half, LANES)] * 2,
            *[lead(half, 2 * LANES)] * 2,
            *[lead(half, LANES)] * 2,
        ],
        out_shape=[
            sds((slots, width), bf16),
            sds((slots, width), bf16),
            sds((slots, hidden), bf16),
            sds((2, slots, hidden), bf16),
            *[sds((groups, half, width), bf16)] * 2,
            *[sds((groups, half, LANES), bf16)] * 2,
            *[sds((groups, half, 2 * LANES), bf16)] * 2,
            *[sds((groups, half, LANES), f32)] * 2,
        ],
        compiler_params=pltpu.CompilerParams(vmem_limit_bytes=58 * 1024 * 1024),
        cost_estimate=pl.CostEstimate(
            flops=rows_cost, bytes_accessed=20 * groups * half * width, transcendentals=0
        ),
    )(
        me,
        hn_own,
        hn_other,
        dy_own,
        dy_other,
        meta_own,
        meta_other,
        gate_up_w,
        down_w,
        first_w,
        sdown_w,
    )


def output_kernel(act, sact_own, sact_other, meta_own, meta_other, down_w, sdown_w, own_out, other_out):
    f32, bf16 = jnp.float32, jnp.bfloat16
    count, half, _ = meta_own.shape
    lane = lax.broadcasted_iota(jnp.int32, (2 * half, LANES), 1).astype(f32)
    out = dot_nn(act[...], down_w[...]).astype(bf16)
    for i in range(count):
        meta = jnp.concatenate([meta_own[i], meta_other[i]], axis=0)
        pick = (meta[:, :1] == lane).astype(bf16)
        sact = jnp.concatenate([sact_own[i], sact_other[i]], axis=0)
        here = slice(i * LANES, (i + 1) * LANES)
        rows = (dot_nn(pick, out[here]) + dot_nn(sact, sdown_w[...])).astype(bf16)
        own_out[i], other_out[i] = rows[:half], rows[half:]


def outputs(act, sact_own, sact_other, meta_own, meta_other, down_w, sdown_w, per_step=4):
    groups, half, _ = meta_own.shape
    hidden, width = down_w.shape
    lead, flat, whole = block_specs(per_step)
    return pl.pallas_call(
        output_kernel,
        grid=(groups // per_step,),
        in_specs=[
            flat(hidden),
            *[lead(half, LANES)] * 4,
            *[whole(a) for a in (down_w, sdown_w)],
        ],
        out_specs=[lead(half, width)] * 2,
        out_shape=[jax.ShapeDtypeStruct((groups, half, width), jnp.bfloat16)] * 2,
        compiler_params=pltpu.CompilerParams(vmem_limit_bytes=58 * 1024 * 1024),
        cost_estimate=pl.CostEstimate(
            flops=groups * half * LANES * width,
            bytes_accessed=groups * half * width,
            transcendentals=0,
        ),
    )(act, sact_own, sact_other, meta_own, meta_other, down_w, sdown_w)


def token_plan(
    inputs,
    attn_gain,
    w_query,
    w_latent,
    latent_gain,
    w_kv,
    w_out,
    ffn_gain,
    w_router,
    shared_gate_up,
    shared_down,
    expert_gate_up,
    expert_down,
    lengths,
    routes,
    cotangent,
):
    f32, bf16 = jnp.float32, jnp.bfloat16
    core, me = lax.axis_index("tensor"), lax.axis_index("expert")
    groups = lax.axis_size("expert")
    deep, place, z = groups // PLANE, me % PLANE, me // PLANE
    tok_rows, width = inputs.shape
    half = tok_rows // 2
    own_at, other_at = core * half, (1 - core) * half
    expert_count = w_router.shape[1]
    route_count = routes.shape[1]
    capacity = tok_rows * route_count * 4 // (3 * expert_count)
    shared_cols = shared_gate_up.shape[2] // groups
    latent_cols, rank_width = w_latent.shape[1], latent_gain.shape[0] * groups
    block_rows = w_query.shape[0]
    kv_rows = w_kv.shape[0]

    query_cols = w_query.shape[1] // PLANE
    out_cols = w_out.shape[0] // PLANE
    used = latent_cols + expert_count + 3
    small = jnp.concatenate(
        [
            w_latent,
            w_router,
            attn_gain[:, None],
            ffn_gain[:, None],
            jnp.pad(latent_gain, (0, block_rows - kv_rows))[:, None],
            jnp.zeros((block_rows, -used % 128), bf16),
        ],
        axis=1,
    )
    small_cols = small.shape[1]
    route_half = take_rows(routes, own_at, half).astype(bf16).reshape(block_rows // 2, -1)
    length_col = jnp.pad(lengths[0].astype(bf16), (0, block_rows // 2 - lengths.shape[1]))[:, None]
    route_cols = route_half.shape[1] + 1
    small_half = jnp.concatenate(
        [
            take_rows(small, core * (block_rows // 2), block_rows // 2),
            jnp.pad(jnp.concatenate([route_half, length_col], axis=1), ((0, 0), (0, -route_cols % 128))),
        ],
        axis=1,
    )
    packed_cols = small_half.shape[1] // 2
    small_packed = jnp.concatenate([small_half[:, :packed_cols], small_half[:, packed_cols:]])
    kv_cols = w_kv.shape[1] // PLANE
    kv_parts = block_rows // kv_rows
    kv_piece = kv_cols // kv_parts
    w_out_t = w_out.T

    def quarter(index):
        kv_here = take_rows(w_kv, index * kv_cols, kv_cols, axis=1)
        kv_here = [kv_here[:, p * kv_piece : (p + 1) * kv_piece] for p in range(kv_parts)]
        return jnp.concatenate(
            [
                take_rows(w_query, index * query_cols, query_cols, axis=1),
                take_rows(w_out_t, index * out_cols, out_cols, axis=1),
                jnp.concatenate(kv_here, axis=0),
            ],
            axis=1,
        )

    near_w = [quarter(place)] + [to_partner(quarter(place ^ r), r) for r in range(1, PLANE)]
    small_line = deep_join(small_packed, deep_pieces(small_packed), z)
    near_w, small_line = tie(near_w, small_line)
    plane_w = jnp.stack(by_place(near_w, place))
    near_sent = jnp.concatenate(
        [
            take_rows(inputs, own_at, half),
            small_line.swapaxes(0, 1).reshape(block_rows, -1),
        ],
        axis=1,
    )
    near_sent, plane_w = tie(near_sent, plane_w)
    near_came = jnp.stack([near_sent, to_partner(near_sent, 1)])
    near_came = jnp.concatenate([near_came, to_partner(near_came, 2)], axis=0)
    near_came, deep_w = tie(near_came, deep_pieces(plane_w))
    x_near_own = near_came[:, :, :width]
    small_parts = near_came[:, :, width:].reshape(PLANE, block_rows, deep, packed_cols)
    small_parts = [small_parts[r].swapaxes(0, 1) for r in range(PLANE)]
    x_near = in_order(core, x_near_own, swap_cores(x_near_own), axis=1)
    x_near = lax.optimization_barrier(x_near.reshape(PLANE * tok_rows, width))
    small_own = jnp.stack(by_place(small_parts, place), axis=1)
    small_own = small_own.reshape(groups, block_rows, packed_cols)
    small_own = jnp.concatenate(
        [small_own[:, : block_rows // 2], small_own[:, block_rows // 2 :]], axis=2
    )
    small_other = swap_cores(small_own)
    small_all = in_order(core, small_own, small_other, axis=1)
    head_w = deep_join(plane_w, deep_w, z)
    length_at = small_cols + route_cols - 1
    lengths_near = take_rows(small_own, z * PLANE, PLANE)[:, : lengths.shape[1], length_at]
    lengths_near = lengths_near.astype(jnp.int32)
    lengths_near = jnp.stack(by_place([lengths_near[r] for r in range(PLANE)], place))
    shared_rows = jnp.concatenate(
        [shared_gate_up[0].T, shared_gate_up[1].T, shared_down], axis=0
    ).reshape(3, groups, shared_cols, block_rows)
    shared_rows = shared_rows.swapaxes(0, 1).reshape(groups, 3 * shared_cols, block_rows)
    dy_sent, head_w = tie(take_rows(cotangent, own_at, half), head_w)
    dy_own_rows = take_rows(cotangent, own_at, half)
    dy_gather = RowGather(dy_sent)
    dy_came = dy_gather.along()
    head_w = head_w.reshape(groups, block_rows, -1)
    flat_head = head_w.reshape(groups * block_rows, -1)
    query_w = flat_head[:, :query_cols]
    at = query_cols + out_cols
    out_wt = flat_head[:, query_cols:at]
    kv_w = head_w[:, :, at : at + kv_piece].reshape(groups, kv_parts, kv_rows, kv_piece)
    kv_w = kv_w.transpose(0, 2, 1, 3).reshape(groups * kv_rows, kv_cols)

    block_index = jnp.arange(groups)
    block_chip = (z - block_index % deep) % deep * PLANE + (place ^ (block_index // deep))
    in_blocks = (block_chip[:, None] == block_index[None, :]).astype(bf16)

    def routes_of(came):
        came = came[:, :, small_cols : small_cols + route_half.shape[1]].reshape(groups, -1)
        came = jnp.dot(in_blocks, came, preferred_element_type=f32)
        return came.astype(jnp.int32).reshape(groups, half, route_count)

    routes_own, routes_other = routes_of(small_own), routes_of(small_other)
    flat_small = small_all.reshape(groups * block_rows, -1)
    latent_w = flat_small[:, :latent_cols]
    at = latent_cols
    router_w = flat_small[:, at : at + expert_count]
    at += expert_count
    gain_one, gain_two = flat_small[:, at], flat_small[:, at + 1]
    latent_g = small_all[:, :kv_rows, at + 2].reshape(-1)

    near_rows = PLANE * tok_rows
    local_heads = query_cols // (DN + DR)
    x_float = x_near.astype(f32)
    relative, visible = jax.vmap(lambda one: doc_layout(one, tok_rows))(lengths_near)
    cosine, sine_tab = rope_tables(relative.reshape(-1), DR)
    q_scale = (DN + DR) ** (-0.5)
    scale_one = lax.rsqrt(jnp.mean(x_float * x_float, axis=-1, keepdims=True) + EPSILON)
    scale_one = lax.optimization_barrier(scale_one)
    normed_b = (x_near.astype(f32) * scale_one * gain_one.astype(f32)).astype(bf16)
    normed_b = lax.optimization_barrier(normed_b)
    queries = jnp.dot(normed_b, query_w, preferred_element_type=f32).reshape(
        near_rows, local_heads, DN + DR
    )
    q_rot = rotate(queries[..., DN:], cosine[:, None, :], sine_tab[:, None, :])
    q_all = jnp.concatenate([queries[..., :DN], q_rot], axis=-1).astype(bf16)
    q_all = q_all.reshape(PLANE, tok_rows, local_heads, DN + DR)
    latent = jnp.dot(normed_b, latent_w, preferred_element_type=f32)
    compressed, _ = rms_forward(latent[:, :rank_width], latent_g.astype(f32))
    compressed_b = compressed.astype(bf16)
    k_rope = rotate(latent[:, rank_width:], cosine, sine_tab).astype(bf16)
    kv_all = jnp.dot(compressed_b, kv_w, preferred_element_type=f32).reshape(
        PLANE, tok_rows, local_heads, DN + DV
    )
    k_nope = kv_all[..., :DN].astype(bf16)
    values = kv_all[..., DN:].astype(bf16)
    k_rope = k_rope.reshape(PLANE, tok_rows, 1, DR)
    key_all = jnp.concatenate(
        [k_nope, jnp.broadcast_to(k_rope, (PLANE, tok_rows, local_heads, DR))], axis=-1
    )

    def score_block():
        raw_scores = (
            jnp.einsum("gqhd,gkhd->ghqk", q_all, key_all, preferred_element_type=f32) * q_scale
        )
        return jnp.where(visible[:, None], raw_scores, NEGATIVE)

    scores = score_block()
    top_score = jnp.max(scores, axis=-1, keepdims=True)
    log_total = top_score + jnp.log(jnp.sum(jnp.exp(scores - top_score), axis=-1, keepdims=True))
    probs_b = jnp.exp(scores - log_total).astype(bf16)
    attended = jnp.einsum("ghqk,gkhd->gqhd", probs_b, values, preferred_element_type=f32)
    attended_b = attended.reshape(near_rows, local_heads * DV).astype(bf16)
    attended_b, dy_came = tie(attended_b, dy_came)

    def sum_heads(part):
        part = part.astype(bf16).reshape(PLANE, tok_rows, -1)
        came = swap_cores(take_rows(part, other_at, half, axis=1))
        both = add_wide(take_rows(part, own_at, half, axis=1), came).astype(bf16)
        return plane_scatter([both[r] for r in range(PLANE)])

    attn_own = sum_heads(contract_cols(attended_b, out_wt))
    x_own = take_rows(inputs, own_at, half).astype(f32)
    hidden = x_own + attn_own
    hnormed, scale_two = rms_forward(hidden, gain_two.astype(f32))
    hnormed_b = hnormed.astype(bf16)
    normed_cols = jnp.concatenate(
        [
            take_rows(normed_b, (k * PLANE + place) * block_rows, block_rows, axis=1)
            for k in range(deep)
        ],
        axis=1,
    )
    hnormed_b, dy_lines, normed_cols, shared_rows = tie(
        hnormed_b, dy_gather.lines(dy_came), normed_cols, shared_rows
    )
    hn_gather = RowGather(hnormed_b)
    hn_came, dy_halves, shared_rows = tie(
        hn_gather.along(), dy_gather.over(dy_lines), shared_rows
    )
    hn_lines, dy_halves, shared_rows = tie(hn_gather.lines(hn_came), dy_halves, shared_rows)
    hn_halves = hn_gather.over(hn_lines)
    shared_w = lax.all_to_all(shared_rows, "expert", split_axis=0, concat_axis=0, tiled=True)
    dy_own = dy_gather.whole(dy_halves)
    dy_other = swap_cores(dy_own)
    hn_halves, shared_w, dy_other = tie(hn_halves, shared_w, dy_other)
    shared_w = shared_w.swapaxes(0, 1).reshape(3 * shared_cols, groups * block_rows)
    hn_own = hn_gather.whole(hn_halves)


    def membership(named):
        one_hot = named[..., None] == jnp.arange(expert_count, dtype=jnp.int32)
        return jnp.any(named == me, axis=-1), jnp.any(one_hot, axis=2)

    member_own, hot_own = membership(routes_own)
    member_other, hot_other = membership(routes_other)
    lower = (
        jnp.arange(half, dtype=jnp.int32)[:, None] <= jnp.arange(half, dtype=jnp.int32)[None, :]
    ).astype(bf16)

    def running(mask):
        counts = jnp.dot(mask.astype(bf16), lower, preferred_element_type=f32)
        return counts.astype(jnp.int32)

    count_own, count_other = running(member_own), running(member_other)
    place_own = jnp.where(member_own, count_own - 1, -1)
    place_other = jnp.where(member_other, count_own[:, -1:] + count_other - 1, -1)

    def metadata(slot, hot):
        return jnp.concatenate(
            [
                slot[..., None].astype(f32),
                jnp.zeros((groups, half, shared_cols - 1), f32),
                hot.astype(f32),
                jnp.zeros((groups, half, LANES - shared_cols - expert_count), f32),
            ],
            axis=-1,
        )

    meta_own, meta_other = metadata(place_own, hot_own), metadata(place_other, hot_other)
    first_w = jnp.concatenate(
        [
            shared_w[:shared_cols],
            router_w.T,
            jnp.zeros((LANES - shared_cols - expert_count, width), bf16),
            shared_w[shared_cols : 2 * shared_cols],
            jnp.zeros((LANES - shared_cols, width), bf16),
        ],
        axis=0,
    )
    sdown_rows = jnp.pad(shared_w[2 * shared_cols :], ((0, LANES - shared_cols), (0, 0)))
    hn_other = swap_cores(hn_own)
    gate_up_w, down_w = jnp.swapaxes(expert_gate_up[0], 1, 2), expert_down[0]
    (
        slot_rows,
        slot_dy,
        slot_act,
        d_gate_up,
        d_rows_own,
        d_rows_other,
        act_own,
        act_other,
        d_shared_own,
        d_shared_other,
        dgate_own,
        dgate_other,
    ) = experts(
        me.reshape(1).astype(jnp.int32),
        hn_own,
        hn_other,
        dy_own,
        dy_other,
        meta_own,
        meta_other,
        gate_up_w,
        down_w,
        first_w,
        sdown_rows,
        shared_cols,
        expert_count,
    )
    d_rows_came = swap_cores(d_rows_other)

    def two_parts(value):
        return value[..., 0] + value[..., 1]

    def flat_rows(value):
        return value.reshape(groups * half, -1)

    first_grad = contract_rows(flat_rows(d_shared_own), flat_rows(hn_own)) + contract_rows(
        flat_rows(d_shared_other), flat_rows(hn_other)
    )
    sdown_grad = contract_rows(flat_rows(act_own), flat_rows(dy_own)) + contract_rows(
        flat_rows(act_other), flat_rows(dy_other)
    )
    dgate_sent = two_parts(dgate_own) + swap_cores(two_parts(dgate_other))
    dgate_high = dgate_sent.astype(bf16)
    dgate_low = (dgate_sent - dgate_high.astype(f32)).astype(bf16)
    grads_sent = jnp.concatenate(
        [
            first_grad[:shared_cols].astype(bf16),
            first_grad[LANES : LANES + shared_cols].astype(bf16),
            sdown_grad[:shared_cols].astype(bf16),
            contract_rows(in_blocks, dgate_high).astype(bf16).reshape(1, -1),
            contract_rows(in_blocks, dgate_low).astype(bf16).reshape(1, -1),
        ],
        axis=0,
    ).reshape(-1, groups, block_rows)
    d_rows_came, grads_sent = tie(d_rows_came, grads_sent)
    d_sum = RowSum(d_rows_own, d_rows_came)
    sends, grads_sent, slot_act = tie(d_sum.sends(), grads_sent, slot_act)
    came = d_sum.move(sends)
    grads_came = lax.all_to_all(grads_sent, "expert", split_axis=1, concat_axis=1, tiled=True)
    out_own, out_other = outputs(
        slot_act, act_own, act_other, meta_own, meta_other, down_w, sdown_rows
    )
    out_came = swap_cores(out_other)
    edown_grad = contract_rows(slot_act, slot_dy)
    came, out_came, edown_grad, grads_came = tie(came, out_came, edown_grad, grads_came)
    sgu_out, sdown_out, dgate = (
        grads_came[: 2 * shared_cols],
        grads_came[2 * shared_cols : 3 * shared_cols],
        add_wide(grads_came[3 * shared_cols], grads_came[3 * shared_cols + 1]).T,
    )
    sgu_out = sgu_out.astype(f32).reshape(2, shared_cols, groups, block_rows)
    sgu_out = sgu_out.transpose(0, 3, 2, 1).reshape(2, block_rows, -1)
    sdown_out = sdown_out.astype(f32).swapaxes(0, 1).reshape(-1, block_rows)
    sends, slot_rows, out_came = tie(d_sum.sends_again(came), slot_rows, out_came)
    came_again = d_sum.move_again(sends)
    egu_grad = jnp.einsum("sd,gsf->gdf", slot_rows, d_gate_up, preferred_element_type=f32)
    out_sum = RowSum(out_own, out_came)
    out_sends = out_sum.sends()
    came_again, egu_grad, out_sends = tie(came_again, egu_grad, out_sends)
    z_sends, out_sends, dgate = tie(
        line_sends(d_sum.line(came, came_again)), out_sends, dgate
    )
    z_came = line_move(z_sends)
    out_first = out_sum.move(out_sends)
    hot_mine = take_rows(
        jnp.any(routes[..., None] == jnp.arange(expert_count, dtype=jnp.int32), axis=1), own_at, half
    )
    sig = jax.nn.sigmoid(jnp.dot(hnormed_b, router_w, preferred_element_type=f32))
    chosen = jnp.where(hot_mine, sig, 0.0)
    chosen_sum = jnp.sum(chosen, axis=1, keepdims=True)
    dgate = jnp.where(hot_mine, dgate, 0.0)
    inner = jnp.sum(dgate * chosen, axis=1, keepdims=True)
    d_chosen = ROUTE_SCALE * (dgate / chosen_sum - inner / (chosen_sum * chosen_sum))
    d_logits = (jnp.where(hot_mine, d_chosen, 0.0) * sig * (1.0 - sig)).astype(bf16)
    router_grad = contract_rows(d_logits, hnormed_b)
    z_came, d_logits, router_grad = tie(z_came, d_logits, router_grad)
    d_hn = add_wide(*z_came)
    d_hn = d_hn + contract_cols(d_logits, router_w)
    d_hidden_norm, gain_two_grad = rms_backward(hidden, scale_two, gain_two.astype(f32), d_hn)
    d_hidden = dy_own_rows.astype(f32) + d_hidden_norm
    d_parts, out_first = tie(plane_gather(d_hidden.astype(bf16)), out_first)
    d_near_own = jnp.stack(d_parts)
    d_near = in_order(core, d_near_own, swap_cores(d_near_own), axis=1).reshape(near_rows, width)

    out_sends, d_near = tie(out_sum.sends_again(out_first), d_near)
    out_second = out_sum.move_again(out_sends)

    grad_att = (
        jnp.dot(d_near, out_wt, preferred_element_type=f32)
        .reshape(PLANE, tok_rows, local_heads, DV)
        .astype(bf16)
    )
    out_grad = contract_rows(d_near, attended_b).astype(bf16)
    out_grad, grad_att = tie(out_grad, grad_att)
    out_sums = sum_planes(out_grad, z)
    probs = jnp.exp(score_block() - log_total)
    probs_again = probs.astype(bf16)
    grad_probs = jnp.einsum("gqhd,gkhd->ghqk", grad_att, values, preferred_element_type=f32)
    grad_vals = jnp.einsum("ghqk,gqhd->gkhd", probs_again, grad_att, preferred_element_type=f32)
    row_delta = jnp.sum(probs * grad_probs, axis=-1, keepdims=True)
    grad_scores = (probs * (grad_probs - row_delta)).astype(bf16)
    grad_q = (
        jnp.einsum("ghqk,gkhd->gqhd", grad_scores, key_all, preferred_element_type=f32) * q_scale
    ).reshape(near_rows, local_heads, DN + DR)
    grad_keys = (
        jnp.einsum("ghqk,gqhd->gkhd", grad_scores, q_all, preferred_element_type=f32) * q_scale
    )
    grad_kv = (
        jnp.concatenate([grad_keys[..., :DN], grad_vals], axis=-1)
        .reshape(near_rows, local_heads * (DN + DV))
        .astype(bf16)
    )
    grad_latent_part = jnp.concatenate(
        [
            contract_cols(grad_kv, kv_w),
            jnp.sum(grad_keys[..., DN:], axis=2).reshape(near_rows, DR),
        ],
        axis=1,
    )
    grad_both = sum_heads(grad_latent_part)
    latent_own = take_rows(latent[:tok_rows], own_at, half)
    cosine_own = take_rows(cosine[:tok_rows], own_at, half)
    sine_own = take_rows(sine_tab[:tok_rows], own_at, half)
    _, scale_kv = rms_forward(latent_own[:, :rank_width], latent_g.astype(f32))
    grad_c, latent_gain_grad = rms_backward(
        latent_own[:, :rank_width], scale_kv, latent_g.astype(f32), grad_both[:, :rank_width]
    )
    grad_latent = jnp.concatenate(
        [grad_c, unrotate(grad_both[:, rank_width:], cosine_own, sine_own)], axis=-1
    ).astype(bf16)
    grad_qrot = unrotate(grad_q[..., DN:], cosine[:, None, :], sine_tab[:, None, :])
    grad_queries = (
        jnp.concatenate([grad_q[..., :DN], grad_qrot], axis=-1)
        .reshape(near_rows, local_heads * (DN + DR))
        .astype(bf16)
    )
    out_second, grad_kv, grad_queries = tie(out_second, grad_kv, grad_queries)
    out_z, grad_kv, grad_queries = tie(
        line_sends(out_sum.line(out_first, out_second)), grad_kv, grad_queries
    )
    out_z = line_move(out_z)
    kv_grad = contract_rows(compressed_b, grad_kv).astype(bf16)
    kv_grad = kv_grad.reshape(groups, kv_rows, kv_parts, kv_piece).transpose(0, 2, 1, 3)
    query_grad = contract_rows(normed_b, grad_queries).astype(bf16)
    first_sums = sum_planes(
        jnp.concatenate([query_grad, kv_grad.reshape(-1, kv_piece)], axis=1), z
    )
    shared_out = share_columns(jnp.concatenate([first_sums, out_sums], axis=2), place)
    at_kv, at_out = query_cols, query_cols + kv_piece
    w_query_grad = jnp.concatenate([p[:, :at_kv] for p in shared_out], axis=1).astype(f32)
    w_kv_grad = jnp.concatenate(
        [
            p[q * kv_rows : (q + 1) * kv_rows, at_kv:at_out]
            for p in shared_out
            for q in range(kv_parts)
        ],
        axis=1,
    ).astype(f32)
    w_out_grad = jnp.concatenate([p[:, at_out:] for p in shared_out], axis=1).astype(f32).T
    grad_normed = sum_heads(contract_cols(grad_queries, query_w))
    grad_normed = grad_normed + contract_cols(grad_latent, latent_w)
    moe_own = add_wide(*out_z)
    mixed_own = (hidden + moe_own).astype(bf16)
    mixed = in_order(core, mixed_own, swap_cores(mixed_own))

    _, scale_own = rms_forward(x_own, gain_one.astype(f32))
    grad_x_norm, gain_one_grad = rms_backward(x_own, scale_own, gain_one.astype(f32), grad_normed)
    input_own = d_hidden + grad_x_norm
    input_grad = in_order(core, input_own, swap_cores(input_own))

    latent_near_own = jnp.stack(plane_gather(grad_latent))
    latent_near = in_order(core, latent_near_own, swap_cores(latent_near_own), axis=1)
    latent_cut = latent_cols // 2
    latent_near = latent_near.reshape(near_rows, latent_cols)
    latent_blocks = contract_rows(
        normed_cols,
        take_rows(latent_near, core * latent_cut, latent_cut, axis=1),
    )
    latent_half = deep_scatter(latent_blocks.astype(bf16).reshape(deep, -1, latent_cut), z)
    w_latent_grad = in_order(core, latent_half, swap_cores(latent_half), axis=1)

    gain_lanes = jnp.pad(
        latent_gain_grad.reshape(groups, kv_rows), ((0, 0), (0, block_rows - kv_rows))
    )
    vectors = jnp.concatenate(
        [
            router_grad,
            gain_one_grad[None],
            gain_two_grad[None],
            gain_lanes.reshape(1, -1),
        ],
        axis=0,
    ).reshape(-1, groups, block_rows)
    arrived = lax.all_to_all(vectors, "expert", split_axis=1, concat_axis=1, tiled=True)
    sums = jnp.sum(arrived, axis=1)
    sums = sums + swap_cores(sums)
    return (
        mixed,
        input_grad,
        sums[expert_count],
        w_query_grad,
        w_latent_grad,
        sums[expert_count + 2, :kv_rows],
        w_kv_grad,
        w_out_grad,
        sums[expert_count + 1],
        sums[:expert_count].T,
        sgu_out,
        sdown_out,
        egu_grad[None],
        edown_grad[None],
    )


def solution(mesh):
    groups = mesh.shape["expert"]
    plan = token_plan if groups <= 16 else weight_plan
    return jax.shard_map(
        plan,
        mesh=mesh,
        in_specs=(
            P("expert", None),
            P("expert"),
            P("expert", "tensor"),
            P("expert", None),
            P("expert"),
            P("expert", "tensor"),
            P("tensor", "expert"),
            P("expert"),
            P("expert", None),
            P(None, "expert", "tensor"),
            P("tensor", "expert"),
            P("expert", None, None, "tensor"),
            P("expert", "tensor", None),
            P("expert", None),
            P("expert", None),
            P("expert", None),
        ),
        out_specs=(
            P("expert", None),
            P("expert", None),
            P("expert"),
            P("expert", "tensor"),
            P("expert", None),
            P("expert"),
            P("expert", "tensor"),
            P("tensor", "expert"),
            P("expert"),
            P("expert", None),
            P(None, "expert", "tensor"),
            P("tensor", "expert"),
            P("expert", None, None, "tensor"),
            P("expert", "tensor", None),
        ),
        check_vma=False,
    )
```

```python
import functools

import jax
import jax.numpy as jnp
from jax import lax
from jax.experimental import pallas as pl
from jax.experimental.pallas import tpu as pltpu
from jax.sharding import PartitionSpec as P

DN = 128
DR = 64
DV = 128
LANES = 128


EPSILON = 1e-06
ROUTE_SCALE = 2.446
ROPE_BASE = 50000.0
NEGATIVE = -1e30


def cut_along(value, dim, length):
    before, after = (value.shape[:dim], value.shape[dim + 1 :])
    return jnp.moveaxis(value.reshape(*before, length, -1, *after), dim, 0)


def summed_on_arrival(value, axis, dim):
    length = lax.axis_size(axis)
    tiles = lax.all_to_all(cut_along(value, dim, length), axis, 0, 0, tiled=True)
    return jnp.sum(tiles.astype(jnp.float32), axis=0)


def sent_together(arrays, axis, dim, along):
    columns = [a.reshape(*a.shape[:along], -1) for a in arrays]
    both = jnp.concatenate(columns, axis=along)
    whole, at, outs = (summed_on_arrival(both, axis, dim), 0, [])
    for a, column in zip(arrays, columns):
        slab = whole[..., at : at + column.shape[along]]
        outs.append(slab.reshape(*slab.shape[:along], *a.shape[along:]))
        at += column.shape[along]
    return tuple(outs)


def contract_rows(left_arr, right_arr):
    return lax.dot_general(
        left_arr, right_arr, (((0,), (0,)), ((), ())), preferred_element_type=jnp.float32
    )


def contract_cols(left_arr, right_arr):
    return lax.dot_general(
        left_arr, right_arr, (((1,), (1,)), ((), ())), preferred_element_type=jnp.float32
    )


def rms_forward(rows_in, gain_vec):
    inverse = lax.rsqrt(jnp.mean(rows_in * rows_in, axis=-1, keepdims=True) + EPSILON)
    return (rows_in * inverse * gain_vec, inverse)


def rms_backward(rows_in, inverse, gain_vec, grad_out):
    gain_grad = jnp.sum(grad_out * rows_in * inverse, axis=0)
    weighted = grad_out * gain_vec
    inner_mean = jnp.mean(weighted * rows_in, axis=-1, keepdims=True)
    return (inverse * weighted - rows_in * inverse * inverse * inverse * inner_mean, gain_grad)


def doc_layout(doc_lengths, row_count):
    ends_at = jnp.cumsum(doc_lengths)
    starts_at = ends_at - doc_lengths
    position = jnp.arange(row_count, dtype=jnp.int32)
    doc_ids = jnp.sum((position[:, None] >= ends_at[None, :]).astype(jnp.int32), axis=1)
    hitting = doc_ids[:, None] == jnp.arange(doc_lengths.shape[0], dtype=jnp.int32)[None, :]
    start_of = jnp.sum(jnp.where(hitting, starts_at[None, :], 0), axis=1)
    relative = position - start_of
    visible = (doc_ids[:, None] == doc_ids[None, :]) & (position[:, None] >= position[None, :])
    return (relative, visible)


def rope_tables(relative, rot_width):
    counter = jnp.arange(rot_width // 2, dtype=jnp.float32)
    frequency = ROPE_BASE ** (-2.0 * counter / rot_width)
    angles = relative.astype(jnp.float32)[:, None] * frequency[None, :]
    return (jnp.cos(angles), jnp.sin(angles))


def rotate(tensor_in, cosine, sine_tab):
    half_width = tensor_in.shape[-1] // 2
    leading = tensor_in[..., :half_width]
    trailing = tensor_in[..., half_width:]
    return jnp.concatenate(
        [leading * cosine - trailing * sine_tab, trailing * cosine + leading * sine_tab], axis=-1
    )


def unrotate(grad_in, cosine, sine_tab):
    half_width = grad_in.shape[-1] // 2
    leading = grad_in[..., :half_width]
    trailing = grad_in[..., half_width:]
    return jnp.concatenate(
        [leading * cosine + trailing * sine_tab, trailing * cosine - leading * sine_tab], axis=-1
    )


def gated_linear_backward(gate_in, up_in, grad_act):
    sigmoid_g = jax.nn.sigmoid(gate_in)
    grad_gate = grad_act * up_in * sigmoid_g * (1.0 + gate_in * (1.0 - sigmoid_g))
    return (grad_gate, grad_act * gate_in * sigmoid_g)


def slot_tables(route_rows, expert_count, capacity):
    flat_routes = route_rows.reshape(-1)
    one_hot = (flat_routes[:, None] == jnp.arange(expert_count, dtype=jnp.int32)[None, :]).astype(
        jnp.int32
    )
    ranking = jnp.sum((jnp.cumsum(one_hot, axis=0) - one_hot) * one_hot, axis=1)
    slot_ids = flat_routes * capacity + ranking
    row_total = flat_routes.shape[0]
    source = (
        jnp.zeros((expert_count * capacity,), jnp.int32)
        .at[slot_ids]
        .set(jnp.arange(row_total, dtype=jnp.int32))
    )
    filled = jnp.zeros((expert_count * capacity,), jnp.int32).at[slot_ids].set(1)
    return (slot_ids, source, filled)


def to_owner(rows_in):
    arrived = lax.all_to_all(rows_in, "expert", split_axis=0, concat_axis=1, tiled=True)
    return arrived


def weight_plan(
    inputs,
    attn_gain,
    w_query,
    w_latent,
    latent_gain,
    w_kv,
    w_out,
    ffn_gain,
    w_router,
    shared_gate_up,
    shared_down,
    expert_gate_up,
    expert_down,
    lengths,
    routes,
    cotangent,
):
    tok_rows = inputs.shape[0]
    model_width = inputs.shape[1]
    expert_count = w_router.shape[1]
    route_count = routes.shape[1]
    capacity = tok_rows * route_count * 4 // (3 * expert_count)
    brain_float16 = jnp.bfloat16
    f32 = jnp.float32
    gathered = (
        lax.all_gather(attn_gain, "expert", axis=0, tiled=True),
        lax.all_gather(w_query, "expert", axis=0, tiled=True),
        lax.all_gather(w_latent, "expert", axis=0, tiled=True),
        lax.all_gather(latent_gain, "expert", axis=0, tiled=True),
        lax.all_gather(w_kv, "expert", axis=0, tiled=True),
        lax.all_gather(w_out, "expert", axis=1, tiled=True),
        lax.all_gather(ffn_gain, "expert", axis=0, tiled=True),
        lax.all_gather(w_router, "expert", axis=0, tiled=True),
        lax.all_gather(shared_gate_up, "expert", axis=1, tiled=True),
        lax.all_gather(shared_down, "expert", axis=1, tiled=True),
    )
    gain_one, query_w, latent_w, latent_g, kv_w, out_w, gain_two, router_w, sgate_up, sdown_w = (
        gathered
    )
    local_heads = query_w.shape[1] // (DN + DR)
    rank_width = latent_g.shape[0]
    x_float = inputs.astype(f32)
    relative, visible = doc_layout(lengths[0], tok_rows)
    cosine, sine_tab = rope_tables(relative, DR)
    q_scale = (DN + DR) ** (-0.5)
    normed, scale_one = rms_forward(x_float, gain_one.astype(f32))
    normed_b = normed.astype(brain_float16)
    queries = jnp.dot(normed_b, query_w, preferred_element_type=f32).reshape(
        tok_rows, local_heads, DN + DR
    )
    q_rot = rotate(queries[..., DN:], cosine[:, None, :], sine_tab[:, None, :])
    q_all = jnp.concatenate([queries[..., :DN], q_rot], axis=-1).astype(brain_float16)
    latent = jnp.dot(normed_b, latent_w, preferred_element_type=f32)
    compressed, scale_kv = rms_forward(latent[:, :rank_width], latent_g.astype(f32))
    compressed_b = compressed.astype(brain_float16)
    k_rope = rotate(latent[:, rank_width:], cosine, sine_tab).astype(brain_float16)
    kv_all = jnp.dot(compressed_b, kv_w, preferred_element_type=f32).reshape(
        tok_rows, local_heads, DN + DV
    )
    k_nope = kv_all[..., :DN].astype(brain_float16)
    values = kv_all[..., DN:].astype(brain_float16)
    key_all = jnp.concatenate(
        [k_nope, jnp.broadcast_to(k_rope[:, None, :], (tok_rows, local_heads, DR))], axis=-1
    )

    def score_block():
        raw_scores = (
            jnp.einsum("qhd,khd->hqk", q_all, key_all, preferred_element_type=f32) * q_scale
        )
        return jnp.where(visible[None], raw_scores, NEGATIVE)

    scores = score_block()
    top_score = jnp.max(scores, axis=-1, keepdims=True)
    log_total = top_score + jnp.log(jnp.sum(jnp.exp(scores - top_score), axis=-1, keepdims=True))
    probs_b = jnp.exp(scores - log_total).astype(brain_float16)
    attended = jnp.einsum("hqk,khd->qhd", probs_b, values, preferred_element_type=f32)
    attended_b = attended.reshape(tok_rows, local_heads * DV).astype(brain_float16)
    attn = lax.psum(jnp.dot(attended_b, out_w, preferred_element_type=f32), "tensor")
    hidden = x_float + attn
    hnormed, scale_two = rms_forward(hidden, gain_two.astype(f32))
    hnormed_b = hnormed.astype(brain_float16)
    logits = jnp.dot(hnormed_b, router_w, preferred_element_type=f32)
    sigmoid_vals = jax.nn.sigmoid(logits)
    route_hot = routes[:, :, None] == jnp.arange(expert_count, dtype=jnp.int32)[None, None, :]
    chosen = jnp.sum(jnp.where(route_hot, sigmoid_vals[:, None, :], 0.0), axis=2)
    chosen_sum = jnp.sum(chosen, axis=1, keepdims=True)
    gate_vals = ROUTE_SCALE * chosen / chosen_sum
    slot_ids, source, filled = slot_tables(routes, expert_count, capacity)
    is_filled = filled[:, None] == 1
    sent_rows = jnp.where(is_filled, hnormed_b[source // route_count], 0).reshape(
        expert_count, capacity, model_width
    )
    received = to_owner(sent_rows)
    gate_up_joined = jnp.einsum(
        "erd,egdf->egrf", received, expert_gate_up, preferred_element_type=f32
    )
    expert_act = (jax.nn.silu(gate_up_joined[:, 0]) * gate_up_joined[:, 1]).astype(brain_float16)
    expert_res = jnp.einsum(
        "erf,efd->erd", expert_act, expert_down, preferred_element_type=f32
    ).astype(brain_float16)
    returned_all = lax.all_to_all(expert_res, "expert", split_axis=1, concat_axis=0, tiled=True)
    returned = returned_all.reshape(expert_count * capacity, model_width)[slot_ids].reshape(
        tok_rows, route_count, model_width
    )
    shared_gu = jnp.einsum("td,gdf->gtf", hnormed_b, sgate_up, preferred_element_type=f32)
    shared_act = (jax.nn.silu(shared_gu[0]) * shared_gu[1]).astype(brain_float16)
    branch_sum = jnp.dot(shared_act, sdown_w, preferred_element_type=f32)
    for route_idx in range(route_count):
        branch_sum = branch_sum + gate_vals[:, route_idx : route_idx + 1] * returned[
            :, route_idx
        ].astype(f32)
    moe_out = lax.psum(branch_sum.astype(jnp.bfloat16), "tensor").astype(jnp.float32)
    mixed = (hidden + moe_out).astype(brain_float16)
    grad_y = cotangent.astype(f32)
    sdown_grad = contract_rows(shared_act, cotangent)
    grad_sact = contract_cols(cotangent, sdown_w)
    grad_sgate, grad_sup = gated_linear_backward(shared_gu[0], shared_gu[1], grad_sact)
    grad_sgu = jnp.stack([grad_sgate, grad_sup], axis=0).astype(brain_float16)
    sgu_grad = jnp.einsum("td,gtf->gdf", hnormed_b, grad_sgu, preferred_element_type=f32)
    grad_hn_part = jnp.einsum("gtf,gdf->td", grad_sgu, sgate_up, preferred_element_type=f32)
    gate_columns = []
    for route_idx in range(route_count):
        gate_columns.append(jnp.sum(grad_y * returned[:, route_idx].astype(f32), axis=1))
    gate_part = jnp.stack(gate_columns, axis=1)
    slot_grads = (
        (gate_vals[:, :, None] * grad_y[:, None, :])
        .reshape(tok_rows * route_count, model_width)
        .astype(brain_float16)
    )
    grad_sent = jnp.where(is_filled, slot_grads[source], 0).reshape(
        expert_count, capacity, model_width
    )
    grad_received = to_owner(grad_sent)
    edown_grad = jnp.einsum("erf,erd->efd", expert_act, grad_received, preferred_element_type=f32)
    expert_activation_gradient = jnp.einsum(
        "erd,efd->erf", grad_received, expert_down, preferred_element_type=f32
    )
    expert_gate_gradient, expert_up_gradient = gated_linear_backward(
        gate_up_joined[:, 0], gate_up_joined[:, 1], expert_activation_gradient
    )
    expert_gate_up_gradient = jnp.stack([expert_gate_gradient, expert_up_gradient], axis=1).astype(
        brain_float16
    )
    egu_grad = jnp.einsum(
        "erd,egrf->egdf", received, expert_gate_up_gradient, preferred_element_type=f32
    )
    grad_rows = jnp.einsum(
        "egrf,egdf->erd", expert_gate_up_gradient, expert_gate_up, preferred_element_type=f32
    ).astype(brain_float16)
    grad_back = lax.all_to_all(grad_rows, "expert", split_axis=1, concat_axis=0, tiled=True)
    grad_routes = grad_back.reshape(expert_count * capacity, model_width)[slot_ids].reshape(
        tok_rows, route_count, model_width
    )
    for route_idx in range(route_count):
        grad_hn_part = grad_hn_part + grad_routes[:, route_idx].astype(f32)
    gate_grads = lax.psum(gate_part, "tensor")
    grad_chosen = ROUTE_SCALE * (
        gate_grads / chosen_sum
        - jnp.sum(gate_grads * chosen, axis=1, keepdims=True) / (chosen_sum * chosen_sum)
    )
    grad_sig = jnp.sum(jnp.where(route_hot, grad_chosen[:, :, None], 0.0), axis=1)
    grad_logits = (grad_sig * sigmoid_vals * (1.0 - sigmoid_vals)).astype(brain_float16)
    router_grad = contract_rows(hnormed_b, grad_logits)
    grad_hn = lax.psum(grad_hn_part, "tensor") + contract_cols(grad_logits, router_w)
    grad_hidden_norm, gain_two_grad = rms_backward(hidden, scale_two, gain_two.astype(f32), grad_hn)
    grad_hidden = grad_y + grad_hidden_norm
    grad_hidden_b = grad_hidden.astype(brain_float16)
    out_grad = contract_rows(attended_b, grad_hidden_b)
    grad_att = (
        contract_cols(grad_hidden_b, out_w).reshape(tok_rows, local_heads, DV).astype(brain_float16)
    )
    probs = jnp.exp(score_block() - log_total)
    probs_again = probs.astype(brain_float16)
    grad_probs = jnp.einsum("qhd,khd->hqk", grad_att, values, preferred_element_type=f32)
    grad_vals = jnp.einsum("hqk,qhd->khd", probs_again, grad_att, preferred_element_type=f32)
    row_delta = jnp.sum(probs * grad_probs, axis=-1, keepdims=True)
    grad_scores = (probs * (grad_probs - row_delta)).astype(brain_float16)
    grad_q = jnp.einsum("hqk,khd->qhd", grad_scores, key_all, preferred_element_type=f32) * q_scale
    grad_keys = jnp.einsum("hqk,qhd->khd", grad_scores, q_all, preferred_element_type=f32) * q_scale
    grad_kv = (
        jnp.concatenate([grad_keys[..., :DN], grad_vals], axis=-1)
        .reshape(tok_rows, local_heads * (DN + DV))
        .astype(brain_float16)
    )
    kv_grad = contract_rows(compressed_b, grad_kv)
    grad_comp_part = contract_cols(grad_kv, kv_w)
    grad_krope_part = jnp.sum(grad_keys[..., DN:], axis=1)
    grad_comp, grad_krope = (
        lax.psum(grad_comp_part.astype(jnp.bfloat16), "tensor").astype(jnp.float32),
        lax.psum(grad_krope_part.astype(jnp.bfloat16), "tensor").astype(jnp.float32),
    )
    grad_c, latent_gain_grad = rms_backward(
        latent[:, :rank_width], scale_kv, latent_g.astype(f32), grad_comp
    )
    grad_latent = jnp.concatenate([grad_c, unrotate(grad_krope, cosine, sine_tab)], axis=-1).astype(
        brain_float16
    )
    grad_qrot = unrotate(grad_q[..., DN:], cosine[:, None, :], sine_tab[:, None, :])
    grad_queries = (
        jnp.concatenate([grad_q[..., :DN], grad_qrot], axis=-1)
        .reshape(tok_rows, local_heads * (DN + DR))
        .astype(brain_float16)
    )
    query_grad = contract_rows(normed_b, grad_queries)
    latent_grad = contract_rows(normed_b, grad_latent)
    grad_normed = lax.psum(
        contract_cols(grad_queries, query_w).astype(jnp.bfloat16), "tensor"
    ).astype(jnp.float32) + contract_cols(grad_latent, latent_w)
    grad_x_norm, gain_one_grad = rms_backward(x_float, scale_one, gain_one.astype(f32), grad_normed)
    input_grad = grad_hidden + grad_x_norm
    first_owned = (
        *sent_together(
            (
                gain_one_grad.astype(jnp.bfloat16),
                query_grad.astype(jnp.bfloat16),
                latent_grad.astype(jnp.bfloat16),
            ),
            "expert",
            0,
            1,
        ),
        *sent_together(
            (latent_gain_grad.astype(jnp.bfloat16), kv_grad.astype(jnp.bfloat16)), "expert", 0, 1
        ),
    )
    second_owned = (
        lax.psum_scatter(out_grad, "expert", scatter_dimension=1, tiled=True),
        lax.psum_scatter(gain_two_grad, "expert", scatter_dimension=0, tiled=True),
        lax.psum_scatter(router_grad, "expert", scatter_dimension=0, tiled=True),
        lax.psum_scatter(sgu_grad, "expert", scatter_dimension=1, tiled=True),
        lax.psum_scatter(sdown_grad, "expert", scatter_dimension=1, tiled=True),
    )
    return (
        mixed,
        input_grad,
        first_owned[0],
        first_owned[1],
        first_owned[2],
        first_owned[3],
        first_owned[4],
        second_owned[0],
        second_owned[1],
        second_owned[2],
        second_owned[3],
        second_owned[4],
        egu_grad,
        edown_grad,
    )


def swap_cores(value):
    return lax.ppermute(value, "tensor", [(0, 1), (1, 0)])


def take_rows(value, start, count, axis=0):
    return lax.dynamic_slice_in_dim(value, start, count, axis=axis)


def in_order(core, own, other, axis=0):
    return jnp.where(
        core == 0,
        jnp.concatenate([own, other], axis=axis),
        jnp.concatenate([other, own], axis=axis),
    )


def add_wide(*parts):
    total = parts[0].astype(jnp.float32)
    for part in parts[1:]:
        total = total + part.astype(jnp.float32)
    return total


PLANE = 4


def to_partner(value, flips):
    groups = lax.axis_size("expert")
    return lax.ppermute(value, "expert", [(g, g ^ flips) for g in range(groups)])


def to_deeper(value, step):
    groups = lax.axis_size("expert")
    pairs = [(g, (g + step * PLANE) % groups) for g in range(groups)]
    return lax.ppermute(value, "expert", pairs)


def plane_gather(value):
    return [value] + [to_partner(value, r) for r in range(1, PLANE)]


def plane_scatter(parts):
    return add_wide(parts[0], *[to_partner(parts[r], r) for r in range(1, PLANE)])


def by_place(parts, place):
    odd, high = place % 2 == 1, place // 2 == 1
    parts = [jnp.where(odd, parts[i ^ 1], parts[i]) for i in range(PLANE)]
    return [jnp.where(high, parts[i ^ 2], parts[i]) for i in range(PLANE)]


def tie(*values):
    return lax.optimization_barrier(values)


def deep_pieces(value):
    deep = lax.axis_size("expert") // PLANE
    return [to_deeper(value, s) for s in range(1, deep)]


def one_plane(value, step):
    groups = lax.axis_size("expert")
    pairs = [(g, g + step * PLANE) for g in range(groups) if 0 <= g + step * PLANE < groups]
    return lax.ppermute(value, "expert", pairs)


def deep_hops(value):
    deep = lax.axis_size("expert") // PLANE
    after, before, down, up = [], [], value, value
    for _ in range(1, deep):
        down, up = one_plane(down, 1), one_plane(up, -1)
        after.append(down)
        before.append(up)
    return after, before


def join_hops(hops):
    after, before = hops
    return [a + b for a, b in zip(after, before[::-1])]


def deep_join(value, pieces, z):
    deep = lax.axis_size("expert") // PLANE
    whole = jnp.zeros((deep, *value.shape), value.dtype)
    whole = lax.dynamic_update_index_in_dim(whole, value, z, 0)
    for step in range(1, deep):
        whole = lax.dynamic_update_index_in_dim(whole, pieces[step - 1], (z - step) % deep, 0)
    return whole


def deep_scatter(blocks, z):
    deep = blocks.shape[0]

    def block(index):
        return lax.dynamic_index_in_dim(blocks, index, 0, keepdims=False)

    return add_wide(
        block(z), *[to_deeper(block((z + step) % deep), step) for step in range(1, deep)]
    )


def sum_planes(grad, z):
    deep = lax.axis_size("expert") // PLANE
    rows = deep_scatter(grad.astype(jnp.bfloat16).reshape(deep, -1, grad.shape[1]), z)
    return rows.astype(jnp.bfloat16).reshape(PLANE, -1, grad.shape[1])


def share_columns(rows, place):
    parts = [at_index(rows, 0, place)]
    for r in range(1, PLANE):
        parts.append(to_partner(at_index(rows, 0, place ^ r), r))
    return by_place(parts, place)


def all_groups(value):
    return lax.all_gather(value, "expert", axis=0, tiled=False)


def at_index(value, axis, index):
    return lax.dynamic_index_in_dim(value, index, axis, keepdims=False)


class RowGather:
    def __init__(self, value):
        self.cut = value.shape[0] // 2
        self.value = value

    def along(self):
        return [self.value] + deep_pieces(self.value)

    def lines(self, came):
        return [jnp.stack([v[: self.cut] for v in came]), jnp.stack([v[self.cut :] for v in came])]

    def over(self, lines):
        first, second = lines
        beside, behind = to_partner(first, 1), to_partner(second, 2)
        return [
            [first, beside, to_partner(first, 2), to_partner(beside, 2)],
            [second, to_partner(second, 1), behind, to_partner(behind, 1)],
        ]

    def whole(self, halves):
        return jnp.concatenate([jnp.concatenate(half, axis=0) for half in halves], axis=1)


class RowSum:
    def __init__(self, *terms):
        groups, rows = terms[0].shape[:2]
        self.type = terms[0].dtype
        cut = rows // 2
        blocks = [v.reshape(PLANE, groups // PLANE, *v.shape[1:]) for v in terms]
        self.halves = (
            ([v[:, :, :cut] for v in blocks], 2, 1),
            ([v[:, :, cut:] for v in blocks], 1, 2),
        )

    def _add(self, parts):
        return add_wide(*parts).astype(self.type)

    def sends(self):
        return [
            jnp.stack([self._add([v[far] for v in held]), self._add([v[far | near] for v in held])])
            for held, far, near in self.halves
        ]

    def move(self, sends):
        return [to_partner(v, far) for v, (_, far, _) in zip(sends, self.halves)]

    def sends_again(self, came):
        return [
            self._add([v[near] for v in held] + [c[1]])
            for c, (held, _, near) in zip(came, self.halves)
        ]

    def move_again(self, sends):
        return [to_partner(v, near) for v, (_, _, near) in zip(sends, self.halves)]

    def line(self, came, came_again):
        sums = [
            self._add([v[0] for v in held] + [c[0], d])
            for c, d, (held, *_) in zip(came, came_again, self.halves)
        ]
        return jnp.concatenate(sums, axis=1)


def line_sends(line):
    return [line[step] for step in range(line.shape[0])]


def line_move(sends):
    return [sends[0]] + [to_deeper(v, -step) for step, v in enumerate(sends) if step > 0]


def dot_nn(left, right):
    return lax.dot_general(left, right, (((1,), (0,)), ((), ())), preferred_element_type=jnp.float32)


def dot_nt(left, right):
    return lax.dot_general(left, right, (((1,), (1,)), ((), ())), preferred_element_type=jnp.float32)


def dot_tn(left, right):
    return lax.dot_general(left, right, (((0,), (0,)), ((), ())), preferred_element_type=jnp.float32)


def two_lanes(column, lane):
    high = column.astype(jnp.bfloat16).astype(jnp.float32)
    spread = jnp.where(lane == 0, high, jnp.where(lane == 1, column - high, 0.0))
    return spread.astype(jnp.bfloat16)


def expert_kernel(
    shared_cols,
    expert_count,
    me_ref,
    hn_own,
    hn_other,
    dy_own,
    dy_other,
    meta_own,
    meta_other,
    gate_up_w,
    down_w,
    first_w,
    sdown_w,
    slots_out,
    slot_dy_out,
    act_out,
    d_gate_up_out,
    rows_own_out,
    rows_other_out,
    sact_own_out,
    sact_other_out,
    shared_grads_out,
    dgate_own_out,
    dgate_other_out,
):
    f32, bf16 = jnp.float32, jnp.bfloat16
    count, half, _ = hn_own.shape
    tokens = 2 * half
    me = me_ref[0]
    lane = lax.broadcasted_iota(jnp.int32, (tokens, LANES), 1)
    is_router = (lane >= shared_cols) & (lane < shared_cols + expert_count)
    first = first_w[...]
    slots, slot_dys, slot_gates, picks, dshs = [], [], [], [], []
    first_grad, sdown_grad = 0.0, 0.0
    for i in range(count):
        rows = jnp.concatenate([hn_own[i], hn_other[i]], axis=0)
        rows_dy = jnp.concatenate([dy_own[i], dy_other[i]], axis=0)
        meta = jnp.concatenate([meta_own[i], meta_other[i]], axis=0)
        products = dot_nt(rows, first)
        gate, up = products[:, :LANES], products[:, LANES:]
        sig = jax.nn.sigmoid(gate)
        total = jnp.sum(jnp.where(is_router, sig * meta, 0.0), axis=1, keepdims=True)
        mine = jnp.sum(jnp.where(lane == shared_cols + me, sig, 0.0), axis=1, keepdims=True)
        token_gate = ROUTE_SCALE * mine / total
        sact = (gate * sig * up).astype(bf16)
        sact_own_out[i], sact_other_out[i] = sact[:half], sact[half:]
        d_sact = dot_nt(rows_dy, sdown_w[...])
        d_sgate = d_sact * up * sig * (1.0 + gate * (1.0 - sig))
        dsh = jnp.concatenate([d_sgate, d_sact * gate * sig], axis=1).astype(bf16)
        dshs.append(dsh)
        first_grad += dot_tn(dsh, rows)
        sdown_grad += dot_tn(sact, rows_dy)
        pick = (meta[:, :1] == lane.astype(f32)).astype(bf16)
        picks.append(pick)
        slots.append(dot_tn(pick, rows).astype(bf16))
        slot_dys.append(dot_tn(pick, rows_dy).astype(bf16))
        slot_gates.append(
            jnp.sum(dot_tn(pick, two_lanes(token_gate, lane)), axis=1, keepdims=True)
        )

    @pl.when(pl.program_id(0) == 0)
    def _():
        shared_grads_out[...] = jnp.zeros_like(shared_grads_out)

    shared_grads_out[:shared_cols] += first_grad[:shared_cols]
    shared_grads_out[shared_cols : 2 * shared_cols] += first_grad[LANES : LANES + shared_cols]
    shared_grads_out[2 * shared_cols :] += sdown_grad[:shared_cols]
    slot_rows = jnp.concatenate(slots, axis=0)
    slot_dy = jnp.concatenate(slot_dys, axis=0)
    slot_gate = jnp.concatenate(slot_gates, axis=0)
    slots_out[...] = slot_rows
    slot_dy_out[...] = slot_dy
    gate = dot_nt(slot_rows, gate_up_w[0])
    up = dot_nt(slot_rows, gate_up_w[1])
    d_act = dot_nt(slot_dy, down_w[...])
    sig = jax.nn.sigmoid(gate)
    silu = gate * sig
    act = silu * up
    slot_dgate = jnp.sum(act * d_act, axis=1, keepdims=True)
    act_out[...] = (slot_gate * act).astype(bf16)
    d_act = slot_gate * d_act
    d_gate = (d_act * up * sig * (1.0 + gate * (1.0 - sig))).astype(bf16)
    d_up = (d_act * silu).astype(bf16)
    d_gate_up_out[0] = d_gate
    d_gate_up_out[1] = d_up
    d_slots = (dot_nn(d_gate, gate_up_w[0]) + dot_nn(d_up, gate_up_w[1])).astype(bf16)
    slot_lane = lax.broadcasted_iota(jnp.int32, (LANES, LANES), 1)
    for i in range(count):
        here = slice(i * LANES, (i + 1) * LANES)
        d_rows = (dot_nn(picks[i], d_slots[here]) + dot_nn(dshs[i], first)).astype(bf16)
        rows_own_out[i], rows_other_out[i] = d_rows[:half], d_rows[half:]
        dgate = dot_nn(picks[i], two_lanes(slot_dgate[here], slot_lane))
        dgate_own_out[i], dgate_other_out[i] = dgate[:half], dgate[half:]


def block_specs(per_step):
    def lead(*tail):
        return pl.BlockSpec((per_step, *tail), lambda i: (i,) + (0,) * len(tail))

    def flat(cols):
        return pl.BlockSpec((per_step * LANES, cols), lambda i: (i, 0))

    def whole(a):
        return pl.BlockSpec(a.shape, lambda i: (0,) * a.ndim, pipeline_mode=pl.Buffered(1))

    return lead, flat, whole


def slots_cost(width, hidden, products):
    return LANES * width * hidden * products


def experts(
    me,
    hn_own,
    hn_other,
    dy_own,
    dy_other,
    meta_own,
    meta_other,
    gate_up_w,
    down_w,
    first_w,
    sdown_w,
    shared_cols,
    expert_count,
    per_step=2,
):
    groups, half, width = hn_own.shape
    hidden = down_w.shape[0]
    slots = groups * LANES
    f32, bf16 = jnp.float32, jnp.bfloat16
    lead, flat, whole = block_specs(per_step)
    sds = jax.ShapeDtypeStruct
    rows_cost = 2 * groups * (2 * half * width * 4 * LANES + slots_cost(width, hidden, 5))
    return pl.pallas_call(
        functools.partial(expert_kernel, shared_cols, expert_count),
        grid=(groups // per_step,),
        in_specs=[
            pl.BlockSpec(memory_space=pltpu.SMEM),
            *[lead(half, width)] * 4,
            *[lead(half, LANES)] * 2,
            *[whole(a) for a in (gate_up_w, down_w, first_w, sdown_w)],
        ],
        out_specs=[
            flat(width),
            flat(width),
            flat(hidden),
            pl.BlockSpec((2, per_step * LANES, hidden), lambda i: (0, i, 0)),
            *[lead(half, width)] * 2,
            *[lead(half, LANES)] * 2,
            pl.BlockSpec((3 * shared_cols, width), lambda i: (0, 0)),
            *[lead(half, LANES)] * 2,
        ],
        out_shape=[
            sds((slots, width), bf16),
            sds((slots, width), bf16),
            sds((slots, hidden), bf16),
            sds((2, slots, hidden), bf16),
            *[sds((groups, half, width), bf16)] * 2,
            *[sds((groups, half, LANES), bf16)] * 2,
            sds((3 * shared_cols, width), f32),
            *[sds((groups, half, LANES), f32)] * 2,
        ],
        compiler_params=pltpu.CompilerParams(vmem_limit_bytes=58 * 1024 * 1024),
        cost_estimate=pl.CostEstimate(
            flops=rows_cost, bytes_accessed=20 * groups * half * width, transcendentals=0
        ),
    )(
        me,
        hn_own,
        hn_other,
        dy_own,
        dy_other,
        meta_own,
        meta_other,
        gate_up_w,
        down_w,
        first_w,
        sdown_w,
    )


def product_kernel(left_ref, right_ref, out_ref):
    out_ref[0] = dot_tn(left_ref[0], right_ref[...])


def column_products(left, right, tile=512):
    count, rows, height = left.shape
    width = right.shape[1]
    return pl.pallas_call(
        product_kernel,
        grid=(width // tile, count),
        in_specs=[
            pl.BlockSpec((1, rows, height), lambda j, i: (i, 0, 0)),
            pl.BlockSpec((rows, tile), lambda j, i: (0, j)),
        ],
        out_specs=pl.BlockSpec((1, height, tile), lambda j, i: (i, 0, j)),
        out_shape=jax.ShapeDtypeStruct((count, height, width), jnp.float32),
        compiler_params=pltpu.CompilerParams(vmem_limit_bytes=58 * 1024 * 1024),
        cost_estimate=pl.CostEstimate(
            flops=rows * width, bytes_accessed=rows * width, transcendentals=0
        ),
    )(left, right)


def output_kernel(act, sact_own, sact_other, meta_own, meta_other, down_w, sdown_w, own_out, other_out):
    f32, bf16 = jnp.float32, jnp.bfloat16
    count, half, _ = meta_own.shape
    lane = lax.broadcasted_iota(jnp.int32, (2 * half, LANES), 1).astype(f32)
    out = dot_nn(act[...], down_w[...]).astype(bf16)
    for i in range(count):
        meta = jnp.concatenate([meta_own[i], meta_other[i]], axis=0)
        pick = (meta[:, :1] == lane).astype(bf16)
        sact = jnp.concatenate([sact_own[i], sact_other[i]], axis=0)
        here = slice(i * LANES, (i + 1) * LANES)
        rows = (dot_nn(pick, out[here]) + dot_nn(sact, sdown_w[...])).astype(bf16)
        own_out[i], other_out[i] = rows[:half], rows[half:]


def outputs(act, sact_own, sact_other, meta_own, meta_other, down_w, sdown_w, per_step=4):
    groups, half, _ = meta_own.shape
    hidden, width = down_w.shape
    lead, flat, whole = block_specs(per_step)
    return pl.pallas_call(
        output_kernel,
        grid=(groups // per_step,),
        in_specs=[
            flat(hidden),
            *[lead(half, LANES)] * 4,
            *[whole(a) for a in (down_w, sdown_w)],
        ],
        out_specs=[lead(half, width)] * 2,
        out_shape=[jax.ShapeDtypeStruct((groups, half, width), jnp.bfloat16)] * 2,
        compiler_params=pltpu.CompilerParams(vmem_limit_bytes=58 * 1024 * 1024),
        cost_estimate=pl.CostEstimate(
            flops=groups * half * LANES * width,
            bytes_accessed=groups * half * width,
            transcendentals=0,
        ),
    )(act, sact_own, sact_other, meta_own, meta_other, down_w, sdown_w)


def token_plan(
    inputs,
    attn_gain,
    w_query,
    w_latent,
    latent_gain,
    w_kv,
    w_out,
    ffn_gain,
    w_router,
    shared_gate_up,
    shared_down,
    expert_gate_up,
    expert_down,
    lengths,
    routes,
    cotangent,
):
    f32, bf16 = jnp.float32, jnp.bfloat16
    core, me = lax.axis_index("tensor"), lax.axis_index("expert")
    groups = lax.axis_size("expert")
    deep, place, z = groups // PLANE, me % PLANE, me // PLANE
    tok_rows, width = inputs.shape
    half = tok_rows // 2
    own_at, other_at = core * half, (1 - core) * half
    expert_count = w_router.shape[1]
    route_count = routes.shape[1]
    capacity = tok_rows * route_count * 4 // (3 * expert_count)
    shared_cols = shared_gate_up.shape[2] // groups
    latent_cols, rank_width = w_latent.shape[1], latent_gain.shape[0] * groups
    block_rows = w_query.shape[0]
    kv_rows = w_kv.shape[0]

    query_cols = w_query.shape[1] // PLANE
    out_cols = w_out.shape[0] // PLANE
    used = latent_cols + expert_count + 3
    small = jnp.concatenate(
        [
            w_latent,
            w_router,
            attn_gain[:, None],
            ffn_gain[:, None],
            jnp.pad(latent_gain, (0, block_rows - kv_rows))[:, None],
            jnp.zeros((block_rows, -used % 128), bf16),
        ],
        axis=1,
    )
    small_cols = small.shape[1]
    route_half = take_rows(routes, own_at, half).astype(bf16).reshape(block_rows // 2, -1)
    length_col = jnp.pad(lengths[0].astype(bf16), (0, block_rows // 2 - lengths.shape[1]))[:, None]
    route_cols = route_half.shape[1] + 1
    small_half = jnp.concatenate(
        [
            take_rows(small, core * (block_rows // 2), block_rows // 2),
            jnp.pad(jnp.concatenate([route_half, length_col], axis=1), ((0, 0), (0, -route_cols % 128))),
        ],
        axis=1,
    )
    packed_cols = small_half.shape[1] // 2
    small_packed = jnp.concatenate([small_half[:, :packed_cols], small_half[:, packed_cols:]])
    kv_cols = w_kv.shape[1] // PLANE
    kv_parts = block_rows // kv_rows
    kv_piece = kv_cols // kv_parts
    w_out_t = w_out.T

    def quarter(index):
        kv_here = take_rows(w_kv, index * kv_cols, kv_cols, axis=1)
        kv_here = [kv_here[:, p * kv_piece : (p + 1) * kv_piece] for p in range(kv_parts)]
        return jnp.concatenate(
            [
                take_rows(w_query, index * query_cols, query_cols, axis=1),
                take_rows(w_out_t, index * out_cols, out_cols, axis=1),
                jnp.concatenate(kv_here, axis=0),
            ],
            axis=1,
        )

    near_w = [quarter(place)] + [to_partner(quarter(place ^ r), r) for r in range(1, PLANE)]
    small_line = deep_join(small_packed, deep_pieces(small_packed), z)
    near_w, small_line = tie(near_w, small_line)
    plane_w = jnp.stack(by_place(near_w, place))
    near_sent = jnp.concatenate(
        [
            take_rows(inputs, own_at, half),
            small_line.swapaxes(0, 1).reshape(block_rows, -1),
        ],
        axis=1,
    )
    near_sent, plane_w = tie(near_sent, plane_w)
    near_came = jnp.stack([near_sent, to_partner(near_sent, 1)])
    near_came = jnp.concatenate([near_came, to_partner(near_came, 2)], axis=0)
    near_came, deep_w = tie(near_came, deep_hops(plane_w))
    x_near_own = near_came[:, :, :width]
    small_parts = near_came[:, :, width:].reshape(PLANE, block_rows, deep, packed_cols)
    small_parts = [small_parts[r].swapaxes(0, 1) for r in range(PLANE)]
    x_near = in_order(core, x_near_own, swap_cores(x_near_own), axis=1)
    x_near = lax.optimization_barrier(x_near.reshape(PLANE * tok_rows, width))
    small_own = jnp.stack(by_place(small_parts, place), axis=1)
    small_own = small_own.reshape(groups, block_rows, packed_cols)
    small_own = jnp.concatenate(
        [small_own[:, : block_rows // 2], small_own[:, block_rows // 2 :]], axis=2
    )
    small_other = swap_cores(small_own)
    small_all = in_order(core, small_own, small_other, axis=1)
    head_w = deep_join(plane_w, join_hops(deep_w), z)
    length_at = small_cols + route_cols - 1
    lengths_near = take_rows(small_own, z * PLANE, PLANE)[:, : lengths.shape[1], length_at]
    lengths_near = lengths_near.astype(jnp.int32)
    lengths_near = jnp.stack(by_place([lengths_near[r] for r in range(PLANE)], place))
    shared_rows = jnp.concatenate(
        [shared_gate_up[0].T, shared_gate_up[1].T, shared_down], axis=0
    ).reshape(3, groups, shared_cols, block_rows)
    shared_rows = shared_rows.swapaxes(0, 1).reshape(groups, 3 * shared_cols, block_rows)
    dy_sent, head_w = tie(take_rows(cotangent, own_at, half), head_w)
    dy_own_rows = take_rows(cotangent, own_at, half)
    dy_gather = RowGather(dy_sent)
    dy_came = dy_gather.along()
    head_w = head_w.reshape(groups, block_rows, -1)
    flat_head = head_w.reshape(groups * block_rows, -1)
    query_w = flat_head[:, :query_cols]
    at = query_cols + out_cols
    out_wt = flat_head[:, query_cols:at]
    kv_w = head_w[:, :, at : at + kv_piece].reshape(groups, kv_parts, kv_rows, kv_piece)
    kv_w = kv_w.transpose(0, 2, 1, 3).reshape(groups * kv_rows, kv_cols)

    block_index = jnp.arange(groups)
    block_chip = (z - block_index % deep) % deep * PLANE + (place ^ (block_index // deep))
    in_blocks = (block_chip[:, None] == block_index[None, :]).astype(bf16)

    def routes_of(came):
        came = came[:, :, small_cols : small_cols + route_half.shape[1]].reshape(groups, -1)
        came = jnp.dot(in_blocks, came, preferred_element_type=f32)
        return came.astype(jnp.int32).reshape(groups, half, route_count)

    routes_own, routes_other = routes_of(small_own), routes_of(small_other)
    flat_small = small_all.reshape(groups * block_rows, -1)
    latent_w = flat_small[:, :latent_cols]
    at = latent_cols
    router_w = flat_small[:, at : at + expert_count]
    at += expert_count
    gain_one, gain_two = flat_small[:, at], flat_small[:, at + 1]
    latent_g = small_all[:, :kv_rows, at + 2].reshape(-1)

    near_rows = PLANE * tok_rows
    local_heads = query_cols // (DN + DR)
    x_float = x_near.astype(f32)
    relative, visible = jax.vmap(lambda one: doc_layout(one, tok_rows))(lengths_near)
    cosine, sine_tab = rope_tables(relative.reshape(-1), DR)
    q_scale = (DN + DR) ** (-0.5)
    scale_one = lax.rsqrt(jnp.mean(x_float * x_float, axis=-1, keepdims=True) + EPSILON)
    scale_one = lax.optimization_barrier(scale_one)
    normed_b = (x_near.astype(f32) * scale_one * gain_one.astype(f32)).astype(bf16)
    normed_b = lax.optimization_barrier(normed_b)
    queries = jnp.dot(normed_b, query_w, preferred_element_type=f32).reshape(
        near_rows, local_heads, DN + DR
    )
    q_rot = rotate(queries[..., DN:], cosine[:, None, :], sine_tab[:, None, :])
    q_all = jnp.concatenate([queries[..., :DN], q_rot], axis=-1).astype(bf16)
    q_all = q_all.reshape(PLANE, tok_rows, local_heads, DN + DR)
    latent = jnp.dot(normed_b, latent_w, preferred_element_type=f32)
    compressed, _ = rms_forward(latent[:, :rank_width], latent_g.astype(f32))
    compressed_b = compressed.astype(bf16)
    k_rope = rotate(latent[:, rank_width:], cosine, sine_tab).astype(bf16)
    kv_all = jnp.dot(compressed_b, kv_w, preferred_element_type=f32).reshape(
        PLANE, tok_rows, local_heads, DN + DV
    )
    k_nope = kv_all[..., :DN].astype(bf16)
    values = kv_all[..., DN:].astype(bf16)
    k_rope = k_rope.reshape(PLANE, tok_rows, 1, DR)
    key_all = jnp.concatenate(
        [k_nope, jnp.broadcast_to(k_rope, (PLANE, tok_rows, local_heads, DR))], axis=-1
    )

    def score_block():
        raw_scores = (
            jnp.einsum("gqhd,gkhd->ghqk", q_all, key_all, preferred_element_type=f32) * q_scale
        )
        return jnp.where(visible[:, None], raw_scores, NEGATIVE)

    scores = score_block()
    top_score = jnp.max(scores, axis=-1, keepdims=True)
    log_total = top_score + jnp.log(jnp.sum(jnp.exp(scores - top_score), axis=-1, keepdims=True))
    probs_b = jnp.exp(scores - log_total).astype(bf16)
    attended = jnp.einsum("ghqk,gkhd->gqhd", probs_b, values, preferred_element_type=f32)
    attended_b = attended.reshape(near_rows, local_heads * DV).astype(bf16)
    attended_b, dy_came = tie(attended_b, dy_came)

    def sum_heads(part):
        part = part.astype(bf16).reshape(PLANE, tok_rows, -1)
        came = swap_cores(take_rows(part, other_at, half, axis=1))
        both = add_wide(take_rows(part, own_at, half, axis=1), came).astype(bf16)
        return plane_scatter([both[r] for r in range(PLANE)])

    attn_own = sum_heads(contract_cols(attended_b, out_wt))
    x_own = take_rows(inputs, own_at, half).astype(f32)
    hidden = x_own + attn_own
    hnormed, scale_two = rms_forward(hidden, gain_two.astype(f32))
    hnormed_b = hnormed.astype(bf16)
    normed_cols = jnp.concatenate(
        [
            take_rows(normed_b, (k * PLANE + place) * block_rows, block_rows, axis=1)
            for k in range(deep)
        ],
        axis=1,
    )
    hnormed_b, dy_lines, normed_cols, shared_rows = tie(
        hnormed_b, dy_gather.lines(dy_came), normed_cols, shared_rows
    )
    def membership(named):
        one_hot = named[..., None] == jnp.arange(expert_count, dtype=jnp.int32)
        return jnp.any(named == me, axis=-1), jnp.any(one_hot, axis=2)

    member_own, hot_own = membership(routes_own)
    member_other, hot_other = membership(routes_other)
    lower = (
        jnp.arange(half, dtype=jnp.int32)[:, None] <= jnp.arange(half, dtype=jnp.int32)[None, :]
    ).astype(bf16)

    def running(mask):
        counts = jnp.dot(mask.astype(bf16), lower, preferred_element_type=f32)
        return counts.astype(jnp.int32)

    count_own, count_other = running(member_own), running(member_other)
    place_own = jnp.where(member_own, count_own - 1, -1)
    place_other = jnp.where(member_other, count_own[:, -1:] + count_other - 1, -1)

    def metadata(slot, hot):
        return jnp.concatenate(
            [
                slot[..., None].astype(f32),
                jnp.zeros((groups, half, shared_cols - 1), f32),
                hot.astype(f32),
                jnp.zeros((groups, half, LANES - shared_cols - expert_count), f32),
            ],
            axis=-1,
        )

    meta_own, meta_other = metadata(place_own, hot_own), metadata(place_other, hot_other)
    hn_gather = RowGather(hnormed_b)
    hn_came, dy_halves, shared_rows = tie(
        hn_gather.along(), dy_gather.over(dy_lines), shared_rows
    )
    hn_lines, dy_halves, shared_rows = tie(hn_gather.lines(hn_came), dy_halves, shared_rows)
    hn_halves = hn_gather.over(hn_lines)
    shared_w = lax.all_to_all(shared_rows, "expert", split_axis=0, concat_axis=0, tiled=True)
    dy_own = dy_gather.whole(dy_halves)
    dy_other = swap_cores(dy_own)
    hn_halves, shared_w, dy_other, meta_own, meta_other = tie(
        hn_halves, shared_w, dy_other, meta_own, meta_other
    )
    shared_w = shared_w.swapaxes(0, 1).reshape(3 * shared_cols, groups * block_rows)
    hn_own = hn_gather.whole(hn_halves)


    first_w = jnp.concatenate(
        [
            shared_w[:shared_cols],
            router_w.T,
            jnp.zeros((LANES - shared_cols - expert_count, width), bf16),
            shared_w[shared_cols : 2 * shared_cols],
            jnp.zeros((LANES - shared_cols, width), bf16),
        ],
        axis=0,
    )
    sdown_rows = jnp.pad(shared_w[2 * shared_cols :], ((0, LANES - shared_cols), (0, 0)))
    hn_other = swap_cores(hn_own)
    gate_up_w, down_w = jnp.swapaxes(expert_gate_up[0], 1, 2), expert_down[0]
    (
        slot_rows,
        slot_dy,
        slot_act,
        d_gate_up,
        d_rows_own,
        d_rows_other,
        act_own,
        act_other,
        shared_grads,
        dgate_own,
        dgate_other,
    ) = experts(
        me.reshape(1).astype(jnp.int32),
        hn_own,
        hn_other,
        dy_own,
        dy_other,
        meta_own,
        meta_other,
        gate_up_w,
        down_w,
        first_w,
        sdown_rows,
        shared_cols,
        expert_count,
    )
    d_rows_came = swap_cores(d_rows_other)

    def two_parts(value):
        return value[..., 0] + value[..., 1]

    dgate_sent = two_parts(dgate_own) + swap_cores(two_parts(dgate_other))
    dgate_high = dgate_sent.astype(bf16)
    dgate_low = (dgate_sent - dgate_high.astype(f32)).astype(bf16)
    d_rows_came, dgate_high, dgate_low = tie(d_rows_came, dgate_high, dgate_low)
    d_sum = RowSum(d_rows_own, d_rows_came)
    sends, shared_grads, slot_act = tie(d_sum.sends(), shared_grads, slot_act)
    came = d_sum.move(sends)
    gate_rows = jnp.stack([contract_rows(in_blocks, v).reshape(-1) for v in (dgate_high, dgate_low)])
    grads_sent = jnp.concatenate([shared_grads, gate_rows], axis=0).astype(bf16)
    grads_sent = grads_sent.reshape(-1, groups, block_rows)
    grads_came = lax.all_to_all(grads_sent, "expert", split_axis=1, concat_axis=1, tiled=True)
    out_own, out_other = outputs(
        slot_act, act_own, act_other, meta_own, meta_other, down_w, sdown_rows
    )
    out_came = swap_cores(out_other)
    edown_grad = column_products(slot_act[None], slot_dy)[0]
    came, out_came, edown_grad, grads_came = tie(came, out_came, edown_grad, grads_came)
    sgu_out, sdown_out, dgate = (
        grads_came[: 2 * shared_cols],
        grads_came[2 * shared_cols : 3 * shared_cols],
        add_wide(grads_came[3 * shared_cols], grads_came[3 * shared_cols + 1]).T,
    )
    sgu_out = sgu_out.astype(f32).reshape(2, shared_cols, groups, block_rows)
    sgu_out = sgu_out.transpose(0, 3, 2, 1).reshape(2, block_rows, -1)
    sdown_out = sdown_out.astype(f32).swapaxes(0, 1).reshape(-1, block_rows)
    sends, slot_rows, out_came = tie(d_sum.sends_again(came), slot_rows, out_came)
    came_again = d_sum.move_again(sends)
    egu_grad = column_products(d_gate_up, slot_rows).swapaxes(1, 2)
    out_sum = RowSum(out_own, out_came)
    out_sends = out_sum.sends()
    came_again, egu_grad, out_sends = tie(came_again, egu_grad, out_sends)
    z_sends, out_sends, dgate = tie(
        line_sends(d_sum.line(came, came_again)), out_sends, dgate
    )
    z_came = line_move(z_sends)
    out_first = out_sum.move(out_sends)
    hot_mine = take_rows(
        jnp.any(routes[..., None] == jnp.arange(expert_count, dtype=jnp.int32), axis=1), own_at, half
    )
    sig = jax.nn.sigmoid(jnp.dot(hnormed_b, router_w, preferred_element_type=f32))
    chosen = jnp.where(hot_mine, sig, 0.0)
    chosen_sum = jnp.sum(chosen, axis=1, keepdims=True)
    dgate = jnp.where(hot_mine, dgate, 0.0)
    inner = jnp.sum(dgate * chosen, axis=1, keepdims=True)
    d_chosen = ROUTE_SCALE * (dgate / chosen_sum - inner / (chosen_sum * chosen_sum))
    d_logits = (jnp.where(hot_mine, d_chosen, 0.0) * sig * (1.0 - sig)).astype(bf16)
    router_grad = contract_rows(d_logits, hnormed_b)
    z_came, d_logits, router_grad = tie(z_came, d_logits, router_grad)
    d_hn = add_wide(*z_came)
    d_hn = d_hn + contract_cols(d_logits, router_w)
    d_hidden_norm, gain_two_grad = rms_backward(hidden, scale_two, gain_two.astype(f32), d_hn)
    d_hidden = dy_own_rows.astype(f32) + d_hidden_norm
    d_parts, out_first = tie(plane_gather(d_hidden.astype(bf16)), out_first)
    d_near_own = jnp.stack(d_parts)
    d_near = in_order(core, d_near_own, swap_cores(d_near_own), axis=1).reshape(near_rows, width)

    out_sends, d_near = tie(out_sum.sends_again(out_first), d_near)
    out_second = out_sum.move_again(out_sends)

    grad_att = (
        jnp.dot(d_near, out_wt, preferred_element_type=f32)
        .reshape(PLANE, tok_rows, local_heads, DV)
        .astype(bf16)
    )
    out_grad = contract_rows(d_near, attended_b).astype(bf16)
    out_grad, grad_att = tie(out_grad, grad_att)
    out_sums = sum_planes(out_grad, z)
    probs = jnp.exp(score_block() - log_total)
    probs_again = probs.astype(bf16)
    grad_probs = jnp.einsum("gqhd,gkhd->ghqk", grad_att, values, preferred_element_type=f32)
    grad_vals = jnp.einsum("ghqk,gqhd->gkhd", probs_again, grad_att, preferred_element_type=f32)
    row_delta = jnp.sum(probs * grad_probs, axis=-1, keepdims=True)
    grad_scores = (probs * (grad_probs - row_delta)).astype(bf16)
    grad_q = (
        jnp.einsum("ghqk,gkhd->gqhd", grad_scores, key_all, preferred_element_type=f32) * q_scale
    ).reshape(near_rows, local_heads, DN + DR)
    grad_keys = (
        jnp.einsum("ghqk,gqhd->gkhd", grad_scores, q_all, preferred_element_type=f32) * q_scale
    )
    grad_kv = (
        jnp.concatenate([grad_keys[..., :DN], grad_vals], axis=-1)
        .reshape(near_rows, local_heads * (DN + DV))
        .astype(bf16)
    )
    grad_latent_part = jnp.concatenate(
        [
            contract_cols(grad_kv, kv_w),
            jnp.sum(grad_keys[..., DN:], axis=2).reshape(near_rows, DR),
        ],
        axis=1,
    )
    grad_both = sum_heads(grad_latent_part)
    latent_own = take_rows(latent[:tok_rows], own_at, half)
    cosine_own = take_rows(cosine[:tok_rows], own_at, half)
    sine_own = take_rows(sine_tab[:tok_rows], own_at, half)
    _, scale_kv = rms_forward(latent_own[:, :rank_width], latent_g.astype(f32))
    grad_c, latent_gain_grad = rms_backward(
        latent_own[:, :rank_width], scale_kv, latent_g.astype(f32), grad_both[:, :rank_width]
    )
    grad_latent = jnp.concatenate(
        [grad_c, unrotate(grad_both[:, rank_width:], cosine_own, sine_own)], axis=-1
    ).astype(bf16)
    grad_qrot = unrotate(grad_q[..., DN:], cosine[:, None, :], sine_tab[:, None, :])
    grad_queries = (
        jnp.concatenate([grad_q[..., :DN], grad_qrot], axis=-1)
        .reshape(near_rows, local_heads * (DN + DR))
        .astype(bf16)
    )
    out_second, grad_kv, grad_queries = tie(out_second, grad_kv, grad_queries)
    out_z, grad_kv, grad_queries = tie(
        line_sends(out_sum.line(out_first, out_second)), grad_kv, grad_queries
    )
    out_z = line_move(out_z)
    kv_grad = contract_rows(compressed_b, grad_kv).astype(bf16)
    kv_grad = kv_grad.reshape(groups, kv_rows, kv_parts, kv_piece).transpose(0, 2, 1, 3)
    query_grad = contract_rows(normed_b, grad_queries).astype(bf16)
    first_sums = sum_planes(
        jnp.concatenate([query_grad, kv_grad.reshape(-1, kv_piece)], axis=1), z
    )
    shared_out = share_columns(jnp.concatenate([first_sums, out_sums], axis=2), place)
    at_kv, at_out = query_cols, query_cols + kv_piece
    w_query_grad = jnp.concatenate([p[:, :at_kv] for p in shared_out], axis=1).astype(f32)
    w_kv_grad = jnp.concatenate(
        [
            p[q * kv_rows : (q + 1) * kv_rows, at_kv:at_out]
            for p in shared_out
            for q in range(kv_parts)
        ],
        axis=1,
    ).astype(f32)
    w_out_grad = jnp.concatenate([p[:, at_out:] for p in shared_out], axis=1).astype(f32).T
    grad_normed = sum_heads(contract_cols(grad_queries, query_w))
    grad_normed = grad_normed + contract_cols(grad_latent, latent_w)
    moe_own = add_wide(*out_z)
    mixed_own = (hidden + moe_own).astype(bf16)
    mixed = in_order(core, mixed_own, swap_cores(mixed_own))

    _, scale_own = rms_forward(x_own, gain_one.astype(f32))
    grad_x_norm, gain_one_grad = rms_backward(x_own, scale_own, gain_one.astype(f32), grad_normed)
    input_own = d_hidden + grad_x_norm
    input_grad = in_order(core, input_own, swap_cores(input_own))

    latent_near_own = jnp.stack(plane_gather(grad_latent))
    latent_near = in_order(core, latent_near_own, swap_cores(latent_near_own), axis=1)
    latent_cut = latent_cols // 2
    latent_near = latent_near.reshape(near_rows, latent_cols)
    latent_blocks = contract_rows(
        normed_cols,
        take_rows(latent_near, core * latent_cut, latent_cut, axis=1),
    )
    latent_half = deep_scatter(latent_blocks.astype(bf16).reshape(deep, -1, latent_cut), z)
    w_latent_grad = in_order(core, latent_half, swap_cores(latent_half), axis=1)

    gain_lanes = jnp.pad(
        latent_gain_grad.reshape(groups, kv_rows), ((0, 0), (0, block_rows - kv_rows))
    )
    vectors = jnp.concatenate(
        [
            router_grad,
            gain_one_grad[None],
            gain_two_grad[None],
            gain_lanes.reshape(1, -1),
        ],
        axis=0,
    ).reshape(-1, groups, block_rows)
    arrived = lax.all_to_all(vectors, "expert", split_axis=1, concat_axis=1, tiled=True)
    sums = jnp.sum(arrived, axis=1)
    sums = sums + swap_cores(sums)
    return (
        mixed,
        input_grad,
        sums[expert_count],
        w_query_grad,
        w_latent_grad,
        sums[expert_count + 2, :kv_rows],
        w_kv_grad,
        w_out_grad,
        sums[expert_count + 1],
        sums[:expert_count].T,
        sgu_out,
        sdown_out,
        egu_grad[None],
        edown_grad[None],
    )


def solution(mesh):
    groups = mesh.shape["expert"]
    plan = token_plan if groups <= 16 else weight_plan
    return jax.shard_map(
        plan,
        mesh=mesh,
        in_specs=(
            P("expert", None),
            P("expert"),
            P("expert", "tensor"),
            P("expert", None),
            P("expert"),
            P("expert", "tensor"),
            P("tensor", "expert"),
            P("expert"),
            P("expert", None),
            P(None, "expert", "tensor"),
            P("tensor", "expert"),
            P("expert", None, None, "tensor"),
            P("expert", "tensor", None),
            P("expert", None),
            P("expert", None),
            P("expert", None),
        ),
        out_specs=(
            P("expert", None),
            P("expert", None),
            P("expert"),
            P("expert", "tensor"),
            P("expert", None),
            P("expert"),
            P("expert", "tensor"),
            P("tensor", "expert"),
            P("expert"),
            P("expert", None),
            P(None, "expert", "tensor"),
            P("tensor", "expert"),
            P("expert", None, None, "tensor"),
            P("expert", "tensor", None),
        ),
        check_vma=False,
    )
```

```python
import functools

import jax
import jax.numpy as jnp
from jax import lax
from jax.experimental import pallas as pl
from jax.experimental.pallas import tpu as pltpu
from jax.sharding import PartitionSpec as P

DN = 128
DR = 64
DV = 128
LANES = 128


EPSILON = 1e-06
ROUTE_SCALE = 2.446
ROPE_BASE = 50000.0
NEGATIVE = -1e30


def cut_along(value, dim, length):
    before, after = (value.shape[:dim], value.shape[dim + 1 :])
    return jnp.moveaxis(value.reshape(*before, length, -1, *after), dim, 0)


def summed_on_arrival(value, axis, dim):
    length = lax.axis_size(axis)
    tiles = lax.all_to_all(cut_along(value, dim, length), axis, 0, 0, tiled=True)
    return jnp.sum(tiles.astype(jnp.float32), axis=0)


def sent_together(arrays, axis, dim, along):
    columns = [a.reshape(*a.shape[:along], -1) for a in arrays]
    both = jnp.concatenate(columns, axis=along)
    whole, at, outs = (summed_on_arrival(both, axis, dim), 0, [])
    for a, column in zip(arrays, columns):
        slab = whole[..., at : at + column.shape[along]]
        outs.append(slab.reshape(*slab.shape[:along], *a.shape[along:]))
        at += column.shape[along]
    return tuple(outs)


def contract_rows(left_arr, right_arr):
    return lax.dot_general(
        left_arr, right_arr, (((0,), (0,)), ((), ())), preferred_element_type=jnp.float32
    )


def contract_cols(left_arr, right_arr):
    return lax.dot_general(
        left_arr, right_arr, (((1,), (1,)), ((), ())), preferred_element_type=jnp.float32
    )


def rms_forward(rows_in, gain_vec):
    inverse = lax.rsqrt(jnp.mean(rows_in * rows_in, axis=-1, keepdims=True) + EPSILON)
    return (rows_in * inverse * gain_vec, inverse)


def rms_backward(rows_in, inverse, gain_vec, grad_out):
    gain_grad = jnp.sum(grad_out * rows_in * inverse, axis=0)
    weighted = grad_out * gain_vec
    inner_mean = jnp.mean(weighted * rows_in, axis=-1, keepdims=True)
    return (inverse * weighted - rows_in * inverse * inverse * inverse * inner_mean, gain_grad)


def doc_layout(doc_lengths, row_count):
    ends_at = jnp.cumsum(doc_lengths)
    starts_at = ends_at - doc_lengths
    position = jnp.arange(row_count, dtype=jnp.int32)
    doc_ids = jnp.sum((position[:, None] >= ends_at[None, :]).astype(jnp.int32), axis=1)
    hitting = doc_ids[:, None] == jnp.arange(doc_lengths.shape[0], dtype=jnp.int32)[None, :]
    start_of = jnp.sum(jnp.where(hitting, starts_at[None, :], 0), axis=1)
    relative = position - start_of
    visible = (doc_ids[:, None] == doc_ids[None, :]) & (position[:, None] >= position[None, :])
    return (relative, visible)


def rope_tables(relative, rot_width):
    counter = jnp.arange(rot_width // 2, dtype=jnp.float32)
    frequency = ROPE_BASE ** (-2.0 * counter / rot_width)
    angles = relative.astype(jnp.float32)[:, None] * frequency[None, :]
    return (jnp.cos(angles), jnp.sin(angles))


def rotate(tensor_in, cosine, sine_tab):
    half_width = tensor_in.shape[-1] // 2
    leading = tensor_in[..., :half_width]
    trailing = tensor_in[..., half_width:]
    return jnp.concatenate(
        [leading * cosine - trailing * sine_tab, trailing * cosine + leading * sine_tab], axis=-1
    )


def unrotate(grad_in, cosine, sine_tab):
    half_width = grad_in.shape[-1] // 2
    leading = grad_in[..., :half_width]
    trailing = grad_in[..., half_width:]
    return jnp.concatenate(
        [leading * cosine + trailing * sine_tab, trailing * cosine - leading * sine_tab], axis=-1
    )


def gated_linear_backward(gate_in, up_in, grad_act):
    sigmoid_g = jax.nn.sigmoid(gate_in)
    grad_gate = grad_act * up_in * sigmoid_g * (1.0 + gate_in * (1.0 - sigmoid_g))
    return (grad_gate, grad_act * gate_in * sigmoid_g)


def slot_tables(route_rows, expert_count, capacity):
    flat_routes = route_rows.reshape(-1)
    one_hot = (flat_routes[:, None] == jnp.arange(expert_count, dtype=jnp.int32)[None, :]).astype(
        jnp.int32
    )
    ranking = jnp.sum((jnp.cumsum(one_hot, axis=0) - one_hot) * one_hot, axis=1)
    slot_ids = flat_routes * capacity + ranking
    row_total = flat_routes.shape[0]
    source = (
        jnp.zeros((expert_count * capacity,), jnp.int32)
        .at[slot_ids]
        .set(jnp.arange(row_total, dtype=jnp.int32))
    )
    filled = jnp.zeros((expert_count * capacity,), jnp.int32).at[slot_ids].set(1)
    return (slot_ids, source, filled)


def to_owner(rows_in):
    arrived = lax.all_to_all(rows_in, "expert", split_axis=0, concat_axis=1, tiled=True)
    return arrived


def weight_plan(
    inputs,
    attn_gain,
    w_query,
    w_latent,
    latent_gain,
    w_kv,
    w_out,
    ffn_gain,
    w_router,
    shared_gate_up,
    shared_down,
    expert_gate_up,
    expert_down,
    lengths,
    routes,
    cotangent,
):
    tok_rows = inputs.shape[0]
    model_width = inputs.shape[1]
    expert_count = w_router.shape[1]
    route_count = routes.shape[1]
    capacity = tok_rows * route_count * 4 // (3 * expert_count)
    brain_float16 = jnp.bfloat16
    f32 = jnp.float32
    gathered = (
        lax.all_gather(attn_gain, "expert", axis=0, tiled=True),
        lax.all_gather(w_query, "expert", axis=0, tiled=True),
        lax.all_gather(w_latent, "expert", axis=0, tiled=True),
        lax.all_gather(latent_gain, "expert", axis=0, tiled=True),
        lax.all_gather(w_kv, "expert", axis=0, tiled=True),
        lax.all_gather(w_out, "expert", axis=1, tiled=True),
        lax.all_gather(ffn_gain, "expert", axis=0, tiled=True),
        lax.all_gather(w_router, "expert", axis=0, tiled=True),
        lax.all_gather(shared_gate_up, "expert", axis=1, tiled=True),
        lax.all_gather(shared_down, "expert", axis=1, tiled=True),
    )
    gain_one, query_w, latent_w, latent_g, kv_w, out_w, gain_two, router_w, sgate_up, sdown_w = (
        gathered
    )
    local_heads = query_w.shape[1] // (DN + DR)
    rank_width = latent_g.shape[0]
    x_float = inputs.astype(f32)
    relative, visible = doc_layout(lengths[0], tok_rows)
    cosine, sine_tab = rope_tables(relative, DR)
    q_scale = (DN + DR) ** (-0.5)
    normed, scale_one = rms_forward(x_float, gain_one.astype(f32))
    normed_b = normed.astype(brain_float16)
    queries = jnp.dot(normed_b, query_w, preferred_element_type=f32).reshape(
        tok_rows, local_heads, DN + DR
    )
    q_rot = rotate(queries[..., DN:], cosine[:, None, :], sine_tab[:, None, :])
    q_all = jnp.concatenate([queries[..., :DN], q_rot], axis=-1).astype(brain_float16)
    latent = jnp.dot(normed_b, latent_w, preferred_element_type=f32)
    compressed, scale_kv = rms_forward(latent[:, :rank_width], latent_g.astype(f32))
    compressed_b = compressed.astype(brain_float16)
    k_rope = rotate(latent[:, rank_width:], cosine, sine_tab).astype(brain_float16)
    kv_all = jnp.dot(compressed_b, kv_w, preferred_element_type=f32).reshape(
        tok_rows, local_heads, DN + DV
    )
    k_nope = kv_all[..., :DN].astype(brain_float16)
    values = kv_all[..., DN:].astype(brain_float16)
    key_all = jnp.concatenate(
        [k_nope, jnp.broadcast_to(k_rope[:, None, :], (tok_rows, local_heads, DR))], axis=-1
    )

    def score_block():
        raw_scores = (
            jnp.einsum("qhd,khd->hqk", q_all, key_all, preferred_element_type=f32) * q_scale
        )
        return jnp.where(visible[None], raw_scores, NEGATIVE)

    scores = score_block()
    top_score = jnp.max(scores, axis=-1, keepdims=True)
    log_total = top_score + jnp.log(jnp.sum(jnp.exp(scores - top_score), axis=-1, keepdims=True))
    probs_b = jnp.exp(scores - log_total).astype(brain_float16)
    attended = jnp.einsum("hqk,khd->qhd", probs_b, values, preferred_element_type=f32)
    attended_b = attended.reshape(tok_rows, local_heads * DV).astype(brain_float16)
    attn = lax.psum(jnp.dot(attended_b, out_w, preferred_element_type=f32), "tensor")
    hidden = x_float + attn
    hnormed, scale_two = rms_forward(hidden, gain_two.astype(f32))
    hnormed_b = hnormed.astype(brain_float16)
    logits = jnp.dot(hnormed_b, router_w, preferred_element_type=f32)
    sigmoid_vals = jax.nn.sigmoid(logits)
    route_hot = routes[:, :, None] == jnp.arange(expert_count, dtype=jnp.int32)[None, None, :]
    chosen = jnp.sum(jnp.where(route_hot, sigmoid_vals[:, None, :], 0.0), axis=2)
    chosen_sum = jnp.sum(chosen, axis=1, keepdims=True)
    gate_vals = ROUTE_SCALE * chosen / chosen_sum
    slot_ids, source, filled = slot_tables(routes, expert_count, capacity)
    is_filled = filled[:, None] == 1
    sent_rows = jnp.where(is_filled, hnormed_b[source // route_count], 0).reshape(
        expert_count, capacity, model_width
    )
    received = to_owner(sent_rows)
    gate_up_joined = jnp.einsum(
        "erd,egdf->egrf", received, expert_gate_up, preferred_element_type=f32
    )
    expert_act = (jax.nn.silu(gate_up_joined[:, 0]) * gate_up_joined[:, 1]).astype(brain_float16)
    expert_res = jnp.einsum(
        "erf,efd->erd", expert_act, expert_down, preferred_element_type=f32
    ).astype(brain_float16)
    returned_all = lax.all_to_all(expert_res, "expert", split_axis=1, concat_axis=0, tiled=True)
    returned = returned_all.reshape(expert_count * capacity, model_width)[slot_ids].reshape(
        tok_rows, route_count, model_width
    )
    shared_gu = jnp.einsum("td,gdf->gtf", hnormed_b, sgate_up, preferred_element_type=f32)
    shared_act = (jax.nn.silu(shared_gu[0]) * shared_gu[1]).astype(brain_float16)
    branch_sum = jnp.dot(shared_act, sdown_w, preferred_element_type=f32)
    for route_idx in range(route_count):
        branch_sum = branch_sum + gate_vals[:, route_idx : route_idx + 1] * returned[
            :, route_idx
        ].astype(f32)
    moe_out = lax.psum(branch_sum.astype(jnp.bfloat16), "tensor").astype(jnp.float32)
    mixed = (hidden + moe_out).astype(brain_float16)
    grad_y = cotangent.astype(f32)
    sdown_grad = contract_rows(shared_act, cotangent)
    grad_sact = contract_cols(cotangent, sdown_w)
    grad_sgate, grad_sup = gated_linear_backward(shared_gu[0], shared_gu[1], grad_sact)
    grad_sgu = jnp.stack([grad_sgate, grad_sup], axis=0).astype(brain_float16)
    sgu_grad = jnp.einsum("td,gtf->gdf", hnormed_b, grad_sgu, preferred_element_type=f32)
    grad_hn_part = jnp.einsum("gtf,gdf->td", grad_sgu, sgate_up, preferred_element_type=f32)
    gate_columns = []
    for route_idx in range(route_count):
        gate_columns.append(jnp.sum(grad_y * returned[:, route_idx].astype(f32), axis=1))
    gate_part = jnp.stack(gate_columns, axis=1)
    slot_grads = (
        (gate_vals[:, :, None] * grad_y[:, None, :])
        .reshape(tok_rows * route_count, model_width)
        .astype(brain_float16)
    )
    grad_sent = jnp.where(is_filled, slot_grads[source], 0).reshape(
        expert_count, capacity, model_width
    )
    grad_received = to_owner(grad_sent)
    edown_grad = jnp.einsum("erf,erd->efd", expert_act, grad_received, preferred_element_type=f32)
    expert_activation_gradient = jnp.einsum(
        "erd,efd->erf", grad_received, expert_down, preferred_element_type=f32
    )
    expert_gate_gradient, expert_up_gradient = gated_linear_backward(
        gate_up_joined[:, 0], gate_up_joined[:, 1], expert_activation_gradient
    )
    expert_gate_up_gradient = jnp.stack([expert_gate_gradient, expert_up_gradient], axis=1).astype(
        brain_float16
    )
    egu_grad = jnp.einsum(
        "erd,egrf->egdf", received, expert_gate_up_gradient, preferred_element_type=f32
    )
    grad_rows = jnp.einsum(
        "egrf,egdf->erd", expert_gate_up_gradient, expert_gate_up, preferred_element_type=f32
    ).astype(brain_float16)
    grad_back = lax.all_to_all(grad_rows, "expert", split_axis=1, concat_axis=0, tiled=True)
    grad_routes = grad_back.reshape(expert_count * capacity, model_width)[slot_ids].reshape(
        tok_rows, route_count, model_width
    )
    for route_idx in range(route_count):
        grad_hn_part = grad_hn_part + grad_routes[:, route_idx].astype(f32)
    gate_grads = lax.psum(gate_part, "tensor")
    grad_chosen = ROUTE_SCALE * (
        gate_grads / chosen_sum
        - jnp.sum(gate_grads * chosen, axis=1, keepdims=True) / (chosen_sum * chosen_sum)
    )
    grad_sig = jnp.sum(jnp.where(route_hot, grad_chosen[:, :, None], 0.0), axis=1)
    grad_logits = (grad_sig * sigmoid_vals * (1.0 - sigmoid_vals)).astype(brain_float16)
    router_grad = contract_rows(hnormed_b, grad_logits)
    grad_hn = lax.psum(grad_hn_part, "tensor") + contract_cols(grad_logits, router_w)
    grad_hidden_norm, gain_two_grad = rms_backward(hidden, scale_two, gain_two.astype(f32), grad_hn)
    grad_hidden = grad_y + grad_hidden_norm
    grad_hidden_b = grad_hidden.astype(brain_float16)
    out_grad = contract_rows(attended_b, grad_hidden_b)
    grad_att = (
        contract_cols(grad_hidden_b, out_w).reshape(tok_rows, local_heads, DV).astype(brain_float16)
    )
    probs = jnp.exp(score_block() - log_total)
    probs_again = probs.astype(brain_float16)
    grad_probs = jnp.einsum("qhd,khd->hqk", grad_att, values, preferred_element_type=f32)
    grad_vals = jnp.einsum("hqk,qhd->khd", probs_again, grad_att, preferred_element_type=f32)
    row_delta = jnp.sum(probs * grad_probs, axis=-1, keepdims=True)
    grad_scores = (probs * (grad_probs - row_delta)).astype(brain_float16)
    grad_q = jnp.einsum("hqk,khd->qhd", grad_scores, key_all, preferred_element_type=f32) * q_scale
    grad_keys = jnp.einsum("hqk,qhd->khd", grad_scores, q_all, preferred_element_type=f32) * q_scale
    grad_kv = (
        jnp.concatenate([grad_keys[..., :DN], grad_vals], axis=-1)
        .reshape(tok_rows, local_heads * (DN + DV))
        .astype(brain_float16)
    )
    kv_grad = contract_rows(compressed_b, grad_kv)
    grad_comp_part = contract_cols(grad_kv, kv_w)
    grad_krope_part = jnp.sum(grad_keys[..., DN:], axis=1)
    grad_comp, grad_krope = (
        lax.psum(grad_comp_part.astype(jnp.bfloat16), "tensor").astype(jnp.float32),
        lax.psum(grad_krope_part.astype(jnp.bfloat16), "tensor").astype(jnp.float32),
    )
    grad_c, latent_gain_grad = rms_backward(
        latent[:, :rank_width], scale_kv, latent_g.astype(f32), grad_comp
    )
    grad_latent = jnp.concatenate([grad_c, unrotate(grad_krope, cosine, sine_tab)], axis=-1).astype(
        brain_float16
    )
    grad_qrot = unrotate(grad_q[..., DN:], cosine[:, None, :], sine_tab[:, None, :])
    grad_queries = (
        jnp.concatenate([grad_q[..., :DN], grad_qrot], axis=-1)
        .reshape(tok_rows, local_heads * (DN + DR))
        .astype(brain_float16)
    )
    query_grad = contract_rows(normed_b, grad_queries)
    latent_grad = contract_rows(normed_b, grad_latent)
    grad_normed = lax.psum(
        contract_cols(grad_queries, query_w).astype(jnp.bfloat16), "tensor"
    ).astype(jnp.float32) + contract_cols(grad_latent, latent_w)
    grad_x_norm, gain_one_grad = rms_backward(x_float, scale_one, gain_one.astype(f32), grad_normed)
    input_grad = grad_hidden + grad_x_norm
    first_owned = (
        *sent_together(
            (
                gain_one_grad.astype(jnp.bfloat16),
                query_grad.astype(jnp.bfloat16),
                latent_grad.astype(jnp.bfloat16),
            ),
            "expert",
            0,
            1,
        ),
        *sent_together(
            (latent_gain_grad.astype(jnp.bfloat16), kv_grad.astype(jnp.bfloat16)), "expert", 0, 1
        ),
    )
    second_owned = (
        lax.psum_scatter(out_grad, "expert", scatter_dimension=1, tiled=True),
        lax.psum_scatter(gain_two_grad, "expert", scatter_dimension=0, tiled=True),
        lax.psum_scatter(router_grad, "expert", scatter_dimension=0, tiled=True),
        lax.psum_scatter(sgu_grad, "expert", scatter_dimension=1, tiled=True),
        lax.psum_scatter(sdown_grad, "expert", scatter_dimension=1, tiled=True),
    )
    return (
        mixed,
        input_grad,
        first_owned[0],
        first_owned[1],
        first_owned[2],
        first_owned[3],
        first_owned[4],
        second_owned[0],
        second_owned[1],
        second_owned[2],
        second_owned[3],
        second_owned[4],
        egu_grad,
        edown_grad,
    )


def swap_cores(value):
    return lax.ppermute(value, "tensor", [(0, 1), (1, 0)])


def take_rows(value, start, count, axis=0):
    return lax.dynamic_slice_in_dim(value, start, count, axis=axis)


def in_order(core, own, other, axis=0):
    return jnp.where(
        core == 0,
        jnp.concatenate([own, other], axis=axis),
        jnp.concatenate([other, own], axis=axis),
    )


def add_wide(*parts):
    total = parts[0].astype(jnp.float32)
    for part in parts[1:]:
        total = total + part.astype(jnp.float32)
    return total


PLANE = 4


def to_partner(value, flips):
    groups = lax.axis_size("expert")
    return lax.ppermute(value, "expert", [(g, g ^ flips) for g in range(groups)])


def to_deeper(value, step):
    groups = lax.axis_size("expert")
    pairs = [(g, (g + step * PLANE) % groups) for g in range(groups)]
    return lax.ppermute(value, "expert", pairs)


def plane_gather(value):
    return [value] + [to_partner(value, r) for r in range(1, PLANE)]


def plane_scatter(parts):
    return add_wide(parts[0], *[to_partner(parts[r], r) for r in range(1, PLANE)])


def by_place(parts, place):
    odd, high = place % 2 == 1, place // 2 == 1
    parts = [jnp.where(odd, parts[i ^ 1], parts[i]) for i in range(PLANE)]
    return [jnp.where(high, parts[i ^ 2], parts[i]) for i in range(PLANE)]


def tie(*values):
    return lax.optimization_barrier(values)


def deep_pieces(value):
    deep = lax.axis_size("expert") // PLANE
    return [to_deeper(value, s) for s in range(1, deep)]


def one_plane(value, step):
    groups = lax.axis_size("expert")
    pairs = [(g, g + step * PLANE) for g in range(groups) if 0 <= g + step * PLANE < groups]
    return lax.ppermute(value, "expert", pairs)


def deep_hops(value):
    deep = lax.axis_size("expert") // PLANE
    after, before, down, up = [], [], value, value
    for _ in range(1, deep):
        down, up = one_plane(down, 1), one_plane(up, -1)
        after.append(down)
        before.append(up)
    return after, before


def join_hops(hops):
    after, before = hops
    return [a + b for a, b in zip(after, before[::-1])]


def deep_join(value, pieces, z):
    deep = lax.axis_size("expert") // PLANE
    whole = jnp.zeros((deep, *value.shape), value.dtype)
    whole = lax.dynamic_update_index_in_dim(whole, value, z, 0)
    for step in range(1, deep):
        whole = lax.dynamic_update_index_in_dim(whole, pieces[step - 1], (z - step) % deep, 0)
    return whole


def deep_scatter(blocks, z):
    deep = blocks.shape[0]

    def block(index):
        return lax.dynamic_index_in_dim(blocks, index, 0, keepdims=False)

    return add_wide(
        block(z), *[to_deeper(block((z + step) % deep), step) for step in range(1, deep)]
    )


def sum_planes(grad, z):
    deep = lax.axis_size("expert") // PLANE
    rows = deep_scatter(grad.astype(jnp.bfloat16).reshape(deep, -1, grad.shape[1]), z)
    return rows.astype(jnp.bfloat16).reshape(PLANE, -1, grad.shape[1])


def share_columns(rows, place):
    parts = [at_index(rows, 0, place)]
    for r in range(1, PLANE):
        parts.append(to_partner(at_index(rows, 0, place ^ r), r))
    return by_place(parts, place)


def all_groups(value):
    return lax.all_gather(value, "expert", axis=0, tiled=False)


def at_index(value, axis, index):
    return lax.dynamic_index_in_dim(value, index, axis, keepdims=False)


def doc_places(doc_lengths, row_count):
    ends_at = jnp.cumsum(doc_lengths)
    position = jnp.arange(row_count, dtype=jnp.int32)
    doc_ids = jnp.sum((position[:, None] >= ends_at[None, :]).astype(jnp.int32), axis=1)
    hitting = doc_ids[:, None] == jnp.arange(doc_lengths.shape[0], dtype=jnp.int32)[None, :]
    start_of = jnp.sum(jnp.where(hitting, (ends_at - doc_lengths)[None, :], 0), axis=1)
    return position - start_of, doc_ids


class RowGather:
    def __init__(self, value):
        self.cut = value.shape[0] // 2
        self.value = value

    def along(self):
        return [self.value] + deep_pieces(self.value)

    def lines(self, came):
        return [jnp.stack([v[: self.cut] for v in came]), jnp.stack([v[self.cut :] for v in came])]

    def over(self, lines):
        first, second = lines
        beside, behind = to_partner(first, 1), to_partner(second, 2)
        return [
            [first, beside, to_partner(first, 2), to_partner(beside, 2)],
            [second, to_partner(second, 1), behind, to_partner(behind, 1)],
        ]

    def whole(self, halves):
        return jnp.concatenate([jnp.concatenate(half, axis=0) for half in halves], axis=1)


class RowSum:
    def __init__(self, *terms):
        groups, rows = terms[0].shape[:2]
        self.type = terms[0].dtype
        cut = rows // 2
        blocks = [v.reshape(PLANE, groups // PLANE, *v.shape[1:]) for v in terms]
        self.halves = (
            ([v[:, :, :cut] for v in blocks], 2, 1),
            ([v[:, :, cut:] for v in blocks], 1, 2),
        )

    def _add(self, parts):
        return add_wide(*parts).astype(self.type)

    def sends(self):
        return [
            jnp.stack([self._add([v[far] for v in held]), self._add([v[far | near] for v in held])])
            for held, far, near in self.halves
        ]

    def move(self, sends):
        return [to_partner(v, far) for v, (_, far, _) in zip(sends, self.halves)]

    def sends_again(self, came):
        return [
            self._add([v[near] for v in held] + [c[1]])
            for c, (held, _, near) in zip(came, self.halves)
        ]

    def move_again(self, sends):
        return [to_partner(v, near) for v, (_, _, near) in zip(sends, self.halves)]

    def line(self, came, came_again):
        sums = [
            self._add([v[0] for v in held] + [c[0], d])
            for c, d, (held, *_) in zip(came, came_again, self.halves)
        ]
        return jnp.concatenate(sums, axis=1)


def line_sends(line):
    return [line[step] for step in range(line.shape[0])]


def line_move(sends):
    return [sends[0]] + [to_deeper(v, -step) for step, v in enumerate(sends) if step > 0]


def dot_nn(left, right):
    return lax.dot_general(left, right, (((1,), (0,)), ((), ())), preferred_element_type=jnp.float32)


def dot_nt(left, right):
    return lax.dot_general(left, right, (((1,), (1,)), ((), ())), preferred_element_type=jnp.float32)


def dot_tn(left, right):
    return lax.dot_general(left, right, (((0,), (0,)), ((), ())), preferred_element_type=jnp.float32)


def two_lanes(column, lane):
    high = column.astype(jnp.bfloat16).astype(jnp.float32)
    spread = jnp.where(lane == 0, high, jnp.where(lane == 1, column - high, 0.0))
    return spread.astype(jnp.bfloat16)


def expert_kernel(
    shared_cols,
    expert_count,
    me_ref,
    hn_own,
    hn_other,
    dy_own,
    dy_other,
    meta_own,
    meta_other,
    gate_up_w,
    down_w,
    first_w,
    sdown_w,
    slots_out,
    slot_dy_out,
    act_out,
    d_gate_up_out,
    rows_own_out,
    rows_other_out,
    sact_own_out,
    sact_other_out,
    shared_grads_out,
    dgate_own_out,
    dgate_other_out,
):
    f32, bf16 = jnp.float32, jnp.bfloat16
    count, half, _ = hn_own.shape
    tokens = 2 * half
    me = me_ref[0]
    lane = lax.broadcasted_iota(jnp.int32, (tokens, LANES), 1)
    is_router = (lane >= shared_cols) & (lane < shared_cols + expert_count)
    first = first_w[...]
    slots, slot_dys, slot_gates, picks, dshs = [], [], [], [], []
    first_grad, sdown_grad = 0.0, 0.0
    for i in range(count):
        rows = jnp.concatenate([hn_own[i], hn_other[i]], axis=0)
        rows_dy = jnp.concatenate([dy_own[i], dy_other[i]], axis=0)
        meta = jnp.concatenate([meta_own[i], meta_other[i]], axis=0)
        products = dot_nt(rows, first)
        gate, up = products[:, :LANES], products[:, LANES:]
        sig = jax.nn.sigmoid(gate)
        total = jnp.sum(jnp.where(is_router, sig * meta, 0.0), axis=1, keepdims=True)
        mine = jnp.sum(jnp.where(lane == shared_cols + me, sig, 0.0), axis=1, keepdims=True)
        token_gate = ROUTE_SCALE * mine / total
        sact = (gate * sig * up).astype(bf16)
        sact_own_out[i], sact_other_out[i] = sact[:half], sact[half:]
        d_sact = dot_nt(rows_dy, sdown_w[...])
        d_sgate = d_sact * up * sig * (1.0 + gate * (1.0 - sig))
        dsh = jnp.concatenate([d_sgate, d_sact * gate * sig], axis=1).astype(bf16)
        dshs.append(dsh)
        first_grad += dot_tn(dsh, rows)
        sdown_grad += dot_tn(sact, rows_dy)
        pick = (meta[:, :1] == lane.astype(f32)).astype(bf16)
        picks.append(pick)
        slots.append(dot_tn(pick, rows).astype(bf16))
        slot_dys.append(dot_tn(pick, rows_dy).astype(bf16))
        slot_gates.append(
            jnp.sum(dot_tn(pick, two_lanes(token_gate, lane)), axis=1, keepdims=True)
        )

    @pl.when(pl.program_id(0) == 0)
    def _():
        shared_grads_out[...] = jnp.zeros_like(shared_grads_out)

    shared_grads_out[:shared_cols] += first_grad[:shared_cols]
    shared_grads_out[shared_cols : 2 * shared_cols] += first_grad[LANES : LANES + shared_cols]
    shared_grads_out[2 * shared_cols :] += sdown_grad[:shared_cols]
    slot_rows = jnp.concatenate(slots, axis=0)
    slot_dy = jnp.concatenate(slot_dys, axis=0)
    slot_gate = jnp.concatenate(slot_gates, axis=0)
    slots_out[...] = slot_rows
    slot_dy_out[...] = slot_dy
    gate = dot_nt(slot_rows, gate_up_w[0])
    up = dot_nt(slot_rows, gate_up_w[1])
    d_act = dot_nt(slot_dy, down_w[...])
    sig = jax.nn.sigmoid(gate)
    silu = gate * sig
    act = silu * up
    slot_dgate = jnp.sum(act * d_act, axis=1, keepdims=True)
    act_out[...] = (slot_gate * act).astype(bf16)
    d_act = slot_gate * d_act
    d_gate = (d_act * up * sig * (1.0 + gate * (1.0 - sig))).astype(bf16)
    d_up = (d_act * silu).astype(bf16)
    d_gate_up_out[0] = d_gate
    d_gate_up_out[1] = d_up
    d_slots = (dot_nn(d_gate, gate_up_w[0]) + dot_nn(d_up, gate_up_w[1])).astype(bf16)
    slot_lane = lax.broadcasted_iota(jnp.int32, (LANES, LANES), 1)
    for i in range(count):
        here = slice(i * LANES, (i + 1) * LANES)
        d_rows = (dot_nn(picks[i], d_slots[here]) + dot_nn(dshs[i], first)).astype(bf16)
        rows_own_out[i], rows_other_out[i] = d_rows[:half], d_rows[half:]
        dgate = dot_nn(picks[i], two_lanes(slot_dgate[here], slot_lane))
        dgate_own_out[i], dgate_other_out[i] = dgate[:half], dgate[half:]


def block_specs(per_step):
    def lead(*tail):
        return pl.BlockSpec((per_step, *tail), lambda i: (i,) + (0,) * len(tail))

    def flat(cols):
        return pl.BlockSpec((per_step * LANES, cols), lambda i: (i, 0))

    def whole(a):
        return pl.BlockSpec(a.shape, lambda i: (0,) * a.ndim, pipeline_mode=pl.Buffered(1))

    return lead, flat, whole


def slots_cost(width, hidden, products):
    return LANES * width * hidden * products


def experts(
    me,
    hn_own,
    hn_other,
    dy_own,
    dy_other,
    meta_own,
    meta_other,
    gate_up_w,
    down_w,
    first_w,
    sdown_w,
    shared_cols,
    expert_count,
    per_step=2,
):
    groups, half, width = hn_own.shape
    hidden = down_w.shape[0]
    slots = groups * LANES
    f32, bf16 = jnp.float32, jnp.bfloat16
    lead, flat, whole = block_specs(per_step)
    sds = jax.ShapeDtypeStruct
    rows_cost = 2 * groups * (2 * half * width * 4 * LANES + slots_cost(width, hidden, 5))
    return pl.pallas_call(
        functools.partial(expert_kernel, shared_cols, expert_count),
        grid=(groups // per_step,),
        in_specs=[
            pl.BlockSpec(memory_space=pltpu.SMEM),
            *[lead(half, width)] * 4,
            *[lead(half, LANES)] * 2,
            *[whole(a) for a in (gate_up_w, down_w, first_w, sdown_w)],
        ],
        out_specs=[
            flat(width),
            flat(width),
            flat(hidden),
            pl.BlockSpec((2, per_step * LANES, hidden), lambda i: (0, i, 0)),
            *[lead(half, width)] * 2,
            *[lead(half, LANES)] * 2,
            pl.BlockSpec((3 * shared_cols, width), lambda i: (0, 0)),
            *[lead(half, LANES)] * 2,
        ],
        out_shape=[
            sds((slots, width), bf16),
            sds((slots, width), bf16),
            sds((slots, hidden), bf16),
            sds((2, slots, hidden), bf16),
            *[sds((groups, half, width), bf16)] * 2,
            *[sds((groups, half, LANES), bf16)] * 2,
            sds((3 * shared_cols, width), f32),
            *[sds((groups, half, LANES), f32)] * 2,
        ],
        compiler_params=pltpu.CompilerParams(vmem_limit_bytes=58 * 1024 * 1024),
        cost_estimate=pl.CostEstimate(
            flops=rows_cost, bytes_accessed=20 * groups * half * width, transcendentals=0
        ),
    )(
        me,
        hn_own,
        hn_other,
        dy_own,
        dy_other,
        meta_own,
        meta_other,
        gate_up_w,
        down_w,
        first_w,
        sdown_w,
    )


def swap_halves(value, lane):
    low = lane % DR < DR // 2
    return jnp.where(low, pltpu.roll(value, LANES - DR // 2, 1), pltpu.roll(value, DR // 2, 1))


def by_core(core, first, second):
    return jnp.where(core == 0, first, second), jnp.where(core == 0, second, first)


def head_scores(q, kv, k_rope, visible, lane, head, heads):
    q_nope = q[:, head * DN : (head + 1) * DN]
    q_rope = jnp.where(lane // DR == head, q[:, heads * DN :], jnp.zeros((), q.dtype))
    at = head * (DN + DV)
    k_nope, value = kv[:, at : at + DN], kv[:, at + DN : at + DN + DV]
    scores = (dot_nt(q_nope, k_nope) + dot_nt(q_rope, k_rope)) * (DN + DR) ** -0.5
    return jnp.where(visible, scores, NEGATIVE), q_nope, q_rope, k_nope, value


def seen(doc_col, doc_row):
    rows = doc_col.shape[0]
    later = lax.broadcasted_iota(jnp.int32, (rows, rows), 0) >= lax.broadcasted_iota(
        jnp.int32, (rows, rows), 1
    )
    return (doc_col == doc_row) & later


def attention_kernel(
    heads,
    rank,
    core_ref,
    x_own,
    x_other,
    gain,
    latent_gain,
    head_w,
    small_w,
    kv_w,
    cosine,
    sine,
    doc_col,
    doc_row,
    normed_out,
    compressed_out,
    q_out,
    kv_out,
    k_rope_out,
    sums_out,
    attended_out,
    latent_out,
    part_own_out,
    part_other_out,
):
    f32, bf16 = jnp.float32, jnp.bfloat16
    core = core_ref[0]
    x = jnp.concatenate(by_core(core, x_own[0], x_other[0]), axis=0).astype(f32)
    rows = x.shape[0]
    half = rows // 2
    lane = lax.broadcasted_iota(jnp.int32, (rows, LANES), 1)
    inverse = lax.rsqrt(jnp.mean(x * x, axis=1, keepdims=True) + EPSILON)
    normed = (x * inverse * gain[...]).astype(bf16)
    normed_out[0] = normed
    q_cols = heads * (DN + DR)
    queries = dot_nn(normed, head_w[:, :q_cols])
    q_rope = queries[:, heads * DN :]
    q_rope = q_rope * cosine[0] + swap_halves(q_rope, lane) * sine[0]
    q = jnp.concatenate([queries[:, : heads * DN], q_rope], axis=1).astype(bf16)
    q_out[0] = q
    latent = dot_nn(normed, small_w[:, : rank + LANES])
    latent_out[0] = latent
    squeezed = latent[:, :rank]
    inverse = lax.rsqrt(jnp.mean(squeezed * squeezed, axis=1, keepdims=True) + EPSILON)
    compressed = (squeezed * inverse * latent_gain[...]).astype(bf16)
    compressed_out[0] = compressed
    k_rope = latent[:, rank:]
    k_rope = (k_rope * cosine[0] + swap_halves(k_rope, lane) * sine[0]).astype(bf16)
    k_rope_out[0] = k_rope
    kv = dot_nn(compressed, kv_w[...]).astype(bf16)
    kv_out[0] = kv
    visible = seen(doc_col[0], doc_row[0])
    attended, sums = [], jnp.zeros((rows, LANES), f32)
    for head in range(heads):
        scores, *_, value = head_scores(q, kv, k_rope, visible, lane, head, heads)
        top = jnp.max(scores, axis=1, keepdims=True)
        log_total = top + jnp.log(jnp.sum(jnp.exp(scores - top), axis=1, keepdims=True))
        sums = jnp.where(lane == head, log_total, sums)
        probs = jnp.exp(scores - log_total).astype(bf16)
        attended.append(dot_nn(probs, value).astype(bf16))
    sums_out[0] = sums
    attended = jnp.concatenate(attended, axis=1)
    attended_out[0] = attended
    part = dot_nt(attended, head_w[:, q_cols : q_cols + heads * DV]).astype(bf16)
    part_own_out[0], part_other_out[0] = by_core(core, part[:half], part[half:])


def attention_backward_kernel(
    heads,
    core_ref,
    d_own,
    d_other,
    normed_ref,
    compressed_ref,
    q_ref,
    kv_ref,
    k_rope_ref,
    sums_ref,
    attended_ref,
    head_w,
    kv_w,
    cosine,
    sine,
    doc_col,
    doc_row,
    head_grad_out,
    kv_grad_out,
    normed_own_out,
    normed_other_out,
    latent_own_out,
    latent_other_out,
    head_acc,
    kv_acc,
):
    f32, bf16 = jnp.float32, jnp.bfloat16
    core, step = core_ref[0], pl.program_id(0)
    scale = (DN + DR) ** -0.5
    d_rows = jnp.concatenate(by_core(core, d_own[0], d_other[0]), axis=0)
    rows = d_rows.shape[0]
    half = rows // 2
    lane = lax.broadcasted_iota(jnp.int32, (rows, LANES), 1)
    q_cols = heads * (DN + DR)
    q, kv, k_rope = q_ref[0], kv_ref[0], k_rope_ref[0]
    d_attended = dot_nn(d_rows, head_w[:, q_cols : q_cols + heads * DV]).astype(bf16)
    visible = seen(doc_col[0], doc_row[0])
    d_q, d_kv = [], []
    d_q_rope, d_k_rope = jnp.zeros((rows, LANES), f32), jnp.zeros((rows, LANES), f32)
    for head in range(heads):
        scores, q_nope, q_rope, k_nope, value = head_scores(
            q, kv, k_rope, visible, lane, head, heads
        )
        probs = jnp.exp(scores - sums_ref[0][:, head : head + 1])
        d_head = d_attended[:, head * DV : (head + 1) * DV]
        d_probs = dot_nt(d_head, value)
        d_value = dot_tn(probs.astype(bf16), d_head)
        delta = jnp.sum(probs * d_probs, axis=1, keepdims=True)
        d_scores = (probs * (d_probs - delta)).astype(bf16)
        d_q.append(dot_nn(d_scores, k_nope) * scale)
        d_q_rope = jnp.where(lane // DR == head, dot_nn(d_scores, k_rope) * scale, d_q_rope)
        d_kv += [dot_tn(d_scores, q_nope) * scale, d_value]
        d_k_rope += dot_tn(d_scores, q_rope) * scale
    d_q_rope = d_q_rope * cosine[0] - swap_halves(d_q_rope, lane) * sine[0]
    d_q = jnp.concatenate(d_q + [d_q_rope], axis=1).astype(bf16)
    d_kv = jnp.concatenate(d_kv, axis=1).astype(bf16)

    @pl.when(step == 0)
    def _():
        head_acc[...] = jnp.zeros_like(head_acc)
        kv_acc[...] = jnp.zeros_like(kv_acc)

    head_acc[:, :q_cols] += dot_tn(normed_ref[0], d_q)
    head_acc[:, q_cols:] += dot_tn(d_rows, attended_ref[0])
    kv_acc[...] += dot_tn(compressed_ref[0], d_kv)

    @pl.when(step == pl.num_programs(0) - 1)
    def _():
        head_grad_out[...] = head_acc[...].astype(bf16)
        kv_grad_out[...] = kv_acc[...].astype(bf16)

    part = dot_nt(d_q, head_w[:, :q_cols]).astype(bf16)
    normed_own_out[0], normed_other_out[0] = by_core(core, part[:half], part[half:])
    latent = jnp.concatenate([dot_nt(d_kv, kv_w[...]), d_k_rope], axis=1).astype(bf16)
    latent_own_out[0], latent_other_out[0] = by_core(core, latent[:half], latent[half:])


def one_each(*tail):
    return pl.BlockSpec((1, *tail), lambda i: (i,) + (0,) * len(tail))


def kept(value):
    return pl.BlockSpec(value.shape, lambda i: (0,) * value.ndim, pipeline_mode=pl.Buffered(1))


def attention(core, x_own, x_other, gain, latent_gain, head_w, small_w, kv_w, cosine, sine, doc):
    near, half, width = x_own.shape
    rows = 2 * half
    rank, kv_cols = kv_w.shape
    heads = kv_cols // (DN + DV)
    f32, bf16 = jnp.float32, jnp.bfloat16
    shapes = [
        ((rows, width), bf16),
        ((rows, rank), bf16),
        ((rows, heads * (DN + DR)), bf16),
        ((rows, kv_cols), bf16),
        ((rows, LANES), bf16),
        ((rows, LANES), f32),
        ((rows, heads * DV), bf16),
        ((rows, rank + LANES), f32),
        ((half, width), bf16),
        ((half, width), bf16),
    ]
    return pl.pallas_call(
        functools.partial(attention_kernel, heads, rank),
        grid=(near,),
        in_specs=[
            pl.BlockSpec(memory_space=pltpu.SMEM),
            *[one_each(half, width)] * 2,
            *[kept(a) for a in (gain, latent_gain, head_w, small_w, kv_w)],
            *[one_each(rows, LANES)] * 2,
            one_each(rows, 1),
            one_each(1, rows),
        ],
        out_specs=[one_each(*shape) for shape, _ in shapes],
        out_shape=[jax.ShapeDtypeStruct((near, *shape), kind) for shape, kind in shapes],
        compiler_params=pltpu.CompilerParams(vmem_limit_bytes=58 * 1024 * 1024),
        cost_estimate=pl.CostEstimate(
            flops=2 * near * rows * width * (rank + 3 * heads * DN),
            bytes_accessed=4 * near * rows * width,
            transcendentals=0,
        ),
    )(
        core,
        x_own,
        x_other,
        gain,
        latent_gain,
        head_w,
        small_w,
        kv_w,
        cosine,
        sine,
        doc[:, :, None],
        doc[:, None, :],
    )


def attention_backward(core, d_own, d_other, kept_rows, head_w, kv_w, cosine, sine, doc):
    near, half, width = d_own.shape
    rows = 2 * half
    rank, kv_cols = kv_w.shape
    heads = kv_cols // (DN + DV)
    head_cols = heads * (DN + DR + DV)
    f32, bf16 = jnp.float32, jnp.bfloat16
    sds = jax.ShapeDtypeStruct
    return pl.pallas_call(
        functools.partial(attention_backward_kernel, heads),
        grid=(near,),
        in_specs=[
            pl.BlockSpec(memory_space=pltpu.SMEM),
            *[one_each(half, width)] * 2,
            *[one_each(*v.shape[1:]) for v in kept_rows],
            *[kept(a) for a in (head_w, kv_w)],
            *[one_each(rows, LANES)] * 2,
            one_each(rows, 1),
            one_each(1, rows),
        ],
        out_specs=[
            pl.BlockSpec((width, head_cols), lambda i: (0, 0)),
            pl.BlockSpec((rank, kv_cols), lambda i: (0, 0)),
            *[one_each(half, width)] * 2,
            *[one_each(half, rank + LANES)] * 2,
        ],
        out_shape=[
            sds((width, head_cols), bf16),
            sds((rank, kv_cols), bf16),
            *[sds((near, half, width), bf16)] * 2,
            *[sds((near, half, rank + LANES), bf16)] * 2,
        ],
        scratch_shapes=[
            pltpu.VMEM((width, head_cols), f32),
            pltpu.VMEM((rank, kv_cols), f32),
        ],
        compiler_params=pltpu.CompilerParams(vmem_limit_bytes=58 * 1024 * 1024),
        cost_estimate=pl.CostEstimate(
            flops=near * rows * width * heads * DN,
            bytes_accessed=2 * near * rows * width,
            transcendentals=0,
        ),
    )(
        core,
        d_own,
        d_other,
        *kept_rows,
        head_w,
        kv_w,
        cosine,
        sine,
        doc[:, :, None],
        doc[:, None, :],
    )


def product_kernel(left_ref, right_ref, out_ref):
    out_ref[0] = dot_tn(left_ref[0], right_ref[...])


def column_products(left, right, tile=512):
    count, rows, height = left.shape
    width = right.shape[1]
    return pl.pallas_call(
        product_kernel,
        grid=(width // tile, count),
        in_specs=[
            pl.BlockSpec((1, rows, height), lambda j, i: (i, 0, 0)),
            pl.BlockSpec((rows, tile), lambda j, i: (0, j)),
        ],
        out_specs=pl.BlockSpec((1, height, tile), lambda j, i: (i, 0, j)),
        out_shape=jax.ShapeDtypeStruct((count, height, width), jnp.float32),
        compiler_params=pltpu.CompilerParams(vmem_limit_bytes=58 * 1024 * 1024),
        cost_estimate=pl.CostEstimate(
            flops=rows * width, bytes_accessed=rows * width, transcendentals=0
        ),
    )(left, right)


def output_kernel(act, sact_own, sact_other, meta_own, meta_other, down_w, sdown_w, own_out, other_out):
    f32, bf16 = jnp.float32, jnp.bfloat16
    count, half, _ = meta_own.shape
    lane = lax.broadcasted_iota(jnp.int32, (2 * half, LANES), 1).astype(f32)
    out = dot_nn(act[...], down_w[...]).astype(bf16)
    for i in range(count):
        meta = jnp.concatenate([meta_own[i], meta_other[i]], axis=0)
        pick = (meta[:, :1] == lane).astype(bf16)
        sact = jnp.concatenate([sact_own[i], sact_other[i]], axis=0)
        here = slice(i * LANES, (i + 1) * LANES)
        rows = (dot_nn(pick, out[here]) + dot_nn(sact, sdown_w[...])).astype(bf16)
        own_out[i], other_out[i] = rows[:half], rows[half:]


def outputs(act, sact_own, sact_other, meta_own, meta_other, down_w, sdown_w, per_step=4):
    groups, half, _ = meta_own.shape
    hidden, width = down_w.shape
    lead, flat, whole = block_specs(per_step)
    return pl.pallas_call(
        output_kernel,
        grid=(groups // per_step,),
        in_specs=[
            flat(hidden),
            *[lead(half, LANES)] * 4,
            *[whole(a) for a in (down_w, sdown_w)],
        ],
        out_specs=[lead(half, width)] * 2,
        out_shape=[jax.ShapeDtypeStruct((groups, half, width), jnp.bfloat16)] * 2,
        compiler_params=pltpu.CompilerParams(vmem_limit_bytes=58 * 1024 * 1024),
        cost_estimate=pl.CostEstimate(
            flops=groups * half * LANES * width,
            bytes_accessed=groups * half * width,
            transcendentals=0,
        ),
    )(act, sact_own, sact_other, meta_own, meta_other, down_w, sdown_w)


def token_plan(
    inputs,
    attn_gain,
    w_query,
    w_latent,
    latent_gain,
    w_kv,
    w_out,
    ffn_gain,
    w_router,
    shared_gate_up,
    shared_down,
    expert_gate_up,
    expert_down,
    lengths,
    routes,
    cotangent,
):
    f32, bf16 = jnp.float32, jnp.bfloat16
    core, me = lax.axis_index("tensor"), lax.axis_index("expert")
    groups = lax.axis_size("expert")
    deep, place, z = groups // PLANE, me % PLANE, me // PLANE
    tok_rows, width = inputs.shape
    half = tok_rows // 2
    own_at, other_at = core * half, (1 - core) * half
    expert_count = w_router.shape[1]
    route_count = routes.shape[1]
    capacity = tok_rows * route_count * 4 // (3 * expert_count)
    shared_cols = shared_gate_up.shape[2] // groups
    latent_cols, rank_width = w_latent.shape[1], latent_gain.shape[0] * groups
    block_rows = w_query.shape[0]
    kv_rows = w_kv.shape[0]

    query_cols = w_query.shape[1] // PLANE
    out_cols = w_out.shape[0] // PLANE
    small = jnp.concatenate(
        [
            w_latent,
            w_latent[:, rank_width:],
            w_router,
            attn_gain[:, None],
            ffn_gain[:, None],
            jnp.pad(latent_gain, (0, block_rows - kv_rows))[:, None],
        ],
        axis=1,
    )
    small_cols = small.shape[1]
    route_half = take_rows(routes, own_at, half).astype(bf16).reshape(block_rows // 2, -1)
    length_col = jnp.pad(lengths[0].astype(bf16), (0, block_rows // 2 - lengths.shape[1]))[:, None]
    route_cols = route_half.shape[1] + 1
    small_half = jnp.concatenate(
        [
            take_rows(small, core * (block_rows // 2), block_rows // 2),
            route_half,
            length_col,
            jnp.zeros((block_rows // 2, -(small_cols + route_cols) % (2 * LANES)), bf16),
        ],
        axis=1,
    )
    packed_cols = small_half.shape[1] // 2
    small_packed = jnp.concatenate([small_half[:, :packed_cols], small_half[:, packed_cols:]])
    kv_cols = w_kv.shape[1] // PLANE
    kv_parts = block_rows // kv_rows
    kv_piece = kv_cols // kv_parts
    w_out_t = w_out.T

    local_heads = query_cols // (DN + DR)

    def by_parts(block):
        heads = [block[:, h * (DN + DR) : (h + 1) * (DN + DR)] for h in range(local_heads)]
        return [h[:, :DN] for h in heads] + [h[:, DN:] for h in heads]

    def quarter(index):
        kv_here = take_rows(w_kv, index * kv_cols, kv_cols, axis=1)
        kv_here = [kv_here[:, p * kv_piece : (p + 1) * kv_piece] for p in range(kv_parts)]
        return jnp.concatenate(
            [
                *by_parts(take_rows(w_query, index * query_cols, query_cols, axis=1)),
                take_rows(w_out_t, index * out_cols, out_cols, axis=1),
                jnp.concatenate(kv_here, axis=0),
            ],
            axis=1,
        )

    near_w = [quarter(place)] + [to_partner(quarter(place ^ r), r) for r in range(1, PLANE)]
    small_line = deep_join(small_packed, deep_pieces(small_packed), z)
    near_w, small_line = tie(near_w, small_line)
    plane_w = jnp.stack(by_place(near_w, place))
    near_sent = jnp.concatenate(
        [
            take_rows(inputs, own_at, half),
            small_line.swapaxes(0, 1).reshape(block_rows, -1),
        ],
        axis=1,
    )
    near_sent, plane_w = tie(near_sent, plane_w)
    near_came = jnp.stack([near_sent, to_partner(near_sent, 1)])
    near_came = jnp.concatenate([near_came, to_partner(near_came, 2)], axis=0)
    near_came, deep_w = tie(near_came, deep_hops(plane_w))
    x_near_own = near_came[:, :, :width]
    small_parts = near_came[:, :, width:].reshape(PLANE, block_rows, deep, packed_cols)
    small_parts = [small_parts[r].swapaxes(0, 1) for r in range(PLANE)]
    x_near_other = swap_cores(x_near_own)
    small_own = jnp.stack(by_place(small_parts, place), axis=1)
    small_own = small_own.reshape(groups, block_rows, packed_cols)
    small_own = jnp.concatenate(
        [small_own[:, : block_rows // 2], small_own[:, block_rows // 2 :]], axis=2
    )
    small_other = swap_cores(small_own)
    small_all = in_order(core, small_own, small_other, axis=1)
    head_w = deep_join(plane_w, join_hops(deep_w), z)
    length_at = small_cols + route_cols - 1
    lengths_near = take_rows(small_own, z * PLANE, PLANE)[:, : lengths.shape[1], length_at]
    lengths_near = lengths_near.astype(jnp.int32)
    lengths_near = jnp.stack(by_place([lengths_near[r] for r in range(PLANE)], place))
    shared_rows = jnp.concatenate(
        [shared_gate_up[0].T, shared_gate_up[1].T, shared_down], axis=0
    ).reshape(3, groups, shared_cols, block_rows)
    shared_rows = shared_rows.swapaxes(0, 1).reshape(groups, 3 * shared_cols, block_rows)
    dy_sent, head_w = tie(take_rows(cotangent, own_at, half), head_w)
    dy_own_rows = take_rows(cotangent, own_at, half)
    dy_gather = RowGather(dy_sent)
    dy_came = dy_gather.along()
    head_w = head_w.reshape(groups, block_rows, -1)
    flat_head = head_w.reshape(groups * block_rows, -1)
    at = query_cols + out_cols
    kv_w = head_w[:, :, at : at + kv_piece].reshape(groups, kv_parts, kv_rows, kv_piece)
    kv_w = kv_w.transpose(0, 2, 1, 3).reshape(groups * kv_rows, kv_cols)

    block_index = jnp.arange(groups)
    block_chip = (z - block_index % deep) % deep * PLANE + (place ^ (block_index // deep))
    in_blocks = (block_chip[:, None] == block_index[None, :]).astype(bf16)

    def routes_of(came):
        came = came[:, :, small_cols : small_cols + route_half.shape[1]].reshape(groups, -1)
        came = jnp.dot(in_blocks, came, preferred_element_type=f32)
        return came.astype(jnp.int32).reshape(groups, half, route_count)

    routes_own, routes_other = routes_of(small_own), routes_of(small_other)
    flat_small = small_all.reshape(groups * block_rows, -1)
    latent_w = flat_small[:, :latent_cols]
    at = rank_width + LANES
    router_w = flat_small[:, at : at + expert_count]
    at += expert_count
    gain_one, gain_two = flat_small[:, at], flat_small[:, at + 1]
    latent_g = small_all[:, :kv_rows, at + 2].reshape(-1)

    near_rows = PLANE * tok_rows
    relative, doc = jax.vmap(lambda one: doc_places(one, tok_rows))(lengths_near)
    cosine, sine_tab = rope_tables(relative.reshape(-1), DR)
    cosine, sine_tab = [v.reshape(PLANE, tok_rows, -1) for v in (cosine, sine_tab)]
    rope = (
        jnp.concatenate([cosine] * 4, axis=-1),
        jnp.concatenate([-sine_tab, sine_tab] * 2, axis=-1),
        doc.astype(f32),
    )
    core_index = core.reshape(1).astype(jnp.int32)
    *kept_rows, latent, part_own, part_other = attention(
        core_index,
        x_near_own,
        x_near_other,
        gain_one.astype(f32)[None],
        latent_g.astype(f32)[None],
        flat_head,
        flat_small,
        kv_w,
        *rope,
    )
    normed_b = kept_rows[0].reshape(near_rows, width)
    part_own, part_other, dy_came = tie(part_own, part_other, dy_came)

    def sum_heads(own, other):
        both = add_wide(own, swap_cores(other)).astype(bf16)
        return plane_scatter([both[r] for r in range(PLANE)])

    attn_own = sum_heads(part_own, part_other)
    x_own = take_rows(inputs, own_at, half).astype(f32)
    hidden = x_own + attn_own
    hnormed, scale_two = rms_forward(hidden, gain_two.astype(f32))
    hnormed_b = hnormed.astype(bf16)
    normed_cols = jnp.concatenate(
        [
            take_rows(normed_b, (k * PLANE + place) * block_rows, block_rows, axis=1)
            for k in range(deep)
        ],
        axis=1,
    )
    hnormed_b, dy_lines, normed_cols, shared_rows = tie(
        hnormed_b, dy_gather.lines(dy_came), normed_cols, shared_rows
    )
    def membership(named):
        one_hot = named[..., None] == jnp.arange(expert_count, dtype=jnp.int32)
        return jnp.any(named == me, axis=-1), jnp.any(one_hot, axis=2)

    member_own, hot_own = membership(routes_own)
    member_other, hot_other = membership(routes_other)
    lower = (
        jnp.arange(half, dtype=jnp.int32)[:, None] <= jnp.arange(half, dtype=jnp.int32)[None, :]
    ).astype(bf16)

    def running(mask):
        counts = jnp.dot(mask.astype(bf16), lower, preferred_element_type=f32)
        return counts.astype(jnp.int32)

    count_own, count_other = running(member_own), running(member_other)
    place_own = jnp.where(member_own, count_own - 1, -1)
    place_other = jnp.where(member_other, count_own[:, -1:] + count_other - 1, -1)

    def metadata(slot, hot):
        return jnp.concatenate(
            [
                slot[..., None].astype(f32),
                jnp.zeros((groups, half, shared_cols - 1), f32),
                hot.astype(f32),
                jnp.zeros((groups, half, LANES - shared_cols - expert_count), f32),
            ],
            axis=-1,
        )

    meta_own, meta_other = metadata(place_own, hot_own), metadata(place_other, hot_other)
    hn_gather = RowGather(hnormed_b)
    hn_came, dy_halves, shared_rows = tie(
        hn_gather.along(), dy_gather.over(dy_lines), shared_rows
    )
    hn_lines, dy_halves, shared_rows = tie(hn_gather.lines(hn_came), dy_halves, shared_rows)
    hn_halves = hn_gather.over(hn_lines)
    shared_w = lax.all_to_all(shared_rows, "expert", split_axis=0, concat_axis=0, tiled=True)
    dy_own = dy_gather.whole(dy_halves)
    dy_other = swap_cores(dy_own)
    hn_halves, shared_w, dy_other, meta_own, meta_other = tie(
        hn_halves, shared_w, dy_other, meta_own, meta_other
    )
    shared_w = shared_w.swapaxes(0, 1).reshape(3 * shared_cols, groups * block_rows)
    hn_own = hn_gather.whole(hn_halves)


    first_w = jnp.concatenate(
        [
            shared_w[:shared_cols],
            router_w.T,
            jnp.zeros((LANES - shared_cols - expert_count, width), bf16),
            shared_w[shared_cols : 2 * shared_cols],
            jnp.zeros((LANES - shared_cols, width), bf16),
        ],
        axis=0,
    )
    sdown_rows = jnp.pad(shared_w[2 * shared_cols :], ((0, LANES - shared_cols), (0, 0)))
    hn_other = swap_cores(hn_own)
    gate_up_w, down_w = jnp.swapaxes(expert_gate_up[0], 1, 2), expert_down[0]
    (
        slot_rows,
        slot_dy,
        slot_act,
        d_gate_up,
        d_rows_own,
        d_rows_other,
        act_own,
        act_other,
        shared_grads,
        dgate_own,
        dgate_other,
    ) = experts(
        me.reshape(1).astype(jnp.int32),
        hn_own,
        hn_other,
        dy_own,
        dy_other,
        meta_own,
        meta_other,
        gate_up_w,
        down_w,
        first_w,
        sdown_rows,
        shared_cols,
        expert_count,
    )
    d_rows_came = swap_cores(d_rows_other)

    def two_parts(value):
        return value[..., 0] + value[..., 1]

    dgate_sent = two_parts(dgate_own) + swap_cores(two_parts(dgate_other))
    dgate_high = dgate_sent.astype(bf16)
    dgate_low = (dgate_sent - dgate_high.astype(f32)).astype(bf16)
    out_own, out_other = outputs(
        slot_act, act_own, act_other, meta_own, meta_other, down_w, sdown_rows
    )
    d_rows_came, dgate_high, dgate_low, out_other = tie(
        d_rows_came, dgate_high, dgate_low, out_other
    )
    d_sum = RowSum(d_rows_own, d_rows_came)
    sends, shared_grads, slot_act, out_other = tie(
        d_sum.sends(), shared_grads, slot_act, out_other
    )
    came = d_sum.move(sends)
    gate_rows = jnp.stack([contract_rows(in_blocks, v).reshape(-1) for v in (dgate_high, dgate_low)])
    grads_sent = jnp.concatenate([shared_grads, gate_rows], axis=0).astype(bf16)
    grads_sent = grads_sent.reshape(-1, groups, block_rows)
    grads_came = lax.all_to_all(grads_sent, "expert", split_axis=1, concat_axis=1, tiled=True)
    out_came = swap_cores(out_other)
    edown_grad = column_products(slot_act[None], slot_dy)[0]
    came, out_came, edown_grad, grads_came = tie(came, out_came, edown_grad, grads_came)
    sgu_out, sdown_out, dgate = (
        grads_came[: 2 * shared_cols],
        grads_came[2 * shared_cols : 3 * shared_cols],
        add_wide(grads_came[3 * shared_cols], grads_came[3 * shared_cols + 1]).T,
    )
    sgu_out = sgu_out.astype(f32).reshape(2, shared_cols, groups, block_rows)
    sgu_out = sgu_out.transpose(0, 3, 2, 1).reshape(2, block_rows, -1)
    sdown_out = sdown_out.astype(f32).swapaxes(0, 1).reshape(-1, block_rows)
    sends, slot_rows, out_came = tie(d_sum.sends_again(came), slot_rows, out_came)
    came_again = d_sum.move_again(sends)
    egu_grad = column_products(d_gate_up, slot_rows).swapaxes(1, 2)
    out_sum = RowSum(out_own, out_came)
    out_sends = out_sum.sends()
    came_again, egu_grad, out_sends = tie(came_again, egu_grad, out_sends)
    z_sends, out_sends, dgate = tie(
        line_sends(d_sum.line(came, came_again)), out_sends, dgate
    )
    z_came = line_move(z_sends)
    out_first = out_sum.move(out_sends)
    hot_mine = take_rows(
        jnp.any(routes[..., None] == jnp.arange(expert_count, dtype=jnp.int32), axis=1), own_at, half
    )
    sig = jax.nn.sigmoid(jnp.dot(hnormed_b, router_w, preferred_element_type=f32))
    chosen = jnp.where(hot_mine, sig, 0.0)
    chosen_sum = jnp.sum(chosen, axis=1, keepdims=True)
    dgate = jnp.where(hot_mine, dgate, 0.0)
    inner = jnp.sum(dgate * chosen, axis=1, keepdims=True)
    d_chosen = ROUTE_SCALE * (dgate / chosen_sum - inner / (chosen_sum * chosen_sum))
    d_logits = (jnp.where(hot_mine, d_chosen, 0.0) * sig * (1.0 - sig)).astype(bf16)
    router_grad = contract_rows(d_logits, hnormed_b)
    z_came, d_logits, router_grad, sgu_out, sdown_out = tie(
        z_came, d_logits, router_grad, sgu_out, sdown_out
    )
    d_hn = add_wide(*z_came)
    d_hn = d_hn + contract_cols(d_logits, router_w)
    d_hidden_norm, gain_two_grad = rms_backward(hidden, scale_two, gain_two.astype(f32), d_hn)
    d_hidden = dy_own_rows.astype(f32) + d_hidden_norm
    d_parts, out_first = tie(plane_gather(d_hidden.astype(bf16)), out_first)
    d_near_own = jnp.stack(d_parts)
    d_near_other = swap_cores(d_near_own)
    out_sends, d_near_other = tie(out_sum.sends_again(out_first), d_near_other)
    out_second = out_sum.move_again(out_sends)

    (
        head_grad,
        kv_grad,
        normed_part_own,
        normed_part_other,
        latent_part_own,
        latent_part_other,
    ) = attention_backward(
        core_index, d_near_own, d_near_other, kept_rows, flat_head, kv_w, *rope
    )
    kv_grad = kv_grad.reshape(groups, kv_rows, kv_parts, kv_piece).transpose(0, 2, 1, 3)
    head_sums = sum_planes(
        jnp.concatenate([head_grad, kv_grad.reshape(-1, kv_piece)], axis=1), z
    )
    grad_both = sum_heads(latent_part_own, latent_part_other)
    grad_rope = grad_both[:, rank_width : rank_width + DR] + grad_both[:, rank_width + DR :]
    out_second, grad_rope = tie(out_second, grad_rope)
    out_z = line_move(line_sends(out_sum.line(out_first, out_second)))
    latent_own = take_rows(latent[0], own_at, half)
    cosine_own = take_rows(cosine[0], own_at, half)
    sine_own = take_rows(sine_tab[0], own_at, half)
    _, scale_kv = rms_forward(latent_own[:, :rank_width], latent_g.astype(f32))
    grad_c, latent_gain_grad = rms_backward(
        latent_own[:, :rank_width], scale_kv, latent_g.astype(f32), grad_both[:, :rank_width]
    )
    grad_latent = jnp.concatenate(
        [grad_c, unrotate(grad_rope, cosine_own, sine_own)], axis=-1
    ).astype(bf16)
    head_shared = share_columns(head_sums, place)

    def by_heads(block):
        rotary = local_heads * DN
        return [
            part
            for h in range(local_heads)
            for part in (
                block[:, h * DN : (h + 1) * DN],
                block[:, rotary + h * DR : rotary + (h + 1) * DR],
            )
        ]

    at_kv = query_cols + out_cols
    w_query_grad = jnp.concatenate([v for p in head_shared for v in by_heads(p)], axis=1)
    w_query_grad = w_query_grad.astype(f32)
    w_kv_grad = jnp.concatenate(
        [
            p[q * kv_rows : (q + 1) * kv_rows, at_kv:]
            for p in head_shared
            for q in range(kv_parts)
        ],
        axis=1,
    ).astype(f32)
    w_out_grad = jnp.concatenate([p[:, query_cols:at_kv] for p in head_shared], axis=1)
    w_out_grad = w_out_grad.astype(f32).T
    grad_normed = sum_heads(normed_part_own, normed_part_other)
    grad_normed = grad_normed + contract_cols(grad_latent, latent_w)
    moe_own = add_wide(*out_z)
    mixed_own = (hidden + moe_own).astype(bf16)
    mixed = in_order(core, mixed_own, swap_cores(mixed_own))

    _, scale_own = rms_forward(x_own, gain_one.astype(f32))
    grad_x_norm, gain_one_grad = rms_backward(x_own, scale_own, gain_one.astype(f32), grad_normed)
    input_own = d_hidden + grad_x_norm
    input_grad = in_order(core, input_own, swap_cores(input_own))

    latent_near_own = jnp.stack(plane_gather(grad_latent))
    latent_near = in_order(core, latent_near_own, swap_cores(latent_near_own), axis=1)
    latent_cut = latent_cols // 2
    latent_near = latent_near.reshape(near_rows, latent_cols)
    latent_blocks = contract_rows(
        normed_cols,
        take_rows(latent_near, core * latent_cut, latent_cut, axis=1),
    )
    latent_half = deep_scatter(latent_blocks.astype(bf16).reshape(deep, -1, latent_cut), z)
    w_latent_grad = in_order(core, latent_half, swap_cores(latent_half), axis=1)

    gain_lanes = jnp.pad(
        latent_gain_grad.reshape(groups, kv_rows), ((0, 0), (0, block_rows - kv_rows))
    )
    vectors = jnp.concatenate(
        [
            router_grad,
            gain_one_grad[None],
            gain_two_grad[None],
            gain_lanes.reshape(1, -1),
        ],
        axis=0,
    ).reshape(-1, groups, block_rows)
    arrived = lax.all_to_all(vectors, "expert", split_axis=1, concat_axis=1, tiled=True)
    sums = jnp.sum(arrived, axis=1)
    sums = sums + swap_cores(sums)
    return (
        mixed,
        input_grad,
        sums[expert_count],
        w_query_grad,
        w_latent_grad,
        sums[expert_count + 2, :kv_rows],
        w_kv_grad,
        w_out_grad,
        sums[expert_count + 1],
        sums[:expert_count].T,
        sgu_out,
        sdown_out,
        egu_grad[None],
        edown_grad[None],
    )


def solution(mesh):
    groups = mesh.shape["expert"]
    plan = token_plan if groups <= 16 else weight_plan
    return jax.shard_map(
        plan,
        mesh=mesh,
        in_specs=(
            P("expert", None),
            P("expert"),
            P("expert", "tensor"),
            P("expert", None),
            P("expert"),
            P("expert", "tensor"),
            P("tensor", "expert"),
            P("expert"),
            P("expert", None),
            P(None, "expert", "tensor"),
            P("tensor", "expert"),
            P("expert", None, None, "tensor"),
            P("expert", "tensor", None),
            P("expert", None),
            P("expert", None),
            P("expert", None),
        ),
        out_specs=(
            P("expert", None),
            P("expert", None),
            P("expert"),
            P("expert", "tensor"),
            P("expert", None),
            P("expert"),
            P("expert", "tensor"),
            P("tensor", "expert"),
            P("expert"),
            P("expert", None),
            P(None, "expert", "tensor"),
            P("tensor", "expert"),
            P("expert", None, None, "tensor"),
            P("expert", "tensor", None),
        ),
        check_vma=False,
    )
```

```python
import functools

import jax
import jax.numpy as jnp
from jax import lax
from jax.experimental import pallas as pl
from jax.experimental.pallas import tpu as pltpu
from jax.sharding import PartitionSpec as P

DN = 128
DR = 64
DV = 128
LANES = 128


EPSILON = 1e-06
ROUTE_SCALE = 2.446
ROPE_BASE = 50000.0
NEGATIVE = -1e30


def cut_along(value, dim, length):
    before, after = (value.shape[:dim], value.shape[dim + 1 :])
    return jnp.moveaxis(value.reshape(*before, length, -1, *after), dim, 0)


def summed_on_arrival(value, axis, dim):
    length = lax.axis_size(axis)
    tiles = lax.all_to_all(cut_along(value, dim, length), axis, 0, 0, tiled=True)
    return jnp.sum(tiles.astype(jnp.float32), axis=0)


def sent_together(arrays, axis, dim, along):
    columns = [a.reshape(*a.shape[:along], -1) for a in arrays]
    both = jnp.concatenate(columns, axis=along)
    whole, at, outs = (summed_on_arrival(both, axis, dim), 0, [])
    for a, column in zip(arrays, columns):
        slab = whole[..., at : at + column.shape[along]]
        outs.append(slab.reshape(*slab.shape[:along], *a.shape[along:]))
        at += column.shape[along]
    return tuple(outs)


def contract_rows(left_arr, right_arr):
    return lax.dot_general(
        left_arr, right_arr, (((0,), (0,)), ((), ())), preferred_element_type=jnp.float32
    )


def contract_cols(left_arr, right_arr):
    return lax.dot_general(
        left_arr, right_arr, (((1,), (1,)), ((), ())), preferred_element_type=jnp.float32
    )


def rms_forward(rows_in, gain_vec):
    inverse = lax.rsqrt(jnp.mean(rows_in * rows_in, axis=-1, keepdims=True) + EPSILON)
    return (rows_in * inverse * gain_vec, inverse)


def rms_backward(rows_in, inverse, gain_vec, grad_out):
    gain_grad = jnp.sum(grad_out * rows_in * inverse, axis=0)
    weighted = grad_out * gain_vec
    inner_mean = jnp.mean(weighted * rows_in, axis=-1, keepdims=True)
    return (inverse * weighted - rows_in * inverse * inverse * inverse * inner_mean, gain_grad)


def doc_layout(doc_lengths, row_count):
    ends_at = jnp.cumsum(doc_lengths)
    starts_at = ends_at - doc_lengths
    position = jnp.arange(row_count, dtype=jnp.int32)
    doc_ids = jnp.sum((position[:, None] >= ends_at[None, :]).astype(jnp.int32), axis=1)
    hitting = doc_ids[:, None] == jnp.arange(doc_lengths.shape[0], dtype=jnp.int32)[None, :]
    start_of = jnp.sum(jnp.where(hitting, starts_at[None, :], 0), axis=1)
    relative = position - start_of
    visible = (doc_ids[:, None] == doc_ids[None, :]) & (position[:, None] >= position[None, :])
    return (relative, visible)


def rope_tables(relative, rot_width):
    counter = jnp.arange(rot_width // 2, dtype=jnp.float32)
    frequency = ROPE_BASE ** (-2.0 * counter / rot_width)
    angles = relative.astype(jnp.float32)[:, None] * frequency[None, :]
    return (jnp.cos(angles), jnp.sin(angles))


def rotate(tensor_in, cosine, sine_tab):
    half_width = tensor_in.shape[-1] // 2
    leading = tensor_in[..., :half_width]
    trailing = tensor_in[..., half_width:]
    return jnp.concatenate(
        [leading * cosine - trailing * sine_tab, trailing * cosine + leading * sine_tab], axis=-1
    )


def unrotate(grad_in, cosine, sine_tab):
    half_width = grad_in.shape[-1] // 2
    leading = grad_in[..., :half_width]
    trailing = grad_in[..., half_width:]
    return jnp.concatenate(
        [leading * cosine + trailing * sine_tab, trailing * cosine - leading * sine_tab], axis=-1
    )


def gated_linear_backward(gate_in, up_in, grad_act):
    sigmoid_g = jax.nn.sigmoid(gate_in)
    grad_gate = grad_act * up_in * sigmoid_g * (1.0 + gate_in * (1.0 - sigmoid_g))
    return (grad_gate, grad_act * gate_in * sigmoid_g)


def slot_tables(route_rows, expert_count, capacity):
    flat_routes = route_rows.reshape(-1)
    one_hot = (flat_routes[:, None] == jnp.arange(expert_count, dtype=jnp.int32)[None, :]).astype(
        jnp.int32
    )
    ranking = jnp.sum((jnp.cumsum(one_hot, axis=0) - one_hot) * one_hot, axis=1)
    slot_ids = flat_routes * capacity + ranking
    row_total = flat_routes.shape[0]
    source = (
        jnp.zeros((expert_count * capacity,), jnp.int32)
        .at[slot_ids]
        .set(jnp.arange(row_total, dtype=jnp.int32))
    )
    filled = jnp.zeros((expert_count * capacity,), jnp.int32).at[slot_ids].set(1)
    return (slot_ids, source, filled)


def to_owner(rows_in):
    arrived = lax.all_to_all(rows_in, "expert", split_axis=0, concat_axis=1, tiled=True)
    return arrived


def weight_plan(
    inputs,
    attn_gain,
    w_query,
    w_latent,
    latent_gain,
    w_kv,
    w_out,
    ffn_gain,
    w_router,
    shared_gate_up,
    shared_down,
    expert_gate_up,
    expert_down,
    lengths,
    routes,
    cotangent,
):
    tok_rows = inputs.shape[0]
    model_width = inputs.shape[1]
    expert_count = w_router.shape[1]
    route_count = routes.shape[1]
    capacity = tok_rows * route_count * 4 // (3 * expert_count)
    brain_float16 = jnp.bfloat16
    f32 = jnp.float32
    gathered = (
        lax.all_gather(attn_gain, "expert", axis=0, tiled=True),
        lax.all_gather(w_query, "expert", axis=0, tiled=True),
        lax.all_gather(w_latent, "expert", axis=0, tiled=True),
        lax.all_gather(latent_gain, "expert", axis=0, tiled=True),
        lax.all_gather(w_kv, "expert", axis=0, tiled=True),
        lax.all_gather(w_out, "expert", axis=1, tiled=True),
        lax.all_gather(ffn_gain, "expert", axis=0, tiled=True),
        lax.all_gather(w_router, "expert", axis=0, tiled=True),
        lax.all_gather(shared_gate_up, "expert", axis=1, tiled=True),
        lax.all_gather(shared_down, "expert", axis=1, tiled=True),
    )
    gain_one, query_w, latent_w, latent_g, kv_w, out_w, gain_two, router_w, sgate_up, sdown_w = (
        gathered
    )
    local_heads = query_w.shape[1] // (DN + DR)
    rank_width = latent_g.shape[0]
    x_float = inputs.astype(f32)
    relative, visible = doc_layout(lengths[0], tok_rows)
    cosine, sine_tab = rope_tables(relative, DR)
    q_scale = (DN + DR) ** (-0.5)
    normed, scale_one = rms_forward(x_float, gain_one.astype(f32))
    normed_b = normed.astype(brain_float16)
    queries = jnp.dot(normed_b, query_w, preferred_element_type=f32).reshape(
        tok_rows, local_heads, DN + DR
    )
    q_rot = rotate(queries[..., DN:], cosine[:, None, :], sine_tab[:, None, :])
    q_all = jnp.concatenate([queries[..., :DN], q_rot], axis=-1).astype(brain_float16)
    latent = jnp.dot(normed_b, latent_w, preferred_element_type=f32)
    compressed, scale_kv = rms_forward(latent[:, :rank_width], latent_g.astype(f32))
    compressed_b = compressed.astype(brain_float16)
    k_rope = rotate(latent[:, rank_width:], cosine, sine_tab).astype(brain_float16)
    kv_all = jnp.dot(compressed_b, kv_w, preferred_element_type=f32).reshape(
        tok_rows, local_heads, DN + DV
    )
    k_nope = kv_all[..., :DN].astype(brain_float16)
    values = kv_all[..., DN:].astype(brain_float16)
    key_all = jnp.concatenate(
        [k_nope, jnp.broadcast_to(k_rope[:, None, :], (tok_rows, local_heads, DR))], axis=-1
    )

    def score_block():
        raw_scores = (
            jnp.einsum("qhd,khd->hqk", q_all, key_all, preferred_element_type=f32) * q_scale
        )
        return jnp.where(visible[None], raw_scores, NEGATIVE)

    scores = score_block()
    top_score = jnp.max(scores, axis=-1, keepdims=True)
    log_total = top_score + jnp.log(jnp.sum(jnp.exp(scores - top_score), axis=-1, keepdims=True))
    probs_b = jnp.exp(scores - log_total).astype(brain_float16)
    attended = jnp.einsum("hqk,khd->qhd", probs_b, values, preferred_element_type=f32)
    attended_b = attended.reshape(tok_rows, local_heads * DV).astype(brain_float16)
    attn = lax.psum(jnp.dot(attended_b, out_w, preferred_element_type=f32), "tensor")
    hidden = x_float + attn
    hnormed, scale_two = rms_forward(hidden, gain_two.astype(f32))
    hnormed_b = hnormed.astype(brain_float16)
    logits = jnp.dot(hnormed_b, router_w, preferred_element_type=f32)
    sigmoid_vals = jax.nn.sigmoid(logits)
    route_hot = routes[:, :, None] == jnp.arange(expert_count, dtype=jnp.int32)[None, None, :]
    chosen = jnp.sum(jnp.where(route_hot, sigmoid_vals[:, None, :], 0.0), axis=2)
    chosen_sum = jnp.sum(chosen, axis=1, keepdims=True)
    gate_vals = ROUTE_SCALE * chosen / chosen_sum
    slot_ids, source, filled = slot_tables(routes, expert_count, capacity)
    is_filled = filled[:, None] == 1
    sent_rows = jnp.where(is_filled, hnormed_b[source // route_count], 0).reshape(
        expert_count, capacity, model_width
    )
    received = to_owner(sent_rows)
    gate_up_joined = jnp.einsum(
        "erd,egdf->egrf", received, expert_gate_up, preferred_element_type=f32
    )
    expert_act = (jax.nn.silu(gate_up_joined[:, 0]) * gate_up_joined[:, 1]).astype(brain_float16)
    expert_res = jnp.einsum(
        "erf,efd->erd", expert_act, expert_down, preferred_element_type=f32
    ).astype(brain_float16)
    returned_all = lax.all_to_all(expert_res, "expert", split_axis=1, concat_axis=0, tiled=True)
    returned = returned_all.reshape(expert_count * capacity, model_width)[slot_ids].reshape(
        tok_rows, route_count, model_width
    )
    shared_gu = jnp.einsum("td,gdf->gtf", hnormed_b, sgate_up, preferred_element_type=f32)
    shared_act = (jax.nn.silu(shared_gu[0]) * shared_gu[1]).astype(brain_float16)
    branch_sum = jnp.dot(shared_act, sdown_w, preferred_element_type=f32)
    for route_idx in range(route_count):
        branch_sum = branch_sum + gate_vals[:, route_idx : route_idx + 1] * returned[
            :, route_idx
        ].astype(f32)
    moe_out = lax.psum(branch_sum.astype(jnp.bfloat16), "tensor").astype(jnp.float32)
    mixed = (hidden + moe_out).astype(brain_float16)
    grad_y = cotangent.astype(f32)
    sdown_grad = contract_rows(shared_act, cotangent)
    grad_sact = contract_cols(cotangent, sdown_w)
    grad_sgate, grad_sup = gated_linear_backward(shared_gu[0], shared_gu[1], grad_sact)
    grad_sgu = jnp.stack([grad_sgate, grad_sup], axis=0).astype(brain_float16)
    sgu_grad = jnp.einsum("td,gtf->gdf", hnormed_b, grad_sgu, preferred_element_type=f32)
    grad_hn_part = jnp.einsum("gtf,gdf->td", grad_sgu, sgate_up, preferred_element_type=f32)
    gate_columns = []
    for route_idx in range(route_count):
        gate_columns.append(jnp.sum(grad_y * returned[:, route_idx].astype(f32), axis=1))
    gate_part = jnp.stack(gate_columns, axis=1)
    slot_grads = (
        (gate_vals[:, :, None] * grad_y[:, None, :])
        .reshape(tok_rows * route_count, model_width)
        .astype(brain_float16)
    )
    grad_sent = jnp.where(is_filled, slot_grads[source], 0).reshape(
        expert_count, capacity, model_width
    )
    grad_received = to_owner(grad_sent)
    edown_grad = jnp.einsum("erf,erd->efd", expert_act, grad_received, preferred_element_type=f32)
    expert_activation_gradient = jnp.einsum(
        "erd,efd->erf", grad_received, expert_down, preferred_element_type=f32
    )
    expert_gate_gradient, expert_up_gradient = gated_linear_backward(
        gate_up_joined[:, 0], gate_up_joined[:, 1], expert_activation_gradient
    )
    expert_gate_up_gradient = jnp.stack([expert_gate_gradient, expert_up_gradient], axis=1).astype(
        brain_float16
    )
    egu_grad = jnp.einsum(
        "erd,egrf->egdf", received, expert_gate_up_gradient, preferred_element_type=f32
    )
    grad_rows = jnp.einsum(
        "egrf,egdf->erd", expert_gate_up_gradient, expert_gate_up, preferred_element_type=f32
    ).astype(brain_float16)
    grad_back = lax.all_to_all(grad_rows, "expert", split_axis=1, concat_axis=0, tiled=True)
    grad_routes = grad_back.reshape(expert_count * capacity, model_width)[slot_ids].reshape(
        tok_rows, route_count, model_width
    )
    for route_idx in range(route_count):
        grad_hn_part = grad_hn_part + grad_routes[:, route_idx].astype(f32)
    gate_grads = lax.psum(gate_part, "tensor")
    grad_chosen = ROUTE_SCALE * (
        gate_grads / chosen_sum
        - jnp.sum(gate_grads * chosen, axis=1, keepdims=True) / (chosen_sum * chosen_sum)
    )
    grad_sig = jnp.sum(jnp.where(route_hot, grad_chosen[:, :, None], 0.0), axis=1)
    grad_logits = (grad_sig * sigmoid_vals * (1.0 - sigmoid_vals)).astype(brain_float16)
    router_grad = contract_rows(hnormed_b, grad_logits)
    grad_hn = lax.psum(grad_hn_part, "tensor") + contract_cols(grad_logits, router_w)
    grad_hidden_norm, gain_two_grad = rms_backward(hidden, scale_two, gain_two.astype(f32), grad_hn)
    grad_hidden = grad_y + grad_hidden_norm
    grad_hidden_b = grad_hidden.astype(brain_float16)
    out_grad = contract_rows(attended_b, grad_hidden_b)
    grad_att = (
        contract_cols(grad_hidden_b, out_w).reshape(tok_rows, local_heads, DV).astype(brain_float16)
    )
    probs = jnp.exp(score_block() - log_total)
    probs_again = probs.astype(brain_float16)
    grad_probs = jnp.einsum("qhd,khd->hqk", grad_att, values, preferred_element_type=f32)
    grad_vals = jnp.einsum("hqk,qhd->khd", probs_again, grad_att, preferred_element_type=f32)
    row_delta = jnp.sum(probs * grad_probs, axis=-1, keepdims=True)
    grad_scores = (probs * (grad_probs - row_delta)).astype(brain_float16)
    grad_q = jnp.einsum("hqk,khd->qhd", grad_scores, key_all, preferred_element_type=f32) * q_scale
    grad_keys = jnp.einsum("hqk,qhd->khd", grad_scores, q_all, preferred_element_type=f32) * q_scale
    grad_kv = (
        jnp.concatenate([grad_keys[..., :DN], grad_vals], axis=-1)
        .reshape(tok_rows, local_heads * (DN + DV))
        .astype(brain_float16)
    )
    kv_grad = contract_rows(compressed_b, grad_kv)
    grad_comp_part = contract_cols(grad_kv, kv_w)
    grad_krope_part = jnp.sum(grad_keys[..., DN:], axis=1)
    grad_comp, grad_krope = (
        lax.psum(grad_comp_part.astype(jnp.bfloat16), "tensor").astype(jnp.float32),
        lax.psum(grad_krope_part.astype(jnp.bfloat16), "tensor").astype(jnp.float32),
    )
    grad_c, latent_gain_grad = rms_backward(
        latent[:, :rank_width], scale_kv, latent_g.astype(f32), grad_comp
    )
    grad_latent = jnp.concatenate([grad_c, unrotate(grad_krope, cosine, sine_tab)], axis=-1).astype(
        brain_float16
    )
    grad_qrot = unrotate(grad_q[..., DN:], cosine[:, None, :], sine_tab[:, None, :])
    grad_queries = (
        jnp.concatenate([grad_q[..., :DN], grad_qrot], axis=-1)
        .reshape(tok_rows, local_heads * (DN + DR))
        .astype(brain_float16)
    )
    query_grad = contract_rows(normed_b, grad_queries)
    latent_grad = contract_rows(normed_b, grad_latent)
    grad_normed = lax.psum(
        contract_cols(grad_queries, query_w).astype(jnp.bfloat16), "tensor"
    ).astype(jnp.float32) + contract_cols(grad_latent, latent_w)
    grad_x_norm, gain_one_grad = rms_backward(x_float, scale_one, gain_one.astype(f32), grad_normed)
    input_grad = grad_hidden + grad_x_norm
    first_owned = (
        *sent_together(
            (
                gain_one_grad.astype(jnp.bfloat16),
                query_grad.astype(jnp.bfloat16),
                latent_grad.astype(jnp.bfloat16),
            ),
            "expert",
            0,
            1,
        ),
        *sent_together(
            (latent_gain_grad.astype(jnp.bfloat16), kv_grad.astype(jnp.bfloat16)), "expert", 0, 1
        ),
    )
    second_owned = (
        lax.psum_scatter(out_grad, "expert", scatter_dimension=1, tiled=True),
        lax.psum_scatter(gain_two_grad, "expert", scatter_dimension=0, tiled=True),
        lax.psum_scatter(router_grad, "expert", scatter_dimension=0, tiled=True),
        lax.psum_scatter(sgu_grad, "expert", scatter_dimension=1, tiled=True),
        lax.psum_scatter(sdown_grad, "expert", scatter_dimension=1, tiled=True),
    )
    return (
        mixed,
        input_grad,
        first_owned[0],
        first_owned[1],
        first_owned[2],
        first_owned[3],
        first_owned[4],
        second_owned[0],
        second_owned[1],
        second_owned[2],
        second_owned[3],
        second_owned[4],
        egu_grad,
        edown_grad,
    )


def swap_cores(value):
    return lax.ppermute(value, "tensor", [(0, 1), (1, 0)])


def take_rows(value, start, count, axis=0):
    return lax.dynamic_slice_in_dim(value, start, count, axis=axis)


def in_order(core, own, other, axis=0):
    return jnp.where(
        core == 0,
        jnp.concatenate([own, other], axis=axis),
        jnp.concatenate([other, own], axis=axis),
    )


def add_wide(*parts):
    total = parts[0].astype(jnp.float32)
    for part in parts[1:]:
        total = total + part.astype(jnp.float32)
    return total


PLANE = 4


def to_partner(value, flips):
    groups = lax.axis_size("expert")
    return lax.ppermute(value, "expert", [(g, g ^ flips) for g in range(groups)])


def to_deeper(value, step):
    groups = lax.axis_size("expert")
    pairs = [(g, (g + step * PLANE) % groups) for g in range(groups)]
    return lax.ppermute(value, "expert", pairs)


def plane_gather(value):
    return [value] + [to_partner(value, r) for r in range(1, PLANE)]


def plane_scatter(parts):
    return add_wide(parts[0], *[to_partner(parts[r], r) for r in range(1, PLANE)])


def by_place(parts, place):
    odd, high = place % 2 == 1, place // 2 == 1
    parts = [jnp.where(odd, parts[i ^ 1], parts[i]) for i in range(PLANE)]
    return [jnp.where(high, parts[i ^ 2], parts[i]) for i in range(PLANE)]


def tie(*values):
    return lax.optimization_barrier(values)


def deep_pieces(value):
    deep = lax.axis_size("expert") // PLANE
    return [to_deeper(value, s) for s in range(1, deep)]


def one_plane(value, step):
    groups = lax.axis_size("expert")
    pairs = [(g, g + step * PLANE) for g in range(groups) if 0 <= g + step * PLANE < groups]
    return lax.ppermute(value, "expert", pairs)


def deep_hops(value):
    deep = lax.axis_size("expert") // PLANE
    after, before, down, up = [], [], value, value
    for _ in range(1, deep):
        down, up = one_plane(down, 1), one_plane(up, -1)
        after.append(down)
        before.append(up)
    return after, before


def join_hops(hops):
    after, before = hops
    return [a + b for a, b in zip(after, before[::-1])]


def deep_join(value, pieces, z):
    deep = lax.axis_size("expert") // PLANE
    whole = jnp.zeros((deep, *value.shape), value.dtype)
    whole = lax.dynamic_update_index_in_dim(whole, value, z, 0)
    for step in range(1, deep):
        whole = lax.dynamic_update_index_in_dim(whole, pieces[step - 1], (z - step) % deep, 0)
    return whole


def deep_move(blocks, z):
    deep = blocks.shape[0]

    def block(index):
        return lax.dynamic_index_in_dim(blocks, index, 0, keepdims=False)

    return [block(z)] + [to_deeper(block((z + step) % deep), step) for step in range(1, deep)]


def deep_scatter(blocks, z):
    return add_wide(*deep_move(blocks, z))


def share_columns(rows, place):
    parts = [at_index(rows, 0, place)]
    for r in range(1, PLANE):
        parts.append(to_partner(at_index(rows, 0, place ^ r), r))
    return by_place(parts, place)


def all_groups(value):
    return lax.all_gather(value, "expert", axis=0, tiled=False)


def at_index(value, axis, index):
    return lax.dynamic_index_in_dim(value, index, axis, keepdims=False)


def doc_places(doc_lengths, row_count):
    ends_at = jnp.cumsum(doc_lengths)
    position = jnp.arange(row_count, dtype=jnp.int32)
    doc_ids = jnp.sum((position[:, None] >= ends_at[None, :]).astype(jnp.int32), axis=1)
    hitting = doc_ids[:, None] == jnp.arange(doc_lengths.shape[0], dtype=jnp.int32)[None, :]
    start_of = jnp.sum(jnp.where(hitting, (ends_at - doc_lengths)[None, :], 0), axis=1)
    return position - start_of, doc_ids


class RowGather:
    def __init__(self, value):
        self.cut = value.shape[0] // 2
        self.value = value

    def along(self):
        return [self.value] + deep_pieces(self.value)

    def lines(self, came):
        return [jnp.stack([v[: self.cut] for v in came]), jnp.stack([v[self.cut :] for v in came])]

    def over(self, lines):
        first, second = lines
        return to_partner(first, 1), to_partner(second, 2)

    def over_again(self, lines, came):
        (first, second), (beside, behind) = lines, came
        return [
            [first, beside, to_partner(first, 2), to_partner(beside, 2)],
            [second, to_partner(second, 1), behind, to_partner(behind, 1)],
        ]

    def whole(self, halves):
        return jnp.concatenate([jnp.concatenate(half, axis=0) for half in halves], axis=1)


class RowSum:
    def __init__(self, *terms):
        groups, rows = terms[0].shape[:2]
        self.type = terms[0].dtype
        cut = rows // 2
        blocks = [v.reshape(PLANE, groups // PLANE, *v.shape[1:]) for v in terms]
        self.halves = (
            ([v[:, :, :cut] for v in blocks], 2, 1),
            ([v[:, :, cut:] for v in blocks], 1, 2),
        )

    def _add(self, parts):
        return add_wide(*parts).astype(self.type)

    def sends(self):
        return [
            jnp.stack([self._add([v[far] for v in held]), self._add([v[far | near] for v in held])])
            for held, far, near in self.halves
        ]

    def move(self, sends):
        return [to_partner(v, far) for v, (_, far, _) in zip(sends, self.halves)]

    def sends_again(self, came):
        return [
            self._add([v[near] for v in held] + [c[1]])
            for c, (held, _, near) in zip(came, self.halves)
        ]

    def move_again(self, sends):
        return [to_partner(v, near) for v, (_, _, near) in zip(sends, self.halves)]

    def line(self, came, came_again):
        sums = [
            self._add([v[0] for v in held] + [c[0], d])
            for c, d, (held, *_) in zip(came, came_again, self.halves)
        ]
        return jnp.concatenate(sums, axis=1)


def line_sends(line):
    return [line[step] for step in range(line.shape[0])]


def line_move(sends):
    return [sends[0]] + [to_deeper(v, -step) for step, v in enumerate(sends) if step > 0]


def dot_nn(left, right):
    return lax.dot_general(left, right, (((1,), (0,)), ((), ())), preferred_element_type=jnp.float32)


def dot_nt(left, right):
    return lax.dot_general(left, right, (((1,), (1,)), ((), ())), preferred_element_type=jnp.float32)


def dot_tn(left, right):
    return lax.dot_general(left, right, (((0,), (0,)), ((), ())), preferred_element_type=jnp.float32)


def two_lanes(column, lane):
    high = column.astype(jnp.bfloat16).astype(jnp.float32)
    spread = jnp.where(lane == 0, high, jnp.where(lane == 1, column - high, 0.0))
    return spread.astype(jnp.bfloat16)


def expert_kernel(
    shared_cols,
    expert_count,
    me_ref,
    hn_own,
    hn_other,
    dy_own,
    dy_other,
    meta_own,
    meta_other,
    gate_up_w,
    down_w,
    first_w,
    sdown_w,
    slots_out,
    slot_dy_out,
    act_out,
    d_gate_up_out,
    rows_own_out,
    rows_other_out,
    sact_own_out,
    sact_other_out,
    shared_grads_out,
    dgate_own_out,
    dgate_other_out,
):
    f32, bf16 = jnp.float32, jnp.bfloat16
    count, half, _ = hn_own.shape
    tokens = 2 * half
    me = me_ref[0]
    lane = lax.broadcasted_iota(jnp.int32, (count * tokens, LANES), 1)
    is_router = (lane >= shared_cols) & (lane < shared_cols + expert_count)
    first = first_w[...]

    def joined(own, other):
        return jnp.concatenate([v[i] for i in range(count) for v in (own, other)], axis=0)

    rows, rows_dy = joined(hn_own, hn_other), joined(dy_own, dy_other)
    meta = joined(meta_own, meta_other)
    products = dot_nt(rows, first)
    gate, up = products[:, :LANES], products[:, LANES:]
    sig = jax.nn.sigmoid(gate)
    total = jnp.sum(jnp.where(is_router, sig * meta, 0.0), axis=1, keepdims=True)
    mine = jnp.sum(jnp.where(lane == shared_cols + me, sig, 0.0), axis=1, keepdims=True)
    token_gate = two_lanes(ROUTE_SCALE * mine / total, lane)
    sact = (gate * sig * up).astype(bf16)
    d_sact = dot_nt(rows_dy, sdown_w[...])
    d_sgate = d_sact * up * sig * (1.0 + gate * (1.0 - sig))
    dsh = jnp.concatenate([d_sgate, d_sact * gate * sig], axis=1).astype(bf16)
    pick = (meta[:, :1] == lane.astype(f32)).astype(bf16)
    groups = [slice(i * tokens, (i + 1) * tokens) for i in range(count)]
    for i in range(count):
        start = i * tokens
        sact_own_out[i] = sact[start : start + half]
        sact_other_out[i] = sact[start + half : start + tokens]
    slots = [dot_tn(pick[g], rows[g]).astype(bf16) for g in groups]
    slot_dys = [dot_tn(pick[g], rows_dy[g]).astype(bf16) for g in groups]
    slot_gates = [
        jnp.sum(dot_tn(pick[g], token_gate[g]), axis=1, keepdims=True) for g in groups
    ]

    @pl.when(pl.program_id(0) == 0)
    def _():
        shared_grads_out[...] = jnp.zeros_like(shared_grads_out)

    first_grad, sdown_grad = dot_tn(dsh, rows), dot_tn(sact, rows_dy)
    shared_grads_out[:shared_cols] += first_grad[:shared_cols]
    shared_grads_out[shared_cols : 2 * shared_cols] += first_grad[LANES : LANES + shared_cols]
    shared_grads_out[2 * shared_cols :] += sdown_grad[:shared_cols]
    slot_rows = jnp.concatenate(slots, axis=0)
    slot_dy = jnp.concatenate(slot_dys, axis=0)
    slot_gate = jnp.concatenate(slot_gates, axis=0)
    slots_out[...] = slot_rows
    slot_dy_out[...] = slot_dy
    gate = dot_nt(slot_rows, gate_up_w[0])
    up = dot_nt(slot_rows, gate_up_w[1])
    d_act = dot_nt(slot_dy, down_w[...])
    sig = jax.nn.sigmoid(gate)
    silu = gate * sig
    act = silu * up
    slot_dgate = jnp.sum(act * d_act, axis=1, keepdims=True)
    act_out[...] = (slot_gate * act).astype(bf16)
    d_act = slot_gate * d_act
    d_gate = (d_act * up * sig * (1.0 + gate * (1.0 - sig))).astype(bf16)
    d_up = (d_act * silu).astype(bf16)
    d_gate_up_out[0] = d_gate
    d_gate_up_out[1] = d_up
    d_slots = (dot_nn(d_gate, gate_up_w[0]) + dot_nn(d_up, gate_up_w[1])).astype(bf16)
    slot_lane = lax.broadcasted_iota(jnp.int32, (LANES, LANES), 1)
    d_shared = dot_nn(dsh, first)
    for i, g in enumerate(groups):
        here = slice(i * LANES, (i + 1) * LANES)
        d_rows = (dot_nn(pick[g], d_slots[here]) + d_shared[g]).astype(bf16)
        rows_own_out[i], rows_other_out[i] = d_rows[:half], d_rows[half:]
        dgate = dot_nn(pick[g], two_lanes(slot_dgate[here], slot_lane))
        dgate_own_out[i], dgate_other_out[i] = dgate[:half], dgate[half:]


def block_specs(per_step):
    def lead(*tail):
        return pl.BlockSpec((per_step, *tail), lambda i: (i,) + (0,) * len(tail))

    def flat(cols):
        return pl.BlockSpec((per_step * LANES, cols), lambda i: (i, 0))

    def whole(a):
        return pl.BlockSpec(a.shape, lambda i: (0,) * a.ndim, pipeline_mode=pl.Buffered(1))

    return lead, flat, whole


def slots_cost(width, hidden, products):
    return LANES * width * hidden * products


def experts(
    me,
    hn_own,
    hn_other,
    dy_own,
    dy_other,
    meta_own,
    meta_other,
    gate_up_w,
    down_w,
    first_w,
    sdown_w,
    shared_cols,
    expert_count,
    per_step=2,
):
    groups, half, width = hn_own.shape
    hidden = down_w.shape[0]
    slots = groups * LANES
    f32, bf16 = jnp.float32, jnp.bfloat16
    lead, flat, whole = block_specs(per_step)
    sds = jax.ShapeDtypeStruct
    rows_cost = 2 * groups * (2 * half * width * 4 * LANES + slots_cost(width, hidden, 5))
    return pl.pallas_call(
        functools.partial(expert_kernel, shared_cols, expert_count),
        grid=(groups // per_step,),
        in_specs=[
            pl.BlockSpec(memory_space=pltpu.SMEM),
            *[lead(half, width)] * 4,
            *[lead(half, LANES)] * 2,
            *[whole(a) for a in (gate_up_w, down_w, first_w, sdown_w)],
        ],
        out_specs=[
            flat(width),
            flat(width),
            flat(hidden),
            pl.BlockSpec((2, per_step * LANES, hidden), lambda i: (0, i, 0)),
            *[lead(half, width)] * 2,
            *[lead(half, LANES)] * 2,
            pl.BlockSpec((3 * shared_cols, width), lambda i: (0, 0)),
            *[lead(half, LANES)] * 2,
        ],
        out_shape=[
            sds((slots, width), bf16),
            sds((slots, width), bf16),
            sds((slots, hidden), bf16),
            sds((2, slots, hidden), bf16),
            *[sds((groups, half, width), bf16)] * 2,
            *[sds((groups, half, LANES), bf16)] * 2,
            sds((3 * shared_cols, width), f32),
            *[sds((groups, half, LANES), f32)] * 2,
        ],
        compiler_params=pltpu.CompilerParams(vmem_limit_bytes=58 * 1024 * 1024),
        cost_estimate=pl.CostEstimate(
            flops=rows_cost, bytes_accessed=20 * groups * half * width, transcendentals=0
        ),
    )(
        me,
        hn_own,
        hn_other,
        dy_own,
        dy_other,
        meta_own,
        meta_other,
        gate_up_w,
        down_w,
        first_w,
        sdown_w,
    )


def swap_halves(value, lane):
    low = lane % DR < DR // 2
    return jnp.where(low, pltpu.roll(value, LANES - DR // 2, 1), pltpu.roll(value, DR // 2, 1))


def by_core(core, first, second):
    return jnp.where(core == 0, first, second), jnp.where(core == 0, second, first)


def head_scores(q, kv, k_rope, visible, lane, head, heads):
    q_nope = q[:, head * DN : (head + 1) * DN]
    q_rope = jnp.where(lane // DR == head, q[:, heads * DN :], jnp.zeros((), q.dtype))
    at = head * (DN + DV)
    k_nope, value = kv[:, at : at + DN], kv[:, at + DN : at + DN + DV]
    scores = (dot_nt(q_nope, k_nope) + dot_nt(q_rope, k_rope)) * (DN + DR) ** -0.5
    return jnp.where(visible, scores, NEGATIVE), q_nope, q_rope, k_nope, value


def seen(doc_col, doc_row):
    rows = doc_col.shape[0]
    later = lax.broadcasted_iota(jnp.int32, (rows, rows), 0) >= lax.broadcasted_iota(
        jnp.int32, (rows, rows), 1
    )
    return (doc_col == doc_row) & later


def attention_kernel(
    heads,
    rank,
    core_ref,
    x_own,
    x_other,
    gain,
    latent_gain,
    head_w,
    small_w,
    kv_w,
    cosine,
    sine,
    doc_col,
    doc_row,
    normed_out,
    compressed_out,
    q_out,
    kv_out,
    k_rope_out,
    sums_out,
    attended_out,
    latent_out,
    part_own_out,
    part_other_out,
):
    f32, bf16 = jnp.float32, jnp.bfloat16
    core = core_ref[0]
    x = jnp.concatenate(by_core(core, x_own[0], x_other[0]), axis=0).astype(f32)
    rows = x.shape[0]
    half = rows // 2
    lane = lax.broadcasted_iota(jnp.int32, (rows, LANES), 1)
    inverse = lax.rsqrt(jnp.mean(x * x, axis=1, keepdims=True) + EPSILON)
    normed = (x * inverse * gain[...]).astype(bf16)
    normed_out[0] = normed
    q_cols = heads * (DN + DR)
    queries = dot_nn(normed, head_w[:, :q_cols])
    q_rope = queries[:, heads * DN :]
    q_rope = q_rope * cosine[0] + swap_halves(q_rope, lane) * sine[0]
    q = jnp.concatenate([queries[:, : heads * DN], q_rope], axis=1).astype(bf16)
    q_out[0] = q
    latent = dot_nn(normed, small_w[:, : rank + LANES])
    latent_out[0] = latent
    squeezed = latent[:, :rank]
    inverse = lax.rsqrt(jnp.mean(squeezed * squeezed, axis=1, keepdims=True) + EPSILON)
    compressed = (squeezed * inverse * latent_gain[...]).astype(bf16)
    compressed_out[0] = compressed
    k_rope = latent[:, rank:]
    k_rope = (k_rope * cosine[0] + swap_halves(k_rope, lane) * sine[0]).astype(bf16)
    k_rope_out[0] = k_rope
    kv = dot_nn(compressed, kv_w[...]).astype(bf16)
    kv_out[0] = kv
    visible = seen(doc_col[0], doc_row[0])
    attended, sums = [], jnp.zeros((rows, LANES), f32)
    for head in range(heads):
        scores, *_, value = head_scores(q, kv, k_rope, visible, lane, head, heads)
        top = jnp.max(scores, axis=1, keepdims=True)
        log_total = top + jnp.log(jnp.sum(jnp.exp(scores - top), axis=1, keepdims=True))
        sums = jnp.where(lane == head, log_total, sums)
        probs = jnp.exp(scores - log_total).astype(bf16)
        attended.append(dot_nn(probs, value).astype(bf16))
    sums_out[0] = sums
    attended = jnp.concatenate(attended, axis=1)
    attended_out[0] = attended
    part = dot_nt(attended, head_w[:, q_cols : q_cols + heads * DV]).astype(bf16)
    part_own_out[0], part_other_out[0] = by_core(core, part[:half], part[half:])


def attention_backward_kernel(
    heads,
    core_ref,
    d_own,
    d_other,
    normed_ref,
    compressed_ref,
    q_ref,
    kv_ref,
    k_rope_ref,
    sums_ref,
    attended_ref,
    head_w,
    kv_w,
    cosine,
    sine,
    doc_col,
    doc_row,
    head_grad_out,
    kv_grad_out,
    normed_own_out,
    normed_other_out,
    latent_own_out,
    latent_other_out,
    head_acc,
    kv_acc,
):
    f32, bf16 = jnp.float32, jnp.bfloat16
    core, step = core_ref[0], pl.program_id(0)
    scale = (DN + DR) ** -0.5
    d_rows = jnp.concatenate(by_core(core, d_own[0], d_other[0]), axis=0)
    rows = d_rows.shape[0]
    half = rows // 2
    lane = lax.broadcasted_iota(jnp.int32, (rows, LANES), 1)
    q_cols = heads * (DN + DR)
    q, kv, k_rope = q_ref[0], kv_ref[0], k_rope_ref[0]
    d_attended = dot_nn(d_rows, head_w[:, q_cols : q_cols + heads * DV]).astype(bf16)
    visible = seen(doc_col[0], doc_row[0])
    d_q, d_kv = [], []
    d_q_rope, d_k_rope = jnp.zeros((rows, LANES), f32), jnp.zeros((rows, LANES), f32)
    for head in range(heads):
        scores, q_nope, q_rope, k_nope, value = head_scores(
            q, kv, k_rope, visible, lane, head, heads
        )
        probs = jnp.exp(scores - sums_ref[0][:, head : head + 1])
        d_head = d_attended[:, head * DV : (head + 1) * DV]
        d_probs = dot_nt(d_head, value)
        d_value = dot_tn(probs.astype(bf16), d_head)
        delta = jnp.sum(probs * d_probs, axis=1, keepdims=True)
        d_scores = (probs * (d_probs - delta)).astype(bf16)
        d_q.append(dot_nn(d_scores, k_nope) * scale)
        d_q_rope = jnp.where(lane // DR == head, dot_nn(d_scores, k_rope) * scale, d_q_rope)
        d_kv += [dot_tn(d_scores, q_nope) * scale, d_value]
        d_k_rope += dot_tn(d_scores, q_rope) * scale
    d_q_rope = d_q_rope * cosine[0] - swap_halves(d_q_rope, lane) * sine[0]
    d_q = jnp.concatenate(d_q + [d_q_rope], axis=1).astype(bf16)
    d_kv = jnp.concatenate(d_kv, axis=1).astype(bf16)

    @pl.when(step == 0)
    def _():
        head_acc[...] = jnp.zeros_like(head_acc)
        kv_acc[...] = jnp.zeros_like(kv_acc)

    head_acc[:, :q_cols] += dot_tn(normed_ref[0], d_q)
    head_acc[:, q_cols:] += dot_tn(d_rows, attended_ref[0])
    kv_acc[...] += dot_tn(compressed_ref[0], d_kv)

    @pl.when(step == pl.num_programs(0) - 1)
    def _():
        head_grad_out[...] = head_acc[...].astype(bf16)
        kv_grad_out[...] = kv_acc[...].astype(bf16)

    part = dot_nt(d_q, head_w[:, :q_cols]).astype(bf16)
    normed_own_out[0], normed_other_out[0] = by_core(core, part[:half], part[half:])
    latent = jnp.concatenate([dot_nt(d_kv, kv_w[...]), d_k_rope], axis=1).astype(bf16)
    latent_own_out[0], latent_other_out[0] = by_core(core, latent[:half], latent[half:])


def one_each(*tail):
    return pl.BlockSpec((1, *tail), lambda i: (i,) + (0,) * len(tail))


def kept(value):
    return pl.BlockSpec(value.shape, lambda i: (0,) * value.ndim, pipeline_mode=pl.Buffered(1))


def attention(core, x_own, x_other, gain, latent_gain, head_w, small_w, kv_w, cosine, sine, doc):
    near, half, width = x_own.shape
    rows = 2 * half
    rank, kv_cols = kv_w.shape
    heads = kv_cols // (DN + DV)
    f32, bf16 = jnp.float32, jnp.bfloat16
    shapes = [
        ((rows, width), bf16),
        ((rows, rank), bf16),
        ((rows, heads * (DN + DR)), bf16),
        ((rows, kv_cols), bf16),
        ((rows, LANES), bf16),
        ((rows, LANES), f32),
        ((rows, heads * DV), bf16),
        ((rows, rank + LANES), f32),
        ((half, width), bf16),
        ((half, width), bf16),
    ]
    return pl.pallas_call(
        functools.partial(attention_kernel, heads, rank),
        grid=(near,),
        in_specs=[
            pl.BlockSpec(memory_space=pltpu.SMEM),
            *[one_each(half, width)] * 2,
            *[kept(a) for a in (gain, latent_gain, head_w, small_w, kv_w)],
            *[one_each(rows, LANES)] * 2,
            one_each(rows, 1),
            one_each(1, rows),
        ],
        out_specs=[one_each(*shape) for shape, _ in shapes],
        out_shape=[jax.ShapeDtypeStruct((near, *shape), kind) for shape, kind in shapes],
        compiler_params=pltpu.CompilerParams(vmem_limit_bytes=58 * 1024 * 1024),
        cost_estimate=pl.CostEstimate(
            flops=2 * near * rows * width * (rank + 3 * heads * DN),
            bytes_accessed=4 * near * rows * width,
            transcendentals=0,
        ),
    )(
        core,
        x_own,
        x_other,
        gain,
        latent_gain,
        head_w,
        small_w,
        kv_w,
        cosine,
        sine,
        doc[:, :, None],
        doc[:, None, :],
    )


def attention_backward(core, d_own, d_other, kept_rows, head_w, kv_w, cosine, sine, doc):
    near, half, width = d_own.shape
    rows = 2 * half
    rank, kv_cols = kv_w.shape
    heads = kv_cols // (DN + DV)
    head_cols = heads * (DN + DR + DV)
    f32, bf16 = jnp.float32, jnp.bfloat16
    sds = jax.ShapeDtypeStruct
    return pl.pallas_call(
        functools.partial(attention_backward_kernel, heads),
        grid=(near,),
        in_specs=[
            pl.BlockSpec(memory_space=pltpu.SMEM),
            *[one_each(half, width)] * 2,
            *[one_each(*v.shape[1:]) for v in kept_rows],
            *[kept(a) for a in (head_w, kv_w)],
            *[one_each(rows, LANES)] * 2,
            one_each(rows, 1),
            one_each(1, rows),
        ],
        out_specs=[
            pl.BlockSpec((width, head_cols), lambda i: (0, 0)),
            pl.BlockSpec((rank, kv_cols), lambda i: (0, 0)),
            *[one_each(half, width)] * 2,
            *[one_each(half, rank + LANES)] * 2,
        ],
        out_shape=[
            sds((width, head_cols), bf16),
            sds((rank, kv_cols), bf16),
            *[sds((near, half, width), bf16)] * 2,
            *[sds((near, half, rank + LANES), bf16)] * 2,
        ],
        scratch_shapes=[
            pltpu.VMEM((width, head_cols), f32),
            pltpu.VMEM((rank, kv_cols), f32),
        ],
        compiler_params=pltpu.CompilerParams(vmem_limit_bytes=58 * 1024 * 1024),
        cost_estimate=pl.CostEstimate(
            flops=near * rows * width * heads * DN,
            bytes_accessed=2 * near * rows * width,
            transcendentals=0,
        ),
    )(
        core,
        d_own,
        d_other,
        *kept_rows,
        head_w,
        kv_w,
        cosine,
        sine,
        doc[:, :, None],
        doc[:, None, :],
    )


def product_kernel(left_ref, right_ref, out_ref):
    out_ref[0] = dot_tn(left_ref[0], right_ref[...])


def column_products(left, right, tile=512):
    count, rows, height = left.shape
    width = right.shape[1]
    return pl.pallas_call(
        product_kernel,
        grid=(width // tile, count),
        in_specs=[
            pl.BlockSpec((1, rows, height), lambda j, i: (i, 0, 0)),
            pl.BlockSpec((rows, tile), lambda j, i: (0, j)),
        ],
        out_specs=pl.BlockSpec((1, height, tile), lambda j, i: (i, 0, j)),
        out_shape=jax.ShapeDtypeStruct((count, height, width), jnp.float32),
        compiler_params=pltpu.CompilerParams(vmem_limit_bytes=58 * 1024 * 1024),
        cost_estimate=pl.CostEstimate(
            flops=rows * width, bytes_accessed=rows * width, transcendentals=0
        ),
    )(left, right)


def output_kernel(act, sact_own, sact_other, meta_own, meta_other, down_w, sdown_w, own_out, other_out):
    f32, bf16 = jnp.float32, jnp.bfloat16
    count, half, _ = meta_own.shape
    lane = lax.broadcasted_iota(jnp.int32, (2 * half, LANES), 1).astype(f32)
    out = dot_nn(act[...], down_w[...]).astype(bf16)
    for i in range(count):
        meta = jnp.concatenate([meta_own[i], meta_other[i]], axis=0)
        pick = (meta[:, :1] == lane).astype(bf16)
        sact = jnp.concatenate([sact_own[i], sact_other[i]], axis=0)
        here = slice(i * LANES, (i + 1) * LANES)
        rows = (dot_nn(pick, out[here]) + dot_nn(sact, sdown_w[...])).astype(bf16)
        own_out[i], other_out[i] = rows[:half], rows[half:]


def outputs(act, sact_own, sact_other, meta_own, meta_other, down_w, sdown_w, per_step=4):
    groups, half, _ = meta_own.shape
    hidden, width = down_w.shape
    lead, flat, whole = block_specs(per_step)
    return pl.pallas_call(
        output_kernel,
        grid=(groups // per_step,),
        in_specs=[
            flat(hidden),
            *[lead(half, LANES)] * 4,
            *[whole(a) for a in (down_w, sdown_w)],
        ],
        out_specs=[lead(half, width)] * 2,
        out_shape=[jax.ShapeDtypeStruct((groups, half, width), jnp.bfloat16)] * 2,
        compiler_params=pltpu.CompilerParams(vmem_limit_bytes=58 * 1024 * 1024),
        cost_estimate=pl.CostEstimate(
            flops=groups * half * LANES * width,
            bytes_accessed=groups * half * width,
            transcendentals=0,
        ),
    )(act, sact_own, sact_other, meta_own, meta_other, down_w, sdown_w)


def token_plan(
    inputs,
    attn_gain,
    w_query,
    w_latent,
    latent_gain,
    w_kv,
    w_out,
    ffn_gain,
    w_router,
    shared_gate_up,
    shared_down,
    expert_gate_up,
    expert_down,
    lengths,
    routes,
    cotangent,
):
    f32, bf16 = jnp.float32, jnp.bfloat16
    core, me = lax.axis_index("tensor"), lax.axis_index("expert")
    groups = lax.axis_size("expert")
    deep, place, z = groups // PLANE, me % PLANE, me // PLANE
    tok_rows, width = inputs.shape
    half = tok_rows // 2
    own_at, other_at = core * half, (1 - core) * half
    expert_count = w_router.shape[1]
    route_count = routes.shape[1]
    capacity = tok_rows * route_count * 4 // (3 * expert_count)
    shared_cols = shared_gate_up.shape[2] // groups
    latent_cols, rank_width = w_latent.shape[1], latent_gain.shape[0] * groups
    block_rows = w_query.shape[0]
    kv_rows = w_kv.shape[0]

    query_cols = w_query.shape[1] // PLANE
    out_cols = w_out.shape[0] // PLANE
    small = jnp.concatenate(
        [
            w_latent,
            w_latent[:, rank_width:],
            w_router,
            attn_gain[:, None],
            ffn_gain[:, None],
            jnp.pad(latent_gain, (0, block_rows - kv_rows))[:, None],
        ],
        axis=1,
    )
    small_cols = small.shape[1]
    route_half = take_rows(routes, own_at, half).astype(bf16).reshape(block_rows // 2, -1)
    length_col = jnp.pad(lengths[0].astype(bf16), (0, block_rows // 2 - lengths.shape[1]))[:, None]
    route_cols = route_half.shape[1] + 1
    small_half = jnp.concatenate(
        [
            take_rows(small, core * (block_rows // 2), block_rows // 2),
            route_half,
            length_col,
            jnp.zeros((block_rows // 2, -(small_cols + route_cols) % (2 * LANES)), bf16),
        ],
        axis=1,
    )
    packed_cols = small_half.shape[1] // 2
    small_packed = jnp.concatenate([small_half[:, :packed_cols], small_half[:, packed_cols:]])
    kv_cols = w_kv.shape[1] // PLANE
    kv_parts = block_rows // kv_rows
    kv_piece = kv_cols // kv_parts
    w_out_t = w_out.T

    local_heads = query_cols // (DN + DR)

    def by_parts(block):
        heads = [block[:, h * (DN + DR) : (h + 1) * (DN + DR)] for h in range(local_heads)]
        return [h[:, :DN] for h in heads] + [h[:, DN:] for h in heads]

    def quarter(index):
        kv_here = take_rows(w_kv, index * kv_cols, kv_cols, axis=1)
        kv_here = [kv_here[:, p * kv_piece : (p + 1) * kv_piece] for p in range(kv_parts)]
        return jnp.concatenate(
            [
                *by_parts(take_rows(w_query, index * query_cols, query_cols, axis=1)),
                take_rows(w_out_t, index * out_cols, out_cols, axis=1),
                jnp.concatenate(kv_here, axis=0),
            ],
            axis=1,
        )

    near_w = [quarter(place)] + [to_partner(quarter(place ^ r), r) for r in range(1, PLANE)]
    small_line = deep_join(small_packed, deep_pieces(small_packed), z)
    near_w, small_line = tie(near_w, small_line)
    plane_w = jnp.stack(by_place(near_w, place))
    small_sent, x_sent, plane_w = tie(
        small_line.swapaxes(0, 1), take_rows(inputs, own_at, half), plane_w
    )
    small_sent = jnp.stack([small_sent, to_partner(small_sent, 1)])
    small_sent = jnp.concatenate([small_sent, to_partner(small_sent, 2)], axis=0)
    x_sent = jnp.stack([x_sent, to_partner(x_sent, 2)])
    x_came = to_partner(x_sent, 1)
    x_near_own = jnp.stack([x_sent[0], x_came[0], x_sent[1], x_came[1]])
    x_near_other = swap_cores(x_near_own)
    deep_w = deep_hops(plane_w)
    small_parts = [small_sent[r].swapaxes(0, 1) for r in range(PLANE)]
    small_own = jnp.stack(by_place(small_parts, place), axis=1)
    small_own = small_own.reshape(groups, block_rows, packed_cols)
    small_own = jnp.concatenate(
        [small_own[:, : block_rows // 2], small_own[:, block_rows // 2 :]], axis=2
    )
    small_other = swap_cores(small_own)
    small_all = in_order(core, small_own, small_other, axis=1)
    small_all, x_near_other, deep_w = tie(small_all, x_near_other, deep_w)
    head_w = deep_join(plane_w, join_hops(deep_w), z)
    length_at = small_cols + route_cols - 1
    lengths_near = take_rows(small_own, z * PLANE, PLANE)[:, : lengths.shape[1], length_at]
    lengths_near = lengths_near.astype(jnp.int32)
    lengths_near = jnp.stack(by_place([lengths_near[r] for r in range(PLANE)], place))
    shared_rows = jnp.concatenate(
        [shared_gate_up[0].T, shared_gate_up[1].T, shared_down], axis=0
    ).reshape(3, groups, shared_cols, block_rows)
    shared_rows = shared_rows.swapaxes(0, 1).reshape(groups, 3 * shared_cols, block_rows)
    dy_sent, head_w = tie(take_rows(cotangent, own_at, half), head_w)
    dy_own_rows = take_rows(cotangent, own_at, half)
    dy_gather = RowGather(dy_sent)
    dy_came = dy_gather.along()
    head_w = head_w.reshape(groups, block_rows, -1)
    flat_head = head_w.reshape(groups * block_rows, -1)
    at = query_cols + out_cols
    kv_w = head_w[:, :, at : at + kv_piece].reshape(groups, kv_parts, kv_rows, kv_piece)
    kv_w = kv_w.transpose(0, 2, 1, 3).reshape(groups * kv_rows, kv_cols)

    block_index = jnp.arange(groups)
    block_chip = (z - block_index % deep) % deep * PLANE + (place ^ (block_index // deep))
    in_blocks = (block_chip[:, None] == block_index[None, :]).astype(bf16)

    def routes_of(came):
        came = came[:, :, small_cols : small_cols + route_half.shape[1]].reshape(groups, -1)
        came = jnp.dot(in_blocks, came, preferred_element_type=f32)
        return came.astype(jnp.int32).reshape(groups, half, route_count)

    routes_own, routes_other = routes_of(small_own), routes_of(small_other)
    flat_small = small_all.reshape(groups * block_rows, -1)
    latent_w = flat_small[:, :latent_cols]
    at = rank_width + LANES
    router_w = flat_small[:, at : at + expert_count]
    at += expert_count
    gain_one, gain_two = flat_small[:, at], flat_small[:, at + 1]
    latent_g = small_all[:, :kv_rows, at + 2].reshape(-1)

    near_rows = PLANE * tok_rows
    relative, doc = jax.vmap(lambda one: doc_places(one, tok_rows))(lengths_near)
    cosine, sine_tab = rope_tables(relative.reshape(-1), DR)
    cosine, sine_tab = [v.reshape(PLANE, tok_rows, -1) for v in (cosine, sine_tab)]
    rope = (
        jnp.concatenate([cosine] * 4, axis=-1),
        jnp.concatenate([-sine_tab, sine_tab] * 2, axis=-1),
        doc.astype(f32),
    )
    core_index = core.reshape(1).astype(jnp.int32)
    *kept_rows, latent, part_own, part_other = attention(
        core_index,
        x_near_own,
        x_near_other,
        gain_one.astype(f32)[None],
        latent_g.astype(f32)[None],
        flat_head,
        flat_small,
        kv_w,
        *rope,
    )
    normed_b = kept_rows[0].reshape(near_rows, width)
    part_own, part_other, dy_came = tie(part_own, part_other, dy_came)

    def sum_heads(own, other):
        both = add_wide(own, swap_cores(other)).astype(bf16)
        return plane_scatter([both[r] for r in range(PLANE)])

    attn_own = sum_heads(part_own, part_other)
    x_own = take_rows(inputs, own_at, half).astype(f32)
    hidden = x_own + attn_own
    hnormed, scale_two = rms_forward(hidden, gain_two.astype(f32))
    hnormed_b = hnormed.astype(bf16)
    normed_cols = jnp.concatenate(
        [
            take_rows(normed_b, (k * PLANE + place) * block_rows, block_rows, axis=1)
            for k in range(deep)
        ],
        axis=1,
    )
    hnormed_b, dy_lines, normed_cols, shared_rows = tie(
        hnormed_b, dy_gather.lines(dy_came), normed_cols, shared_rows
    )
    def membership(named):
        one_hot = named[..., None] == jnp.arange(expert_count, dtype=jnp.int32)
        return jnp.any(named == me, axis=-1), jnp.any(one_hot, axis=2)

    member_own, hot_own = membership(routes_own)
    member_other, hot_other = membership(routes_other)
    lower = (
        jnp.arange(half, dtype=jnp.int32)[:, None] <= jnp.arange(half, dtype=jnp.int32)[None, :]
    ).astype(bf16)

    def running(mask):
        counts = jnp.dot(mask.astype(bf16), lower, preferred_element_type=f32)
        return counts.astype(jnp.int32)

    count_own, count_other = running(member_own), running(member_other)
    place_own = jnp.where(member_own, count_own - 1, -1)
    place_other = jnp.where(member_other, count_own[:, -1:] + count_other - 1, -1)

    def metadata(slot, hot):
        return jnp.concatenate(
            [
                slot[..., None].astype(f32),
                jnp.zeros((groups, half, shared_cols - 1), f32),
                hot.astype(f32),
                jnp.zeros((groups, half, LANES - shared_cols - expert_count), f32),
            ],
            axis=-1,
        )

    meta_own, meta_other = metadata(place_own, hot_own), metadata(place_other, hot_other)
    hn_gather = RowGather(hnormed_b)
    hn_came, dy_halves, shared_rows = tie(
        hn_gather.along(),
        dy_gather.over_again(dy_lines, dy_gather.over(dy_lines)),
        shared_rows,
    )
    hn_lines, dy_halves, shared_rows = tie(hn_gather.lines(hn_came), dy_halves, shared_rows)
    hn_over, dy_halves, shared_rows = tie(hn_gather.over(hn_lines), dy_halves, shared_rows)
    hn_halves = hn_gather.over_again(hn_lines, hn_over)
    shared_w = lax.all_to_all(shared_rows, "expert", split_axis=0, concat_axis=0, tiled=True)
    dy_own = dy_gather.whole(dy_halves)
    dy_other = swap_cores(dy_own)
    hn_halves, shared_w, dy_other, meta_own, meta_other = tie(
        hn_halves, shared_w, dy_other, meta_own, meta_other
    )
    shared_w = shared_w.swapaxes(0, 1).reshape(3 * shared_cols, groups * block_rows)
    hn_own = hn_gather.whole(hn_halves)


    first_w = jnp.concatenate(
        [
            shared_w[:shared_cols],
            router_w.T,
            jnp.zeros((LANES - shared_cols - expert_count, width), bf16),
            shared_w[shared_cols : 2 * shared_cols],
            jnp.zeros((LANES - shared_cols, width), bf16),
        ],
        axis=0,
    )
    sdown_rows = jnp.pad(shared_w[2 * shared_cols :], ((0, LANES - shared_cols), (0, 0)))
    hn_other = swap_cores(hn_own)
    gate_up_w, down_w = jnp.swapaxes(expert_gate_up[0], 1, 2), expert_down[0]
    (
        slot_rows,
        slot_dy,
        slot_act,
        d_gate_up,
        d_rows_own,
        d_rows_other,
        act_own,
        act_other,
        shared_grads,
        dgate_own,
        dgate_other,
    ) = experts(
        me.reshape(1).astype(jnp.int32),
        hn_own,
        hn_other,
        dy_own,
        dy_other,
        meta_own,
        meta_other,
        gate_up_w,
        down_w,
        first_w,
        sdown_rows,
        shared_cols,
        expert_count,
    )
    d_rows_came = swap_cores(d_rows_other)

    def two_parts(value):
        return value[..., 0] + value[..., 1]

    dgate_sent = two_parts(dgate_own) + swap_cores(two_parts(dgate_other))
    dgate_high = dgate_sent.astype(bf16)
    dgate_low = (dgate_sent - dgate_high.astype(f32)).astype(bf16)
    out_own, out_other = outputs(
        slot_act, act_own, act_other, meta_own, meta_other, down_w, sdown_rows
    )
    d_rows_came, dgate_high, dgate_low, out_other = tie(
        d_rows_came, dgate_high, dgate_low, out_other
    )
    d_sum = RowSum(d_rows_own, d_rows_came)
    sends, shared_grads, slot_act, out_other = tie(
        d_sum.sends(), shared_grads, slot_act, out_other
    )
    came = d_sum.move(sends)
    gate_rows = [contract_rows(in_blocks, v) for v in (dgate_high, dgate_low)]
    dgate = lax.all_to_all(add_wide(*gate_rows), "expert", split_axis=0, concat_axis=0, tiled=True)
    dgate = dgate.T
    out_came = swap_cores(out_other)
    edown_grad = column_products(slot_act[None], slot_dy)[0]
    came, out_came, edown_grad, dgate = tie(came, out_came, edown_grad, dgate)
    sends, slot_rows, out_came = tie(d_sum.sends_again(came), slot_rows, out_came)
    came_again = d_sum.move_again(sends)
    egu_grad = column_products(d_gate_up, slot_rows).swapaxes(1, 2)
    out_sum = RowSum(out_own, out_came)
    out_sends = out_sum.sends()
    came_again, egu_grad, out_sends = tie(came_again, egu_grad, out_sends)
    z_sends, out_sends, dgate = tie(
        line_sends(d_sum.line(came, came_again)), out_sends, dgate
    )
    z_came = line_move(z_sends)
    out_first = out_sum.move(out_sends)
    hot_mine = take_rows(
        jnp.any(routes[..., None] == jnp.arange(expert_count, dtype=jnp.int32), axis=1), own_at, half
    )
    sig = jax.nn.sigmoid(jnp.dot(hnormed_b, router_w, preferred_element_type=f32))
    chosen = jnp.where(hot_mine, sig, 0.0)
    chosen_sum = jnp.sum(chosen, axis=1, keepdims=True)
    dgate = jnp.where(hot_mine, dgate, 0.0)
    inner = jnp.sum(dgate * chosen, axis=1, keepdims=True)
    d_chosen = ROUTE_SCALE * (dgate / chosen_sum - inner / (chosen_sum * chosen_sum))
    d_logits = (jnp.where(hot_mine, d_chosen, 0.0) * sig * (1.0 - sig)).astype(bf16)
    router_grad = contract_rows(d_logits, hnormed_b)
    z_came, d_logits, router_grad = tie(z_came, d_logits, router_grad)
    d_hn = add_wide(*z_came)
    d_hn = d_hn + contract_cols(d_logits, router_w)
    d_hidden_norm, gain_two_grad = rms_backward(hidden, scale_two, gain_two.astype(f32), d_hn)
    d_hidden = dy_own_rows.astype(f32) + d_hidden_norm
    d_hidden_b, shared_grads = tie(d_hidden.astype(bf16), shared_grads)
    d_parts, out_first = tie(plane_gather(d_hidden_b), out_first)
    d_near_own = jnp.stack(d_parts)
    d_near_other = swap_cores(d_near_own)
    grads_sent = shared_grads.astype(bf16).reshape(-1, groups, block_rows)
    grads_came = lax.all_to_all(grads_sent, "expert", split_axis=1, concat_axis=1, tiled=True)
    out_sends, d_near_other = tie(out_sum.sends_again(out_first), d_near_other)
    out_second = out_sum.move_again(out_sends)

    (
        head_grad,
        kv_grad,
        normed_part_own,
        normed_part_other,
        latent_part_own,
        latent_part_other,
    ) = attention_backward(
        core_index, d_near_own, d_near_other, kept_rows, flat_head, kv_w, *rope
    )
    kv_grad = kv_grad.reshape(groups, kv_rows, kv_parts, kv_piece).transpose(0, 2, 1, 3)
    head_grad = jnp.concatenate([head_grad, kv_grad.reshape(-1, kv_piece)], axis=1)
    head_came = deep_move(head_grad.reshape(deep, -1, head_grad.shape[1]), z)
    grad_both = sum_heads(latent_part_own, latent_part_other)
    grad_rope = grad_both[:, rank_width : rank_width + DR] + grad_both[:, rank_width + DR :]
    latent_own = take_rows(latent[0], own_at, half)
    cosine_own = take_rows(cosine[0], own_at, half)
    sine_own = take_rows(sine_tab[0], own_at, half)
    _, scale_kv = rms_forward(latent_own[:, :rank_width], latent_g.astype(f32))
    grad_c, latent_gain_grad = rms_backward(
        latent_own[:, :rank_width], scale_kv, latent_g.astype(f32), grad_both[:, :rank_width]
    )
    grad_latent = jnp.concatenate(
        [grad_c, unrotate(grad_rope, cosine_own, sine_own)], axis=-1
    ).astype(bf16)
    latent_near_own = jnp.stack(plane_gather(grad_latent))
    latent_near = in_order(core, latent_near_own, swap_cores(latent_near_own), axis=1)
    grad_normed = sum_heads(normed_part_own, normed_part_other)
    head_came, latent_near, grad_normed, out_second, grads_came = tie(
        head_came, latent_near, grad_normed, out_second, grads_came
    )
    latent_cut = latent_cols // 2
    latent_near = latent_near.reshape(near_rows, latent_cols)
    latent_blocks = contract_rows(
        normed_cols,
        take_rows(latent_near, core * latent_cut, latent_cut, axis=1),
    )
    latent_half = deep_scatter(latent_blocks.astype(bf16).reshape(deep, -1, latent_cut), z)
    w_latent_grad = in_order(core, latent_half, swap_cores(latent_half), axis=1)

    out_z = line_move(line_sends(out_sum.line(out_first, out_second)))
    head_sums = add_wide(*head_came).astype(bf16).reshape(PLANE, block_rows, -1)
    head_shared = share_columns(head_sums, place)

    def by_heads(block):
        rotary = local_heads * DN
        return [
            part
            for h in range(local_heads)
            for part in (
                block[:, h * DN : (h + 1) * DN],
                block[:, rotary + h * DR : rotary + (h + 1) * DR],
            )
        ]

    at_kv = query_cols + out_cols
    w_query_grad = jnp.concatenate([v for p in head_shared for v in by_heads(p)], axis=1)
    w_query_grad = w_query_grad.astype(f32)
    w_kv_grad = jnp.concatenate(
        [
            p[q * kv_rows : (q + 1) * kv_rows, at_kv:]
            for p in head_shared
            for q in range(kv_parts)
        ],
        axis=1,
    ).astype(f32)
    w_out_grad = jnp.concatenate([p[:, query_cols:at_kv] for p in head_shared], axis=1)
    w_out_grad = w_out_grad.astype(f32).T
    sgu_out = grads_came[: 2 * shared_cols].astype(f32)
    sgu_out = sgu_out.reshape(2, shared_cols, groups, block_rows)
    sgu_out = sgu_out.transpose(0, 3, 2, 1).reshape(2, block_rows, -1)
    sdown_out = grads_came[2 * shared_cols :].astype(f32).swapaxes(0, 1).reshape(-1, block_rows)
    grad_normed = grad_normed + contract_cols(grad_latent, latent_w)
    moe_own = add_wide(*out_z)
    mixed_own = (hidden + moe_own).astype(bf16)
    mixed = in_order(core, mixed_own, swap_cores(mixed_own))

    _, scale_own = rms_forward(x_own, gain_one.astype(f32))
    grad_x_norm, gain_one_grad = rms_backward(x_own, scale_own, gain_one.astype(f32), grad_normed)
    input_own = d_hidden + grad_x_norm
    input_grad = in_order(core, input_own, swap_cores(input_own))

    gain_lanes = jnp.pad(
        latent_gain_grad.reshape(groups, kv_rows), ((0, 0), (0, block_rows - kv_rows))
    )
    vectors = jnp.concatenate(
        [
            router_grad,
            gain_one_grad[None],
            gain_two_grad[None],
            gain_lanes.reshape(1, -1),
        ],
        axis=0,
    ).reshape(-1, groups, block_rows)
    arrived = lax.all_to_all(vectors, "expert", split_axis=1, concat_axis=1, tiled=True)
    sums = jnp.sum(arrived, axis=1)
    sums = sums + swap_cores(sums)
    return (
        mixed,
        input_grad,
        sums[expert_count],
        w_query_grad,
        w_latent_grad,
        sums[expert_count + 2, :kv_rows],
        w_kv_grad,
        w_out_grad,
        sums[expert_count + 1],
        sums[:expert_count].T,
        sgu_out,
        sdown_out,
        egu_grad[None],
        edown_grad[None],
    )


def solution(mesh):
    groups = mesh.shape["expert"]
    plan = token_plan if groups <= 16 else weight_plan
    return jax.shard_map(
        plan,
        mesh=mesh,
        in_specs=(
            P("expert", None),
            P("expert"),
            P("expert", "tensor"),
            P("expert", None),
            P("expert"),
            P("expert", "tensor"),
            P("tensor", "expert"),
            P("expert"),
            P("expert", None),
            P(None, "expert", "tensor"),
            P("tensor", "expert"),
            P("expert", None, None, "tensor"),
            P("expert", "tensor", None),
            P("expert", None),
            P("expert", None),
            P("expert", None),
        ),
        out_specs=(
            P("expert", None),
            P("expert", None),
            P("expert"),
            P("expert", "tensor"),
            P("expert", None),
            P("expert"),
            P("expert", "tensor"),
            P("tensor", "expert"),
            P("expert"),
            P("expert", None),
            P(None, "expert", "tensor"),
            P("tensor", "expert"),
            P("expert", None, None, "tensor"),
            P("expert", "tensor", None),
        ),
        check_vma=False,
    )
```

```python
import functools

import jax
import jax.numpy as jnp
from jax import lax
from jax.experimental import pallas as pl
from jax.experimental.pallas import tpu as pltpu
from jax.sharding import PartitionSpec as P

DN = 128
DR = 64
DV = 128
LANES = 128


EPSILON = 1e-06
ROUTE_SCALE = 2.446
ROPE_BASE = 50000.0
NEGATIVE = -1e30


def cut_along(value, dim, length):
    before, after = (value.shape[:dim], value.shape[dim + 1 :])
    return jnp.moveaxis(value.reshape(*before, length, -1, *after), dim, 0)


def summed_on_arrival(value, axis, dim):
    length = lax.axis_size(axis)
    tiles = lax.all_to_all(cut_along(value, dim, length), axis, 0, 0, tiled=True)
    return jnp.sum(tiles.astype(jnp.float32), axis=0)


def sent_together(arrays, axis, dim, along):
    columns = [a.reshape(*a.shape[:along], -1) for a in arrays]
    both = jnp.concatenate(columns, axis=along)
    whole, at, outs = (summed_on_arrival(both, axis, dim), 0, [])
    for a, column in zip(arrays, columns):
        slab = whole[..., at : at + column.shape[along]]
        outs.append(slab.reshape(*slab.shape[:along], *a.shape[along:]))
        at += column.shape[along]
    return tuple(outs)


def contract_rows(left_arr, right_arr):
    return lax.dot_general(
        left_arr, right_arr, (((0,), (0,)), ((), ())), preferred_element_type=jnp.float32
    )


def contract_cols(left_arr, right_arr):
    return lax.dot_general(
        left_arr, right_arr, (((1,), (1,)), ((), ())), preferred_element_type=jnp.float32
    )


def rms_forward(rows_in, gain_vec):
    inverse = lax.rsqrt(jnp.mean(rows_in * rows_in, axis=-1, keepdims=True) + EPSILON)
    return (rows_in * inverse * gain_vec, inverse)


def rms_backward(rows_in, inverse, gain_vec, grad_out):
    gain_grad = jnp.sum(grad_out * rows_in * inverse, axis=0)
    weighted = grad_out * gain_vec
    inner_mean = jnp.mean(weighted * rows_in, axis=-1, keepdims=True)
    return (inverse * weighted - rows_in * inverse * inverse * inverse * inner_mean, gain_grad)


def doc_layout(doc_lengths, row_count):
    ends_at = jnp.cumsum(doc_lengths)
    starts_at = ends_at - doc_lengths
    position = jnp.arange(row_count, dtype=jnp.int32)
    doc_ids = jnp.sum((position[:, None] >= ends_at[None, :]).astype(jnp.int32), axis=1)
    hitting = doc_ids[:, None] == jnp.arange(doc_lengths.shape[0], dtype=jnp.int32)[None, :]
    start_of = jnp.sum(jnp.where(hitting, starts_at[None, :], 0), axis=1)
    relative = position - start_of
    visible = (doc_ids[:, None] == doc_ids[None, :]) & (position[:, None] >= position[None, :])
    return (relative, visible)


def rope_tables(relative, rot_width):
    counter = jnp.arange(rot_width // 2, dtype=jnp.float32)
    frequency = ROPE_BASE ** (-2.0 * counter / rot_width)
    angles = relative.astype(jnp.float32)[:, None] * frequency[None, :]
    return (jnp.cos(angles), jnp.sin(angles))


def rotate(tensor_in, cosine, sine_tab):
    half_width = tensor_in.shape[-1] // 2
    leading = tensor_in[..., :half_width]
    trailing = tensor_in[..., half_width:]
    return jnp.concatenate(
        [leading * cosine - trailing * sine_tab, trailing * cosine + leading * sine_tab], axis=-1
    )


def unrotate(grad_in, cosine, sine_tab):
    half_width = grad_in.shape[-1] // 2
    leading = grad_in[..., :half_width]
    trailing = grad_in[..., half_width:]
    return jnp.concatenate(
        [leading * cosine + trailing * sine_tab, trailing * cosine - leading * sine_tab], axis=-1
    )


def gated_linear_backward(gate_in, up_in, grad_act):
    sigmoid_g = jax.nn.sigmoid(gate_in)
    grad_gate = grad_act * up_in * sigmoid_g * (1.0 + gate_in * (1.0 - sigmoid_g))
    return (grad_gate, grad_act * gate_in * sigmoid_g)


def slot_tables(route_rows, expert_count, capacity):
    flat_routes = route_rows.reshape(-1)
    one_hot = (flat_routes[:, None] == jnp.arange(expert_count, dtype=jnp.int32)[None, :]).astype(
        jnp.int32
    )
    ranking = jnp.sum((jnp.cumsum(one_hot, axis=0) - one_hot) * one_hot, axis=1)
    slot_ids = flat_routes * capacity + ranking
    row_total = flat_routes.shape[0]
    source = (
        jnp.zeros((expert_count * capacity,), jnp.int32)
        .at[slot_ids]
        .set(jnp.arange(row_total, dtype=jnp.int32))
    )
    filled = jnp.zeros((expert_count * capacity,), jnp.int32).at[slot_ids].set(1)
    return (slot_ids, source, filled)


def to_owner(rows_in):
    arrived = lax.all_to_all(rows_in, "expert", split_axis=0, concat_axis=1, tiled=True)
    return arrived


def weight_plan(
    inputs,
    attn_gain,
    w_query,
    w_latent,
    latent_gain,
    w_kv,
    w_out,
    ffn_gain,
    w_router,
    shared_gate_up,
    shared_down,
    expert_gate_up,
    expert_down,
    lengths,
    routes,
    cotangent,
):
    tok_rows = inputs.shape[0]
    model_width = inputs.shape[1]
    expert_count = w_router.shape[1]
    route_count = routes.shape[1]
    capacity = tok_rows * route_count * 4 // (3 * expert_count)
    brain_float16 = jnp.bfloat16
    f32 = jnp.float32
    gathered = (
        lax.all_gather(attn_gain, "expert", axis=0, tiled=True),
        lax.all_gather(w_query, "expert", axis=0, tiled=True),
        lax.all_gather(w_latent, "expert", axis=0, tiled=True),
        lax.all_gather(latent_gain, "expert", axis=0, tiled=True),
        lax.all_gather(w_kv, "expert", axis=0, tiled=True),
        lax.all_gather(w_out, "expert", axis=1, tiled=True),
        lax.all_gather(ffn_gain, "expert", axis=0, tiled=True),
        lax.all_gather(w_router, "expert", axis=0, tiled=True),
        lax.all_gather(shared_gate_up, "expert", axis=1, tiled=True),
        lax.all_gather(shared_down, "expert", axis=1, tiled=True),
    )
    gain_one, query_w, latent_w, latent_g, kv_w, out_w, gain_two, router_w, sgate_up, sdown_w = (
        gathered
    )
    local_heads = query_w.shape[1] // (DN + DR)
    rank_width = latent_g.shape[0]
    x_float = inputs.astype(f32)
    relative, visible = doc_layout(lengths[0], tok_rows)
    cosine, sine_tab = rope_tables(relative, DR)
    q_scale = (DN + DR) ** (-0.5)
    normed, scale_one = rms_forward(x_float, gain_one.astype(f32))
    normed_b = normed.astype(brain_float16)
    queries = jnp.dot(normed_b, query_w, preferred_element_type=f32).reshape(
        tok_rows, local_heads, DN + DR
    )
    q_rot = rotate(queries[..., DN:], cosine[:, None, :], sine_tab[:, None, :])
    q_all = jnp.concatenate([queries[..., :DN], q_rot], axis=-1).astype(brain_float16)
    latent = jnp.dot(normed_b, latent_w, preferred_element_type=f32)
    compressed, scale_kv = rms_forward(latent[:, :rank_width], latent_g.astype(f32))
    compressed_b = compressed.astype(brain_float16)
    k_rope = rotate(latent[:, rank_width:], cosine, sine_tab).astype(brain_float16)
    kv_all = jnp.dot(compressed_b, kv_w, preferred_element_type=f32).reshape(
        tok_rows, local_heads, DN + DV
    )
    k_nope = kv_all[..., :DN].astype(brain_float16)
    values = kv_all[..., DN:].astype(brain_float16)
    key_all = jnp.concatenate(
        [k_nope, jnp.broadcast_to(k_rope[:, None, :], (tok_rows, local_heads, DR))], axis=-1
    )

    def score_block():
        raw_scores = (
            jnp.einsum("qhd,khd->hqk", q_all, key_all, preferred_element_type=f32) * q_scale
        )
        return jnp.where(visible[None], raw_scores, NEGATIVE)

    scores = score_block()
    top_score = jnp.max(scores, axis=-1, keepdims=True)
    log_total = top_score + jnp.log(jnp.sum(jnp.exp(scores - top_score), axis=-1, keepdims=True))
    probs_b = jnp.exp(scores - log_total).astype(brain_float16)
    attended = jnp.einsum("hqk,khd->qhd", probs_b, values, preferred_element_type=f32)
    attended_b = attended.reshape(tok_rows, local_heads * DV).astype(brain_float16)
    attn = lax.psum(jnp.dot(attended_b, out_w, preferred_element_type=f32), "tensor")
    hidden = x_float + attn
    hnormed, scale_two = rms_forward(hidden, gain_two.astype(f32))
    hnormed_b = hnormed.astype(brain_float16)
    logits = jnp.dot(hnormed_b, router_w, preferred_element_type=f32)
    sigmoid_vals = jax.nn.sigmoid(logits)
    route_hot = routes[:, :, None] == jnp.arange(expert_count, dtype=jnp.int32)[None, None, :]
    chosen = jnp.sum(jnp.where(route_hot, sigmoid_vals[:, None, :], 0.0), axis=2)
    chosen_sum = jnp.sum(chosen, axis=1, keepdims=True)
    gate_vals = ROUTE_SCALE * chosen / chosen_sum
    slot_ids, source, filled = slot_tables(routes, expert_count, capacity)
    is_filled = filled[:, None] == 1
    sent_rows = jnp.where(is_filled, hnormed_b[source // route_count], 0).reshape(
        expert_count, capacity, model_width
    )
    received = to_owner(sent_rows)
    gate_up_joined = jnp.einsum(
        "erd,egdf->egrf", received, expert_gate_up, preferred_element_type=f32
    )
    expert_act = (jax.nn.silu(gate_up_joined[:, 0]) * gate_up_joined[:, 1]).astype(brain_float16)
    expert_res = jnp.einsum(
        "erf,efd->erd", expert_act, expert_down, preferred_element_type=f32
    ).astype(brain_float16)
    returned_all = lax.all_to_all(expert_res, "expert", split_axis=1, concat_axis=0, tiled=True)
    returned = returned_all.reshape(expert_count * capacity, model_width)[slot_ids].reshape(
        tok_rows, route_count, model_width
    )
    shared_gu = jnp.einsum("td,gdf->gtf", hnormed_b, sgate_up, preferred_element_type=f32)
    shared_act = (jax.nn.silu(shared_gu[0]) * shared_gu[1]).astype(brain_float16)
    branch_sum = jnp.dot(shared_act, sdown_w, preferred_element_type=f32)
    for route_idx in range(route_count):
        branch_sum = branch_sum + gate_vals[:, route_idx : route_idx + 1] * returned[
            :, route_idx
        ].astype(f32)
    moe_out = lax.psum(branch_sum.astype(jnp.bfloat16), "tensor").astype(jnp.float32)
    mixed = (hidden + moe_out).astype(brain_float16)
    grad_y = cotangent.astype(f32)
    sdown_grad = contract_rows(shared_act, cotangent)
    grad_sact = contract_cols(cotangent, sdown_w)
    grad_sgate, grad_sup = gated_linear_backward(shared_gu[0], shared_gu[1], grad_sact)
    grad_sgu = jnp.stack([grad_sgate, grad_sup], axis=0).astype(brain_float16)
    sgu_grad = jnp.einsum("td,gtf->gdf", hnormed_b, grad_sgu, preferred_element_type=f32)
    grad_hn_part = jnp.einsum("gtf,gdf->td", grad_sgu, sgate_up, preferred_element_type=f32)
    gate_columns = []
    for route_idx in range(route_count):
        gate_columns.append(jnp.sum(grad_y * returned[:, route_idx].astype(f32), axis=1))
    gate_part = jnp.stack(gate_columns, axis=1)
    slot_grads = (
        (gate_vals[:, :, None] * grad_y[:, None, :])
        .reshape(tok_rows * route_count, model_width)
        .astype(brain_float16)
    )
    grad_sent = jnp.where(is_filled, slot_grads[source], 0).reshape(
        expert_count, capacity, model_width
    )
    grad_received = to_owner(grad_sent)
    edown_grad = jnp.einsum("erf,erd->efd", expert_act, grad_received, preferred_element_type=f32)
    expert_activation_gradient = jnp.einsum(
        "erd,efd->erf", grad_received, expert_down, preferred_element_type=f32
    )
    expert_gate_gradient, expert_up_gradient = gated_linear_backward(
        gate_up_joined[:, 0], gate_up_joined[:, 1], expert_activation_gradient
    )
    expert_gate_up_gradient = jnp.stack([expert_gate_gradient, expert_up_gradient], axis=1).astype(
        brain_float16
    )
    egu_grad = jnp.einsum(
        "erd,egrf->egdf", received, expert_gate_up_gradient, preferred_element_type=f32
    )
    grad_rows = jnp.einsum(
        "egrf,egdf->erd", expert_gate_up_gradient, expert_gate_up, preferred_element_type=f32
    ).astype(brain_float16)
    grad_back = lax.all_to_all(grad_rows, "expert", split_axis=1, concat_axis=0, tiled=True)
    grad_routes = grad_back.reshape(expert_count * capacity, model_width)[slot_ids].reshape(
        tok_rows, route_count, model_width
    )
    for route_idx in range(route_count):
        grad_hn_part = grad_hn_part + grad_routes[:, route_idx].astype(f32)
    gate_grads = lax.psum(gate_part, "tensor")
    grad_chosen = ROUTE_SCALE * (
        gate_grads / chosen_sum
        - jnp.sum(gate_grads * chosen, axis=1, keepdims=True) / (chosen_sum * chosen_sum)
    )
    grad_sig = jnp.sum(jnp.where(route_hot, grad_chosen[:, :, None], 0.0), axis=1)
    grad_logits = (grad_sig * sigmoid_vals * (1.0 - sigmoid_vals)).astype(brain_float16)
    router_grad = contract_rows(hnormed_b, grad_logits)
    grad_hn = lax.psum(grad_hn_part, "tensor") + contract_cols(grad_logits, router_w)
    grad_hidden_norm, gain_two_grad = rms_backward(hidden, scale_two, gain_two.astype(f32), grad_hn)
    grad_hidden = grad_y + grad_hidden_norm
    grad_hidden_b = grad_hidden.astype(brain_float16)
    out_grad = contract_rows(attended_b, grad_hidden_b)
    grad_att = (
        contract_cols(grad_hidden_b, out_w).reshape(tok_rows, local_heads, DV).astype(brain_float16)
    )
    probs = jnp.exp(score_block() - log_total)
    probs_again = probs.astype(brain_float16)
    grad_probs = jnp.einsum("qhd,khd->hqk", grad_att, values, preferred_element_type=f32)
    grad_vals = jnp.einsum("hqk,qhd->khd", probs_again, grad_att, preferred_element_type=f32)
    row_delta = jnp.sum(probs * grad_probs, axis=-1, keepdims=True)
    grad_scores = (probs * (grad_probs - row_delta)).astype(brain_float16)
    grad_q = jnp.einsum("hqk,khd->qhd", grad_scores, key_all, preferred_element_type=f32) * q_scale
    grad_keys = jnp.einsum("hqk,qhd->khd", grad_scores, q_all, preferred_element_type=f32) * q_scale
    grad_kv = (
        jnp.concatenate([grad_keys[..., :DN], grad_vals], axis=-1)
        .reshape(tok_rows, local_heads * (DN + DV))
        .astype(brain_float16)
    )
    kv_grad = contract_rows(compressed_b, grad_kv)
    grad_comp_part = contract_cols(grad_kv, kv_w)
    grad_krope_part = jnp.sum(grad_keys[..., DN:], axis=1)
    grad_comp, grad_krope = (
        lax.psum(grad_comp_part.astype(jnp.bfloat16), "tensor").astype(jnp.float32),
        lax.psum(grad_krope_part.astype(jnp.bfloat16), "tensor").astype(jnp.float32),
    )
    grad_c, latent_gain_grad = rms_backward(
        latent[:, :rank_width], scale_kv, latent_g.astype(f32), grad_comp
    )
    grad_latent = jnp.concatenate([grad_c, unrotate(grad_krope, cosine, sine_tab)], axis=-1).astype(
        brain_float16
    )
    grad_qrot = unrotate(grad_q[..., DN:], cosine[:, None, :], sine_tab[:, None, :])
    grad_queries = (
        jnp.concatenate([grad_q[..., :DN], grad_qrot], axis=-1)
        .reshape(tok_rows, local_heads * (DN + DR))
        .astype(brain_float16)
    )
    query_grad = contract_rows(normed_b, grad_queries)
    latent_grad = contract_rows(normed_b, grad_latent)
    grad_normed = lax.psum(
        contract_cols(grad_queries, query_w).astype(jnp.bfloat16), "tensor"
    ).astype(jnp.float32) + contract_cols(grad_latent, latent_w)
    grad_x_norm, gain_one_grad = rms_backward(x_float, scale_one, gain_one.astype(f32), grad_normed)
    input_grad = grad_hidden + grad_x_norm
    first_owned = (
        *sent_together(
            (
                gain_one_grad.astype(jnp.bfloat16),
                query_grad.astype(jnp.bfloat16),
                latent_grad.astype(jnp.bfloat16),
            ),
            "expert",
            0,
            1,
        ),
        *sent_together(
            (latent_gain_grad.astype(jnp.bfloat16), kv_grad.astype(jnp.bfloat16)), "expert", 0, 1
        ),
    )
    second_owned = (
        lax.psum_scatter(out_grad, "expert", scatter_dimension=1, tiled=True),
        lax.psum_scatter(gain_two_grad, "expert", scatter_dimension=0, tiled=True),
        lax.psum_scatter(router_grad, "expert", scatter_dimension=0, tiled=True),
        lax.psum_scatter(sgu_grad, "expert", scatter_dimension=1, tiled=True),
        lax.psum_scatter(sdown_grad, "expert", scatter_dimension=1, tiled=True),
    )
    return (
        mixed,
        input_grad,
        first_owned[0],
        first_owned[1],
        first_owned[2],
        first_owned[3],
        first_owned[4],
        second_owned[0],
        second_owned[1],
        second_owned[2],
        second_owned[3],
        second_owned[4],
        egu_grad,
        edown_grad,
    )


def swap_cores(value):
    return lax.ppermute(value, "tensor", [(0, 1), (1, 0)])


def take_rows(value, start, count, axis=0):
    return lax.dynamic_slice_in_dim(value, start, count, axis=axis)


def in_order(core, own, other, axis=0):
    return jnp.where(
        core == 0,
        jnp.concatenate([own, other], axis=axis),
        jnp.concatenate([other, own], axis=axis),
    )


def add_wide(*parts):
    total = parts[0].astype(jnp.float32)
    for part in parts[1:]:
        total = total + part.astype(jnp.float32)
    return total


PLANE = 4


def to_partner(value, flips):
    groups = lax.axis_size("expert")
    return lax.ppermute(value, "expert", [(g, g ^ flips) for g in range(groups)])


def to_deeper(value, step):
    groups = lax.axis_size("expert")
    pairs = [(g, (g + step * PLANE) % groups) for g in range(groups)]
    return lax.ppermute(value, "expert", pairs)


def plane_gather(value):
    return [value] + [to_partner(value, r) for r in range(1, PLANE)]


def plane_scatter(parts):
    return add_wide(parts[0], *[to_partner(parts[r], r) for r in range(1, PLANE)])


def by_place(parts, place):
    odd, high = place % 2 == 1, place // 2 == 1
    parts = [jnp.where(odd, parts[i ^ 1], parts[i]) for i in range(PLANE)]
    return [jnp.where(high, parts[i ^ 2], parts[i]) for i in range(PLANE)]


def tie(*values):
    return lax.optimization_barrier(values)


def deep_pieces(value):
    deep = lax.axis_size("expert") // PLANE
    return [to_deeper(value, s) for s in range(1, deep)]


def one_plane(value, step):
    groups = lax.axis_size("expert")
    pairs = [(g, g + step * PLANE) for g in range(groups) if 0 <= g + step * PLANE < groups]
    return lax.ppermute(value, "expert", pairs)


def deep_hops(value):
    deep = lax.axis_size("expert") // PLANE
    after, before, down, up = [], [], value, value
    for _ in range(1, deep):
        down, up = one_plane(down, 1), one_plane(up, -1)
        after.append(down)
        before.append(up)
    return after, before


def join_hops(hops):
    after, before = hops
    return [a + b for a, b in zip(after, before[::-1])]


def deep_join(value, pieces, z):
    deep = lax.axis_size("expert") // PLANE
    whole = jnp.zeros((deep, *value.shape), value.dtype)
    whole = lax.dynamic_update_index_in_dim(whole, value, z, 0)
    for step in range(1, deep):
        whole = lax.dynamic_update_index_in_dim(whole, pieces[step - 1], (z - step) % deep, 0)
    return whole


def deep_move(blocks, z):
    deep = blocks.shape[0]

    def block(index):
        return lax.dynamic_index_in_dim(blocks, index, 0, keepdims=False)

    return [block(z)] + [to_deeper(block((z + step) % deep), step) for step in range(1, deep)]


def deep_scatter(blocks, z):
    return add_wide(*deep_move(blocks, z))


def share_columns(rows, place):
    parts = [at_index(rows, 0, place)]
    for r in range(1, PLANE):
        parts.append(to_partner(at_index(rows, 0, place ^ r), r))
    return by_place(parts, place)


def all_groups(value):
    return lax.all_gather(value, "expert", axis=0, tiled=False)


def at_index(value, axis, index):
    return lax.dynamic_index_in_dim(value, index, axis, keepdims=False)


def doc_places(doc_lengths, row_count):
    ends_at = jnp.cumsum(doc_lengths)
    position = jnp.arange(row_count, dtype=jnp.int32)
    doc_ids = jnp.sum((position[:, None] >= ends_at[None, :]).astype(jnp.int32), axis=1)
    hitting = doc_ids[:, None] == jnp.arange(doc_lengths.shape[0], dtype=jnp.int32)[None, :]
    start_of = jnp.sum(jnp.where(hitting, (ends_at - doc_lengths)[None, :], 0), axis=1)
    return position - start_of, doc_ids


def hop_sum(pieces):
    groups = lax.axis_size("expert")
    deep = groups // PLANE
    z = lax.axis_index("expert") // PLANE
    ends = []
    for way in (1, -1):
        came = None
        for step in range(1, deep):
            gone = pieces(jnp.clip(z + way * (deep - step), 0, deep - 1))
            if came is not None:
                gone = add_wide(gone, came).astype(gone.dtype)
            first = range(step) if way == 1 else range(deep - step, deep)
            pairs = [
                (p * PLANE + q, (p + way) * PLANE + q) for p in first for q in range(PLANE)
            ]
            came = lax.ppermute(gone, "expert", pairs)
        ends.append(came)
    return [pieces(z), *ends]


class RowGather:
    def __init__(self, value):
        self.cut = value.shape[0] // 2
        self.value = value

    def along(self):
        return [self.value] + deep_pieces(self.value)

    def lines(self, came):
        return [jnp.stack([v[: self.cut] for v in came]), jnp.stack([v[self.cut :] for v in came])]

    def over(self, lines):
        first, second = lines
        return to_partner(first, 1), to_partner(second, 2)

    def over_again(self, lines, came):
        (first, second), (beside, behind) = lines, came
        return [
            [first, beside, to_partner(first, 2), to_partner(beside, 2)],
            [second, to_partner(second, 1), behind, to_partner(behind, 1)],
        ]

    def whole(self, halves):
        return jnp.concatenate([jnp.concatenate(half, axis=0) for half in halves], axis=1)


class RowSum:
    def __init__(self, *terms):
        groups, rows = terms[0].shape[:2]
        self.type = terms[0].dtype
        cut = rows // 2
        blocks = [v.reshape(PLANE, groups // PLANE, *v.shape[1:]) for v in terms]
        self.halves = (
            ([v[:, :, :cut] for v in blocks], 2, 1),
            ([v[:, :, cut:] for v in blocks], 1, 2),
        )

    def _add(self, parts):
        return add_wide(*parts).astype(self.type)

    def sends(self):
        return [
            jnp.stack([self._add([v[far] for v in held]), self._add([v[far | near] for v in held])])
            for held, far, near in self.halves
        ]

    def move(self, sends):
        return [to_partner(v, far) for v, (_, far, _) in zip(sends, self.halves)]

    def sends_again(self, came):
        return [
            self._add([v[near] for v in held] + [c[1]])
            for c, (held, _, near) in zip(came, self.halves)
        ]

    def move_again(self, sends):
        return [to_partner(v, near) for v, (_, _, near) in zip(sends, self.halves)]

    def line(self, came, came_again):
        sums = [
            self._add([v[0] for v in held] + [c[0], d])
            for c, d, (held, *_) in zip(came, came_again, self.halves)
        ]
        return jnp.concatenate(sums, axis=1)


def line_sends(line):
    return [line[step] for step in range(line.shape[0])]


def line_move(sends):
    return [sends[0]] + [to_deeper(v, -step) for step, v in enumerate(sends) if step > 0]


def dot_nn(left, right):
    return lax.dot_general(left, right, (((1,), (0,)), ((), ())), preferred_element_type=jnp.float32)


def dot_nt(left, right):
    return lax.dot_general(left, right, (((1,), (1,)), ((), ())), preferred_element_type=jnp.float32)


def dot_tn(left, right):
    return lax.dot_general(left, right, (((0,), (0,)), ((), ())), preferred_element_type=jnp.float32)


def two_lanes(column, lane):
    high = column.astype(jnp.bfloat16).astype(jnp.float32)
    spread = jnp.where(lane == 0, high, jnp.where(lane == 1, column - high, 0.0))
    return spread.astype(jnp.bfloat16)


def expert_kernel(
    shared_cols,
    expert_count,
    me_ref,
    hn_own,
    hn_other,
    dy_own,
    dy_other,
    meta_own,
    meta_other,
    gate_up_w,
    down_w,
    first_w,
    sdown_w,
    slots_out,
    slot_dy_out,
    act_out,
    d_gate_up_out,
    rows_own_out,
    rows_other_out,
    sact_own_out,
    sact_other_out,
    shared_grads_out,
    dgate_own_out,
    dgate_other_out,
):
    f32, bf16 = jnp.float32, jnp.bfloat16
    count, half, _ = hn_own.shape
    tokens = 2 * half
    me = me_ref[0]
    lane = lax.broadcasted_iota(jnp.int32, (count * tokens, LANES), 1)
    is_router = (lane >= shared_cols) & (lane < shared_cols + expert_count)
    first = first_w[...]

    def joined(own, other):
        return jnp.concatenate([v[i] for i in range(count) for v in (own, other)], axis=0)

    rows, rows_dy = joined(hn_own, hn_other), joined(dy_own, dy_other)
    meta = joined(meta_own, meta_other)
    products = dot_nt(rows, first)
    gate, up = products[:, :LANES], products[:, LANES:]
    sig = jax.nn.sigmoid(gate)
    total = jnp.sum(jnp.where(is_router, sig * meta, 0.0), axis=1, keepdims=True)
    mine = jnp.sum(jnp.where(lane == shared_cols + me, sig, 0.0), axis=1, keepdims=True)
    token_gate = two_lanes(ROUTE_SCALE * mine / total, lane)
    sact = (gate * sig * up).astype(bf16)
    d_sact = dot_nt(rows_dy, sdown_w[...])
    d_sgate = d_sact * up * sig * (1.0 + gate * (1.0 - sig))
    dsh = jnp.concatenate([d_sgate, d_sact * gate * sig], axis=1).astype(bf16)
    pick = (meta[:, :1] == lane.astype(f32)).astype(bf16)
    groups = [slice(i * tokens, (i + 1) * tokens) for i in range(count)]
    for i in range(count):
        start = i * tokens
        sact_own_out[i] = sact[start : start + half]
        sact_other_out[i] = sact[start + half : start + tokens]
    slots = [dot_tn(pick[g], rows[g]).astype(bf16) for g in groups]
    slot_dys = [dot_tn(pick[g], rows_dy[g]).astype(bf16) for g in groups]
    slot_gates = [
        jnp.sum(dot_tn(pick[g], token_gate[g]), axis=1, keepdims=True) for g in groups
    ]

    @pl.when(pl.program_id(0) == 0)
    def _():
        shared_grads_out[...] = jnp.zeros_like(shared_grads_out)

    first_grad, sdown_grad = dot_tn(dsh, rows), dot_tn(sact, rows_dy)
    shared_grads_out[:shared_cols] += first_grad[:shared_cols]
    shared_grads_out[shared_cols : 2 * shared_cols] += first_grad[LANES : LANES + shared_cols]
    shared_grads_out[2 * shared_cols :] += sdown_grad[:shared_cols]
    slot_rows = jnp.concatenate(slots, axis=0)
    slot_dy = jnp.concatenate(slot_dys, axis=0)
    slot_gate = jnp.concatenate(slot_gates, axis=0)
    slots_out[...] = slot_rows
    slot_dy_out[...] = slot_dy
    gate = dot_nt(slot_rows, gate_up_w[0])
    up = dot_nt(slot_rows, gate_up_w[1])
    d_act = dot_nt(slot_dy, down_w[...])
    sig = jax.nn.sigmoid(gate)
    silu = gate * sig
    act = silu * up
    slot_dgate = jnp.sum(act * d_act, axis=1, keepdims=True)
    act_out[...] = (slot_gate * act).astype(bf16)
    d_act = slot_gate * d_act
    d_gate = (d_act * up * sig * (1.0 + gate * (1.0 - sig))).astype(bf16)
    d_up = (d_act * silu).astype(bf16)
    d_gate_up_out[0] = d_gate
    d_gate_up_out[1] = d_up
    d_slots = (dot_nn(d_gate, gate_up_w[0]) + dot_nn(d_up, gate_up_w[1])).astype(bf16)
    slot_lane = lax.broadcasted_iota(jnp.int32, (LANES, LANES), 1)
    d_shared = dot_nn(dsh, first)
    for i, g in enumerate(groups):
        here = slice(i * LANES, (i + 1) * LANES)
        d_rows = (dot_nn(pick[g], d_slots[here]) + d_shared[g]).astype(bf16)
        rows_own_out[i], rows_other_out[i] = d_rows[:half], d_rows[half:]
        dgate = dot_nn(pick[g], two_lanes(slot_dgate[here], slot_lane))
        dgate_own_out[i], dgate_other_out[i] = dgate[:half], dgate[half:]


def block_specs(per_step):
    def lead(*tail):
        return pl.BlockSpec((per_step, *tail), lambda i: (i,) + (0,) * len(tail))

    def flat(cols):
        return pl.BlockSpec((per_step * LANES, cols), lambda i: (i, 0))

    def whole(a):
        return pl.BlockSpec(a.shape, lambda i: (0,) * a.ndim, pipeline_mode=pl.Buffered(1))

    return lead, flat, whole


def slots_cost(width, hidden, products):
    return LANES * width * hidden * products


def experts(
    me,
    hn_own,
    hn_other,
    dy_own,
    dy_other,
    meta_own,
    meta_other,
    gate_up_w,
    down_w,
    first_w,
    sdown_w,
    shared_cols,
    expert_count,
    per_step=2,
):
    groups, half, width = hn_own.shape
    hidden = down_w.shape[0]
    slots = groups * LANES
    f32, bf16 = jnp.float32, jnp.bfloat16
    lead, flat, whole = block_specs(per_step)
    sds = jax.ShapeDtypeStruct
    rows_cost = 2 * groups * (2 * half * width * 4 * LANES + slots_cost(width, hidden, 5))
    return pl.pallas_call(
        functools.partial(expert_kernel, shared_cols, expert_count),
        grid=(groups // per_step,),
        in_specs=[
            pl.BlockSpec(memory_space=pltpu.SMEM),
            *[lead(half, width)] * 4,
            *[lead(half, LANES)] * 2,
            *[whole(a) for a in (gate_up_w, down_w, first_w, sdown_w)],
        ],
        out_specs=[
            flat(width),
            flat(width),
            flat(hidden),
            pl.BlockSpec((2, per_step * LANES, hidden), lambda i: (0, i, 0)),
            *[lead(half, width)] * 2,
            *[lead(half, LANES)] * 2,
            pl.BlockSpec((3 * shared_cols, width), lambda i: (0, 0)),
            *[lead(half, LANES)] * 2,
        ],
        out_shape=[
            sds((slots, width), bf16),
            sds((slots, width), bf16),
            sds((slots, hidden), bf16),
            sds((2, slots, hidden), bf16),
            *[sds((groups, half, width), bf16)] * 2,
            *[sds((groups, half, LANES), bf16)] * 2,
            sds((3 * shared_cols, width), f32),
            *[sds((groups, half, LANES), f32)] * 2,
        ],
        compiler_params=pltpu.CompilerParams(vmem_limit_bytes=58 * 1024 * 1024),
        cost_estimate=pl.CostEstimate(
            flops=rows_cost, bytes_accessed=20 * groups * half * width, transcendentals=0
        ),
    )(
        me,
        hn_own,
        hn_other,
        dy_own,
        dy_other,
        meta_own,
        meta_other,
        gate_up_w,
        down_w,
        first_w,
        sdown_w,
    )


def swap_halves(value, lane):
    low = lane % DR < DR // 2
    return jnp.where(low, pltpu.roll(value, LANES - DR // 2, 1), pltpu.roll(value, DR // 2, 1))


def by_core(core, first, second):
    return jnp.where(core == 0, first, second), jnp.where(core == 0, second, first)


def head_scores(q, kv, k_rope, visible, lane, head, heads):
    q_nope = q[:, head * DN : (head + 1) * DN]
    q_rope = jnp.where(lane // DR == head, q[:, heads * DN :], jnp.zeros((), q.dtype))
    at = head * (DN + DV)
    k_nope, value = kv[:, at : at + DN], kv[:, at + DN : at + DN + DV]
    scores = (dot_nt(q_nope, k_nope) + dot_nt(q_rope, k_rope)) * (DN + DR) ** -0.5
    return jnp.where(visible, scores, NEGATIVE), q_nope, q_rope, k_nope, value


def seen(doc_col, doc_row):
    rows = doc_col.shape[0]
    later = lax.broadcasted_iota(jnp.int32, (rows, rows), 0) >= lax.broadcasted_iota(
        jnp.int32, (rows, rows), 1
    )
    return (doc_col == doc_row) & later


def attention_kernel(
    heads,
    rank,
    core_ref,
    x_own,
    x_other,
    gain,
    latent_gain,
    head_w,
    small_w,
    kv_w,
    cosine,
    sine,
    doc_col,
    doc_row,
    normed_out,
    compressed_out,
    q_out,
    kv_out,
    k_rope_out,
    sums_out,
    attended_out,
    latent_out,
    part_own_out,
    part_other_out,
):
    f32, bf16 = jnp.float32, jnp.bfloat16
    core = core_ref[0]
    x = jnp.concatenate(by_core(core, x_own[0], x_other[0]), axis=0).astype(f32)
    rows = x.shape[0]
    half = rows // 2
    lane = lax.broadcasted_iota(jnp.int32, (rows, LANES), 1)
    inverse = lax.rsqrt(jnp.mean(x * x, axis=1, keepdims=True) + EPSILON)
    normed = (x * inverse * gain[...]).astype(bf16)
    normed_out[0] = normed
    q_cols = heads * (DN + DR)
    queries = dot_nn(normed, head_w[:, :q_cols])
    q_rope = queries[:, heads * DN :]
    q_rope = q_rope * cosine[0] + swap_halves(q_rope, lane) * sine[0]
    q = jnp.concatenate([queries[:, : heads * DN], q_rope], axis=1).astype(bf16)
    q_out[0] = q
    latent = dot_nn(normed, small_w[:, : rank + LANES])
    latent_out[0] = latent
    squeezed = latent[:, :rank]
    inverse = lax.rsqrt(jnp.mean(squeezed * squeezed, axis=1, keepdims=True) + EPSILON)
    compressed = (squeezed * inverse * latent_gain[...]).astype(bf16)
    compressed_out[0] = compressed
    k_rope = latent[:, rank:]
    k_rope = (k_rope * cosine[0] + swap_halves(k_rope, lane) * sine[0]).astype(bf16)
    k_rope_out[0] = k_rope
    kv = dot_nn(compressed, kv_w[...]).astype(bf16)
    kv_out[0] = kv
    visible = seen(doc_col[0], doc_row[0])
    attended, sums = [], jnp.zeros((rows, LANES), f32)
    for head in range(heads):
        scores, *_, value = head_scores(q, kv, k_rope, visible, lane, head, heads)
        top = jnp.max(scores, axis=1, keepdims=True)
        log_total = top + jnp.log(jnp.sum(jnp.exp(scores - top), axis=1, keepdims=True))
        sums = jnp.where(lane == head, log_total, sums)
        probs = jnp.exp(scores - log_total).astype(bf16)
        attended.append(dot_nn(probs, value).astype(bf16))
    sums_out[0] = sums
    attended = jnp.concatenate(attended, axis=1)
    attended_out[0] = attended
    part = dot_nt(attended, head_w[:, q_cols : q_cols + heads * DV]).astype(bf16)
    part_own_out[0], part_other_out[0] = by_core(core, part[:half], part[half:])


def attention_backward_kernel(
    heads,
    core_ref,
    d_own,
    d_other,
    normed_ref,
    compressed_ref,
    q_ref,
    kv_ref,
    k_rope_ref,
    sums_ref,
    attended_ref,
    head_w,
    kv_w,
    cosine,
    sine,
    doc_col,
    doc_row,
    head_grad_out,
    kv_grad_out,
    normed_own_out,
    normed_other_out,
    latent_own_out,
    latent_other_out,
    head_acc,
    kv_acc,
):
    f32, bf16 = jnp.float32, jnp.bfloat16
    core, step = core_ref[0], pl.program_id(0)
    scale = (DN + DR) ** -0.5
    d_rows = jnp.concatenate(by_core(core, d_own[0], d_other[0]), axis=0)
    rows = d_rows.shape[0]
    half = rows // 2
    lane = lax.broadcasted_iota(jnp.int32, (rows, LANES), 1)
    q_cols = heads * (DN + DR)
    q, kv, k_rope = q_ref[0], kv_ref[0], k_rope_ref[0]
    d_attended = dot_nn(d_rows, head_w[:, q_cols : q_cols + heads * DV]).astype(bf16)
    visible = seen(doc_col[0], doc_row[0])
    d_q, d_kv = [], []
    d_q_rope, d_k_rope = jnp.zeros((rows, LANES), f32), jnp.zeros((rows, LANES), f32)
    for head in range(heads):
        scores, q_nope, q_rope, k_nope, value = head_scores(
            q, kv, k_rope, visible, lane, head, heads
        )
        probs = jnp.exp(scores - sums_ref[0][:, head : head + 1])
        d_head = d_attended[:, head * DV : (head + 1) * DV]
        d_probs = dot_nt(d_head, value)
        d_value = dot_tn(probs.astype(bf16), d_head)
        delta = jnp.sum(probs * d_probs, axis=1, keepdims=True)
        d_scores = (probs * (d_probs - delta)).astype(bf16)
        d_q.append(dot_nn(d_scores, k_nope) * scale)
        d_q_rope = jnp.where(lane // DR == head, dot_nn(d_scores, k_rope) * scale, d_q_rope)
        d_kv += [dot_tn(d_scores, q_nope) * scale, d_value]
        d_k_rope += dot_tn(d_scores, q_rope) * scale
    d_q_rope = d_q_rope * cosine[0] - swap_halves(d_q_rope, lane) * sine[0]
    d_q = jnp.concatenate(d_q + [d_q_rope], axis=1).astype(bf16)
    d_kv = jnp.concatenate(d_kv, axis=1).astype(bf16)

    @pl.when(step == 0)
    def _():
        head_acc[...] = jnp.zeros_like(head_acc)
        kv_acc[...] = jnp.zeros_like(kv_acc)

    head_acc[:, :q_cols] += dot_tn(normed_ref[0], d_q)
    head_acc[:, q_cols:] += dot_tn(d_rows, attended_ref[0])
    kv_acc[...] += dot_tn(compressed_ref[0], d_kv)

    @pl.when(step == pl.num_programs(0) - 1)
    def _():
        head_grad_out[...] = head_acc[...].astype(bf16)
        kv_grad_out[...] = kv_acc[...].astype(bf16)

    part = dot_nt(d_q, head_w[:, :q_cols]).astype(bf16)
    normed_own_out[0], normed_other_out[0] = by_core(core, part[:half], part[half:])
    latent = jnp.concatenate([dot_nt(d_kv, kv_w[...]), d_k_rope], axis=1).astype(bf16)
    latent_own_out[0], latent_other_out[0] = by_core(core, latent[:half], latent[half:])


def one_each(*tail):
    return pl.BlockSpec((1, *tail), lambda i: (i,) + (0,) * len(tail))


def kept(value):
    return pl.BlockSpec(value.shape, lambda i: (0,) * value.ndim, pipeline_mode=pl.Buffered(1))


def attention(core, x_own, x_other, gain, latent_gain, head_w, small_w, kv_w, cosine, sine, doc):
    near, half, width = x_own.shape
    rows = 2 * half
    rank, kv_cols = kv_w.shape
    heads = kv_cols // (DN + DV)
    f32, bf16 = jnp.float32, jnp.bfloat16
    shapes = [
        ((rows, width), bf16),
        ((rows, rank), bf16),
        ((rows, heads * (DN + DR)), bf16),
        ((rows, kv_cols), bf16),
        ((rows, LANES), bf16),
        ((rows, LANES), f32),
        ((rows, heads * DV), bf16),
        ((rows, rank + LANES), f32),
        ((half, width), bf16),
        ((half, width), bf16),
    ]
    return pl.pallas_call(
        functools.partial(attention_kernel, heads, rank),
        grid=(near,),
        in_specs=[
            pl.BlockSpec(memory_space=pltpu.SMEM),
            *[one_each(half, width)] * 2,
            *[kept(a) for a in (gain, latent_gain, head_w, small_w, kv_w)],
            *[one_each(rows, LANES)] * 2,
            one_each(rows, 1),
            one_each(1, rows),
        ],
        out_specs=[one_each(*shape) for shape, _ in shapes],
        out_shape=[jax.ShapeDtypeStruct((near, *shape), kind) for shape, kind in shapes],
        compiler_params=pltpu.CompilerParams(vmem_limit_bytes=58 * 1024 * 1024),
        cost_estimate=pl.CostEstimate(
            flops=2 * near * rows * width * (rank + 3 * heads * DN),
            bytes_accessed=4 * near * rows * width,
            transcendentals=0,
        ),
    )(
        core,
        x_own,
        x_other,
        gain,
        latent_gain,
        head_w,
        small_w,
        kv_w,
        cosine,
        sine,
        doc[:, :, None],
        doc[:, None, :],
    )


def attention_backward(core, d_own, d_other, kept_rows, head_w, kv_w, cosine, sine, doc):
    near, half, width = d_own.shape
    rows = 2 * half
    rank, kv_cols = kv_w.shape
    heads = kv_cols // (DN + DV)
    head_cols = heads * (DN + DR + DV)
    f32, bf16 = jnp.float32, jnp.bfloat16
    sds = jax.ShapeDtypeStruct
    return pl.pallas_call(
        functools.partial(attention_backward_kernel, heads),
        grid=(near,),
        in_specs=[
            pl.BlockSpec(memory_space=pltpu.SMEM),
            *[one_each(half, width)] * 2,
            *[one_each(*v.shape[1:]) for v in kept_rows],
            *[kept(a) for a in (head_w, kv_w)],
            *[one_each(rows, LANES)] * 2,
            one_each(rows, 1),
            one_each(1, rows),
        ],
        out_specs=[
            pl.BlockSpec((width, head_cols), lambda i: (0, 0)),
            pl.BlockSpec((rank, kv_cols), lambda i: (0, 0)),
            *[one_each(half, width)] * 2,
            *[one_each(half, rank + LANES)] * 2,
        ],
        out_shape=[
            sds((width, head_cols), bf16),
            sds((rank, kv_cols), bf16),
            *[sds((near, half, width), bf16)] * 2,
            *[sds((near, half, rank + LANES), bf16)] * 2,
        ],
        scratch_shapes=[
            pltpu.VMEM((width, head_cols), f32),
            pltpu.VMEM((rank, kv_cols), f32),
        ],
        compiler_params=pltpu.CompilerParams(vmem_limit_bytes=58 * 1024 * 1024),
        cost_estimate=pl.CostEstimate(
            flops=near * rows * width * heads * DN,
            bytes_accessed=2 * near * rows * width,
            transcendentals=0,
        ),
    )(
        core,
        d_own,
        d_other,
        *kept_rows,
        head_w,
        kv_w,
        cosine,
        sine,
        doc[:, :, None],
        doc[:, None, :],
    )


def product_kernel(left_ref, right_ref, out_ref):
    out_ref[0] = dot_tn(left_ref[0], right_ref[...])


def column_products(left, right, tile=512):
    count, rows, height = left.shape
    width = right.shape[1]
    return pl.pallas_call(
        product_kernel,
        grid=(width // tile, count),
        in_specs=[
            pl.BlockSpec((1, rows, height), lambda j, i: (i, 0, 0)),
            pl.BlockSpec((rows, tile), lambda j, i: (0, j)),
        ],
        out_specs=pl.BlockSpec((1, height, tile), lambda j, i: (i, 0, j)),
        out_shape=jax.ShapeDtypeStruct((count, height, width), jnp.float32),
        compiler_params=pltpu.CompilerParams(vmem_limit_bytes=58 * 1024 * 1024),
        cost_estimate=pl.CostEstimate(
            flops=rows * width, bytes_accessed=rows * width, transcendentals=0
        ),
    )(left, right)


def output_kernel(act, sact_own, sact_other, meta_own, meta_other, down_w, sdown_w, own_out, other_out):
    f32, bf16 = jnp.float32, jnp.bfloat16
    count, half, _ = meta_own.shape
    lane = lax.broadcasted_iota(jnp.int32, (2 * half, LANES), 1).astype(f32)
    out = dot_nn(act[...], down_w[...]).astype(bf16)
    for i in range(count):
        meta = jnp.concatenate([meta_own[i], meta_other[i]], axis=0)
        pick = (meta[:, :1] == lane).astype(bf16)
        sact = jnp.concatenate([sact_own[i], sact_other[i]], axis=0)
        here = slice(i * LANES, (i + 1) * LANES)
        rows = (dot_nn(pick, out[here]) + dot_nn(sact, sdown_w[...])).astype(bf16)
        own_out[i], other_out[i] = rows[:half], rows[half:]


def outputs(act, sact_own, sact_other, meta_own, meta_other, down_w, sdown_w, per_step=4):
    groups, half, _ = meta_own.shape
    hidden, width = down_w.shape
    lead, flat, whole = block_specs(per_step)
    return pl.pallas_call(
        output_kernel,
        grid=(groups // per_step,),
        in_specs=[
            flat(hidden),
            *[lead(half, LANES)] * 4,
            *[whole(a) for a in (down_w, sdown_w)],
        ],
        out_specs=[lead(half, width)] * 2,
        out_shape=[jax.ShapeDtypeStruct((groups, half, width), jnp.bfloat16)] * 2,
        compiler_params=pltpu.CompilerParams(vmem_limit_bytes=58 * 1024 * 1024),
        cost_estimate=pl.CostEstimate(
            flops=groups * half * LANES * width,
            bytes_accessed=groups * half * width,
            transcendentals=0,
        ),
    )(act, sact_own, sact_other, meta_own, meta_other, down_w, sdown_w)


def token_plan(
    inputs,
    attn_gain,
    w_query,
    w_latent,
    latent_gain,
    w_kv,
    w_out,
    ffn_gain,
    w_router,
    shared_gate_up,
    shared_down,
    expert_gate_up,
    expert_down,
    lengths,
    routes,
    cotangent,
):
    f32, bf16 = jnp.float32, jnp.bfloat16
    core, me = lax.axis_index("tensor"), lax.axis_index("expert")
    groups = lax.axis_size("expert")
    deep, place, z = groups // PLANE, me % PLANE, me // PLANE
    tok_rows, width = inputs.shape
    half = tok_rows // 2
    own_at, other_at = core * half, (1 - core) * half
    expert_count = w_router.shape[1]
    route_count = routes.shape[1]
    capacity = tok_rows * route_count * 4 // (3 * expert_count)
    shared_cols = shared_gate_up.shape[2] // groups
    latent_cols, rank_width = w_latent.shape[1], latent_gain.shape[0] * groups
    block_rows = w_query.shape[0]
    kv_rows = w_kv.shape[0]

    query_cols = w_query.shape[1] // PLANE
    out_cols = w_out.shape[0] // PLANE
    small = jnp.concatenate(
        [
            w_latent,
            w_latent[:, rank_width:],
            w_router,
            attn_gain[:, None],
            ffn_gain[:, None],
            jnp.pad(latent_gain, (0, block_rows - kv_rows))[:, None],
        ],
        axis=1,
    )
    small_cols = small.shape[1]
    route_half = take_rows(routes, own_at, half).astype(bf16).reshape(block_rows // 2, -1)
    length_col = jnp.pad(lengths[0].astype(bf16), (0, block_rows // 2 - lengths.shape[1]))[:, None]
    route_cols = route_half.shape[1] + 1
    small_half = jnp.concatenate(
        [
            take_rows(small, core * (block_rows // 2), block_rows // 2),
            route_half,
            length_col,
            jnp.zeros((block_rows // 2, -(small_cols + route_cols) % (2 * LANES)), bf16),
        ],
        axis=1,
    )
    packed_cols = small_half.shape[1] // 2
    small_packed = jnp.concatenate([small_half[:, :packed_cols], small_half[:, packed_cols:]])
    kv_cols = w_kv.shape[1] // PLANE
    kv_parts = block_rows // kv_rows
    kv_piece = kv_cols // kv_parts
    w_out_t = w_out.T

    local_heads = query_cols // (DN + DR)

    def by_parts(block):
        heads = [block[:, h * (DN + DR) : (h + 1) * (DN + DR)] for h in range(local_heads)]
        return [h[:, :DN] for h in heads] + [h[:, DN:] for h in heads]

    def quarter(index):
        kv_here = take_rows(w_kv, index * kv_cols, kv_cols, axis=1)
        kv_here = [kv_here[:, p * kv_piece : (p + 1) * kv_piece] for p in range(kv_parts)]
        return jnp.concatenate(
            [
                *by_parts(take_rows(w_query, index * query_cols, query_cols, axis=1)),
                take_rows(w_out_t, index * out_cols, out_cols, axis=1),
                jnp.concatenate(kv_here, axis=0),
            ],
            axis=1,
        )

    near_w = [quarter(place)] + [to_partner(quarter(place ^ r), r) for r in range(1, PLANE)]
    small_line = deep_join(small_packed, deep_pieces(small_packed), z)
    near_w, small_line = tie(near_w, small_line)
    plane_w = jnp.stack(by_place(near_w, place))
    small_sent, x_sent, plane_w = tie(
        small_line.swapaxes(0, 1), take_rows(inputs, own_at, half), plane_w
    )
    small_sent = jnp.stack([small_sent, to_partner(small_sent, 1)])
    small_sent = jnp.concatenate([small_sent, to_partner(small_sent, 2)], axis=0)
    x_sent = jnp.stack([x_sent, to_partner(x_sent, 2)])
    x_came = to_partner(x_sent, 1)
    x_near_own = jnp.stack([x_sent[0], x_came[0], x_sent[1], x_came[1]])
    x_near_other = swap_cores(x_near_own)
    deep_w = deep_hops(plane_w)
    small_parts = [small_sent[r].swapaxes(0, 1) for r in range(PLANE)]
    small_own = jnp.stack(by_place(small_parts, place), axis=1)
    small_own = small_own.reshape(groups, block_rows, packed_cols)
    small_own = jnp.concatenate(
        [small_own[:, : block_rows // 2], small_own[:, block_rows // 2 :]], axis=2
    )
    small_other = swap_cores(small_own)
    small_all = in_order(core, small_own, small_other, axis=1)
    small_all, x_near_other, deep_w = tie(small_all, x_near_other, deep_w)
    head_w = deep_join(plane_w, join_hops(deep_w), z)
    length_at = small_cols + route_cols - 1
    lengths_near = take_rows(small_own, z * PLANE, PLANE)[:, : lengths.shape[1], length_at]
    lengths_near = lengths_near.astype(jnp.int32)
    lengths_near = jnp.stack(by_place([lengths_near[r] for r in range(PLANE)], place))
    shared_rows = jnp.concatenate(
        [shared_gate_up[0].T, shared_gate_up[1].T, shared_down], axis=0
    ).reshape(3, groups, shared_cols, block_rows)
    shared_rows = shared_rows.swapaxes(0, 1).reshape(groups, 3 * shared_cols, block_rows)
    dy_sent, head_w = tie(take_rows(cotangent, own_at, half), head_w)
    dy_own_rows = take_rows(cotangent, own_at, half)
    dy_gather = RowGather(dy_sent)
    dy_came = dy_gather.along()
    head_w = head_w.reshape(groups, block_rows, -1)
    flat_head = head_w.reshape(groups * block_rows, -1)
    at = query_cols + out_cols
    kv_w = head_w[:, :, at : at + kv_piece].reshape(groups, kv_parts, kv_rows, kv_piece)
    kv_w = kv_w.transpose(0, 2, 1, 3).reshape(groups * kv_rows, kv_cols)

    block_index = jnp.arange(groups)
    block_chip = (z - block_index % deep) % deep * PLANE + (place ^ (block_index // deep))
    in_blocks = (block_chip[:, None] == block_index[None, :]).astype(bf16)

    def routes_of(came):
        came = came[:, :, small_cols : small_cols + route_half.shape[1]].reshape(groups, -1)
        came = jnp.dot(in_blocks, came, preferred_element_type=f32)
        return came.astype(jnp.int32).reshape(groups, half, route_count)

    routes_own, routes_other = routes_of(small_own), routes_of(small_other)
    flat_small = small_all.reshape(groups * block_rows, -1)
    latent_w = flat_small[:, :latent_cols]
    at = rank_width + LANES
    router_w = flat_small[:, at : at + expert_count]
    at += expert_count
    gain_one, gain_two = flat_small[:, at], flat_small[:, at + 1]
    latent_g = small_all[:, :kv_rows, at + 2].reshape(-1)

    near_rows = PLANE * tok_rows
    relative, doc = jax.vmap(lambda one: doc_places(one, tok_rows))(lengths_near)
    cosine, sine_tab = rope_tables(relative.reshape(-1), DR)
    cosine, sine_tab = [v.reshape(PLANE, tok_rows, -1) for v in (cosine, sine_tab)]
    rope = (
        jnp.concatenate([cosine] * 4, axis=-1),
        jnp.concatenate([-sine_tab, sine_tab] * 2, axis=-1),
        doc.astype(f32),
    )
    core_index = core.reshape(1).astype(jnp.int32)
    *kept_rows, latent, part_own, part_other = attention(
        core_index,
        x_near_own,
        x_near_other,
        gain_one.astype(f32)[None],
        latent_g.astype(f32)[None],
        flat_head,
        flat_small,
        kv_w,
        *rope,
    )
    normed_b = kept_rows[0].reshape(near_rows, width)

    def sum_heads(own, other):
        both = add_wide(own, swap_cores(other)).astype(bf16)
        return plane_scatter([both[r] for r in range(PLANE)])

    attn_own = sum_heads(part_own, part_other)
    x_own = take_rows(inputs, own_at, half).astype(f32)
    hidden = x_own + attn_own
    hnormed, scale_two = rms_forward(hidden, gain_two.astype(f32))
    hnormed_b = hnormed.astype(bf16)
    normed_cols = jnp.concatenate(
        [
            take_rows(normed_b, (k * PLANE + place) * block_rows, block_rows, axis=1)
            for k in range(deep)
        ],
        axis=1,
    )
    hnormed_b, dy_came, normed_cols, shared_rows = tie(
        hnormed_b, dy_came, normed_cols, shared_rows
    )
    dy_lines = dy_gather.lines(dy_came)
    def membership(named):
        one_hot = named[..., None] == jnp.arange(expert_count, dtype=jnp.int32)
        return jnp.any(named == me, axis=-1), jnp.any(one_hot, axis=2)

    member_own, hot_own = membership(routes_own)
    member_other, hot_other = membership(routes_other)
    lower = (
        jnp.arange(half, dtype=jnp.int32)[:, None] <= jnp.arange(half, dtype=jnp.int32)[None, :]
    ).astype(bf16)

    def running(mask):
        counts = jnp.dot(mask.astype(bf16), lower, preferred_element_type=f32)
        return counts.astype(jnp.int32)

    count_own, count_other = running(member_own), running(member_other)
    place_own = jnp.where(member_own, count_own - 1, -1)
    place_other = jnp.where(member_other, count_own[:, -1:] + count_other - 1, -1)

    def metadata(slot, hot):
        return jnp.concatenate(
            [
                slot[..., None].astype(f32),
                jnp.zeros((groups, half, shared_cols - 1), f32),
                hot.astype(f32),
                jnp.zeros((groups, half, LANES - shared_cols - expert_count), f32),
            ],
            axis=-1,
        )

    meta_own, meta_other = metadata(place_own, hot_own), metadata(place_other, hot_other)
    hn_gather = RowGather(hnormed_b)
    hn_came, dy_halves, shared_rows = tie(
        hn_gather.along(),
        dy_gather.over_again(dy_lines, dy_gather.over(dy_lines)),
        shared_rows,
    )
    hn_lines, dy_halves, shared_rows = tie(hn_gather.lines(hn_came), dy_halves, shared_rows)
    dy_own = dy_gather.whole(dy_halves)
    hn_over, dy_own, shared_rows = tie(hn_gather.over(hn_lines), dy_own, shared_rows)
    hn_halves = hn_gather.over_again(hn_lines, hn_over)
    shared_w = lax.all_to_all(shared_rows, "expert", split_axis=0, concat_axis=0, tiled=True)
    dy_other = swap_cores(dy_own)
    hn_halves, shared_w, dy_other, meta_own, meta_other = tie(
        hn_halves, shared_w, dy_other, meta_own, meta_other
    )
    shared_w = shared_w.swapaxes(0, 1).reshape(3 * shared_cols, groups * block_rows)
    hn_own = hn_gather.whole(hn_halves)


    first_w = jnp.concatenate(
        [
            shared_w[:shared_cols],
            router_w.T,
            jnp.zeros((LANES - shared_cols - expert_count, width), bf16),
            shared_w[shared_cols : 2 * shared_cols],
            jnp.zeros((LANES - shared_cols, width), bf16),
        ],
        axis=0,
    )
    sdown_rows = jnp.pad(shared_w[2 * shared_cols :], ((0, LANES - shared_cols), (0, 0)))
    hn_other = swap_cores(hn_own)
    gate_up_w, down_w = jnp.swapaxes(expert_gate_up[0], 1, 2), expert_down[0]
    (
        slot_rows,
        slot_dy,
        slot_act,
        d_gate_up,
        d_rows_own,
        d_rows_other,
        act_own,
        act_other,
        shared_grads,
        dgate_own,
        dgate_other,
    ) = experts(
        me.reshape(1).astype(jnp.int32),
        hn_own,
        hn_other,
        dy_own,
        dy_other,
        meta_own,
        meta_other,
        gate_up_w,
        down_w,
        first_w,
        sdown_rows,
        shared_cols,
        expert_count,
    )
    d_rows_came = swap_cores(d_rows_other)

    def two_parts(value):
        return value[..., 0] + value[..., 1]

    dgate_sent = two_parts(dgate_own) + swap_cores(two_parts(dgate_other))
    dgate_high = dgate_sent.astype(bf16)
    dgate_low = (dgate_sent - dgate_high.astype(f32)).astype(bf16)
    out_own, out_other = outputs(
        slot_act, act_own, act_other, meta_own, meta_other, down_w, sdown_rows
    )
    d_rows_came, dgate_high, dgate_low, out_other = tie(
        d_rows_came, dgate_high, dgate_low, out_other
    )
    d_sum = RowSum(d_rows_own, d_rows_came)
    sends, shared_grads, slot_act, out_other = tie(
        d_sum.sends(), shared_grads, slot_act, out_other
    )
    came = d_sum.move(sends)
    gate_rows = [contract_rows(in_blocks, v) for v in (dgate_high, dgate_low)]
    dgate = lax.all_to_all(add_wide(*gate_rows), "expert", split_axis=0, concat_axis=0, tiled=True)
    dgate = dgate.T
    out_came = swap_cores(out_other)
    edown_grad = column_products(slot_act[None], slot_dy)[0]
    came, out_came, edown_grad, dgate = tie(came, out_came, edown_grad, dgate)
    sends, slot_rows, out_came = tie(d_sum.sends_again(came), slot_rows, out_came)
    came_again = d_sum.move_again(sends)
    egu_grad = column_products(d_gate_up, slot_rows).swapaxes(1, 2)
    out_sum = RowSum(out_own, out_came)
    out_sends = out_sum.sends()
    came_again, egu_grad, out_sends = tie(came_again, egu_grad, out_sends)
    z_sends, out_sends, dgate = tie(
        line_sends(d_sum.line(came, came_again)), out_sends, dgate
    )
    z_came = line_move(z_sends)
    out_first = out_sum.move(out_sends)
    hot_mine = take_rows(
        jnp.any(routes[..., None] == jnp.arange(expert_count, dtype=jnp.int32), axis=1), own_at, half
    )
    sig = jax.nn.sigmoid(jnp.dot(hnormed_b, router_w, preferred_element_type=f32))
    chosen = jnp.where(hot_mine, sig, 0.0)
    chosen_sum = jnp.sum(chosen, axis=1, keepdims=True)
    dgate = jnp.where(hot_mine, dgate, 0.0)
    inner = jnp.sum(dgate * chosen, axis=1, keepdims=True)
    d_chosen = ROUTE_SCALE * (dgate / chosen_sum - inner / (chosen_sum * chosen_sum))
    d_logits = (jnp.where(hot_mine, d_chosen, 0.0) * sig * (1.0 - sig)).astype(bf16)
    router_grad = contract_rows(d_logits, hnormed_b)
    z_came, d_logits, router_grad = tie(z_came, d_logits, router_grad)
    d_hn = add_wide(*z_came)
    d_hn = d_hn + contract_cols(d_logits, router_w)
    d_hidden_norm, gain_two_grad = rms_backward(hidden, scale_two, gain_two.astype(f32), d_hn)
    d_hidden = dy_own_rows.astype(f32) + d_hidden_norm
    d_hidden_b, shared_grads = tie(d_hidden.astype(bf16), shared_grads)
    d_parts, out_first = tie(plane_gather(d_hidden_b), out_first)
    d_near_own = jnp.stack(d_parts)
    d_near_other = swap_cores(d_near_own)
    grads_sent = shared_grads.astype(bf16).reshape(-1, groups, block_rows)
    grads_came = lax.all_to_all(grads_sent, "expert", split_axis=1, concat_axis=1, tiled=True)
    out_sends, d_near_other = tie(out_sum.sends_again(out_first), d_near_other)
    out_second = out_sum.move_again(out_sends)

    (
        head_grad,
        kv_grad,
        normed_part_own,
        normed_part_other,
        latent_part_own,
        latent_part_other,
    ) = attention_backward(
        core_index, d_near_own, d_near_other, kept_rows, flat_head, kv_w, *rope
    )
    kv_grad = kv_grad.reshape(groups, kv_rows, kv_parts, kv_piece).transpose(0, 2, 1, 3)
    head_grad = jnp.concatenate([head_grad, kv_grad.reshape(-1, kv_piece)], axis=1)
    head_blocks = head_grad.reshape(deep, -1, head_grad.shape[1])
    head_came = hop_sum(lambda t: at_index(head_blocks, 0, t))
    grad_both = sum_heads(latent_part_own, latent_part_other)
    grad_rope = grad_both[:, rank_width : rank_width + DR] + grad_both[:, rank_width + DR :]
    latent_own = take_rows(latent[0], own_at, half)
    cosine_own = take_rows(cosine[0], own_at, half)
    sine_own = take_rows(sine_tab[0], own_at, half)
    _, scale_kv = rms_forward(latent_own[:, :rank_width], latent_g.astype(f32))
    grad_c, latent_gain_grad = rms_backward(
        latent_own[:, :rank_width], scale_kv, latent_g.astype(f32), grad_both[:, :rank_width]
    )
    grad_latent = jnp.concatenate(
        [grad_c, unrotate(grad_rope, cosine_own, sine_own)], axis=-1
    ).astype(bf16)
    latent_near_own = jnp.stack(plane_gather(grad_latent))
    latent_near = in_order(core, latent_near_own, swap_cores(latent_near_own), axis=1)
    grad_normed = sum_heads(normed_part_own, normed_part_other)
    out_line = out_sum.line(out_first, out_second)
    out_z = hop_sum(lambda t: at_index(out_line, 0, (z - t) % deep))
    head_came, latent_near, grad_normed, out_z, grads_came = tie(
        head_came, latent_near, grad_normed, out_z, grads_came
    )
    latent_cut = latent_cols // 2
    latent_near = latent_near.reshape(near_rows, latent_cols)
    latent_blocks = contract_rows(
        normed_cols,
        take_rows(latent_near, core * latent_cut, latent_cut, axis=1),
    )
    latent_half = deep_scatter(latent_blocks.astype(bf16).reshape(deep, -1, latent_cut), z)
    w_latent_grad = in_order(core, latent_half, swap_cores(latent_half), axis=1)

    head_sums = add_wide(*head_came).astype(bf16).reshape(PLANE, block_rows, -1)
    head_shared = share_columns(head_sums, place)

    def by_heads(block):
        rotary = local_heads * DN
        return [
            part
            for h in range(local_heads)
            for part in (
                block[:, h * DN : (h + 1) * DN],
                block[:, rotary + h * DR : rotary + (h + 1) * DR],
            )
        ]

    at_kv = query_cols + out_cols
    w_query_grad = jnp.concatenate([v for p in head_shared for v in by_heads(p)], axis=1)
    w_query_grad = w_query_grad.astype(f32)
    w_kv_grad = jnp.concatenate(
        [
            p[q * kv_rows : (q + 1) * kv_rows, at_kv:]
            for p in head_shared
            for q in range(kv_parts)
        ],
        axis=1,
    ).astype(f32)
    w_out_grad = jnp.concatenate([p[:, query_cols:at_kv] for p in head_shared], axis=1)
    w_out_grad = w_out_grad.astype(f32).T
    sgu_out = grads_came[: 2 * shared_cols].astype(f32)
    sgu_out = sgu_out.reshape(2, shared_cols, groups, block_rows)
    sgu_out = sgu_out.transpose(0, 3, 2, 1).reshape(2, block_rows, -1)
    sdown_out = grads_came[2 * shared_cols :].astype(f32).swapaxes(0, 1).reshape(-1, block_rows)
    grad_normed = grad_normed + contract_cols(grad_latent, latent_w)
    moe_own = add_wide(*out_z)
    mixed_own = (hidden + moe_own).astype(bf16)
    mixed = in_order(core, mixed_own, swap_cores(mixed_own))

    _, scale_own = rms_forward(x_own, gain_one.astype(f32))
    grad_x_norm, gain_one_grad = rms_backward(x_own, scale_own, gain_one.astype(f32), grad_normed)
    input_own = d_hidden + grad_x_norm
    input_grad = in_order(core, input_own, swap_cores(input_own))

    gain_lanes = jnp.pad(
        latent_gain_grad.reshape(groups, kv_rows), ((0, 0), (0, block_rows - kv_rows))
    )
    vectors = jnp.concatenate(
        [
            router_grad,
            gain_one_grad[None],
            gain_two_grad[None],
            gain_lanes.reshape(1, -1),
        ],
        axis=0,
    ).reshape(-1, groups, block_rows)
    arrived = lax.all_to_all(vectors, "expert", split_axis=1, concat_axis=1, tiled=True)
    sums = jnp.sum(arrived, axis=1)
    sums = sums + swap_cores(sums)
    return (
        mixed,
        input_grad,
        sums[expert_count],
        w_query_grad,
        w_latent_grad,
        sums[expert_count + 2, :kv_rows],
        w_kv_grad,
        w_out_grad,
        sums[expert_count + 1],
        sums[:expert_count].T,
        sgu_out,
        sdown_out,
        egu_grad[None],
        edown_grad[None],
    )


def solution(mesh):
    groups = mesh.shape["expert"]
    plan = token_plan if groups <= 16 else weight_plan
    return jax.shard_map(
        plan,
        mesh=mesh,
        in_specs=(
            P("expert", None),
            P("expert"),
            P("expert", "tensor"),
            P("expert", None),
            P("expert"),
            P("expert", "tensor"),
            P("tensor", "expert"),
            P("expert"),
            P("expert", None),
            P(None, "expert", "tensor"),
            P("tensor", "expert"),
            P("expert", None, None, "tensor"),
            P("expert", "tensor", None),
            P("expert", None),
            P("expert", None),
            P("expert", None),
        ),
        out_specs=(
            P("expert", None),
            P("expert", None),
            P("expert"),
            P("expert", "tensor"),
            P("expert", None),
            P("expert"),
            P("expert", "tensor"),
            P("tensor", "expert"),
            P("expert"),
            P("expert", None),
            P(None, "expert", "tensor"),
            P("tensor", "expert"),
            P("expert", None, None, "tensor"),
            P("expert", "tensor", None),
        ),
        check_vma=False,
    )
```

```python
import functools

import jax
import jax.numpy as jnp
from jax import lax
from jax.experimental import pallas as pl
from jax.experimental.pallas import tpu as pltpu
from jax.sharding import PartitionSpec as P

DN = 128
DR = 64
DV = 128
LANES = 128


EPSILON = 1e-06
ROUTE_SCALE = 2.446
ROPE_BASE = 50000.0
NEGATIVE = -1e30


def cut_along(value, dim, length):
    before, after = (value.shape[:dim], value.shape[dim + 1 :])
    return jnp.moveaxis(value.reshape(*before, length, -1, *after), dim, 0)


def summed_on_arrival(value, axis, dim):
    length = lax.axis_size(axis)
    tiles = lax.all_to_all(cut_along(value, dim, length), axis, 0, 0, tiled=True)
    return jnp.sum(tiles.astype(jnp.float32), axis=0)


def sent_together(arrays, axis, dim, along):
    columns = [a.reshape(*a.shape[:along], -1) for a in arrays]
    both = jnp.concatenate(columns, axis=along)
    whole, at, outs = (summed_on_arrival(both, axis, dim), 0, [])
    for a, column in zip(arrays, columns):
        slab = whole[..., at : at + column.shape[along]]
        outs.append(slab.reshape(*slab.shape[:along], *a.shape[along:]))
        at += column.shape[along]
    return tuple(outs)


def contract_rows(left_arr, right_arr):
    return lax.dot_general(
        left_arr, right_arr, (((0,), (0,)), ((), ())), preferred_element_type=jnp.float32
    )


def contract_cols(left_arr, right_arr):
    return lax.dot_general(
        left_arr, right_arr, (((1,), (1,)), ((), ())), preferred_element_type=jnp.float32
    )


def rms_forward(rows_in, gain_vec):
    inverse = lax.rsqrt(jnp.mean(rows_in * rows_in, axis=-1, keepdims=True) + EPSILON)
    return (rows_in * inverse * gain_vec, inverse)


def rms_backward(rows_in, inverse, gain_vec, grad_out):
    gain_grad = jnp.sum(grad_out * rows_in * inverse, axis=0)
    weighted = grad_out * gain_vec
    inner_mean = jnp.mean(weighted * rows_in, axis=-1, keepdims=True)
    return (inverse * weighted - rows_in * inverse * inverse * inverse * inner_mean, gain_grad)


def doc_layout(doc_lengths, row_count):
    ends_at = jnp.cumsum(doc_lengths)
    starts_at = ends_at - doc_lengths
    position = jnp.arange(row_count, dtype=jnp.int32)
    doc_ids = jnp.sum((position[:, None] >= ends_at[None, :]).astype(jnp.int32), axis=1)
    hitting = doc_ids[:, None] == jnp.arange(doc_lengths.shape[0], dtype=jnp.int32)[None, :]
    start_of = jnp.sum(jnp.where(hitting, starts_at[None, :], 0), axis=1)
    relative = position - start_of
    visible = (doc_ids[:, None] == doc_ids[None, :]) & (position[:, None] >= position[None, :])
    return (relative, visible)


def rope_tables(relative, rot_width):
    counter = jnp.arange(rot_width // 2, dtype=jnp.float32)
    frequency = ROPE_BASE ** (-2.0 * counter / rot_width)
    angles = relative.astype(jnp.float32)[:, None] * frequency[None, :]
    return (jnp.cos(angles), jnp.sin(angles))


def rotate(tensor_in, cosine, sine_tab):
    half_width = tensor_in.shape[-1] // 2
    leading = tensor_in[..., :half_width]
    trailing = tensor_in[..., half_width:]
    return jnp.concatenate(
        [leading * cosine - trailing * sine_tab, trailing * cosine + leading * sine_tab], axis=-1
    )


def unrotate(grad_in, cosine, sine_tab):
    half_width = grad_in.shape[-1] // 2
    leading = grad_in[..., :half_width]
    trailing = grad_in[..., half_width:]
    return jnp.concatenate(
        [leading * cosine + trailing * sine_tab, trailing * cosine - leading * sine_tab], axis=-1
    )


def gated_linear_backward(gate_in, up_in, grad_act):
    sigmoid_g = jax.nn.sigmoid(gate_in)
    grad_gate = grad_act * up_in * sigmoid_g * (1.0 + gate_in * (1.0 - sigmoid_g))
    return (grad_gate, grad_act * gate_in * sigmoid_g)


def slot_tables(route_rows, expert_count, capacity):
    flat_routes = route_rows.reshape(-1)
    one_hot = (flat_routes[:, None] == jnp.arange(expert_count, dtype=jnp.int32)[None, :]).astype(
        jnp.int32
    )
    ranking = jnp.sum((jnp.cumsum(one_hot, axis=0) - one_hot) * one_hot, axis=1)
    slot_ids = flat_routes * capacity + ranking
    row_total = flat_routes.shape[0]
    source = (
        jnp.zeros((expert_count * capacity,), jnp.int32)
        .at[slot_ids]
        .set(jnp.arange(row_total, dtype=jnp.int32))
    )
    filled = jnp.zeros((expert_count * capacity,), jnp.int32).at[slot_ids].set(1)
    return (slot_ids, source, filled)


def to_owner(rows_in):
    arrived = lax.all_to_all(rows_in, "expert", split_axis=0, concat_axis=1, tiled=True)
    return arrived


def weight_plan(
    inputs,
    attn_gain,
    w_query,
    w_latent,
    latent_gain,
    w_kv,
    w_out,
    ffn_gain,
    w_router,
    shared_gate_up,
    shared_down,
    expert_gate_up,
    expert_down,
    lengths,
    routes,
    cotangent,
):
    tok_rows = inputs.shape[0]
    model_width = inputs.shape[1]
    expert_count = w_router.shape[1]
    route_count = routes.shape[1]
    capacity = tok_rows * route_count * 4 // (3 * expert_count)
    brain_float16 = jnp.bfloat16
    f32 = jnp.float32
    gathered = (
        lax.all_gather(attn_gain, "expert", axis=0, tiled=True),
        lax.all_gather(w_query, "expert", axis=0, tiled=True),
        lax.all_gather(w_latent, "expert", axis=0, tiled=True),
        lax.all_gather(latent_gain, "expert", axis=0, tiled=True),
        lax.all_gather(w_kv, "expert", axis=0, tiled=True),
        lax.all_gather(w_out, "expert", axis=1, tiled=True),
        lax.all_gather(ffn_gain, "expert", axis=0, tiled=True),
        lax.all_gather(w_router, "expert", axis=0, tiled=True),
        lax.all_gather(shared_gate_up, "expert", axis=1, tiled=True),
        lax.all_gather(shared_down, "expert", axis=1, tiled=True),
    )
    gain_one, query_w, latent_w, latent_g, kv_w, out_w, gain_two, router_w, sgate_up, sdown_w = (
        gathered
    )
    local_heads = query_w.shape[1] // (DN + DR)
    rank_width = latent_g.shape[0]
    x_float = inputs.astype(f32)
    relative, visible = doc_layout(lengths[0], tok_rows)
    cosine, sine_tab = rope_tables(relative, DR)
    q_scale = (DN + DR) ** (-0.5)
    normed, scale_one = rms_forward(x_float, gain_one.astype(f32))
    normed_b = normed.astype(brain_float16)
    queries = jnp.dot(normed_b, query_w, preferred_element_type=f32).reshape(
        tok_rows, local_heads, DN + DR
    )
    q_rot = rotate(queries[..., DN:], cosine[:, None, :], sine_tab[:, None, :])
    q_all = jnp.concatenate([queries[..., :DN], q_rot], axis=-1).astype(brain_float16)
    latent = jnp.dot(normed_b, latent_w, preferred_element_type=f32)
    compressed, scale_kv = rms_forward(latent[:, :rank_width], latent_g.astype(f32))
    compressed_b = compressed.astype(brain_float16)
    k_rope = rotate(latent[:, rank_width:], cosine, sine_tab).astype(brain_float16)
    kv_all = jnp.dot(compressed_b, kv_w, preferred_element_type=f32).reshape(
        tok_rows, local_heads, DN + DV
    )
    k_nope = kv_all[..., :DN].astype(brain_float16)
    values = kv_all[..., DN:].astype(brain_float16)
    key_all = jnp.concatenate(
        [k_nope, jnp.broadcast_to(k_rope[:, None, :], (tok_rows, local_heads, DR))], axis=-1
    )

    def score_block():
        raw_scores = (
            jnp.einsum("qhd,khd->hqk", q_all, key_all, preferred_element_type=f32) * q_scale
        )
        return jnp.where(visible[None], raw_scores, NEGATIVE)

    scores = score_block()
    top_score = jnp.max(scores, axis=-1, keepdims=True)
    log_total = top_score + jnp.log(jnp.sum(jnp.exp(scores - top_score), axis=-1, keepdims=True))
    probs_b = jnp.exp(scores - log_total).astype(brain_float16)
    attended = jnp.einsum("hqk,khd->qhd", probs_b, values, preferred_element_type=f32)
    attended_b = attended.reshape(tok_rows, local_heads * DV).astype(brain_float16)
    attn = lax.psum(jnp.dot(attended_b, out_w, preferred_element_type=f32), "tensor")
    hidden = x_float + attn
    hnormed, scale_two = rms_forward(hidden, gain_two.astype(f32))
    hnormed_b = hnormed.astype(brain_float16)
    logits = jnp.dot(hnormed_b, router_w, preferred_element_type=f32)
    sigmoid_vals = jax.nn.sigmoid(logits)
    route_hot = routes[:, :, None] == jnp.arange(expert_count, dtype=jnp.int32)[None, None, :]
    chosen = jnp.sum(jnp.where(route_hot, sigmoid_vals[:, None, :], 0.0), axis=2)
    chosen_sum = jnp.sum(chosen, axis=1, keepdims=True)
    gate_vals = ROUTE_SCALE * chosen / chosen_sum
    slot_ids, source, filled = slot_tables(routes, expert_count, capacity)
    is_filled = filled[:, None] == 1
    sent_rows = jnp.where(is_filled, hnormed_b[source // route_count], 0).reshape(
        expert_count, capacity, model_width
    )
    received = to_owner(sent_rows)
    gate_up_joined = jnp.einsum(
        "erd,egdf->egrf", received, expert_gate_up, preferred_element_type=f32
    )
    expert_act = (jax.nn.silu(gate_up_joined[:, 0]) * gate_up_joined[:, 1]).astype(brain_float16)
    expert_res = jnp.einsum(
        "erf,efd->erd", expert_act, expert_down, preferred_element_type=f32
    ).astype(brain_float16)
    returned_all = lax.all_to_all(expert_res, "expert", split_axis=1, concat_axis=0, tiled=True)
    returned = returned_all.reshape(expert_count * capacity, model_width)[slot_ids].reshape(
        tok_rows, route_count, model_width
    )
    shared_gu = jnp.einsum("td,gdf->gtf", hnormed_b, sgate_up, preferred_element_type=f32)
    shared_act = (jax.nn.silu(shared_gu[0]) * shared_gu[1]).astype(brain_float16)
    branch_sum = jnp.dot(shared_act, sdown_w, preferred_element_type=f32)
    for route_idx in range(route_count):
        branch_sum = branch_sum + gate_vals[:, route_idx : route_idx + 1] * returned[
            :, route_idx
        ].astype(f32)
    moe_out = lax.psum(branch_sum.astype(jnp.bfloat16), "tensor").astype(jnp.float32)
    mixed = (hidden + moe_out).astype(brain_float16)
    grad_y = cotangent.astype(f32)
    sdown_grad = contract_rows(shared_act, cotangent)
    grad_sact = contract_cols(cotangent, sdown_w)
    grad_sgate, grad_sup = gated_linear_backward(shared_gu[0], shared_gu[1], grad_sact)
    grad_sgu = jnp.stack([grad_sgate, grad_sup], axis=0).astype(brain_float16)
    sgu_grad = jnp.einsum("td,gtf->gdf", hnormed_b, grad_sgu, preferred_element_type=f32)
    grad_hn_part = jnp.einsum("gtf,gdf->td", grad_sgu, sgate_up, preferred_element_type=f32)
    gate_columns = []
    for route_idx in range(route_count):
        gate_columns.append(jnp.sum(grad_y * returned[:, route_idx].astype(f32), axis=1))
    gate_part = jnp.stack(gate_columns, axis=1)
    slot_grads = (
        (gate_vals[:, :, None] * grad_y[:, None, :])
        .reshape(tok_rows * route_count, model_width)
        .astype(brain_float16)
    )
    grad_sent = jnp.where(is_filled, slot_grads[source], 0).reshape(
        expert_count, capacity, model_width
    )
    grad_received = to_owner(grad_sent)
    edown_grad = jnp.einsum("erf,erd->efd", expert_act, grad_received, preferred_element_type=f32)
    expert_activation_gradient = jnp.einsum(
        "erd,efd->erf", grad_received, expert_down, preferred_element_type=f32
    )
    expert_gate_gradient, expert_up_gradient = gated_linear_backward(
        gate_up_joined[:, 0], gate_up_joined[:, 1], expert_activation_gradient
    )
    expert_gate_up_gradient = jnp.stack([expert_gate_gradient, expert_up_gradient], axis=1).astype(
        brain_float16
    )
    egu_grad = jnp.einsum(
        "erd,egrf->egdf", received, expert_gate_up_gradient, preferred_element_type=f32
    )
    grad_rows = jnp.einsum(
        "egrf,egdf->erd", expert_gate_up_gradient, expert_gate_up, preferred_element_type=f32
    ).astype(brain_float16)
    grad_back = lax.all_to_all(grad_rows, "expert", split_axis=1, concat_axis=0, tiled=True)
    grad_routes = grad_back.reshape(expert_count * capacity, model_width)[slot_ids].reshape(
        tok_rows, route_count, model_width
    )
    for route_idx in range(route_count):
        grad_hn_part = grad_hn_part + grad_routes[:, route_idx].astype(f32)
    gate_grads = lax.psum(gate_part, "tensor")
    grad_chosen = ROUTE_SCALE * (
        gate_grads / chosen_sum
        - jnp.sum(gate_grads * chosen, axis=1, keepdims=True) / (chosen_sum * chosen_sum)
    )
    grad_sig = jnp.sum(jnp.where(route_hot, grad_chosen[:, :, None], 0.0), axis=1)
    grad_logits = (grad_sig * sigmoid_vals * (1.0 - sigmoid_vals)).astype(brain_float16)
    router_grad = contract_rows(hnormed_b, grad_logits)
    grad_hn = lax.psum(grad_hn_part, "tensor") + contract_cols(grad_logits, router_w)
    grad_hidden_norm, gain_two_grad = rms_backward(hidden, scale_two, gain_two.astype(f32), grad_hn)
    grad_hidden = grad_y + grad_hidden_norm
    grad_hidden_b = grad_hidden.astype(brain_float16)
    out_grad = contract_rows(attended_b, grad_hidden_b)
    grad_att = (
        contract_cols(grad_hidden_b, out_w).reshape(tok_rows, local_heads, DV).astype(brain_float16)
    )
    probs = jnp.exp(score_block() - log_total)
    probs_again = probs.astype(brain_float16)
    grad_probs = jnp.einsum("qhd,khd->hqk", grad_att, values, preferred_element_type=f32)
    grad_vals = jnp.einsum("hqk,qhd->khd", probs_again, grad_att, preferred_element_type=f32)
    row_delta = jnp.sum(probs * grad_probs, axis=-1, keepdims=True)
    grad_scores = (probs * (grad_probs - row_delta)).astype(brain_float16)
    grad_q = jnp.einsum("hqk,khd->qhd", grad_scores, key_all, preferred_element_type=f32) * q_scale
    grad_keys = jnp.einsum("hqk,qhd->khd", grad_scores, q_all, preferred_element_type=f32) * q_scale
    grad_kv = (
        jnp.concatenate([grad_keys[..., :DN], grad_vals], axis=-1)
        .reshape(tok_rows, local_heads * (DN + DV))
        .astype(brain_float16)
    )
    kv_grad = contract_rows(compressed_b, grad_kv)
    grad_comp_part = contract_cols(grad_kv, kv_w)
    grad_krope_part = jnp.sum(grad_keys[..., DN:], axis=1)
    grad_comp, grad_krope = (
        lax.psum(grad_comp_part.astype(jnp.bfloat16), "tensor").astype(jnp.float32),
        lax.psum(grad_krope_part.astype(jnp.bfloat16), "tensor").astype(jnp.float32),
    )
    grad_c, latent_gain_grad = rms_backward(
        latent[:, :rank_width], scale_kv, latent_g.astype(f32), grad_comp
    )
    grad_latent = jnp.concatenate([grad_c, unrotate(grad_krope, cosine, sine_tab)], axis=-1).astype(
        brain_float16
    )
    grad_qrot = unrotate(grad_q[..., DN:], cosine[:, None, :], sine_tab[:, None, :])
    grad_queries = (
        jnp.concatenate([grad_q[..., :DN], grad_qrot], axis=-1)
        .reshape(tok_rows, local_heads * (DN + DR))
        .astype(brain_float16)
    )
    query_grad = contract_rows(normed_b, grad_queries)
    latent_grad = contract_rows(normed_b, grad_latent)
    grad_normed = lax.psum(
        contract_cols(grad_queries, query_w).astype(jnp.bfloat16), "tensor"
    ).astype(jnp.float32) + contract_cols(grad_latent, latent_w)
    grad_x_norm, gain_one_grad = rms_backward(x_float, scale_one, gain_one.astype(f32), grad_normed)
    input_grad = grad_hidden + grad_x_norm
    first_owned = (
        *sent_together(
            (
                gain_one_grad.astype(jnp.bfloat16),
                query_grad.astype(jnp.bfloat16),
                latent_grad.astype(jnp.bfloat16),
            ),
            "expert",
            0,
            1,
        ),
        *sent_together(
            (latent_gain_grad.astype(jnp.bfloat16), kv_grad.astype(jnp.bfloat16)), "expert", 0, 1
        ),
    )
    second_owned = (
        lax.psum_scatter(out_grad, "expert", scatter_dimension=1, tiled=True),
        lax.psum_scatter(gain_two_grad, "expert", scatter_dimension=0, tiled=True),
        lax.psum_scatter(router_grad, "expert", scatter_dimension=0, tiled=True),
        lax.psum_scatter(sgu_grad, "expert", scatter_dimension=1, tiled=True),
        lax.psum_scatter(sdown_grad, "expert", scatter_dimension=1, tiled=True),
    )
    return (
        mixed,
        input_grad,
        first_owned[0],
        first_owned[1],
        first_owned[2],
        first_owned[3],
        first_owned[4],
        second_owned[0],
        second_owned[1],
        second_owned[2],
        second_owned[3],
        second_owned[4],
        egu_grad,
        edown_grad,
    )


def swap_cores(value):
    return lax.ppermute(value, "tensor", [(0, 1), (1, 0)])


def take_rows(value, start, count, axis=0):
    return lax.dynamic_slice_in_dim(value, start, count, axis=axis)


def in_order(core, own, other, axis=0):
    return jnp.where(
        core == 0,
        jnp.concatenate([own, other], axis=axis),
        jnp.concatenate([other, own], axis=axis),
    )


def add_wide(*parts):
    total = parts[0].astype(jnp.float32)
    for part in parts[1:]:
        total = total + part.astype(jnp.float32)
    return total


PLANE = 4


def to_partner(value, flips):
    groups = lax.axis_size("expert")
    return lax.ppermute(value, "expert", [(g, g ^ flips) for g in range(groups)])


def to_deeper(value, step):
    groups = lax.axis_size("expert")
    pairs = [(g, (g + step * PLANE) % groups) for g in range(groups)]
    return lax.ppermute(value, "expert", pairs)


def plane_gather(value):
    return [value] + [to_partner(value, r) for r in range(1, PLANE)]


def plane_scatter(parts):
    return add_wide(parts[0], *[to_partner(parts[r], r) for r in range(1, PLANE)])


def by_place(parts, place):
    odd, high = place % 2 == 1, place // 2 == 1
    parts = [jnp.where(odd, parts[i ^ 1], parts[i]) for i in range(PLANE)]
    return [jnp.where(high, parts[i ^ 2], parts[i]) for i in range(PLANE)]


def tie(*values):
    return lax.optimization_barrier(values)


def deep_pieces(value):
    deep = lax.axis_size("expert") // PLANE
    return [to_deeper(value, s) for s in range(1, deep)]


def one_plane(value, step):
    groups = lax.axis_size("expert")
    pairs = [(g, g + step * PLANE) for g in range(groups) if 0 <= g + step * PLANE < groups]
    return lax.ppermute(value, "expert", pairs)


def deep_hops(value):
    deep = lax.axis_size("expert") // PLANE
    after, before, down, up = [], [], value, value
    for _ in range(1, deep):
        down, up = one_plane(down, 1), one_plane(up, -1)
        after.append(down)
        before.append(up)
    return after, before


def join_hops(hops):
    after, before = hops
    return [a + b for a, b in zip(after, before[::-1])]


def deep_join(value, pieces, z):
    deep = lax.axis_size("expert") // PLANE
    whole = jnp.zeros((deep, *value.shape), value.dtype)
    whole = lax.dynamic_update_index_in_dim(whole, value, z, 0)
    for step in range(1, deep):
        whole = lax.dynamic_update_index_in_dim(whole, pieces[step - 1], (z - step) % deep, 0)
    return whole


def deep_move(blocks, z):
    deep = blocks.shape[0]

    def block(index):
        return lax.dynamic_index_in_dim(blocks, index, 0, keepdims=False)

    return [block(z)] + [to_deeper(block((z + step) % deep), step) for step in range(1, deep)]


def deep_scatter(blocks, z):
    return add_wide(*deep_move(blocks, z))


def share_columns(rows, place):
    parts = [at_index(rows, 0, place)]
    for r in range(1, PLANE):
        parts.append(to_partner(at_index(rows, 0, place ^ r), r))
    return by_place(parts, place)


def all_groups(value):
    return lax.all_gather(value, "expert", axis=0, tiled=False)


def at_index(value, axis, index):
    return lax.dynamic_index_in_dim(value, index, axis, keepdims=False)


def doc_places(doc_lengths, row_count):
    ends_at = jnp.cumsum(doc_lengths)
    position = jnp.arange(row_count, dtype=jnp.int32)
    doc_ids = jnp.sum((position[:, None] >= ends_at[None, :]).astype(jnp.int32), axis=1)
    hitting = doc_ids[:, None] == jnp.arange(doc_lengths.shape[0], dtype=jnp.int32)[None, :]
    start_of = jnp.sum(jnp.where(hitting, (ends_at - doc_lengths)[None, :], 0), axis=1)
    return position - start_of, doc_ids


class HopSum:
    def __init__(self, pieces):
        self.groups = lax.axis_size("expert")
        self.deep = self.groups // PLANE
        self.z = lax.axis_index("expert") // PLANE
        self.pieces = pieces

    def hop(self, step, came=None):
        arrived = []
        for side, way in enumerate((1, -1)):
            target = jnp.clip(self.z + way * (self.deep - step), 0, self.deep - 1)
            gone = self.pieces(target)
            if came is not None:
                gone = add_wide(gone, came[side]).astype(gone.dtype)
            first = range(step) if way == 1 else range(self.deep - step, self.deep)
            pairs = [
                (p * PLANE + q, (p + way) * PLANE + q) for p in first for q in range(PLANE)
            ]
            arrived.append(lax.ppermute(gone, "expert", pairs))
        return arrived

    def total(self, came):
        return add_wide(self.pieces(self.z), *came)


def doc_places(doc_lengths, row_count):
    ends_at = jnp.cumsum(doc_lengths)
    position = jnp.arange(row_count, dtype=jnp.int32)
    doc_ids = jnp.sum((position[:, None] >= ends_at[None, :]).astype(jnp.int32), axis=1)
    hitting = doc_ids[:, None] == jnp.arange(doc_lengths.shape[0], dtype=jnp.int32)[None, :]
    start_of = jnp.sum(jnp.where(hitting, (ends_at - doc_lengths)[None, :], 0), axis=1)
    return position - start_of, doc_ids


def hop_sum(pieces):
    groups = lax.axis_size("expert")
    deep = groups // PLANE
    z = lax.axis_index("expert") // PLANE
    ends = []
    for way in (1, -1):
        came = None
        for step in range(1, deep):
            gone = pieces(jnp.clip(z + way * (deep - step), 0, deep - 1))
            if came is not None:
                gone = add_wide(gone, came).astype(gone.dtype)
            first = range(step) if way == 1 else range(deep - step, deep)
            pairs = [
                (p * PLANE + q, (p + way) * PLANE + q) for p in first for q in range(PLANE)
            ]
            came = lax.ppermute(gone, "expert", pairs)
        ends.append(came)
    return [pieces(z), *ends]


class RowGather:
    def __init__(self, value):
        self.cut = value.shape[0] // 2
        self.value = value

    def along(self):
        return [self.value], *deep_hops(self.value)

    def lines(self, came):
        own, *hops = came
        came = own + join_hops(hops)
        return [jnp.stack([v[: self.cut] for v in came]), jnp.stack([v[self.cut :] for v in came])]

    def over(self, lines):
        first, second = lines
        return to_partner(first, 1), to_partner(second, 2)

    def over_again(self, lines, came):
        (first, second), (beside, behind) = lines, came
        return [
            [first, beside, to_partner(first, 2), to_partner(beside, 2)],
            [second, to_partner(second, 1), behind, to_partner(behind, 1)],
        ]

    def whole(self, halves):
        return jnp.concatenate([jnp.concatenate(half, axis=0) for half in halves], axis=1)


class RowSum:
    def __init__(self, *terms):
        groups, rows = terms[0].shape[:2]
        self.type = terms[0].dtype
        cut = rows // 2
        blocks = [v.reshape(PLANE, groups // PLANE, *v.shape[1:]) for v in terms]
        self.halves = (
            ([v[:, :, :cut] for v in blocks], 2, 1),
            ([v[:, :, cut:] for v in blocks], 1, 2),
        )

    def _add(self, parts):
        return add_wide(*parts).astype(self.type)

    def sends(self):
        return [
            jnp.stack([self._add([v[far] for v in held]), self._add([v[far | near] for v in held])])
            for held, far, near in self.halves
        ]

    def move(self, sends):
        return [to_partner(v, far) for v, (_, far, _) in zip(sends, self.halves)]

    def sends_again(self, came):
        return [
            self._add([v[near] for v in held] + [c[1]])
            for c, (held, _, near) in zip(came, self.halves)
        ]

    def move_again(self, sends):
        return [to_partner(v, near) for v, (_, _, near) in zip(sends, self.halves)]

    def line(self, came, came_again):
        sums = [
            self._add([v[0] for v in held] + [c[0], d])
            for c, d, (held, *_) in zip(came, came_again, self.halves)
        ]
        return jnp.concatenate(sums, axis=1)


def line_sends(line):
    return [line[step] for step in range(line.shape[0])]


def line_move(sends):
    return [sends[0]] + [to_deeper(v, -step) for step, v in enumerate(sends) if step > 0]


def dot_nn(left, right):
    return lax.dot_general(left, right, (((1,), (0,)), ((), ())), preferred_element_type=jnp.float32)


def dot_nt(left, right):
    return lax.dot_general(left, right, (((1,), (1,)), ((), ())), preferred_element_type=jnp.float32)


def dot_tn(left, right):
    return lax.dot_general(left, right, (((0,), (0,)), ((), ())), preferred_element_type=jnp.float32)


def two_lanes(column, lane):
    high = column.astype(jnp.bfloat16).astype(jnp.float32)
    spread = jnp.where(lane == 0, high, jnp.where(lane == 1, column - high, 0.0))
    return spread.astype(jnp.bfloat16)


def expert_kernel(
    shared_cols,
    expert_count,
    me_ref,
    hn_own,
    hn_other,
    dy_own,
    dy_other,
    meta_own,
    meta_other,
    gate_up_w,
    down_w,
    first_w,
    sdown_w,
    slots_out,
    slot_dy_out,
    act_out,
    d_gate_up_out,
    rows_own_out,
    rows_other_out,
    sact_own_out,
    sact_other_out,
    shared_grads_out,
    dgate_own_out,
    dgate_other_out,
):
    f32, bf16 = jnp.float32, jnp.bfloat16
    count, half, _ = hn_own.shape
    tokens = 2 * half
    me = me_ref[0]
    lane = lax.broadcasted_iota(jnp.int32, (count * tokens, LANES), 1)
    is_router = (lane >= shared_cols) & (lane < shared_cols + expert_count)
    first = first_w[...]

    def joined(own, other):
        return jnp.concatenate([v[i] for i in range(count) for v in (own, other)], axis=0)

    rows, rows_dy = joined(hn_own, hn_other), joined(dy_own, dy_other)
    meta = joined(meta_own, meta_other)
    products = dot_nt(rows, first)
    gate, up = products[:, :LANES], products[:, LANES:]
    sig = jax.nn.sigmoid(gate)
    total = jnp.sum(jnp.where(is_router, sig * meta, 0.0), axis=1, keepdims=True)
    mine = jnp.sum(jnp.where(lane == shared_cols + me, sig, 0.0), axis=1, keepdims=True)
    token_gate = two_lanes(ROUTE_SCALE * mine / total, lane)
    sact = (gate * sig * up).astype(bf16)
    d_sact = dot_nt(rows_dy, sdown_w[...])
    d_sgate = d_sact * up * sig * (1.0 + gate * (1.0 - sig))
    dsh = jnp.concatenate([d_sgate, d_sact * gate * sig], axis=1).astype(bf16)
    pick = (meta[:, :1] == lane.astype(f32)).astype(bf16)
    groups = [slice(i * tokens, (i + 1) * tokens) for i in range(count)]
    for i in range(count):
        start = i * tokens
        sact_own_out[i] = sact[start : start + half]
        sact_other_out[i] = sact[start + half : start + tokens]
    slots = [dot_tn(pick[g], rows[g]).astype(bf16) for g in groups]
    slot_dys = [dot_tn(pick[g], rows_dy[g]).astype(bf16) for g in groups]
    slot_gates = [
        jnp.sum(dot_tn(pick[g], token_gate[g]), axis=1, keepdims=True) for g in groups
    ]

    @pl.when(pl.program_id(0) == 0)
    def _():
        shared_grads_out[...] = jnp.zeros_like(shared_grads_out)

    first_grad, sdown_grad = dot_tn(dsh, rows), dot_tn(sact, rows_dy)
    shared_grads_out[:shared_cols] += first_grad[:shared_cols]
    shared_grads_out[shared_cols : 2 * shared_cols] += first_grad[LANES : LANES + shared_cols]
    shared_grads_out[2 * shared_cols :] += sdown_grad[:shared_cols]
    slot_rows = jnp.concatenate(slots, axis=0)
    slot_dy = jnp.concatenate(slot_dys, axis=0)
    slot_gate = jnp.concatenate(slot_gates, axis=0)
    slots_out[...] = slot_rows
    slot_dy_out[...] = slot_dy
    gate = dot_nt(slot_rows, gate_up_w[0])
    up = dot_nt(slot_rows, gate_up_w[1])
    d_act = dot_nt(slot_dy, down_w[...])
    sig = jax.nn.sigmoid(gate)
    silu = gate * sig
    act = silu * up
    slot_dgate = jnp.sum(act * d_act, axis=1, keepdims=True)
    act_out[...] = (slot_gate * act).astype(bf16)
    d_act = slot_gate * d_act
    d_gate = (d_act * up * sig * (1.0 + gate * (1.0 - sig))).astype(bf16)
    d_up = (d_act * silu).astype(bf16)
    d_gate_up_out[0] = d_gate
    d_gate_up_out[1] = d_up
    d_slots = (dot_nn(d_gate, gate_up_w[0]) + dot_nn(d_up, gate_up_w[1])).astype(bf16)
    slot_lane = lax.broadcasted_iota(jnp.int32, (LANES, LANES), 1)
    d_shared = dot_nn(dsh, first)
    for i, g in enumerate(groups):
        here = slice(i * LANES, (i + 1) * LANES)
        d_rows = (dot_nn(pick[g], d_slots[here]) + d_shared[g]).astype(bf16)
        rows_own_out[i], rows_other_out[i] = d_rows[:half], d_rows[half:]
        dgate = dot_nn(pick[g], two_lanes(slot_dgate[here], slot_lane))
        dgate_own_out[i], dgate_other_out[i] = dgate[:half], dgate[half:]


def block_specs(per_step):
    def lead(*tail):
        return pl.BlockSpec((per_step, *tail), lambda i: (i,) + (0,) * len(tail))

    def flat(cols):
        return pl.BlockSpec((per_step * LANES, cols), lambda i: (i, 0))

    def whole(a):
        return pl.BlockSpec(a.shape, lambda i: (0,) * a.ndim, pipeline_mode=pl.Buffered(1))

    return lead, flat, whole


def slots_cost(width, hidden, products):
    return LANES * width * hidden * products


def experts(
    me,
    hn_own,
    hn_other,
    dy_own,
    dy_other,
    meta_own,
    meta_other,
    gate_up_w,
    down_w,
    first_w,
    sdown_w,
    shared_cols,
    expert_count,
    per_step=2,
):
    groups, half, width = hn_own.shape
    hidden = down_w.shape[0]
    slots = groups * LANES
    f32, bf16 = jnp.float32, jnp.bfloat16
    lead, flat, whole = block_specs(per_step)
    sds = jax.ShapeDtypeStruct
    rows_cost = 2 * groups * (2 * half * width * 4 * LANES + slots_cost(width, hidden, 5))
    return pl.pallas_call(
        functools.partial(expert_kernel, shared_cols, expert_count),
        grid=(groups // per_step,),
        in_specs=[
            pl.BlockSpec(memory_space=pltpu.SMEM),
            *[lead(half, width)] * 4,
            *[lead(half, LANES)] * 2,
            *[whole(a) for a in (gate_up_w, down_w, first_w, sdown_w)],
        ],
        out_specs=[
            flat(width),
            flat(width),
            flat(hidden),
            pl.BlockSpec((2, per_step * LANES, hidden), lambda i: (0, i, 0)),
            *[lead(half, width)] * 2,
            *[lead(half, LANES)] * 2,
            pl.BlockSpec((3 * shared_cols, width), lambda i: (0, 0)),
            *[lead(half, LANES)] * 2,
        ],
        out_shape=[
            sds((slots, width), bf16),
            sds((slots, width), bf16),
            sds((slots, hidden), bf16),
            sds((2, slots, hidden), bf16),
            *[sds((groups, half, width), bf16)] * 2,
            *[sds((groups, half, LANES), bf16)] * 2,
            sds((3 * shared_cols, width), f32),
            *[sds((groups, half, LANES), f32)] * 2,
        ],
        compiler_params=pltpu.CompilerParams(vmem_limit_bytes=58 * 1024 * 1024),
        cost_estimate=pl.CostEstimate(
            flops=rows_cost, bytes_accessed=20 * groups * half * width, transcendentals=0
        ),
    )(
        me,
        hn_own,
        hn_other,
        dy_own,
        dy_other,
        meta_own,
        meta_other,
        gate_up_w,
        down_w,
        first_w,
        sdown_w,
    )


def swap_halves(value, lane):
    low = lane % DR < DR // 2
    return jnp.where(low, pltpu.roll(value, LANES - DR // 2, 1), pltpu.roll(value, DR // 2, 1))


def by_core(core, first, second):
    return jnp.where(core == 0, first, second), jnp.where(core == 0, second, first)


def head_scores(q, kv, k_rope, visible, lane, head, heads):
    q_nope = q[:, head * DN : (head + 1) * DN]
    q_rope = jnp.where(lane // DR == head, q[:, heads * DN :], jnp.zeros((), q.dtype))
    at = head * (DN + DV)
    k_nope, value = kv[:, at : at + DN], kv[:, at + DN : at + DN + DV]
    scores = (dot_nt(q_nope, k_nope) + dot_nt(q_rope, k_rope)) * (DN + DR) ** -0.5
    return jnp.where(visible, scores, NEGATIVE), q_nope, q_rope, k_nope, value


def seen(doc_col, doc_row):
    rows = doc_col.shape[0]
    later = lax.broadcasted_iota(jnp.int32, (rows, rows), 0) >= lax.broadcasted_iota(
        jnp.int32, (rows, rows), 1
    )
    return (doc_col == doc_row) & later


def attention_kernel(
    heads,
    rank,
    core_ref,
    x_own,
    x_other,
    gain,
    latent_gain,
    head_w,
    small_w,
    kv_w,
    cosine,
    sine,
    doc_col,
    doc_row,
    normed_out,
    compressed_out,
    q_out,
    kv_out,
    k_rope_out,
    sums_out,
    attended_out,
    latent_out,
    part_own_out,
    part_other_out,
):
    f32, bf16 = jnp.float32, jnp.bfloat16
    core = core_ref[0]
    x = jnp.concatenate(by_core(core, x_own[0], x_other[0]), axis=0).astype(f32)
    rows = x.shape[0]
    half = rows // 2
    lane = lax.broadcasted_iota(jnp.int32, (rows, LANES), 1)
    inverse = lax.rsqrt(jnp.mean(x * x, axis=1, keepdims=True) + EPSILON)
    normed = (x * inverse * gain[...]).astype(bf16)
    normed_out[0] = normed
    q_cols = heads * (DN + DR)
    queries = dot_nn(normed, head_w[:, :q_cols])
    q_rope = queries[:, heads * DN :]
    q_rope = q_rope * cosine[0] + swap_halves(q_rope, lane) * sine[0]
    q = jnp.concatenate([queries[:, : heads * DN], q_rope], axis=1).astype(bf16)
    q_out[0] = q
    latent = dot_nn(normed, small_w[:, : rank + LANES])
    latent_out[0] = latent
    squeezed = latent[:, :rank]
    inverse = lax.rsqrt(jnp.mean(squeezed * squeezed, axis=1, keepdims=True) + EPSILON)
    compressed = (squeezed * inverse * latent_gain[...]).astype(bf16)
    compressed_out[0] = compressed
    k_rope = latent[:, rank:]
    k_rope = (k_rope * cosine[0] + swap_halves(k_rope, lane) * sine[0]).astype(bf16)
    k_rope_out[0] = k_rope
    kv = dot_nn(compressed, kv_w[...]).astype(bf16)
    kv_out[0] = kv
    visible = seen(doc_col[0], doc_row[0])
    attended, sums = [], jnp.zeros((rows, LANES), f32)
    for head in range(heads):
        scores, *_, value = head_scores(q, kv, k_rope, visible, lane, head, heads)
        top = jnp.max(scores, axis=1, keepdims=True)
        log_total = top + jnp.log(jnp.sum(jnp.exp(scores - top), axis=1, keepdims=True))
        sums = jnp.where(lane == head, log_total, sums)
        probs = jnp.exp(scores - log_total).astype(bf16)
        attended.append(dot_nn(probs, value).astype(bf16))
    sums_out[0] = sums
    attended = jnp.concatenate(attended, axis=1)
    attended_out[0] = attended
    part = dot_nt(attended, head_w[:, q_cols : q_cols + heads * DV]).astype(bf16)
    part_own_out[0], part_other_out[0] = by_core(core, part[:half], part[half:])


def attention_backward_kernel(
    heads,
    core_ref,
    d_own,
    d_other,
    normed_ref,
    compressed_ref,
    q_ref,
    kv_ref,
    k_rope_ref,
    sums_ref,
    attended_ref,
    head_w,
    kv_w,
    cosine,
    sine,
    doc_col,
    doc_row,
    head_grad_out,
    kv_grad_out,
    normed_own_out,
    normed_other_out,
    latent_own_out,
    latent_other_out,
    head_acc,
    kv_acc,
):
    f32, bf16 = jnp.float32, jnp.bfloat16
    core, step = core_ref[0], pl.program_id(0)
    scale = (DN + DR) ** -0.5
    d_rows = jnp.concatenate(by_core(core, d_own[0], d_other[0]), axis=0)
    rows = d_rows.shape[0]
    half = rows // 2
    lane = lax.broadcasted_iota(jnp.int32, (rows, LANES), 1)
    q_cols = heads * (DN + DR)
    q, kv, k_rope = q_ref[0], kv_ref[0], k_rope_ref[0]
    d_attended = dot_nn(d_rows, head_w[:, q_cols : q_cols + heads * DV]).astype(bf16)
    visible = seen(doc_col[0], doc_row[0])
    d_q, d_kv = [], []
    d_q_rope, d_k_rope = jnp.zeros((rows, LANES), f32), jnp.zeros((rows, LANES), f32)
    for head in range(heads):
        scores, q_nope, q_rope, k_nope, value = head_scores(
            q, kv, k_rope, visible, lane, head, heads
        )
        probs = jnp.exp(scores - sums_ref[0][:, head : head + 1])
        d_head = d_attended[:, head * DV : (head + 1) * DV]
        d_probs = dot_nt(d_head, value)
        d_value = dot_tn(probs.astype(bf16), d_head)
        delta = jnp.sum(probs * d_probs, axis=1, keepdims=True)
        d_scores = (probs * (d_probs - delta)).astype(bf16)
        d_q.append(dot_nn(d_scores, k_nope) * scale)
        d_q_rope = jnp.where(lane // DR == head, dot_nn(d_scores, k_rope) * scale, d_q_rope)
        d_kv += [dot_tn(d_scores, q_nope) * scale, d_value]
        d_k_rope += dot_tn(d_scores, q_rope) * scale
    d_q_rope = d_q_rope * cosine[0] - swap_halves(d_q_rope, lane) * sine[0]
    d_q = jnp.concatenate(d_q + [d_q_rope], axis=1).astype(bf16)
    d_kv = jnp.concatenate(d_kv, axis=1).astype(bf16)

    @pl.when(step == 0)
    def _():
        head_acc[...] = jnp.zeros_like(head_acc)
        kv_acc[...] = jnp.zeros_like(kv_acc)

    head_acc[:, :q_cols] += dot_tn(normed_ref[0], d_q)
    head_acc[:, q_cols:] += dot_tn(d_rows, attended_ref[0])
    kv_acc[...] += dot_tn(compressed_ref[0], d_kv)

    @pl.when(step == pl.num_programs(0) - 1)
    def _():
        head_grad_out[...] = head_acc[...].astype(bf16)
        kv_grad_out[...] = kv_acc[...].astype(bf16)

    part = dot_nt(d_q, head_w[:, :q_cols]).astype(bf16)
    normed_own_out[0], normed_other_out[0] = by_core(core, part[:half], part[half:])
    latent = jnp.concatenate([dot_nt(d_kv, kv_w[...]), d_k_rope], axis=1).astype(bf16)
    latent_own_out[0], latent_other_out[0] = by_core(core, latent[:half], latent[half:])


def one_each(*tail):
    return pl.BlockSpec((1, *tail), lambda i: (i,) + (0,) * len(tail))


def kept(value):
    return pl.BlockSpec(value.shape, lambda i: (0,) * value.ndim, pipeline_mode=pl.Buffered(1))


def attention(core, x_own, x_other, gain, latent_gain, head_w, small_w, kv_w, cosine, sine, doc):
    near, half, width = x_own.shape
    rows = 2 * half
    rank, kv_cols = kv_w.shape
    heads = kv_cols // (DN + DV)
    f32, bf16 = jnp.float32, jnp.bfloat16
    shapes = [
        ((rows, width), bf16),
        ((rows, rank), bf16),
        ((rows, heads * (DN + DR)), bf16),
        ((rows, kv_cols), bf16),
        ((rows, LANES), bf16),
        ((rows, LANES), f32),
        ((rows, heads * DV), bf16),
        ((rows, rank + LANES), f32),
        ((half, width), bf16),
        ((half, width), bf16),
    ]
    return pl.pallas_call(
        functools.partial(attention_kernel, heads, rank),
        grid=(near,),
        in_specs=[
            pl.BlockSpec(memory_space=pltpu.SMEM),
            *[one_each(half, width)] * 2,
            *[kept(a) for a in (gain, latent_gain, head_w, small_w, kv_w)],
            *[one_each(rows, LANES)] * 2,
            one_each(rows, 1),
            one_each(1, rows),
        ],
        out_specs=[one_each(*shape) for shape, _ in shapes],
        out_shape=[jax.ShapeDtypeStruct((near, *shape), kind) for shape, kind in shapes],
        compiler_params=pltpu.CompilerParams(vmem_limit_bytes=58 * 1024 * 1024),
        cost_estimate=pl.CostEstimate(
            flops=2 * near * rows * width * (rank + 3 * heads * DN),
            bytes_accessed=4 * near * rows * width,
            transcendentals=0,
        ),
    )(
        core,
        x_own,
        x_other,
        gain,
        latent_gain,
        head_w,
        small_w,
        kv_w,
        cosine,
        sine,
        doc[:, :, None],
        doc[:, None, :],
    )


def attention_backward(core, d_own, d_other, kept_rows, head_w, kv_w, cosine, sine, doc):
    near, half, width = d_own.shape
    rows = 2 * half
    rank, kv_cols = kv_w.shape
    heads = kv_cols // (DN + DV)
    head_cols = heads * (DN + DR + DV)
    f32, bf16 = jnp.float32, jnp.bfloat16
    sds = jax.ShapeDtypeStruct
    return pl.pallas_call(
        functools.partial(attention_backward_kernel, heads),
        grid=(near,),
        in_specs=[
            pl.BlockSpec(memory_space=pltpu.SMEM),
            *[one_each(half, width)] * 2,
            *[one_each(*v.shape[1:]) for v in kept_rows],
            *[kept(a) for a in (head_w, kv_w)],
            *[one_each(rows, LANES)] * 2,
            one_each(rows, 1),
            one_each(1, rows),
        ],
        out_specs=[
            pl.BlockSpec((width, head_cols), lambda i: (0, 0)),
            pl.BlockSpec((rank, kv_cols), lambda i: (0, 0)),
            *[one_each(half, width)] * 2,
            *[one_each(half, rank + LANES)] * 2,
        ],
        out_shape=[
            sds((width, head_cols), bf16),
            sds((rank, kv_cols), bf16),
            *[sds((near, half, width), bf16)] * 2,
            *[sds((near, half, rank + LANES), bf16)] * 2,
        ],
        scratch_shapes=[
            pltpu.VMEM((width, head_cols), f32),
            pltpu.VMEM((rank, kv_cols), f32),
        ],
        compiler_params=pltpu.CompilerParams(vmem_limit_bytes=58 * 1024 * 1024),
        cost_estimate=pl.CostEstimate(
            flops=near * rows * width * heads * DN,
            bytes_accessed=2 * near * rows * width,
            transcendentals=0,
        ),
    )(
        core,
        d_own,
        d_other,
        *kept_rows,
        head_w,
        kv_w,
        cosine,
        sine,
        doc[:, :, None],
        doc[:, None, :],
    )


def product_kernel(left_ref, right_ref, out_ref):
    out_ref[0] = dot_tn(left_ref[0], right_ref[...])


def column_products(left, right, tile=512):
    count, rows, height = left.shape
    width = right.shape[1]
    return pl.pallas_call(
        product_kernel,
        grid=(width // tile, count),
        in_specs=[
            pl.BlockSpec((1, rows, height), lambda j, i: (i, 0, 0)),
            pl.BlockSpec((rows, tile), lambda j, i: (0, j)),
        ],
        out_specs=pl.BlockSpec((1, height, tile), lambda j, i: (i, 0, j)),
        out_shape=jax.ShapeDtypeStruct((count, height, width), jnp.float32),
        compiler_params=pltpu.CompilerParams(vmem_limit_bytes=58 * 1024 * 1024),
        cost_estimate=pl.CostEstimate(
            flops=rows * width, bytes_accessed=rows * width, transcendentals=0
        ),
    )(left, right)


def output_kernel(act, sact_own, sact_other, meta_own, meta_other, down_w, sdown_w, own_out, other_out):
    f32, bf16 = jnp.float32, jnp.bfloat16
    count, half, _ = meta_own.shape
    lane = lax.broadcasted_iota(jnp.int32, (2 * half, LANES), 1).astype(f32)
    out = dot_nn(act[...], down_w[...]).astype(bf16)
    for i in range(count):
        meta = jnp.concatenate([meta_own[i], meta_other[i]], axis=0)
        pick = (meta[:, :1] == lane).astype(bf16)
        sact = jnp.concatenate([sact_own[i], sact_other[i]], axis=0)
        here = slice(i * LANES, (i + 1) * LANES)
        rows = (dot_nn(pick, out[here]) + dot_nn(sact, sdown_w[...])).astype(bf16)
        own_out[i], other_out[i] = rows[:half], rows[half:]


def outputs(act, sact_own, sact_other, meta_own, meta_other, down_w, sdown_w, per_step=4):
    groups, half, _ = meta_own.shape
    hidden, width = down_w.shape
    lead, flat, whole = block_specs(per_step)
    return pl.pallas_call(
        output_kernel,
        grid=(groups // per_step,),
        in_specs=[
            flat(hidden),
            *[lead(half, LANES)] * 4,
            *[whole(a) for a in (down_w, sdown_w)],
        ],
        out_specs=[lead(half, width)] * 2,
        out_shape=[jax.ShapeDtypeStruct((groups, half, width), jnp.bfloat16)] * 2,
        compiler_params=pltpu.CompilerParams(vmem_limit_bytes=58 * 1024 * 1024),
        cost_estimate=pl.CostEstimate(
            flops=groups * half * LANES * width,
            bytes_accessed=groups * half * width,
            transcendentals=0,
        ),
    )(act, sact_own, sact_other, meta_own, meta_other, down_w, sdown_w)


def token_plan(
    inputs,
    attn_gain,
    w_query,
    w_latent,
    latent_gain,
    w_kv,
    w_out,
    ffn_gain,
    w_router,
    shared_gate_up,
    shared_down,
    expert_gate_up,
    expert_down,
    lengths,
    routes,
    cotangent,
):
    f32, bf16 = jnp.float32, jnp.bfloat16
    core, me = lax.axis_index("tensor"), lax.axis_index("expert")
    groups = lax.axis_size("expert")
    deep, place, z = groups // PLANE, me % PLANE, me // PLANE
    tok_rows, width = inputs.shape
    half = tok_rows // 2
    own_at, other_at = core * half, (1 - core) * half
    expert_count = w_router.shape[1]
    route_count = routes.shape[1]
    capacity = tok_rows * route_count * 4 // (3 * expert_count)
    shared_cols = shared_gate_up.shape[2] // groups
    latent_cols, rank_width = w_latent.shape[1], latent_gain.shape[0] * groups
    block_rows = w_query.shape[0]
    kv_rows = w_kv.shape[0]

    query_cols = w_query.shape[1] // PLANE
    out_cols = w_out.shape[0] // PLANE
    small = jnp.concatenate(
        [
            w_latent,
            w_latent[:, rank_width:],
            w_router,
            attn_gain[:, None],
            ffn_gain[:, None],
            jnp.pad(latent_gain, (0, block_rows - kv_rows))[:, None],
        ],
        axis=1,
    )
    small_cols = small.shape[1]
    route_half = take_rows(routes, own_at, half).astype(bf16).reshape(block_rows // 2, -1)
    length_col = jnp.pad(lengths[0].astype(bf16), (0, block_rows // 2 - lengths.shape[1]))[:, None]
    route_cols = route_half.shape[1] + 1
    small_half = jnp.concatenate(
        [
            take_rows(small, core * (block_rows // 2), block_rows // 2),
            route_half,
            length_col,
            jnp.zeros((block_rows // 2, -(small_cols + route_cols) % (2 * LANES)), bf16),
        ],
        axis=1,
    )
    packed_cols = small_half.shape[1] // 2
    small_packed = jnp.concatenate([small_half[:, :packed_cols], small_half[:, packed_cols:]])
    kv_cols = w_kv.shape[1] // PLANE
    kv_parts = block_rows // kv_rows
    kv_piece = kv_cols // kv_parts
    w_out_t = w_out.T

    local_heads = query_cols // (DN + DR)

    def by_parts(block):
        heads = [block[:, h * (DN + DR) : (h + 1) * (DN + DR)] for h in range(local_heads)]
        return [h[:, :DN] for h in heads] + [h[:, DN:] for h in heads]

    def quarter(index):
        kv_here = take_rows(w_kv, index * kv_cols, kv_cols, axis=1)
        kv_here = [kv_here[:, p * kv_piece : (p + 1) * kv_piece] for p in range(kv_parts)]
        return jnp.concatenate(
            [
                *by_parts(take_rows(w_query, index * query_cols, query_cols, axis=1)),
                take_rows(w_out_t, index * out_cols, out_cols, axis=1),
                jnp.concatenate(kv_here, axis=0),
            ],
            axis=1,
        )

    near_w = [quarter(place)] + [to_partner(quarter(place ^ r), r) for r in range(1, PLANE)]
    small_line = deep_join(small_packed, deep_pieces(small_packed), z)
    near_w, small_line = tie(near_w, small_line)
    plane_w = jnp.stack(by_place(near_w, place))
    small_sent, x_sent, plane_w = tie(
        small_line.swapaxes(0, 1), take_rows(inputs, own_at, half), plane_w
    )
    small_sent = jnp.stack([small_sent, to_partner(small_sent, 1)])
    small_sent = jnp.concatenate([small_sent, to_partner(small_sent, 2)], axis=0)
    x_sent = jnp.stack([x_sent, to_partner(x_sent, 2)])
    x_came = to_partner(x_sent, 1)
    x_near_own = jnp.stack([x_sent[0], x_came[0], x_sent[1], x_came[1]])
    x_near_other = swap_cores(x_near_own)
    deep_w = deep_hops(plane_w)
    small_parts = [small_sent[r].swapaxes(0, 1) for r in range(PLANE)]
    small_own = jnp.stack(by_place(small_parts, place), axis=1)
    small_own = small_own.reshape(groups, block_rows, packed_cols)
    small_own = jnp.concatenate(
        [small_own[:, : block_rows // 2], small_own[:, block_rows // 2 :]], axis=2
    )
    small_other = swap_cores(small_own)
    small_all = in_order(core, small_own, small_other, axis=1)
    small_all, x_near_other, deep_w = tie(small_all, x_near_other, deep_w)
    head_w = deep_join(plane_w, join_hops(deep_w), z)
    length_at = small_cols + route_cols - 1
    lengths_near = take_rows(small_own, z * PLANE, PLANE)[:, : lengths.shape[1], length_at]
    lengths_near = lengths_near.astype(jnp.int32)
    lengths_near = jnp.stack(by_place([lengths_near[r] for r in range(PLANE)], place))
    shared_rows = jnp.concatenate(
        [shared_gate_up[0].T, shared_gate_up[1].T, shared_down], axis=0
    ).reshape(3, groups, shared_cols, block_rows)
    shared_rows = shared_rows.swapaxes(0, 1).reshape(groups, 3 * shared_cols, block_rows)
    dy_sent, head_w = tie(take_rows(cotangent, own_at, half), head_w)
    dy_own_rows = take_rows(cotangent, own_at, half)
    dy_gather = RowGather(dy_sent)
    dy_came = dy_gather.along()
    head_w = head_w.reshape(groups, block_rows, -1)
    flat_head = head_w.reshape(groups * block_rows, -1)
    at = query_cols + out_cols
    kv_w = head_w[:, :, at : at + kv_piece].reshape(groups, kv_parts, kv_rows, kv_piece)
    kv_w = kv_w.transpose(0, 2, 1, 3).reshape(groups * kv_rows, kv_cols)

    block_index = jnp.arange(groups)
    block_chip = (z - block_index % deep) % deep * PLANE + (place ^ (block_index // deep))
    in_blocks = (block_chip[:, None] == block_index[None, :]).astype(bf16)

    def routes_of(came):
        came = came[:, :, small_cols : small_cols + route_half.shape[1]].reshape(groups, -1)
        came = jnp.dot(in_blocks, came, preferred_element_type=f32)
        return came.astype(jnp.int32).reshape(groups, half, route_count)

    routes_own, routes_other = routes_of(small_own), routes_of(small_other)
    flat_small = small_all.reshape(groups * block_rows, -1)
    latent_w = flat_small[:, :latent_cols]
    at = rank_width + LANES
    router_w = flat_small[:, at : at + expert_count]
    at += expert_count
    gain_one, gain_two = flat_small[:, at], flat_small[:, at + 1]
    latent_g = small_all[:, :kv_rows, at + 2].reshape(-1)

    near_rows = PLANE * tok_rows
    relative, doc = jax.vmap(lambda one: doc_places(one, tok_rows))(lengths_near)
    cosine, sine_tab = rope_tables(relative.reshape(-1), DR)
    cosine, sine_tab = [v.reshape(PLANE, tok_rows, -1) for v in (cosine, sine_tab)]
    rope = (
        jnp.concatenate([cosine] * 4, axis=-1),
        jnp.concatenate([-sine_tab, sine_tab] * 2, axis=-1),
        doc.astype(f32),
    )
    core_index = core.reshape(1).astype(jnp.int32)
    *kept_rows, latent, part_own, part_other = attention(
        core_index,
        x_near_own,
        x_near_other,
        gain_one.astype(f32)[None],
        latent_g.astype(f32)[None],
        flat_head,
        flat_small,
        kv_w,
        *rope,
    )
    normed_b = kept_rows[0].reshape(near_rows, width)

    def sum_cores(own, other):
        return add_wide(own, swap_cores(other)).astype(bf16)

    def sum_plane(both):
        return plane_scatter([both[r] for r in range(PLANE)])

    part_own, part_other, dy_came, shared_rows = tie(part_own, part_other, dy_came, shared_rows)
    dy_lines = dy_gather.lines(dy_came)
    dy_over = dy_gather.over(dy_lines)
    shared_w = lax.all_to_all(shared_rows, "expert", split_axis=0, concat_axis=0, tiled=True)
    attn_own, dy_over, shared_w = tie(
        sum_plane(sum_cores(part_own, part_other)), dy_over, shared_w
    )
    x_own = take_rows(inputs, own_at, half).astype(f32)
    hidden = x_own + attn_own
    hnormed, scale_two = rms_forward(hidden, gain_two.astype(f32))
    hnormed_b = hnormed.astype(bf16)
    normed_cols = jnp.concatenate(
        [
            take_rows(normed_b, (k * PLANE + place) * block_rows, block_rows, axis=1)
            for k in range(deep)
        ],
        axis=1,
    )
    hnormed_b, normed_cols = tie(hnormed_b, normed_cols)
    def membership(named):
        one_hot = named[..., None] == jnp.arange(expert_count, dtype=jnp.int32)
        return jnp.any(named == me, axis=-1), jnp.any(one_hot, axis=2)

    member_own, hot_own = membership(routes_own)
    member_other, hot_other = membership(routes_other)
    lower = (
        jnp.arange(half, dtype=jnp.int32)[:, None] <= jnp.arange(half, dtype=jnp.int32)[None, :]
    ).astype(bf16)

    def running(mask):
        counts = jnp.dot(mask.astype(bf16), lower, preferred_element_type=f32)
        return counts.astype(jnp.int32)

    count_own, count_other = running(member_own), running(member_other)
    place_own = jnp.where(member_own, count_own - 1, -1)
    place_other = jnp.where(member_other, count_own[:, -1:] + count_other - 1, -1)

    def metadata(slot, hot):
        return jnp.concatenate(
            [
                slot[..., None].astype(f32),
                jnp.zeros((groups, half, shared_cols - 1), f32),
                hot.astype(f32),
                jnp.zeros((groups, half, LANES - shared_cols - expert_count), f32),
            ],
            axis=-1,
        )

    meta_own, meta_other = metadata(place_own, hot_own), metadata(place_other, hot_other)
    hn_gather = RowGather(hnormed_b)
    hn_came, dy_halves = tie(hn_gather.along(), dy_gather.over_again(dy_lines, dy_over))
    hn_lines, dy_halves = tie(hn_gather.lines(hn_came), dy_halves)
    dy_own = dy_gather.whole(dy_halves)
    hn_over, dy_own = tie(hn_gather.over(hn_lines), dy_own)
    hn_halves = hn_gather.over_again(hn_lines, hn_over)
    dy_other = swap_cores(dy_own)
    hn_halves, shared_w, dy_other, meta_own, meta_other = tie(
        hn_halves, shared_w, dy_other, meta_own, meta_other
    )
    shared_w = shared_w.swapaxes(0, 1).reshape(3 * shared_cols, groups * block_rows)
    hn_own = hn_gather.whole(hn_halves)


    first_w = jnp.concatenate(
        [
            shared_w[:shared_cols],
            router_w.T,
            jnp.zeros((LANES - shared_cols - expert_count, width), bf16),
            shared_w[shared_cols : 2 * shared_cols],
            jnp.zeros((LANES - shared_cols, width), bf16),
        ],
        axis=0,
    )
    sdown_rows = jnp.pad(shared_w[2 * shared_cols :], ((0, LANES - shared_cols), (0, 0)))
    hn_other = swap_cores(hn_own)
    gate_up_w, down_w = jnp.swapaxes(expert_gate_up[0], 1, 2), expert_down[0]
    (
        slot_rows,
        slot_dy,
        slot_act,
        d_gate_up,
        d_rows_own,
        d_rows_other,
        act_own,
        act_other,
        shared_grads,
        dgate_own,
        dgate_other,
    ) = experts(
        me.reshape(1).astype(jnp.int32),
        hn_own,
        hn_other,
        dy_own,
        dy_other,
        meta_own,
        meta_other,
        gate_up_w,
        down_w,
        first_w,
        sdown_rows,
        shared_cols,
        expert_count,
    )
    d_rows_came = swap_cores(d_rows_other)

    def two_parts(value):
        return value[..., 0] + value[..., 1]

    dgate_sent = two_parts(dgate_own) + swap_cores(two_parts(dgate_other))
    dgate_high = dgate_sent.astype(bf16)
    dgate_low = (dgate_sent - dgate_high.astype(f32)).astype(bf16)
    out_own, out_other = outputs(
        slot_act, act_own, act_other, meta_own, meta_other, down_w, sdown_rows
    )
    d_rows_came, dgate_high, dgate_low, out_other = tie(
        d_rows_came, dgate_high, dgate_low, out_other
    )
    d_sum = RowSum(d_rows_own, d_rows_came)
    sends, shared_grads, slot_act, out_other = tie(
        d_sum.sends(), shared_grads, slot_act, out_other
    )
    came = d_sum.move(sends)
    gate_rows = jnp.stack([contract_rows(in_blocks, v).reshape(-1) for v in (dgate_high, dgate_low)])
    grads_sent = jnp.concatenate([shared_grads, gate_rows], axis=0).astype(bf16)
    grads_sent = grads_sent.reshape(-1, groups, block_rows)
    grads_came = lax.all_to_all(grads_sent, "expert", split_axis=1, concat_axis=1, tiled=True)
    out_came = swap_cores(out_other)
    edown_grad = column_products(slot_act[None], slot_dy)[0]
    came, out_came, edown_grad, grads_came = tie(came, out_came, edown_grad, grads_came)
    dgate = add_wide(grads_came[3 * shared_cols], grads_came[3 * shared_cols + 1]).T
    sends, slot_rows, out_came = tie(d_sum.sends_again(came), slot_rows, out_came)
    came_again = d_sum.move_again(sends)
    egu_grad = column_products(d_gate_up, slot_rows).swapaxes(1, 2)
    out_sum = RowSum(out_own, out_came)
    out_sends = out_sum.sends()
    came_again, egu_grad, out_sends = tie(came_again, egu_grad, out_sends)
    z_sends, out_sends, dgate = tie(
        line_sends(d_sum.line(came, came_again)), out_sends, dgate
    )
    z_came = line_move(z_sends)
    out_first = out_sum.move(out_sends)
    hot_mine = take_rows(
        jnp.any(routes[..., None] == jnp.arange(expert_count, dtype=jnp.int32), axis=1), own_at, half
    )
    sig = jax.nn.sigmoid(jnp.dot(hnormed_b, router_w, preferred_element_type=f32))
    chosen = jnp.where(hot_mine, sig, 0.0)
    chosen_sum = jnp.sum(chosen, axis=1, keepdims=True)
    dgate = jnp.where(hot_mine, dgate, 0.0)
    inner = jnp.sum(dgate * chosen, axis=1, keepdims=True)
    d_chosen = ROUTE_SCALE * (dgate / chosen_sum - inner / (chosen_sum * chosen_sum))
    d_logits = (jnp.where(hot_mine, d_chosen, 0.0) * sig * (1.0 - sig)).astype(bf16)
    router_grad = contract_rows(d_logits, hnormed_b)
    z_came, d_logits, router_grad = tie(z_came, d_logits, router_grad)
    d_hn = add_wide(*z_came)
    d_hn = d_hn + contract_cols(d_logits, router_w)
    d_hidden_norm, gain_two_grad = rms_backward(hidden, scale_two, gain_two.astype(f32), d_hn)
    d_hidden = dy_own_rows.astype(f32) + d_hidden_norm
    d_parts, out_first = tie(plane_gather(d_hidden.astype(bf16)), out_first)
    d_near_own = jnp.stack(d_parts)
    d_near_other = swap_cores(d_near_own)
    out_sends, d_near_other = tie(out_sum.sends_again(out_first), d_near_other)
    out_second = out_sum.move_again(out_sends)

    (
        head_grad,
        kv_grad,
        normed_part_own,
        normed_part_other,
        latent_part_own,
        latent_part_other,
    ) = attention_backward(
        core_index, d_near_own, d_near_other, kept_rows, flat_head, kv_w, *rope
    )
    kv_grad = kv_grad.reshape(groups, kv_rows, kv_parts, kv_piece).transpose(0, 2, 1, 3)
    head_grad = jnp.concatenate([head_grad, kv_grad.reshape(-1, kv_piece)], axis=1)
    head_blocks = head_grad.reshape(deep, -1, head_grad.shape[1])
    head_hops = HopSum(lambda t: at_index(head_blocks, 0, t))
    came, latent_both, normed_both, out_second = tie(
        head_hops.hop(1),
        sum_cores(latent_part_own, latent_part_other),
        sum_cores(normed_part_own, normed_part_other),
        out_second,
    )
    came, grad_both = tie(head_hops.hop(2, came), sum_plane(latent_both))
    grad_rope = grad_both[:, rank_width : rank_width + DR] + grad_both[:, rank_width + DR :]
    latent_own = take_rows(latent[0], own_at, half)
    cosine_own = take_rows(cosine[0], own_at, half)
    sine_own = take_rows(sine_tab[0], own_at, half)
    _, scale_kv = rms_forward(latent_own[:, :rank_width], latent_g.astype(f32))
    grad_c, latent_gain_grad = rms_backward(
        latent_own[:, :rank_width], scale_kv, latent_g.astype(f32), grad_both[:, :rank_width]
    )
    grad_latent = jnp.concatenate(
        [grad_c, unrotate(grad_rope, cosine_own, sine_own)], axis=-1
    ).astype(bf16)
    out_line = out_sum.line(out_first, out_second)
    came, latent_parts, grad_normed, out_line = tie(
        head_hops.hop(3, came), plane_gather(grad_latent), sum_plane(normed_both), out_line
    )
    out_hops = HopSum(lambda t: at_index(out_line, 0, (z - t) % deep))
    latent_near_own = jnp.stack(latent_parts)
    latent_near = in_order(core, latent_near_own, swap_cores(latent_near_own), axis=1)
    head_sums = head_hops.total(came).astype(bf16).reshape(PLANE, block_rows, -1)
    out_z, latent_near, head_shared = tie(
        out_hops.hop(1), latent_near, share_columns(head_sums, place)
    )
    out_z = out_hops.hop(2, out_z)
    out_z = out_hops.hop(3, out_z)
    latent_cut = latent_cols // 2
    latent_near = latent_near.reshape(near_rows, latent_cols)
    latent_blocks = contract_rows(
        normed_cols,
        take_rows(latent_near, core * latent_cut, latent_cut, axis=1),
    )
    latent_half = deep_scatter(latent_blocks.astype(bf16).reshape(deep, -1, latent_cut), z)
    w_latent_grad = in_order(core, latent_half, swap_cores(latent_half), axis=1)


    def by_heads(block):
        rotary = local_heads * DN
        return [
            part
            for h in range(local_heads)
            for part in (
                block[:, h * DN : (h + 1) * DN],
                block[:, rotary + h * DR : rotary + (h + 1) * DR],
            )
        ]

    at_kv = query_cols + out_cols
    w_query_grad = jnp.concatenate([v for p in head_shared for v in by_heads(p)], axis=1)
    w_query_grad = w_query_grad.astype(f32)
    w_kv_grad = jnp.concatenate(
        [
            p[q * kv_rows : (q + 1) * kv_rows, at_kv:]
            for p in head_shared
            for q in range(kv_parts)
        ],
        axis=1,
    ).astype(f32)
    w_out_grad = jnp.concatenate([p[:, query_cols:at_kv] for p in head_shared], axis=1)
    w_out_grad = w_out_grad.astype(f32).T
    sgu_out = grads_came[: 2 * shared_cols].astype(f32)
    sgu_out = sgu_out.reshape(2, shared_cols, groups, block_rows)
    sgu_out = sgu_out.transpose(0, 3, 2, 1).reshape(2, block_rows, -1)
    sdown_out = grads_came[2 * shared_cols : 3 * shared_cols].astype(f32).swapaxes(0, 1).reshape(-1, block_rows)
    grad_normed = grad_normed + contract_cols(grad_latent, latent_w)
    moe_own = out_hops.total(out_z)
    mixed_own = (hidden + moe_own).astype(bf16)
    mixed = in_order(core, mixed_own, swap_cores(mixed_own))

    _, scale_own = rms_forward(x_own, gain_one.astype(f32))
    grad_x_norm, gain_one_grad = rms_backward(x_own, scale_own, gain_one.astype(f32), grad_normed)
    input_own = d_hidden + grad_x_norm
    input_grad = in_order(core, input_own, swap_cores(input_own))

    gain_lanes = jnp.pad(
        latent_gain_grad.reshape(groups, kv_rows), ((0, 0), (0, block_rows - kv_rows))
    )
    vectors = jnp.concatenate(
        [
            router_grad,
            gain_one_grad[None],
            gain_two_grad[None],
            gain_lanes.reshape(1, -1),
        ],
        axis=0,
    ).reshape(-1, groups, block_rows)
    arrived = lax.all_to_all(vectors, "expert", split_axis=1, concat_axis=1, tiled=True)
    sums = jnp.sum(arrived, axis=1)
    sums = sums + swap_cores(sums)
    return (
        mixed,
        input_grad,
        sums[expert_count],
        w_query_grad,
        w_latent_grad,
        sums[expert_count + 2, :kv_rows],
        w_kv_grad,
        w_out_grad,
        sums[expert_count + 1],
        sums[:expert_count].T,
        sgu_out,
        sdown_out,
        egu_grad[None],
        edown_grad[None],
    )


def solution(mesh):
    groups = mesh.shape["expert"]
    plan = token_plan if groups <= 16 else weight_plan
    return jax.shard_map(
        plan,
        mesh=mesh,
        in_specs=(
            P("expert", None),
            P("expert"),
            P("expert", "tensor"),
            P("expert", None),
            P("expert"),
            P("expert", "tensor"),
            P("tensor", "expert"),
            P("expert"),
            P("expert", None),
            P(None, "expert", "tensor"),
            P("tensor", "expert"),
            P("expert", None, None, "tensor"),
            P("expert", "tensor", None),
            P("expert", None),
            P("expert", None),
            P("expert", None),
        ),
        out_specs=(
            P("expert", None),
            P("expert", None),
            P("expert"),
            P("expert", "tensor"),
            P("expert", None),
            P("expert"),
            P("expert", "tensor"),
            P("tensor", "expert"),
            P("expert"),
            P("expert", None),
            P(None, "expert", "tensor"),
            P("tensor", "expert"),
            P("expert", None, None, "tensor"),
            P("expert", "tensor", None),
        ),
        check_vma=False,
    )
```

```python
import functools

import jax
import jax.numpy as jnp
from jax import lax
from jax.experimental import pallas as pl
from jax.experimental.pallas import tpu as pltpu
from jax.sharding import PartitionSpec as P

DN = 128
DR = 64
DV = 128
LANES = 128


EPSILON = 1e-06
ROUTE_SCALE = 2.446
ROPE_BASE = 50000.0
NEGATIVE = -1e30


def cut_along(value, dim, length):
    before, after = (value.shape[:dim], value.shape[dim + 1 :])
    return jnp.moveaxis(value.reshape(*before, length, -1, *after), dim, 0)


def summed_on_arrival(value, axis, dim):
    length = lax.axis_size(axis)
    tiles = lax.all_to_all(cut_along(value, dim, length), axis, 0, 0, tiled=True)
    return jnp.sum(tiles.astype(jnp.float32), axis=0)


def sent_together(arrays, axis, dim, along):
    columns = [a.reshape(*a.shape[:along], -1) for a in arrays]
    both = jnp.concatenate(columns, axis=along)
    whole, at, outs = (summed_on_arrival(both, axis, dim), 0, [])
    for a, column in zip(arrays, columns):
        slab = whole[..., at : at + column.shape[along]]
        outs.append(slab.reshape(*slab.shape[:along], *a.shape[along:]))
        at += column.shape[along]
    return tuple(outs)


def contract_rows(left_arr, right_arr):
    return lax.dot_general(
        left_arr, right_arr, (((0,), (0,)), ((), ())), preferred_element_type=jnp.float32
    )


def contract_cols(left_arr, right_arr):
    return lax.dot_general(
        left_arr, right_arr, (((1,), (1,)), ((), ())), preferred_element_type=jnp.float32
    )


def rms_forward(rows_in, gain_vec):
    inverse = lax.rsqrt(jnp.mean(rows_in * rows_in, axis=-1, keepdims=True) + EPSILON)
    return (rows_in * inverse * gain_vec, inverse)


def rms_backward(rows_in, inverse, gain_vec, grad_out):
    gain_grad = jnp.sum(grad_out * rows_in * inverse, axis=0)
    weighted = grad_out * gain_vec
    inner_mean = jnp.mean(weighted * rows_in, axis=-1, keepdims=True)
    return (inverse * weighted - rows_in * inverse * inverse * inverse * inner_mean, gain_grad)


def doc_layout(doc_lengths, row_count):
    ends_at = jnp.cumsum(doc_lengths)
    starts_at = ends_at - doc_lengths
    position = jnp.arange(row_count, dtype=jnp.int32)
    doc_ids = jnp.sum((position[:, None] >= ends_at[None, :]).astype(jnp.int32), axis=1)
    hitting = doc_ids[:, None] == jnp.arange(doc_lengths.shape[0], dtype=jnp.int32)[None, :]
    start_of = jnp.sum(jnp.where(hitting, starts_at[None, :], 0), axis=1)
    relative = position - start_of
    visible = (doc_ids[:, None] == doc_ids[None, :]) & (position[:, None] >= position[None, :])
    return (relative, visible)


def rope_tables(relative, rot_width):
    counter = jnp.arange(rot_width // 2, dtype=jnp.float32)
    frequency = ROPE_BASE ** (-2.0 * counter / rot_width)
    angles = relative.astype(jnp.float32)[:, None] * frequency[None, :]
    return (jnp.cos(angles), jnp.sin(angles))


def rotate(tensor_in, cosine, sine_tab):
    half_width = tensor_in.shape[-1] // 2
    leading = tensor_in[..., :half_width]
    trailing = tensor_in[..., half_width:]
    return jnp.concatenate(
        [leading * cosine - trailing * sine_tab, trailing * cosine + leading * sine_tab], axis=-1
    )


def unrotate(grad_in, cosine, sine_tab):
    half_width = grad_in.shape[-1] // 2
    leading = grad_in[..., :half_width]
    trailing = grad_in[..., half_width:]
    return jnp.concatenate(
        [leading * cosine + trailing * sine_tab, trailing * cosine - leading * sine_tab], axis=-1
    )


def gated_linear_backward(gate_in, up_in, grad_act):
    sigmoid_g = jax.nn.sigmoid(gate_in)
    grad_gate = grad_act * up_in * sigmoid_g * (1.0 + gate_in * (1.0 - sigmoid_g))
    return (grad_gate, grad_act * gate_in * sigmoid_g)


def slot_tables(route_rows, expert_count, capacity):
    flat_routes = route_rows.reshape(-1)
    one_hot = (flat_routes[:, None] == jnp.arange(expert_count, dtype=jnp.int32)[None, :]).astype(
        jnp.int32
    )
    ranking = jnp.sum((jnp.cumsum(one_hot, axis=0) - one_hot) * one_hot, axis=1)
    slot_ids = flat_routes * capacity + ranking
    row_total = flat_routes.shape[0]
    source = (
        jnp.zeros((expert_count * capacity,), jnp.int32)
        .at[slot_ids]
        .set(jnp.arange(row_total, dtype=jnp.int32))
    )
    filled = jnp.zeros((expert_count * capacity,), jnp.int32).at[slot_ids].set(1)
    return (slot_ids, source, filled)


def to_owner(rows_in):
    arrived = lax.all_to_all(rows_in, "expert", split_axis=0, concat_axis=1, tiled=True)
    return arrived


def weight_plan(
    inputs,
    attn_gain,
    w_query,
    w_latent,
    latent_gain,
    w_kv,
    w_out,
    ffn_gain,
    w_router,
    shared_gate_up,
    shared_down,
    expert_gate_up,
    expert_down,
    lengths,
    routes,
    cotangent,
):
    tok_rows = inputs.shape[0]
    model_width = inputs.shape[1]
    expert_count = w_router.shape[1]
    route_count = routes.shape[1]
    capacity = tok_rows * route_count * 4 // (3 * expert_count)
    brain_float16 = jnp.bfloat16
    f32 = jnp.float32
    gathered = (
        lax.all_gather(attn_gain, "expert", axis=0, tiled=True),
        lax.all_gather(w_query, "expert", axis=0, tiled=True),
        lax.all_gather(w_latent, "expert", axis=0, tiled=True),
        lax.all_gather(latent_gain, "expert", axis=0, tiled=True),
        lax.all_gather(w_kv, "expert", axis=0, tiled=True),
        lax.all_gather(w_out, "expert", axis=1, tiled=True),
        lax.all_gather(ffn_gain, "expert", axis=0, tiled=True),
        lax.all_gather(w_router, "expert", axis=0, tiled=True),
        lax.all_gather(shared_gate_up, "expert", axis=1, tiled=True),
        lax.all_gather(shared_down, "expert", axis=1, tiled=True),
    )
    gain_one, query_w, latent_w, latent_g, kv_w, out_w, gain_two, router_w, sgate_up, sdown_w = (
        gathered
    )
    local_heads = query_w.shape[1] // (DN + DR)
    rank_width = latent_g.shape[0]
    x_float = inputs.astype(f32)
    relative, visible = doc_layout(lengths[0], tok_rows)
    cosine, sine_tab = rope_tables(relative, DR)
    q_scale = (DN + DR) ** (-0.5)
    normed, scale_one = rms_forward(x_float, gain_one.astype(f32))
    normed_b = normed.astype(brain_float16)
    queries = jnp.dot(normed_b, query_w, preferred_element_type=f32).reshape(
        tok_rows, local_heads, DN + DR
    )
    q_rot = rotate(queries[..., DN:], cosine[:, None, :], sine_tab[:, None, :])
    q_all = jnp.concatenate([queries[..., :DN], q_rot], axis=-1).astype(brain_float16)
    latent = jnp.dot(normed_b, latent_w, preferred_element_type=f32)
    compressed, scale_kv = rms_forward(latent[:, :rank_width], latent_g.astype(f32))
    compressed_b = compressed.astype(brain_float16)
    k_rope = rotate(latent[:, rank_width:], cosine, sine_tab).astype(brain_float16)
    kv_all = jnp.dot(compressed_b, kv_w, preferred_element_type=f32).reshape(
        tok_rows, local_heads, DN + DV
    )
    k_nope = kv_all[..., :DN].astype(brain_float16)
    values = kv_all[..., DN:].astype(brain_float16)
    key_all = jnp.concatenate(
        [k_nope, jnp.broadcast_to(k_rope[:, None, :], (tok_rows, local_heads, DR))], axis=-1
    )

    def score_block():
        raw_scores = (
            jnp.einsum("qhd,khd->hqk", q_all, key_all, preferred_element_type=f32) * q_scale
        )
        return jnp.where(visible[None], raw_scores, NEGATIVE)

    scores = score_block()
    top_score = jnp.max(scores, axis=-1, keepdims=True)
    log_total = top_score + jnp.log(jnp.sum(jnp.exp(scores - top_score), axis=-1, keepdims=True))
    probs_b = jnp.exp(scores - log_total).astype(brain_float16)
    attended = jnp.einsum("hqk,khd->qhd", probs_b, values, preferred_element_type=f32)
    attended_b = attended.reshape(tok_rows, local_heads * DV).astype(brain_float16)
    attn = lax.psum(jnp.dot(attended_b, out_w, preferred_element_type=f32), "tensor")
    hidden = x_float + attn
    hnormed, scale_two = rms_forward(hidden, gain_two.astype(f32))
    hnormed_b = hnormed.astype(brain_float16)
    logits = jnp.dot(hnormed_b, router_w, preferred_element_type=f32)
    sigmoid_vals = jax.nn.sigmoid(logits)
    route_hot = routes[:, :, None] == jnp.arange(expert_count, dtype=jnp.int32)[None, None, :]
    chosen = jnp.sum(jnp.where(route_hot, sigmoid_vals[:, None, :], 0.0), axis=2)
    chosen_sum = jnp.sum(chosen, axis=1, keepdims=True)
    gate_vals = ROUTE_SCALE * chosen / chosen_sum
    slot_ids, source, filled = slot_tables(routes, expert_count, capacity)
    is_filled = filled[:, None] == 1
    sent_rows = jnp.where(is_filled, hnormed_b[source // route_count], 0).reshape(
        expert_count, capacity, model_width
    )
    received = to_owner(sent_rows)
    gate_up_joined = jnp.einsum(
        "erd,egdf->egrf", received, expert_gate_up, preferred_element_type=f32
    )
    expert_act = (jax.nn.silu(gate_up_joined[:, 0]) * gate_up_joined[:, 1]).astype(brain_float16)
    expert_res = jnp.einsum(
        "erf,efd->erd", expert_act, expert_down, preferred_element_type=f32
    ).astype(brain_float16)
    returned_all = lax.all_to_all(expert_res, "expert", split_axis=1, concat_axis=0, tiled=True)
    returned = returned_all.reshape(expert_count * capacity, model_width)[slot_ids].reshape(
        tok_rows, route_count, model_width
    )
    shared_gu = jnp.einsum("td,gdf->gtf", hnormed_b, sgate_up, preferred_element_type=f32)
    shared_act = (jax.nn.silu(shared_gu[0]) * shared_gu[1]).astype(brain_float16)
    branch_sum = jnp.dot(shared_act, sdown_w, preferred_element_type=f32)
    for route_idx in range(route_count):
        branch_sum = branch_sum + gate_vals[:, route_idx : route_idx + 1] * returned[
            :, route_idx
        ].astype(f32)
    moe_out = lax.psum(branch_sum.astype(jnp.bfloat16), "tensor").astype(jnp.float32)
    mixed = (hidden + moe_out).astype(brain_float16)
    grad_y = cotangent.astype(f32)
    sdown_grad = contract_rows(shared_act, cotangent)
    grad_sact = contract_cols(cotangent, sdown_w)
    grad_sgate, grad_sup = gated_linear_backward(shared_gu[0], shared_gu[1], grad_sact)
    grad_sgu = jnp.stack([grad_sgate, grad_sup], axis=0).astype(brain_float16)
    sgu_grad = jnp.einsum("td,gtf->gdf", hnormed_b, grad_sgu, preferred_element_type=f32)
    grad_hn_part = jnp.einsum("gtf,gdf->td", grad_sgu, sgate_up, preferred_element_type=f32)
    gate_columns = []
    for route_idx in range(route_count):
        gate_columns.append(jnp.sum(grad_y * returned[:, route_idx].astype(f32), axis=1))
    gate_part = jnp.stack(gate_columns, axis=1)
    slot_grads = (
        (gate_vals[:, :, None] * grad_y[:, None, :])
        .reshape(tok_rows * route_count, model_width)
        .astype(brain_float16)
    )
    grad_sent = jnp.where(is_filled, slot_grads[source], 0).reshape(
        expert_count, capacity, model_width
    )
    grad_received = to_owner(grad_sent)
    edown_grad = jnp.einsum("erf,erd->efd", expert_act, grad_received, preferred_element_type=f32)
    expert_activation_gradient = jnp.einsum(
        "erd,efd->erf", grad_received, expert_down, preferred_element_type=f32
    )
    expert_gate_gradient, expert_up_gradient = gated_linear_backward(
        gate_up_joined[:, 0], gate_up_joined[:, 1], expert_activation_gradient
    )
    expert_gate_up_gradient = jnp.stack([expert_gate_gradient, expert_up_gradient], axis=1).astype(
        brain_float16
    )
    egu_grad = jnp.einsum(
        "erd,egrf->egdf", received, expert_gate_up_gradient, preferred_element_type=f32
    )
    grad_rows = jnp.einsum(
        "egrf,egdf->erd", expert_gate_up_gradient, expert_gate_up, preferred_element_type=f32
    ).astype(brain_float16)
    grad_back = lax.all_to_all(grad_rows, "expert", split_axis=1, concat_axis=0, tiled=True)
    grad_routes = grad_back.reshape(expert_count * capacity, model_width)[slot_ids].reshape(
        tok_rows, route_count, model_width
    )
    for route_idx in range(route_count):
        grad_hn_part = grad_hn_part + grad_routes[:, route_idx].astype(f32)
    gate_grads = lax.psum(gate_part, "tensor")
    grad_chosen = ROUTE_SCALE * (
        gate_grads / chosen_sum
        - jnp.sum(gate_grads * chosen, axis=1, keepdims=True) / (chosen_sum * chosen_sum)
    )
    grad_sig = jnp.sum(jnp.where(route_hot, grad_chosen[:, :, None], 0.0), axis=1)
    grad_logits = (grad_sig * sigmoid_vals * (1.0 - sigmoid_vals)).astype(brain_float16)
    router_grad = contract_rows(hnormed_b, grad_logits)
    grad_hn = lax.psum(grad_hn_part, "tensor") + contract_cols(grad_logits, router_w)
    grad_hidden_norm, gain_two_grad = rms_backward(hidden, scale_two, gain_two.astype(f32), grad_hn)
    grad_hidden = grad_y + grad_hidden_norm
    grad_hidden_b = grad_hidden.astype(brain_float16)
    out_grad = contract_rows(attended_b, grad_hidden_b)
    grad_att = (
        contract_cols(grad_hidden_b, out_w).reshape(tok_rows, local_heads, DV).astype(brain_float16)
    )
    probs = jnp.exp(score_block() - log_total)
    probs_again = probs.astype(brain_float16)
    grad_probs = jnp.einsum("qhd,khd->hqk", grad_att, values, preferred_element_type=f32)
    grad_vals = jnp.einsum("hqk,qhd->khd", probs_again, grad_att, preferred_element_type=f32)
    row_delta = jnp.sum(probs * grad_probs, axis=-1, keepdims=True)
    grad_scores = (probs * (grad_probs - row_delta)).astype(brain_float16)
    grad_q = jnp.einsum("hqk,khd->qhd", grad_scores, key_all, preferred_element_type=f32) * q_scale
    grad_keys = jnp.einsum("hqk,qhd->khd", grad_scores, q_all, preferred_element_type=f32) * q_scale
    grad_kv = (
        jnp.concatenate([grad_keys[..., :DN], grad_vals], axis=-1)
        .reshape(tok_rows, local_heads * (DN + DV))
        .astype(brain_float16)
    )
    kv_grad = contract_rows(compressed_b, grad_kv)
    grad_comp_part = contract_cols(grad_kv, kv_w)
    grad_krope_part = jnp.sum(grad_keys[..., DN:], axis=1)
    grad_comp, grad_krope = (
        lax.psum(grad_comp_part.astype(jnp.bfloat16), "tensor").astype(jnp.float32),
        lax.psum(grad_krope_part.astype(jnp.bfloat16), "tensor").astype(jnp.float32),
    )
    grad_c, latent_gain_grad = rms_backward(
        latent[:, :rank_width], scale_kv, latent_g.astype(f32), grad_comp
    )
    grad_latent = jnp.concatenate([grad_c, unrotate(grad_krope, cosine, sine_tab)], axis=-1).astype(
        brain_float16
    )
    grad_qrot = unrotate(grad_q[..., DN:], cosine[:, None, :], sine_tab[:, None, :])
    grad_queries = (
        jnp.concatenate([grad_q[..., :DN], grad_qrot], axis=-1)
        .reshape(tok_rows, local_heads * (DN + DR))
        .astype(brain_float16)
    )
    query_grad = contract_rows(normed_b, grad_queries)
    latent_grad = contract_rows(normed_b, grad_latent)
    grad_normed = lax.psum(
        contract_cols(grad_queries, query_w).astype(jnp.bfloat16), "tensor"
    ).astype(jnp.float32) + contract_cols(grad_latent, latent_w)
    grad_x_norm, gain_one_grad = rms_backward(x_float, scale_one, gain_one.astype(f32), grad_normed)
    input_grad = grad_hidden + grad_x_norm
    first_owned = (
        *sent_together(
            (
                gain_one_grad.astype(jnp.bfloat16),
                query_grad.astype(jnp.bfloat16),
                latent_grad.astype(jnp.bfloat16),
            ),
            "expert",
            0,
            1,
        ),
        *sent_together(
            (latent_gain_grad.astype(jnp.bfloat16), kv_grad.astype(jnp.bfloat16)), "expert", 0, 1
        ),
    )
    second_owned = (
        lax.psum_scatter(out_grad, "expert", scatter_dimension=1, tiled=True),
        lax.psum_scatter(gain_two_grad, "expert", scatter_dimension=0, tiled=True),
        lax.psum_scatter(router_grad, "expert", scatter_dimension=0, tiled=True),
        lax.psum_scatter(sgu_grad, "expert", scatter_dimension=1, tiled=True),
        lax.psum_scatter(sdown_grad, "expert", scatter_dimension=1, tiled=True),
    )
    return (
        mixed,
        input_grad,
        first_owned[0],
        first_owned[1],
        first_owned[2],
        first_owned[3],
        first_owned[4],
        second_owned[0],
        second_owned[1],
        second_owned[2],
        second_owned[3],
        second_owned[4],
        egu_grad,
        edown_grad,
    )


def swap_cores(value):
    return lax.ppermute(value, "tensor", [(0, 1), (1, 0)])


def take_rows(value, start, count, axis=0):
    return lax.dynamic_slice_in_dim(value, start, count, axis=axis)


def in_order(core, own, other, axis=0):
    return jnp.where(
        core == 0,
        jnp.concatenate([own, other], axis=axis),
        jnp.concatenate([other, own], axis=axis),
    )


def add_wide(*parts):
    total = parts[0].astype(jnp.float32)
    for part in parts[1:]:
        total = total + part.astype(jnp.float32)
    return total


PLANE = 4


def to_partner(value, flips):
    groups = lax.axis_size("expert")
    return lax.ppermute(value, "expert", [(g, g ^ flips) for g in range(groups)])


def to_deeper(value, step):
    groups = lax.axis_size("expert")
    pairs = [(g, (g + step * PLANE) % groups) for g in range(groups)]
    return lax.ppermute(value, "expert", pairs)


def plane_gather(value):
    return [value] + [to_partner(value, r) for r in range(1, PLANE)]


def plane_scatter(parts):
    return add_wide(parts[0], *[to_partner(parts[r], r) for r in range(1, PLANE)])


def by_place(parts, place):
    odd, high = place % 2 == 1, place // 2 == 1
    parts = [jnp.where(odd, parts[i ^ 1], parts[i]) for i in range(PLANE)]
    return [jnp.where(high, parts[i ^ 2], parts[i]) for i in range(PLANE)]


def tie(*values):
    return lax.optimization_barrier(values)


def deep_pieces(value):
    deep = lax.axis_size("expert") // PLANE
    return [to_deeper(value, s) for s in range(1, deep)]


def one_plane(value, step):
    groups = lax.axis_size("expert")
    pairs = [(g, g + step * PLANE) for g in range(groups) if 0 <= g + step * PLANE < groups]
    return lax.ppermute(value, "expert", pairs)


def deep_hops(value):
    deep = lax.axis_size("expert") // PLANE
    after, before, down, up = [], [], value, value
    for _ in range(1, deep):
        down, up = one_plane(down, 1), one_plane(up, -1)
        after.append(down)
        before.append(up)
    return after, before


def join_hops(hops):
    after, before = hops
    return [a + b for a, b in zip(after, before[::-1])]


def deep_join(value, pieces, z):
    deep = lax.axis_size("expert") // PLANE
    whole = jnp.zeros((deep, *value.shape), value.dtype)
    whole = lax.dynamic_update_index_in_dim(whole, value, z, 0)
    for step in range(1, deep):
        whole = lax.dynamic_update_index_in_dim(whole, pieces[step - 1], (z - step) % deep, 0)
    return whole


def deep_move(blocks, z):
    deep = blocks.shape[0]

    def block(index):
        return lax.dynamic_index_in_dim(blocks, index, 0, keepdims=False)

    return [block(z)] + [to_deeper(block((z + step) % deep), step) for step in range(1, deep)]


def deep_scatter(blocks, z):
    return add_wide(*deep_move(blocks, z))


def share_columns(rows, place):
    parts = [at_index(rows, 0, place)]
    for r in range(1, PLANE):
        parts.append(to_partner(at_index(rows, 0, place ^ r), r))
    return by_place(parts, place)


def all_groups(value):
    return lax.all_gather(value, "expert", axis=0, tiled=False)


def at_index(value, axis, index):
    return lax.dynamic_index_in_dim(value, index, axis, keepdims=False)


def doc_places(doc_lengths, row_count):
    ends_at = jnp.cumsum(doc_lengths)
    position = jnp.arange(row_count, dtype=jnp.int32)
    doc_ids = jnp.sum((position[:, None] >= ends_at[None, :]).astype(jnp.int32), axis=1)
    hitting = doc_ids[:, None] == jnp.arange(doc_lengths.shape[0], dtype=jnp.int32)[None, :]
    start_of = jnp.sum(jnp.where(hitting, (ends_at - doc_lengths)[None, :], 0), axis=1)
    return position - start_of, doc_ids


class HopSum:
    def __init__(self, pieces):
        self.groups = lax.axis_size("expert")
        self.deep = self.groups // PLANE
        self.z = lax.axis_index("expert") // PLANE
        self.pieces = pieces

    def hop(self, step, came=None):
        arrived = []
        for side, way in enumerate((1, -1)):
            target = jnp.clip(self.z + way * (self.deep - step), 0, self.deep - 1)
            gone = self.pieces(target)
            if came is not None:
                gone = add_wide(gone, came[side]).astype(gone.dtype)
            first = range(step) if way == 1 else range(self.deep - step, self.deep)
            pairs = [
                (p * PLANE + q, (p + way) * PLANE + q) for p in first for q in range(PLANE)
            ]
            arrived.append(lax.ppermute(gone, "expert", pairs))
        return arrived

    def total(self, came):
        return add_wide(self.pieces(self.z), *came)


def doc_places(doc_lengths, row_count):
    ends_at = jnp.cumsum(doc_lengths)
    position = jnp.arange(row_count, dtype=jnp.int32)
    doc_ids = jnp.sum((position[:, None] >= ends_at[None, :]).astype(jnp.int32), axis=1)
    hitting = doc_ids[:, None] == jnp.arange(doc_lengths.shape[0], dtype=jnp.int32)[None, :]
    start_of = jnp.sum(jnp.where(hitting, (ends_at - doc_lengths)[None, :], 0), axis=1)
    return position - start_of, doc_ids


def hop_sum(pieces):
    groups = lax.axis_size("expert")
    deep = groups // PLANE
    z = lax.axis_index("expert") // PLANE
    ends = []
    for way in (1, -1):
        came = None
        for step in range(1, deep):
            gone = pieces(jnp.clip(z + way * (deep - step), 0, deep - 1))
            if came is not None:
                gone = add_wide(gone, came).astype(gone.dtype)
            first = range(step) if way == 1 else range(deep - step, deep)
            pairs = [
                (p * PLANE + q, (p + way) * PLANE + q) for p in first for q in range(PLANE)
            ]
            came = lax.ppermute(gone, "expert", pairs)
        ends.append(came)
    return [pieces(z), *ends]


class RowGather:
    def __init__(self, value):
        self.cut = value.shape[0] // 2
        self.value = value

    def along(self):
        return [self.value] + deep_pieces(self.value)

    def lines(self, came):
        return [jnp.stack([v[: self.cut] for v in came]), jnp.stack([v[self.cut :] for v in came])]

    def over(self, lines):
        first, second = lines
        return to_partner(first, 1), to_partner(second, 2)

    def over_other(self, lines):
        first, second = lines
        return to_partner(first, 2), to_partner(second, 1)

    def over_again(self, came):
        beside, behind = came
        return to_partner(beside, 2), to_partner(behind, 1)


def blocks_of(lines, over, over_other, over_again, which):
    first = [lines[0], over[0], over_other[0], over_again and over_again[0]]
    second = [lines[1], over_other[1], over[1], over_again and over_again[1]]
    halves = [jnp.concatenate([half[r] for r in which], axis=0) for half in (first, second)]
    return jnp.concatenate(halves, axis=1)


class RowSum:
    def __init__(self, *terms):
        self.type = terms[0][0].dtype
        cut = terms[0][0].shape[1] // 2
        self.halves = (
            ([[b[:, :cut] for b in v] for v in terms], 2, 1),
            ([[b[:, cut:] for b in v] for v in terms], 1, 2),
        )

    def _add(self, parts):
        return add_wide(*parts).astype(self.type)

    def sends(self):
        return [
            jnp.stack([self._add([v[far] for v in held]), self._add([v[far | near] for v in held])])
            for held, far, near in self.halves
        ]

    def move(self, sends):
        return [to_partner(v, far) for v, (_, far, _) in zip(sends, self.halves)]

    def sends_again(self, came):
        return [
            self._add([v[near] for v in held] + [c[1]])
            for c, (held, _, near) in zip(came, self.halves)
        ]

    def move_again(self, sends):
        return [to_partner(v, near) for v, (_, _, near) in zip(sends, self.halves)]

    def line(self, came, came_again):
        sums = [
            self._add([v[0] for v in held] + [c[0], d])
            for c, d, (held, *_) in zip(came, came_again, self.halves)
        ]
        return jnp.concatenate(sums, axis=1)


def line_sends(line):
    return [line[step] for step in range(line.shape[0])]


def line_move(sends):
    return [sends[0]] + [to_deeper(v, -step) for step, v in enumerate(sends) if step > 0]


def dot_nn(left, right):
    return lax.dot_general(left, right, (((1,), (0,)), ((), ())), preferred_element_type=jnp.float32)


def dot_nt(left, right):
    return lax.dot_general(left, right, (((1,), (1,)), ((), ())), preferred_element_type=jnp.float32)


def dot_tn(left, right):
    return lax.dot_general(left, right, (((0,), (0,)), ((), ())), preferred_element_type=jnp.float32)


def two_lanes(column, lane):
    high = column.astype(jnp.bfloat16).astype(jnp.float32)
    spread = jnp.where(lane == 0, high, jnp.where(lane == 1, column - high, 0.0))
    return spread.astype(jnp.bfloat16)


def expert_kernel(
    shared_cols,
    expert_count,
    me_ref,
    hn_own,
    hn_other,
    dy_own,
    dy_other,
    meta_own,
    meta_other,
    gate_up_w,
    down_w,
    first_w,
    sdown_w,
    slots_out,
    slot_dy_out,
    act_out,
    d_gate_up_out,
    rows_own_out,
    rows_other_out,
    sact_own_out,
    sact_other_out,
    shared_grads_out,
    dgate_own_out,
    dgate_other_out,
):
    f32, bf16 = jnp.float32, jnp.bfloat16
    count, half, _ = hn_own.shape
    tokens = 2 * half
    me = me_ref[0]
    lane = lax.broadcasted_iota(jnp.int32, (count * tokens, LANES), 1)
    is_router = (lane >= shared_cols) & (lane < shared_cols + expert_count)
    first = first_w[...]

    def joined(own, other):
        return jnp.concatenate([v[i] for i in range(count) for v in (own, other)], axis=0)

    rows, rows_dy = joined(hn_own, hn_other), joined(dy_own, dy_other)
    meta = joined(meta_own, meta_other)
    products = dot_nt(rows, first)
    gate, up = products[:, :LANES], products[:, LANES:]
    sig = jax.nn.sigmoid(gate)
    total = jnp.sum(jnp.where(is_router, sig * meta, 0.0), axis=1, keepdims=True)
    mine = jnp.sum(jnp.where(lane == shared_cols + me, sig, 0.0), axis=1, keepdims=True)
    token_gate = two_lanes(ROUTE_SCALE * mine / total, lane)
    sact = (gate * sig * up).astype(bf16)
    d_sact = dot_nt(rows_dy, sdown_w[...])
    d_sgate = d_sact * up * sig * (1.0 + gate * (1.0 - sig))
    dsh = jnp.concatenate([d_sgate, d_sact * gate * sig], axis=1).astype(bf16)
    pick = (meta[:, :1] == lane.astype(f32)).astype(bf16)
    groups = [slice(i * tokens, (i + 1) * tokens) for i in range(count)]
    for i in range(count):
        start = i * tokens
        sact_own_out[i] = sact[start : start + half]
        sact_other_out[i] = sact[start + half : start + tokens]
    slots = [dot_tn(pick[g], rows[g]).astype(bf16) for g in groups]
    slot_dys = [dot_tn(pick[g], rows_dy[g]).astype(bf16) for g in groups]
    slot_gates = [
        jnp.sum(dot_tn(pick[g], token_gate[g]), axis=1, keepdims=True) for g in groups
    ]

    @pl.when(pl.program_id(0) == 0)
    def _():
        shared_grads_out[...] = jnp.zeros_like(shared_grads_out)

    first_grad, sdown_grad = dot_tn(dsh, rows), dot_tn(sact, rows_dy)
    shared_grads_out[:shared_cols] += first_grad[:shared_cols]
    shared_grads_out[shared_cols : 2 * shared_cols] += first_grad[LANES : LANES + shared_cols]
    shared_grads_out[2 * shared_cols :] += sdown_grad[:shared_cols]
    slot_rows = jnp.concatenate(slots, axis=0)
    slot_dy = jnp.concatenate(slot_dys, axis=0)
    slot_gate = jnp.concatenate(slot_gates, axis=0)
    slots_out[...] = slot_rows
    slot_dy_out[...] = slot_dy
    gate = dot_nt(slot_rows, gate_up_w[0])
    up = dot_nt(slot_rows, gate_up_w[1])
    d_act = dot_nt(slot_dy, down_w[...])
    sig = jax.nn.sigmoid(gate)
    silu = gate * sig
    act = silu * up
    slot_dgate = jnp.sum(act * d_act, axis=1, keepdims=True)
    act_out[...] = (slot_gate * act).astype(bf16)
    d_act = slot_gate * d_act
    d_gate = (d_act * up * sig * (1.0 + gate * (1.0 - sig))).astype(bf16)
    d_up = (d_act * silu).astype(bf16)
    d_gate_up_out[0] = d_gate
    d_gate_up_out[1] = d_up
    d_slots = (dot_nn(d_gate, gate_up_w[0]) + dot_nn(d_up, gate_up_w[1])).astype(bf16)
    slot_lane = lax.broadcasted_iota(jnp.int32, (LANES, LANES), 1)
    d_shared = dot_nn(dsh, first)
    for i, g in enumerate(groups):
        here = slice(i * LANES, (i + 1) * LANES)
        d_rows = (dot_nn(pick[g], d_slots[here]) + d_shared[g]).astype(bf16)
        rows_own_out[i], rows_other_out[i] = d_rows[:half], d_rows[half:]
        dgate = dot_nn(pick[g], two_lanes(slot_dgate[here], slot_lane))
        dgate_own_out[i], dgate_other_out[i] = dgate[:half], dgate[half:]


def block_specs(per_step):
    def lead(*tail):
        return pl.BlockSpec((per_step, *tail), lambda i: (i,) + (0,) * len(tail))

    def flat(cols):
        return pl.BlockSpec((per_step * LANES, cols), lambda i: (i, 0))

    def whole(a):
        return pl.BlockSpec(a.shape, lambda i: (0,) * a.ndim, pipeline_mode=pl.Buffered(1))

    return lead, flat, whole


def experts(
    me,
    hn_own,
    hn_other,
    dy_own,
    dy_other,
    meta_own,
    meta_other,
    gate_up_w,
    down_w,
    first_w,
    sdown_w,
    shared_cols,
    expert_count,
    per_step=2,
):
    groups, half, width = hn_own.shape
    hidden = down_w.shape[0]
    slots = groups * LANES
    f32, bf16 = jnp.float32, jnp.bfloat16
    lead, flat, whole = block_specs(per_step)
    sds = jax.ShapeDtypeStruct
    return pl.pallas_call(
        functools.partial(expert_kernel, shared_cols, expert_count),
        grid=(groups // per_step,),
        in_specs=[
            pl.BlockSpec(memory_space=pltpu.SMEM),
            *[lead(half, width)] * 4,
            *[lead(half, LANES)] * 2,
            *[whole(a) for a in (gate_up_w, down_w, first_w, sdown_w)],
        ],
        out_specs=[
            flat(width),
            flat(width),
            flat(hidden),
            pl.BlockSpec((2, per_step * LANES, hidden), lambda i: (0, i, 0)),
            *[lead(half, width)] * 2,
            *[lead(half, LANES)] * 2,
            pl.BlockSpec((3 * shared_cols, width), lambda i: (0, 0)),
            *[lead(half, LANES)] * 2,
        ],
        out_shape=[
            sds((slots, width), bf16),
            sds((slots, width), bf16),
            sds((slots, hidden), bf16),
            sds((2, slots, hidden), bf16),
            *[sds((groups, half, width), bf16)] * 2,
            *[sds((groups, half, LANES), bf16)] * 2,
            sds((3 * shared_cols, width), f32),
            *[sds((groups, half, LANES), f32)] * 2,
        ],
        compiler_params=pltpu.CompilerParams(vmem_limit_bytes=58 * 1024 * 1024),
        cost_estimate=pl.CostEstimate(
            flops=groups * width, bytes_accessed=groups * width, transcendentals=0
        ),
    )(
        me,
        hn_own,
        hn_other,
        dy_own,
        dy_other,
        meta_own,
        meta_other,
        gate_up_w,
        down_w,
        first_w,
        sdown_w,
    )


def swap_halves(value, lane):
    low = lane % DR < DR // 2
    return jnp.where(low, pltpu.roll(value, LANES - DR // 2, 1), pltpu.roll(value, DR // 2, 1))


def by_core(core, first, second):
    return jnp.where(core == 0, first, second), jnp.where(core == 0, second, first)


def head_scores(q, kv, k_rope, visible, lane, head, heads):
    q_nope = q[:, head * DN : (head + 1) * DN]
    q_rope = jnp.where(lane // DR == head, q[:, heads * DN :], jnp.zeros((), q.dtype))
    at = head * (DN + DV)
    k_nope, value = kv[:, at : at + DN], kv[:, at + DN : at + DN + DV]
    scores = (dot_nt(q_nope, k_nope) + dot_nt(q_rope, k_rope)) * (DN + DR) ** -0.5
    return jnp.where(visible, scores, NEGATIVE), q_nope, q_rope, k_nope, value


def seen(doc_col, doc_row):
    rows = doc_col.shape[0]
    later = lax.broadcasted_iota(jnp.int32, (rows, rows), 0) >= lax.broadcasted_iota(
        jnp.int32, (rows, rows), 1
    )
    return (doc_col == doc_row) & later


def attention_kernel(
    heads,
    rank,
    core_ref,
    x_own,
    x_other,
    gain,
    latent_gain,
    head_w,
    small_w,
    kv_w,
    cosine,
    sine,
    doc_col,
    doc_row,
    normed_out,
    compressed_out,
    q_out,
    kv_out,
    k_rope_out,
    sums_out,
    attended_out,
    latent_out,
    part_own_out,
    part_other_out,
):
    f32, bf16 = jnp.float32, jnp.bfloat16
    core = core_ref[0]
    x = jnp.concatenate(by_core(core, x_own[0], x_other[0]), axis=0).astype(f32)
    rows = x.shape[0]
    half = rows // 2
    lane = lax.broadcasted_iota(jnp.int32, (rows, LANES), 1)
    inverse = lax.rsqrt(jnp.mean(x * x, axis=1, keepdims=True) + EPSILON)
    normed = (x * inverse * gain[...]).astype(bf16)
    normed_out[0] = normed
    q_cols = heads * (DN + DR)
    queries = dot_nn(normed, head_w[:, :q_cols])
    q_rope = queries[:, heads * DN :]
    q_rope = q_rope * cosine[0] + swap_halves(q_rope, lane) * sine[0]
    q = jnp.concatenate([queries[:, : heads * DN], q_rope], axis=1).astype(bf16)
    q_out[0] = q
    latent = dot_nn(normed, small_w[:, : rank + LANES])
    latent_out[0] = latent
    squeezed = latent[:, :rank]
    inverse = lax.rsqrt(jnp.mean(squeezed * squeezed, axis=1, keepdims=True) + EPSILON)
    compressed = (squeezed * inverse * latent_gain[...]).astype(bf16)
    compressed_out[0] = compressed
    k_rope = latent[:, rank:]
    k_rope = (k_rope * cosine[0] + swap_halves(k_rope, lane) * sine[0]).astype(bf16)
    k_rope_out[0] = k_rope
    kv = dot_nn(compressed, kv_w[...]).astype(bf16)
    kv_out[0] = kv
    visible = seen(doc_col[0], doc_row[0])
    attended, sums = [], jnp.zeros((rows, LANES), f32)
    for head in range(heads):
        scores, *_, value = head_scores(q, kv, k_rope, visible, lane, head, heads)
        top = jnp.max(scores, axis=1, keepdims=True)
        log_total = top + jnp.log(jnp.sum(jnp.exp(scores - top), axis=1, keepdims=True))
        sums = jnp.where(lane == head, log_total, sums)
        probs = jnp.exp(scores - log_total).astype(bf16)
        attended.append(dot_nn(probs, value).astype(bf16))
    sums_out[0] = sums
    attended = jnp.concatenate(attended, axis=1)
    attended_out[0] = attended
    part = dot_nt(attended, head_w[:, q_cols : q_cols + heads * DV]).astype(bf16)
    part_own_out[0], part_other_out[0] = by_core(core, part[:half], part[half:])


def attention_backward_kernel(
    heads,
    core_ref,
    d_own,
    d_other,
    normed_ref,
    compressed_ref,
    q_ref,
    kv_ref,
    k_rope_ref,
    sums_ref,
    attended_ref,
    head_w,
    kv_w,
    cosine,
    sine,
    doc_col,
    doc_row,
    head_grad_out,
    kv_grad_out,
    normed_own_out,
    normed_other_out,
    latent_own_out,
    latent_other_out,
    head_acc,
    kv_acc,
):
    f32, bf16 = jnp.float32, jnp.bfloat16
    core, step = core_ref[0], pl.program_id(0)
    scale = (DN + DR) ** -0.5
    d_rows = jnp.concatenate(by_core(core, d_own[0], d_other[0]), axis=0)
    rows = d_rows.shape[0]
    half = rows // 2
    lane = lax.broadcasted_iota(jnp.int32, (rows, LANES), 1)
    q_cols = heads * (DN + DR)
    q, kv, k_rope = q_ref[0], kv_ref[0], k_rope_ref[0]
    d_attended = dot_nn(d_rows, head_w[:, q_cols : q_cols + heads * DV]).astype(bf16)
    visible = seen(doc_col[0], doc_row[0])
    d_q, d_kv = [], []
    d_q_rope, d_k_rope = jnp.zeros((rows, LANES), f32), jnp.zeros((rows, LANES), f32)
    for head in range(heads):
        scores, q_nope, q_rope, k_nope, value = head_scores(
            q, kv, k_rope, visible, lane, head, heads
        )
        probs = jnp.exp(scores - sums_ref[0][:, head : head + 1])
        d_head = d_attended[:, head * DV : (head + 1) * DV]
        d_probs = dot_nt(d_head, value)
        d_value = dot_tn(probs.astype(bf16), d_head)
        delta = jnp.sum(probs * d_probs, axis=1, keepdims=True)
        d_scores = (probs * (d_probs - delta)).astype(bf16)
        d_q.append(dot_nn(d_scores, k_nope) * scale)
        d_q_rope = jnp.where(lane // DR == head, dot_nn(d_scores, k_rope) * scale, d_q_rope)
        d_kv += [dot_tn(d_scores, q_nope) * scale, d_value]
        d_k_rope += dot_tn(d_scores, q_rope) * scale
    d_q_rope = d_q_rope * cosine[0] - swap_halves(d_q_rope, lane) * sine[0]
    d_q = jnp.concatenate(d_q + [d_q_rope], axis=1).astype(bf16)
    d_kv = jnp.concatenate(d_kv, axis=1).astype(bf16)

    @pl.when(step == 0)
    def _():
        head_acc[...] = jnp.zeros_like(head_acc)
        kv_acc[...] = jnp.zeros_like(kv_acc)

    head_acc[:, :q_cols] += dot_tn(normed_ref[0], d_q)
    head_acc[:, q_cols:] += dot_tn(d_rows, attended_ref[0])
    kv_acc[...] += dot_tn(compressed_ref[0], d_kv)

    @pl.when(step == pl.num_programs(0) - 1)
    def _():
        head_grad_out[...] = head_acc[...].astype(bf16)
        kv_grad_out[...] = kv_acc[...].astype(bf16)

    part = dot_nt(d_q, head_w[:, :q_cols]).astype(bf16)
    normed_own_out[0], normed_other_out[0] = by_core(core, part[:half], part[half:])
    latent = jnp.concatenate([dot_nt(d_kv, kv_w[...]), d_k_rope], axis=1).astype(bf16)
    latent_own_out[0], latent_other_out[0] = by_core(core, latent[:half], latent[half:])


def one_each(*tail):
    return pl.BlockSpec((1, *tail), lambda i: (i,) + (0,) * len(tail))


def kept(value):
    return pl.BlockSpec(value.shape, lambda i: (0,) * value.ndim, pipeline_mode=pl.Buffered(1))


def attention(core, x_own, x_other, gain, latent_gain, head_w, small_w, kv_w, cosine, sine, doc):
    near, half, width = x_own.shape
    rows = 2 * half
    rank, kv_cols = kv_w.shape
    heads = kv_cols // (DN + DV)
    f32, bf16 = jnp.float32, jnp.bfloat16
    shapes = [
        ((rows, width), bf16),
        ((rows, rank), bf16),
        ((rows, heads * (DN + DR)), bf16),
        ((rows, kv_cols), bf16),
        ((rows, LANES), bf16),
        ((rows, LANES), f32),
        ((rows, heads * DV), bf16),
        ((rows, rank + LANES), f32),
        ((half, width), bf16),
        ((half, width), bf16),
    ]
    return pl.pallas_call(
        functools.partial(attention_kernel, heads, rank),
        grid=(near,),
        in_specs=[
            pl.BlockSpec(memory_space=pltpu.SMEM),
            *[one_each(half, width)] * 2,
            *[kept(a) for a in (gain, latent_gain, head_w, small_w, kv_w)],
            *[one_each(rows, LANES)] * 2,
            one_each(rows, 1),
            one_each(1, rows),
        ],
        out_specs=[one_each(*shape) for shape, _ in shapes],
        out_shape=[jax.ShapeDtypeStruct((near, *shape), kind) for shape, kind in shapes],
        compiler_params=pltpu.CompilerParams(vmem_limit_bytes=58 * 1024 * 1024),
        cost_estimate=pl.CostEstimate(
            flops=2 * near * rows * width * (rank + 3 * heads * DN),
            bytes_accessed=4 * near * rows * width,
            transcendentals=0,
        ),
    )(
        core,
        x_own,
        x_other,
        gain,
        latent_gain,
        head_w,
        small_w,
        kv_w,
        cosine,
        sine,
        doc[:, :, None],
        doc[:, None, :],
    )


def attention_backward(core, d_own, d_other, kept_rows, head_w, kv_w, cosine, sine, doc):
    near, half, width = d_own.shape
    rows = 2 * half
    rank, kv_cols = kv_w.shape
    heads = kv_cols // (DN + DV)
    head_cols = heads * (DN + DR + DV)
    f32, bf16 = jnp.float32, jnp.bfloat16
    sds = jax.ShapeDtypeStruct
    return pl.pallas_call(
        functools.partial(attention_backward_kernel, heads),
        grid=(near,),
        in_specs=[
            pl.BlockSpec(memory_space=pltpu.SMEM),
            *[one_each(half, width)] * 2,
            *[one_each(*v.shape[1:]) for v in kept_rows],
            *[kept(a) for a in (head_w, kv_w)],
            *[one_each(rows, LANES)] * 2,
            one_each(rows, 1),
            one_each(1, rows),
        ],
        out_specs=[
            pl.BlockSpec((width, head_cols), lambda i: (0, 0)),
            pl.BlockSpec((rank, kv_cols), lambda i: (0, 0)),
            *[one_each(half, width)] * 2,
            *[one_each(half, rank + LANES)] * 2,
        ],
        out_shape=[
            sds((width, head_cols), bf16),
            sds((rank, kv_cols), bf16),
            *[sds((near, half, width), bf16)] * 2,
            *[sds((near, half, rank + LANES), bf16)] * 2,
        ],
        scratch_shapes=[
            pltpu.VMEM((width, head_cols), f32),
            pltpu.VMEM((rank, kv_cols), f32),
        ],
        compiler_params=pltpu.CompilerParams(vmem_limit_bytes=58 * 1024 * 1024),
        cost_estimate=pl.CostEstimate(
            flops=near * rows * width * heads * DN,
            bytes_accessed=2 * near * rows * width,
            transcendentals=0,
        ),
    )(
        core,
        d_own,
        d_other,
        *kept_rows,
        head_w,
        kv_w,
        cosine,
        sine,
        doc[:, :, None],
        doc[:, None, :],
    )


def product_kernel(*refs):
    *operands, out_ref = refs
    count = len(operands) // 2
    total = 0.0
    for left_ref, right_ref in zip(operands[:count], operands[count:]):
        total += dot_tn(left_ref[0], right_ref[...])
    out_ref[0] = total


def column_products(lefts, rights, tile=512):
    count, _, height = lefts[0].shape
    width = rights[0].shape[1]
    return pl.pallas_call(
        product_kernel,
        grid=(width // tile, count),
        in_specs=[
            *[pl.BlockSpec((1, v.shape[1], height), lambda j, i: (i, 0, 0)) for v in lefts],
            *[pl.BlockSpec((v.shape[0], tile), lambda j, i: (0, j)) for v in rights],
        ],
        out_specs=pl.BlockSpec((1, height, tile), lambda j, i: (i, 0, j)),
        out_shape=jax.ShapeDtypeStruct((count, height, width), jnp.float32),
        compiler_params=pltpu.CompilerParams(vmem_limit_bytes=58 * 1024 * 1024),
        cost_estimate=pl.CostEstimate(flops=width, bytes_accessed=width, transcendentals=0),
    )(*lefts, *rights)


def output_kernel(act, sact_own, sact_other, meta_own, meta_other, down_w, sdown_w, own_out, other_out):
    f32, bf16 = jnp.float32, jnp.bfloat16
    count, half, _ = meta_own.shape
    lane = lax.broadcasted_iota(jnp.int32, (2 * half, LANES), 1).astype(f32)
    out = dot_nn(act[...], down_w[...]).astype(bf16)
    for i in range(count):
        meta = jnp.concatenate([meta_own[i], meta_other[i]], axis=0)
        pick = (meta[:, :1] == lane).astype(bf16)
        sact = jnp.concatenate([sact_own[i], sact_other[i]], axis=0)
        here = slice(i * LANES, (i + 1) * LANES)
        rows = (dot_nn(pick, out[here]) + dot_nn(sact, sdown_w[...])).astype(bf16)
        own_out[i], other_out[i] = rows[:half], rows[half:]


def outputs(act, sact_own, sact_other, meta_own, meta_other, down_w, sdown_w, per_step=4):
    groups, half, _ = meta_own.shape
    hidden, width = down_w.shape
    lead, flat, whole = block_specs(per_step)
    return pl.pallas_call(
        output_kernel,
        grid=(groups // per_step,),
        in_specs=[
            flat(hidden),
            *[lead(half, LANES)] * 4,
            *[whole(a) for a in (down_w, sdown_w)],
        ],
        out_specs=[lead(half, width)] * 2,
        out_shape=[jax.ShapeDtypeStruct((groups, half, width), jnp.bfloat16)] * 2,
        compiler_params=pltpu.CompilerParams(vmem_limit_bytes=58 * 1024 * 1024),
        cost_estimate=pl.CostEstimate(
            flops=groups * half * LANES * width,
            bytes_accessed=groups * half * width,
            transcendentals=0,
        ),
    )(act, sact_own, sact_other, meta_own, meta_other, down_w, sdown_w)


def token_plan(
    inputs,
    attn_gain,
    w_query,
    w_latent,
    latent_gain,
    w_kv,
    w_out,
    ffn_gain,
    w_router,
    shared_gate_up,
    shared_down,
    expert_gate_up,
    expert_down,
    lengths,
    routes,
    cotangent,
):
    f32, bf16 = jnp.float32, jnp.bfloat16
    core, me = lax.axis_index("tensor"), lax.axis_index("expert")
    groups = lax.axis_size("expert")
    deep, place, z = groups // PLANE, me % PLANE, me // PLANE
    tok_rows, width = inputs.shape
    half = tok_rows // 2
    own_at, other_at = core * half, (1 - core) * half
    expert_count = w_router.shape[1]
    route_count = routes.shape[1]
    capacity = tok_rows * route_count * 4 // (3 * expert_count)
    shared_cols = shared_gate_up.shape[2] // groups
    latent_cols, rank_width = w_latent.shape[1], latent_gain.shape[0] * groups
    block_rows = w_query.shape[0]
    kv_rows = w_kv.shape[0]

    query_cols = w_query.shape[1] // PLANE
    out_cols = w_out.shape[0] // PLANE
    small = jnp.concatenate(
        [
            w_latent,
            w_latent[:, rank_width:],
            w_router,
            attn_gain[:, None],
            ffn_gain[:, None],
            jnp.pad(latent_gain, (0, block_rows - kv_rows))[:, None],
        ],
        axis=1,
    )
    small_cols = small.shape[1]
    route_half = take_rows(routes, own_at, half).astype(bf16).reshape(block_rows // 2, -1)
    length_col = jnp.pad(lengths[0].astype(bf16), (0, block_rows // 2 - lengths.shape[1]))[:, None]
    route_cols = route_half.shape[1] + 1
    small_half = jnp.concatenate(
        [
            take_rows(small, core * (block_rows // 2), block_rows // 2),
            route_half,
            length_col,
            jnp.zeros((block_rows // 2, -(small_cols + route_cols) % (2 * LANES)), bf16),
        ],
        axis=1,
    )
    packed_cols = small_half.shape[1] // 2
    small_packed = jnp.concatenate([small_half[:, :packed_cols], small_half[:, packed_cols:]])
    kv_cols = w_kv.shape[1] // PLANE
    kv_parts = block_rows // kv_rows
    kv_piece = kv_cols // kv_parts
    w_out_t = w_out.T

    local_heads = query_cols // (DN + DR)

    def by_parts(block):
        heads = [block[:, h * (DN + DR) : (h + 1) * (DN + DR)] for h in range(local_heads)]
        return [h[:, :DN] for h in heads] + [h[:, DN:] for h in heads]

    def quarter(index):
        kv_here = take_rows(w_kv, index * kv_cols, kv_cols, axis=1)
        kv_here = [kv_here[:, p * kv_piece : (p + 1) * kv_piece] for p in range(kv_parts)]
        return jnp.concatenate(
            [
                *by_parts(take_rows(w_query, index * query_cols, query_cols, axis=1)),
                take_rows(w_out_t, index * out_cols, out_cols, axis=1),
                jnp.concatenate(kv_here, axis=0),
            ],
            axis=1,
        )

    near_w = [quarter(place)] + [to_partner(quarter(place ^ r), r) for r in range(1, PLANE)]
    small_line = deep_join(small_packed, deep_pieces(small_packed), z)
    near_w, small_line = tie(near_w, small_line)
    plane_w = jnp.stack(by_place(near_w, place))
    small_sent, x_sent, plane_w = tie(
        small_line.swapaxes(0, 1), take_rows(inputs, own_at, half), plane_w
    )
    small_sent = jnp.stack([small_sent, to_partner(small_sent, 1)])
    small_sent = jnp.concatenate([small_sent, to_partner(small_sent, 2)], axis=0)
    x_sent = jnp.stack([x_sent, to_partner(x_sent, 2)])
    x_came = to_partner(x_sent, 1)
    x_near_own = jnp.stack([x_sent[0], x_came[0], x_sent[1], x_came[1]])
    x_near_other = swap_cores(x_near_own)
    deep_w = deep_hops(plane_w)
    small_parts = [small_sent[r].swapaxes(0, 1) for r in range(PLANE)]
    small_own = jnp.stack(by_place(small_parts, place), axis=1)
    small_own = small_own.reshape(groups, block_rows, packed_cols)
    small_own = jnp.concatenate(
        [small_own[:, : block_rows // 2], small_own[:, block_rows // 2 :]], axis=2
    )
    small_other = swap_cores(small_own)
    small_all = in_order(core, small_own, small_other, axis=1)
    small_all, x_near_other, deep_w = tie(small_all, x_near_other, deep_w)
    head_w = deep_join(plane_w, join_hops(deep_w), z)
    length_at = small_cols + route_cols - 1
    lengths_near = take_rows(small_own, z * PLANE, PLANE)[:, : lengths.shape[1], length_at]
    lengths_near = lengths_near.astype(jnp.int32)
    lengths_near = jnp.stack(by_place([lengths_near[r] for r in range(PLANE)], place))
    shared_rows = jnp.concatenate(
        [shared_gate_up[0].T, shared_gate_up[1].T, shared_down], axis=0
    ).reshape(3, groups, shared_cols, block_rows)
    shared_rows = shared_rows.swapaxes(0, 1).reshape(groups, 3 * shared_cols, block_rows)
    dy_sent, head_w = tie(take_rows(cotangent, own_at, half), head_w)
    dy_own_rows = take_rows(cotangent, own_at, half)
    dy_gather = RowGather(dy_sent)
    dy_came = dy_gather.along()
    head_w = head_w.reshape(groups, block_rows, -1)
    flat_head = head_w.reshape(groups * block_rows, -1)
    at = query_cols + out_cols
    kv_w = head_w[:, :, at : at + kv_piece].reshape(groups, kv_parts, kv_rows, kv_piece)
    kv_w = kv_w.transpose(0, 2, 1, 3).reshape(groups * kv_rows, kv_cols)

    block_index = jnp.arange(groups)
    block_chip = (z - block_index % deep) % deep * PLANE + (place ^ (block_index // deep))
    in_blocks = (block_chip[:, None] == block_index[None, :]).astype(bf16)

    def routes_of(came):
        came = came[:, :, small_cols : small_cols + route_half.shape[1]].reshape(groups, -1)
        came = jnp.dot(in_blocks, came, preferred_element_type=f32)
        return came.astype(jnp.int32).reshape(groups, half, route_count)

    routes_own, routes_other = routes_of(small_own), routes_of(small_other)
    flat_small = small_all.reshape(groups * block_rows, -1)
    latent_w = flat_small[:, :latent_cols]
    at = rank_width + LANES
    router_w = flat_small[:, at : at + expert_count]
    at += expert_count
    gain_one, gain_two = flat_small[:, at], flat_small[:, at + 1]
    latent_g = small_all[:, :kv_rows, at + 2].reshape(-1)

    near_rows = PLANE * tok_rows
    relative, doc = jax.vmap(lambda one: doc_places(one, tok_rows))(lengths_near)
    cosine, sine_tab = rope_tables(relative.reshape(-1), DR)
    cosine, sine_tab = [v.reshape(PLANE, tok_rows, -1) for v in (cosine, sine_tab)]
    rope = (
        jnp.concatenate([cosine] * 4, axis=-1),
        jnp.concatenate([-sine_tab, sine_tab] * 2, axis=-1),
        doc.astype(f32),
    )
    core_index = core.reshape(1).astype(jnp.int32)
    *kept_rows, latent, part_own, part_other = attention(
        core_index,
        x_near_own,
        x_near_other,
        gain_one.astype(f32)[None],
        latent_g.astype(f32)[None],
        flat_head,
        flat_small,
        kv_w,
        *rope,
    )
    normed_b = kept_rows[0].reshape(near_rows, width)

    def sum_cores(own, other):
        return add_wide(own, swap_cores(other)).astype(bf16)

    def sum_plane(both):
        return plane_scatter([both[r] for r in range(PLANE)])

    part_own, part_other, dy_came = tie(part_own, part_other, dy_came)
    attn_own = sum_plane(sum_cores(part_own, part_other))
    x_own = take_rows(inputs, own_at, half).astype(f32)
    hidden = x_own + attn_own
    hnormed, scale_two = rms_forward(hidden, gain_two.astype(f32))
    hnormed_b = hnormed.astype(bf16)
    normed_cols = jnp.concatenate(
        [
            take_rows(normed_b, (k * PLANE + place) * block_rows, block_rows, axis=1)
            for k in range(deep)
        ],
        axis=1,
    )
    hnormed_b, normed_cols, shared_rows = tie(hnormed_b, normed_cols, shared_rows)
    dy_lines = dy_gather.lines(dy_came)
    def membership(named):
        one_hot = named[..., None] == jnp.arange(expert_count, dtype=jnp.int32)
        return jnp.any(named == me, axis=-1), jnp.any(one_hot, axis=2)

    member_own, hot_own = membership(routes_own)
    member_other, hot_other = membership(routes_other)
    lower = (
        jnp.arange(half, dtype=jnp.int32)[:, None] <= jnp.arange(half, dtype=jnp.int32)[None, :]
    ).astype(bf16)

    def running(mask):
        counts = jnp.dot(mask.astype(bf16), lower, preferred_element_type=f32)
        return counts.astype(jnp.int32)

    count_own, count_other = running(member_own), running(member_other)
    place_own = jnp.where(member_own, count_own - 1, -1)
    place_other = jnp.where(member_other, count_own[:, -1:] + count_other - 1, -1)

    def metadata(slot, hot):
        return jnp.concatenate(
            [
                slot[..., None].astype(f32),
                jnp.zeros((groups, half, shared_cols - 1), f32),
                hot.astype(f32),
                jnp.zeros((groups, half, LANES - shared_cols - expert_count), f32),
            ],
            axis=-1,
        )

    meta_own, meta_other = metadata(place_own, hot_own), metadata(place_other, hot_other)
    hn_gather = RowGather(hnormed_b)
    dy_over, dy_other_way = dy_gather.over(dy_lines), dy_gather.over_other(dy_lines)
    dy_again = dy_gather.over_again(dy_over)
    shared_w = lax.all_to_all(shared_rows, "expert", split_axis=0, concat_axis=0, tiled=True)
    hn_came, dy_over, dy_other_way, dy_again, shared_w = tie(
        hn_gather.along(), dy_over, dy_other_way, dy_again, shared_w
    )
    shared_w = shared_w.swapaxes(0, 1).reshape(3 * shared_cols, groups * block_rows)
    first_w = jnp.concatenate(
        [
            shared_w[:shared_cols],
            router_w.T,
            jnp.zeros((LANES - shared_cols - expert_count, width), bf16),
            shared_w[shared_cols : 2 * shared_cols],
            jnp.zeros((LANES - shared_cols, width), bf16),
        ],
        axis=0,
    )
    sdown_rows = jnp.pad(shared_w[2 * shared_cols :], ((0, LANES - shared_cols), (0, 0)))
    gate_up_w, down_w = jnp.swapaxes(expert_gate_up[0], 1, 2), expert_down[0]

    def run_experts(which, hn_part, hn_part_other):
        at, to = which[0] * deep, (which[-1] + 1) * deep
        return experts(
            me.reshape(1).astype(jnp.int32),
            hn_part,
            hn_part_other,
            *dy_parts[which],
            meta_own[at:to],
            meta_other[at:to],
            gate_up_w,
            down_w,
            first_w,
            sdown_rows,
            shared_cols,
            expert_count,
        )

    hn_lines = hn_gather.lines(hn_came)
    hn_lines, dy_over = tie(hn_lines, dy_over)
    parts = ((0,), (1, 2), (3,))
    dy_mine = [blocks_of(dy_lines, dy_over, dy_other_way, dy_again, p) for p in parts]
    dy_parts = [(v, swap_cores(v)) for v in dy_mine]
    hn_line = jnp.concatenate(hn_lines, axis=1)
    hn_over, hn_line_other, dy_parts, meta_own, meta_other, first_w, sdown_rows = tie(
        hn_gather.over(hn_lines),
        swap_cores(hn_line),
        dy_parts,
        meta_own,
        meta_other,
        first_w,
        sdown_rows,
    )
    dy_parts = dict(zip(parts, dy_parts))
    hn_other_way, done_line = tie(
        hn_gather.over_other(hn_lines), run_experts(parts[0], hn_line, hn_line_other)
    )
    d_line_came = swap_cores(done_line[5])
    hn_near = blocks_of(hn_lines, hn_over, hn_other_way, None, parts[1])
    hn_again, done_near = tie(
        hn_gather.over_again(hn_over), run_experts(parts[1], hn_near, swap_cores(hn_near))
    )
    d_near_came = swap_cores(done_near[5])
    hn_far = blocks_of(hn_lines, hn_over, hn_other_way, hn_again, parts[2])
    done_far = run_experts(parts[2], hn_far, swap_cores(hn_far))
    done = (done_line, done_near, done_far)
    slot_rows, slot_dy, slot_act, d_gate_up = [[v[i] for v in done] for i in range(4)]
    shared_grads = add_wide(*[v[8] for v in done])

    def by_flips(line, near, far):
        return [line, near[:deep], near[deep:], far]

    d_rows_own = by_flips(*[v[4] for v in done])
    d_rows_came = by_flips(d_line_came, d_near_came, swap_cores(done_far[5]))

    def two_parts(value):
        return value[..., 0] + value[..., 1]

    dgate_own, dgate_other = [
        jnp.concatenate([two_parts(v[i]) for v in done], axis=0) for i in (9, 10)
    ]
    dgate_sent = dgate_own + swap_cores(dgate_other)
    dgate_high = dgate_sent.astype(bf16)
    dgate_low = (dgate_sent - dgate_high.astype(f32)).astype(bf16)
    d_rows_came, dgate_high, dgate_low = tie(d_rows_came, dgate_high, dgate_low)
    d_sum = RowSum(d_rows_own, d_rows_came)
    sends, shared_grads, slot_act = tie(d_sum.sends(), shared_grads, slot_act)
    came = d_sum.move(sends)
    gate_rows = jnp.stack([contract_rows(in_blocks, v).reshape(-1) for v in (dgate_high, dgate_low)])
    grads_sent = jnp.concatenate([shared_grads, gate_rows], axis=0).astype(bf16)
    grads_sent = grads_sent.reshape(-1, groups, block_rows)
    grads_came = lax.all_to_all(grads_sent, "expert", split_axis=1, concat_axis=1, tiled=True)
    out_done = [
        outputs(
            act,
            v[6],
            v[7],
            meta_own[p[0] * deep : (p[-1] + 1) * deep],
            meta_other[p[0] * deep : (p[-1] + 1) * deep],
            down_w,
            sdown_rows,
        )
        for act, v, p in zip(slot_act, done, parts)
    ]
    edown_grad = column_products([v[None] for v in slot_act], slot_dy)[0]
    came, out_done, edown_grad, grads_came = tie(came, out_done, edown_grad, grads_came)
    dgate = add_wide(grads_came[3 * shared_cols], grads_came[3 * shared_cols + 1]).T
    sends, slot_rows, out_done = tie(d_sum.sends_again(came), slot_rows, out_done)
    came_again = d_sum.move_again(sends)
    egu_grad = column_products(d_gate_up, slot_rows).swapaxes(1, 2)
    out_own = by_flips(*[v[0] for v in out_done])
    out_came = by_flips(*[swap_cores(v[1]) for v in out_done])
    out_sum = RowSum(out_own, out_came)
    out_sends = out_sum.sends()
    came_again, egu_grad, out_sends = tie(came_again, egu_grad, out_sends)
    z_sends, out_sends, dgate = tie(
        line_sends(d_sum.line(came, came_again)), out_sends, dgate
    )
    z_came = line_move(z_sends)
    out_first = out_sum.move(out_sends)
    hot_mine = take_rows(
        jnp.any(routes[..., None] == jnp.arange(expert_count, dtype=jnp.int32), axis=1), own_at, half
    )
    sig = jax.nn.sigmoid(jnp.dot(hnormed_b, router_w, preferred_element_type=f32))
    chosen = jnp.where(hot_mine, sig, 0.0)
    chosen_sum = jnp.sum(chosen, axis=1, keepdims=True)
    dgate = jnp.where(hot_mine, dgate, 0.0)
    inner = jnp.sum(dgate * chosen, axis=1, keepdims=True)
    d_chosen = ROUTE_SCALE * (dgate / chosen_sum - inner / (chosen_sum * chosen_sum))
    d_logits = (jnp.where(hot_mine, d_chosen, 0.0) * sig * (1.0 - sig)).astype(bf16)
    router_grad = contract_rows(d_logits, hnormed_b)
    z_came, d_logits, router_grad = tie(z_came, d_logits, router_grad)
    d_hn = add_wide(*z_came)
    d_hn = d_hn + contract_cols(d_logits, router_w)
    d_hidden_norm, gain_two_grad = rms_backward(hidden, scale_two, gain_two.astype(f32), d_hn)
    d_hidden = dy_own_rows.astype(f32) + d_hidden_norm
    d_parts, out_first = tie(plane_gather(d_hidden.astype(bf16)), out_first)
    d_near_own = jnp.stack(d_parts)
    d_near_other = swap_cores(d_near_own)
    out_sends, d_near_other = tie(out_sum.sends_again(out_first), d_near_other)
    out_second = out_sum.move_again(out_sends)

    (
        head_grad,
        kv_grad,
        normed_part_own,
        normed_part_other,
        latent_part_own,
        latent_part_other,
    ) = attention_backward(
        core_index, d_near_own, d_near_other, kept_rows, flat_head, kv_w, *rope
    )
    kv_grad = kv_grad.reshape(groups, kv_rows, kv_parts, kv_piece).transpose(0, 2, 1, 3)
    head_grad = jnp.concatenate([head_grad, kv_grad.reshape(-1, kv_piece)], axis=1)
    head_blocks = head_grad.reshape(deep, -1, head_grad.shape[1])
    head_hops = HopSum(lambda t: at_index(head_blocks, 0, t))
    came, latent_both, normed_both, out_second = tie(
        head_hops.hop(1),
        sum_cores(latent_part_own, latent_part_other),
        sum_cores(normed_part_own, normed_part_other),
        out_second,
    )
    out_line = out_sum.line(out_first, out_second)
    came, grad_both, out_line = tie(head_hops.hop(2, came), sum_plane(latent_both), out_line)
    grad_rope = grad_both[:, rank_width : rank_width + DR] + grad_both[:, rank_width + DR :]
    latent_own = take_rows(latent[0], own_at, half)
    cosine_own = take_rows(cosine[0], own_at, half)
    sine_own = take_rows(sine_tab[0], own_at, half)
    _, scale_kv = rms_forward(latent_own[:, :rank_width], latent_g.astype(f32))
    grad_c, latent_gain_grad = rms_backward(
        latent_own[:, :rank_width], scale_kv, latent_g.astype(f32), grad_both[:, :rank_width]
    )
    grad_latent = jnp.concatenate(
        [grad_c, unrotate(grad_rope, cosine_own, sine_own)], axis=-1
    ).astype(bf16)
    out_hops = HopSum(lambda t: at_index(out_line, 0, (z - t) % deep))
    came, latent_parts, grad_normed, out_z = tie(
        head_hops.hop(3, came), plane_gather(grad_latent), sum_plane(normed_both), out_hops.hop(1)
    )
    latent_near_own = jnp.stack(latent_parts)
    latent_near = in_order(core, latent_near_own, swap_cores(latent_near_own), axis=1)
    head_sums = head_hops.total(came).astype(bf16).reshape(PLANE, block_rows, -1)
    out_z, latent_near, head_shared, grads_came = tie(
        out_hops.hop(2, out_z), latent_near, share_columns(head_sums, place), grads_came
    )
    out_z = out_hops.hop(3, out_z)
    latent_cut = latent_cols // 2
    latent_near = latent_near.reshape(near_rows, latent_cols)
    latent_blocks = contract_rows(
        normed_cols,
        take_rows(latent_near, core * latent_cut, latent_cut, axis=1),
    )
    latent_half = deep_scatter(latent_blocks.astype(bf16).reshape(deep, -1, latent_cut), z)
    w_latent_grad = in_order(core, latent_half, swap_cores(latent_half), axis=1)


    def by_heads(block):
        rotary = local_heads * DN
        return [
            part
            for h in range(local_heads)
            for part in (
                block[:, h * DN : (h + 1) * DN],
                block[:, rotary + h * DR : rotary + (h + 1) * DR],
            )
        ]

    at_kv = query_cols + out_cols
    w_query_grad = jnp.concatenate([v for p in head_shared for v in by_heads(p)], axis=1)
    w_query_grad = w_query_grad.astype(f32)
    w_kv_grad = jnp.concatenate(
        [
            p[q * kv_rows : (q + 1) * kv_rows, at_kv:]
            for p in head_shared
            for q in range(kv_parts)
        ],
        axis=1,
    ).astype(f32)
    w_out_grad = jnp.concatenate([p[:, query_cols:at_kv] for p in head_shared], axis=1)
    w_out_grad = w_out_grad.astype(f32).T
    sgu_out = grads_came[: 2 * shared_cols].astype(f32)
    sgu_out = sgu_out.reshape(2, shared_cols, groups, block_rows)
    sgu_out = sgu_out.transpose(0, 3, 2, 1).reshape(2, block_rows, -1)
    sdown_out = grads_came[2 * shared_cols : 3 * shared_cols].astype(f32).swapaxes(0, 1).reshape(-1, block_rows)
    grad_normed = grad_normed + contract_cols(grad_latent, latent_w)
    moe_own = out_hops.total(out_z)
    mixed_own = (hidden + moe_own).astype(bf16)
    mixed = in_order(core, mixed_own, swap_cores(mixed_own))

    _, scale_own = rms_forward(x_own, gain_one.astype(f32))
    grad_x_norm, gain_one_grad = rms_backward(x_own, scale_own, gain_one.astype(f32), grad_normed)
    input_own = d_hidden + grad_x_norm
    input_grad = in_order(core, input_own, swap_cores(input_own))

    gain_lanes = jnp.pad(
        latent_gain_grad.reshape(groups, kv_rows), ((0, 0), (0, block_rows - kv_rows))
    )
    vectors = jnp.concatenate(
        [
            router_grad,
            gain_one_grad[None],
            gain_two_grad[None],
            gain_lanes.reshape(1, -1),
        ],
        axis=0,
    ).reshape(-1, groups, block_rows)
    arrived = lax.all_to_all(vectors, "expert", split_axis=1, concat_axis=1, tiled=True)
    sums = jnp.sum(arrived, axis=1)
    sums = sums + swap_cores(sums)
    return (
        mixed,
        input_grad,
        sums[expert_count],
        w_query_grad,
        w_latent_grad,
        sums[expert_count + 2, :kv_rows],
        w_kv_grad,
        w_out_grad,
        sums[expert_count + 1],
        sums[:expert_count].T,
        sgu_out,
        sdown_out,
        egu_grad[None],
        edown_grad[None],
    )


def solution(mesh):
    groups = mesh.shape["expert"]
    plan = token_plan if groups <= 16 else weight_plan
    return jax.shard_map(
        plan,
        mesh=mesh,
        in_specs=(
            P("expert", None),
            P("expert"),
            P("expert", "tensor"),
            P("expert", None),
            P("expert"),
            P("expert", "tensor"),
            P("tensor", "expert"),
            P("expert"),
            P("expert", None),
            P(None, "expert", "tensor"),
            P("tensor", "expert"),
            P("expert", None, None, "tensor"),
            P("expert", "tensor", None),
            P("expert", None),
            P("expert", None),
            P("expert", None),
        ),
        out_specs=(
            P("expert", None),
            P("expert", None),
            P("expert"),
            P("expert", "tensor"),
            P("expert", None),
            P("expert"),
            P("expert", "tensor"),
            P("tensor", "expert"),
            P("expert"),
            P("expert", None),
            P(None, "expert", "tensor"),
            P("tensor", "expert"),
            P("expert", None, None, "tensor"),
            P("expert", "tensor", None),
        ),
        check_vma=False,
    )
```

```python
import functools

import jax
import jax.numpy as jnp
from jax import lax
from jax.experimental import pallas as pl
from jax.experimental.pallas import tpu as pltpu
from jax.sharding import PartitionSpec as P

DN = 128
DR = 64
DV = 128
LANES = 128


EPSILON = 1e-06
ROUTE_SCALE = 2.446
ROPE_BASE = 50000.0
NEGATIVE = -1e30


def cut_along(value, dim, length):
    before, after = (value.shape[:dim], value.shape[dim + 1 :])
    return jnp.moveaxis(value.reshape(*before, length, -1, *after), dim, 0)


def summed_on_arrival(value, axis, dim):
    length = lax.axis_size(axis)
    tiles = lax.all_to_all(cut_along(value, dim, length), axis, 0, 0, tiled=True)
    return jnp.sum(tiles.astype(jnp.float32), axis=0)


def sent_together(arrays, axis, dim, along):
    columns = [a.reshape(*a.shape[:along], -1) for a in arrays]
    both = jnp.concatenate(columns, axis=along)
    whole, at, outs = (summed_on_arrival(both, axis, dim), 0, [])
    for a, column in zip(arrays, columns):
        slab = whole[..., at : at + column.shape[along]]
        outs.append(slab.reshape(*slab.shape[:along], *a.shape[along:]))
        at += column.shape[along]
    return tuple(outs)


def contract_rows(left_arr, right_arr):
    return lax.dot_general(
        left_arr, right_arr, (((0,), (0,)), ((), ())), preferred_element_type=jnp.float32
    )


def contract_cols(left_arr, right_arr):
    return lax.dot_general(
        left_arr, right_arr, (((1,), (1,)), ((), ())), preferred_element_type=jnp.float32
    )


def rms_forward(rows_in, gain_vec):
    inverse = lax.rsqrt(jnp.mean(rows_in * rows_in, axis=-1, keepdims=True) + EPSILON)
    return (rows_in * inverse * gain_vec, inverse)


def rms_backward(rows_in, inverse, gain_vec, grad_out):
    gain_grad = jnp.sum(grad_out * rows_in * inverse, axis=0)
    weighted = grad_out * gain_vec
    inner_mean = jnp.mean(weighted * rows_in, axis=-1, keepdims=True)
    return (inverse * weighted - rows_in * inverse * inverse * inverse * inner_mean, gain_grad)


def doc_layout(doc_lengths, row_count):
    ends_at = jnp.cumsum(doc_lengths)
    starts_at = ends_at - doc_lengths
    position = jnp.arange(row_count, dtype=jnp.int32)
    doc_ids = jnp.sum((position[:, None] >= ends_at[None, :]).astype(jnp.int32), axis=1)
    hitting = doc_ids[:, None] == jnp.arange(doc_lengths.shape[0], dtype=jnp.int32)[None, :]
    start_of = jnp.sum(jnp.where(hitting, starts_at[None, :], 0), axis=1)
    relative = position - start_of
    visible = (doc_ids[:, None] == doc_ids[None, :]) & (position[:, None] >= position[None, :])
    return (relative, visible)


def rope_tables(relative, rot_width):
    counter = jnp.arange(rot_width // 2, dtype=jnp.float32)
    frequency = ROPE_BASE ** (-2.0 * counter / rot_width)
    angles = relative.astype(jnp.float32)[:, None] * frequency[None, :]
    return (jnp.cos(angles), jnp.sin(angles))


def rotate(tensor_in, cosine, sine_tab):
    half_width = tensor_in.shape[-1] // 2
    leading = tensor_in[..., :half_width]
    trailing = tensor_in[..., half_width:]
    return jnp.concatenate(
        [leading * cosine - trailing * sine_tab, trailing * cosine + leading * sine_tab], axis=-1
    )


def unrotate(grad_in, cosine, sine_tab):
    half_width = grad_in.shape[-1] // 2
    leading = grad_in[..., :half_width]
    trailing = grad_in[..., half_width:]
    return jnp.concatenate(
        [leading * cosine + trailing * sine_tab, trailing * cosine - leading * sine_tab], axis=-1
    )


def gated_linear_backward(gate_in, up_in, grad_act):
    sigmoid_g = jax.nn.sigmoid(gate_in)
    grad_gate = grad_act * up_in * sigmoid_g * (1.0 + gate_in * (1.0 - sigmoid_g))
    return (grad_gate, grad_act * gate_in * sigmoid_g)


def slot_tables(route_rows, expert_count, capacity):
    flat_routes = route_rows.reshape(-1)
    one_hot = (flat_routes[:, None] == jnp.arange(expert_count, dtype=jnp.int32)[None, :]).astype(
        jnp.int32
    )
    ranking = jnp.sum((jnp.cumsum(one_hot, axis=0) - one_hot) * one_hot, axis=1)
    slot_ids = flat_routes * capacity + ranking
    row_total = flat_routes.shape[0]
    source = (
        jnp.zeros((expert_count * capacity,), jnp.int32)
        .at[slot_ids]
        .set(jnp.arange(row_total, dtype=jnp.int32))
    )
    filled = jnp.zeros((expert_count * capacity,), jnp.int32).at[slot_ids].set(1)
    return (slot_ids, source, filled)


def to_owner(rows_in):
    arrived = lax.all_to_all(rows_in, "expert", split_axis=0, concat_axis=1, tiled=True)
    return arrived


def weight_plan(
    inputs,
    attn_gain,
    w_query,
    w_latent,
    latent_gain,
    w_kv,
    w_out,
    ffn_gain,
    w_router,
    shared_gate_up,
    shared_down,
    expert_gate_up,
    expert_down,
    lengths,
    routes,
    cotangent,
):
    tok_rows = inputs.shape[0]
    model_width = inputs.shape[1]
    expert_count = w_router.shape[1]
    route_count = routes.shape[1]
    capacity = tok_rows * route_count * 4 // (3 * expert_count)
    brain_float16 = jnp.bfloat16
    f32 = jnp.float32
    gathered = (
        lax.all_gather(attn_gain, "expert", axis=0, tiled=True),
        lax.all_gather(w_query, "expert", axis=0, tiled=True),
        lax.all_gather(w_latent, "expert", axis=0, tiled=True),
        lax.all_gather(latent_gain, "expert", axis=0, tiled=True),
        lax.all_gather(w_kv, "expert", axis=0, tiled=True),
        lax.all_gather(w_out, "expert", axis=1, tiled=True),
        lax.all_gather(ffn_gain, "expert", axis=0, tiled=True),
        lax.all_gather(w_router, "expert", axis=0, tiled=True),
        lax.all_gather(shared_gate_up, "expert", axis=1, tiled=True),
        lax.all_gather(shared_down, "expert", axis=1, tiled=True),
    )
    gain_one, query_w, latent_w, latent_g, kv_w, out_w, gain_two, router_w, sgate_up, sdown_w = (
        gathered
    )
    local_heads = query_w.shape[1] // (DN + DR)
    rank_width = latent_g.shape[0]
    x_float = inputs.astype(f32)
    relative, visible = doc_layout(lengths[0], tok_rows)
    cosine, sine_tab = rope_tables(relative, DR)
    q_scale = (DN + DR) ** (-0.5)
    normed, scale_one = rms_forward(x_float, gain_one.astype(f32))
    normed_b = normed.astype(brain_float16)
    queries = jnp.dot(normed_b, query_w, preferred_element_type=f32).reshape(
        tok_rows, local_heads, DN + DR
    )
    q_rot = rotate(queries[..., DN:], cosine[:, None, :], sine_tab[:, None, :])
    q_all = jnp.concatenate([queries[..., :DN], q_rot], axis=-1).astype(brain_float16)
    latent = jnp.dot(normed_b, latent_w, preferred_element_type=f32)
    compressed, scale_kv = rms_forward(latent[:, :rank_width], latent_g.astype(f32))
    compressed_b = compressed.astype(brain_float16)
    k_rope = rotate(latent[:, rank_width:], cosine, sine_tab).astype(brain_float16)
    kv_all = jnp.dot(compressed_b, kv_w, preferred_element_type=f32).reshape(
        tok_rows, local_heads, DN + DV
    )
    k_nope = kv_all[..., :DN].astype(brain_float16)
    values = kv_all[..., DN:].astype(brain_float16)
    key_all = jnp.concatenate(
        [k_nope, jnp.broadcast_to(k_rope[:, None, :], (tok_rows, local_heads, DR))], axis=-1
    )

    def score_block():
        raw_scores = (
            jnp.einsum("qhd,khd->hqk", q_all, key_all, preferred_element_type=f32) * q_scale
        )
        return jnp.where(visible[None], raw_scores, NEGATIVE)

    scores = score_block()
    top_score = jnp.max(scores, axis=-1, keepdims=True)
    log_total = top_score + jnp.log(jnp.sum(jnp.exp(scores - top_score), axis=-1, keepdims=True))
    probs_b = jnp.exp(scores - log_total).astype(brain_float16)
    attended = jnp.einsum("hqk,khd->qhd", probs_b, values, preferred_element_type=f32)
    attended_b = attended.reshape(tok_rows, local_heads * DV).astype(brain_float16)
    attn = lax.psum(jnp.dot(attended_b, out_w, preferred_element_type=f32), "tensor")
    hidden = x_float + attn
    hnormed, scale_two = rms_forward(hidden, gain_two.astype(f32))
    hnormed_b = hnormed.astype(brain_float16)
    logits = jnp.dot(hnormed_b, router_w, preferred_element_type=f32)
    sigmoid_vals = jax.nn.sigmoid(logits)
    route_hot = routes[:, :, None] == jnp.arange(expert_count, dtype=jnp.int32)[None, None, :]
    chosen = jnp.sum(jnp.where(route_hot, sigmoid_vals[:, None, :], 0.0), axis=2)
    chosen_sum = jnp.sum(chosen, axis=1, keepdims=True)
    gate_vals = ROUTE_SCALE * chosen / chosen_sum
    slot_ids, source, filled = slot_tables(routes, expert_count, capacity)
    is_filled = filled[:, None] == 1
    sent_rows = jnp.where(is_filled, hnormed_b[source // route_count], 0).reshape(
        expert_count, capacity, model_width
    )
    received = to_owner(sent_rows)
    gate_up_joined = jnp.einsum(
        "erd,egdf->egrf", received, expert_gate_up, preferred_element_type=f32
    )
    expert_act = (jax.nn.silu(gate_up_joined[:, 0]) * gate_up_joined[:, 1]).astype(brain_float16)
    expert_res = jnp.einsum(
        "erf,efd->erd", expert_act, expert_down, preferred_element_type=f32
    ).astype(brain_float16)
    returned_all = lax.all_to_all(expert_res, "expert", split_axis=1, concat_axis=0, tiled=True)
    returned = returned_all.reshape(expert_count * capacity, model_width)[slot_ids].reshape(
        tok_rows, route_count, model_width
    )
    shared_gu = jnp.einsum("td,gdf->gtf", hnormed_b, sgate_up, preferred_element_type=f32)
    shared_act = (jax.nn.silu(shared_gu[0]) * shared_gu[1]).astype(brain_float16)
    branch_sum = jnp.dot(shared_act, sdown_w, preferred_element_type=f32)
    for route_idx in range(route_count):
        branch_sum = branch_sum + gate_vals[:, route_idx : route_idx + 1] * returned[
            :, route_idx
        ].astype(f32)
    moe_out = lax.psum(branch_sum.astype(jnp.bfloat16), "tensor").astype(jnp.float32)
    mixed = (hidden + moe_out).astype(brain_float16)
    grad_y = cotangent.astype(f32)
    sdown_grad = contract_rows(shared_act, cotangent)
    grad_sact = contract_cols(cotangent, sdown_w)
    grad_sgate, grad_sup = gated_linear_backward(shared_gu[0], shared_gu[1], grad_sact)
    grad_sgu = jnp.stack([grad_sgate, grad_sup], axis=0).astype(brain_float16)
    sgu_grad = jnp.einsum("td,gtf->gdf", hnormed_b, grad_sgu, preferred_element_type=f32)
    grad_hn_part = jnp.einsum("gtf,gdf->td", grad_sgu, sgate_up, preferred_element_type=f32)
    gate_columns = []
    for route_idx in range(route_count):
        gate_columns.append(jnp.sum(grad_y * returned[:, route_idx].astype(f32), axis=1))
    gate_part = jnp.stack(gate_columns, axis=1)
    slot_grads = (
        (gate_vals[:, :, None] * grad_y[:, None, :])
        .reshape(tok_rows * route_count, model_width)
        .astype(brain_float16)
    )
    grad_sent = jnp.where(is_filled, slot_grads[source], 0).reshape(
        expert_count, capacity, model_width
    )
    grad_received = to_owner(grad_sent)
    edown_grad = jnp.einsum("erf,erd->efd", expert_act, grad_received, preferred_element_type=f32)
    expert_activation_gradient = jnp.einsum(
        "erd,efd->erf", grad_received, expert_down, preferred_element_type=f32
    )
    expert_gate_gradient, expert_up_gradient = gated_linear_backward(
        gate_up_joined[:, 0], gate_up_joined[:, 1], expert_activation_gradient
    )
    expert_gate_up_gradient = jnp.stack([expert_gate_gradient, expert_up_gradient], axis=1).astype(
        brain_float16
    )
    egu_grad = jnp.einsum(
        "erd,egrf->egdf", received, expert_gate_up_gradient, preferred_element_type=f32
    )
    grad_rows = jnp.einsum(
        "egrf,egdf->erd", expert_gate_up_gradient, expert_gate_up, preferred_element_type=f32
    ).astype(brain_float16)
    grad_back = lax.all_to_all(grad_rows, "expert", split_axis=1, concat_axis=0, tiled=True)
    grad_routes = grad_back.reshape(expert_count * capacity, model_width)[slot_ids].reshape(
        tok_rows, route_count, model_width
    )
    for route_idx in range(route_count):
        grad_hn_part = grad_hn_part + grad_routes[:, route_idx].astype(f32)
    gate_grads = lax.psum(gate_part, "tensor")
    grad_chosen = ROUTE_SCALE * (
        gate_grads / chosen_sum
        - jnp.sum(gate_grads * chosen, axis=1, keepdims=True) / (chosen_sum * chosen_sum)
    )
    grad_sig = jnp.sum(jnp.where(route_hot, grad_chosen[:, :, None], 0.0), axis=1)
    grad_logits = (grad_sig * sigmoid_vals * (1.0 - sigmoid_vals)).astype(brain_float16)
    router_grad = contract_rows(hnormed_b, grad_logits)
    grad_hn = lax.psum(grad_hn_part, "tensor") + contract_cols(grad_logits, router_w)
    grad_hidden_norm, gain_two_grad = rms_backward(hidden, scale_two, gain_two.astype(f32), grad_hn)
    grad_hidden = grad_y + grad_hidden_norm
    grad_hidden_b = grad_hidden.astype(brain_float16)
    out_grad = contract_rows(attended_b, grad_hidden_b)
    grad_att = (
        contract_cols(grad_hidden_b, out_w).reshape(tok_rows, local_heads, DV).astype(brain_float16)
    )
    probs = jnp.exp(score_block() - log_total)
    probs_again = probs.astype(brain_float16)
    grad_probs = jnp.einsum("qhd,khd->hqk", grad_att, values, preferred_element_type=f32)
    grad_vals = jnp.einsum("hqk,qhd->khd", probs_again, grad_att, preferred_element_type=f32)
    row_delta = jnp.sum(probs * grad_probs, axis=-1, keepdims=True)
    grad_scores = (probs * (grad_probs - row_delta)).astype(brain_float16)
    grad_q = jnp.einsum("hqk,khd->qhd", grad_scores, key_all, preferred_element_type=f32) * q_scale
    grad_keys = jnp.einsum("hqk,qhd->khd", grad_scores, q_all, preferred_element_type=f32) * q_scale
    grad_kv = (
        jnp.concatenate([grad_keys[..., :DN], grad_vals], axis=-1)
        .reshape(tok_rows, local_heads * (DN + DV))
        .astype(brain_float16)
    )
    kv_grad = contract_rows(compressed_b, grad_kv)
    grad_comp_part = contract_cols(grad_kv, kv_w)
    grad_krope_part = jnp.sum(grad_keys[..., DN:], axis=1)
    grad_comp, grad_krope = (
        lax.psum(grad_comp_part.astype(jnp.bfloat16), "tensor").astype(jnp.float32),
        lax.psum(grad_krope_part.astype(jnp.bfloat16), "tensor").astype(jnp.float32),
    )
    grad_c, latent_gain_grad = rms_backward(
        latent[:, :rank_width], scale_kv, latent_g.astype(f32), grad_comp
    )
    grad_latent = jnp.concatenate([grad_c, unrotate(grad_krope, cosine, sine_tab)], axis=-1).astype(
        brain_float16
    )
    grad_qrot = unrotate(grad_q[..., DN:], cosine[:, None, :], sine_tab[:, None, :])
    grad_queries = (
        jnp.concatenate([grad_q[..., :DN], grad_qrot], axis=-1)
        .reshape(tok_rows, local_heads * (DN + DR))
        .astype(brain_float16)
    )
    query_grad = contract_rows(normed_b, grad_queries)
    latent_grad = contract_rows(normed_b, grad_latent)
    grad_normed = lax.psum(
        contract_cols(grad_queries, query_w).astype(jnp.bfloat16), "tensor"
    ).astype(jnp.float32) + contract_cols(grad_latent, latent_w)
    grad_x_norm, gain_one_grad = rms_backward(x_float, scale_one, gain_one.astype(f32), grad_normed)
    input_grad = grad_hidden + grad_x_norm
    first_owned = (
        *sent_together(
            (
                gain_one_grad.astype(jnp.bfloat16),
                query_grad.astype(jnp.bfloat16),
                latent_grad.astype(jnp.bfloat16),
            ),
            "expert",
            0,
            1,
        ),
        *sent_together(
            (latent_gain_grad.astype(jnp.bfloat16), kv_grad.astype(jnp.bfloat16)), "expert", 0, 1
        ),
    )
    second_owned = (
        lax.psum_scatter(out_grad, "expert", scatter_dimension=1, tiled=True),
        lax.psum_scatter(gain_two_grad, "expert", scatter_dimension=0, tiled=True),
        lax.psum_scatter(router_grad, "expert", scatter_dimension=0, tiled=True),
        lax.psum_scatter(sgu_grad, "expert", scatter_dimension=1, tiled=True),
        lax.psum_scatter(sdown_grad, "expert", scatter_dimension=1, tiled=True),
    )
    return (
        mixed,
        input_grad,
        first_owned[0],
        first_owned[1],
        first_owned[2],
        first_owned[3],
        first_owned[4],
        second_owned[0],
        second_owned[1],
        second_owned[2],
        second_owned[3],
        second_owned[4],
        egu_grad,
        edown_grad,
    )


def swap_cores(value):
    return lax.ppermute(value, "tensor", [(0, 1), (1, 0)])


def take_rows(value, start, count, axis=0):
    return lax.dynamic_slice_in_dim(value, start, count, axis=axis)


def in_order(core, own, other, axis=0):
    return jnp.where(
        core == 0,
        jnp.concatenate([own, other], axis=axis),
        jnp.concatenate([other, own], axis=axis),
    )


def add_wide(*parts):
    total = parts[0].astype(jnp.float32)
    for part in parts[1:]:
        total = total + part.astype(jnp.float32)
    return total


PLANE = 4


def to_partner(value, flips):
    groups = lax.axis_size("expert")
    return lax.ppermute(value, "expert", [(g, g ^ flips) for g in range(groups)])


def to_deeper(value, step):
    groups = lax.axis_size("expert")
    pairs = [(g, (g + step * PLANE) % groups) for g in range(groups)]
    return lax.ppermute(value, "expert", pairs)


def plane_gather(value):
    return [value] + [to_partner(value, r) for r in range(1, PLANE)]


def plane_scatter(parts):
    return add_wide(parts[0], *[to_partner(parts[r], r) for r in range(1, PLANE)])


def by_place(parts, place):
    odd, high = place % 2 == 1, place // 2 == 1
    parts = [jnp.where(odd, parts[i ^ 1], parts[i]) for i in range(PLANE)]
    return [jnp.where(high, parts[i ^ 2], parts[i]) for i in range(PLANE)]


def tie(*values):
    return lax.optimization_barrier(values)


def deep_pieces(value):
    deep = lax.axis_size("expert") // PLANE
    return [to_deeper(value, s) for s in range(1, deep)]


def one_plane(value, step):
    groups = lax.axis_size("expert")
    pairs = [(g, g + step * PLANE) for g in range(groups) if 0 <= g + step * PLANE < groups]
    return lax.ppermute(value, "expert", pairs)


def deep_hops(value):
    deep = lax.axis_size("expert") // PLANE
    after, before, down, up = [], [], value, value
    for _ in range(1, deep):
        down, up = one_plane(down, 1), one_plane(up, -1)
        after.append(down)
        before.append(up)
    return after, before


def join_hops(hops):
    after, before = hops
    return [a + b for a, b in zip(after, before[::-1])]


def deep_join(value, pieces, z):
    deep = lax.axis_size("expert") // PLANE
    whole = jnp.zeros((deep, *value.shape), value.dtype)
    whole = lax.dynamic_update_index_in_dim(whole, value, z, 0)
    for step in range(1, deep):
        whole = lax.dynamic_update_index_in_dim(whole, pieces[step - 1], (z - step) % deep, 0)
    return whole


def deep_move(blocks, z):
    deep = blocks.shape[0]

    def block(index):
        return lax.dynamic_index_in_dim(blocks, index, 0, keepdims=False)

    return [block(z)] + [to_deeper(block((z + step) % deep), step) for step in range(1, deep)]


def deep_scatter(blocks, z):
    return add_wide(*deep_move(blocks, z))


def share_columns(rows, place):
    parts = [at_index(rows, 0, place)]
    for r in range(1, PLANE):
        parts.append(to_partner(at_index(rows, 0, place ^ r), r))
    return by_place(parts, place)


def all_groups(value):
    return lax.all_gather(value, "expert", axis=0, tiled=False)


def at_index(value, axis, index):
    return lax.dynamic_index_in_dim(value, index, axis, keepdims=False)


def doc_places(doc_lengths, row_count):
    ends_at = jnp.cumsum(doc_lengths)
    position = jnp.arange(row_count, dtype=jnp.int32)
    doc_ids = jnp.sum((position[:, None] >= ends_at[None, :]).astype(jnp.int32), axis=1)
    hitting = doc_ids[:, None] == jnp.arange(doc_lengths.shape[0], dtype=jnp.int32)[None, :]
    start_of = jnp.sum(jnp.where(hitting, (ends_at - doc_lengths)[None, :], 0), axis=1)
    return position - start_of, doc_ids


class HopSum:
    def __init__(self, pieces):
        self.groups = lax.axis_size("expert")
        self.deep = self.groups // PLANE
        self.z = lax.axis_index("expert") // PLANE
        self.pieces = pieces

    def hop(self, step, came=None):
        arrived = []
        for side, way in enumerate((1, -1)):
            target = jnp.clip(self.z + way * (self.deep - step), 0, self.deep - 1)
            gone = self.pieces(target)
            if came is not None:
                gone = add_wide(gone, came[side]).astype(gone.dtype)
            first = range(step) if way == 1 else range(self.deep - step, self.deep)
            pairs = [
                (p * PLANE + q, (p + way) * PLANE + q) for p in first for q in range(PLANE)
            ]
            arrived.append(lax.ppermute(gone, "expert", pairs))
        return arrived

    def total(self, came):
        return add_wide(self.pieces(self.z), *came)


def doc_places(doc_lengths, row_count):
    ends_at = jnp.cumsum(doc_lengths)
    position = jnp.arange(row_count, dtype=jnp.int32)
    doc_ids = jnp.sum((position[:, None] >= ends_at[None, :]).astype(jnp.int32), axis=1)
    hitting = doc_ids[:, None] == jnp.arange(doc_lengths.shape[0], dtype=jnp.int32)[None, :]
    start_of = jnp.sum(jnp.where(hitting, (ends_at - doc_lengths)[None, :], 0), axis=1)
    return position - start_of, doc_ids


def hop_sum(pieces):
    groups = lax.axis_size("expert")
    deep = groups // PLANE
    z = lax.axis_index("expert") // PLANE
    ends = []
    for way in (1, -1):
        came = None
        for step in range(1, deep):
            gone = pieces(jnp.clip(z + way * (deep - step), 0, deep - 1))
            if came is not None:
                gone = add_wide(gone, came).astype(gone.dtype)
            first = range(step) if way == 1 else range(deep - step, deep)
            pairs = [
                (p * PLANE + q, (p + way) * PLANE + q) for p in first for q in range(PLANE)
            ]
            came = lax.ppermute(gone, "expert", pairs)
        ends.append(came)
    return [pieces(z), *ends]


class RowGather:
    def __init__(self, value):
        self.cut = value.shape[0] // 2
        self.value = value

    def along(self):
        return [self.value] + deep_pieces(self.value)

    def lines(self, came):
        return [jnp.stack([v[: self.cut] for v in came]), jnp.stack([v[self.cut :] for v in came])]

    def over(self, lines):
        first, second = lines
        return to_partner(first, 1), to_partner(second, 2)

    def over_other(self, lines):
        first, second = lines
        return to_partner(first, 2), to_partner(second, 1)

    def over_again(self, came):
        beside, behind = came
        return to_partner(beside, 2), to_partner(behind, 1)


def blocks_of(lines, over, over_other, over_again, which):
    first = [lines[0], over[0], over_other[0], over_again and over_again[0]]
    second = [lines[1], over_other[1], over[1], over_again and over_again[1]]
    halves = [jnp.concatenate([half[r] for r in which], axis=0) for half in (first, second)]
    return jnp.concatenate(halves, axis=1)


class RowSum:
    def __init__(self, *terms):
        self.type = terms[0][0].dtype
        cut = terms[0][0].shape[1] // 2
        self.halves = (
            ([[b[:, :cut] for b in v] for v in terms], 2, 1),
            ([[b[:, cut:] for b in v] for v in terms], 1, 2),
        )

    def _add(self, parts):
        return add_wide(*parts).astype(self.type)

    def sends(self):
        return [
            jnp.stack([self._add([v[far] for v in held]), self._add([v[far | near] for v in held])])
            for held, far, near in self.halves
        ]

    def move(self, sends):
        return [to_partner(v, far) for v, (_, far, _) in zip(sends, self.halves)]

    def sends_again(self, came):
        return [
            self._add([v[near] for v in held] + [c[1]])
            for c, (held, _, near) in zip(came, self.halves)
        ]

    def move_again(self, sends):
        return [to_partner(v, near) for v, (_, _, near) in zip(sends, self.halves)]

    def line(self, came, came_again):
        sums = [
            self._add([v[0] for v in held] + [c[0], d])
            for c, d, (held, *_) in zip(came, came_again, self.halves)
        ]
        return jnp.concatenate(sums, axis=1)


def line_sends(line):
    return [line[step] for step in range(line.shape[0])]


def line_move(sends):
    return [sends[0]] + [to_deeper(v, -step) for step, v in enumerate(sends) if step > 0]


def dot_nn(left, right):
    return lax.dot_general(left, right, (((1,), (0,)), ((), ())), preferred_element_type=jnp.float32)


def dot_nt(left, right):
    return lax.dot_general(left, right, (((1,), (1,)), ((), ())), preferred_element_type=jnp.float32)


def dot_tn(left, right):
    return lax.dot_general(left, right, (((0,), (0,)), ((), ())), preferred_element_type=jnp.float32)


def two_lanes(column, lane):
    high = column.astype(jnp.bfloat16).astype(jnp.float32)
    spread = jnp.where(lane == 0, high, jnp.where(lane == 1, column - high, 0.0))
    return spread.astype(jnp.bfloat16)


def expert_kernel(
    shared_cols,
    expert_count,
    me_ref,
    hn_own,
    hn_other,
    dy_own,
    dy_other,
    meta_own,
    meta_other,
    gate_up_w,
    down_w,
    first_w,
    sdown_w,
    slots_out,
    slot_dy_out,
    act_out,
    d_gate_up_out,
    rows_own_out,
    rows_other_out,
    sact_own_out,
    sact_other_out,
    shared_grads_out,
    dgate_own_out,
    dgate_other_out,
):
    f32, bf16 = jnp.float32, jnp.bfloat16
    count, half, _ = hn_own.shape
    tokens = 2 * half
    me = me_ref[0]
    lane = lax.broadcasted_iota(jnp.int32, (count * tokens, LANES), 1)
    is_router = (lane >= shared_cols) & (lane < shared_cols + expert_count)
    first = first_w[...]

    def joined(own, other):
        return jnp.concatenate([v[i] for i in range(count) for v in (own, other)], axis=0)

    rows, rows_dy = joined(hn_own, hn_other), joined(dy_own, dy_other)
    meta = joined(meta_own, meta_other)
    products = dot_nt(rows, first)
    gate, up = products[:, :LANES], products[:, LANES:]
    sig = jax.nn.sigmoid(gate)
    total = jnp.sum(jnp.where(is_router, sig * meta, 0.0), axis=1, keepdims=True)
    mine = jnp.sum(jnp.where(lane == shared_cols + me, sig, 0.0), axis=1, keepdims=True)
    token_gate = two_lanes(ROUTE_SCALE * mine / total, lane)
    sact = (gate * sig * up).astype(bf16)
    d_sact = dot_nt(rows_dy, sdown_w[...])
    d_sgate = d_sact * up * sig * (1.0 + gate * (1.0 - sig))
    dsh = jnp.concatenate([d_sgate, d_sact * gate * sig], axis=1).astype(bf16)
    pick = (meta[:, :1] == lane.astype(f32)).astype(bf16)
    groups = [slice(i * tokens, (i + 1) * tokens) for i in range(count)]
    for i in range(count):
        start = i * tokens
        sact_own_out[i] = sact[start : start + half]
        sact_other_out[i] = sact[start + half : start + tokens]
    slots = [dot_tn(pick[g], rows[g]).astype(bf16) for g in groups]
    slot_dys = [dot_tn(pick[g], rows_dy[g]).astype(bf16) for g in groups]
    slot_gates = [
        jnp.sum(dot_tn(pick[g], token_gate[g]), axis=1, keepdims=True) for g in groups
    ]

    @pl.when(pl.program_id(0) == 0)
    def _():
        shared_grads_out[...] = jnp.zeros_like(shared_grads_out)

    first_grad, sdown_grad = dot_tn(dsh, rows), dot_tn(sact, rows_dy)
    shared_grads_out[:shared_cols] += first_grad[:shared_cols]
    shared_grads_out[shared_cols : 2 * shared_cols] += first_grad[LANES : LANES + shared_cols]
    shared_grads_out[2 * shared_cols :] += sdown_grad[:shared_cols]
    slot_rows = jnp.concatenate(slots, axis=0)
    slot_dy = jnp.concatenate(slot_dys, axis=0)
    slot_gate = jnp.concatenate(slot_gates, axis=0)
    slots_out[...] = slot_rows
    slot_dy_out[...] = slot_dy
    gate = dot_nt(slot_rows, gate_up_w[0])
    up = dot_nt(slot_rows, gate_up_w[1])
    d_act = dot_nt(slot_dy, down_w[...])
    sig = jax.nn.sigmoid(gate)
    silu = gate * sig
    act = silu * up
    slot_dgate = jnp.sum(act * d_act, axis=1, keepdims=True)
    act_out[...] = (slot_gate * act).astype(bf16)
    d_act = slot_gate * d_act
    d_gate = (d_act * up * sig * (1.0 + gate * (1.0 - sig))).astype(bf16)
    d_up = (d_act * silu).astype(bf16)
    d_gate_up_out[0] = d_gate
    d_gate_up_out[1] = d_up
    d_slots = (dot_nn(d_gate, gate_up_w[0]) + dot_nn(d_up, gate_up_w[1])).astype(bf16)
    slot_lane = lax.broadcasted_iota(jnp.int32, (LANES, LANES), 1)
    d_shared = dot_nn(dsh, first)
    for i, g in enumerate(groups):
        here = slice(i * LANES, (i + 1) * LANES)
        d_rows = (dot_nn(pick[g], d_slots[here]) + d_shared[g]).astype(bf16)
        rows_own_out[i], rows_other_out[i] = d_rows[:half], d_rows[half:]
        dgate = dot_nn(pick[g], two_lanes(slot_dgate[here], slot_lane))
        dgate_own_out[i], dgate_other_out[i] = dgate[:half], dgate[half:]


def block_specs(per_step):
    def lead(*tail):
        return pl.BlockSpec((per_step, *tail), lambda i: (i,) + (0,) * len(tail))

    def flat(cols):
        return pl.BlockSpec((per_step * LANES, cols), lambda i: (i, 0))

    def whole(a):
        return pl.BlockSpec(a.shape, lambda i: (0,) * a.ndim, pipeline_mode=pl.Buffered(1))

    return lead, flat, whole


def experts(
    me,
    hn_own,
    hn_other,
    dy_own,
    dy_other,
    meta_own,
    meta_other,
    gate_up_w,
    down_w,
    first_w,
    sdown_w,
    shared_cols,
    expert_count,
    per_step=2,
):
    groups, half, width = hn_own.shape
    hidden = down_w.shape[0]
    slots = groups * LANES
    f32, bf16 = jnp.float32, jnp.bfloat16
    lead, flat, whole = block_specs(per_step)
    sds = jax.ShapeDtypeStruct
    return pl.pallas_call(
        functools.partial(expert_kernel, shared_cols, expert_count),
        grid=(groups // per_step,),
        in_specs=[
            pl.BlockSpec(memory_space=pltpu.SMEM),
            *[lead(half, width)] * 4,
            *[lead(half, LANES)] * 2,
            *[whole(a) for a in (gate_up_w, down_w, first_w, sdown_w)],
        ],
        out_specs=[
            flat(width),
            flat(width),
            flat(hidden),
            pl.BlockSpec((2, per_step * LANES, hidden), lambda i: (0, i, 0)),
            *[lead(half, width)] * 2,
            *[lead(half, LANES)] * 2,
            pl.BlockSpec((3 * shared_cols, width), lambda i: (0, 0)),
            *[lead(half, LANES)] * 2,
        ],
        out_shape=[
            sds((slots, width), bf16),
            sds((slots, width), bf16),
            sds((slots, hidden), bf16),
            sds((2, slots, hidden), bf16),
            *[sds((groups, half, width), bf16)] * 2,
            *[sds((groups, half, LANES), bf16)] * 2,
            sds((3 * shared_cols, width), f32),
            *[sds((groups, half, LANES), f32)] * 2,
        ],
        compiler_params=pltpu.CompilerParams(vmem_limit_bytes=58 * 1024 * 1024),
        cost_estimate=pl.CostEstimate(
            flops=groups * width, bytes_accessed=groups * width, transcendentals=0
        ),
    )(
        me,
        hn_own,
        hn_other,
        dy_own,
        dy_other,
        meta_own,
        meta_other,
        gate_up_w,
        down_w,
        first_w,
        sdown_w,
    )


def swap_halves(value, lane):
    low = lane % DR < DR // 2
    return jnp.where(low, pltpu.roll(value, LANES - DR // 2, 1), pltpu.roll(value, DR // 2, 1))


def by_core(core, first, second):
    return jnp.where(core == 0, first, second), jnp.where(core == 0, second, first)


def head_scores(q, kv, k_rope, visible, lane, head, heads):
    q_nope = q[:, head * DN : (head + 1) * DN]
    q_rope = jnp.where(lane // DR == head, q[:, heads * DN :], jnp.zeros((), q.dtype))
    at = head * (DN + DV)
    k_nope, value = kv[:, at : at + DN], kv[:, at + DN : at + DN + DV]
    scores = (dot_nt(q_nope, k_nope) + dot_nt(q_rope, k_rope)) * (DN + DR) ** -0.5
    return jnp.where(visible, scores, NEGATIVE), q_nope, q_rope, k_nope, value


def seen(doc_col, doc_row):
    rows = doc_col.shape[0]
    later = lax.broadcasted_iota(jnp.int32, (rows, rows), 0) >= lax.broadcasted_iota(
        jnp.int32, (rows, rows), 1
    )
    return (doc_col == doc_row) & later


def attention_kernel(
    heads,
    rank,
    core_ref,
    x_own,
    x_other,
    gain,
    latent_gain,
    head_w,
    small_w,
    kv_w,
    cosine,
    sine,
    doc_col,
    doc_row,
    normed_out,
    compressed_out,
    q_out,
    kv_out,
    k_rope_out,
    sums_out,
    attended_out,
    latent_out,
    part_own_out,
    part_other_out,
):
    f32, bf16 = jnp.float32, jnp.bfloat16
    core = core_ref[0]
    x = jnp.concatenate(by_core(core, x_own[0], x_other[0]), axis=0).astype(f32)
    rows = x.shape[0]
    half = rows // 2
    lane = lax.broadcasted_iota(jnp.int32, (rows, LANES), 1)
    inverse = lax.rsqrt(jnp.mean(x * x, axis=1, keepdims=True) + EPSILON)
    normed = (x * inverse * gain[...]).astype(bf16)
    normed_out[0] = normed
    q_cols = heads * (DN + DR)
    queries = dot_nn(normed, head_w[:, :q_cols])
    q_rope = queries[:, heads * DN :]
    q_rope = q_rope * cosine[0] + swap_halves(q_rope, lane) * sine[0]
    q = jnp.concatenate([queries[:, : heads * DN], q_rope], axis=1).astype(bf16)
    q_out[0] = q
    latent = dot_nn(normed, small_w[:, : rank + LANES])
    latent_out[0] = latent
    squeezed = latent[:, :rank]
    inverse = lax.rsqrt(jnp.mean(squeezed * squeezed, axis=1, keepdims=True) + EPSILON)
    compressed = (squeezed * inverse * latent_gain[...]).astype(bf16)
    compressed_out[0] = compressed
    k_rope = latent[:, rank:]
    k_rope = (k_rope * cosine[0] + swap_halves(k_rope, lane) * sine[0]).astype(bf16)
    k_rope_out[0] = k_rope
    kv = dot_nn(compressed, kv_w[...]).astype(bf16)
    kv_out[0] = kv
    visible = seen(doc_col[0], doc_row[0])
    attended, sums = [], jnp.zeros((rows, LANES), f32)
    for head in range(heads):
        scores, *_, value = head_scores(q, kv, k_rope, visible, lane, head, heads)
        top = jnp.max(scores, axis=1, keepdims=True)
        log_total = top + jnp.log(jnp.sum(jnp.exp(scores - top), axis=1, keepdims=True))
        sums = jnp.where(lane == head, log_total, sums)
        probs = jnp.exp(scores - log_total).astype(bf16)
        attended.append(dot_nn(probs, value).astype(bf16))
    sums_out[0] = sums
    attended = jnp.concatenate(attended, axis=1)
    attended_out[0] = attended
    part = dot_nt(attended, head_w[:, q_cols : q_cols + heads * DV]).astype(bf16)
    part_own_out[0], part_other_out[0] = by_core(core, part[:half], part[half:])


def attention_backward_kernel(
    heads,
    core_ref,
    d_own,
    d_other,
    normed_ref,
    compressed_ref,
    q_ref,
    kv_ref,
    k_rope_ref,
    sums_ref,
    attended_ref,
    head_w,
    kv_w,
    cosine,
    sine,
    doc_col,
    doc_row,
    head_grad_out,
    kv_grad_out,
    normed_own_out,
    normed_other_out,
    latent_own_out,
    latent_other_out,
    head_acc,
    kv_acc,
):
    f32, bf16 = jnp.float32, jnp.bfloat16
    core, step = core_ref[0], pl.program_id(0)
    scale = (DN + DR) ** -0.5
    d_rows = jnp.concatenate(by_core(core, d_own[0], d_other[0]), axis=0)
    rows = d_rows.shape[0]
    half = rows // 2
    lane = lax.broadcasted_iota(jnp.int32, (rows, LANES), 1)
    q_cols = heads * (DN + DR)
    q, kv, k_rope = q_ref[0], kv_ref[0], k_rope_ref[0]
    d_attended = dot_nn(d_rows, head_w[:, q_cols : q_cols + heads * DV]).astype(bf16)
    visible = seen(doc_col[0], doc_row[0])
    d_q, d_kv = [], []
    d_q_rope, d_k_rope = jnp.zeros((rows, LANES), f32), jnp.zeros((rows, LANES), f32)
    for head in range(heads):
        scores, q_nope, q_rope, k_nope, value = head_scores(
            q, kv, k_rope, visible, lane, head, heads
        )
        probs = jnp.exp(scores - sums_ref[0][:, head : head + 1])
        d_head = d_attended[:, head * DV : (head + 1) * DV]
        d_probs = dot_nt(d_head, value)
        d_value = dot_tn(probs.astype(bf16), d_head)
        delta = jnp.sum(probs * d_probs, axis=1, keepdims=True)
        d_scores = (probs * (d_probs - delta)).astype(bf16)
        d_q.append(dot_nn(d_scores, k_nope) * scale)
        d_q_rope = jnp.where(lane // DR == head, dot_nn(d_scores, k_rope) * scale, d_q_rope)
        d_kv += [dot_tn(d_scores, q_nope) * scale, d_value]
        d_k_rope += dot_tn(d_scores, q_rope) * scale
    d_q_rope = d_q_rope * cosine[0] - swap_halves(d_q_rope, lane) * sine[0]
    d_q = jnp.concatenate(d_q + [d_q_rope], axis=1).astype(bf16)
    d_kv = jnp.concatenate(d_kv, axis=1).astype(bf16)

    @pl.when(step == 0)
    def _():
        head_acc[...] = jnp.zeros_like(head_acc)
        kv_acc[...] = jnp.zeros_like(kv_acc)

    head_acc[:, :q_cols] += dot_tn(normed_ref[0], d_q)
    head_acc[:, q_cols:] += dot_tn(d_rows, attended_ref[0])
    kv_acc[...] += dot_tn(compressed_ref[0], d_kv)

    @pl.when(step == pl.num_programs(0) - 1)
    def _():
        head_grad_out[...] = head_acc[...].astype(bf16)
        kv_grad_out[...] = kv_acc[...].astype(bf16)

    part = dot_nt(d_q, head_w[:, :q_cols]).astype(bf16)
    normed_own_out[0], normed_other_out[0] = by_core(core, part[:half], part[half:])
    latent = jnp.concatenate([dot_nt(d_kv, kv_w[...]), d_k_rope], axis=1).astype(bf16)
    latent_own_out[0], latent_other_out[0] = by_core(core, latent[:half], latent[half:])


def one_each(*tail):
    return pl.BlockSpec((1, *tail), lambda i: (i,) + (0,) * len(tail))


def kept(value):
    return pl.BlockSpec(value.shape, lambda i: (0,) * value.ndim, pipeline_mode=pl.Buffered(1))


def attention(core, x_own, x_other, gain, latent_gain, head_w, small_w, kv_w, cosine, sine, doc):
    near, half, width = x_own.shape
    rows = 2 * half
    rank, kv_cols = kv_w.shape
    heads = kv_cols // (DN + DV)
    f32, bf16 = jnp.float32, jnp.bfloat16
    shapes = [
        ((rows, width), bf16),
        ((rows, rank), bf16),
        ((rows, heads * (DN + DR)), bf16),
        ((rows, kv_cols), bf16),
        ((rows, LANES), bf16),
        ((rows, LANES), f32),
        ((rows, heads * DV), bf16),
        ((rows, rank + LANES), f32),
        ((half, width), bf16),
        ((half, width), bf16),
    ]
    return pl.pallas_call(
        functools.partial(attention_kernel, heads, rank),
        grid=(near,),
        in_specs=[
            pl.BlockSpec(memory_space=pltpu.SMEM),
            *[one_each(half, width)] * 2,
            *[kept(a) for a in (gain, latent_gain, head_w, small_w, kv_w)],
            *[one_each(rows, LANES)] * 2,
            one_each(rows, 1),
            one_each(1, rows),
        ],
        out_specs=[one_each(*shape) for shape, _ in shapes],
        out_shape=[jax.ShapeDtypeStruct((near, *shape), kind) for shape, kind in shapes],
        compiler_params=pltpu.CompilerParams(vmem_limit_bytes=58 * 1024 * 1024),
        cost_estimate=pl.CostEstimate(
            flops=2 * near * rows * width * (rank + 3 * heads * DN),
            bytes_accessed=4 * near * rows * width,
            transcendentals=0,
        ),
    )(
        core,
        x_own,
        x_other,
        gain,
        latent_gain,
        head_w,
        small_w,
        kv_w,
        cosine,
        sine,
        doc[:, :, None],
        doc[:, None, :],
    )


def attention_backward(core, d_own, d_other, kept_rows, head_w, kv_w, cosine, sine, doc):
    near, half, width = d_own.shape
    rows = 2 * half
    rank, kv_cols = kv_w.shape
    heads = kv_cols // (DN + DV)
    head_cols = heads * (DN + DR + DV)
    f32, bf16 = jnp.float32, jnp.bfloat16
    sds = jax.ShapeDtypeStruct
    return pl.pallas_call(
        functools.partial(attention_backward_kernel, heads),
        grid=(near,),
        in_specs=[
            pl.BlockSpec(memory_space=pltpu.SMEM),
            *[one_each(half, width)] * 2,
            *[one_each(*v.shape[1:]) for v in kept_rows],
            *[kept(a) for a in (head_w, kv_w)],
            *[one_each(rows, LANES)] * 2,
            one_each(rows, 1),
            one_each(1, rows),
        ],
        out_specs=[
            pl.BlockSpec((width, head_cols), lambda i: (0, 0)),
            pl.BlockSpec((rank, kv_cols), lambda i: (0, 0)),
            *[one_each(half, width)] * 2,
            *[one_each(half, rank + LANES)] * 2,
        ],
        out_shape=[
            sds((width, head_cols), bf16),
            sds((rank, kv_cols), bf16),
            *[sds((near, half, width), bf16)] * 2,
            *[sds((near, half, rank + LANES), bf16)] * 2,
        ],
        scratch_shapes=[
            pltpu.VMEM((width, head_cols), f32),
            pltpu.VMEM((rank, kv_cols), f32),
        ],
        compiler_params=pltpu.CompilerParams(vmem_limit_bytes=58 * 1024 * 1024),
        cost_estimate=pl.CostEstimate(
            flops=near * rows * width * heads * DN,
            bytes_accessed=2 * near * rows * width,
            transcendentals=0,
        ),
    )(
        core,
        d_own,
        d_other,
        *kept_rows,
        head_w,
        kv_w,
        cosine,
        sine,
        doc[:, :, None],
        doc[:, None, :],
    )


def product_kernel(*refs):
    *operands, out_ref = refs
    count = len(operands) // 2
    total = 0.0
    for left_ref, right_ref in zip(operands[:count], operands[count:]):
        total += dot_tn(left_ref[0], right_ref[...])
    out_ref[0] = total


def column_products(lefts, rights, tile=512):
    count, _, height = lefts[0].shape
    width = rights[0].shape[1]
    return pl.pallas_call(
        product_kernel,
        grid=(width // tile, count),
        in_specs=[
            *[pl.BlockSpec((1, v.shape[1], height), lambda j, i: (i, 0, 0)) for v in lefts],
            *[pl.BlockSpec((v.shape[0], tile), lambda j, i: (0, j)) for v in rights],
        ],
        out_specs=pl.BlockSpec((1, height, tile), lambda j, i: (i, 0, j)),
        out_shape=jax.ShapeDtypeStruct((count, height, width), jnp.float32),
        compiler_params=pltpu.CompilerParams(vmem_limit_bytes=58 * 1024 * 1024),
        cost_estimate=pl.CostEstimate(flops=width, bytes_accessed=width, transcendentals=0),
    )(*lefts, *rights)


def output_kernel(act, sact_own, sact_other, meta_own, meta_other, down_w, sdown_w, own_out, other_out):
    f32, bf16 = jnp.float32, jnp.bfloat16
    count, half, _ = meta_own.shape
    lane = lax.broadcasted_iota(jnp.int32, (2 * half, LANES), 1).astype(f32)
    out = dot_nn(act[...], down_w[...]).astype(bf16)
    for i in range(count):
        meta = jnp.concatenate([meta_own[i], meta_other[i]], axis=0)
        pick = (meta[:, :1] == lane).astype(bf16)
        sact = jnp.concatenate([sact_own[i], sact_other[i]], axis=0)
        here = slice(i * LANES, (i + 1) * LANES)
        rows = (dot_nn(pick, out[here]) + dot_nn(sact, sdown_w[...])).astype(bf16)
        own_out[i], other_out[i] = rows[:half], rows[half:]


def outputs(act, sact_own, sact_other, meta_own, meta_other, down_w, sdown_w, per_step=4):
    groups, half, _ = meta_own.shape
    hidden, width = down_w.shape
    lead, flat, whole = block_specs(per_step)
    return pl.pallas_call(
        output_kernel,
        grid=(groups // per_step,),
        in_specs=[
            flat(hidden),
            *[lead(half, LANES)] * 4,
            *[whole(a) for a in (down_w, sdown_w)],
        ],
        out_specs=[lead(half, width)] * 2,
        out_shape=[jax.ShapeDtypeStruct((groups, half, width), jnp.bfloat16)] * 2,
        compiler_params=pltpu.CompilerParams(vmem_limit_bytes=58 * 1024 * 1024),
        cost_estimate=pl.CostEstimate(
            flops=groups * half * LANES * width,
            bytes_accessed=groups * half * width,
            transcendentals=0,
        ),
    )(act, sact_own, sact_other, meta_own, meta_other, down_w, sdown_w)


def token_plan(
    inputs,
    attn_gain,
    w_query,
    w_latent,
    latent_gain,
    w_kv,
    w_out,
    ffn_gain,
    w_router,
    shared_gate_up,
    shared_down,
    expert_gate_up,
    expert_down,
    lengths,
    routes,
    cotangent,
):
    f32, bf16 = jnp.float32, jnp.bfloat16
    core, me = lax.axis_index("tensor"), lax.axis_index("expert")
    groups = lax.axis_size("expert")
    deep, place, z = groups // PLANE, me % PLANE, me // PLANE
    tok_rows, width = inputs.shape
    half = tok_rows // 2
    own_at, other_at = core * half, (1 - core) * half
    expert_count = w_router.shape[1]
    route_count = routes.shape[1]
    capacity = tok_rows * route_count * 4 // (3 * expert_count)
    shared_cols = shared_gate_up.shape[2] // groups
    latent_cols, rank_width = w_latent.shape[1], latent_gain.shape[0] * groups
    block_rows = w_query.shape[0]
    kv_rows = w_kv.shape[0]

    query_cols = w_query.shape[1] // PLANE
    out_cols = w_out.shape[0] // PLANE
    small = jnp.concatenate(
        [
            w_latent,
            w_latent[:, rank_width:],
            w_router,
            attn_gain[:, None],
            ffn_gain[:, None],
            jnp.pad(latent_gain, (0, block_rows - kv_rows))[:, None],
        ],
        axis=1,
    )
    small_cols = small.shape[1]
    route_half = take_rows(routes, own_at, half).astype(bf16).reshape(block_rows // 2, -1)
    length_col = jnp.pad(lengths[0].astype(bf16), (0, block_rows // 2 - lengths.shape[1]))[:, None]
    route_cols = route_half.shape[1] + 1
    small_half = jnp.concatenate(
        [
            take_rows(small, core * (block_rows // 2), block_rows // 2),
            route_half,
            length_col,
            jnp.zeros((block_rows // 2, -(small_cols + route_cols) % (2 * LANES)), bf16),
        ],
        axis=1,
    )
    packed_cols = small_half.shape[1] // 2
    small_packed = jnp.concatenate([small_half[:, :packed_cols], small_half[:, packed_cols:]])
    kv_cols = w_kv.shape[1] // PLANE
    kv_parts = block_rows // kv_rows
    kv_piece = kv_cols // kv_parts
    w_out_t = w_out.T

    local_heads = query_cols // (DN + DR)

    def by_parts(block):
        heads = [block[:, h * (DN + DR) : (h + 1) * (DN + DR)] for h in range(local_heads)]
        return [h[:, :DN] for h in heads] + [h[:, DN:] for h in heads]

    def quarter(index):
        kv_here = take_rows(w_kv, index * kv_cols, kv_cols, axis=1)
        kv_here = [kv_here[:, p * kv_piece : (p + 1) * kv_piece] for p in range(kv_parts)]
        return jnp.concatenate(
            [
                *by_parts(take_rows(w_query, index * query_cols, query_cols, axis=1)),
                take_rows(w_out_t, index * out_cols, out_cols, axis=1),
                jnp.concatenate(kv_here, axis=0),
            ],
            axis=1,
        )

    near_w = [quarter(place)] + [to_partner(quarter(place ^ r), r) for r in range(1, PLANE)]
    small_line = deep_join(small_packed, deep_pieces(small_packed), z)
    near_w, small_line = tie(near_w, small_line)
    plane_w = jnp.stack(by_place(near_w, place))
    small_sent, x_sent, plane_w = tie(
        small_line.swapaxes(0, 1), take_rows(inputs, own_at, half), plane_w
    )
    small_sent = jnp.stack([small_sent, to_partner(small_sent, 1)])
    small_sent = jnp.concatenate([small_sent, to_partner(small_sent, 2)], axis=0)
    x_sent = jnp.stack([x_sent, to_partner(x_sent, 2)])
    x_came = to_partner(x_sent, 1)
    x_near_own = jnp.stack([x_sent[0], x_came[0], x_sent[1], x_came[1]])
    x_near_other = swap_cores(x_near_own)
    deep_w = deep_hops(plane_w)
    small_parts = [small_sent[r].swapaxes(0, 1) for r in range(PLANE)]
    small_own = jnp.stack(by_place(small_parts, place), axis=1)
    small_own = small_own.reshape(groups, block_rows, packed_cols)
    small_own = jnp.concatenate(
        [small_own[:, : block_rows // 2], small_own[:, block_rows // 2 :]], axis=2
    )
    small_other = swap_cores(small_own)
    small_all = in_order(core, small_own, small_other, axis=1)
    small_all, x_near_other, deep_w = tie(small_all, x_near_other, deep_w)
    head_w = deep_join(plane_w, join_hops(deep_w), z)
    length_at = small_cols + route_cols - 1
    lengths_near = take_rows(small_own, z * PLANE, PLANE)[:, : lengths.shape[1], length_at]
    lengths_near = lengths_near.astype(jnp.int32)
    lengths_near = jnp.stack(by_place([lengths_near[r] for r in range(PLANE)], place))
    shared_rows = jnp.concatenate(
        [shared_gate_up[0].T, shared_gate_up[1].T, shared_down], axis=0
    ).reshape(3, groups, shared_cols, block_rows)
    shared_rows = shared_rows.swapaxes(0, 1).reshape(groups, 3 * shared_cols, block_rows)
    dy_sent, head_w = tie(take_rows(cotangent, own_at, half), head_w)
    dy_own_rows = take_rows(cotangent, own_at, half)
    dy_gather = RowGather(dy_sent)
    dy_came = dy_gather.along()
    head_w = head_w.reshape(groups, block_rows, -1)
    flat_head = head_w.reshape(groups * block_rows, -1)
    at = query_cols + out_cols
    kv_w = head_w[:, :, at : at + kv_piece].reshape(groups, kv_parts, kv_rows, kv_piece)
    kv_w = kv_w.transpose(0, 2, 1, 3).reshape(groups * kv_rows, kv_cols)

    block_index = jnp.arange(groups)
    block_chip = (z - block_index % deep) % deep * PLANE + (place ^ (block_index // deep))
    in_blocks = (block_chip[:, None] == block_index[None, :]).astype(bf16)

    def routes_of(came):
        came = came[:, :, small_cols : small_cols + route_half.shape[1]].reshape(groups, -1)
        came = jnp.dot(in_blocks, came, preferred_element_type=f32)
        return came.astype(jnp.int32).reshape(groups, half, route_count)

    routes_own, routes_other = routes_of(small_own), routes_of(small_other)
    flat_small = small_all.reshape(groups * block_rows, -1)
    latent_w = flat_small[:, :latent_cols]
    at = rank_width + LANES
    router_w = flat_small[:, at : at + expert_count]
    at += expert_count
    gain_one, gain_two = flat_small[:, at], flat_small[:, at + 1]
    latent_g = small_all[:, :kv_rows, at + 2].reshape(-1)

    near_rows = PLANE * tok_rows
    relative, doc = jax.vmap(lambda one: doc_places(one, tok_rows))(lengths_near)
    cosine, sine_tab = rope_tables(relative.reshape(-1), DR)
    cosine, sine_tab = [v.reshape(PLANE, tok_rows, -1) for v in (cosine, sine_tab)]
    rope = (
        jnp.concatenate([cosine] * 4, axis=-1),
        jnp.concatenate([-sine_tab, sine_tab] * 2, axis=-1),
        doc.astype(f32),
    )
    core_index = core.reshape(1).astype(jnp.int32)
    *kept_rows, latent, part_own, part_other = attention(
        core_index,
        x_near_own,
        x_near_other,
        gain_one.astype(f32)[None],
        latent_g.astype(f32)[None],
        flat_head,
        flat_small,
        kv_w,
        *rope,
    )
    normed_b = kept_rows[0].reshape(near_rows, width)

    def sum_cores(own, other):
        return add_wide(own, swap_cores(other)).astype(bf16)

    def sum_plane(both):
        return plane_scatter([both[r] for r in range(PLANE)])

    part_own, part_other, dy_came = tie(part_own, part_other, dy_came)
    attn_own = sum_plane(sum_cores(part_own, part_other))
    x_own = take_rows(inputs, own_at, half).astype(f32)
    hidden = x_own + attn_own
    hnormed, scale_two = rms_forward(hidden, gain_two.astype(f32))
    hnormed_b = hnormed.astype(bf16)
    normed_cols = jnp.concatenate(
        [
            take_rows(normed_b, (k * PLANE + place) * block_rows, block_rows, axis=1)
            for k in range(deep)
        ],
        axis=1,
    )
    hnormed_b, normed_cols, shared_rows = tie(hnormed_b, normed_cols, shared_rows)
    dy_lines = dy_gather.lines(dy_came)
    def membership(named):
        one_hot = named[..., None] == jnp.arange(expert_count, dtype=jnp.int32)
        return jnp.any(named == me, axis=-1), jnp.any(one_hot, axis=2)

    member_own, hot_own = membership(routes_own)
    member_other, hot_other = membership(routes_other)
    lower = (
        jnp.arange(half, dtype=jnp.int32)[:, None] <= jnp.arange(half, dtype=jnp.int32)[None, :]
    ).astype(bf16)

    def running(mask):
        counts = jnp.dot(mask.astype(bf16), lower, preferred_element_type=f32)
        return counts.astype(jnp.int32)

    count_own, count_other = running(member_own), running(member_other)
    place_own = jnp.where(member_own, count_own - 1, -1)
    place_other = jnp.where(member_other, count_own[:, -1:] + count_other - 1, -1)

    def metadata(slot, hot):
        return jnp.concatenate(
            [
                slot[..., None].astype(f32),
                jnp.zeros((groups, half, shared_cols - 1), f32),
                hot.astype(f32),
                jnp.zeros((groups, half, LANES - shared_cols - expert_count), f32),
            ],
            axis=-1,
        )

    meta_own, meta_other = metadata(place_own, hot_own), metadata(place_other, hot_other)
    hn_gather = RowGather(hnormed_b)
    hn_came, dy_over, dy_other_way, meta_own, meta_other = tie(
        hn_gather.along(),
        dy_gather.over(dy_lines),
        dy_gather.over_other(dy_lines),
        meta_own,
        meta_other,
    )
    hn_lines, dy_over, shared_rows = tie(hn_gather.lines(hn_came), dy_over, shared_rows)
    shared_w = lax.all_to_all(shared_rows, "expert", split_axis=0, concat_axis=0, tiled=True)
    dy_line = jnp.concatenate(dy_lines, axis=1)
    hn_line = jnp.concatenate(hn_lines, axis=1)
    hn_over, dy_again, hn_line_other, dy_line_other, shared_w = tie(
        hn_gather.over(hn_lines),
        dy_gather.over_again(dy_over),
        swap_cores(hn_line),
        swap_cores(dy_line),
        shared_w,
    )
    shared_w = shared_w.swapaxes(0, 1).reshape(3 * shared_cols, groups * block_rows)
    first_w = jnp.concatenate(
        [
            shared_w[:shared_cols],
            router_w.T,
            jnp.zeros((LANES - shared_cols - expert_count, width), bf16),
            shared_w[shared_cols : 2 * shared_cols],
            jnp.zeros((LANES - shared_cols, width), bf16),
        ],
        axis=0,
    )
    sdown_rows = jnp.pad(shared_w[2 * shared_cols :], ((0, LANES - shared_cols), (0, 0)))
    gate_up_w, down_w = jnp.swapaxes(expert_gate_up[0], 1, 2), expert_down[0]

    def run_experts(which, hn_part, hn_part_other):
        at, to = which[0] * deep, (which[-1] + 1) * deep
        return experts(
            me.reshape(1).astype(jnp.int32),
            hn_part,
            hn_part_other,
            *dy_parts[which],
            meta_own[at:to],
            meta_other[at:to],
            gate_up_w,
            down_w,
            first_w,
            sdown_rows,
            shared_cols,
            expert_count,
        )

    parts = ((0,), (1, 2), (3,))
    dy_parts = {parts[0]: (dy_line, dy_line_other)}
    dy_mine = [blocks_of(dy_lines, dy_over, dy_other_way, dy_again, p) for p in parts[1:]]
    hn_other_way, done_line, dy_mine = tie(
        hn_gather.over_other(hn_lines),
        run_experts(parts[0], hn_line, hn_line_other),
        [(v, swap_cores(v)) for v in dy_mine],
    )
    dy_parts.update(zip(parts[1:], dy_mine))
    d_line_came = swap_cores(done_line[5])
    hn_near = blocks_of(hn_lines, hn_over, hn_other_way, None, parts[1])
    hn_again, done_near = tie(
        hn_gather.over_again(hn_over), run_experts(parts[1], hn_near, swap_cores(hn_near))
    )
    d_near_came = swap_cores(done_near[5])
    hn_far = blocks_of(hn_lines, hn_over, hn_other_way, hn_again, parts[2])
    done_far = run_experts(parts[2], hn_far, swap_cores(hn_far))
    done = (done_line, done_near, done_far)
    slot_rows, slot_dy, slot_act, d_gate_up = [[v[i] for v in done] for i in range(4)]
    shared_grads = add_wide(*[v[8] for v in done])

    def by_flips(line, near, far):
        return [line, near[:deep], near[deep:], far]

    d_rows_own = by_flips(*[v[4] for v in done])
    d_rows_came = by_flips(d_line_came, d_near_came, swap_cores(done_far[5]))

    def two_parts(value):
        return value[..., 0] + value[..., 1]

    dgate_own, dgate_other = [
        jnp.concatenate([two_parts(v[i]) for v in done], axis=0) for i in (9, 10)
    ]
    dgate_sent = dgate_own + swap_cores(dgate_other)
    dgate_high = dgate_sent.astype(bf16)
    dgate_low = (dgate_sent - dgate_high.astype(f32)).astype(bf16)
    d_rows_came, dgate_high, dgate_low = tie(d_rows_came, dgate_high, dgate_low)
    d_sum = RowSum(d_rows_own, d_rows_came)
    sends, shared_grads, slot_act = tie(d_sum.sends(), shared_grads, slot_act)
    came = d_sum.move(sends)
    gate_rows = jnp.stack([contract_rows(in_blocks, v).reshape(-1) for v in (dgate_high, dgate_low)])
    grads_sent = jnp.concatenate([shared_grads, gate_rows], axis=0).astype(bf16)
    grads_sent = grads_sent.reshape(-1, groups, block_rows)
    grads_came = lax.all_to_all(grads_sent, "expert", split_axis=1, concat_axis=1, tiled=True)
    out_done = [
        outputs(
            act,
            v[6],
            v[7],
            meta_own[p[0] * deep : (p[-1] + 1) * deep],
            meta_other[p[0] * deep : (p[-1] + 1) * deep],
            down_w,
            sdown_rows,
        )
        for act, v, p in zip(slot_act, done, parts)
    ]
    edown_grad = column_products([v[None] for v in slot_act], slot_dy)[0]
    came, out_done, edown_grad, grads_came = tie(came, out_done, edown_grad, grads_came)
    dgate = add_wide(grads_came[3 * shared_cols], grads_came[3 * shared_cols + 1]).T
    sends, slot_rows, out_done = tie(d_sum.sends_again(came), slot_rows, out_done)
    came_again = d_sum.move_again(sends)
    egu_grad = column_products(d_gate_up, slot_rows).swapaxes(1, 2)
    out_own = by_flips(*[v[0] for v in out_done])
    out_came = by_flips(*[swap_cores(v[1]) for v in out_done])
    out_sum = RowSum(out_own, out_came)
    out_sends = out_sum.sends()
    came_again, egu_grad, out_sends = tie(came_again, egu_grad, out_sends)
    z_sends, out_sends, dgate = tie(
        line_sends(d_sum.line(came, came_again)), out_sends, dgate
    )
    z_came = line_move(z_sends)
    out_first = out_sum.move(out_sends)
    hot_mine = take_rows(
        jnp.any(routes[..., None] == jnp.arange(expert_count, dtype=jnp.int32), axis=1), own_at, half
    )
    sig = jax.nn.sigmoid(jnp.dot(hnormed_b, router_w, preferred_element_type=f32))
    chosen = jnp.where(hot_mine, sig, 0.0)
    chosen_sum = jnp.sum(chosen, axis=1, keepdims=True)
    dgate = jnp.where(hot_mine, dgate, 0.0)
    inner = jnp.sum(dgate * chosen, axis=1, keepdims=True)
    d_chosen = ROUTE_SCALE * (dgate / chosen_sum - inner / (chosen_sum * chosen_sum))
    d_logits = (jnp.where(hot_mine, d_chosen, 0.0) * sig * (1.0 - sig)).astype(bf16)
    router_grad = contract_rows(d_logits, hnormed_b)
    z_came, d_logits, router_grad = tie(z_came, d_logits, router_grad)
    d_hn = add_wide(*z_came)
    d_hn = d_hn + contract_cols(d_logits, router_w)
    d_hidden_norm, gain_two_grad = rms_backward(hidden, scale_two, gain_two.astype(f32), d_hn)
    d_hidden = dy_own_rows.astype(f32) + d_hidden_norm
    d_parts, out_first = tie(plane_gather(d_hidden.astype(bf16)), out_first)
    d_near_own = jnp.stack(d_parts)
    d_near_other = swap_cores(d_near_own)
    out_sends, d_near_other = tie(out_sum.sends_again(out_first), d_near_other)
    out_second = out_sum.move_again(out_sends)

    (
        head_grad,
        kv_grad,
        normed_part_own,
        normed_part_other,
        latent_part_own,
        latent_part_other,
    ) = attention_backward(
        core_index, d_near_own, d_near_other, kept_rows, flat_head, kv_w, *rope
    )
    kv_grad = kv_grad.reshape(groups, kv_rows, kv_parts, kv_piece).transpose(0, 2, 1, 3)
    head_grad = jnp.concatenate([head_grad, kv_grad.reshape(-1, kv_piece)], axis=1)
    head_blocks = head_grad.reshape(deep, -1, head_grad.shape[1])
    head_hops = HopSum(lambda t: at_index(head_blocks, 0, t))
    came, latent_both, normed_both, out_second = tie(
        head_hops.hop(1),
        sum_cores(latent_part_own, latent_part_other),
        sum_cores(normed_part_own, normed_part_other),
        out_second,
    )
    out_line = out_sum.line(out_first, out_second)
    out_hops = HopSum(lambda t: at_index(out_line, 0, (z - t) % deep))
    came, grad_both, out_z = tie(
        head_hops.hop(2, came), sum_plane(latent_both), out_hops.hop(1)
    )
    grad_rope = grad_both[:, rank_width : rank_width + DR] + grad_both[:, rank_width + DR :]
    latent_own = take_rows(latent[0], own_at, half)
    cosine_own = take_rows(cosine[0], own_at, half)
    sine_own = take_rows(sine_tab[0], own_at, half)
    _, scale_kv = rms_forward(latent_own[:, :rank_width], latent_g.astype(f32))
    grad_c, latent_gain_grad = rms_backward(
        latent_own[:, :rank_width], scale_kv, latent_g.astype(f32), grad_both[:, :rank_width]
    )
    grad_latent = jnp.concatenate(
        [grad_c, unrotate(grad_rope, cosine_own, sine_own)], axis=-1
    ).astype(bf16)
    came, latent_parts, grad_normed, out_z = tie(
        head_hops.hop(3, came),
        plane_gather(grad_latent),
        sum_plane(normed_both),
        out_hops.hop(2, out_z),
    )
    latent_near_own = jnp.stack(latent_parts)
    latent_near = in_order(core, latent_near_own, swap_cores(latent_near_own), axis=1)
    head_sums = head_hops.total(came).astype(bf16).reshape(PLANE, block_rows, -1)
    out_z, latent_near, head_shared, grads_came = tie(
        out_hops.hop(3, out_z), latent_near, share_columns(head_sums, place), grads_came
    )
    latent_cut = latent_cols // 2
    latent_near = latent_near.reshape(near_rows, latent_cols)
    latent_blocks = contract_rows(
        normed_cols,
        take_rows(latent_near, core * latent_cut, latent_cut, axis=1),
    )
    latent_half = deep_scatter(latent_blocks.astype(bf16).reshape(deep, -1, latent_cut), z)
    w_latent_grad = in_order(core, latent_half, swap_cores(latent_half), axis=1)


    def by_heads(block):
        rotary = local_heads * DN
        return [
            part
            for h in range(local_heads)
            for part in (
                block[:, h * DN : (h + 1) * DN],
                block[:, rotary + h * DR : rotary + (h + 1) * DR],
            )
        ]

    at_kv = query_cols + out_cols
    w_query_grad = jnp.concatenate([v for p in head_shared for v in by_heads(p)], axis=1)
    w_query_grad = w_query_grad.astype(f32)
    w_kv_grad = jnp.concatenate(
        [
            p[q * kv_rows : (q + 1) * kv_rows, at_kv:]
            for p in head_shared
            for q in range(kv_parts)
        ],
        axis=1,
    ).astype(f32)
    w_out_grad = jnp.concatenate([p[:, query_cols:at_kv] for p in head_shared], axis=1)
    w_out_grad = w_out_grad.astype(f32).T
    sgu_out = grads_came[: 2 * shared_cols].astype(f32)
    sgu_out = sgu_out.reshape(2, shared_cols, groups, block_rows)
    sgu_out = sgu_out.transpose(0, 3, 2, 1).reshape(2, block_rows, -1)
    sdown_out = grads_came[2 * shared_cols : 3 * shared_cols].astype(f32).swapaxes(0, 1).reshape(-1, block_rows)
    grad_normed = grad_normed + contract_cols(grad_latent, latent_w)
    moe_own = out_hops.total(out_z)
    mixed_own = (hidden + moe_own).astype(bf16)
    mixed = in_order(core, mixed_own, swap_cores(mixed_own))

    _, scale_own = rms_forward(x_own, gain_one.astype(f32))
    grad_x_norm, gain_one_grad = rms_backward(x_own, scale_own, gain_one.astype(f32), grad_normed)
    input_own = d_hidden + grad_x_norm
    input_grad = in_order(core, input_own, swap_cores(input_own))

    gain_lanes = jnp.pad(
        latent_gain_grad.reshape(groups, kv_rows), ((0, 0), (0, block_rows - kv_rows))
    )
    vectors = jnp.concatenate(
        [
            router_grad,
            gain_one_grad[None],
            gain_two_grad[None],
            gain_lanes.reshape(1, -1),
        ],
        axis=0,
    ).reshape(-1, groups, block_rows)
    arrived = lax.all_to_all(vectors, "expert", split_axis=1, concat_axis=1, tiled=True)
    sums = jnp.sum(arrived, axis=1)
    sums = sums + swap_cores(sums)
    return (
        mixed,
        input_grad,
        sums[expert_count],
        w_query_grad,
        w_latent_grad,
        sums[expert_count + 2, :kv_rows],
        w_kv_grad,
        w_out_grad,
        sums[expert_count + 1],
        sums[:expert_count].T,
        sgu_out,
        sdown_out,
        egu_grad[None],
        edown_grad[None],
    )


def solution(mesh):
    groups = mesh.shape["expert"]
    plan = token_plan if groups <= 16 else weight_plan
    return jax.shard_map(
        plan,
        mesh=mesh,
        in_specs=(
            P("expert", None),
            P("expert"),
            P("expert", "tensor"),
            P("expert", None),
            P("expert"),
            P("expert", "tensor"),
            P("tensor", "expert"),
            P("expert"),
            P("expert", None),
            P(None, "expert", "tensor"),
            P("tensor", "expert"),
            P("expert", None, None, "tensor"),
            P("expert", "tensor", None),
            P("expert", None),
            P("expert", None),
            P("expert", None),
        ),
        out_specs=(
            P("expert", None),
            P("expert", None),
            P("expert"),
            P("expert", "tensor"),
            P("expert", None),
            P("expert"),
            P("expert", "tensor"),
            P("tensor", "expert"),
            P("expert"),
            P("expert", None),
            P(None, "expert", "tensor"),
            P("tensor", "expert"),
            P("expert", None, None, "tensor"),
            P("expert", "tensor", None),
        ),
        check_vma=False,
    )
```

```python
import functools

import jax
import jax.numpy as jnp
from jax import lax
from jax.experimental import pallas as pl
from jax.experimental.pallas import tpu as pltpu
from jax.sharding import PartitionSpec as P

DN = 128
DR = 64
DV = 128
LANES = 128


EPSILON = 1e-06
ROUTE_SCALE = 2.446
ROPE_BASE = 50000.0
NEGATIVE = -1e30


def cut_along(value, dim, length):
    before, after = (value.shape[:dim], value.shape[dim + 1 :])
    return jnp.moveaxis(value.reshape(*before, length, -1, *after), dim, 0)


def summed_on_arrival(value, axis, dim):
    length = lax.axis_size(axis)
    tiles = lax.all_to_all(cut_along(value, dim, length), axis, 0, 0, tiled=True)
    return jnp.sum(tiles.astype(jnp.float32), axis=0)


def sent_together(arrays, axis, dim, along):
    columns = [a.reshape(*a.shape[:along], -1) for a in arrays]
    both = jnp.concatenate(columns, axis=along)
    whole, at, outs = (summed_on_arrival(both, axis, dim), 0, [])
    for a, column in zip(arrays, columns):
        slab = whole[..., at : at + column.shape[along]]
        outs.append(slab.reshape(*slab.shape[:along], *a.shape[along:]))
        at += column.shape[along]
    return tuple(outs)


def contract_rows(left_arr, right_arr):
    return lax.dot_general(
        left_arr, right_arr, (((0,), (0,)), ((), ())), preferred_element_type=jnp.float32
    )


def contract_cols(left_arr, right_arr):
    return lax.dot_general(
        left_arr, right_arr, (((1,), (1,)), ((), ())), preferred_element_type=jnp.float32
    )


def rms_forward(rows_in, gain_vec):
    inverse = lax.rsqrt(jnp.mean(rows_in * rows_in, axis=-1, keepdims=True) + EPSILON)
    return (rows_in * inverse * gain_vec, inverse)


def rms_backward(rows_in, inverse, gain_vec, grad_out):
    gain_grad = jnp.sum(grad_out * rows_in * inverse, axis=0)
    weighted = grad_out * gain_vec
    inner_mean = jnp.mean(weighted * rows_in, axis=-1, keepdims=True)
    return (inverse * weighted - rows_in * inverse * inverse * inverse * inner_mean, gain_grad)


def doc_layout(doc_lengths, row_count):
    ends_at = jnp.cumsum(doc_lengths)
    starts_at = ends_at - doc_lengths
    position = jnp.arange(row_count, dtype=jnp.int32)
    doc_ids = jnp.sum((position[:, None] >= ends_at[None, :]).astype(jnp.int32), axis=1)
    hitting = doc_ids[:, None] == jnp.arange(doc_lengths.shape[0], dtype=jnp.int32)[None, :]
    start_of = jnp.sum(jnp.where(hitting, starts_at[None, :], 0), axis=1)
    relative = position - start_of
    visible = (doc_ids[:, None] == doc_ids[None, :]) & (position[:, None] >= position[None, :])
    return (relative, visible)


def rope_tables(relative, rot_width):
    counter = jnp.arange(rot_width // 2, dtype=jnp.float32)
    frequency = ROPE_BASE ** (-2.0 * counter / rot_width)
    angles = relative.astype(jnp.float32)[:, None] * frequency[None, :]
    return (jnp.cos(angles), jnp.sin(angles))


def rotate(tensor_in, cosine, sine_tab):
    half_width = tensor_in.shape[-1] // 2
    leading = tensor_in[..., :half_width]
    trailing = tensor_in[..., half_width:]
    return jnp.concatenate(
        [leading * cosine - trailing * sine_tab, trailing * cosine + leading * sine_tab], axis=-1
    )


def unrotate(grad_in, cosine, sine_tab):
    half_width = grad_in.shape[-1] // 2
    leading = grad_in[..., :half_width]
    trailing = grad_in[..., half_width:]
    return jnp.concatenate(
        [leading * cosine + trailing * sine_tab, trailing * cosine - leading * sine_tab], axis=-1
    )


def gated_linear_backward(gate_in, up_in, grad_act):
    sigmoid_g = jax.nn.sigmoid(gate_in)
    grad_gate = grad_act * up_in * sigmoid_g * (1.0 + gate_in * (1.0 - sigmoid_g))
    return (grad_gate, grad_act * gate_in * sigmoid_g)


def slot_tables(route_rows, expert_count, capacity):
    flat_routes = route_rows.reshape(-1)
    one_hot = (flat_routes[:, None] == jnp.arange(expert_count, dtype=jnp.int32)[None, :]).astype(
        jnp.int32
    )
    ranking = jnp.sum((jnp.cumsum(one_hot, axis=0) - one_hot) * one_hot, axis=1)
    slot_ids = flat_routes * capacity + ranking
    row_total = flat_routes.shape[0]
    source = (
        jnp.zeros((expert_count * capacity,), jnp.int32)
        .at[slot_ids]
        .set(jnp.arange(row_total, dtype=jnp.int32))
    )
    filled = jnp.zeros((expert_count * capacity,), jnp.int32).at[slot_ids].set(1)
    return (slot_ids, source, filled)


def to_owner(rows_in):
    arrived = lax.all_to_all(rows_in, "expert", split_axis=0, concat_axis=1, tiled=True)
    return arrived


def weight_plan(
    inputs,
    attn_gain,
    w_query,
    w_latent,
    latent_gain,
    w_kv,
    w_out,
    ffn_gain,
    w_router,
    shared_gate_up,
    shared_down,
    expert_gate_up,
    expert_down,
    lengths,
    routes,
    cotangent,
):
    tok_rows = inputs.shape[0]
    model_width = inputs.shape[1]
    expert_count = w_router.shape[1]
    route_count = routes.shape[1]
    capacity = tok_rows * route_count * 4 // (3 * expert_count)
    brain_float16 = jnp.bfloat16
    f32 = jnp.float32
    gathered = (
        lax.all_gather(attn_gain, "expert", axis=0, tiled=True),
        lax.all_gather(w_query, "expert", axis=0, tiled=True),
        lax.all_gather(w_latent, "expert", axis=0, tiled=True),
        lax.all_gather(latent_gain, "expert", axis=0, tiled=True),
        lax.all_gather(w_kv, "expert", axis=0, tiled=True),
        lax.all_gather(w_out, "expert", axis=1, tiled=True),
        lax.all_gather(ffn_gain, "expert", axis=0, tiled=True),
        lax.all_gather(w_router, "expert", axis=0, tiled=True),
        lax.all_gather(shared_gate_up, "expert", axis=1, tiled=True),
        lax.all_gather(shared_down, "expert", axis=1, tiled=True),
    )
    gain_one, query_w, latent_w, latent_g, kv_w, out_w, gain_two, router_w, sgate_up, sdown_w = (
        gathered
    )
    local_heads = query_w.shape[1] // (DN + DR)
    rank_width = latent_g.shape[0]
    x_float = inputs.astype(f32)
    relative, visible = doc_layout(lengths[0], tok_rows)
    cosine, sine_tab = rope_tables(relative, DR)
    q_scale = (DN + DR) ** (-0.5)
    normed, scale_one = rms_forward(x_float, gain_one.astype(f32))
    normed_b = normed.astype(brain_float16)
    queries = jnp.dot(normed_b, query_w, preferred_element_type=f32).reshape(
        tok_rows, local_heads, DN + DR
    )
    q_rot = rotate(queries[..., DN:], cosine[:, None, :], sine_tab[:, None, :])
    q_all = jnp.concatenate([queries[..., :DN], q_rot], axis=-1).astype(brain_float16)
    latent = jnp.dot(normed_b, latent_w, preferred_element_type=f32)
    compressed, scale_kv = rms_forward(latent[:, :rank_width], latent_g.astype(f32))
    compressed_b = compressed.astype(brain_float16)
    k_rope = rotate(latent[:, rank_width:], cosine, sine_tab).astype(brain_float16)
    kv_all = jnp.dot(compressed_b, kv_w, preferred_element_type=f32).reshape(
        tok_rows, local_heads, DN + DV
    )
    k_nope = kv_all[..., :DN].astype(brain_float16)
    values = kv_all[..., DN:].astype(brain_float16)
    key_all = jnp.concatenate(
        [k_nope, jnp.broadcast_to(k_rope[:, None, :], (tok_rows, local_heads, DR))], axis=-1
    )

    def score_block():
        raw_scores = (
            jnp.einsum("qhd,khd->hqk", q_all, key_all, preferred_element_type=f32) * q_scale
        )
        return jnp.where(visible[None], raw_scores, NEGATIVE)

    scores = score_block()
    top_score = jnp.max(scores, axis=-1, keepdims=True)
    log_total = top_score + jnp.log(jnp.sum(jnp.exp(scores - top_score), axis=-1, keepdims=True))
    probs_b = jnp.exp(scores - log_total).astype(brain_float16)
    attended = jnp.einsum("hqk,khd->qhd", probs_b, values, preferred_element_type=f32)
    attended_b = attended.reshape(tok_rows, local_heads * DV).astype(brain_float16)
    attn = lax.psum(jnp.dot(attended_b, out_w, preferred_element_type=f32), "tensor")
    hidden = x_float + attn
    hnormed, scale_two = rms_forward(hidden, gain_two.astype(f32))
    hnormed_b = hnormed.astype(brain_float16)
    logits = jnp.dot(hnormed_b, router_w, preferred_element_type=f32)
    sigmoid_vals = jax.nn.sigmoid(logits)
    route_hot = routes[:, :, None] == jnp.arange(expert_count, dtype=jnp.int32)[None, None, :]
    chosen = jnp.sum(jnp.where(route_hot, sigmoid_vals[:, None, :], 0.0), axis=2)
    chosen_sum = jnp.sum(chosen, axis=1, keepdims=True)
    gate_vals = ROUTE_SCALE * chosen / chosen_sum
    slot_ids, source, filled = slot_tables(routes, expert_count, capacity)
    is_filled = filled[:, None] == 1
    sent_rows = jnp.where(is_filled, hnormed_b[source // route_count], 0).reshape(
        expert_count, capacity, model_width
    )
    received = to_owner(sent_rows)
    gate_up_joined = jnp.einsum(
        "erd,egdf->egrf", received, expert_gate_up, preferred_element_type=f32
    )
    expert_act = (jax.nn.silu(gate_up_joined[:, 0]) * gate_up_joined[:, 1]).astype(brain_float16)
    expert_res = jnp.einsum(
        "erf,efd->erd", expert_act, expert_down, preferred_element_type=f32
    ).astype(brain_float16)
    returned_all = lax.all_to_all(expert_res, "expert", split_axis=1, concat_axis=0, tiled=True)
    returned = returned_all.reshape(expert_count * capacity, model_width)[slot_ids].reshape(
        tok_rows, route_count, model_width
    )
    shared_gu = jnp.einsum("td,gdf->gtf", hnormed_b, sgate_up, preferred_element_type=f32)
    shared_act = (jax.nn.silu(shared_gu[0]) * shared_gu[1]).astype(brain_float16)
    branch_sum = jnp.dot(shared_act, sdown_w, preferred_element_type=f32)
    for route_idx in range(route_count):
        branch_sum = branch_sum + gate_vals[:, route_idx : route_idx + 1] * returned[
            :, route_idx
        ].astype(f32)
    moe_out = lax.psum(branch_sum.astype(jnp.bfloat16), "tensor").astype(jnp.float32)
    mixed = (hidden + moe_out).astype(brain_float16)
    grad_y = cotangent.astype(f32)
    sdown_grad = contract_rows(shared_act, cotangent)
    grad_sact = contract_cols(cotangent, sdown_w)
    grad_sgate, grad_sup = gated_linear_backward(shared_gu[0], shared_gu[1], grad_sact)
    grad_sgu = jnp.stack([grad_sgate, grad_sup], axis=0).astype(brain_float16)
    sgu_grad = jnp.einsum("td,gtf->gdf", hnormed_b, grad_sgu, preferred_element_type=f32)
    grad_hn_part = jnp.einsum("gtf,gdf->td", grad_sgu, sgate_up, preferred_element_type=f32)
    gate_columns = []
    for route_idx in range(route_count):
        gate_columns.append(jnp.sum(grad_y * returned[:, route_idx].astype(f32), axis=1))
    gate_part = jnp.stack(gate_columns, axis=1)
    slot_grads = (
        (gate_vals[:, :, None] * grad_y[:, None, :])
        .reshape(tok_rows * route_count, model_width)
        .astype(brain_float16)
    )
    grad_sent = jnp.where(is_filled, slot_grads[source], 0).reshape(
        expert_count, capacity, model_width
    )
    grad_received = to_owner(grad_sent)
    edown_grad = jnp.einsum("erf,erd->efd", expert_act, grad_received, preferred_element_type=f32)
    expert_activation_gradient = jnp.einsum(
        "erd,efd->erf", grad_received, expert_down, preferred_element_type=f32
    )
    expert_gate_gradient, expert_up_gradient = gated_linear_backward(
        gate_up_joined[:, 0], gate_up_joined[:, 1], expert_activation_gradient
    )
    expert_gate_up_gradient = jnp.stack([expert_gate_gradient, expert_up_gradient], axis=1).astype(
        brain_float16
    )
    egu_grad = jnp.einsum(
        "erd,egrf->egdf", received, expert_gate_up_gradient, preferred_element_type=f32
    )
    grad_rows = jnp.einsum(
        "egrf,egdf->erd", expert_gate_up_gradient, expert_gate_up, preferred_element_type=f32
    ).astype(brain_float16)
    grad_back = lax.all_to_all(grad_rows, "expert", split_axis=1, concat_axis=0, tiled=True)
    grad_routes = grad_back.reshape(expert_count * capacity, model_width)[slot_ids].reshape(
        tok_rows, route_count, model_width
    )
    for route_idx in range(route_count):
        grad_hn_part = grad_hn_part + grad_routes[:, route_idx].astype(f32)
    gate_grads = lax.psum(gate_part, "tensor")
    grad_chosen = ROUTE_SCALE * (
        gate_grads / chosen_sum
        - jnp.sum(gate_grads * chosen, axis=1, keepdims=True) / (chosen_sum * chosen_sum)
    )
    grad_sig = jnp.sum(jnp.where(route_hot, grad_chosen[:, :, None], 0.0), axis=1)
    grad_logits = (grad_sig * sigmoid_vals * (1.0 - sigmoid_vals)).astype(brain_float16)
    router_grad = contract_rows(hnormed_b, grad_logits)
    grad_hn = lax.psum(grad_hn_part, "tensor") + contract_cols(grad_logits, router_w)
    grad_hidden_norm, gain_two_grad = rms_backward(hidden, scale_two, gain_two.astype(f32), grad_hn)
    grad_hidden = grad_y + grad_hidden_norm
    grad_hidden_b = grad_hidden.astype(brain_float16)
    out_grad = contract_rows(attended_b, grad_hidden_b)
    grad_att = (
        contract_cols(grad_hidden_b, out_w).reshape(tok_rows, local_heads, DV).astype(brain_float16)
    )
    probs = jnp.exp(score_block() - log_total)
    probs_again = probs.astype(brain_float16)
    grad_probs = jnp.einsum("qhd,khd->hqk", grad_att, values, preferred_element_type=f32)
    grad_vals = jnp.einsum("hqk,qhd->khd", probs_again, grad_att, preferred_element_type=f32)
    row_delta = jnp.sum(probs * grad_probs, axis=-1, keepdims=True)
    grad_scores = (probs * (grad_probs - row_delta)).astype(brain_float16)
    grad_q = jnp.einsum("hqk,khd->qhd", grad_scores, key_all, preferred_element_type=f32) * q_scale
    grad_keys = jnp.einsum("hqk,qhd->khd", grad_scores, q_all, preferred_element_type=f32) * q_scale
    grad_kv = (
        jnp.concatenate([grad_keys[..., :DN], grad_vals], axis=-1)
        .reshape(tok_rows, local_heads * (DN + DV))
        .astype(brain_float16)
    )
    kv_grad = contract_rows(compressed_b, grad_kv)
    grad_comp_part = contract_cols(grad_kv, kv_w)
    grad_krope_part = jnp.sum(grad_keys[..., DN:], axis=1)
    grad_comp, grad_krope = (
        lax.psum(grad_comp_part.astype(jnp.bfloat16), "tensor").astype(jnp.float32),
        lax.psum(grad_krope_part.astype(jnp.bfloat16), "tensor").astype(jnp.float32),
    )
    grad_c, latent_gain_grad = rms_backward(
        latent[:, :rank_width], scale_kv, latent_g.astype(f32), grad_comp
    )
    grad_latent = jnp.concatenate([grad_c, unrotate(grad_krope, cosine, sine_tab)], axis=-1).astype(
        brain_float16
    )
    grad_qrot = unrotate(grad_q[..., DN:], cosine[:, None, :], sine_tab[:, None, :])
    grad_queries = (
        jnp.concatenate([grad_q[..., :DN], grad_qrot], axis=-1)
        .reshape(tok_rows, local_heads * (DN + DR))
        .astype(brain_float16)
    )
    query_grad = contract_rows(normed_b, grad_queries)
    latent_grad = contract_rows(normed_b, grad_latent)
    grad_normed = lax.psum(
        contract_cols(grad_queries, query_w).astype(jnp.bfloat16), "tensor"
    ).astype(jnp.float32) + contract_cols(grad_latent, latent_w)
    grad_x_norm, gain_one_grad = rms_backward(x_float, scale_one, gain_one.astype(f32), grad_normed)
    input_grad = grad_hidden + grad_x_norm
    first_owned = (
        *sent_together(
            (
                gain_one_grad.astype(jnp.bfloat16),
                query_grad.astype(jnp.bfloat16),
                latent_grad.astype(jnp.bfloat16),
            ),
            "expert",
            0,
            1,
        ),
        *sent_together(
            (latent_gain_grad.astype(jnp.bfloat16), kv_grad.astype(jnp.bfloat16)), "expert", 0, 1
        ),
    )
    second_owned = (
        lax.psum_scatter(out_grad, "expert", scatter_dimension=1, tiled=True),
        lax.psum_scatter(gain_two_grad, "expert", scatter_dimension=0, tiled=True),
        lax.psum_scatter(router_grad, "expert", scatter_dimension=0, tiled=True),
        lax.psum_scatter(sgu_grad, "expert", scatter_dimension=1, tiled=True),
        lax.psum_scatter(sdown_grad, "expert", scatter_dimension=1, tiled=True),
    )
    return (
        mixed,
        input_grad,
        first_owned[0],
        first_owned[1],
        first_owned[2],
        first_owned[3],
        first_owned[4],
        second_owned[0],
        second_owned[1],
        second_owned[2],
        second_owned[3],
        second_owned[4],
        egu_grad,
        edown_grad,
    )


def swap_cores(value):
    return lax.ppermute(value, "tensor", [(0, 1), (1, 0)])


def take_rows(value, start, count, axis=0):
    return lax.dynamic_slice_in_dim(value, start, count, axis=axis)


def in_order(core, own, other, axis=0):
    return jnp.where(
        core == 0,
        jnp.concatenate([own, other], axis=axis),
        jnp.concatenate([other, own], axis=axis),
    )


def add_wide(*parts):
    total = parts[0].astype(jnp.float32)
    for part in parts[1:]:
        total = total + part.astype(jnp.float32)
    return total


PLANE = 4


def to_partner(value, flips):
    groups = lax.axis_size("expert")
    return lax.ppermute(value, "expert", [(g, g ^ flips) for g in range(groups)])


def to_deeper(value, step):
    groups = lax.axis_size("expert")
    pairs = [(g, (g + step * PLANE) % groups) for g in range(groups)]
    return lax.ppermute(value, "expert", pairs)


def plane_gather(value):
    return [value] + [to_partner(value, r) for r in range(1, PLANE)]


def plane_scatter(parts):
    return add_wide(parts[0], *[to_partner(parts[r], r) for r in range(1, PLANE)])


def by_place(parts, place):
    odd, high = place % 2 == 1, place // 2 == 1
    parts = [jnp.where(odd, parts[i ^ 1], parts[i]) for i in range(PLANE)]
    return [jnp.where(high, parts[i ^ 2], parts[i]) for i in range(PLANE)]


def tie(*values):
    return lax.optimization_barrier(values)


def deep_pieces(value):
    deep = lax.axis_size("expert") // PLANE
    return [to_deeper(value, s) for s in range(1, deep)]


def one_plane(value, step):
    groups = lax.axis_size("expert")
    pairs = [(g, g + step * PLANE) for g in range(groups) if 0 <= g + step * PLANE < groups]
    return lax.ppermute(value, "expert", pairs)


def deep_hops(value):
    deep = lax.axis_size("expert") // PLANE
    after, before, down, up = [], [], value, value
    for _ in range(1, deep):
        down, up = one_plane(down, 1), one_plane(up, -1)
        after.append(down)
        before.append(up)
    return after, before


def join_hops(hops):
    after, before = hops
    return [a + b for a, b in zip(after, before[::-1])]


def deep_join(value, pieces, z):
    deep = lax.axis_size("expert") // PLANE
    whole = jnp.zeros((deep, *value.shape), value.dtype)
    whole = lax.dynamic_update_index_in_dim(whole, value, z, 0)
    for step in range(1, deep):
        whole = lax.dynamic_update_index_in_dim(whole, pieces[step - 1], (z - step) % deep, 0)
    return whole


def deep_move(blocks, z):
    deep = blocks.shape[0]

    def block(index):
        return lax.dynamic_index_in_dim(blocks, index, 0, keepdims=False)

    return [block(z)] + [to_deeper(block((z + step) % deep), step) for step in range(1, deep)]


def deep_scatter(blocks, z):
    return add_wide(*deep_move(blocks, z))


def share_columns(rows, place):
    parts = [at_index(rows, 0, place)]
    for r in range(1, PLANE):
        parts.append(to_partner(at_index(rows, 0, place ^ r), r))
    return by_place(parts, place)


def all_groups(value):
    return lax.all_gather(value, "expert", axis=0, tiled=False)


def at_index(value, axis, index):
    return lax.dynamic_index_in_dim(value, index, axis, keepdims=False)


def doc_places(doc_lengths, row_count):
    ends_at = jnp.cumsum(doc_lengths)
    position = jnp.arange(row_count, dtype=jnp.int32)
    doc_ids = jnp.sum((position[:, None] >= ends_at[None, :]).astype(jnp.int32), axis=1)
    hitting = doc_ids[:, None] == jnp.arange(doc_lengths.shape[0], dtype=jnp.int32)[None, :]
    start_of = jnp.sum(jnp.where(hitting, (ends_at - doc_lengths)[None, :], 0), axis=1)
    return position - start_of, doc_ids


class HopSum:
    def __init__(self, pieces):
        self.groups = lax.axis_size("expert")
        self.deep = self.groups // PLANE
        self.z = lax.axis_index("expert") // PLANE
        self.pieces = pieces

    def hop(self, step, came=None):
        arrived = []
        for side, way in enumerate((1, -1)):
            target = jnp.clip(self.z + way * (self.deep - step), 0, self.deep - 1)
            gone = self.pieces(target)
            if came is not None:
                gone = add_wide(gone, came[side]).astype(gone.dtype)
            first = range(step) if way == 1 else range(self.deep - step, self.deep)
            pairs = [
                (p * PLANE + q, (p + way) * PLANE + q) for p in first for q in range(PLANE)
            ]
            arrived.append(lax.ppermute(gone, "expert", pairs))
        return arrived

    def total(self, came):
        return add_wide(self.pieces(self.z), *came)


def doc_places(doc_lengths, row_count):
    ends_at = jnp.cumsum(doc_lengths)
    position = jnp.arange(row_count, dtype=jnp.int32)
    doc_ids = jnp.sum((position[:, None] >= ends_at[None, :]).astype(jnp.int32), axis=1)
    hitting = doc_ids[:, None] == jnp.arange(doc_lengths.shape[0], dtype=jnp.int32)[None, :]
    start_of = jnp.sum(jnp.where(hitting, (ends_at - doc_lengths)[None, :], 0), axis=1)
    return position - start_of, doc_ids


def hop_sum(pieces):
    groups = lax.axis_size("expert")
    deep = groups // PLANE
    z = lax.axis_index("expert") // PLANE
    ends = []
    for way in (1, -1):
        came = None
        for step in range(1, deep):
            gone = pieces(jnp.clip(z + way * (deep - step), 0, deep - 1))
            if came is not None:
                gone = add_wide(gone, came).astype(gone.dtype)
            first = range(step) if way == 1 else range(deep - step, deep)
            pairs = [
                (p * PLANE + q, (p + way) * PLANE + q) for p in first for q in range(PLANE)
            ]
            came = lax.ppermute(gone, "expert", pairs)
        ends.append(came)
    return [pieces(z), *ends]


class RowGather:
    def __init__(self, value):
        self.cut = value.shape[0] // 2
        self.value = value

    def along(self):
        return [self.value] + deep_pieces(self.value)

    def lines(self, came):
        return [jnp.stack([v[: self.cut] for v in came]), jnp.stack([v[self.cut :] for v in came])]

    def over(self, lines):
        first, second = lines
        return to_partner(first, 1), to_partner(second, 2)

    def over_other(self, lines):
        first, second = lines
        return to_partner(first, 2), to_partner(second, 1)

    def over_again(self, came):
        beside, behind = came
        return to_partner(beside, 2), to_partner(behind, 1)


def blocks_of(lines, over, over_other, over_again, which):
    first = [lines[0], over[0], over_other[0], over_again and over_again[0]]
    second = [lines[1], over_other[1], over[1], over_again and over_again[1]]
    halves = [jnp.concatenate([half[r] for r in which], axis=0) for half in (first, second)]
    return jnp.concatenate(halves, axis=1)


class RowSum:
    def __init__(self, *terms):
        self.type = terms[0][0].dtype
        cut = terms[0][0].shape[1] // 2
        self.halves = (
            ([[b[:, :cut] for b in v] for v in terms], 2, 1),
            ([[b[:, cut:] for b in v] for v in terms], 1, 2),
        )

    def _add(self, parts):
        return add_wide(*parts).astype(self.type)

    def sends(self):
        return [
            jnp.stack([self._add([v[far] for v in held]), self._add([v[far | near] for v in held])])
            for held, far, near in self.halves
        ]

    def move(self, sends):
        return [to_partner(v, far) for v, (_, far, _) in zip(sends, self.halves)]

    def sends_again(self, came):
        return [
            self._add([v[near] for v in held] + [c[1]])
            for c, (held, _, near) in zip(came, self.halves)
        ]

    def move_again(self, sends):
        return [to_partner(v, near) for v, (_, _, near) in zip(sends, self.halves)]

    def line(self, came, came_again):
        sums = [
            self._add([v[0] for v in held] + [c[0], d])
            for c, d, (held, *_) in zip(came, came_again, self.halves)
        ]
        return jnp.concatenate(sums, axis=1)


def line_sends(line):
    return [line[step] for step in range(line.shape[0])]


def line_move(sends):
    return [sends[0]] + [to_deeper(v, -step) for step, v in enumerate(sends) if step > 0]


def dot_nn(left, right):
    return lax.dot_general(left, right, (((1,), (0,)), ((), ())), preferred_element_type=jnp.float32)


def dot_nt(left, right):
    return lax.dot_general(left, right, (((1,), (1,)), ((), ())), preferred_element_type=jnp.float32)


def dot_tn(left, right):
    return lax.dot_general(left, right, (((0,), (0,)), ((), ())), preferred_element_type=jnp.float32)


def two_lanes(column, lane):
    high = column.astype(jnp.bfloat16).astype(jnp.float32)
    spread = jnp.where(lane == 0, high, jnp.where(lane == 1, column - high, 0.0))
    return spread.astype(jnp.bfloat16)


def expert_kernel(
    shared_cols,
    expert_count,
    me_ref,
    hn_own,
    hn_other,
    dy_own,
    dy_other,
    meta_own,
    meta_other,
    gate_up_w,
    down_w,
    first_w,
    sdown_w,
    slots_out,
    slot_dy_out,
    act_out,
    d_gate_up_out,
    rows_own_out,
    rows_other_out,
    sact_own_out,
    sact_other_out,
    shared_grads_out,
    dgate_own_out,
    dgate_other_out,
):
    f32, bf16 = jnp.float32, jnp.bfloat16
    count, half, _ = hn_own.shape
    tokens = 2 * half
    me = me_ref[0]
    lane = lax.broadcasted_iota(jnp.int32, (count * tokens, LANES), 1)
    is_router = (lane >= shared_cols) & (lane < shared_cols + expert_count)
    first = first_w[...]

    def joined(own, other):
        return jnp.concatenate([v[i] for i in range(count) for v in (own, other)], axis=0)

    rows, rows_dy = joined(hn_own, hn_other), joined(dy_own, dy_other)
    meta = joined(meta_own, meta_other)
    products = dot_nt(rows, first)
    gate, up = products[:, :LANES], products[:, LANES:]
    sig = jax.nn.sigmoid(gate)
    total = jnp.sum(jnp.where(is_router, sig * meta, 0.0), axis=1, keepdims=True)
    mine = jnp.sum(jnp.where(lane == shared_cols + me, sig, 0.0), axis=1, keepdims=True)
    token_gate = two_lanes(ROUTE_SCALE * mine / total, lane)
    sact = (gate * sig * up).astype(bf16)
    d_sact = dot_nt(rows_dy, sdown_w[...])
    d_sgate = d_sact * up * sig * (1.0 + gate * (1.0 - sig))
    dsh = jnp.concatenate([d_sgate, d_sact * gate * sig], axis=1).astype(bf16)
    pick = (meta[:, :1] == lane.astype(f32)).astype(bf16)
    groups = [slice(i * tokens, (i + 1) * tokens) for i in range(count)]
    for i in range(count):
        start = i * tokens
        sact_own_out[i] = sact[start : start + half]
        sact_other_out[i] = sact[start + half : start + tokens]
    slots = [dot_tn(pick[g], rows[g]).astype(bf16) for g in groups]
    slot_dys = [dot_tn(pick[g], rows_dy[g]).astype(bf16) for g in groups]
    slot_gates = [
        jnp.sum(dot_tn(pick[g], token_gate[g]), axis=1, keepdims=True) for g in groups
    ]

    @pl.when(pl.program_id(0) == 0)
    def _():
        shared_grads_out[...] = jnp.zeros_like(shared_grads_out)

    first_grad, sdown_grad = dot_tn(dsh, rows), dot_tn(sact, rows_dy)
    shared_grads_out[:shared_cols] += first_grad[:shared_cols]
    shared_grads_out[shared_cols : 2 * shared_cols] += first_grad[LANES : LANES + shared_cols]
    shared_grads_out[2 * shared_cols :] += sdown_grad[:shared_cols]
    slot_rows = jnp.concatenate(slots, axis=0)
    slot_dy = jnp.concatenate(slot_dys, axis=0)
    slot_gate = jnp.concatenate(slot_gates, axis=0)
    slots_out[...] = slot_rows
    slot_dy_out[...] = slot_dy
    gate = dot_nt(slot_rows, gate_up_w[0])
    up = dot_nt(slot_rows, gate_up_w[1])
    d_act = dot_nt(slot_dy, down_w[...])
    sig = jax.nn.sigmoid(gate)
    silu = gate * sig
    act = silu * up
    slot_dgate = jnp.sum(act * d_act, axis=1, keepdims=True)
    act_out[...] = (slot_gate * act).astype(bf16)
    d_act = slot_gate * d_act
    d_gate = (d_act * up * sig * (1.0 + gate * (1.0 - sig))).astype(bf16)
    d_up = (d_act * silu).astype(bf16)
    d_gate_up_out[0] = d_gate
    d_gate_up_out[1] = d_up
    d_slots = (dot_nn(d_gate, gate_up_w[0]) + dot_nn(d_up, gate_up_w[1])).astype(bf16)
    slot_lane = lax.broadcasted_iota(jnp.int32, (LANES, LANES), 1)
    d_shared = dot_nn(dsh, first)
    for i, g in enumerate(groups):
        here = slice(i * LANES, (i + 1) * LANES)
        d_rows = (dot_nn(pick[g], d_slots[here]) + d_shared[g]).astype(bf16)
        rows_own_out[i], rows_other_out[i] = d_rows[:half], d_rows[half:]
        dgate = dot_nn(pick[g], two_lanes(slot_dgate[here], slot_lane))
        dgate_own_out[i], dgate_other_out[i] = dgate[:half], dgate[half:]


def block_specs(per_step):
    def lead(*tail):
        return pl.BlockSpec((per_step, *tail), lambda i: (i,) + (0,) * len(tail))

    def flat(cols):
        return pl.BlockSpec((per_step * LANES, cols), lambda i: (i, 0))

    def whole(a):
        return pl.BlockSpec(a.shape, lambda i: (0,) * a.ndim, pipeline_mode=pl.Buffered(1))

    return lead, flat, whole


def experts(
    me,
    hn_own,
    hn_other,
    dy_own,
    dy_other,
    meta_own,
    meta_other,
    gate_up_w,
    down_w,
    first_w,
    sdown_w,
    shared_cols,
    expert_count,
    per_step=2,
):
    groups, half, width = hn_own.shape
    hidden = down_w.shape[0]
    slots = groups * LANES
    f32, bf16 = jnp.float32, jnp.bfloat16
    lead, flat, whole = block_specs(per_step)
    sds = jax.ShapeDtypeStruct
    return pl.pallas_call(
        functools.partial(expert_kernel, shared_cols, expert_count),
        grid=(groups // per_step,),
        in_specs=[
            pl.BlockSpec(memory_space=pltpu.SMEM),
            *[lead(half, width)] * 4,
            *[lead(half, LANES)] * 2,
            *[whole(a) for a in (gate_up_w, down_w, first_w, sdown_w)],
        ],
        out_specs=[
            flat(width),
            flat(width),
            flat(hidden),
            pl.BlockSpec((2, per_step * LANES, hidden), lambda i: (0, i, 0)),
            *[lead(half, width)] * 2,
            *[lead(half, LANES)] * 2,
            pl.BlockSpec((3 * shared_cols, width), lambda i: (0, 0)),
            *[lead(half, LANES)] * 2,
        ],
        out_shape=[
            sds((slots, width), bf16),
            sds((slots, width), bf16),
            sds((slots, hidden), bf16),
            sds((2, slots, hidden), bf16),
            *[sds((groups, half, width), bf16)] * 2,
            *[sds((groups, half, LANES), bf16)] * 2,
            sds((3 * shared_cols, width), f32),
            *[sds((groups, half, LANES), f32)] * 2,
        ],
        compiler_params=pltpu.CompilerParams(vmem_limit_bytes=58 * 1024 * 1024),
        cost_estimate=pl.CostEstimate(
            flops=groups * width, bytes_accessed=groups * width, transcendentals=0
        ),
    )(
        me,
        hn_own,
        hn_other,
        dy_own,
        dy_other,
        meta_own,
        meta_other,
        gate_up_w,
        down_w,
        first_w,
        sdown_w,
    )


def swap_halves(value, lane):
    low = lane % DR < DR // 2
    return jnp.where(low, pltpu.roll(value, LANES - DR // 2, 1), pltpu.roll(value, DR // 2, 1))


def by_core(core, first, second):
    return jnp.where(core == 0, first, second), jnp.where(core == 0, second, first)


def head_scores(q, kv, k_rope, visible, lane, head, heads):
    q_nope = q[:, head * DN : (head + 1) * DN]
    q_rope = jnp.where(lane // DR == head, q[:, heads * DN :], jnp.zeros((), q.dtype))
    at = head * (DN + DV)
    k_nope, value = kv[:, at : at + DN], kv[:, at + DN : at + DN + DV]
    scores = (dot_nt(q_nope, k_nope) + dot_nt(q_rope, k_rope)) * (DN + DR) ** -0.5
    return jnp.where(visible, scores, NEGATIVE), q_nope, q_rope, k_nope, value


def seen(doc_col, doc_row):
    rows = doc_col.shape[0]
    later = lax.broadcasted_iota(jnp.int32, (rows, rows), 0) >= lax.broadcasted_iota(
        jnp.int32, (rows, rows), 1
    )
    return (doc_col == doc_row) & later


def attention_kernel(
    heads,
    rank,
    core_ref,
    x_own,
    x_other,
    gain,
    latent_gain,
    head_w,
    small_w,
    kv_w,
    cosine,
    sine,
    doc_col,
    doc_row,
    normed_out,
    compressed_out,
    q_out,
    kv_out,
    k_rope_out,
    sums_out,
    attended_out,
    latent_out,
    part_own_out,
    part_other_out,
):
    f32, bf16 = jnp.float32, jnp.bfloat16
    core = core_ref[0]
    x = jnp.concatenate(by_core(core, x_own[0], x_other[0]), axis=0).astype(f32)
    rows = x.shape[0]
    half = rows // 2
    lane = lax.broadcasted_iota(jnp.int32, (rows, LANES), 1)
    inverse = lax.rsqrt(jnp.mean(x * x, axis=1, keepdims=True) + EPSILON)
    normed = (x * inverse * gain[...]).astype(bf16)
    normed_out[0] = normed
    q_cols = heads * (DN + DR)
    queries = dot_nn(normed, head_w[:, :q_cols])
    q_rope = queries[:, heads * DN :]
    q_rope = q_rope * cosine[0] + swap_halves(q_rope, lane) * sine[0]
    q = jnp.concatenate([queries[:, : heads * DN], q_rope], axis=1).astype(bf16)
    q_out[0] = q
    latent = dot_nn(normed, small_w[:, : rank + LANES])
    latent_out[0] = latent
    squeezed = latent[:, :rank]
    inverse = lax.rsqrt(jnp.mean(squeezed * squeezed, axis=1, keepdims=True) + EPSILON)
    compressed = (squeezed * inverse * latent_gain[...]).astype(bf16)
    compressed_out[0] = compressed
    k_rope = latent[:, rank:]
    k_rope = (k_rope * cosine[0] + swap_halves(k_rope, lane) * sine[0]).astype(bf16)
    k_rope_out[0] = k_rope
    kv = dot_nn(compressed, kv_w[...]).astype(bf16)
    kv_out[0] = kv
    visible = seen(doc_col[0], doc_row[0])
    attended, sums = [], jnp.zeros((rows, LANES), f32)
    for head in range(heads):
        scores, *_, value = head_scores(q, kv, k_rope, visible, lane, head, heads)
        top = jnp.max(scores, axis=1, keepdims=True)
        log_total = top + jnp.log(jnp.sum(jnp.exp(scores - top), axis=1, keepdims=True))
        sums = jnp.where(lane == head, log_total, sums)
        probs = jnp.exp(scores - log_total).astype(bf16)
        attended.append(dot_nn(probs, value).astype(bf16))
    sums_out[0] = sums
    attended = jnp.concatenate(attended, axis=1)
    attended_out[0] = attended
    part = dot_nt(attended, head_w[:, q_cols : q_cols + heads * DV]).astype(bf16)
    part_own_out[0], part_other_out[0] = by_core(core, part[:half], part[half:])


def attention_backward_kernel(
    heads,
    core_ref,
    d_own,
    d_other,
    normed_ref,
    compressed_ref,
    q_ref,
    kv_ref,
    k_rope_ref,
    sums_ref,
    attended_ref,
    head_w,
    kv_w,
    cosine,
    sine,
    doc_col,
    doc_row,
    head_grad_out,
    kv_grad_out,
    normed_own_out,
    normed_other_out,
    latent_own_out,
    latent_other_out,
    head_acc,
    kv_acc,
):
    f32, bf16 = jnp.float32, jnp.bfloat16
    core, step = core_ref[0], pl.program_id(0)
    scale = (DN + DR) ** -0.5
    d_rows = jnp.concatenate(by_core(core, d_own[0], d_other[0]), axis=0)
    rows = d_rows.shape[0]
    half = rows // 2
    lane = lax.broadcasted_iota(jnp.int32, (rows, LANES), 1)
    q_cols = heads * (DN + DR)
    q, kv, k_rope = q_ref[0], kv_ref[0], k_rope_ref[0]
    d_attended = dot_nn(d_rows, head_w[:, q_cols : q_cols + heads * DV]).astype(bf16)
    visible = seen(doc_col[0], doc_row[0])
    d_q, d_kv = [], []
    d_q_rope, d_k_rope = jnp.zeros((rows, LANES), f32), jnp.zeros((rows, LANES), f32)
    for head in range(heads):
        scores, q_nope, q_rope, k_nope, value = head_scores(
            q, kv, k_rope, visible, lane, head, heads
        )
        probs = jnp.exp(scores - sums_ref[0][:, head : head + 1])
        d_head = d_attended[:, head * DV : (head + 1) * DV]
        d_probs = dot_nt(d_head, value)
        d_value = dot_tn(probs.astype(bf16), d_head)
        delta = jnp.sum(probs * d_probs, axis=1, keepdims=True)
        d_scores = (probs * (d_probs - delta)).astype(bf16)
        d_q.append(dot_nn(d_scores, k_nope) * scale)
        d_q_rope = jnp.where(lane // DR == head, dot_nn(d_scores, k_rope) * scale, d_q_rope)
        d_kv += [dot_tn(d_scores, q_nope) * scale, d_value]
        d_k_rope += dot_tn(d_scores, q_rope) * scale
    d_q_rope = d_q_rope * cosine[0] - swap_halves(d_q_rope, lane) * sine[0]
    d_q = jnp.concatenate(d_q + [d_q_rope], axis=1).astype(bf16)
    d_kv = jnp.concatenate(d_kv, axis=1).astype(bf16)

    @pl.when(step == 0)
    def _():
        head_acc[...] = jnp.zeros_like(head_acc)
        kv_acc[...] = jnp.zeros_like(kv_acc)

    head_acc[:, :q_cols] += dot_tn(normed_ref[0], d_q)
    head_acc[:, q_cols:] += dot_tn(d_rows, attended_ref[0])
    kv_acc[...] += dot_tn(compressed_ref[0], d_kv)

    @pl.when(step == pl.num_programs(0) - 1)
    def _():
        head_grad_out[...] = head_acc[...].astype(bf16)
        kv_grad_out[...] = kv_acc[...].astype(bf16)

    part = dot_nt(d_q, head_w[:, :q_cols]).astype(bf16)
    normed_own_out[0], normed_other_out[0] = by_core(core, part[:half], part[half:])
    latent = jnp.concatenate([dot_nt(d_kv, kv_w[...]), d_k_rope], axis=1).astype(bf16)
    latent_own_out[0], latent_other_out[0] = by_core(core, latent[:half], latent[half:])


def one_each(*tail):
    return pl.BlockSpec((1, *tail), lambda i: (i,) + (0,) * len(tail))


def kept(value):
    return pl.BlockSpec(value.shape, lambda i: (0,) * value.ndim, pipeline_mode=pl.Buffered(1))


def attention(core, x_own, x_other, gain, latent_gain, head_w, small_w, kv_w, cosine, sine, doc):
    near, half, width = x_own.shape
    rows = 2 * half
    rank, kv_cols = kv_w.shape
    heads = kv_cols // (DN + DV)
    f32, bf16 = jnp.float32, jnp.bfloat16
    shapes = [
        ((rows, width), bf16),
        ((rows, rank), bf16),
        ((rows, heads * (DN + DR)), bf16),
        ((rows, kv_cols), bf16),
        ((rows, LANES), bf16),
        ((rows, LANES), f32),
        ((rows, heads * DV), bf16),
        ((rows, rank + LANES), f32),
        ((half, width), bf16),
        ((half, width), bf16),
    ]
    return pl.pallas_call(
        functools.partial(attention_kernel, heads, rank),
        grid=(near,),
        in_specs=[
            pl.BlockSpec(memory_space=pltpu.SMEM),
            *[one_each(half, width)] * 2,
            *[kept(a) for a in (gain, latent_gain, head_w, small_w, kv_w)],
            *[one_each(rows, LANES)] * 2,
            one_each(rows, 1),
            one_each(1, rows),
        ],
        out_specs=[one_each(*shape) for shape, _ in shapes],
        out_shape=[jax.ShapeDtypeStruct((near, *shape), kind) for shape, kind in shapes],
        compiler_params=pltpu.CompilerParams(vmem_limit_bytes=58 * 1024 * 1024),
        cost_estimate=pl.CostEstimate(
            flops=2 * near * rows * width * (rank + 3 * heads * DN),
            bytes_accessed=4 * near * rows * width,
            transcendentals=0,
        ),
    )(
        core,
        x_own,
        x_other,
        gain,
        latent_gain,
        head_w,
        small_w,
        kv_w,
        cosine,
        sine,
        doc[:, :, None],
        doc[:, None, :],
    )


def attention_backward(core, d_own, d_other, kept_rows, head_w, kv_w, cosine, sine, doc):
    near, half, width = d_own.shape
    rows = 2 * half
    rank, kv_cols = kv_w.shape
    heads = kv_cols // (DN + DV)
    head_cols = heads * (DN + DR + DV)
    f32, bf16 = jnp.float32, jnp.bfloat16
    sds = jax.ShapeDtypeStruct
    return pl.pallas_call(
        functools.partial(attention_backward_kernel, heads),
        grid=(near,),
        in_specs=[
            pl.BlockSpec(memory_space=pltpu.SMEM),
            *[one_each(half, width)] * 2,
            *[one_each(*v.shape[1:]) for v in kept_rows],
            *[kept(a) for a in (head_w, kv_w)],
            *[one_each(rows, LANES)] * 2,
            one_each(rows, 1),
            one_each(1, rows),
        ],
        out_specs=[
            pl.BlockSpec((width, head_cols), lambda i: (0, 0)),
            pl.BlockSpec((rank, kv_cols), lambda i: (0, 0)),
            *[one_each(half, width)] * 2,
            *[one_each(half, rank + LANES)] * 2,
        ],
        out_shape=[
            sds((width, head_cols), bf16),
            sds((rank, kv_cols), bf16),
            *[sds((near, half, width), bf16)] * 2,
            *[sds((near, half, rank + LANES), bf16)] * 2,
        ],
        scratch_shapes=[
            pltpu.VMEM((width, head_cols), f32),
            pltpu.VMEM((rank, kv_cols), f32),
        ],
        compiler_params=pltpu.CompilerParams(vmem_limit_bytes=58 * 1024 * 1024),
        cost_estimate=pl.CostEstimate(
            flops=near * rows * width * heads * DN,
            bytes_accessed=2 * near * rows * width,
            transcendentals=0,
        ),
    )(
        core,
        d_own,
        d_other,
        *kept_rows,
        head_w,
        kv_w,
        cosine,
        sine,
        doc[:, :, None],
        doc[:, None, :],
    )


def product_kernel(*refs):
    *operands, out_ref = refs
    count = len(operands) // 2
    total = 0.0
    for left_ref, right_ref in zip(operands[:count], operands[count:]):
        total += dot_tn(left_ref[0], right_ref[...])
    out_ref[0] = total


def column_products(lefts, rights, tile=512):
    count, _, height = lefts[0].shape
    width = rights[0].shape[1]
    return pl.pallas_call(
        product_kernel,
        grid=(width // tile, count),
        in_specs=[
            *[pl.BlockSpec((1, v.shape[1], height), lambda j, i: (i, 0, 0)) for v in lefts],
            *[pl.BlockSpec((v.shape[0], tile), lambda j, i: (0, j)) for v in rights],
        ],
        out_specs=pl.BlockSpec((1, height, tile), lambda j, i: (i, 0, j)),
        out_shape=jax.ShapeDtypeStruct((count, height, width), jnp.float32),
        compiler_params=pltpu.CompilerParams(vmem_limit_bytes=58 * 1024 * 1024),
        cost_estimate=pl.CostEstimate(flops=width, bytes_accessed=width, transcendentals=0),
    )(*lefts, *rights)


def output_kernel(act, sact_own, sact_other, meta_own, meta_other, down_w, sdown_w, own_out, other_out):
    f32, bf16 = jnp.float32, jnp.bfloat16
    count, half, _ = meta_own.shape
    lane = lax.broadcasted_iota(jnp.int32, (2 * half, LANES), 1).astype(f32)
    out = dot_nn(act[...], down_w[...]).astype(bf16)
    for i in range(count):
        meta = jnp.concatenate([meta_own[i], meta_other[i]], axis=0)
        pick = (meta[:, :1] == lane).astype(bf16)
        sact = jnp.concatenate([sact_own[i], sact_other[i]], axis=0)
        here = slice(i * LANES, (i + 1) * LANES)
        rows = (dot_nn(pick, out[here]) + dot_nn(sact, sdown_w[...])).astype(bf16)
        own_out[i], other_out[i] = rows[:half], rows[half:]


def outputs(act, sact_own, sact_other, meta_own, meta_other, down_w, sdown_w, per_step=4):
    groups, half, _ = meta_own.shape
    hidden, width = down_w.shape
    lead, flat, whole = block_specs(per_step)
    return pl.pallas_call(
        output_kernel,
        grid=(groups // per_step,),
        in_specs=[
            flat(hidden),
            *[lead(half, LANES)] * 4,
            *[whole(a) for a in (down_w, sdown_w)],
        ],
        out_specs=[lead(half, width)] * 2,
        out_shape=[jax.ShapeDtypeStruct((groups, half, width), jnp.bfloat16)] * 2,
        compiler_params=pltpu.CompilerParams(vmem_limit_bytes=58 * 1024 * 1024),
        cost_estimate=pl.CostEstimate(
            flops=groups * half * LANES * width,
            bytes_accessed=groups * half * width,
            transcendentals=0,
        ),
    )(act, sact_own, sact_other, meta_own, meta_other, down_w, sdown_w)


def token_plan(
    inputs,
    attn_gain,
    w_query,
    w_latent,
    latent_gain,
    w_kv,
    w_out,
    ffn_gain,
    w_router,
    shared_gate_up,
    shared_down,
    expert_gate_up,
    expert_down,
    lengths,
    routes,
    cotangent,
):
    f32, bf16 = jnp.float32, jnp.bfloat16
    core, me = lax.axis_index("tensor"), lax.axis_index("expert")
    groups = lax.axis_size("expert")
    deep, place, z = groups // PLANE, me % PLANE, me // PLANE
    tok_rows, width = inputs.shape
    half = tok_rows // 2
    own_at, other_at = core * half, (1 - core) * half
    expert_count = w_router.shape[1]
    route_count = routes.shape[1]
    capacity = tok_rows * route_count * 4 // (3 * expert_count)
    shared_cols = shared_gate_up.shape[2] // groups
    latent_cols, rank_width = w_latent.shape[1], latent_gain.shape[0] * groups
    block_rows = w_query.shape[0]
    kv_rows = w_kv.shape[0]

    query_cols = w_query.shape[1] // PLANE
    out_cols = w_out.shape[0] // PLANE
    small = jnp.concatenate(
        [
            w_latent,
            w_latent[:, rank_width:],
            w_router,
            attn_gain[:, None],
            ffn_gain[:, None],
            jnp.pad(latent_gain, (0, block_rows - kv_rows))[:, None],
        ],
        axis=1,
    )
    small_cols = small.shape[1]
    route_half = take_rows(routes, own_at, half).astype(bf16).reshape(block_rows // 2, -1)
    length_col = jnp.pad(lengths[0].astype(bf16), (0, block_rows // 2 - lengths.shape[1]))[:, None]
    route_cols = route_half.shape[1] + 1
    small_half = jnp.concatenate(
        [
            take_rows(small, core * (block_rows // 2), block_rows // 2),
            route_half,
            length_col,
            jnp.zeros((block_rows // 2, -(small_cols + route_cols) % (2 * LANES)), bf16),
        ],
        axis=1,
    )
    packed_cols = small_half.shape[1] // 2
    small_packed = jnp.concatenate([small_half[:, :packed_cols], small_half[:, packed_cols:]])
    kv_cols = w_kv.shape[1] // PLANE
    kv_parts = block_rows // kv_rows
    kv_piece = kv_cols // kv_parts
    w_out_t = w_out.T

    local_heads = query_cols // (DN + DR)

    def by_parts(block):
        heads = [block[:, h * (DN + DR) : (h + 1) * (DN + DR)] for h in range(local_heads)]
        return [h[:, :DN] for h in heads] + [h[:, DN:] for h in heads]

    def quarter(index):
        kv_here = take_rows(w_kv, index * kv_cols, kv_cols, axis=1)
        kv_here = [kv_here[:, p * kv_piece : (p + 1) * kv_piece] for p in range(kv_parts)]
        return jnp.concatenate(
            [
                *by_parts(take_rows(w_query, index * query_cols, query_cols, axis=1)),
                take_rows(w_out_t, index * out_cols, out_cols, axis=1),
                jnp.concatenate(kv_here, axis=0),
            ],
            axis=1,
        )

    near_w = [quarter(place)] + [to_partner(quarter(place ^ r), r) for r in range(1, PLANE)]
    small_line = deep_join(small_packed, deep_pieces(small_packed), z)
    near_w, small_line = tie(near_w, small_line)
    plane_w = jnp.stack(by_place(near_w, place))
    small_sent, x_sent, plane_w = tie(
        small_line.swapaxes(0, 1), take_rows(inputs, own_at, half), plane_w
    )
    small_sent = jnp.stack([small_sent, to_partner(small_sent, 1)])
    small_sent = jnp.concatenate([small_sent, to_partner(small_sent, 2)], axis=0)
    x_sent = jnp.stack([x_sent, to_partner(x_sent, 2)])
    x_came = to_partner(x_sent, 1)
    x_near_own = jnp.stack([x_sent[0], x_came[0], x_sent[1], x_came[1]])
    x_near_other = swap_cores(x_near_own)
    deep_w = deep_hops(plane_w)
    small_parts = [small_sent[r].swapaxes(0, 1) for r in range(PLANE)]
    small_own = jnp.stack(by_place(small_parts, place), axis=1)
    small_own = small_own.reshape(groups, block_rows, packed_cols)
    small_own = jnp.concatenate(
        [small_own[:, : block_rows // 2], small_own[:, block_rows // 2 :]], axis=2
    )
    small_other = swap_cores(small_own)
    small_all = in_order(core, small_own, small_other, axis=1)
    small_all, x_near_other, deep_w = tie(small_all, x_near_other, deep_w)
    head_w = deep_join(plane_w, join_hops(deep_w), z)
    length_at = small_cols + route_cols - 1
    lengths_near = take_rows(small_own, z * PLANE, PLANE)[:, : lengths.shape[1], length_at]
    lengths_near = lengths_near.astype(jnp.int32)
    lengths_near = jnp.stack(by_place([lengths_near[r] for r in range(PLANE)], place))
    shared_rows = jnp.concatenate(
        [shared_gate_up[0].T, shared_gate_up[1].T, shared_down], axis=0
    ).reshape(3, groups, shared_cols, block_rows)
    shared_rows = shared_rows.swapaxes(0, 1).reshape(groups, 3 * shared_cols, block_rows)
    dy_sent, head_w = tie(take_rows(cotangent, own_at, half), head_w)
    dy_own_rows = take_rows(cotangent, own_at, half)
    dy_gather = RowGather(dy_sent)
    dy_came = dy_gather.along()
    head_w = head_w.reshape(groups, block_rows, -1)
    flat_head = head_w.reshape(groups * block_rows, -1)
    at = query_cols + out_cols
    kv_w = head_w[:, :, at : at + kv_piece].reshape(groups, kv_parts, kv_rows, kv_piece)
    kv_w = kv_w.transpose(0, 2, 1, 3).reshape(groups * kv_rows, kv_cols)

    block_index = jnp.arange(groups)
    block_chip = (z - block_index % deep) % deep * PLANE + (place ^ (block_index // deep))
    in_blocks = (block_chip[:, None] == block_index[None, :]).astype(bf16)

    def routes_of(came):
        came = came[:, :, small_cols : small_cols + route_half.shape[1]].reshape(groups, -1)
        came = jnp.dot(in_blocks, came, preferred_element_type=f32)
        return came.astype(jnp.int32).reshape(groups, half, route_count)

    routes_own, routes_other = routes_of(small_own), routes_of(small_other)
    flat_small = small_all.reshape(groups * block_rows, -1)
    latent_w = flat_small[:, :latent_cols]
    at = rank_width + LANES
    router_w = flat_small[:, at : at + expert_count]
    at += expert_count
    gain_one, gain_two = flat_small[:, at], flat_small[:, at + 1]
    latent_g = small_all[:, :kv_rows, at + 2].reshape(-1)

    near_rows = PLANE * tok_rows
    relative, doc = jax.vmap(lambda one: doc_places(one, tok_rows))(lengths_near)
    cosine, sine_tab = rope_tables(relative.reshape(-1), DR)
    cosine, sine_tab = [v.reshape(PLANE, tok_rows, -1) for v in (cosine, sine_tab)]
    rope = (
        jnp.concatenate([cosine] * 4, axis=-1),
        jnp.concatenate([-sine_tab, sine_tab] * 2, axis=-1),
        doc.astype(f32),
    )
    core_index = core.reshape(1).astype(jnp.int32)
    *kept_rows, latent, part_own, part_other = attention(
        core_index,
        x_near_own,
        x_near_other,
        gain_one.astype(f32)[None],
        latent_g.astype(f32)[None],
        flat_head,
        flat_small,
        kv_w,
        *rope,
    )
    normed_b = kept_rows[0].reshape(near_rows, width)

    def sum_cores(own, other):
        return add_wide(own, swap_cores(other)).astype(bf16)

    def sum_plane(both):
        return plane_scatter([both[r] for r in range(PLANE)])

    part_own, part_other, dy_came = tie(part_own, part_other, dy_came)
    attn_own = sum_plane(sum_cores(part_own, part_other))
    x_own = take_rows(inputs, own_at, half).astype(f32)
    hidden = x_own + attn_own
    hnormed, scale_two = rms_forward(hidden, gain_two.astype(f32))
    hnormed_b = hnormed.astype(bf16)
    normed_cols = jnp.concatenate(
        [
            take_rows(normed_b, (k * PLANE + place) * block_rows, block_rows, axis=1)
            for k in range(deep)
        ],
        axis=1,
    )
    hnormed_b, normed_cols, shared_rows, routes_own, routes_other = tie(
        hnormed_b, normed_cols, shared_rows, routes_own, routes_other
    )
    dy_lines = dy_gather.lines(dy_came)
    def membership(named):
        one_hot = named[..., None] == jnp.arange(expert_count, dtype=jnp.int32)
        return jnp.any(named == me, axis=-1), jnp.any(one_hot, axis=2)

    member_own, hot_own = membership(routes_own)
    member_other, hot_other = membership(routes_other)
    lower = (
        jnp.arange(half, dtype=jnp.int32)[:, None] <= jnp.arange(half, dtype=jnp.int32)[None, :]
    ).astype(bf16)

    def running(mask):
        counts = jnp.dot(mask.astype(bf16), lower, preferred_element_type=f32)
        return counts.astype(jnp.int32)

    count_own, count_other = running(member_own), running(member_other)
    place_own = jnp.where(member_own, count_own - 1, -1)
    place_other = jnp.where(member_other, count_own[:, -1:] + count_other - 1, -1)

    def metadata(slot, hot):
        return jnp.concatenate(
            [
                slot[..., None].astype(f32),
                jnp.zeros((groups, half, shared_cols - 1), f32),
                hot.astype(f32),
                jnp.zeros((groups, half, LANES - shared_cols - expert_count), f32),
            ],
            axis=-1,
        )

    meta_own, meta_other = metadata(place_own, hot_own), metadata(place_other, hot_other)
    hn_gather = RowGather(hnormed_b)
    hn_came, dy_over, meta_own, meta_other = tie(
        hn_gather.along(), dy_gather.over(dy_lines), meta_own, meta_other
    )
    hn_lines, dy_over, shared_rows = tie(hn_gather.lines(hn_came), dy_over, shared_rows)
    shared_w = lax.all_to_all(shared_rows, "expert", split_axis=0, concat_axis=0, tiled=True)
    dy_line = jnp.concatenate(dy_lines, axis=1)
    hn_line = jnp.concatenate(hn_lines, axis=1)
    hn_over, dy_again, hn_line_other, dy_line_other, shared_w = tie(
        hn_gather.over(hn_lines),
        dy_gather.over_again(dy_over),
        swap_cores(hn_line),
        swap_cores(dy_line),
        shared_w,
    )
    shared_w = shared_w.swapaxes(0, 1).reshape(3 * shared_cols, groups * block_rows)
    first_w = jnp.concatenate(
        [
            shared_w[:shared_cols],
            router_w.T,
            jnp.zeros((LANES - shared_cols - expert_count, width), bf16),
            shared_w[shared_cols : 2 * shared_cols],
            jnp.zeros((LANES - shared_cols, width), bf16),
        ],
        axis=0,
    )
    sdown_rows = jnp.pad(shared_w[2 * shared_cols :], ((0, LANES - shared_cols), (0, 0)))
    gate_up_w, down_w = jnp.swapaxes(expert_gate_up[0], 1, 2), expert_down[0]

    def run_experts(which, hn_part, hn_part_other):
        at, to = which[0] * deep, (which[-1] + 1) * deep
        return experts(
            me.reshape(1).astype(jnp.int32),
            hn_part,
            hn_part_other,
            *dy_parts[which],
            meta_own[at:to],
            meta_other[at:to],
            gate_up_w,
            down_w,
            first_w,
            sdown_rows,
            shared_cols,
            expert_count,
        )

    parts = ((0,), (1, 2), (3,))
    dy_parts = {parts[0]: (dy_line, dy_line_other)}
    hn_other_way, dy_other_way, done_line = tie(
        hn_gather.over_other(hn_lines),
        dy_gather.over_other(dy_lines),
        run_experts(parts[0], hn_line, hn_line_other),
    )
    dy_mine = [blocks_of(dy_lines, dy_over, dy_other_way, dy_again, p) for p in parts[1:]]
    dy_parts.update((p, (v, swap_cores(v))) for p, v in zip(parts[1:], dy_mine))
    d_line_came = swap_cores(done_line[5])
    hn_near = blocks_of(hn_lines, hn_over, hn_other_way, None, parts[1])
    hn_again, done_near = tie(
        hn_gather.over_again(hn_over), run_experts(parts[1], hn_near, swap_cores(hn_near))
    )
    d_near_came = swap_cores(done_near[5])
    hn_far = blocks_of(hn_lines, hn_over, hn_other_way, hn_again, parts[2])
    done_far = run_experts(parts[2], hn_far, swap_cores(hn_far))
    done = (done_line, done_near, done_far)
    slot_rows, slot_dy, slot_act, d_gate_up = [[v[i] for v in done] for i in range(4)]
    shared_grads = add_wide(*[v[8] for v in done])

    def by_flips(line, near, far):
        return [line, near[:deep], near[deep:], far]

    d_rows_own = by_flips(*[v[4] for v in done])
    d_rows_came = by_flips(d_line_came, d_near_came, swap_cores(done_far[5]))

    def two_parts(value):
        return value[..., 0] + value[..., 1]

    dgate_own, dgate_other = [
        jnp.concatenate([two_parts(v[i]) for v in done], axis=0) for i in (9, 10)
    ]
    dgate_sent = dgate_own + swap_cores(dgate_other)
    dgate_high = dgate_sent.astype(bf16)
    dgate_low = (dgate_sent - dgate_high.astype(f32)).astype(bf16)
    d_rows_came, dgate_high, dgate_low = tie(d_rows_came, dgate_high, dgate_low)
    d_sum = RowSum(d_rows_own, d_rows_came)
    sends, shared_grads, slot_act = tie(d_sum.sends(), shared_grads, slot_act)
    came = d_sum.move(sends)
    gate_rows = jnp.stack([contract_rows(in_blocks, v).reshape(-1) for v in (dgate_high, dgate_low)])
    grads_sent = jnp.concatenate([shared_grads, gate_rows], axis=0).astype(bf16)
    grads_sent = grads_sent.reshape(-1, groups, block_rows)
    grads_came = lax.all_to_all(grads_sent, "expert", split_axis=1, concat_axis=1, tiled=True)
    out_done = [
        outputs(
            act,
            v[6],
            v[7],
            meta_own[p[0] * deep : (p[-1] + 1) * deep],
            meta_other[p[0] * deep : (p[-1] + 1) * deep],
            down_w,
            sdown_rows,
        )
        for act, v, p in zip(slot_act, done, parts)
    ]
    edown_grad = column_products([v[None] for v in slot_act], slot_dy)[0]
    came, out_done, edown_grad, grads_came = tie(came, out_done, edown_grad, grads_came)
    dgate = add_wide(grads_came[3 * shared_cols], grads_came[3 * shared_cols + 1]).T
    sends, slot_rows, out_done = tie(d_sum.sends_again(came), slot_rows, out_done)
    came_again = d_sum.move_again(sends)
    egu_grad = column_products(d_gate_up, slot_rows).swapaxes(1, 2)
    out_own = by_flips(*[v[0] for v in out_done])
    out_came = by_flips(*[swap_cores(v[1]) for v in out_done])
    out_sum = RowSum(out_own, out_came)
    out_sends = out_sum.sends()
    came_again, egu_grad, out_sends = tie(came_again, egu_grad, out_sends)
    z_sends, out_sends, dgate = tie(
        line_sends(d_sum.line(came, came_again)), out_sends, dgate
    )
    z_came = line_move(z_sends)
    out_first = out_sum.move(out_sends)
    hot_mine = take_rows(
        jnp.any(routes[..., None] == jnp.arange(expert_count, dtype=jnp.int32), axis=1), own_at, half
    )
    sig = jax.nn.sigmoid(jnp.dot(hnormed_b, router_w, preferred_element_type=f32))
    chosen = jnp.where(hot_mine, sig, 0.0)
    chosen_sum = jnp.sum(chosen, axis=1, keepdims=True)
    dgate = jnp.where(hot_mine, dgate, 0.0)
    inner = jnp.sum(dgate * chosen, axis=1, keepdims=True)
    d_chosen = ROUTE_SCALE * (dgate / chosen_sum - inner / (chosen_sum * chosen_sum))
    d_logits = (jnp.where(hot_mine, d_chosen, 0.0) * sig * (1.0 - sig)).astype(bf16)
    router_grad = contract_rows(d_logits, hnormed_b)
    z_came, d_logits, router_grad = tie(z_came, d_logits, router_grad)
    d_hn = add_wide(*z_came)
    d_hn = d_hn + contract_cols(d_logits, router_w)
    d_hidden_norm, gain_two_grad = rms_backward(hidden, scale_two, gain_two.astype(f32), d_hn)
    d_hidden = dy_own_rows.astype(f32) + d_hidden_norm
    d_parts, out_first = tie(plane_gather(d_hidden.astype(bf16)), out_first)
    d_near_own = jnp.stack(d_parts)
    d_near_other = swap_cores(d_near_own)
    out_sends, d_near_other = tie(out_sum.sends_again(out_first), d_near_other)
    out_second = out_sum.move_again(out_sends)

    (
        head_grad,
        kv_grad,
        normed_part_own,
        normed_part_other,
        latent_part_own,
        latent_part_other,
    ) = attention_backward(
        core_index, d_near_own, d_near_other, kept_rows, flat_head, kv_w, *rope
    )
    kv_grad = kv_grad.reshape(groups, kv_rows, kv_parts, kv_piece).transpose(0, 2, 1, 3)
    head_grad = jnp.concatenate([head_grad, kv_grad.reshape(-1, kv_piece)], axis=1)
    head_blocks = head_grad.reshape(deep, -1, head_grad.shape[1])
    head_hops = HopSum(lambda t: at_index(head_blocks, 0, t))
    came, latent_both, normed_both, out_second = tie(
        head_hops.hop(1),
        sum_cores(latent_part_own, latent_part_other),
        sum_cores(normed_part_own, normed_part_other),
        out_second,
    )
    out_line = out_sum.line(out_first, out_second)
    came, grad_both, out_line = tie(head_hops.hop(2, came), sum_plane(latent_both), out_line)
    grad_rope = grad_both[:, rank_width : rank_width + DR] + grad_both[:, rank_width + DR :]
    latent_own = take_rows(latent[0], own_at, half)
    cosine_own = take_rows(cosine[0], own_at, half)
    sine_own = take_rows(sine_tab[0], own_at, half)
    _, scale_kv = rms_forward(latent_own[:, :rank_width], latent_g.astype(f32))
    grad_c, latent_gain_grad = rms_backward(
        latent_own[:, :rank_width], scale_kv, latent_g.astype(f32), grad_both[:, :rank_width]
    )
    grad_latent = jnp.concatenate(
        [grad_c, unrotate(grad_rope, cosine_own, sine_own)], axis=-1
    ).astype(bf16)
    out_hops = HopSum(lambda t: at_index(out_line, 0, (z - t) % deep))
    came, latent_parts, grad_normed, out_z = tie(
        head_hops.hop(3, came), plane_gather(grad_latent), sum_plane(normed_both), out_hops.hop(1)
    )
    latent_near_own = jnp.stack(latent_parts)
    latent_near = in_order(core, latent_near_own, swap_cores(latent_near_own), axis=1)
    head_sums = head_hops.total(came).astype(bf16).reshape(PLANE, block_rows, -1)
    out_z, latent_near, head_shared, grads_came = tie(
        out_hops.hop(2, out_z), latent_near, share_columns(head_sums, place), grads_came
    )
    out_z = out_hops.hop(3, out_z)
    latent_cut = latent_cols // 2
    latent_near = latent_near.reshape(near_rows, latent_cols)
    latent_blocks = contract_rows(
        normed_cols,
        take_rows(latent_near, core * latent_cut, latent_cut, axis=1),
    )
    latent_half = deep_scatter(latent_blocks.astype(bf16).reshape(deep, -1, latent_cut), z)
    w_latent_grad = in_order(core, latent_half, swap_cores(latent_half), axis=1)


    def by_heads(block):
        rotary = local_heads * DN
        return [
            part
            for h in range(local_heads)
            for part in (
                block[:, h * DN : (h + 1) * DN],
                block[:, rotary + h * DR : rotary + (h + 1) * DR],
            )
        ]

    at_kv = query_cols + out_cols
    w_query_grad = jnp.concatenate([v for p in head_shared for v in by_heads(p)], axis=1)
    w_query_grad = w_query_grad.astype(f32)
    w_kv_grad = jnp.concatenate(
        [
            p[q * kv_rows : (q + 1) * kv_rows, at_kv:]
            for p in head_shared
            for q in range(kv_parts)
        ],
        axis=1,
    ).astype(f32)
    w_out_grad = jnp.concatenate([p[:, query_cols:at_kv] for p in head_shared], axis=1)
    w_out_grad = w_out_grad.astype(f32).T
    sgu_out = grads_came[: 2 * shared_cols].astype(f32)
    sgu_out = sgu_out.reshape(2, shared_cols, groups, block_rows)
    sgu_out = sgu_out.transpose(0, 3, 2, 1).reshape(2, block_rows, -1)
    sdown_out = grads_came[2 * shared_cols : 3 * shared_cols].astype(f32).swapaxes(0, 1).reshape(-1, block_rows)
    grad_normed = grad_normed + contract_cols(grad_latent, latent_w)
    moe_own = out_hops.total(out_z)
    mixed_own = (hidden + moe_own).astype(bf16)
    mixed = in_order(core, mixed_own, swap_cores(mixed_own))

    _, scale_own = rms_forward(x_own, gain_one.astype(f32))
    grad_x_norm, gain_one_grad = rms_backward(x_own, scale_own, gain_one.astype(f32), grad_normed)
    input_own = d_hidden + grad_x_norm
    input_grad = in_order(core, input_own, swap_cores(input_own))

    gain_lanes = jnp.pad(
        latent_gain_grad.reshape(groups, kv_rows), ((0, 0), (0, block_rows - kv_rows))
    )
    vectors = jnp.concatenate(
        [
            router_grad,
            gain_one_grad[None],
            gain_two_grad[None],
            gain_lanes.reshape(1, -1),
        ],
        axis=0,
    ).reshape(-1, groups, block_rows)
    arrived = lax.all_to_all(vectors, "expert", split_axis=1, concat_axis=1, tiled=True)
    sums = jnp.sum(arrived, axis=1)
    sums = sums + swap_cores(sums)
    return (
        mixed,
        input_grad,
        sums[expert_count],
        w_query_grad,
        w_latent_grad,
        sums[expert_count + 2, :kv_rows],
        w_kv_grad,
        w_out_grad,
        sums[expert_count + 1],
        sums[:expert_count].T,
        sgu_out,
        sdown_out,
        egu_grad[None],
        edown_grad[None],
    )


def solution(mesh):
    groups = mesh.shape["expert"]
    plan = token_plan if groups <= 16 else weight_plan
    return jax.shard_map(
        plan,
        mesh=mesh,
        in_specs=(
            P("expert", None),
            P("expert"),
            P("expert", "tensor"),
            P("expert", None),
            P("expert"),
            P("expert", "tensor"),
            P("tensor", "expert"),
            P("expert"),
            P("expert", None),
            P(None, "expert", "tensor"),
            P("tensor", "expert"),
            P("expert", None, None, "tensor"),
            P("expert", "tensor", None),
            P("expert", None),
            P("expert", None),
            P("expert", None),
        ),
        out_specs=(
            P("expert", None),
            P("expert", None),
            P("expert"),
            P("expert", "tensor"),
            P("expert", None),
            P("expert"),
            P("expert", "tensor"),
            P("tensor", "expert"),
            P("expert"),
            P("expert", None),
            P(None, "expert", "tensor"),
            P("tensor", "expert"),
            P("expert", None, None, "tensor"),
            P("expert", "tensor", None),
        ),
        check_vma=False,
    )
```

```python
import functools

import jax
import jax.numpy as jnp
from jax import lax
from jax.experimental import pallas as pl
from jax.experimental.pallas import tpu as pltpu
from jax.sharding import PartitionSpec as P

DN = 128
DR = 64
DV = 128
LANES = 128


EPSILON = 1e-06
ROUTE_SCALE = 2.446
ROPE_BASE = 50000.0
NEGATIVE = -1e30


def cut_along(value, dim, length):
    before, after = (value.shape[:dim], value.shape[dim + 1 :])
    return jnp.moveaxis(value.reshape(*before, length, -1, *after), dim, 0)


def summed_on_arrival(value, axis, dim):
    length = lax.axis_size(axis)
    tiles = lax.all_to_all(cut_along(value, dim, length), axis, 0, 0, tiled=True)
    return jnp.sum(tiles.astype(jnp.float32), axis=0)


def sent_together(arrays, axis, dim, along):
    columns = [a.reshape(*a.shape[:along], -1) for a in arrays]
    both = jnp.concatenate(columns, axis=along)
    whole, at, outs = (summed_on_arrival(both, axis, dim), 0, [])
    for a, column in zip(arrays, columns):
        slab = whole[..., at : at + column.shape[along]]
        outs.append(slab.reshape(*slab.shape[:along], *a.shape[along:]))
        at += column.shape[along]
    return tuple(outs)


def contract_rows(left_arr, right_arr):
    return lax.dot_general(
        left_arr, right_arr, (((0,), (0,)), ((), ())), preferred_element_type=jnp.float32
    )


def contract_cols(left_arr, right_arr):
    return lax.dot_general(
        left_arr, right_arr, (((1,), (1,)), ((), ())), preferred_element_type=jnp.float32
    )


def rms_forward(rows_in, gain_vec):
    inverse = lax.rsqrt(jnp.mean(rows_in * rows_in, axis=-1, keepdims=True) + EPSILON)
    return (rows_in * inverse * gain_vec, inverse)


def rms_backward(rows_in, inverse, gain_vec, grad_out):
    gain_grad = jnp.sum(grad_out * rows_in * inverse, axis=0)
    weighted = grad_out * gain_vec
    inner_mean = jnp.mean(weighted * rows_in, axis=-1, keepdims=True)
    return (inverse * weighted - rows_in * inverse * inverse * inverse * inner_mean, gain_grad)


def doc_layout(doc_lengths, row_count):
    ends_at = jnp.cumsum(doc_lengths)
    starts_at = ends_at - doc_lengths
    position = jnp.arange(row_count, dtype=jnp.int32)
    doc_ids = jnp.sum((position[:, None] >= ends_at[None, :]).astype(jnp.int32), axis=1)
    hitting = doc_ids[:, None] == jnp.arange(doc_lengths.shape[0], dtype=jnp.int32)[None, :]
    start_of = jnp.sum(jnp.where(hitting, starts_at[None, :], 0), axis=1)
    relative = position - start_of
    visible = (doc_ids[:, None] == doc_ids[None, :]) & (position[:, None] >= position[None, :])
    return (relative, visible)


def rope_tables(relative, rot_width):
    counter = jnp.arange(rot_width // 2, dtype=jnp.float32)
    frequency = ROPE_BASE ** (-2.0 * counter / rot_width)
    angles = relative.astype(jnp.float32)[:, None] * frequency[None, :]
    return (jnp.cos(angles), jnp.sin(angles))


def rotate(tensor_in, cosine, sine_tab):
    half_width = tensor_in.shape[-1] // 2
    leading = tensor_in[..., :half_width]
    trailing = tensor_in[..., half_width:]
    return jnp.concatenate(
        [leading * cosine - trailing * sine_tab, trailing * cosine + leading * sine_tab], axis=-1
    )


def unrotate(grad_in, cosine, sine_tab):
    half_width = grad_in.shape[-1] // 2
    leading = grad_in[..., :half_width]
    trailing = grad_in[..., half_width:]
    return jnp.concatenate(
        [leading * cosine + trailing * sine_tab, trailing * cosine - leading * sine_tab], axis=-1
    )


def gated_linear_backward(gate_in, up_in, grad_act):
    sigmoid_g = jax.nn.sigmoid(gate_in)
    grad_gate = grad_act * up_in * sigmoid_g * (1.0 + gate_in * (1.0 - sigmoid_g))
    return (grad_gate, grad_act * gate_in * sigmoid_g)


def slot_tables(route_rows, expert_count, capacity):
    flat_routes = route_rows.reshape(-1)
    one_hot = (flat_routes[:, None] == jnp.arange(expert_count, dtype=jnp.int32)[None, :]).astype(
        jnp.int32
    )
    ranking = jnp.sum((jnp.cumsum(one_hot, axis=0) - one_hot) * one_hot, axis=1)
    slot_ids = flat_routes * capacity + ranking
    row_total = flat_routes.shape[0]
    source = (
        jnp.zeros((expert_count * capacity,), jnp.int32)
        .at[slot_ids]
        .set(jnp.arange(row_total, dtype=jnp.int32))
    )
    filled = jnp.zeros((expert_count * capacity,), jnp.int32).at[slot_ids].set(1)
    return (slot_ids, source, filled)


def to_owner(rows_in):
    arrived = lax.all_to_all(rows_in, "expert", split_axis=0, concat_axis=1, tiled=True)
    return arrived


def weight_plan(
    inputs,
    attn_gain,
    w_query,
    w_latent,
    latent_gain,
    w_kv,
    w_out,
    ffn_gain,
    w_router,
    shared_gate_up,
    shared_down,
    expert_gate_up,
    expert_down,
    lengths,
    routes,
    cotangent,
):
    tok_rows = inputs.shape[0]
    model_width = inputs.shape[1]
    expert_count = w_router.shape[1]
    route_count = routes.shape[1]
    capacity = tok_rows * route_count * 4 // (3 * expert_count)
    brain_float16 = jnp.bfloat16
    f32 = jnp.float32
    gathered = (
        lax.all_gather(attn_gain, "expert", axis=0, tiled=True),
        lax.all_gather(w_query, "expert", axis=0, tiled=True),
        lax.all_gather(w_latent, "expert", axis=0, tiled=True),
        lax.all_gather(latent_gain, "expert", axis=0, tiled=True),
        lax.all_gather(w_kv, "expert", axis=0, tiled=True),
        lax.all_gather(w_out, "expert", axis=1, tiled=True),
        lax.all_gather(ffn_gain, "expert", axis=0, tiled=True),
        lax.all_gather(w_router, "expert", axis=0, tiled=True),
        lax.all_gather(shared_gate_up, "expert", axis=1, tiled=True),
        lax.all_gather(shared_down, "expert", axis=1, tiled=True),
    )
    gain_one, query_w, latent_w, latent_g, kv_w, out_w, gain_two, router_w, sgate_up, sdown_w = (
        gathered
    )
    local_heads = query_w.shape[1] // (DN + DR)
    rank_width = latent_g.shape[0]
    x_float = inputs.astype(f32)
    relative, visible = doc_layout(lengths[0], tok_rows)
    cosine, sine_tab = rope_tables(relative, DR)
    q_scale = (DN + DR) ** (-0.5)
    normed, scale_one = rms_forward(x_float, gain_one.astype(f32))
    normed_b = normed.astype(brain_float16)
    queries = jnp.dot(normed_b, query_w, preferred_element_type=f32).reshape(
        tok_rows, local_heads, DN + DR
    )
    q_rot = rotate(queries[..., DN:], cosine[:, None, :], sine_tab[:, None, :])
    q_all = jnp.concatenate([queries[..., :DN], q_rot], axis=-1).astype(brain_float16)
    latent = jnp.dot(normed_b, latent_w, preferred_element_type=f32)
    compressed, scale_kv = rms_forward(latent[:, :rank_width], latent_g.astype(f32))
    compressed_b = compressed.astype(brain_float16)
    k_rope = rotate(latent[:, rank_width:], cosine, sine_tab).astype(brain_float16)
    kv_all = jnp.dot(compressed_b, kv_w, preferred_element_type=f32).reshape(
        tok_rows, local_heads, DN + DV
    )
    k_nope = kv_all[..., :DN].astype(brain_float16)
    values = kv_all[..., DN:].astype(brain_float16)
    key_all = jnp.concatenate(
        [k_nope, jnp.broadcast_to(k_rope[:, None, :], (tok_rows, local_heads, DR))], axis=-1
    )

    def score_block():
        raw_scores = (
            jnp.einsum("qhd,khd->hqk", q_all, key_all, preferred_element_type=f32) * q_scale
        )
        return jnp.where(visible[None], raw_scores, NEGATIVE)

    scores = score_block()
    top_score = jnp.max(scores, axis=-1, keepdims=True)
    log_total = top_score + jnp.log(jnp.sum(jnp.exp(scores - top_score), axis=-1, keepdims=True))
    probs_b = jnp.exp(scores - log_total).astype(brain_float16)
    attended = jnp.einsum("hqk,khd->qhd", probs_b, values, preferred_element_type=f32)
    attended_b = attended.reshape(tok_rows, local_heads * DV).astype(brain_float16)
    attn = lax.psum(jnp.dot(attended_b, out_w, preferred_element_type=f32), "tensor")
    hidden = x_float + attn
    hnormed, scale_two = rms_forward(hidden, gain_two.astype(f32))
    hnormed_b = hnormed.astype(brain_float16)
    logits = jnp.dot(hnormed_b, router_w, preferred_element_type=f32)
    sigmoid_vals = jax.nn.sigmoid(logits)
    route_hot = routes[:, :, None] == jnp.arange(expert_count, dtype=jnp.int32)[None, None, :]
    chosen = jnp.sum(jnp.where(route_hot, sigmoid_vals[:, None, :], 0.0), axis=2)
    chosen_sum = jnp.sum(chosen, axis=1, keepdims=True)
    gate_vals = ROUTE_SCALE * chosen / chosen_sum
    slot_ids, source, filled = slot_tables(routes, expert_count, capacity)
    is_filled = filled[:, None] == 1
    sent_rows = jnp.where(is_filled, hnormed_b[source // route_count], 0).reshape(
        expert_count, capacity, model_width
    )
    received = to_owner(sent_rows)
    gate_up_joined = jnp.einsum(
        "erd,egdf->egrf", received, expert_gate_up, preferred_element_type=f32
    )
    expert_act = (jax.nn.silu(gate_up_joined[:, 0]) * gate_up_joined[:, 1]).astype(brain_float16)
    expert_res = jnp.einsum(
        "erf,efd->erd", expert_act, expert_down, preferred_element_type=f32
    ).astype(brain_float16)
    returned_all = lax.all_to_all(expert_res, "expert", split_axis=1, concat_axis=0, tiled=True)
    returned = returned_all.reshape(expert_count * capacity, model_width)[slot_ids].reshape(
        tok_rows, route_count, model_width
    )
    shared_gu = jnp.einsum("td,gdf->gtf", hnormed_b, sgate_up, preferred_element_type=f32)
    shared_act = (jax.nn.silu(shared_gu[0]) * shared_gu[1]).astype(brain_float16)
    branch_sum = jnp.dot(shared_act, sdown_w, preferred_element_type=f32)
    for route_idx in range(route_count):
        branch_sum = branch_sum + gate_vals[:, route_idx : route_idx + 1] * returned[
            :, route_idx
        ].astype(f32)
    moe_out = lax.psum(branch_sum.astype(jnp.bfloat16), "tensor").astype(jnp.float32)
    mixed = (hidden + moe_out).astype(brain_float16)
    grad_y = cotangent.astype(f32)
    sdown_grad = contract_rows(shared_act, cotangent)
    grad_sact = contract_cols(cotangent, sdown_w)
    grad_sgate, grad_sup = gated_linear_backward(shared_gu[0], shared_gu[1], grad_sact)
    grad_sgu = jnp.stack([grad_sgate, grad_sup], axis=0).astype(brain_float16)
    sgu_grad = jnp.einsum("td,gtf->gdf", hnormed_b, grad_sgu, preferred_element_type=f32)
    grad_hn_part = jnp.einsum("gtf,gdf->td", grad_sgu, sgate_up, preferred_element_type=f32)
    gate_columns = []
    for route_idx in range(route_count):
        gate_columns.append(jnp.sum(grad_y * returned[:, route_idx].astype(f32), axis=1))
    gate_part = jnp.stack(gate_columns, axis=1)
    slot_grads = (
        (gate_vals[:, :, None] * grad_y[:, None, :])
        .reshape(tok_rows * route_count, model_width)
        .astype(brain_float16)
    )
    grad_sent = jnp.where(is_filled, slot_grads[source], 0).reshape(
        expert_count, capacity, model_width
    )
    grad_received = to_owner(grad_sent)
    edown_grad = jnp.einsum("erf,erd->efd", expert_act, grad_received, preferred_element_type=f32)
    expert_activation_gradient = jnp.einsum(
        "erd,efd->erf", grad_received, expert_down, preferred_element_type=f32
    )
    expert_gate_gradient, expert_up_gradient = gated_linear_backward(
        gate_up_joined[:, 0], gate_up_joined[:, 1], expert_activation_gradient
    )
    expert_gate_up_gradient = jnp.stack([expert_gate_gradient, expert_up_gradient], axis=1).astype(
        brain_float16
    )
    egu_grad = jnp.einsum(
        "erd,egrf->egdf", received, expert_gate_up_gradient, preferred_element_type=f32
    )
    grad_rows = jnp.einsum(
        "egrf,egdf->erd", expert_gate_up_gradient, expert_gate_up, preferred_element_type=f32
    ).astype(brain_float16)
    grad_back = lax.all_to_all(grad_rows, "expert", split_axis=1, concat_axis=0, tiled=True)
    grad_routes = grad_back.reshape(expert_count * capacity, model_width)[slot_ids].reshape(
        tok_rows, route_count, model_width
    )
    for route_idx in range(route_count):
        grad_hn_part = grad_hn_part + grad_routes[:, route_idx].astype(f32)
    gate_grads = lax.psum(gate_part, "tensor")
    grad_chosen = ROUTE_SCALE * (
        gate_grads / chosen_sum
        - jnp.sum(gate_grads * chosen, axis=1, keepdims=True) / (chosen_sum * chosen_sum)
    )
    grad_sig = jnp.sum(jnp.where(route_hot, grad_chosen[:, :, None], 0.0), axis=1)
    grad_logits = (grad_sig * sigmoid_vals * (1.0 - sigmoid_vals)).astype(brain_float16)
    router_grad = contract_rows(hnormed_b, grad_logits)
    grad_hn = lax.psum(grad_hn_part, "tensor") + contract_cols(grad_logits, router_w)
    grad_hidden_norm, gain_two_grad = rms_backward(hidden, scale_two, gain_two.astype(f32), grad_hn)
    grad_hidden = grad_y + grad_hidden_norm
    grad_hidden_b = grad_hidden.astype(brain_float16)
    out_grad = contract_rows(attended_b, grad_hidden_b)
    grad_att = (
        contract_cols(grad_hidden_b, out_w).reshape(tok_rows, local_heads, DV).astype(brain_float16)
    )
    probs = jnp.exp(score_block() - log_total)
    probs_again = probs.astype(brain_float16)
    grad_probs = jnp.einsum("qhd,khd->hqk", grad_att, values, preferred_element_type=f32)
    grad_vals = jnp.einsum("hqk,qhd->khd", probs_again, grad_att, preferred_element_type=f32)
    row_delta = jnp.sum(probs * grad_probs, axis=-1, keepdims=True)
    grad_scores = (probs * (grad_probs - row_delta)).astype(brain_float16)
    grad_q = jnp.einsum("hqk,khd->qhd", grad_scores, key_all, preferred_element_type=f32) * q_scale
    grad_keys = jnp.einsum("hqk,qhd->khd", grad_scores, q_all, preferred_element_type=f32) * q_scale
    grad_kv = (
        jnp.concatenate([grad_keys[..., :DN], grad_vals], axis=-1)
        .reshape(tok_rows, local_heads * (DN + DV))
        .astype(brain_float16)
    )
    kv_grad = contract_rows(compressed_b, grad_kv)
    grad_comp_part = contract_cols(grad_kv, kv_w)
    grad_krope_part = jnp.sum(grad_keys[..., DN:], axis=1)
    grad_comp, grad_krope = (
        lax.psum(grad_comp_part.astype(jnp.bfloat16), "tensor").astype(jnp.float32),
        lax.psum(grad_krope_part.astype(jnp.bfloat16), "tensor").astype(jnp.float32),
    )
    grad_c, latent_gain_grad = rms_backward(
        latent[:, :rank_width], scale_kv, latent_g.astype(f32), grad_comp
    )
    grad_latent = jnp.concatenate([grad_c, unrotate(grad_krope, cosine, sine_tab)], axis=-1).astype(
        brain_float16
    )
    grad_qrot = unrotate(grad_q[..., DN:], cosine[:, None, :], sine_tab[:, None, :])
    grad_queries = (
        jnp.concatenate([grad_q[..., :DN], grad_qrot], axis=-1)
        .reshape(tok_rows, local_heads * (DN + DR))
        .astype(brain_float16)
    )
    query_grad = contract_rows(normed_b, grad_queries)
    latent_grad = contract_rows(normed_b, grad_latent)
    grad_normed = lax.psum(
        contract_cols(grad_queries, query_w).astype(jnp.bfloat16), "tensor"
    ).astype(jnp.float32) + contract_cols(grad_latent, latent_w)
    grad_x_norm, gain_one_grad = rms_backward(x_float, scale_one, gain_one.astype(f32), grad_normed)
    input_grad = grad_hidden + grad_x_norm
    first_owned = (
        *sent_together(
            (
                gain_one_grad.astype(jnp.bfloat16),
                query_grad.astype(jnp.bfloat16),
                latent_grad.astype(jnp.bfloat16),
            ),
            "expert",
            0,
            1,
        ),
        *sent_together(
            (latent_gain_grad.astype(jnp.bfloat16), kv_grad.astype(jnp.bfloat16)), "expert", 0, 1
        ),
    )
    second_owned = (
        lax.psum_scatter(out_grad, "expert", scatter_dimension=1, tiled=True),
        lax.psum_scatter(gain_two_grad, "expert", scatter_dimension=0, tiled=True),
        lax.psum_scatter(router_grad, "expert", scatter_dimension=0, tiled=True),
        lax.psum_scatter(sgu_grad, "expert", scatter_dimension=1, tiled=True),
        lax.psum_scatter(sdown_grad, "expert", scatter_dimension=1, tiled=True),
    )
    return (
        mixed,
        input_grad,
        first_owned[0],
        first_owned[1],
        first_owned[2],
        first_owned[3],
        first_owned[4],
        second_owned[0],
        second_owned[1],
        second_owned[2],
        second_owned[3],
        second_owned[4],
        egu_grad,
        edown_grad,
    )


def swap_cores(value):
    return lax.ppermute(value, "tensor", [(0, 1), (1, 0)])


def take_rows(value, start, count, axis=0):
    return lax.dynamic_slice_in_dim(value, start, count, axis=axis)


def in_order(core, own, other, axis=0):
    return jnp.where(
        core == 0,
        jnp.concatenate([own, other], axis=axis),
        jnp.concatenate([other, own], axis=axis),
    )


def add_wide(*parts):
    total = parts[0].astype(jnp.float32)
    for part in parts[1:]:
        total = total + part.astype(jnp.float32)
    return total


PLANE = 4


def to_partner(value, flips):
    groups = lax.axis_size("expert")
    return lax.ppermute(value, "expert", [(g, g ^ flips) for g in range(groups)])


def to_deeper(value, step):
    groups = lax.axis_size("expert")
    pairs = [(g, (g + step * PLANE) % groups) for g in range(groups)]
    return lax.ppermute(value, "expert", pairs)


def plane_gather(value):
    return [value] + [to_partner(value, r) for r in range(1, PLANE)]


def plane_scatter(parts):
    return add_wide(parts[0], *[to_partner(parts[r], r) for r in range(1, PLANE)])


def by_place(parts, place):
    odd, high = place % 2 == 1, place // 2 == 1
    parts = [jnp.where(odd, parts[i ^ 1], parts[i]) for i in range(PLANE)]
    return [jnp.where(high, parts[i ^ 2], parts[i]) for i in range(PLANE)]


def tie(*values):
    return lax.optimization_barrier(values)


def deep_pieces(value):
    deep = lax.axis_size("expert") // PLANE
    return [to_deeper(value, s) for s in range(1, deep)]


def one_plane(value, step):
    groups = lax.axis_size("expert")
    pairs = [(g, g + step * PLANE) for g in range(groups) if 0 <= g + step * PLANE < groups]
    return lax.ppermute(value, "expert", pairs)


def deep_hops(value):
    deep = lax.axis_size("expert") // PLANE
    after, before, down, up = [], [], value, value
    for _ in range(1, deep):
        down, up = one_plane(down, 1), one_plane(up, -1)
        after.append(down)
        before.append(up)
    return after, before


def join_hops(hops):
    after, before = hops
    return [a + b for a, b in zip(after, before[::-1])]


def deep_join(value, pieces, z):
    deep = lax.axis_size("expert") // PLANE
    whole = jnp.zeros((deep, *value.shape), value.dtype)
    whole = lax.dynamic_update_index_in_dim(whole, value, z, 0)
    for step in range(1, deep):
        whole = lax.dynamic_update_index_in_dim(whole, pieces[step - 1], (z - step) % deep, 0)
    return whole


def deep_move(blocks, z):
    deep = blocks.shape[0]

    def block(index):
        return lax.dynamic_index_in_dim(blocks, index, 0, keepdims=False)

    return [block(z)] + [to_deeper(block((z + step) % deep), step) for step in range(1, deep)]


def deep_scatter(blocks, z):
    return add_wide(*deep_move(blocks, z))


def share_columns(rows, place):
    parts = [at_index(rows, 0, place)]
    for r in range(1, PLANE):
        parts.append(to_partner(at_index(rows, 0, place ^ r), r))
    return by_place(parts, place)


def all_groups(value):
    return lax.all_gather(value, "expert", axis=0, tiled=False)


def at_index(value, axis, index):
    return lax.dynamic_index_in_dim(value, index, axis, keepdims=False)


def doc_places(doc_lengths, row_count):
    ends_at = jnp.cumsum(doc_lengths)
    position = jnp.arange(row_count, dtype=jnp.int32)
    doc_ids = jnp.sum((position[:, None] >= ends_at[None, :]).astype(jnp.int32), axis=1)
    hitting = doc_ids[:, None] == jnp.arange(doc_lengths.shape[0], dtype=jnp.int32)[None, :]
    start_of = jnp.sum(jnp.where(hitting, (ends_at - doc_lengths)[None, :], 0), axis=1)
    return position - start_of, doc_ids


class HopSum:
    def __init__(self, pieces):
        self.groups = lax.axis_size("expert")
        self.deep = self.groups // PLANE
        self.z = lax.axis_index("expert") // PLANE
        self.pieces = pieces

    def hop(self, step, came=None):
        arrived = []
        for side, way in enumerate((1, -1)):
            target = jnp.clip(self.z + way * (self.deep - step), 0, self.deep - 1)
            gone = self.pieces(target)
            if came is not None:
                gone = add_wide(gone, came[side]).astype(gone.dtype)
            first = range(step) if way == 1 else range(self.deep - step, self.deep)
            pairs = [
                (p * PLANE + q, (p + way) * PLANE + q) for p in first for q in range(PLANE)
            ]
            arrived.append(lax.ppermute(gone, "expert", pairs))
        return arrived

    def total(self, came):
        return add_wide(self.pieces(self.z), *came)


def doc_places(doc_lengths, row_count):
    ends_at = jnp.cumsum(doc_lengths)
    position = jnp.arange(row_count, dtype=jnp.int32)
    doc_ids = jnp.sum((position[:, None] >= ends_at[None, :]).astype(jnp.int32), axis=1)
    hitting = doc_ids[:, None] == jnp.arange(doc_lengths.shape[0], dtype=jnp.int32)[None, :]
    start_of = jnp.sum(jnp.where(hitting, (ends_at - doc_lengths)[None, :], 0), axis=1)
    return position - start_of, doc_ids


def hop_sum(pieces):
    groups = lax.axis_size("expert")
    deep = groups // PLANE
    z = lax.axis_index("expert") // PLANE
    ends = []
    for way in (1, -1):
        came = None
        for step in range(1, deep):
            gone = pieces(jnp.clip(z + way * (deep - step), 0, deep - 1))
            if came is not None:
                gone = add_wide(gone, came).astype(gone.dtype)
            first = range(step) if way == 1 else range(deep - step, deep)
            pairs = [
                (p * PLANE + q, (p + way) * PLANE + q) for p in first for q in range(PLANE)
            ]
            came = lax.ppermute(gone, "expert", pairs)
        ends.append(came)
    return [pieces(z), *ends]


class RowGather:
    def __init__(self, value):
        self.cut = value.shape[0] // 2
        self.value = value

    def along(self):
        return [self.value] + deep_pieces(self.value)

    def beside(self, line):
        return to_partner(line, 1), to_partner(line, 2)

    def far(self, beside):
        return to_partner(beside[0][:, : self.cut], 2), to_partner(beside[1][:, self.cut :], 1)


class RowSum:
    def __init__(self, *terms):
        self.type = terms[0][0].dtype
        cut = terms[0][0].shape[1] // 2
        self.halves = (
            ([[b[:, :cut] for b in v] for v in terms], 2, 1),
            ([[b[:, cut:] for b in v] for v in terms], 1, 2),
        )

    def _add(self, parts):
        return add_wide(*parts).astype(self.type)

    def sends(self):
        return [
            jnp.stack([self._add([v[far] for v in held]), self._add([v[far | near] for v in held])])
            for held, far, near in self.halves
        ]

    def move(self, sends):
        return [to_partner(v, far) for v, (_, far, _) in zip(sends, self.halves)]

    def sends_again(self, came):
        return [
            self._add([v[near] for v in held] + [c[1]])
            for c, (held, _, near) in zip(came, self.halves)
        ]

    def move_again(self, sends):
        return [to_partner(v, near) for v, (_, _, near) in zip(sends, self.halves)]

    def line(self, came, came_again):
        sums = [
            self._add([v[0] for v in held] + [c[0], d])
            for c, d, (held, *_) in zip(came, came_again, self.halves)
        ]
        return jnp.concatenate(sums, axis=1)


def line_sends(line):
    return [line[step] for step in range(line.shape[0])]


def line_move(sends):
    return [sends[0]] + [to_deeper(v, -step) for step, v in enumerate(sends) if step > 0]


def dot_nn(left, right):
    return lax.dot_general(left, right, (((1,), (0,)), ((), ())), preferred_element_type=jnp.float32)


def dot_nt(left, right):
    return lax.dot_general(left, right, (((1,), (1,)), ((), ())), preferred_element_type=jnp.float32)


def dot_tn(left, right):
    return lax.dot_general(left, right, (((0,), (0,)), ((), ())), preferred_element_type=jnp.float32)


def two_lanes(column, lane):
    high = column.astype(jnp.bfloat16).astype(jnp.float32)
    spread = jnp.where(lane == 0, high, jnp.where(lane == 1, column - high, 0.0))
    return spread.astype(jnp.bfloat16)


def expert_kernel(
    shared_cols,
    expert_count,
    me_ref,
    hn_own,
    hn_other,
    dy_own,
    dy_other,
    meta_own,
    meta_other,
    gate_up_w,
    down_w,
    first_w,
    sdown_w,
    slots_out,
    slot_dy_out,
    act_out,
    d_gate_up_out,
    rows_own_out,
    rows_other_out,
    sact_own_out,
    sact_other_out,
    shared_grads_out,
    dgate_own_out,
    dgate_other_out,
):
    f32, bf16 = jnp.float32, jnp.bfloat16
    count, half, _ = hn_own.shape
    tokens = 2 * half
    me = me_ref[0]
    lane = lax.broadcasted_iota(jnp.int32, (count * tokens, LANES), 1)
    is_router = (lane >= shared_cols) & (lane < shared_cols + expert_count)
    first = first_w[...]

    def joined(own, other):
        return jnp.concatenate([v[i] for i in range(count) for v in (own, other)], axis=0)

    rows, rows_dy = joined(hn_own, hn_other), joined(dy_own, dy_other)
    meta = joined(meta_own, meta_other)
    products = dot_nt(rows, first)
    gate, up = products[:, :LANES], products[:, LANES:]
    sig = jax.nn.sigmoid(gate)
    total = jnp.sum(jnp.where(is_router, sig * meta, 0.0), axis=1, keepdims=True)
    mine = jnp.sum(jnp.where(lane == shared_cols + me, sig, 0.0), axis=1, keepdims=True)
    token_gate = two_lanes(ROUTE_SCALE * mine / total, lane)
    sact = (gate * sig * up).astype(bf16)
    d_sact = dot_nt(rows_dy, sdown_w[...])
    d_sgate = d_sact * up * sig * (1.0 + gate * (1.0 - sig))
    dsh = jnp.concatenate([d_sgate, d_sact * gate * sig], axis=1).astype(bf16)
    pick = (meta[:, :1] == lane.astype(f32)).astype(bf16)
    groups = [slice(i * tokens, (i + 1) * tokens) for i in range(count)]
    for i in range(count):
        start = i * tokens
        sact_own_out[i] = sact[start : start + half]
        sact_other_out[i] = sact[start + half : start + tokens]
    slots = [dot_tn(pick[g], rows[g]).astype(bf16) for g in groups]
    slot_dys = [dot_tn(pick[g], rows_dy[g]).astype(bf16) for g in groups]
    slot_gates = [
        jnp.sum(dot_tn(pick[g], token_gate[g]), axis=1, keepdims=True) for g in groups
    ]

    @pl.when(pl.program_id(0) == 0)
    def _():
        shared_grads_out[...] = jnp.zeros_like(shared_grads_out)

    first_grad, sdown_grad = dot_tn(dsh, rows), dot_tn(sact, rows_dy)
    shared_grads_out[:shared_cols] += first_grad[:shared_cols]
    shared_grads_out[shared_cols : 2 * shared_cols] += first_grad[LANES : LANES + shared_cols]
    shared_grads_out[2 * shared_cols :] += sdown_grad[:shared_cols]
    slot_rows = jnp.concatenate(slots, axis=0)
    slot_dy = jnp.concatenate(slot_dys, axis=0)
    slot_gate = jnp.concatenate(slot_gates, axis=0)
    slots_out[...] = slot_rows
    slot_dy_out[...] = slot_dy
    gate = dot_nt(slot_rows, gate_up_w[0])
    up = dot_nt(slot_rows, gate_up_w[1])
    d_act = dot_nt(slot_dy, down_w[...])
    sig = jax.nn.sigmoid(gate)
    silu = gate * sig
    act = silu * up
    slot_dgate = jnp.sum(act * d_act, axis=1, keepdims=True)
    act_out[...] = (slot_gate * act).astype(bf16)
    d_act = slot_gate * d_act
    d_gate = (d_act * up * sig * (1.0 + gate * (1.0 - sig))).astype(bf16)
    d_up = (d_act * silu).astype(bf16)
    d_gate_up_out[0] = d_gate
    d_gate_up_out[1] = d_up
    d_slots = (dot_nn(d_gate, gate_up_w[0]) + dot_nn(d_up, gate_up_w[1])).astype(bf16)
    slot_lane = lax.broadcasted_iota(jnp.int32, (LANES, LANES), 1)
    d_shared = dot_nn(dsh, first)
    for i, g in enumerate(groups):
        here = slice(i * LANES, (i + 1) * LANES)
        d_rows = (dot_nn(pick[g], d_slots[here]) + d_shared[g]).astype(bf16)
        rows_own_out[i], rows_other_out[i] = d_rows[:half], d_rows[half:]
        dgate = dot_nn(pick[g], two_lanes(slot_dgate[here], slot_lane))
        dgate_own_out[i], dgate_other_out[i] = dgate[:half], dgate[half:]


def block_specs(per_step):
    def lead(*tail):
        return pl.BlockSpec((per_step, *tail), lambda i: (i,) + (0,) * len(tail))

    def flat(cols):
        return pl.BlockSpec((per_step * LANES, cols), lambda i: (i, 0))

    def whole(a):
        return pl.BlockSpec(a.shape, lambda i: (0,) * a.ndim, pipeline_mode=pl.Buffered(1))

    return lead, flat, whole


def experts(
    me,
    hn_own,
    hn_other,
    dy_own,
    dy_other,
    meta_own,
    meta_other,
    gate_up_w,
    down_w,
    first_w,
    sdown_w,
    shared_cols,
    expert_count,
    per_step=2,
):
    groups, half, width = hn_own.shape
    hidden = down_w.shape[0]
    slots = groups * LANES
    f32, bf16 = jnp.float32, jnp.bfloat16
    lead, flat, whole = block_specs(per_step)
    sds = jax.ShapeDtypeStruct
    return pl.pallas_call(
        functools.partial(expert_kernel, shared_cols, expert_count),
        grid=(groups // per_step,),
        in_specs=[
            pl.BlockSpec(memory_space=pltpu.SMEM),
            *[lead(half, width)] * 4,
            *[lead(half, LANES)] * 2,
            *[whole(a) for a in (gate_up_w, down_w, first_w, sdown_w)],
        ],
        out_specs=[
            flat(width),
            flat(width),
            flat(hidden),
            pl.BlockSpec((2, per_step * LANES, hidden), lambda i: (0, i, 0)),
            *[lead(half, width)] * 2,
            *[lead(half, LANES)] * 2,
            pl.BlockSpec((3 * shared_cols, width), lambda i: (0, 0)),
            *[lead(half, LANES)] * 2,
        ],
        out_shape=[
            sds((slots, width), bf16),
            sds((slots, width), bf16),
            sds((slots, hidden), bf16),
            sds((2, slots, hidden), bf16),
            *[sds((groups, half, width), bf16)] * 2,
            *[sds((groups, half, LANES), bf16)] * 2,
            sds((3 * shared_cols, width), f32),
            *[sds((groups, half, LANES), f32)] * 2,
        ],
        compiler_params=pltpu.CompilerParams(vmem_limit_bytes=58 * 1024 * 1024),
        cost_estimate=pl.CostEstimate(
            flops=groups * width, bytes_accessed=groups * width, transcendentals=0
        ),
    )(
        me,
        hn_own,
        hn_other,
        dy_own,
        dy_other,
        meta_own,
        meta_other,
        gate_up_w,
        down_w,
        first_w,
        sdown_w,
    )


def swap_halves(value, lane):
    low = lane % DR < DR // 2
    return jnp.where(low, pltpu.roll(value, LANES - DR // 2, 1), pltpu.roll(value, DR // 2, 1))


def by_core(core, first, second):
    return jnp.where(core == 0, first, second), jnp.where(core == 0, second, first)


def head_scores(q, kv, k_rope, visible, lane, head, heads):
    q_nope = q[:, head * DN : (head + 1) * DN]
    q_rope = jnp.where(lane // DR == head, q[:, heads * DN :], jnp.zeros((), q.dtype))
    at = head * (DN + DV)
    k_nope, value = kv[:, at : at + DN], kv[:, at + DN : at + DN + DV]
    scores = (dot_nt(q_nope, k_nope) + dot_nt(q_rope, k_rope)) * (DN + DR) ** -0.5
    return jnp.where(visible, scores, NEGATIVE), q_nope, q_rope, k_nope, value


def seen(doc_col, doc_row):
    rows = doc_col.shape[0]
    later = lax.broadcasted_iota(jnp.int32, (rows, rows), 0) >= lax.broadcasted_iota(
        jnp.int32, (rows, rows), 1
    )
    return (doc_col == doc_row) & later


def attention_kernel(
    heads,
    rank,
    core_ref,
    x_own,
    x_other,
    gain,
    latent_gain,
    head_w,
    small_w,
    kv_w,
    cosine,
    sine,
    doc_col,
    doc_row,
    normed_out,
    compressed_out,
    q_out,
    kv_out,
    k_rope_out,
    sums_out,
    attended_out,
    latent_out,
    part_own_out,
    part_other_out,
):
    f32, bf16 = jnp.float32, jnp.bfloat16
    core = core_ref[0]
    x = jnp.concatenate(by_core(core, x_own[0], x_other[0]), axis=0).astype(f32)
    rows = x.shape[0]
    half = rows // 2
    lane = lax.broadcasted_iota(jnp.int32, (rows, LANES), 1)
    inverse = lax.rsqrt(jnp.mean(x * x, axis=1, keepdims=True) + EPSILON)
    normed = (x * inverse * gain[...]).astype(bf16)
    normed_out[0] = normed
    q_cols = heads * (DN + DR)
    queries = dot_nn(normed, head_w[:, :q_cols])
    q_rope = queries[:, heads * DN :]
    q_rope = q_rope * cosine[0] + swap_halves(q_rope, lane) * sine[0]
    q = jnp.concatenate([queries[:, : heads * DN], q_rope], axis=1).astype(bf16)
    q_out[0] = q
    latent = dot_nn(normed, small_w[:, : rank + LANES])
    latent_out[0] = latent
    squeezed = latent[:, :rank]
    inverse = lax.rsqrt(jnp.mean(squeezed * squeezed, axis=1, keepdims=True) + EPSILON)
    compressed = (squeezed * inverse * latent_gain[...]).astype(bf16)
    compressed_out[0] = compressed
    k_rope = latent[:, rank:]
    k_rope = (k_rope * cosine[0] + swap_halves(k_rope, lane) * sine[0]).astype(bf16)
    k_rope_out[0] = k_rope
    kv = dot_nn(compressed, kv_w[...]).astype(bf16)
    kv_out[0] = kv
    visible = seen(doc_col[0], doc_row[0])
    attended, sums = [], jnp.zeros((rows, LANES), f32)
    for head in range(heads):
        scores, *_, value = head_scores(q, kv, k_rope, visible, lane, head, heads)
        top = jnp.max(scores, axis=1, keepdims=True)
        log_total = top + jnp.log(jnp.sum(jnp.exp(scores - top), axis=1, keepdims=True))
        sums = jnp.where(lane == head, log_total, sums)
        probs = jnp.exp(scores - log_total).astype(bf16)
        attended.append(dot_nn(probs, value).astype(bf16))
    sums_out[0] = sums
    attended = jnp.concatenate(attended, axis=1)
    attended_out[0] = attended
    part = dot_nt(attended, head_w[:, q_cols : q_cols + heads * DV]).astype(bf16)
    part_own_out[0], part_other_out[0] = by_core(core, part[:half], part[half:])


def attention_backward_kernel(
    heads,
    core_ref,
    d_own,
    d_other,
    normed_ref,
    compressed_ref,
    q_ref,
    kv_ref,
    k_rope_ref,
    sums_ref,
    attended_ref,
    head_w,
    kv_w,
    cosine,
    sine,
    doc_col,
    doc_row,
    head_grad_out,
    kv_grad_out,
    normed_own_out,
    normed_other_out,
    latent_own_out,
    latent_other_out,
    head_acc,
    kv_acc,
):
    f32, bf16 = jnp.float32, jnp.bfloat16
    core, step = core_ref[0], pl.program_id(0)
    scale = (DN + DR) ** -0.5
    d_rows = jnp.concatenate(by_core(core, d_own[0], d_other[0]), axis=0)
    rows = d_rows.shape[0]
    half = rows // 2
    lane = lax.broadcasted_iota(jnp.int32, (rows, LANES), 1)
    q_cols = heads * (DN + DR)
    q, kv, k_rope = q_ref[0], kv_ref[0], k_rope_ref[0]
    d_attended = dot_nn(d_rows, head_w[:, q_cols : q_cols + heads * DV]).astype(bf16)
    visible = seen(doc_col[0], doc_row[0])
    d_q, d_kv = [], []
    d_q_rope, d_k_rope = jnp.zeros((rows, LANES), f32), jnp.zeros((rows, LANES), f32)
    for head in range(heads):
        scores, q_nope, q_rope, k_nope, value = head_scores(
            q, kv, k_rope, visible, lane, head, heads
        )
        probs = jnp.exp(scores - sums_ref[0][:, head : head + 1])
        d_head = d_attended[:, head * DV : (head + 1) * DV]
        d_probs = dot_nt(d_head, value)
        d_value = dot_tn(probs.astype(bf16), d_head)
        delta = jnp.sum(probs * d_probs, axis=1, keepdims=True)
        d_scores = (probs * (d_probs - delta)).astype(bf16)
        d_q.append(dot_nn(d_scores, k_nope) * scale)
        d_q_rope = jnp.where(lane // DR == head, dot_nn(d_scores, k_rope) * scale, d_q_rope)
        d_kv += [dot_tn(d_scores, q_nope) * scale, d_value]
        d_k_rope += dot_tn(d_scores, q_rope) * scale
    d_q_rope = d_q_rope * cosine[0] - swap_halves(d_q_rope, lane) * sine[0]
    d_q = jnp.concatenate(d_q + [d_q_rope], axis=1).astype(bf16)
    d_kv = jnp.concatenate(d_kv, axis=1).astype(bf16)

    @pl.when(step == 0)
    def _():
        head_acc[...] = jnp.zeros_like(head_acc)
        kv_acc[...] = jnp.zeros_like(kv_acc)

    head_acc[:, :q_cols] += dot_tn(normed_ref[0], d_q)
    head_acc[:, q_cols:] += dot_tn(d_rows, attended_ref[0])
    kv_acc[...] += dot_tn(compressed_ref[0], d_kv)

    @pl.when(step == pl.num_programs(0) - 1)
    def _():
        head_grad_out[...] = head_acc[...].astype(bf16)
        kv_grad_out[...] = kv_acc[...].astype(bf16)

    part = dot_nt(d_q, head_w[:, :q_cols]).astype(bf16)
    normed_own_out[0], normed_other_out[0] = by_core(core, part[:half], part[half:])
    latent = jnp.concatenate([dot_nt(d_kv, kv_w[...]), d_k_rope], axis=1).astype(bf16)
    latent_own_out[0], latent_other_out[0] = by_core(core, latent[:half], latent[half:])


def one_each(*tail):
    return pl.BlockSpec((1, *tail), lambda i: (i,) + (0,) * len(tail))


def kept(value):
    return pl.BlockSpec(value.shape, lambda i: (0,) * value.ndim, pipeline_mode=pl.Buffered(1))


def attention(core, x_own, x_other, gain, latent_gain, head_w, small_w, kv_w, cosine, sine, doc):
    near, half, width = x_own.shape
    rows = 2 * half
    rank, kv_cols = kv_w.shape
    heads = kv_cols // (DN + DV)
    f32, bf16 = jnp.float32, jnp.bfloat16
    shapes = [
        ((rows, width), bf16),
        ((rows, rank), bf16),
        ((rows, heads * (DN + DR)), bf16),
        ((rows, kv_cols), bf16),
        ((rows, LANES), bf16),
        ((rows, LANES), f32),
        ((rows, heads * DV), bf16),
        ((rows, rank + LANES), f32),
        ((half, width), bf16),
        ((half, width), bf16),
    ]
    return pl.pallas_call(
        functools.partial(attention_kernel, heads, rank),
        grid=(near,),
        in_specs=[
            pl.BlockSpec(memory_space=pltpu.SMEM),
            *[one_each(half, width)] * 2,
            *[kept(a) for a in (gain, latent_gain, head_w, small_w, kv_w)],
            *[one_each(rows, LANES)] * 2,
            one_each(rows, 1),
            one_each(1, rows),
        ],
        out_specs=[one_each(*shape) for shape, _ in shapes],
        out_shape=[jax.ShapeDtypeStruct((near, *shape), kind) for shape, kind in shapes],
        compiler_params=pltpu.CompilerParams(vmem_limit_bytes=58 * 1024 * 1024),
        cost_estimate=pl.CostEstimate(
            flops=2 * near * rows * width * (rank + 3 * heads * DN),
            bytes_accessed=4 * near * rows * width,
            transcendentals=0,
        ),
    )(
        core,
        x_own,
        x_other,
        gain,
        latent_gain,
        head_w,
        small_w,
        kv_w,
        cosine,
        sine,
        doc[:, :, None],
        doc[:, None, :],
    )


def attention_backward(core, d_own, d_other, kept_rows, head_w, kv_w, cosine, sine, doc):
    near, half, width = d_own.shape
    rows = 2 * half
    rank, kv_cols = kv_w.shape
    heads = kv_cols // (DN + DV)
    head_cols = heads * (DN + DR + DV)
    f32, bf16 = jnp.float32, jnp.bfloat16
    sds = jax.ShapeDtypeStruct
    return pl.pallas_call(
        functools.partial(attention_backward_kernel, heads),
        grid=(near,),
        in_specs=[
            pl.BlockSpec(memory_space=pltpu.SMEM),
            *[one_each(half, width)] * 2,
            *[one_each(*v.shape[1:]) for v in kept_rows],
            *[kept(a) for a in (head_w, kv_w)],
            *[one_each(rows, LANES)] * 2,
            one_each(rows, 1),
            one_each(1, rows),
        ],
        out_specs=[
            pl.BlockSpec((width, head_cols), lambda i: (0, 0)),
            pl.BlockSpec((rank, kv_cols), lambda i: (0, 0)),
            *[one_each(half, width)] * 2,
            *[one_each(half, rank + LANES)] * 2,
        ],
        out_shape=[
            sds((width, head_cols), bf16),
            sds((rank, kv_cols), bf16),
            *[sds((near, half, width), bf16)] * 2,
            *[sds((near, half, rank + LANES), bf16)] * 2,
        ],
        scratch_shapes=[
            pltpu.VMEM((width, head_cols), f32),
            pltpu.VMEM((rank, kv_cols), f32),
        ],
        compiler_params=pltpu.CompilerParams(vmem_limit_bytes=58 * 1024 * 1024),
        cost_estimate=pl.CostEstimate(
            flops=near * rows * width * heads * DN,
            bytes_accessed=2 * near * rows * width,
            transcendentals=0,
        ),
    )(
        core,
        d_own,
        d_other,
        *kept_rows,
        head_w,
        kv_w,
        cosine,
        sine,
        doc[:, :, None],
        doc[:, None, :],
    )


def product_kernel(*refs):
    *operands, out_ref = refs
    count = len(operands) // 2
    total = 0.0
    for left_ref, right_ref in zip(operands[:count], operands[count:]):
        total += dot_tn(left_ref[0], right_ref[...])
    out_ref[0] = total


def column_products(lefts, rights, tile=512):
    count, _, height = lefts[0].shape
    width = rights[0].shape[1]
    return pl.pallas_call(
        product_kernel,
        grid=(width // tile, count),
        in_specs=[
            *[pl.BlockSpec((1, v.shape[1], height), lambda j, i: (i, 0, 0)) for v in lefts],
            *[pl.BlockSpec((v.shape[0], tile), lambda j, i: (0, j)) for v in rights],
        ],
        out_specs=pl.BlockSpec((1, height, tile), lambda j, i: (i, 0, j)),
        out_shape=jax.ShapeDtypeStruct((count, height, width), jnp.float32),
        compiler_params=pltpu.CompilerParams(vmem_limit_bytes=58 * 1024 * 1024),
        cost_estimate=pl.CostEstimate(flops=width, bytes_accessed=width, transcendentals=0),
    )(*lefts, *rights)


def output_kernel(act, sact_own, sact_other, meta_own, meta_other, down_w, sdown_w, own_out, other_out):
    f32, bf16 = jnp.float32, jnp.bfloat16
    count, half, _ = meta_own.shape
    lane = lax.broadcasted_iota(jnp.int32, (2 * half, LANES), 1).astype(f32)
    out = dot_nn(act[...], down_w[...]).astype(bf16)
    for i in range(count):
        meta = jnp.concatenate([meta_own[i], meta_other[i]], axis=0)
        pick = (meta[:, :1] == lane).astype(bf16)
        sact = jnp.concatenate([sact_own[i], sact_other[i]], axis=0)
        here = slice(i * LANES, (i + 1) * LANES)
        rows = (dot_nn(pick, out[here]) + dot_nn(sact, sdown_w[...])).astype(bf16)
        own_out[i], other_out[i] = rows[:half], rows[half:]


def outputs(act, sact_own, sact_other, meta_own, meta_other, down_w, sdown_w, per_step=4):
    groups, half, _ = meta_own.shape
    hidden, width = down_w.shape
    lead, flat, whole = block_specs(per_step)
    return pl.pallas_call(
        output_kernel,
        grid=(groups // per_step,),
        in_specs=[
            flat(hidden),
            *[lead(half, LANES)] * 4,
            *[whole(a) for a in (down_w, sdown_w)],
        ],
        out_specs=[lead(half, width)] * 2,
        out_shape=[jax.ShapeDtypeStruct((groups, half, width), jnp.bfloat16)] * 2,
        compiler_params=pltpu.CompilerParams(vmem_limit_bytes=58 * 1024 * 1024),
        cost_estimate=pl.CostEstimate(
            flops=groups * half * LANES * width,
            bytes_accessed=groups * half * width,
            transcendentals=0,
        ),
    )(act, sact_own, sact_other, meta_own, meta_other, down_w, sdown_w)


def token_plan(
    inputs,
    attn_gain,
    w_query,
    w_latent,
    latent_gain,
    w_kv,
    w_out,
    ffn_gain,
    w_router,
    shared_gate_up,
    shared_down,
    expert_gate_up,
    expert_down,
    lengths,
    routes,
    cotangent,
):
    f32, bf16 = jnp.float32, jnp.bfloat16
    core, me = lax.axis_index("tensor"), lax.axis_index("expert")
    groups = lax.axis_size("expert")
    deep, place, z = groups // PLANE, me % PLANE, me // PLANE
    tok_rows, width = inputs.shape
    half = tok_rows // 2
    own_at, other_at = core * half, (1 - core) * half
    expert_count = w_router.shape[1]
    route_count = routes.shape[1]
    capacity = tok_rows * route_count * 4 // (3 * expert_count)
    shared_cols = shared_gate_up.shape[2] // groups
    latent_cols, rank_width = w_latent.shape[1], latent_gain.shape[0] * groups
    block_rows = w_query.shape[0]
    kv_rows = w_kv.shape[0]

    query_cols = w_query.shape[1] // PLANE
    out_cols = w_out.shape[0] // PLANE
    small = jnp.concatenate(
        [
            w_latent,
            w_latent[:, rank_width:],
            w_router,
            attn_gain[:, None],
            ffn_gain[:, None],
            jnp.pad(latent_gain, (0, block_rows - kv_rows))[:, None],
        ],
        axis=1,
    )
    small_cols = small.shape[1]
    route_half = take_rows(routes, own_at, half).astype(bf16).reshape(block_rows // 2, -1)
    length_col = jnp.pad(lengths[0].astype(bf16), (0, block_rows // 2 - lengths.shape[1]))[:, None]
    route_cols = route_half.shape[1] + 1
    small_half = jnp.concatenate(
        [
            take_rows(small, core * (block_rows // 2), block_rows // 2),
            route_half,
            length_col,
            jnp.zeros((block_rows // 2, -(small_cols + route_cols) % (2 * LANES)), bf16),
        ],
        axis=1,
    )
    packed_cols = small_half.shape[1] // 2
    small_packed = jnp.concatenate([small_half[:, :packed_cols], small_half[:, packed_cols:]])
    kv_cols = w_kv.shape[1] // PLANE
    kv_parts = block_rows // kv_rows
    kv_piece = kv_cols // kv_parts
    w_out_t = w_out.T

    local_heads = query_cols // (DN + DR)

    def by_parts(block):
        heads = [block[:, h * (DN + DR) : (h + 1) * (DN + DR)] for h in range(local_heads)]
        return [h[:, :DN] for h in heads] + [h[:, DN:] for h in heads]

    def quarter(index):
        kv_here = take_rows(w_kv, index * kv_cols, kv_cols, axis=1)
        kv_here = [kv_here[:, p * kv_piece : (p + 1) * kv_piece] for p in range(kv_parts)]
        return jnp.concatenate(
            [
                *by_parts(take_rows(w_query, index * query_cols, query_cols, axis=1)),
                take_rows(w_out_t, index * out_cols, out_cols, axis=1),
                jnp.concatenate(kv_here, axis=0),
            ],
            axis=1,
        )

    near_w = [quarter(place)] + [to_partner(quarter(place ^ r), r) for r in range(1, PLANE)]
    small_line = deep_join(small_packed, deep_pieces(small_packed), z)
    near_w, small_line = tie(near_w, small_line)
    plane_w = jnp.stack(by_place(near_w, place))
    small_sent, x_sent, plane_w = tie(
        small_line.swapaxes(0, 1), take_rows(inputs, own_at, half), plane_w
    )
    small_sent = jnp.stack([small_sent, to_partner(small_sent, 1)])
    small_sent = jnp.concatenate([small_sent, to_partner(small_sent, 2)], axis=0)
    x_sent = jnp.stack([x_sent, to_partner(x_sent, 2)])
    x_came = to_partner(x_sent, 1)
    x_near_own = jnp.stack([x_sent[0], x_came[0], x_sent[1], x_came[1]])
    x_near_other = swap_cores(x_near_own)
    deep_w = deep_hops(plane_w)
    small_parts = [small_sent[r].swapaxes(0, 1) for r in range(PLANE)]
    small_own = jnp.stack(by_place(small_parts, place), axis=1)
    small_own = small_own.reshape(groups, block_rows, packed_cols)
    small_own = jnp.concatenate(
        [small_own[:, : block_rows // 2], small_own[:, block_rows // 2 :]], axis=2
    )
    small_other = swap_cores(small_own)
    small_all = in_order(core, small_own, small_other, axis=1)
    small_all, x_near_other, deep_w = tie(small_all, x_near_other, deep_w)
    head_w = deep_join(plane_w, join_hops(deep_w), z)
    length_at = small_cols + route_cols - 1
    lengths_near = take_rows(small_own, z * PLANE, PLANE)[:, : lengths.shape[1], length_at]
    lengths_near = lengths_near.astype(jnp.int32)
    lengths_near = jnp.stack(by_place([lengths_near[r] for r in range(PLANE)], place))
    shared_rows = jnp.concatenate(
        [shared_gate_up[0].T, shared_gate_up[1].T, shared_down], axis=0
    ).reshape(3, groups, shared_cols, block_rows)
    shared_rows = shared_rows.swapaxes(0, 1).reshape(groups, 3 * shared_cols, block_rows)
    dy_sent, head_w = tie(take_rows(cotangent, own_at, half), head_w)
    dy_own_rows = take_rows(cotangent, own_at, half)
    dy_gather = RowGather(dy_sent)
    dy_came = dy_gather.along()
    head_w = head_w.reshape(groups, block_rows, -1)
    flat_head = head_w.reshape(groups * block_rows, -1)
    at = query_cols + out_cols
    kv_w = head_w[:, :, at : at + kv_piece].reshape(groups, kv_parts, kv_rows, kv_piece)
    kv_w = kv_w.transpose(0, 2, 1, 3).reshape(groups * kv_rows, kv_cols)

    block_index = jnp.arange(groups)
    block_chip = (z - block_index % deep) % deep * PLANE + (place ^ (block_index // deep))
    in_blocks = (block_chip[:, None] == block_index[None, :]).astype(bf16)

    def routes_of(came):
        came = came[:, :, small_cols : small_cols + route_half.shape[1]].reshape(groups, -1)
        came = jnp.dot(in_blocks, came, preferred_element_type=f32)
        return came.astype(jnp.int32).reshape(groups, half, route_count)

    routes_own, routes_other = routes_of(small_own), routes_of(small_other)
    flat_small = small_all.reshape(groups * block_rows, -1)
    latent_w = flat_small[:, :latent_cols]
    at = rank_width + LANES
    router_w = flat_small[:, at : at + expert_count]
    at += expert_count
    gain_one, gain_two = flat_small[:, at], flat_small[:, at + 1]
    latent_g = small_all[:, :kv_rows, at + 2].reshape(-1)

    near_rows = PLANE * tok_rows
    relative, doc = jax.vmap(lambda one: doc_places(one, tok_rows))(lengths_near)
    cosine, sine_tab = rope_tables(relative.reshape(-1), DR)
    cosine, sine_tab = [v.reshape(PLANE, tok_rows, -1) for v in (cosine, sine_tab)]
    rope = (
        jnp.concatenate([cosine] * 4, axis=-1),
        jnp.concatenate([-sine_tab, sine_tab] * 2, axis=-1),
        doc.astype(f32),
    )
    core_index = core.reshape(1).astype(jnp.int32)
    *kept_rows, latent, part_own, part_other = attention(
        core_index,
        x_near_own,
        x_near_other,
        gain_one.astype(f32)[None],
        latent_g.astype(f32)[None],
        flat_head,
        flat_small,
        kv_w,
        *rope,
    )
    normed_b = kept_rows[0].reshape(near_rows, width)

    def sum_cores(own, other):
        return add_wide(own, swap_cores(other)).astype(bf16)

    def sum_plane(both):
        return plane_scatter([both[r] for r in range(PLANE)])

    part_own, part_other, dy_came = tie(part_own, part_other, dy_came)
    attn_own = sum_plane(sum_cores(part_own, part_other))
    x_own = take_rows(inputs, own_at, half).astype(f32)
    hidden = x_own + attn_own
    hnormed, scale_two = rms_forward(hidden, gain_two.astype(f32))
    hnormed_b = hnormed.astype(bf16)
    normed_cols = jnp.concatenate(
        [
            take_rows(normed_b, (k * PLANE + place) * block_rows, block_rows, axis=1)
            for k in range(deep)
        ],
        axis=1,
    )
    hnormed_b, normed_cols, shared_rows, routes_own, routes_other = tie(
        hnormed_b, normed_cols, shared_rows, routes_own, routes_other
    )
    dy_line = jnp.stack(dy_came)
    def membership(named):
        one_hot = named[..., None] == jnp.arange(expert_count, dtype=jnp.int32)
        return jnp.any(named == me, axis=-1), jnp.any(one_hot, axis=2)

    member_own, hot_own = membership(routes_own)
    member_other, hot_other = membership(routes_other)
    lower = (
        jnp.arange(half, dtype=jnp.int32)[:, None] <= jnp.arange(half, dtype=jnp.int32)[None, :]
    ).astype(bf16)

    def running(mask):
        counts = jnp.dot(mask.astype(bf16), lower, preferred_element_type=f32)
        return counts.astype(jnp.int32)

    count_own, count_other = running(member_own), running(member_other)
    place_own = jnp.where(member_own, count_own - 1, -1)
    place_other = jnp.where(member_other, count_own[:, -1:] + count_other - 1, -1)

    def metadata(slot, hot):
        return jnp.concatenate(
            [
                slot[..., None].astype(f32),
                jnp.zeros((groups, half, shared_cols - 1), f32),
                hot.astype(f32),
                jnp.zeros((groups, half, LANES - shared_cols - expert_count), f32),
            ],
            axis=-1,
        )

    meta_own, meta_other = metadata(place_own, hot_own), metadata(place_other, hot_other)
    hn_gather = RowGather(hnormed_b)
    shared_w = lax.all_to_all(shared_rows, "expert", split_axis=0, concat_axis=0, tiled=True)
    hn_came, dy_beside, dy_line_other, shared_w, meta_own, meta_other = tie(
        hn_gather.along(),
        dy_gather.beside(dy_line),
        swap_cores(dy_line),
        shared_w,
        meta_own,
        meta_other,
    )
    shared_w = shared_w.swapaxes(0, 1).reshape(3 * shared_cols, groups * block_rows)
    first_w = jnp.concatenate(
        [
            shared_w[:shared_cols],
            router_w.T,
            jnp.zeros((LANES - shared_cols - expert_count, width), bf16),
            shared_w[shared_cols : 2 * shared_cols],
            jnp.zeros((LANES - shared_cols, width), bf16),
        ],
        axis=0,
    )
    sdown_rows = jnp.pad(shared_w[2 * shared_cols :], ((0, LANES - shared_cols), (0, 0)))
    gate_up_w, down_w = jnp.swapaxes(expert_gate_up[0], 1, 2), expert_down[0]

    def run_experts(which, hn_part, hn_part_other):
        at, to = which[0] * deep, (which[-1] + 1) * deep
        return experts(
            me.reshape(1).astype(jnp.int32),
            hn_part,
            hn_part_other,
            *dy_parts[which],
            meta_own[at:to],
            meta_other[at:to],
            gate_up_w,
            down_w,
            first_w,
            sdown_rows,
            shared_cols,
            expert_count,
        )

    parts = ((0,), (1, 2), (3,))
    dy_parts = {parts[0]: (dy_line, dy_line_other)}
    hn_line, dy_beside = tie(jnp.stack(hn_came), dy_beside)
    dy_near = jnp.concatenate(dy_beside, axis=0)
    hn_beside, dy_far, done_line, *dy_parts[parts[1]] = tie(
        hn_gather.beside(hn_line),
        dy_gather.far(dy_beside),
        run_experts(parts[0], hn_line, swap_cores(hn_line)),
        dy_near,
        swap_cores(dy_near),
    )
    d_line_came = swap_cores(done_line[5])
    hn_near, dy_far = jnp.concatenate(hn_beside, axis=0), jnp.concatenate(dy_far, axis=1)
    hn_far, done_near, *dy_parts[parts[2]] = tie(
        hn_gather.far(hn_beside),
        run_experts(parts[1], hn_near, swap_cores(hn_near)),
        dy_far,
        swap_cores(dy_far),
    )
    d_near_came = swap_cores(done_near[5])
    hn_far = jnp.concatenate(hn_far, axis=1)
    done_far = run_experts(parts[2], hn_far, swap_cores(hn_far))
    done = (done_line, done_near, done_far)
    slot_rows, slot_dy, slot_act, d_gate_up = [[v[i] for v in done] for i in range(4)]
    shared_grads = add_wide(*[v[8] for v in done])

    def by_flips(line, near, far):
        return [line, near[:deep], near[deep:], far]

    d_rows_own = by_flips(*[v[4] for v in done])
    d_rows_came = by_flips(d_line_came, d_near_came, swap_cores(done_far[5]))

    def two_parts(value):
        return value[..., 0] + value[..., 1]

    dgate_own, dgate_other = [
        jnp.concatenate([two_parts(v[i]) for v in done], axis=0) for i in (9, 10)
    ]
    dgate_sent = dgate_own + swap_cores(dgate_other)
    dgate_high = dgate_sent.astype(bf16)
    dgate_low = (dgate_sent - dgate_high.astype(f32)).astype(bf16)
    d_rows_came, dgate_high, dgate_low = tie(d_rows_came, dgate_high, dgate_low)
    d_sum = RowSum(d_rows_own, d_rows_came)
    sends, shared_grads, slot_act = tie(d_sum.sends(), shared_grads, slot_act)
    came = d_sum.move(sends)
    gate_rows = jnp.stack([contract_rows(in_blocks, v).reshape(-1) for v in (dgate_high, dgate_low)])
    grads_sent = jnp.concatenate([shared_grads, gate_rows], axis=0).astype(bf16)
    grads_sent = grads_sent.reshape(-1, groups, block_rows)
    grads_came = lax.all_to_all(grads_sent, "expert", split_axis=1, concat_axis=1, tiled=True)
    out_done = [
        outputs(
            act,
            v[6],
            v[7],
            meta_own[p[0] * deep : (p[-1] + 1) * deep],
            meta_other[p[0] * deep : (p[-1] + 1) * deep],
            down_w,
            sdown_rows,
        )
        for act, v, p in zip(slot_act, done, parts)
    ]
    edown_grad = column_products([v[None] for v in slot_act], slot_dy)[0]
    came, out_done, edown_grad, grads_came = tie(came, out_done, edown_grad, grads_came)
    dgate = add_wide(grads_came[3 * shared_cols], grads_came[3 * shared_cols + 1]).T
    sends, slot_rows, out_done = tie(d_sum.sends_again(came), slot_rows, out_done)
    came_again = d_sum.move_again(sends)
    egu_grad = column_products(d_gate_up, slot_rows).swapaxes(1, 2)
    out_own = by_flips(*[v[0] for v in out_done])
    out_came = by_flips(*[swap_cores(v[1]) for v in out_done])
    out_sum = RowSum(out_own, out_came)
    out_sends = out_sum.sends()
    came_again, egu_grad, out_sends = tie(came_again, egu_grad, out_sends)
    z_sends, out_sends, dgate = tie(
        line_sends(d_sum.line(came, came_again)), out_sends, dgate
    )
    z_came = line_move(z_sends)
    out_first = out_sum.move(out_sends)
    hot_mine = take_rows(
        jnp.any(routes[..., None] == jnp.arange(expert_count, dtype=jnp.int32), axis=1), own_at, half
    )
    sig = jax.nn.sigmoid(jnp.dot(hnormed_b, router_w, preferred_element_type=f32))
    chosen = jnp.where(hot_mine, sig, 0.0)
    chosen_sum = jnp.sum(chosen, axis=1, keepdims=True)
    dgate = jnp.where(hot_mine, dgate, 0.0)
    inner = jnp.sum(dgate * chosen, axis=1, keepdims=True)
    d_chosen = ROUTE_SCALE * (dgate / chosen_sum - inner / (chosen_sum * chosen_sum))
    d_logits = (jnp.where(hot_mine, d_chosen, 0.0) * sig * (1.0 - sig)).astype(bf16)
    router_grad = contract_rows(d_logits, hnormed_b)
    z_came, d_logits, router_grad = tie(z_came, d_logits, router_grad)
    d_hn = add_wide(*z_came)
    d_hn = d_hn + contract_cols(d_logits, router_w)
    d_hidden_norm, gain_two_grad = rms_backward(hidden, scale_two, gain_two.astype(f32), d_hn)
    d_hidden = dy_own_rows.astype(f32) + d_hidden_norm
    d_parts, out_first = tie(plane_gather(d_hidden.astype(bf16)), out_first)
    d_near_own = jnp.stack(d_parts)
    d_near_other = swap_cores(d_near_own)
    out_sends, d_near_other = tie(out_sum.sends_again(out_first), d_near_other)
    out_second = out_sum.move_again(out_sends)

    (
        head_grad,
        kv_grad,
        normed_part_own,
        normed_part_other,
        latent_part_own,
        latent_part_other,
    ) = attention_backward(
        core_index, d_near_own, d_near_other, kept_rows, flat_head, kv_w, *rope
    )
    kv_grad = kv_grad.reshape(groups, kv_rows, kv_parts, kv_piece).transpose(0, 2, 1, 3)
    head_grad = jnp.concatenate([head_grad, kv_grad.reshape(-1, kv_piece)], axis=1)
    head_blocks = head_grad.reshape(deep, -1, head_grad.shape[1])
    head_hops = HopSum(lambda t: at_index(head_blocks, 0, t))
    came, latent_both, normed_both, out_second = tie(
        head_hops.hop(1),
        sum_cores(latent_part_own, latent_part_other),
        sum_cores(normed_part_own, normed_part_other),
        out_second,
    )
    out_line = out_sum.line(out_first, out_second)
    came, grad_both, out_line = tie(head_hops.hop(2, came), sum_plane(latent_both), out_line)
    grad_rope = grad_both[:, rank_width : rank_width + DR] + grad_both[:, rank_width + DR :]
    latent_own = take_rows(latent[0], own_at, half)
    cosine_own = take_rows(cosine[0], own_at, half)
    sine_own = take_rows(sine_tab[0], own_at, half)
    _, scale_kv = rms_forward(latent_own[:, :rank_width], latent_g.astype(f32))
    grad_c, latent_gain_grad = rms_backward(
        latent_own[:, :rank_width], scale_kv, latent_g.astype(f32), grad_both[:, :rank_width]
    )
    grad_latent = jnp.concatenate(
        [grad_c, unrotate(grad_rope, cosine_own, sine_own)], axis=-1
    ).astype(bf16)
    out_hops = HopSum(lambda t: at_index(out_line, 0, (z - t) % deep))
    came, latent_parts, grad_normed, out_z = tie(
        head_hops.hop(3, came), plane_gather(grad_latent), sum_plane(normed_both), out_hops.hop(1)
    )
    latent_near_own = jnp.stack(latent_parts)
    latent_near = in_order(core, latent_near_own, swap_cores(latent_near_own), axis=1)
    head_sums = head_hops.total(came).astype(bf16).reshape(PLANE, block_rows, -1)
    out_z, latent_near, head_shared, grads_came = tie(
        out_hops.hop(2, out_z), latent_near, share_columns(head_sums, place), grads_came
    )
    out_z = out_hops.hop(3, out_z)
    latent_cut = latent_cols // 2
    latent_near = latent_near.reshape(near_rows, latent_cols)
    latent_blocks = contract_rows(
        normed_cols,
        take_rows(latent_near, core * latent_cut, latent_cut, axis=1),
    )
    latent_half = deep_scatter(latent_blocks.astype(bf16).reshape(deep, -1, latent_cut), z)
    w_latent_grad = in_order(core, latent_half, swap_cores(latent_half), axis=1)


    def by_heads(block):
        rotary = local_heads * DN
        return [
            part
            for h in range(local_heads)
            for part in (
                block[:, h * DN : (h + 1) * DN],
                block[:, rotary + h * DR : rotary + (h + 1) * DR],
            )
        ]

    at_kv = query_cols + out_cols
    w_query_grad = jnp.concatenate([v for p in head_shared for v in by_heads(p)], axis=1)
    w_query_grad = w_query_grad.astype(f32)
    w_kv_grad = jnp.concatenate(
        [
            p[q * kv_rows : (q + 1) * kv_rows, at_kv:]
            for p in head_shared
            for q in range(kv_parts)
        ],
        axis=1,
    ).astype(f32)
    w_out_grad = jnp.concatenate([p[:, query_cols:at_kv] for p in head_shared], axis=1)
    w_out_grad = w_out_grad.astype(f32).T
    sgu_out = grads_came[: 2 * shared_cols].astype(f32)
    sgu_out = sgu_out.reshape(2, shared_cols, groups, block_rows)
    sgu_out = sgu_out.transpose(0, 3, 2, 1).reshape(2, block_rows, -1)
    sdown_out = grads_came[2 * shared_cols : 3 * shared_cols].astype(f32).swapaxes(0, 1).reshape(-1, block_rows)
    grad_normed = grad_normed + contract_cols(grad_latent, latent_w)
    moe_own = out_hops.total(out_z)
    mixed_own = (hidden + moe_own).astype(bf16)
    mixed = in_order(core, mixed_own, swap_cores(mixed_own))

    _, scale_own = rms_forward(x_own, gain_one.astype(f32))
    grad_x_norm, gain_one_grad = rms_backward(x_own, scale_own, gain_one.astype(f32), grad_normed)
    input_own = d_hidden + grad_x_norm
    input_grad = in_order(core, input_own, swap_cores(input_own))

    gain_lanes = jnp.pad(
        latent_gain_grad.reshape(groups, kv_rows), ((0, 0), (0, block_rows - kv_rows))
    )
    vectors = jnp.concatenate(
        [
            router_grad,
            gain_one_grad[None],
            gain_two_grad[None],
            gain_lanes.reshape(1, -1),
        ],
        axis=0,
    ).reshape(-1, groups, block_rows)
    arrived = lax.all_to_all(vectors, "expert", split_axis=1, concat_axis=1, tiled=True)
    sums = jnp.sum(arrived, axis=1)
    sums = sums + swap_cores(sums)
    return (
        mixed,
        input_grad,
        sums[expert_count],
        w_query_grad,
        w_latent_grad,
        sums[expert_count + 2, :kv_rows],
        w_kv_grad,
        w_out_grad,
        sums[expert_count + 1],
        sums[:expert_count].T,
        sgu_out,
        sdown_out,
        egu_grad[None],
        edown_grad[None],
    )


def solution(mesh):
    groups = mesh.shape["expert"]
    plan = token_plan if groups <= 16 else weight_plan
    return jax.shard_map(
        plan,
        mesh=mesh,
        in_specs=(
            P("expert", None),
            P("expert"),
            P("expert", "tensor"),
            P("expert", None),
            P("expert"),
            P("expert", "tensor"),
            P("tensor", "expert"),
            P("expert"),
            P("expert", None),
            P(None, "expert", "tensor"),
            P("tensor", "expert"),
            P("expert", None, None, "tensor"),
            P("expert", "tensor", None),
            P("expert", None),
            P("expert", None),
            P("expert", None),
        ),
        out_specs=(
            P("expert", None),
            P("expert", None),
            P("expert"),
            P("expert", "tensor"),
            P("expert", None),
            P("expert"),
            P("expert", "tensor"),
            P("tensor", "expert"),
            P("expert"),
            P("expert", None),
            P(None, "expert", "tensor"),
            P("tensor", "expert"),
            P("expert", None, None, "tensor"),
            P("expert", "tensor", None),
        ),
        check_vma=False,
    )
```

```python
import functools

import jax
import jax.numpy as jnp
from jax import lax
from jax.experimental import pallas as pl
from jax.experimental.pallas import tpu as pltpu
from jax.sharding import PartitionSpec as P

DN = 128
DR = 64
DV = 128
LANES = 128


EPSILON = 1e-06
ROUTE_SCALE = 2.446
ROPE_BASE = 50000.0
NEGATIVE = -1e30


def cut_along(value, dim, length):
    before, after = (value.shape[:dim], value.shape[dim + 1 :])
    return jnp.moveaxis(value.reshape(*before, length, -1, *after), dim, 0)


def summed_on_arrival(value, axis, dim):
    length = lax.axis_size(axis)
    tiles = lax.all_to_all(cut_along(value, dim, length), axis, 0, 0, tiled=True)
    return jnp.sum(tiles.astype(jnp.float32), axis=0)


def sent_together(arrays, axis, dim, along):
    columns = [a.reshape(*a.shape[:along], -1) for a in arrays]
    both = jnp.concatenate(columns, axis=along)
    whole, at, outs = (summed_on_arrival(both, axis, dim), 0, [])
    for a, column in zip(arrays, columns):
        slab = whole[..., at : at + column.shape[along]]
        outs.append(slab.reshape(*slab.shape[:along], *a.shape[along:]))
        at += column.shape[along]
    return tuple(outs)


def contract_rows(left_arr, right_arr):
    return lax.dot_general(
        left_arr, right_arr, (((0,), (0,)), ((), ())), preferred_element_type=jnp.float32
    )


def contract_cols(left_arr, right_arr):
    return lax.dot_general(
        left_arr, right_arr, (((1,), (1,)), ((), ())), preferred_element_type=jnp.float32
    )


def rms_forward(rows_in, gain_vec):
    inverse = lax.rsqrt(jnp.mean(rows_in * rows_in, axis=-1, keepdims=True) + EPSILON)
    return (rows_in * inverse * gain_vec, inverse)


def rms_backward(rows_in, inverse, gain_vec, grad_out):
    gain_grad = jnp.sum(grad_out * rows_in * inverse, axis=0)
    weighted = grad_out * gain_vec
    inner_mean = jnp.mean(weighted * rows_in, axis=-1, keepdims=True)
    return (inverse * weighted - rows_in * inverse * inverse * inverse * inner_mean, gain_grad)


def doc_layout(doc_lengths, row_count):
    ends_at = jnp.cumsum(doc_lengths)
    starts_at = ends_at - doc_lengths
    position = jnp.arange(row_count, dtype=jnp.int32)
    doc_ids = jnp.sum((position[:, None] >= ends_at[None, :]).astype(jnp.int32), axis=1)
    hitting = doc_ids[:, None] == jnp.arange(doc_lengths.shape[0], dtype=jnp.int32)[None, :]
    start_of = jnp.sum(jnp.where(hitting, starts_at[None, :], 0), axis=1)
    relative = position - start_of
    visible = (doc_ids[:, None] == doc_ids[None, :]) & (position[:, None] >= position[None, :])
    return (relative, visible)


def rope_tables(relative, rot_width):
    counter = jnp.arange(rot_width // 2, dtype=jnp.float32)
    frequency = ROPE_BASE ** (-2.0 * counter / rot_width)
    angles = relative.astype(jnp.float32)[:, None] * frequency[None, :]
    return (jnp.cos(angles), jnp.sin(angles))


def rotate(tensor_in, cosine, sine_tab):
    half_width = tensor_in.shape[-1] // 2
    leading = tensor_in[..., :half_width]
    trailing = tensor_in[..., half_width:]
    return jnp.concatenate(
        [leading * cosine - trailing * sine_tab, trailing * cosine + leading * sine_tab], axis=-1
    )


def unrotate(grad_in, cosine, sine_tab):
    half_width = grad_in.shape[-1] // 2
    leading = grad_in[..., :half_width]
    trailing = grad_in[..., half_width:]
    return jnp.concatenate(
        [leading * cosine + trailing * sine_tab, trailing * cosine - leading * sine_tab], axis=-1
    )


def gated_linear_backward(gate_in, up_in, grad_act):
    sigmoid_g = jax.nn.sigmoid(gate_in)
    grad_gate = grad_act * up_in * sigmoid_g * (1.0 + gate_in * (1.0 - sigmoid_g))
    return (grad_gate, grad_act * gate_in * sigmoid_g)


def slot_tables(route_rows, expert_count, capacity):
    flat_routes = route_rows.reshape(-1)
    one_hot = (flat_routes[:, None] == jnp.arange(expert_count, dtype=jnp.int32)[None, :]).astype(
        jnp.int32
    )
    ranking = jnp.sum((jnp.cumsum(one_hot, axis=0) - one_hot) * one_hot, axis=1)
    slot_ids = flat_routes * capacity + ranking
    row_total = flat_routes.shape[0]
    source = (
        jnp.zeros((expert_count * capacity,), jnp.int32)
        .at[slot_ids]
        .set(jnp.arange(row_total, dtype=jnp.int32))
    )
    filled = jnp.zeros((expert_count * capacity,), jnp.int32).at[slot_ids].set(1)
    return (slot_ids, source, filled)


def to_owner(rows_in):
    arrived = lax.all_to_all(rows_in, "expert", split_axis=0, concat_axis=1, tiled=True)
    return arrived


def weight_plan(
    inputs,
    attn_gain,
    w_query,
    w_latent,
    latent_gain,
    w_kv,
    w_out,
    ffn_gain,
    w_router,
    shared_gate_up,
    shared_down,
    expert_gate_up,
    expert_down,
    lengths,
    routes,
    cotangent,
):
    tok_rows = inputs.shape[0]
    model_width = inputs.shape[1]
    expert_count = w_router.shape[1]
    route_count = routes.shape[1]
    capacity = tok_rows * route_count * 4 // (3 * expert_count)
    brain_float16 = jnp.bfloat16
    f32 = jnp.float32
    gathered = (
        lax.all_gather(attn_gain, "expert", axis=0, tiled=True),
        lax.all_gather(w_query, "expert", axis=0, tiled=True),
        lax.all_gather(w_latent, "expert", axis=0, tiled=True),
        lax.all_gather(latent_gain, "expert", axis=0, tiled=True),
        lax.all_gather(w_kv, "expert", axis=0, tiled=True),
        lax.all_gather(w_out, "expert", axis=1, tiled=True),
        lax.all_gather(ffn_gain, "expert", axis=0, tiled=True),
        lax.all_gather(w_router, "expert", axis=0, tiled=True),
        lax.all_gather(shared_gate_up, "expert", axis=1, tiled=True),
        lax.all_gather(shared_down, "expert", axis=1, tiled=True),
    )
    gain_one, query_w, latent_w, latent_g, kv_w, out_w, gain_two, router_w, sgate_up, sdown_w = (
        gathered
    )
    local_heads = query_w.shape[1] // (DN + DR)
    rank_width = latent_g.shape[0]
    x_float = inputs.astype(f32)
    relative, visible = doc_layout(lengths[0], tok_rows)
    cosine, sine_tab = rope_tables(relative, DR)
    q_scale = (DN + DR) ** (-0.5)
    normed, scale_one = rms_forward(x_float, gain_one.astype(f32))
    normed_b = normed.astype(brain_float16)
    queries = jnp.dot(normed_b, query_w, preferred_element_type=f32).reshape(
        tok_rows, local_heads, DN + DR
    )
    q_rot = rotate(queries[..., DN:], cosine[:, None, :], sine_tab[:, None, :])
    q_all = jnp.concatenate([queries[..., :DN], q_rot], axis=-1).astype(brain_float16)
    latent = jnp.dot(normed_b, latent_w, preferred_element_type=f32)
    compressed, scale_kv = rms_forward(latent[:, :rank_width], latent_g.astype(f32))
    compressed_b = compressed.astype(brain_float16)
    k_rope = rotate(latent[:, rank_width:], cosine, sine_tab).astype(brain_float16)
    kv_all = jnp.dot(compressed_b, kv_w, preferred_element_type=f32).reshape(
        tok_rows, local_heads, DN + DV
    )
    k_nope = kv_all[..., :DN].astype(brain_float16)
    values = kv_all[..., DN:].astype(brain_float16)
    key_all = jnp.concatenate(
        [k_nope, jnp.broadcast_to(k_rope[:, None, :], (tok_rows, local_heads, DR))], axis=-1
    )

    def score_block():
        raw_scores = (
            jnp.einsum("qhd,khd->hqk", q_all, key_all, preferred_element_type=f32) * q_scale
        )
        return jnp.where(visible[None], raw_scores, NEGATIVE)

    scores = score_block()
    top_score = jnp.max(scores, axis=-1, keepdims=True)
    log_total = top_score + jnp.log(jnp.sum(jnp.exp(scores - top_score), axis=-1, keepdims=True))
    probs_b = jnp.exp(scores - log_total).astype(brain_float16)
    attended = jnp.einsum("hqk,khd->qhd", probs_b, values, preferred_element_type=f32)
    attended_b = attended.reshape(tok_rows, local_heads * DV).astype(brain_float16)
    attn = lax.psum(jnp.dot(attended_b, out_w, preferred_element_type=f32), "tensor")
    hidden = x_float + attn
    hnormed, scale_two = rms_forward(hidden, gain_two.astype(f32))
    hnormed_b = hnormed.astype(brain_float16)
    logits = jnp.dot(hnormed_b, router_w, preferred_element_type=f32)
    sigmoid_vals = jax.nn.sigmoid(logits)
    route_hot = routes[:, :, None] == jnp.arange(expert_count, dtype=jnp.int32)[None, None, :]
    chosen = jnp.sum(jnp.where(route_hot, sigmoid_vals[:, None, :], 0.0), axis=2)
    chosen_sum = jnp.sum(chosen, axis=1, keepdims=True)
    gate_vals = ROUTE_SCALE * chosen / chosen_sum
    slot_ids, source, filled = slot_tables(routes, expert_count, capacity)
    is_filled = filled[:, None] == 1
    sent_rows = jnp.where(is_filled, hnormed_b[source // route_count], 0).reshape(
        expert_count, capacity, model_width
    )
    received = to_owner(sent_rows)
    gate_up_joined = jnp.einsum(
        "erd,egdf->egrf", received, expert_gate_up, preferred_element_type=f32
    )
    expert_act = (jax.nn.silu(gate_up_joined[:, 0]) * gate_up_joined[:, 1]).astype(brain_float16)
    expert_res = jnp.einsum(
        "erf,efd->erd", expert_act, expert_down, preferred_element_type=f32
    ).astype(brain_float16)
    returned_all = lax.all_to_all(expert_res, "expert", split_axis=1, concat_axis=0, tiled=True)
    returned = returned_all.reshape(expert_count * capacity, model_width)[slot_ids].reshape(
        tok_rows, route_count, model_width
    )
    shared_gu = jnp.einsum("td,gdf->gtf", hnormed_b, sgate_up, preferred_element_type=f32)
    shared_act = (jax.nn.silu(shared_gu[0]) * shared_gu[1]).astype(brain_float16)
    branch_sum = jnp.dot(shared_act, sdown_w, preferred_element_type=f32)
    for route_idx in range(route_count):
        branch_sum = branch_sum + gate_vals[:, route_idx : route_idx + 1] * returned[
            :, route_idx
        ].astype(f32)
    moe_out = lax.psum(branch_sum.astype(jnp.bfloat16), "tensor").astype(jnp.float32)
    mixed = (hidden + moe_out).astype(brain_float16)
    grad_y = cotangent.astype(f32)
    sdown_grad = contract_rows(shared_act, cotangent)
    grad_sact = contract_cols(cotangent, sdown_w)
    grad_sgate, grad_sup = gated_linear_backward(shared_gu[0], shared_gu[1], grad_sact)
    grad_sgu = jnp.stack([grad_sgate, grad_sup], axis=0).astype(brain_float16)
    sgu_grad = jnp.einsum("td,gtf->gdf", hnormed_b, grad_sgu, preferred_element_type=f32)
    grad_hn_part = jnp.einsum("gtf,gdf->td", grad_sgu, sgate_up, preferred_element_type=f32)
    gate_columns = []
    for route_idx in range(route_count):
        gate_columns.append(jnp.sum(grad_y * returned[:, route_idx].astype(f32), axis=1))
    gate_part = jnp.stack(gate_columns, axis=1)
    slot_grads = (
        (gate_vals[:, :, None] * grad_y[:, None, :])
        .reshape(tok_rows * route_count, model_width)
        .astype(brain_float16)
    )
    grad_sent = jnp.where(is_filled, slot_grads[source], 0).reshape(
        expert_count, capacity, model_width
    )
    grad_received = to_owner(grad_sent)
    edown_grad = jnp.einsum("erf,erd->efd", expert_act, grad_received, preferred_element_type=f32)
    expert_activation_gradient = jnp.einsum(
        "erd,efd->erf", grad_received, expert_down, preferred_element_type=f32
    )
    expert_gate_gradient, expert_up_gradient = gated_linear_backward(
        gate_up_joined[:, 0], gate_up_joined[:, 1], expert_activation_gradient
    )
    expert_gate_up_gradient = jnp.stack([expert_gate_gradient, expert_up_gradient], axis=1).astype(
        brain_float16
    )
    egu_grad = jnp.einsum(
        "erd,egrf->egdf", received, expert_gate_up_gradient, preferred_element_type=f32
    )
    grad_rows = jnp.einsum(
        "egrf,egdf->erd", expert_gate_up_gradient, expert_gate_up, preferred_element_type=f32
    ).astype(brain_float16)
    grad_back = lax.all_to_all(grad_rows, "expert", split_axis=1, concat_axis=0, tiled=True)
    grad_routes = grad_back.reshape(expert_count * capacity, model_width)[slot_ids].reshape(
        tok_rows, route_count, model_width
    )
    for route_idx in range(route_count):
        grad_hn_part = grad_hn_part + grad_routes[:, route_idx].astype(f32)
    gate_grads = lax.psum(gate_part, "tensor")
    grad_chosen = ROUTE_SCALE * (
        gate_grads / chosen_sum
        - jnp.sum(gate_grads * chosen, axis=1, keepdims=True) / (chosen_sum * chosen_sum)
    )
    grad_sig = jnp.sum(jnp.where(route_hot, grad_chosen[:, :, None], 0.0), axis=1)
    grad_logits = (grad_sig * sigmoid_vals * (1.0 - sigmoid_vals)).astype(brain_float16)
    router_grad = contract_rows(hnormed_b, grad_logits)
    grad_hn = lax.psum(grad_hn_part, "tensor") + contract_cols(grad_logits, router_w)
    grad_hidden_norm, gain_two_grad = rms_backward(hidden, scale_two, gain_two.astype(f32), grad_hn)
    grad_hidden = grad_y + grad_hidden_norm
    grad_hidden_b = grad_hidden.astype(brain_float16)
    out_grad = contract_rows(attended_b, grad_hidden_b)
    grad_att = (
        contract_cols(grad_hidden_b, out_w).reshape(tok_rows, local_heads, DV).astype(brain_float16)
    )
    probs = jnp.exp(score_block() - log_total)
    probs_again = probs.astype(brain_float16)
    grad_probs = jnp.einsum("qhd,khd->hqk", grad_att, values, preferred_element_type=f32)
    grad_vals = jnp.einsum("hqk,qhd->khd", probs_again, grad_att, preferred_element_type=f32)
    row_delta = jnp.sum(probs * grad_probs, axis=-1, keepdims=True)
    grad_scores = (probs * (grad_probs - row_delta)).astype(brain_float16)
    grad_q = jnp.einsum("hqk,khd->qhd", grad_scores, key_all, preferred_element_type=f32) * q_scale
    grad_keys = jnp.einsum("hqk,qhd->khd", grad_scores, q_all, preferred_element_type=f32) * q_scale
    grad_kv = (
        jnp.concatenate([grad_keys[..., :DN], grad_vals], axis=-1)
        .reshape(tok_rows, local_heads * (DN + DV))
        .astype(brain_float16)
    )
    kv_grad = contract_rows(compressed_b, grad_kv)
    grad_comp_part = contract_cols(grad_kv, kv_w)
    grad_krope_part = jnp.sum(grad_keys[..., DN:], axis=1)
    grad_comp, grad_krope = (
        lax.psum(grad_comp_part.astype(jnp.bfloat16), "tensor").astype(jnp.float32),
        lax.psum(grad_krope_part.astype(jnp.bfloat16), "tensor").astype(jnp.float32),
    )
    grad_c, latent_gain_grad = rms_backward(
        latent[:, :rank_width], scale_kv, latent_g.astype(f32), grad_comp
    )
    grad_latent = jnp.concatenate([grad_c, unrotate(grad_krope, cosine, sine_tab)], axis=-1).astype(
        brain_float16
    )
    grad_qrot = unrotate(grad_q[..., DN:], cosine[:, None, :], sine_tab[:, None, :])
    grad_queries = (
        jnp.concatenate([grad_q[..., :DN], grad_qrot], axis=-1)
        .reshape(tok_rows, local_heads * (DN + DR))
        .astype(brain_float16)
    )
    query_grad = contract_rows(normed_b, grad_queries)
    latent_grad = contract_rows(normed_b, grad_latent)
    grad_normed = lax.psum(
        contract_cols(grad_queries, query_w).astype(jnp.bfloat16), "tensor"
    ).astype(jnp.float32) + contract_cols(grad_latent, latent_w)
    grad_x_norm, gain_one_grad = rms_backward(x_float, scale_one, gain_one.astype(f32), grad_normed)
    input_grad = grad_hidden + grad_x_norm
    first_owned = (
        *sent_together(
            (
                gain_one_grad.astype(jnp.bfloat16),
                query_grad.astype(jnp.bfloat16),
                latent_grad.astype(jnp.bfloat16),
            ),
            "expert",
            0,
            1,
        ),
        *sent_together(
            (latent_gain_grad.astype(jnp.bfloat16), kv_grad.astype(jnp.bfloat16)), "expert", 0, 1
        ),
    )
    second_owned = (
        lax.psum_scatter(out_grad, "expert", scatter_dimension=1, tiled=True),
        lax.psum_scatter(gain_two_grad, "expert", scatter_dimension=0, tiled=True),
        lax.psum_scatter(router_grad, "expert", scatter_dimension=0, tiled=True),
        lax.psum_scatter(sgu_grad, "expert", scatter_dimension=1, tiled=True),
        lax.psum_scatter(sdown_grad, "expert", scatter_dimension=1, tiled=True),
    )
    return (
        mixed,
        input_grad,
        first_owned[0],
        first_owned[1],
        first_owned[2],
        first_owned[3],
        first_owned[4],
        second_owned[0],
        second_owned[1],
        second_owned[2],
        second_owned[3],
        second_owned[4],
        egu_grad,
        edown_grad,
    )


def swap_cores(value):
    return lax.ppermute(value, "tensor", [(0, 1), (1, 0)])


def take_rows(value, start, count, axis=0):
    return lax.dynamic_slice_in_dim(value, start, count, axis=axis)


def in_order(core, own, other, axis=0):
    return jnp.where(
        core == 0,
        jnp.concatenate([own, other], axis=axis),
        jnp.concatenate([other, own], axis=axis),
    )


def add_wide(*parts):
    total = parts[0].astype(jnp.float32)
    for part in parts[1:]:
        total = total + part.astype(jnp.float32)
    return total


PLANE = 4


def to_partner(value, flips):
    groups = lax.axis_size("expert")
    return lax.ppermute(value, "expert", [(g, g ^ flips) for g in range(groups)])


def to_deeper(value, step):
    groups = lax.axis_size("expert")
    pairs = [(g, (g + step * PLANE) % groups) for g in range(groups)]
    return lax.ppermute(value, "expert", pairs)


def plane_gather(value):
    return [value] + [to_partner(value, r) for r in range(1, PLANE)]


def plane_scatter(parts):
    return add_wide(parts[0], *[to_partner(parts[r], r) for r in range(1, PLANE)])


def by_place(parts, place):
    odd, high = place % 2 == 1, place // 2 == 1
    parts = [jnp.where(odd, parts[i ^ 1], parts[i]) for i in range(PLANE)]
    return [jnp.where(high, parts[i ^ 2], parts[i]) for i in range(PLANE)]


def tie(*values):
    return lax.optimization_barrier(values)


def deep_pieces(value):
    deep = lax.axis_size("expert") // PLANE
    return [to_deeper(value, s) for s in range(1, deep)]


def one_plane(value, step):
    groups = lax.axis_size("expert")
    pairs = [(g, g + step * PLANE) for g in range(groups) if 0 <= g + step * PLANE < groups]
    return lax.ppermute(value, "expert", pairs)


def deep_hops(value):
    deep = lax.axis_size("expert") // PLANE
    after, before, down, up = [], [], value, value
    for _ in range(1, deep):
        down, up = one_plane(down, 1), one_plane(up, -1)
        after.append(down)
        before.append(up)
    return after, before


def join_hops(hops):
    after, before = hops
    return [a + b for a, b in zip(after, before[::-1])]


def deep_join(value, pieces, z):
    deep = lax.axis_size("expert") // PLANE
    whole = jnp.zeros((deep, *value.shape), value.dtype)
    whole = lax.dynamic_update_index_in_dim(whole, value, z, 0)
    for step in range(1, deep):
        whole = lax.dynamic_update_index_in_dim(whole, pieces[step - 1], (z - step) % deep, 0)
    return whole


def deep_move(blocks, z):
    deep = blocks.shape[0]

    def block(index):
        return lax.dynamic_index_in_dim(blocks, index, 0, keepdims=False)

    return [block(z)] + [to_deeper(block((z + step) % deep), step) for step in range(1, deep)]


def deep_scatter(blocks, z):
    return add_wide(*deep_move(blocks, z))


def share_columns(rows, place):
    parts = [at_index(rows, 0, place)]
    for r in range(1, PLANE):
        parts.append(to_partner(at_index(rows, 0, place ^ r), r))
    return by_place(parts, place)


def all_groups(value):
    return lax.all_gather(value, "expert", axis=0, tiled=False)


def at_index(value, axis, index):
    return lax.dynamic_index_in_dim(value, index, axis, keepdims=False)


def doc_places(doc_lengths, row_count):
    ends_at = jnp.cumsum(doc_lengths)
    position = jnp.arange(row_count, dtype=jnp.int32)
    doc_ids = jnp.sum((position[:, None] >= ends_at[None, :]).astype(jnp.int32), axis=1)
    hitting = doc_ids[:, None] == jnp.arange(doc_lengths.shape[0], dtype=jnp.int32)[None, :]
    start_of = jnp.sum(jnp.where(hitting, (ends_at - doc_lengths)[None, :], 0), axis=1)
    return position - start_of, doc_ids


class HopSum:
    def __init__(self, pieces):
        self.groups = lax.axis_size("expert")
        self.deep = self.groups // PLANE
        self.z = lax.axis_index("expert") // PLANE
        self.pieces = pieces

    def hop(self, step, came=None):
        arrived = []
        for side, way in enumerate((1, -1)):
            target = jnp.clip(self.z + way * (self.deep - step), 0, self.deep - 1)
            gone = self.pieces(target)
            if came is not None:
                gone = add_wide(gone, came[side]).astype(gone.dtype)
            first = range(step) if way == 1 else range(self.deep - step, self.deep)
            pairs = [
                (p * PLANE + q, (p + way) * PLANE + q) for p in first for q in range(PLANE)
            ]
            arrived.append(lax.ppermute(gone, "expert", pairs))
        return arrived

    def total(self, came):
        return add_wide(self.pieces(self.z), *came)


def doc_places(doc_lengths, row_count):
    ends_at = jnp.cumsum(doc_lengths)
    position = jnp.arange(row_count, dtype=jnp.int32)
    doc_ids = jnp.sum((position[:, None] >= ends_at[None, :]).astype(jnp.int32), axis=1)
    hitting = doc_ids[:, None] == jnp.arange(doc_lengths.shape[0], dtype=jnp.int32)[None, :]
    start_of = jnp.sum(jnp.where(hitting, (ends_at - doc_lengths)[None, :], 0), axis=1)
    return position - start_of, doc_ids


def hop_sum(pieces):
    groups = lax.axis_size("expert")
    deep = groups // PLANE
    z = lax.axis_index("expert") // PLANE
    ends = []
    for way in (1, -1):
        came = None
        for step in range(1, deep):
            gone = pieces(jnp.clip(z + way * (deep - step), 0, deep - 1))
            if came is not None:
                gone = add_wide(gone, came).astype(gone.dtype)
            first = range(step) if way == 1 else range(deep - step, deep)
            pairs = [
                (p * PLANE + q, (p + way) * PLANE + q) for p in first for q in range(PLANE)
            ]
            came = lax.ppermute(gone, "expert", pairs)
        ends.append(came)
    return [pieces(z), *ends]


class RowGather:
    def __init__(self, value):
        self.cut = value.shape[0] // 2
        self.value = value

    def along(self):
        return [self.value] + deep_pieces(self.value)

    def beside(self, line):
        return to_partner(line, 1), to_partner(line, 2)

    def far(self, beside):
        return to_partner(beside[0][:, : self.cut], 2), to_partner(beside[1][:, self.cut :], 1)


class RowSum:
    def __init__(self, *terms):
        self.type = terms[0][0].dtype
        cut = terms[0][0].shape[1] // 2
        self.halves = (
            ([[b[:, :cut] for b in v] for v in terms], 2, 1),
            ([[b[:, cut:] for b in v] for v in terms], 1, 2),
        )

    def _add(self, parts):
        return add_wide(*parts).astype(self.type)

    def sends(self):
        return [
            jnp.stack([self._add([v[far] for v in held]), self._add([v[far | near] for v in held])])
            for held, far, near in self.halves
        ]

    def move(self, sends):
        return [to_partner(v, far) for v, (_, far, _) in zip(sends, self.halves)]

    def sends_again(self, came):
        return [
            self._add([v[near] for v in held] + [c[1]])
            for c, (held, _, near) in zip(came, self.halves)
        ]

    def move_again(self, sends):
        return [to_partner(v, near) for v, (_, _, near) in zip(sends, self.halves)]

    def line(self, came, came_again):
        sums = [
            self._add([v[0] for v in held] + [c[0], d])
            for c, d, (held, *_) in zip(came, came_again, self.halves)
        ]
        return jnp.concatenate(sums, axis=1)


def line_sends(line):
    return [line[step] for step in range(line.shape[0])]


def line_move(sends):
    return [sends[0]] + [to_deeper(v, -step) for step, v in enumerate(sends) if step > 0]


def dot_nn(left, right):
    return lax.dot_general(left, right, (((1,), (0,)), ((), ())), preferred_element_type=jnp.float32)


def dot_nt(left, right):
    return lax.dot_general(left, right, (((1,), (1,)), ((), ())), preferred_element_type=jnp.float32)


def dot_tn(left, right):
    return lax.dot_general(left, right, (((0,), (0,)), ((), ())), preferred_element_type=jnp.float32)


def two_lanes(column, lane):
    high = column.astype(jnp.bfloat16).astype(jnp.float32)
    spread = jnp.where(lane == 0, high, jnp.where(lane == 1, column - high, 0.0))
    return spread.astype(jnp.bfloat16)


def expert_kernel(
    shared_cols,
    expert_count,
    me_ref,
    hn_own,
    hn_other,
    dy_own,
    dy_other,
    meta_own,
    meta_other,
    gate_up_w,
    down_w,
    first_w,
    sdown_w,
    slots_out,
    slot_dy_out,
    act_out,
    d_gate_up_out,
    rows_own_out,
    rows_other_out,
    sact_own_out,
    sact_other_out,
    shared_grads_out,
    dgate_own_out,
    dgate_other_out,
):
    f32, bf16 = jnp.float32, jnp.bfloat16
    count, half, _ = hn_own.shape
    tokens = 2 * half
    me = me_ref[0]
    lane = lax.broadcasted_iota(jnp.int32, (count * tokens, LANES), 1)
    is_router = (lane >= shared_cols) & (lane < shared_cols + expert_count)
    first = first_w[...]

    def joined(own, other):
        return jnp.concatenate([v[i] for i in range(count) for v in (own, other)], axis=0)

    rows, rows_dy = joined(hn_own, hn_other), joined(dy_own, dy_other)
    meta = joined(meta_own, meta_other)
    products = dot_nt(rows, first)
    gate, up = products[:, :LANES], products[:, LANES:]
    sig = jax.nn.sigmoid(gate)
    total = jnp.sum(jnp.where(is_router, sig * meta, 0.0), axis=1, keepdims=True)
    mine = jnp.sum(jnp.where(lane == shared_cols + me, sig, 0.0), axis=1, keepdims=True)
    token_gate = two_lanes(ROUTE_SCALE * mine / total, lane)
    sact = (gate * sig * up).astype(bf16)
    d_sact = dot_nt(rows_dy, sdown_w[...])
    d_sgate = d_sact * up * sig * (1.0 + gate * (1.0 - sig))
    dsh = jnp.concatenate([d_sgate, d_sact * gate * sig], axis=1).astype(bf16)
    pick = (meta[:, :1] == lane.astype(f32)).astype(bf16)
    groups = [slice(i * tokens, (i + 1) * tokens) for i in range(count)]
    for i in range(count):
        start = i * tokens
        sact_own_out[i] = sact[start : start + half]
        sact_other_out[i] = sact[start + half : start + tokens]
    slots = [dot_tn(pick[g], rows[g]).astype(bf16) for g in groups]
    slot_dys = [dot_tn(pick[g], rows_dy[g]).astype(bf16) for g in groups]
    slot_gates = [
        jnp.sum(dot_tn(pick[g], token_gate[g]), axis=1, keepdims=True) for g in groups
    ]

    @pl.when(pl.program_id(0) == 0)
    def _():
        shared_grads_out[...] = jnp.zeros_like(shared_grads_out)

    first_grad, sdown_grad = dot_tn(dsh, rows), dot_tn(sact, rows_dy)
    shared_grads_out[:shared_cols] += first_grad[:shared_cols]
    shared_grads_out[shared_cols : 2 * shared_cols] += first_grad[LANES : LANES + shared_cols]
    shared_grads_out[2 * shared_cols :] += sdown_grad[:shared_cols]
    slot_rows = jnp.concatenate(slots, axis=0)
    slot_dy = jnp.concatenate(slot_dys, axis=0)
    slot_gate = jnp.concatenate(slot_gates, axis=0)
    slots_out[...] = slot_rows
    slot_dy_out[...] = slot_dy
    gate = dot_nt(slot_rows, gate_up_w[0])
    up = dot_nt(slot_rows, gate_up_w[1])
    d_act = dot_nt(slot_dy, down_w[...])
    sig = jax.nn.sigmoid(gate)
    silu = gate * sig
    act = silu * up
    slot_dgate = jnp.sum(act * d_act, axis=1, keepdims=True)
    act_out[...] = (slot_gate * act).astype(bf16)
    d_act = slot_gate * d_act
    d_gate = (d_act * up * sig * (1.0 + gate * (1.0 - sig))).astype(bf16)
    d_up = (d_act * silu).astype(bf16)
    d_gate_up_out[0] = d_gate
    d_gate_up_out[1] = d_up
    d_slots = (dot_nn(d_gate, gate_up_w[0]) + dot_nn(d_up, gate_up_w[1])).astype(bf16)
    slot_lane = lax.broadcasted_iota(jnp.int32, (LANES, LANES), 1)
    d_shared = dot_nn(dsh, first)
    for i, g in enumerate(groups):
        here = slice(i * LANES, (i + 1) * LANES)
        d_rows = (dot_nn(pick[g], d_slots[here]) + d_shared[g]).astype(bf16)
        rows_own_out[i], rows_other_out[i] = d_rows[:half], d_rows[half:]
        dgate = dot_nn(pick[g], two_lanes(slot_dgate[here], slot_lane))
        dgate_own_out[i], dgate_other_out[i] = dgate[:half], dgate[half:]


def block_specs(per_step):
    def lead(*tail):
        return pl.BlockSpec((per_step, *tail), lambda i: (i,) + (0,) * len(tail))

    def flat(cols):
        return pl.BlockSpec((per_step * LANES, cols), lambda i: (i, 0))

    def whole(a):
        return pl.BlockSpec(a.shape, lambda i: (0,) * a.ndim, pipeline_mode=pl.Buffered(1))

    return lead, flat, whole


def experts(
    me,
    hn_own,
    hn_other,
    dy_own,
    dy_other,
    meta_own,
    meta_other,
    gate_up_w,
    down_w,
    first_w,
    sdown_w,
    shared_cols,
    expert_count,
    per_step=2,
):
    groups, half, width = hn_own.shape
    hidden = down_w.shape[0]
    slots = groups * LANES
    f32, bf16 = jnp.float32, jnp.bfloat16
    lead, flat, whole = block_specs(per_step)
    sds = jax.ShapeDtypeStruct
    return pl.pallas_call(
        functools.partial(expert_kernel, shared_cols, expert_count),
        grid=(groups // per_step,),
        in_specs=[
            pl.BlockSpec(memory_space=pltpu.SMEM),
            *[lead(half, width)] * 4,
            *[lead(half, LANES)] * 2,
            *[whole(a) for a in (gate_up_w, down_w, first_w, sdown_w)],
        ],
        out_specs=[
            flat(width),
            flat(width),
            flat(hidden),
            pl.BlockSpec((2, per_step * LANES, hidden), lambda i: (0, i, 0)),
            *[lead(half, width)] * 2,
            *[lead(half, LANES)] * 2,
            pl.BlockSpec((3 * shared_cols, width), lambda i: (0, 0)),
            *[lead(half, LANES)] * 2,
        ],
        out_shape=[
            sds((slots, width), bf16),
            sds((slots, width), bf16),
            sds((slots, hidden), bf16),
            sds((2, slots, hidden), bf16),
            *[sds((groups, half, width), bf16)] * 2,
            *[sds((groups, half, LANES), bf16)] * 2,
            sds((3 * shared_cols, width), f32),
            *[sds((groups, half, LANES), f32)] * 2,
        ],
        compiler_params=pltpu.CompilerParams(vmem_limit_bytes=58 * 1024 * 1024),
        cost_estimate=pl.CostEstimate(
            flops=groups * width, bytes_accessed=groups * width, transcendentals=0
        ),
    )(
        me,
        hn_own,
        hn_other,
        dy_own,
        dy_other,
        meta_own,
        meta_other,
        gate_up_w,
        down_w,
        first_w,
        sdown_w,
    )


def swap_halves(value, lane):
    low = lane % DR < DR // 2
    return jnp.where(low, pltpu.roll(value, LANES - DR // 2, 1), pltpu.roll(value, DR // 2, 1))


def by_core(core, first, second):
    return jnp.where(core == 0, first, second), jnp.where(core == 0, second, first)


def head_scores(q, kv, k_rope, visible, lane, head, heads):
    q_nope = q[:, head * DN : (head + 1) * DN]
    q_rope = jnp.where(lane // DR == head, q[:, heads * DN :], jnp.zeros((), q.dtype))
    at = head * (DN + DV)
    k_nope, value = kv[:, at : at + DN], kv[:, at + DN : at + DN + DV]
    scores = (dot_nt(q_nope, k_nope) + dot_nt(q_rope, k_rope)) * (DN + DR) ** -0.5
    return jnp.where(visible, scores, NEGATIVE), q_nope, q_rope, k_nope, value


def seen(doc_col, doc_row):
    rows = doc_col.shape[0]
    later = lax.broadcasted_iota(jnp.int32, (rows, rows), 0) >= lax.broadcasted_iota(
        jnp.int32, (rows, rows), 1
    )
    return (doc_col == doc_row) & later


def attention_kernel(
    heads,
    rank,
    core_ref,
    x_own,
    x_other,
    gain,
    latent_gain,
    head_w,
    small_w,
    kv_w,
    cosine,
    sine,
    doc_col,
    doc_row,
    normed_out,
    compressed_out,
    q_out,
    kv_out,
    k_rope_out,
    sums_out,
    attended_out,
    latent_out,
    part_own_out,
    part_other_out,
):
    f32, bf16 = jnp.float32, jnp.bfloat16
    core = core_ref[0]
    x = jnp.concatenate(by_core(core, x_own[0], x_other[0]), axis=0).astype(f32)
    rows = x.shape[0]
    half = rows // 2
    lane = lax.broadcasted_iota(jnp.int32, (rows, LANES), 1)
    inverse = lax.rsqrt(jnp.mean(x * x, axis=1, keepdims=True) + EPSILON)
    normed = (x * inverse * gain[...]).astype(bf16)
    normed_out[0] = normed
    q_cols = heads * (DN + DR)
    queries = dot_nn(normed, head_w[:, :q_cols])
    q_rope = queries[:, heads * DN :]
    q_rope = q_rope * cosine[0] + swap_halves(q_rope, lane) * sine[0]
    q = jnp.concatenate([queries[:, : heads * DN], q_rope], axis=1).astype(bf16)
    q_out[0] = q
    latent = dot_nn(normed, small_w[:, : rank + LANES])
    latent_out[0] = latent
    squeezed = latent[:, :rank]
    inverse = lax.rsqrt(jnp.mean(squeezed * squeezed, axis=1, keepdims=True) + EPSILON)
    compressed = (squeezed * inverse * latent_gain[...]).astype(bf16)
    compressed_out[0] = compressed
    k_rope = latent[:, rank:]
    k_rope = (k_rope * cosine[0] + swap_halves(k_rope, lane) * sine[0]).astype(bf16)
    k_rope_out[0] = k_rope
    kv = dot_nn(compressed, kv_w[...]).astype(bf16)
    kv_out[0] = kv
    visible = seen(doc_col[0], doc_row[0])
    attended, sums = [], jnp.zeros((rows, LANES), f32)
    for head in range(heads):
        scores, *_, value = head_scores(q, kv, k_rope, visible, lane, head, heads)
        top = jnp.max(scores, axis=1, keepdims=True)
        log_total = top + jnp.log(jnp.sum(jnp.exp(scores - top), axis=1, keepdims=True))
        sums = jnp.where(lane == head, log_total, sums)
        probs = jnp.exp(scores - log_total).astype(bf16)
        attended.append(dot_nn(probs, value).astype(bf16))
    sums_out[0] = sums
    attended = jnp.concatenate(attended, axis=1)
    attended_out[0] = attended
    part = dot_nt(attended, head_w[:, q_cols : q_cols + heads * DV]).astype(bf16)
    part_own_out[0], part_other_out[0] = by_core(core, part[:half], part[half:])


def attention_backward_kernel(
    heads,
    core_ref,
    d_own,
    d_other,
    normed_ref,
    compressed_ref,
    q_ref,
    kv_ref,
    k_rope_ref,
    sums_ref,
    attended_ref,
    head_w,
    kv_w,
    cosine,
    sine,
    doc_col,
    doc_row,
    head_grad_out,
    kv_grad_out,
    normed_own_out,
    normed_other_out,
    latent_own_out,
    latent_other_out,
    head_acc,
    kv_acc,
):
    f32, bf16 = jnp.float32, jnp.bfloat16
    core, step = core_ref[0], pl.program_id(0)
    scale = (DN + DR) ** -0.5
    d_rows = jnp.concatenate(by_core(core, d_own[0], d_other[0]), axis=0)
    rows = d_rows.shape[0]
    half = rows // 2
    lane = lax.broadcasted_iota(jnp.int32, (rows, LANES), 1)
    q_cols = heads * (DN + DR)
    q, kv, k_rope = q_ref[0], kv_ref[0], k_rope_ref[0]
    d_attended = dot_nn(d_rows, head_w[:, q_cols : q_cols + heads * DV]).astype(bf16)
    visible = seen(doc_col[0], doc_row[0])
    d_q, d_kv = [], []
    d_q_rope, d_k_rope = jnp.zeros((rows, LANES), f32), jnp.zeros((rows, LANES), f32)
    for head in range(heads):
        scores, q_nope, q_rope, k_nope, value = head_scores(
            q, kv, k_rope, visible, lane, head, heads
        )
        probs = jnp.exp(scores - sums_ref[0][:, head : head + 1])
        d_head = d_attended[:, head * DV : (head + 1) * DV]
        d_probs = dot_nt(d_head, value)
        d_value = dot_tn(probs.astype(bf16), d_head)
        delta = jnp.sum(probs * d_probs, axis=1, keepdims=True)
        d_scores = (probs * (d_probs - delta)).astype(bf16)
        d_q.append(dot_nn(d_scores, k_nope) * scale)
        d_q_rope = jnp.where(lane // DR == head, dot_nn(d_scores, k_rope) * scale, d_q_rope)
        d_kv += [dot_tn(d_scores, q_nope) * scale, d_value]
        d_k_rope += dot_tn(d_scores, q_rope) * scale
    d_q_rope = d_q_rope * cosine[0] - swap_halves(d_q_rope, lane) * sine[0]
    d_q = jnp.concatenate(d_q + [d_q_rope], axis=1).astype(bf16)
    d_kv = jnp.concatenate(d_kv, axis=1).astype(bf16)

    @pl.when(step == 0)
    def _():
        head_acc[...] = jnp.zeros_like(head_acc)
        kv_acc[...] = jnp.zeros_like(kv_acc)

    head_acc[:, :q_cols] += dot_tn(normed_ref[0], d_q)
    head_acc[:, q_cols:] += dot_tn(d_rows, attended_ref[0])
    kv_acc[...] += dot_tn(compressed_ref[0], d_kv)

    @pl.when(step == pl.num_programs(0) - 1)
    def _():
        head_grad_out[...] = head_acc[...].astype(bf16)
        kv_grad_out[...] = kv_acc[...].astype(bf16)

    part = dot_nt(d_q, head_w[:, :q_cols]).astype(bf16)
    normed_own_out[0], normed_other_out[0] = by_core(core, part[:half], part[half:])
    latent = jnp.concatenate([dot_nt(d_kv, kv_w[...]), d_k_rope], axis=1).astype(bf16)
    latent_own_out[0], latent_other_out[0] = by_core(core, latent[:half], latent[half:])


def one_each(*tail):
    return pl.BlockSpec((1, *tail), lambda i: (i,) + (0,) * len(tail))


def kept(value):
    return pl.BlockSpec(value.shape, lambda i: (0,) * value.ndim, pipeline_mode=pl.Buffered(1))


def attention(core, x_own, x_other, gain, latent_gain, head_w, small_w, kv_w, cosine, sine, doc):
    near, half, width = x_own.shape
    rows = 2 * half
    rank, kv_cols = kv_w.shape
    heads = kv_cols // (DN + DV)
    f32, bf16 = jnp.float32, jnp.bfloat16
    shapes = [
        ((rows, width), bf16),
        ((rows, rank), bf16),
        ((rows, heads * (DN + DR)), bf16),
        ((rows, kv_cols), bf16),
        ((rows, LANES), bf16),
        ((rows, LANES), f32),
        ((rows, heads * DV), bf16),
        ((rows, rank + LANES), f32),
        ((half, width), bf16),
        ((half, width), bf16),
    ]
    return pl.pallas_call(
        functools.partial(attention_kernel, heads, rank),
        grid=(near,),
        in_specs=[
            pl.BlockSpec(memory_space=pltpu.SMEM),
            *[one_each(half, width)] * 2,
            *[kept(a) for a in (gain, latent_gain, head_w, small_w, kv_w)],
            *[one_each(rows, LANES)] * 2,
            one_each(rows, 1),
            one_each(1, rows),
        ],
        out_specs=[one_each(*shape) for shape, _ in shapes],
        out_shape=[jax.ShapeDtypeStruct((near, *shape), kind) for shape, kind in shapes],
        compiler_params=pltpu.CompilerParams(vmem_limit_bytes=58 * 1024 * 1024),
        cost_estimate=pl.CostEstimate(
            flops=2 * near * rows * width * (rank + 3 * heads * DN),
            bytes_accessed=4 * near * rows * width,
            transcendentals=0,
        ),
    )(
        core,
        x_own,
        x_other,
        gain,
        latent_gain,
        head_w,
        small_w,
        kv_w,
        cosine,
        sine,
        doc[:, :, None],
        doc[:, None, :],
    )


def attention_backward(core, d_own, d_other, kept_rows, head_w, kv_w, cosine, sine, doc):
    near, half, width = d_own.shape
    rows = 2 * half
    rank, kv_cols = kv_w.shape
    heads = kv_cols // (DN + DV)
    head_cols = heads * (DN + DR + DV)
    f32, bf16 = jnp.float32, jnp.bfloat16
    sds = jax.ShapeDtypeStruct
    return pl.pallas_call(
        functools.partial(attention_backward_kernel, heads),
        grid=(near,),
        in_specs=[
            pl.BlockSpec(memory_space=pltpu.SMEM),
            *[one_each(half, width)] * 2,
            *[one_each(*v.shape[1:]) for v in kept_rows],
            *[kept(a) for a in (head_w, kv_w)],
            *[one_each(rows, LANES)] * 2,
            one_each(rows, 1),
            one_each(1, rows),
        ],
        out_specs=[
            pl.BlockSpec((width, head_cols), lambda i: (0, 0)),
            pl.BlockSpec((rank, kv_cols), lambda i: (0, 0)),
            *[one_each(half, width)] * 2,
            *[one_each(half, rank + LANES)] * 2,
        ],
        out_shape=[
            sds((width, head_cols), bf16),
            sds((rank, kv_cols), bf16),
            *[sds((near, half, width), bf16)] * 2,
            *[sds((near, half, rank + LANES), bf16)] * 2,
        ],
        scratch_shapes=[
            pltpu.VMEM((width, head_cols), f32),
            pltpu.VMEM((rank, kv_cols), f32),
        ],
        compiler_params=pltpu.CompilerParams(vmem_limit_bytes=58 * 1024 * 1024),
        cost_estimate=pl.CostEstimate(
            flops=near * rows * width * heads * DN,
            bytes_accessed=2 * near * rows * width,
            transcendentals=0,
        ),
    )(
        core,
        d_own,
        d_other,
        *kept_rows,
        head_w,
        kv_w,
        cosine,
        sine,
        doc[:, :, None],
        doc[:, None, :],
    )


def product_kernel(*refs):
    *operands, out_ref = refs
    count = len(operands) // 2
    total = 0.0
    for left_ref, right_ref in zip(operands[:count], operands[count:]):
        total += dot_tn(left_ref[0], right_ref[...])
    out_ref[0] = total


def column_products(lefts, rights, tile=512):
    count, _, height = lefts[0].shape
    width = rights[0].shape[1]
    return pl.pallas_call(
        product_kernel,
        grid=(width // tile, count),
        in_specs=[
            *[pl.BlockSpec((1, v.shape[1], height), lambda j, i: (i, 0, 0)) for v in lefts],
            *[pl.BlockSpec((v.shape[0], tile), lambda j, i: (0, j)) for v in rights],
        ],
        out_specs=pl.BlockSpec((1, height, tile), lambda j, i: (i, 0, j)),
        out_shape=jax.ShapeDtypeStruct((count, height, width), jnp.float32),
        compiler_params=pltpu.CompilerParams(vmem_limit_bytes=58 * 1024 * 1024),
        cost_estimate=pl.CostEstimate(flops=width, bytes_accessed=width, transcendentals=0),
    )(*lefts, *rights)


def output_kernel(act, sact_own, sact_other, meta_own, meta_other, down_w, sdown_w, own_out, other_out):
    f32, bf16 = jnp.float32, jnp.bfloat16
    count, half, _ = meta_own.shape
    lane = lax.broadcasted_iota(jnp.int32, (2 * half, LANES), 1).astype(f32)
    out = dot_nn(act[...], down_w[...]).astype(bf16)
    for i in range(count):
        meta = jnp.concatenate([meta_own[i], meta_other[i]], axis=0)
        pick = (meta[:, :1] == lane).astype(bf16)
        sact = jnp.concatenate([sact_own[i], sact_other[i]], axis=0)
        here = slice(i * LANES, (i + 1) * LANES)
        rows = (dot_nn(pick, out[here]) + dot_nn(sact, sdown_w[...])).astype(bf16)
        own_out[i], other_out[i] = rows[:half], rows[half:]


def outputs(act, sact_own, sact_other, meta_own, meta_other, down_w, sdown_w, per_step=4):
    groups, half, _ = meta_own.shape
    hidden, width = down_w.shape
    lead, flat, whole = block_specs(per_step)
    return pl.pallas_call(
        output_kernel,
        grid=(groups // per_step,),
        in_specs=[
            flat(hidden),
            *[lead(half, LANES)] * 4,
            *[whole(a) for a in (down_w, sdown_w)],
        ],
        out_specs=[lead(half, width)] * 2,
        out_shape=[jax.ShapeDtypeStruct((groups, half, width), jnp.bfloat16)] * 2,
        compiler_params=pltpu.CompilerParams(vmem_limit_bytes=58 * 1024 * 1024),
        cost_estimate=pl.CostEstimate(
            flops=groups * half * LANES * width,
            bytes_accessed=groups * half * width,
            transcendentals=0,
        ),
    )(act, sact_own, sact_other, meta_own, meta_other, down_w, sdown_w)


def token_plan(
    inputs,
    attn_gain,
    w_query,
    w_latent,
    latent_gain,
    w_kv,
    w_out,
    ffn_gain,
    w_router,
    shared_gate_up,
    shared_down,
    expert_gate_up,
    expert_down,
    lengths,
    routes,
    cotangent,
):
    f32, bf16 = jnp.float32, jnp.bfloat16
    core, me = lax.axis_index("tensor"), lax.axis_index("expert")
    groups = lax.axis_size("expert")
    deep, place, z = groups // PLANE, me % PLANE, me // PLANE
    tok_rows, width = inputs.shape
    half = tok_rows // 2
    own_at, other_at = core * half, (1 - core) * half
    expert_count = w_router.shape[1]
    route_count = routes.shape[1]
    capacity = tok_rows * route_count * 4 // (3 * expert_count)
    shared_cols = shared_gate_up.shape[2] // groups
    latent_cols, rank_width = w_latent.shape[1], latent_gain.shape[0] * groups
    block_rows = w_query.shape[0]
    kv_rows = w_kv.shape[0]

    query_cols = w_query.shape[1] // PLANE
    out_cols = w_out.shape[0] // PLANE
    small = jnp.concatenate(
        [
            w_latent,
            w_latent[:, rank_width:],
            w_router,
            attn_gain[:, None],
            ffn_gain[:, None],
            jnp.pad(latent_gain, (0, block_rows - kv_rows))[:, None],
        ],
        axis=1,
    )
    small_cols = small.shape[1]
    route_half = take_rows(routes, own_at, half).astype(bf16).reshape(block_rows // 2, -1)
    length_col = jnp.pad(lengths[0].astype(bf16), (0, block_rows // 2 - lengths.shape[1]))[:, None]
    route_cols = route_half.shape[1] + 1
    small_half = jnp.concatenate(
        [
            take_rows(small, core * (block_rows // 2), block_rows // 2),
            route_half,
            length_col,
            jnp.zeros((block_rows // 2, -(small_cols + route_cols) % (2 * LANES)), bf16),
        ],
        axis=1,
    )
    packed_cols = small_half.shape[1] // 2
    small_packed = jnp.concatenate([small_half[:, :packed_cols], small_half[:, packed_cols:]])
    kv_cols = w_kv.shape[1] // PLANE
    kv_parts = block_rows // kv_rows
    kv_piece = kv_cols // kv_parts
    w_out_t = w_out.T

    local_heads = query_cols // (DN + DR)

    def by_parts(block):
        heads = [block[:, h * (DN + DR) : (h + 1) * (DN + DR)] for h in range(local_heads)]
        return [h[:, :DN] for h in heads] + [h[:, DN:] for h in heads]

    def quarter(index):
        kv_here = take_rows(w_kv, index * kv_cols, kv_cols, axis=1)
        kv_here = [kv_here[:, p * kv_piece : (p + 1) * kv_piece] for p in range(kv_parts)]
        return jnp.concatenate(
            [
                *by_parts(take_rows(w_query, index * query_cols, query_cols, axis=1)),
                take_rows(w_out_t, index * out_cols, out_cols, axis=1),
                jnp.concatenate(kv_here, axis=0),
            ],
            axis=1,
        )

    near_w = [quarter(place)] + [to_partner(quarter(place ^ r), r) for r in range(1, PLANE)]
    small_line = deep_join(small_packed, deep_pieces(small_packed), z)
    near_w, small_line = tie(near_w, small_line)
    plane_w = jnp.stack(by_place(near_w, place))
    small_sent, x_sent, plane_w = tie(
        small_line.swapaxes(0, 1), take_rows(inputs, own_at, half), plane_w
    )
    small_sent = jnp.stack([small_sent, to_partner(small_sent, 1)])
    small_sent = jnp.concatenate([small_sent, to_partner(small_sent, 2)], axis=0)
    x_sent = jnp.stack([x_sent, to_partner(x_sent, 2)])
    x_came = to_partner(x_sent, 1)
    x_near_own = jnp.stack([x_sent[0], x_came[0], x_sent[1], x_came[1]])
    x_near_other = swap_cores(x_near_own)
    deep_w = deep_hops(plane_w)
    small_parts = [small_sent[r].swapaxes(0, 1) for r in range(PLANE)]
    small_own = jnp.stack(by_place(small_parts, place), axis=1)
    small_own = small_own.reshape(groups, block_rows, packed_cols)
    small_own = jnp.concatenate(
        [small_own[:, : block_rows // 2], small_own[:, block_rows // 2 :]], axis=2
    )
    small_other = swap_cores(small_own)
    small_all = in_order(core, small_own, small_other, axis=1)
    small_all, x_near_other, deep_w = tie(small_all, x_near_other, deep_w)
    head_w = deep_join(plane_w, join_hops(deep_w), z)
    length_at = small_cols + route_cols - 1
    lengths_near = take_rows(small_own, z * PLANE, PLANE)[:, : lengths.shape[1], length_at]
    lengths_near = lengths_near.astype(jnp.int32)
    lengths_near = jnp.stack(by_place([lengths_near[r] for r in range(PLANE)], place))
    shared_rows = jnp.concatenate(
        [shared_gate_up[0].T, shared_gate_up[1].T, shared_down], axis=0
    ).reshape(3, groups, shared_cols, block_rows)
    shared_rows = shared_rows.swapaxes(0, 1).reshape(groups, 3 * shared_cols, block_rows)
    dy_sent, head_w = tie(take_rows(cotangent, own_at, half), head_w)
    dy_own_rows = take_rows(cotangent, own_at, half)
    dy_gather = RowGather(dy_sent)
    dy_came = dy_gather.along()
    head_w = head_w.reshape(groups, block_rows, -1)
    flat_head = head_w.reshape(groups * block_rows, -1)
    at = query_cols + out_cols
    kv_w = head_w[:, :, at : at + kv_piece].reshape(groups, kv_parts, kv_rows, kv_piece)
    kv_w = kv_w.transpose(0, 2, 1, 3).reshape(groups * kv_rows, kv_cols)

    block_index = jnp.arange(groups)
    block_chip = (z - block_index % deep) % deep * PLANE + (place ^ (block_index // deep))
    in_blocks = (block_chip[:, None] == block_index[None, :]).astype(bf16)

    def routes_of(came):
        came = came[:, :, small_cols : small_cols + route_half.shape[1]].reshape(groups, -1)
        came = jnp.dot(in_blocks, came, preferred_element_type=f32)
        return came.astype(jnp.int32).reshape(groups, half, route_count)

    routes_own, routes_other = routes_of(small_own), routes_of(small_other)
    flat_small = small_all.reshape(groups * block_rows, -1)
    latent_w = flat_small[:, :latent_cols]
    at = rank_width + LANES
    router_w = flat_small[:, at : at + expert_count]
    at += expert_count
    gain_one, gain_two = flat_small[:, at], flat_small[:, at + 1]
    latent_g = small_all[:, :kv_rows, at + 2].reshape(-1)

    near_rows = PLANE * tok_rows
    relative, doc = jax.vmap(lambda one: doc_places(one, tok_rows))(lengths_near)
    cosine, sine_tab = rope_tables(relative.reshape(-1), DR)
    cosine, sine_tab = [v.reshape(PLANE, tok_rows, -1) for v in (cosine, sine_tab)]
    rope = (
        jnp.concatenate([cosine] * 4, axis=-1),
        jnp.concatenate([-sine_tab, sine_tab] * 2, axis=-1),
        doc.astype(f32),
    )
    core_index = core.reshape(1).astype(jnp.int32)
    *kept_rows, latent, part_own, part_other = attention(
        core_index,
        x_near_own,
        x_near_other,
        gain_one.astype(f32)[None],
        latent_g.astype(f32)[None],
        flat_head,
        flat_small,
        kv_w,
        *rope,
    )
    normed_b = kept_rows[0].reshape(near_rows, width)

    def sum_cores(own, other):
        return add_wide(own, swap_cores(other)).astype(bf16)

    def sum_plane(both):
        return plane_scatter([both[r] for r in range(PLANE)])

    part_own, part_other, dy_came = tie(part_own, part_other, dy_came)
    attn_own = sum_plane(sum_cores(part_own, part_other))
    x_own = take_rows(inputs, own_at, half).astype(f32)
    hidden = x_own + attn_own
    hnormed, scale_two = rms_forward(hidden, gain_two.astype(f32))
    hnormed_b = hnormed.astype(bf16)
    normed_cols = jnp.concatenate(
        [
            take_rows(normed_b, (k * PLANE + place) * block_rows, block_rows, axis=1)
            for k in range(deep)
        ],
        axis=1,
    )
    hnormed_b, normed_cols, shared_rows, routes_own, routes_other = tie(
        hnormed_b, normed_cols, shared_rows, routes_own, routes_other
    )
    dy_line = jnp.stack(dy_came)
    def membership(named):
        one_hot = named[..., None] == jnp.arange(expert_count, dtype=jnp.int32)
        return jnp.any(named == me, axis=-1), jnp.any(one_hot, axis=2)

    member_own, hot_own = membership(routes_own)
    member_other, hot_other = membership(routes_other)
    lower = (
        jnp.arange(half, dtype=jnp.int32)[:, None] <= jnp.arange(half, dtype=jnp.int32)[None, :]
    ).astype(bf16)

    def running(mask):
        counts = jnp.dot(mask.astype(bf16), lower, preferred_element_type=f32)
        return counts.astype(jnp.int32)

    count_own, count_other = running(member_own), running(member_other)
    place_own = jnp.where(member_own, count_own - 1, -1)
    place_other = jnp.where(member_other, count_own[:, -1:] + count_other - 1, -1)

    def metadata(slot, hot):
        return jnp.concatenate(
            [
                slot[..., None].astype(f32),
                jnp.zeros((groups, half, shared_cols - 1), f32),
                hot.astype(f32),
                jnp.zeros((groups, half, LANES - shared_cols - expert_count), f32),
            ],
            axis=-1,
        )

    meta_own, meta_other = metadata(place_own, hot_own), metadata(place_other, hot_other)
    hn_gather = RowGather(hnormed_b)
    shared_w = lax.all_to_all(shared_rows, "expert", split_axis=0, concat_axis=0, tiled=True)
    hn_came, dy_beside, dy_line_other, shared_w, meta_own, meta_other = tie(
        hn_gather.along(),
        dy_gather.beside(dy_line),
        swap_cores(dy_line),
        shared_w,
        meta_own,
        meta_other,
    )
    shared_w = shared_w.swapaxes(0, 1).reshape(3 * shared_cols, groups * block_rows)
    first_w = jnp.concatenate(
        [
            shared_w[:shared_cols],
            router_w.T,
            jnp.zeros((LANES - shared_cols - expert_count, width), bf16),
            shared_w[shared_cols : 2 * shared_cols],
            jnp.zeros((LANES - shared_cols, width), bf16),
        ],
        axis=0,
    )
    sdown_rows = jnp.pad(shared_w[2 * shared_cols :], ((0, LANES - shared_cols), (0, 0)))
    gate_up_w, down_w = jnp.swapaxes(expert_gate_up[0], 1, 2), expert_down[0]

    def run_experts(which, hn_part, hn_part_other):
        at, to = which[0] * deep, (which[-1] + 1) * deep
        return experts(
            me.reshape(1).astype(jnp.int32),
            hn_part,
            hn_part_other,
            *dy_parts[which],
            meta_own[at:to],
            meta_other[at:to],
            gate_up_w,
            down_w,
            first_w,
            sdown_rows,
            shared_cols,
            expert_count,
        )

    parts = ((0,), (1, 2), (3,))
    dy_parts = {parts[0]: (dy_line, dy_line_other)}
    hn_line, dy_beside = tie(jnp.stack(hn_came), dy_beside)
    dy_near = jnp.concatenate(dy_beside, axis=0)
    hn_beside, dy_beside, done_line, *dy_parts[parts[1]] = tie(
        hn_gather.beside(hn_line),
        dy_beside,
        run_experts(parts[0], hn_line, swap_cores(hn_line)),
        dy_near,
        swap_cores(dy_near),
    )
    d_line_came = swap_cores(done_line[5])
    hn_near = jnp.concatenate(hn_beside, axis=0)
    hn_far, dy_far, done_near = tie(
        hn_gather.far(hn_beside),
        dy_gather.far(dy_beside),
        run_experts(parts[1], hn_near, swap_cores(hn_near)),
    )
    dy_far = jnp.concatenate(dy_far, axis=1)
    dy_parts[parts[2]] = dy_far, swap_cores(dy_far)
    d_near_came = swap_cores(done_near[5])
    hn_far = jnp.concatenate(hn_far, axis=1)
    done_far = run_experts(parts[2], hn_far, swap_cores(hn_far))
    done = (done_line, done_near, done_far)
    slot_rows, slot_dy, slot_act, d_gate_up = [[v[i] for v in done] for i in range(4)]
    shared_grads = add_wide(*[v[8] for v in done])

    def by_flips(line, near, far):
        return [line, near[:deep], near[deep:], far]

    d_rows_own = by_flips(*[v[4] for v in done])
    d_rows_came = by_flips(d_line_came, d_near_came, swap_cores(done_far[5]))

    def two_parts(value):
        return value[..., 0] + value[..., 1]

    dgate_own, dgate_other = [
        jnp.concatenate([two_parts(v[i]) for v in done], axis=0) for i in (9, 10)
    ]
    dgate_sent = dgate_own + swap_cores(dgate_other)
    dgate_high = dgate_sent.astype(bf16)
    dgate_low = (dgate_sent - dgate_high.astype(f32)).astype(bf16)
    d_rows_came, dgate_high, dgate_low = tie(d_rows_came, dgate_high, dgate_low)
    d_sum = RowSum(d_rows_own, d_rows_came)
    sends, shared_grads, slot_act = tie(d_sum.sends(), shared_grads, slot_act)
    came = d_sum.move(sends)
    gate_rows = jnp.stack([contract_rows(in_blocks, v).reshape(-1) for v in (dgate_high, dgate_low)])
    grads_sent = jnp.concatenate([shared_grads, gate_rows], axis=0).astype(bf16)
    grads_sent = grads_sent.reshape(-1, groups, block_rows)
    grads_came = lax.all_to_all(grads_sent, "expert", split_axis=1, concat_axis=1, tiled=True)
    out_done = [
        outputs(
            act,
            v[6],
            v[7],
            meta_own[p[0] * deep : (p[-1] + 1) * deep],
            meta_other[p[0] * deep : (p[-1] + 1) * deep],
            down_w,
            sdown_rows,
        )
        for act, v, p in zip(slot_act, done, parts)
    ]
    edown_grad = column_products([v[None] for v in slot_act], slot_dy)[0]
    came, out_done, edown_grad, grads_came = tie(came, out_done, edown_grad, grads_came)
    dgate = add_wide(grads_came[3 * shared_cols], grads_came[3 * shared_cols + 1]).T
    sends, slot_rows, out_done = tie(d_sum.sends_again(came), slot_rows, out_done)
    came_again = d_sum.move_again(sends)
    egu_grad = column_products(d_gate_up, slot_rows).swapaxes(1, 2)
    out_own = by_flips(*[v[0] for v in out_done])
    out_came = by_flips(*[swap_cores(v[1]) for v in out_done])
    out_sum = RowSum(out_own, out_came)
    out_sends = out_sum.sends()
    came_again, egu_grad, out_sends = tie(came_again, egu_grad, out_sends)
    z_sends, out_sends, dgate = tie(
        line_sends(d_sum.line(came, came_again)), out_sends, dgate
    )
    z_came = line_move(z_sends)
    out_first = out_sum.move(out_sends)
    hot_mine = take_rows(
        jnp.any(routes[..., None] == jnp.arange(expert_count, dtype=jnp.int32), axis=1), own_at, half
    )
    sig = jax.nn.sigmoid(jnp.dot(hnormed_b, router_w, preferred_element_type=f32))
    chosen = jnp.where(hot_mine, sig, 0.0)
    chosen_sum = jnp.sum(chosen, axis=1, keepdims=True)
    dgate = jnp.where(hot_mine, dgate, 0.0)
    inner = jnp.sum(dgate * chosen, axis=1, keepdims=True)
    d_chosen = ROUTE_SCALE * (dgate / chosen_sum - inner / (chosen_sum * chosen_sum))
    d_logits = (jnp.where(hot_mine, d_chosen, 0.0) * sig * (1.0 - sig)).astype(bf16)
    router_grad = contract_rows(d_logits, hnormed_b)
    z_came, d_logits, router_grad = tie(z_came, d_logits, router_grad)
    d_hn = add_wide(*z_came)
    d_hn = d_hn + contract_cols(d_logits, router_w)
    d_hidden_norm, gain_two_grad = rms_backward(hidden, scale_two, gain_two.astype(f32), d_hn)
    d_hidden = dy_own_rows.astype(f32) + d_hidden_norm
    d_parts, out_first = tie(plane_gather(d_hidden.astype(bf16)), out_first)
    d_near_own = jnp.stack(d_parts)
    d_near_other = swap_cores(d_near_own)
    out_sends, d_near_other = tie(out_sum.sends_again(out_first), d_near_other)
    out_second = out_sum.move_again(out_sends)

    (
        head_grad,
        kv_grad,
        normed_part_own,
        normed_part_other,
        latent_part_own,
        latent_part_other,
    ) = attention_backward(
        core_index, d_near_own, d_near_other, kept_rows, flat_head, kv_w, *rope
    )
    kv_grad = kv_grad.reshape(groups, kv_rows, kv_parts, kv_piece).transpose(0, 2, 1, 3)
    head_grad = jnp.concatenate([head_grad, kv_grad.reshape(-1, kv_piece)], axis=1)
    head_blocks = head_grad.reshape(deep, -1, head_grad.shape[1])
    head_hops = HopSum(lambda t: at_index(head_blocks, 0, t))
    came, latent_both, normed_both, out_second = tie(
        head_hops.hop(1),
        sum_cores(latent_part_own, latent_part_other),
        sum_cores(normed_part_own, normed_part_other),
        out_second,
    )
    out_line = out_sum.line(out_first, out_second)
    came, grad_both, out_line = tie(head_hops.hop(2, came), sum_plane(latent_both), out_line)
    grad_rope = grad_both[:, rank_width : rank_width + DR] + grad_both[:, rank_width + DR :]
    latent_own = take_rows(latent[0], own_at, half)
    cosine_own = take_rows(cosine[0], own_at, half)
    sine_own = take_rows(sine_tab[0], own_at, half)
    _, scale_kv = rms_forward(latent_own[:, :rank_width], latent_g.astype(f32))
    grad_c, latent_gain_grad = rms_backward(
        latent_own[:, :rank_width], scale_kv, latent_g.astype(f32), grad_both[:, :rank_width]
    )
    grad_latent = jnp.concatenate(
        [grad_c, unrotate(grad_rope, cosine_own, sine_own)], axis=-1
    ).astype(bf16)
    out_hops = HopSum(lambda t: at_index(out_line, 0, (z - t) % deep))
    came, latent_parts, grad_normed, out_z = tie(
        head_hops.hop(3, came), plane_gather(grad_latent), sum_plane(normed_both), out_hops.hop(1)
    )
    latent_near_own = jnp.stack(latent_parts)
    latent_near = in_order(core, latent_near_own, swap_cores(latent_near_own), axis=1)
    head_sums = head_hops.total(came).astype(bf16).reshape(PLANE, block_rows, -1)
    out_z, latent_near, head_shared, grads_came = tie(
        out_hops.hop(2, out_z), latent_near, share_columns(head_sums, place), grads_came
    )
    out_z = out_hops.hop(3, out_z)
    latent_cut = latent_cols // 2
    latent_near = latent_near.reshape(near_rows, latent_cols)
    latent_blocks = contract_rows(
        normed_cols,
        take_rows(latent_near, core * latent_cut, latent_cut, axis=1),
    )
    latent_half = deep_scatter(latent_blocks.astype(bf16).reshape(deep, -1, latent_cut), z)
    w_latent_grad = in_order(core, latent_half, swap_cores(latent_half), axis=1)


    def by_heads(block):
        rotary = local_heads * DN
        return [
            part
            for h in range(local_heads)
            for part in (
                block[:, h * DN : (h + 1) * DN],
                block[:, rotary + h * DR : rotary + (h + 1) * DR],
            )
        ]

    at_kv = query_cols + out_cols
    w_query_grad = jnp.concatenate([v for p in head_shared for v in by_heads(p)], axis=1)
    w_query_grad = w_query_grad.astype(f32)
    w_kv_grad = jnp.concatenate(
        [
            p[q * kv_rows : (q + 1) * kv_rows, at_kv:]
            for p in head_shared
            for q in range(kv_parts)
        ],
        axis=1,
    ).astype(f32)
    w_out_grad = jnp.concatenate([p[:, query_cols:at_kv] for p in head_shared], axis=1)
    w_out_grad = w_out_grad.astype(f32).T
    sgu_out = grads_came[: 2 * shared_cols].astype(f32)
    sgu_out = sgu_out.reshape(2, shared_cols, groups, block_rows)
    sgu_out = sgu_out.transpose(0, 3, 2, 1).reshape(2, block_rows, -1)
    sdown_out = grads_came[2 * shared_cols : 3 * shared_cols].astype(f32).swapaxes(0, 1).reshape(-1, block_rows)
    grad_normed = grad_normed + contract_cols(grad_latent, latent_w)
    moe_own = out_hops.total(out_z)
    mixed_own = (hidden + moe_own).astype(bf16)
    mixed = in_order(core, mixed_own, swap_cores(mixed_own))

    _, scale_own = rms_forward(x_own, gain_one.astype(f32))
    grad_x_norm, gain_one_grad = rms_backward(x_own, scale_own, gain_one.astype(f32), grad_normed)
    input_own = d_hidden + grad_x_norm
    input_grad = in_order(core, input_own, swap_cores(input_own))

    gain_lanes = jnp.pad(
        latent_gain_grad.reshape(groups, kv_rows), ((0, 0), (0, block_rows - kv_rows))
    )
    vectors = jnp.concatenate(
        [
            router_grad,
            gain_one_grad[None],
            gain_two_grad[None],
            gain_lanes.reshape(1, -1),
        ],
        axis=0,
    ).reshape(-1, groups, block_rows)
    arrived = lax.all_to_all(vectors, "expert", split_axis=1, concat_axis=1, tiled=True)
    sums = jnp.sum(arrived, axis=1)
    sums = sums + swap_cores(sums)
    return (
        mixed,
        input_grad,
        sums[expert_count],
        w_query_grad,
        w_latent_grad,
        sums[expert_count + 2, :kv_rows],
        w_kv_grad,
        w_out_grad,
        sums[expert_count + 1],
        sums[:expert_count].T,
        sgu_out,
        sdown_out,
        egu_grad[None],
        edown_grad[None],
    )


def solution(mesh):
    groups = mesh.shape["expert"]
    plan = token_plan if groups <= 16 else weight_plan
    return jax.shard_map(
        plan,
        mesh=mesh,
        in_specs=(
            P("expert", None),
            P("expert"),
            P("expert", "tensor"),
            P("expert", None),
            P("expert"),
            P("expert", "tensor"),
            P("tensor", "expert"),
            P("expert"),
            P("expert", None),
            P(None, "expert", "tensor"),
            P("tensor", "expert"),
            P("expert", None, None, "tensor"),
            P("expert", "tensor", None),
            P("expert", None),
            P("expert", None),
            P("expert", None),
        ),
        out_specs=(
            P("expert", None),
            P("expert", None),
            P("expert"),
            P("expert", "tensor"),
            P("expert", None),
            P("expert"),
            P("expert", "tensor"),
            P("tensor", "expert"),
            P("expert"),
            P("expert", None),
            P(None, "expert", "tensor"),
            P("tensor", "expert"),
            P("expert", None, None, "tensor"),
            P("expert", "tensor", None),
        ),
        check_vma=False,
    )
```

```python
import functools

import jax
import jax.numpy as jnp
from jax import lax
from jax.experimental import pallas as pl
from jax.experimental.pallas import tpu as pltpu
from jax.sharding import PartitionSpec as P

DN = 128
DR = 64
DV = 128
LANES = 128


EPSILON = 1e-06
ROUTE_SCALE = 2.446
ROPE_BASE = 50000.0
NEGATIVE = -1e30


def cut_along(value, dim, length):
    before, after = (value.shape[:dim], value.shape[dim + 1 :])
    return jnp.moveaxis(value.reshape(*before, length, -1, *after), dim, 0)


def summed_on_arrival(value, axis, dim):
    length = lax.axis_size(axis)
    tiles = lax.all_to_all(cut_along(value, dim, length), axis, 0, 0, tiled=True)
    return jnp.sum(tiles.astype(jnp.float32), axis=0)


def sent_together(arrays, axis, dim, along):
    columns = [a.reshape(*a.shape[:along], -1) for a in arrays]
    both = jnp.concatenate(columns, axis=along)
    whole, at, outs = (summed_on_arrival(both, axis, dim), 0, [])
    for a, column in zip(arrays, columns):
        slab = whole[..., at : at + column.shape[along]]
        outs.append(slab.reshape(*slab.shape[:along], *a.shape[along:]))
        at += column.shape[along]
    return tuple(outs)


def contract_rows(left_arr, right_arr):
    return lax.dot_general(
        left_arr, right_arr, (((0,), (0,)), ((), ())), preferred_element_type=jnp.float32
    )


def contract_cols(left_arr, right_arr):
    return lax.dot_general(
        left_arr, right_arr, (((1,), (1,)), ((), ())), preferred_element_type=jnp.float32
    )


def rms_forward(rows_in, gain_vec):
    inverse = lax.rsqrt(jnp.mean(rows_in * rows_in, axis=-1, keepdims=True) + EPSILON)
    return (rows_in * inverse * gain_vec, inverse)


def rms_backward(rows_in, inverse, gain_vec, grad_out):
    gain_grad = jnp.sum(grad_out * rows_in * inverse, axis=0)
    weighted = grad_out * gain_vec
    inner_mean = jnp.mean(weighted * rows_in, axis=-1, keepdims=True)
    return (inverse * weighted - rows_in * inverse * inverse * inverse * inner_mean, gain_grad)


def doc_layout(doc_lengths, row_count):
    ends_at = jnp.cumsum(doc_lengths)
    starts_at = ends_at - doc_lengths
    position = jnp.arange(row_count, dtype=jnp.int32)
    doc_ids = jnp.sum((position[:, None] >= ends_at[None, :]).astype(jnp.int32), axis=1)
    hitting = doc_ids[:, None] == jnp.arange(doc_lengths.shape[0], dtype=jnp.int32)[None, :]
    start_of = jnp.sum(jnp.where(hitting, starts_at[None, :], 0), axis=1)
    relative = position - start_of
    visible = (doc_ids[:, None] == doc_ids[None, :]) & (position[:, None] >= position[None, :])
    return (relative, visible)


def rope_tables(relative, rot_width):
    counter = jnp.arange(rot_width // 2, dtype=jnp.float32)
    frequency = ROPE_BASE ** (-2.0 * counter / rot_width)
    angles = relative.astype(jnp.float32)[:, None] * frequency[None, :]
    return (jnp.cos(angles), jnp.sin(angles))


def rotate(tensor_in, cosine, sine_tab):
    half_width = tensor_in.shape[-1] // 2
    leading = tensor_in[..., :half_width]
    trailing = tensor_in[..., half_width:]
    return jnp.concatenate(
        [leading * cosine - trailing * sine_tab, trailing * cosine + leading * sine_tab], axis=-1
    )


def unrotate(grad_in, cosine, sine_tab):
    half_width = grad_in.shape[-1] // 2
    leading = grad_in[..., :half_width]
    trailing = grad_in[..., half_width:]
    return jnp.concatenate(
        [leading * cosine + trailing * sine_tab, trailing * cosine - leading * sine_tab], axis=-1
    )


def gated_linear_backward(gate_in, up_in, grad_act):
    sigmoid_g = jax.nn.sigmoid(gate_in)
    grad_gate = grad_act * up_in * sigmoid_g * (1.0 + gate_in * (1.0 - sigmoid_g))
    return (grad_gate, grad_act * gate_in * sigmoid_g)


def slot_tables(route_rows, expert_count, capacity):
    flat_routes = route_rows.reshape(-1)
    one_hot = (flat_routes[:, None] == jnp.arange(expert_count, dtype=jnp.int32)[None, :]).astype(
        jnp.int32
    )
    ranking = jnp.sum((jnp.cumsum(one_hot, axis=0) - one_hot) * one_hot, axis=1)
    slot_ids = flat_routes * capacity + ranking
    row_total = flat_routes.shape[0]
    source = (
        jnp.zeros((expert_count * capacity,), jnp.int32)
        .at[slot_ids]
        .set(jnp.arange(row_total, dtype=jnp.int32))
    )
    filled = jnp.zeros((expert_count * capacity,), jnp.int32).at[slot_ids].set(1)
    return (slot_ids, source, filled)


def to_owner(rows_in):
    arrived = lax.all_to_all(rows_in, "expert", split_axis=0, concat_axis=1, tiled=True)
    return arrived


def weight_plan(
    inputs,
    attn_gain,
    w_query,
    w_latent,
    latent_gain,
    w_kv,
    w_out,
    ffn_gain,
    w_router,
    shared_gate_up,
    shared_down,
    expert_gate_up,
    expert_down,
    lengths,
    routes,
    cotangent,
):
    tok_rows = inputs.shape[0]
    model_width = inputs.shape[1]
    expert_count = w_router.shape[1]
    route_count = routes.shape[1]
    capacity = tok_rows * route_count * 4 // (3 * expert_count)
    brain_float16 = jnp.bfloat16
    f32 = jnp.float32
    gathered = (
        lax.all_gather(attn_gain, "expert", axis=0, tiled=True),
        lax.all_gather(w_query, "expert", axis=0, tiled=True),
        lax.all_gather(w_latent, "expert", axis=0, tiled=True),
        lax.all_gather(latent_gain, "expert", axis=0, tiled=True),
        lax.all_gather(w_kv, "expert", axis=0, tiled=True),
        lax.all_gather(w_out, "expert", axis=1, tiled=True),
        lax.all_gather(ffn_gain, "expert", axis=0, tiled=True),
        lax.all_gather(w_router, "expert", axis=0, tiled=True),
        lax.all_gather(shared_gate_up, "expert", axis=1, tiled=True),
        lax.all_gather(shared_down, "expert", axis=1, tiled=True),
    )
    gain_one, query_w, latent_w, latent_g, kv_w, out_w, gain_two, router_w, sgate_up, sdown_w = (
        gathered
    )
    local_heads = query_w.shape[1] // (DN + DR)
    rank_width = latent_g.shape[0]
    x_float = inputs.astype(f32)
    relative, visible = doc_layout(lengths[0], tok_rows)
    cosine, sine_tab = rope_tables(relative, DR)
    q_scale = (DN + DR) ** (-0.5)
    normed, scale_one = rms_forward(x_float, gain_one.astype(f32))
    normed_b = normed.astype(brain_float16)
    queries = jnp.dot(normed_b, query_w, preferred_element_type=f32).reshape(
        tok_rows, local_heads, DN + DR
    )
    q_rot = rotate(queries[..., DN:], cosine[:, None, :], sine_tab[:, None, :])
    q_all = jnp.concatenate([queries[..., :DN], q_rot], axis=-1).astype(brain_float16)
    latent = jnp.dot(normed_b, latent_w, preferred_element_type=f32)
    compressed, scale_kv = rms_forward(latent[:, :rank_width], latent_g.astype(f32))
    compressed_b = compressed.astype(brain_float16)
    k_rope = rotate(latent[:, rank_width:], cosine, sine_tab).astype(brain_float16)
    kv_all = jnp.dot(compressed_b, kv_w, preferred_element_type=f32).reshape(
        tok_rows, local_heads, DN + DV
    )
    k_nope = kv_all[..., :DN].astype(brain_float16)
    values = kv_all[..., DN:].astype(brain_float16)
    key_all = jnp.concatenate(
        [k_nope, jnp.broadcast_to(k_rope[:, None, :], (tok_rows, local_heads, DR))], axis=-1
    )

    def score_block():
        raw_scores = (
            jnp.einsum("qhd,khd->hqk", q_all, key_all, preferred_element_type=f32) * q_scale
        )
        return jnp.where(visible[None], raw_scores, NEGATIVE)

    scores = score_block()
    top_score = jnp.max(scores, axis=-1, keepdims=True)
    log_total = top_score + jnp.log(jnp.sum(jnp.exp(scores - top_score), axis=-1, keepdims=True))
    probs_b = jnp.exp(scores - log_total).astype(brain_float16)
    attended = jnp.einsum("hqk,khd->qhd", probs_b, values, preferred_element_type=f32)
    attended_b = attended.reshape(tok_rows, local_heads * DV).astype(brain_float16)
    attn = lax.psum(jnp.dot(attended_b, out_w, preferred_element_type=f32), "tensor")
    hidden = x_float + attn
    hnormed, scale_two = rms_forward(hidden, gain_two.astype(f32))
    hnormed_b = hnormed.astype(brain_float16)
    logits = jnp.dot(hnormed_b, router_w, preferred_element_type=f32)
    sigmoid_vals = jax.nn.sigmoid(logits)
    route_hot = routes[:, :, None] == jnp.arange(expert_count, dtype=jnp.int32)[None, None, :]
    chosen = jnp.sum(jnp.where(route_hot, sigmoid_vals[:, None, :], 0.0), axis=2)
    chosen_sum = jnp.sum(chosen, axis=1, keepdims=True)
    gate_vals = ROUTE_SCALE * chosen / chosen_sum
    slot_ids, source, filled = slot_tables(routes, expert_count, capacity)
    is_filled = filled[:, None] == 1
    sent_rows = jnp.where(is_filled, hnormed_b[source // route_count], 0).reshape(
        expert_count, capacity, model_width
    )
    received = to_owner(sent_rows)
    gate_up_joined = jnp.einsum(
        "erd,egdf->egrf", received, expert_gate_up, preferred_element_type=f32
    )
    expert_act = (jax.nn.silu(gate_up_joined[:, 0]) * gate_up_joined[:, 1]).astype(brain_float16)
    expert_res = jnp.einsum(
        "erf,efd->erd", expert_act, expert_down, preferred_element_type=f32
    ).astype(brain_float16)
    returned_all = lax.all_to_all(expert_res, "expert", split_axis=1, concat_axis=0, tiled=True)
    returned = returned_all.reshape(expert_count * capacity, model_width)[slot_ids].reshape(
        tok_rows, route_count, model_width
    )
    shared_gu = jnp.einsum("td,gdf->gtf", hnormed_b, sgate_up, preferred_element_type=f32)
    shared_act = (jax.nn.silu(shared_gu[0]) * shared_gu[1]).astype(brain_float16)
    branch_sum = jnp.dot(shared_act, sdown_w, preferred_element_type=f32)
    for route_idx in range(route_count):
        branch_sum = branch_sum + gate_vals[:, route_idx : route_idx + 1] * returned[
            :, route_idx
        ].astype(f32)
    moe_out = lax.psum(branch_sum.astype(jnp.bfloat16), "tensor").astype(jnp.float32)
    mixed = (hidden + moe_out).astype(brain_float16)
    grad_y = cotangent.astype(f32)
    sdown_grad = contract_rows(shared_act, cotangent)
    grad_sact = contract_cols(cotangent, sdown_w)
    grad_sgate, grad_sup = gated_linear_backward(shared_gu[0], shared_gu[1], grad_sact)
    grad_sgu = jnp.stack([grad_sgate, grad_sup], axis=0).astype(brain_float16)
    sgu_grad = jnp.einsum("td,gtf->gdf", hnormed_b, grad_sgu, preferred_element_type=f32)
    grad_hn_part = jnp.einsum("gtf,gdf->td", grad_sgu, sgate_up, preferred_element_type=f32)
    gate_columns = []
    for route_idx in range(route_count):
        gate_columns.append(jnp.sum(grad_y * returned[:, route_idx].astype(f32), axis=1))
    gate_part = jnp.stack(gate_columns, axis=1)
    slot_grads = (
        (gate_vals[:, :, None] * grad_y[:, None, :])
        .reshape(tok_rows * route_count, model_width)
        .astype(brain_float16)
    )
    grad_sent = jnp.where(is_filled, slot_grads[source], 0).reshape(
        expert_count, capacity, model_width
    )
    grad_received = to_owner(grad_sent)
    edown_grad = jnp.einsum("erf,erd->efd", expert_act, grad_received, preferred_element_type=f32)
    expert_activation_gradient = jnp.einsum(
        "erd,efd->erf", grad_received, expert_down, preferred_element_type=f32
    )
    expert_gate_gradient, expert_up_gradient = gated_linear_backward(
        gate_up_joined[:, 0], gate_up_joined[:, 1], expert_activation_gradient
    )
    expert_gate_up_gradient = jnp.stack([expert_gate_gradient, expert_up_gradient], axis=1).astype(
        brain_float16
    )
    egu_grad = jnp.einsum(
        "erd,egrf->egdf", received, expert_gate_up_gradient, preferred_element_type=f32
    )
    grad_rows = jnp.einsum(
        "egrf,egdf->erd", expert_gate_up_gradient, expert_gate_up, preferred_element_type=f32
    ).astype(brain_float16)
    grad_back = lax.all_to_all(grad_rows, "expert", split_axis=1, concat_axis=0, tiled=True)
    grad_routes = grad_back.reshape(expert_count * capacity, model_width)[slot_ids].reshape(
        tok_rows, route_count, model_width
    )
    for route_idx in range(route_count):
        grad_hn_part = grad_hn_part + grad_routes[:, route_idx].astype(f32)
    gate_grads = lax.psum(gate_part, "tensor")
    grad_chosen = ROUTE_SCALE * (
        gate_grads / chosen_sum
        - jnp.sum(gate_grads * chosen, axis=1, keepdims=True) / (chosen_sum * chosen_sum)
    )
    grad_sig = jnp.sum(jnp.where(route_hot, grad_chosen[:, :, None], 0.0), axis=1)
    grad_logits = (grad_sig * sigmoid_vals * (1.0 - sigmoid_vals)).astype(brain_float16)
    router_grad = contract_rows(hnormed_b, grad_logits)
    grad_hn = lax.psum(grad_hn_part, "tensor") + contract_cols(grad_logits, router_w)
    grad_hidden_norm, gain_two_grad = rms_backward(hidden, scale_two, gain_two.astype(f32), grad_hn)
    grad_hidden = grad_y + grad_hidden_norm
    grad_hidden_b = grad_hidden.astype(brain_float16)
    out_grad = contract_rows(attended_b, grad_hidden_b)
    grad_att = (
        contract_cols(grad_hidden_b, out_w).reshape(tok_rows, local_heads, DV).astype(brain_float16)
    )
    probs = jnp.exp(score_block() - log_total)
    probs_again = probs.astype(brain_float16)
    grad_probs = jnp.einsum("qhd,khd->hqk", grad_att, values, preferred_element_type=f32)
    grad_vals = jnp.einsum("hqk,qhd->khd", probs_again, grad_att, preferred_element_type=f32)
    row_delta = jnp.sum(probs * grad_probs, axis=-1, keepdims=True)
    grad_scores = (probs * (grad_probs - row_delta)).astype(brain_float16)
    grad_q = jnp.einsum("hqk,khd->qhd", grad_scores, key_all, preferred_element_type=f32) * q_scale
    grad_keys = jnp.einsum("hqk,qhd->khd", grad_scores, q_all, preferred_element_type=f32) * q_scale
    grad_kv = (
        jnp.concatenate([grad_keys[..., :DN], grad_vals], axis=-1)
        .reshape(tok_rows, local_heads * (DN + DV))
        .astype(brain_float16)
    )
    kv_grad = contract_rows(compressed_b, grad_kv)
    grad_comp_part = contract_cols(grad_kv, kv_w)
    grad_krope_part = jnp.sum(grad_keys[..., DN:], axis=1)
    grad_comp, grad_krope = (
        lax.psum(grad_comp_part.astype(jnp.bfloat16), "tensor").astype(jnp.float32),
        lax.psum(grad_krope_part.astype(jnp.bfloat16), "tensor").astype(jnp.float32),
    )
    grad_c, latent_gain_grad = rms_backward(
        latent[:, :rank_width], scale_kv, latent_g.astype(f32), grad_comp
    )
    grad_latent = jnp.concatenate([grad_c, unrotate(grad_krope, cosine, sine_tab)], axis=-1).astype(
        brain_float16
    )
    grad_qrot = unrotate(grad_q[..., DN:], cosine[:, None, :], sine_tab[:, None, :])
    grad_queries = (
        jnp.concatenate([grad_q[..., :DN], grad_qrot], axis=-1)
        .reshape(tok_rows, local_heads * (DN + DR))
        .astype(brain_float16)
    )
    query_grad = contract_rows(normed_b, grad_queries)
    latent_grad = contract_rows(normed_b, grad_latent)
    grad_normed = lax.psum(
        contract_cols(grad_queries, query_w).astype(jnp.bfloat16), "tensor"
    ).astype(jnp.float32) + contract_cols(grad_latent, latent_w)
    grad_x_norm, gain_one_grad = rms_backward(x_float, scale_one, gain_one.astype(f32), grad_normed)
    input_grad = grad_hidden + grad_x_norm
    first_owned = (
        *sent_together(
            (
                gain_one_grad.astype(jnp.bfloat16),
                query_grad.astype(jnp.bfloat16),
                latent_grad.astype(jnp.bfloat16),
            ),
            "expert",
            0,
            1,
        ),
        *sent_together(
            (latent_gain_grad.astype(jnp.bfloat16), kv_grad.astype(jnp.bfloat16)), "expert", 0, 1
        ),
    )
    second_owned = (
        lax.psum_scatter(out_grad, "expert", scatter_dimension=1, tiled=True),
        lax.psum_scatter(gain_two_grad, "expert", scatter_dimension=0, tiled=True),
        lax.psum_scatter(router_grad, "expert", scatter_dimension=0, tiled=True),
        lax.psum_scatter(sgu_grad, "expert", scatter_dimension=1, tiled=True),
        lax.psum_scatter(sdown_grad, "expert", scatter_dimension=1, tiled=True),
    )
    return (
        mixed,
        input_grad,
        first_owned[0],
        first_owned[1],
        first_owned[2],
        first_owned[3],
        first_owned[4],
        second_owned[0],
        second_owned[1],
        second_owned[2],
        second_owned[3],
        second_owned[4],
        egu_grad,
        edown_grad,
    )


def swap_cores(value):
    return lax.ppermute(value, "tensor", [(0, 1), (1, 0)])


def take_rows(value, start, count, axis=0):
    return lax.dynamic_slice_in_dim(value, start, count, axis=axis)


def in_order(core, own, other, axis=0):
    return jnp.where(
        core == 0,
        jnp.concatenate([own, other], axis=axis),
        jnp.concatenate([other, own], axis=axis),
    )


def add_wide(*parts):
    total = parts[0].astype(jnp.float32)
    for part in parts[1:]:
        total = total + part.astype(jnp.float32)
    return total


PLANE = 4


def to_partner(value, flips):
    groups = lax.axis_size("expert")
    return lax.ppermute(value, "expert", [(g, g ^ flips) for g in range(groups)])


def to_deeper(value, step):
    groups = lax.axis_size("expert")
    pairs = [(g, (g + step * PLANE) % groups) for g in range(groups)]
    return lax.ppermute(value, "expert", pairs)


def plane_gather(value):
    return [value] + [to_partner(value, r) for r in range(1, PLANE)]


def plane_scatter(parts):
    return add_wide(parts[0], *[to_partner(parts[r], r) for r in range(1, PLANE)])


def by_place(parts, place):
    odd, high = place % 2 == 1, place // 2 == 1
    parts = [jnp.where(odd, parts[i ^ 1], parts[i]) for i in range(PLANE)]
    return [jnp.where(high, parts[i ^ 2], parts[i]) for i in range(PLANE)]


def tie(*values):
    return lax.optimization_barrier(values)


def deep_pieces(value):
    deep = lax.axis_size("expert") // PLANE
    return [to_deeper(value, s) for s in range(1, deep)]


def one_plane(value, step):
    groups = lax.axis_size("expert")
    pairs = [(g, g + step * PLANE) for g in range(groups) if 0 <= g + step * PLANE < groups]
    return lax.ppermute(value, "expert", pairs)


def deep_hops(value):
    deep = lax.axis_size("expert") // PLANE
    after, before, down, up = [], [], value, value
    for _ in range(1, deep):
        down, up = one_plane(down, 1), one_plane(up, -1)
        after.append(down)
        before.append(up)
    return after, before


def join_hops(hops):
    after, before = hops
    return [a + b for a, b in zip(after, before[::-1])]


def deep_join(value, pieces, z):
    deep = lax.axis_size("expert") // PLANE
    whole = jnp.zeros((deep, *value.shape), value.dtype)
    whole = lax.dynamic_update_index_in_dim(whole, value, z, 0)
    for step in range(1, deep):
        whole = lax.dynamic_update_index_in_dim(whole, pieces[step - 1], (z - step) % deep, 0)
    return whole


def deep_move(blocks, z):
    deep = blocks.shape[0]

    def block(index):
        return lax.dynamic_index_in_dim(blocks, index, 0, keepdims=False)

    return [block(z)] + [to_deeper(block((z + step) % deep), step) for step in range(1, deep)]


def deep_scatter(blocks, z):
    return add_wide(*deep_move(blocks, z))


def share_columns(rows, place):
    parts = [at_index(rows, 0, place)]
    for r in range(1, PLANE):
        parts.append(to_partner(at_index(rows, 0, place ^ r), r))
    return by_place(parts, place)


def all_groups(value):
    return lax.all_gather(value, "expert", axis=0, tiled=False)


def at_index(value, axis, index):
    return lax.dynamic_index_in_dim(value, index, axis, keepdims=False)


def doc_places(doc_lengths, row_count):
    ends_at = jnp.cumsum(doc_lengths)
    position = jnp.arange(row_count, dtype=jnp.int32)
    doc_ids = jnp.sum((position[:, None] >= ends_at[None, :]).astype(jnp.int32), axis=1)
    hitting = doc_ids[:, None] == jnp.arange(doc_lengths.shape[0], dtype=jnp.int32)[None, :]
    start_of = jnp.sum(jnp.where(hitting, (ends_at - doc_lengths)[None, :], 0), axis=1)
    return position - start_of, doc_ids


class HopSum:
    def __init__(self, pieces):
        self.groups = lax.axis_size("expert")
        self.deep = self.groups // PLANE
        self.z = lax.axis_index("expert") // PLANE
        self.pieces = pieces

    def hop(self, step, came=None):
        arrived = []
        for side, way in enumerate((1, -1)):
            target = jnp.clip(self.z + way * (self.deep - step), 0, self.deep - 1)
            gone = self.pieces(target)
            if came is not None:
                gone = add_wide(gone, came[side]).astype(gone.dtype)
            first = range(step) if way == 1 else range(self.deep - step, self.deep)
            pairs = [
                (p * PLANE + q, (p + way) * PLANE + q) for p in first for q in range(PLANE)
            ]
            arrived.append(lax.ppermute(gone, "expert", pairs))
        return arrived

    def total(self, came):
        return add_wide(self.pieces(self.z), *came)


def doc_places(doc_lengths, row_count):
    ends_at = jnp.cumsum(doc_lengths)
    position = jnp.arange(row_count, dtype=jnp.int32)
    doc_ids = jnp.sum((position[:, None] >= ends_at[None, :]).astype(jnp.int32), axis=1)
    hitting = doc_ids[:, None] == jnp.arange(doc_lengths.shape[0], dtype=jnp.int32)[None, :]
    start_of = jnp.sum(jnp.where(hitting, (ends_at - doc_lengths)[None, :], 0), axis=1)
    return position - start_of, doc_ids


def hop_sum(pieces):
    groups = lax.axis_size("expert")
    deep = groups // PLANE
    z = lax.axis_index("expert") // PLANE
    ends = []
    for way in (1, -1):
        came = None
        for step in range(1, deep):
            gone = pieces(jnp.clip(z + way * (deep - step), 0, deep - 1))
            if came is not None:
                gone = add_wide(gone, came).astype(gone.dtype)
            first = range(step) if way == 1 else range(deep - step, deep)
            pairs = [
                (p * PLANE + q, (p + way) * PLANE + q) for p in first for q in range(PLANE)
            ]
            came = lax.ppermute(gone, "expert", pairs)
        ends.append(came)
    return [pieces(z), *ends]


class RowGather:
    def __init__(self, value):
        self.cut = value.shape[0] // 2
        self.value = value

    def along(self):
        return [self.value] + deep_pieces(self.value)

    def beside(self, line):
        return to_partner(line, 1), to_partner(line, 2)

    def far(self, beside):
        return to_partner(beside[0][:, : self.cut], 2), to_partner(beside[1][:, self.cut :], 1)


class RowSum:
    def __init__(self, *terms):
        self.type = terms[0][0].dtype
        cut = terms[0][0].shape[1] // 2
        self.halves = (
            ([[b[:, :cut] for b in v] for v in terms], 2, 1),
            ([[b[:, cut:] for b in v] for v in terms], 1, 2),
        )

    def _add(self, parts):
        return add_wide(*parts).astype(self.type)

    def sends(self):
        return [
            jnp.stack([self._add([v[far] for v in held]), self._add([v[far | near] for v in held])])
            for held, far, near in self.halves
        ]

    def move(self, sends):
        return [to_partner(v, far) for v, (_, far, _) in zip(sends, self.halves)]

    def sends_again(self, came):
        return [
            self._add([v[near] for v in held] + [c[1]])
            for c, (held, _, near) in zip(came, self.halves)
        ]

    def move_again(self, sends):
        return [to_partner(v, near) for v, (_, _, near) in zip(sends, self.halves)]

    def line(self, came, came_again):
        sums = [
            self._add([v[0] for v in held] + [c[0], d])
            for c, d, (held, *_) in zip(came, came_again, self.halves)
        ]
        return jnp.concatenate(sums, axis=1)


def line_sends(line):
    return [line[step] for step in range(line.shape[0])]


def line_move(sends):
    return [sends[0]] + [to_deeper(v, -step) for step, v in enumerate(sends) if step > 0]


def dot_nn(left, right):
    return lax.dot_general(left, right, (((1,), (0,)), ((), ())), preferred_element_type=jnp.float32)


def dot_nt(left, right):
    return lax.dot_general(left, right, (((1,), (1,)), ((), ())), preferred_element_type=jnp.float32)


def dot_tn(left, right):
    return lax.dot_general(left, right, (((0,), (0,)), ((), ())), preferred_element_type=jnp.float32)


def two_lanes(column, lane):
    high = column.astype(jnp.bfloat16).astype(jnp.float32)
    spread = jnp.where(lane == 0, high, jnp.where(lane == 1, column - high, 0.0))
    return spread.astype(jnp.bfloat16)


def expert_kernel(
    shared_cols,
    expert_count,
    me_ref,
    hn_own,
    hn_other,
    dy_own,
    dy_other,
    meta_own,
    meta_other,
    gate_up_w,
    down_w,
    first_w,
    sdown_w,
    slots_out,
    slot_dy_out,
    act_out,
    d_gate_up_out,
    rows_own_out,
    rows_other_out,
    sact_own_out,
    sact_other_out,
    shared_grads_out,
    dgate_own_out,
    dgate_other_out,
):
    f32, bf16 = jnp.float32, jnp.bfloat16
    count, half, _ = hn_own.shape
    tokens = 2 * half
    me = me_ref[0]
    lane = lax.broadcasted_iota(jnp.int32, (count * tokens, LANES), 1)
    is_router = (lane >= shared_cols) & (lane < shared_cols + expert_count)
    first = first_w[...]

    def joined(own, other):
        return jnp.concatenate([v[i] for i in range(count) for v in (own, other)], axis=0)

    rows, rows_dy = joined(hn_own, hn_other), joined(dy_own, dy_other)
    meta = joined(meta_own, meta_other)
    products = dot_nt(rows, first)
    gate, up = products[:, :LANES], products[:, LANES:]
    sig = jax.nn.sigmoid(gate)
    total = jnp.sum(jnp.where(is_router, sig * meta, 0.0), axis=1, keepdims=True)
    mine = jnp.sum(jnp.where(lane == shared_cols + me, sig, 0.0), axis=1, keepdims=True)
    token_gate = two_lanes(ROUTE_SCALE * mine / total, lane)
    sact = (gate * sig * up).astype(bf16)
    d_sact = dot_nt(rows_dy, sdown_w[...])
    d_sgate = d_sact * up * sig * (1.0 + gate * (1.0 - sig))
    dsh = jnp.concatenate([d_sgate, d_sact * gate * sig], axis=1).astype(bf16)
    pick = (meta[:, :1] == lane.astype(f32)).astype(bf16)
    groups = [slice(i * tokens, (i + 1) * tokens) for i in range(count)]
    for i in range(count):
        start = i * tokens
        sact_own_out[i] = sact[start : start + half]
        sact_other_out[i] = sact[start + half : start + tokens]
    slots = [dot_tn(pick[g], rows[g]).astype(bf16) for g in groups]
    slot_dys = [dot_tn(pick[g], rows_dy[g]).astype(bf16) for g in groups]
    slot_gates = [
        jnp.sum(dot_tn(pick[g], token_gate[g]), axis=1, keepdims=True) for g in groups
    ]

    @pl.when(pl.program_id(0) == 0)
    def _():
        shared_grads_out[...] = jnp.zeros_like(shared_grads_out)

    first_grad, sdown_grad = dot_tn(dsh, rows), dot_tn(sact, rows_dy)
    shared_grads_out[:shared_cols] += first_grad[:shared_cols]
    shared_grads_out[shared_cols : 2 * shared_cols] += first_grad[LANES : LANES + shared_cols]
    shared_grads_out[2 * shared_cols :] += sdown_grad[:shared_cols]
    slot_rows = jnp.concatenate(slots, axis=0)
    slot_dy = jnp.concatenate(slot_dys, axis=0)
    slot_gate = jnp.concatenate(slot_gates, axis=0)
    slots_out[...] = slot_rows
    slot_dy_out[...] = slot_dy
    gate = dot_nt(slot_rows, gate_up_w[0])
    up = dot_nt(slot_rows, gate_up_w[1])
    d_act = dot_nt(slot_dy, down_w[...])
    sig = jax.nn.sigmoid(gate)
    silu = gate * sig
    act = silu * up
    slot_dgate = jnp.sum(act * d_act, axis=1, keepdims=True)
    act_out[...] = (slot_gate * act).astype(bf16)
    d_act = slot_gate * d_act
    d_gate = (d_act * up * sig * (1.0 + gate * (1.0 - sig))).astype(bf16)
    d_up = (d_act * silu).astype(bf16)
    d_gate_up_out[0] = d_gate
    d_gate_up_out[1] = d_up
    d_slots = (dot_nn(d_gate, gate_up_w[0]) + dot_nn(d_up, gate_up_w[1])).astype(bf16)
    slot_lane = lax.broadcasted_iota(jnp.int32, (LANES, LANES), 1)
    d_shared = dot_nn(dsh, first)
    for i, g in enumerate(groups):
        here = slice(i * LANES, (i + 1) * LANES)
        d_rows = (dot_nn(pick[g], d_slots[here]) + d_shared[g]).astype(bf16)
        rows_own_out[i], rows_other_out[i] = d_rows[:half], d_rows[half:]
        dgate = dot_nn(pick[g], two_lanes(slot_dgate[here], slot_lane))
        dgate_own_out[i], dgate_other_out[i] = dgate[:half], dgate[half:]


def block_specs(per_step):
    def lead(*tail):
        return pl.BlockSpec((per_step, *tail), lambda i: (i,) + (0,) * len(tail))

    def flat(cols):
        return pl.BlockSpec((per_step * LANES, cols), lambda i: (i, 0))

    def whole(a):
        return pl.BlockSpec(a.shape, lambda i: (0,) * a.ndim, pipeline_mode=pl.Buffered(1))

    return lead, flat, whole


def experts(
    me,
    hn_own,
    hn_other,
    dy_own,
    dy_other,
    meta_own,
    meta_other,
    gate_up_w,
    down_w,
    first_w,
    sdown_w,
    shared_cols,
    expert_count,
    per_step=2,
):
    groups, half, width = hn_own.shape
    hidden = down_w.shape[0]
    slots = groups * LANES
    f32, bf16 = jnp.float32, jnp.bfloat16
    lead, flat, whole = block_specs(per_step)
    sds = jax.ShapeDtypeStruct
    return pl.pallas_call(
        functools.partial(expert_kernel, shared_cols, expert_count),
        grid=(groups // per_step,),
        in_specs=[
            pl.BlockSpec(memory_space=pltpu.SMEM),
            *[lead(half, width)] * 4,
            *[lead(half, LANES)] * 2,
            *[whole(a) for a in (gate_up_w, down_w, first_w, sdown_w)],
        ],
        out_specs=[
            flat(width),
            flat(width),
            flat(hidden),
            pl.BlockSpec((2, per_step * LANES, hidden), lambda i: (0, i, 0)),
            *[lead(half, width)] * 2,
            *[lead(half, LANES)] * 2,
            pl.BlockSpec((3 * shared_cols, width), lambda i: (0, 0)),
            *[lead(half, LANES)] * 2,
        ],
        out_shape=[
            sds((slots, width), bf16),
            sds((slots, width), bf16),
            sds((slots, hidden), bf16),
            sds((2, slots, hidden), bf16),
            *[sds((groups, half, width), bf16)] * 2,
            *[sds((groups, half, LANES), bf16)] * 2,
            sds((3 * shared_cols, width), f32),
            *[sds((groups, half, LANES), f32)] * 2,
        ],
        compiler_params=pltpu.CompilerParams(vmem_limit_bytes=58 * 1024 * 1024),
        cost_estimate=pl.CostEstimate(
            flops=groups * width, bytes_accessed=groups * width, transcendentals=0
        ),
    )(
        me,
        hn_own,
        hn_other,
        dy_own,
        dy_other,
        meta_own,
        meta_other,
        gate_up_w,
        down_w,
        first_w,
        sdown_w,
    )


def swap_halves(value, lane):
    low = lane % DR < DR // 2
    return jnp.where(low, pltpu.roll(value, LANES - DR // 2, 1), pltpu.roll(value, DR // 2, 1))


def by_core(core, first, second):
    return jnp.where(core == 0, first, second), jnp.where(core == 0, second, first)


def head_scores(q, kv, k_rope, visible, lane, head, heads):
    q_nope = q[:, head * DN : (head + 1) * DN]
    q_rope = jnp.where(lane // DR == head, q[:, heads * DN :], jnp.zeros((), q.dtype))
    at = head * (DN + DV)
    k_nope, value = kv[:, at : at + DN], kv[:, at + DN : at + DN + DV]
    scores = (dot_nt(q_nope, k_nope) + dot_nt(q_rope, k_rope)) * (DN + DR) ** -0.5
    return jnp.where(visible, scores, NEGATIVE), q_nope, q_rope, k_nope, value


def seen(doc_col, doc_row):
    rows = doc_col.shape[0]
    later = lax.broadcasted_iota(jnp.int32, (rows, rows), 0) >= lax.broadcasted_iota(
        jnp.int32, (rows, rows), 1
    )
    return (doc_col == doc_row) & later


def attention_kernel(
    heads,
    rank,
    core_ref,
    x_own,
    x_other,
    gain,
    latent_gain,
    head_w,
    small_w,
    kv_w,
    cosine,
    sine,
    doc_col,
    doc_row,
    normed_out,
    compressed_out,
    q_out,
    kv_out,
    k_rope_out,
    sums_out,
    attended_out,
    latent_out,
    part_own_out,
    part_other_out,
):
    f32, bf16 = jnp.float32, jnp.bfloat16
    core = core_ref[0]
    x = jnp.concatenate(by_core(core, x_own[0], x_other[0]), axis=0).astype(f32)
    rows = x.shape[0]
    half = rows // 2
    lane = lax.broadcasted_iota(jnp.int32, (rows, LANES), 1)
    inverse = lax.rsqrt(jnp.mean(x * x, axis=1, keepdims=True) + EPSILON)
    normed = (x * inverse * gain[...]).astype(bf16)
    normed_out[0] = normed
    q_cols = heads * (DN + DR)
    queries = dot_nn(normed, head_w[:, :q_cols])
    q_rope = queries[:, heads * DN :]
    q_rope = q_rope * cosine[0] + swap_halves(q_rope, lane) * sine[0]
    q = jnp.concatenate([queries[:, : heads * DN], q_rope], axis=1).astype(bf16)
    q_out[0] = q
    latent = dot_nn(normed, small_w[:, : rank + LANES])
    latent_out[0] = latent
    squeezed = latent[:, :rank]
    inverse = lax.rsqrt(jnp.mean(squeezed * squeezed, axis=1, keepdims=True) + EPSILON)
    compressed = (squeezed * inverse * latent_gain[...]).astype(bf16)
    compressed_out[0] = compressed
    k_rope = latent[:, rank:]
    k_rope = (k_rope * cosine[0] + swap_halves(k_rope, lane) * sine[0]).astype(bf16)
    k_rope_out[0] = k_rope
    kv = dot_nn(compressed, kv_w[...]).astype(bf16)
    kv_out[0] = kv
    visible = seen(doc_col[0], doc_row[0])
    attended, sums = [], jnp.zeros((rows, LANES), f32)
    for head in range(heads):
        scores, *_, value = head_scores(q, kv, k_rope, visible, lane, head, heads)
        top = jnp.max(scores, axis=1, keepdims=True)
        log_total = top + jnp.log(jnp.sum(jnp.exp(scores - top), axis=1, keepdims=True))
        sums = jnp.where(lane == head, log_total, sums)
        probs = jnp.exp(scores - log_total).astype(bf16)
        attended.append(dot_nn(probs, value).astype(bf16))
    sums_out[0] = sums
    attended = jnp.concatenate(attended, axis=1)
    attended_out[0] = attended
    part = dot_nt(attended, head_w[:, q_cols : q_cols + heads * DV]).astype(bf16)
    part_own_out[0], part_other_out[0] = by_core(core, part[:half], part[half:])


def attention_backward_kernel(
    heads,
    core_ref,
    d_own,
    d_other,
    normed_ref,
    compressed_ref,
    q_ref,
    kv_ref,
    k_rope_ref,
    sums_ref,
    attended_ref,
    head_w,
    kv_w,
    cosine,
    sine,
    doc_col,
    doc_row,
    head_grad_out,
    kv_grad_out,
    normed_own_out,
    normed_other_out,
    latent_own_out,
    latent_other_out,
    head_acc,
    kv_acc,
):
    f32, bf16 = jnp.float32, jnp.bfloat16
    core, step = core_ref[0], pl.program_id(0)
    scale = (DN + DR) ** -0.5
    d_rows = jnp.concatenate(by_core(core, d_own[0], d_other[0]), axis=0)
    rows = d_rows.shape[0]
    half = rows // 2
    lane = lax.broadcasted_iota(jnp.int32, (rows, LANES), 1)
    q_cols = heads * (DN + DR)
    q, kv, k_rope = q_ref[0], kv_ref[0], k_rope_ref[0]
    d_attended = dot_nn(d_rows, head_w[:, q_cols : q_cols + heads * DV]).astype(bf16)
    visible = seen(doc_col[0], doc_row[0])
    d_q, d_kv = [], []
    d_q_rope, d_k_rope = jnp.zeros((rows, LANES), f32), jnp.zeros((rows, LANES), f32)
    for head in range(heads):
        scores, q_nope, q_rope, k_nope, value = head_scores(
            q, kv, k_rope, visible, lane, head, heads
        )
        probs = jnp.exp(scores - sums_ref[0][:, head : head + 1])
        d_head = d_attended[:, head * DV : (head + 1) * DV]
        d_probs = dot_nt(d_head, value)
        d_value = dot_tn(probs.astype(bf16), d_head)
        delta = jnp.sum(probs * d_probs, axis=1, keepdims=True)
        d_scores = (probs * (d_probs - delta)).astype(bf16)
        d_q.append(dot_nn(d_scores, k_nope) * scale)
        d_q_rope = jnp.where(lane // DR == head, dot_nn(d_scores, k_rope) * scale, d_q_rope)
        d_kv += [dot_tn(d_scores, q_nope) * scale, d_value]
        d_k_rope += dot_tn(d_scores, q_rope) * scale
    d_q_rope = d_q_rope * cosine[0] - swap_halves(d_q_rope, lane) * sine[0]
    d_q = jnp.concatenate(d_q + [d_q_rope], axis=1).astype(bf16)
    d_kv = jnp.concatenate(d_kv, axis=1).astype(bf16)

    @pl.when(step == 0)
    def _():
        head_acc[...] = jnp.zeros_like(head_acc)
        kv_acc[...] = jnp.zeros_like(kv_acc)

    head_acc[:, :q_cols] += dot_tn(normed_ref[0], d_q)
    head_acc[:, q_cols:] += dot_tn(d_rows, attended_ref[0])
    kv_acc[...] += dot_tn(compressed_ref[0], d_kv)

    @pl.when(step == pl.num_programs(0) - 1)
    def _():
        head_grad_out[...] = head_acc[...].astype(bf16)
        kv_grad_out[...] = kv_acc[...].astype(bf16)

    part = dot_nt(d_q, head_w[:, :q_cols]).astype(bf16)
    normed_own_out[0], normed_other_out[0] = by_core(core, part[:half], part[half:])
    latent = jnp.concatenate([dot_nt(d_kv, kv_w[...]), d_k_rope], axis=1).astype(bf16)
    latent_own_out[0], latent_other_out[0] = by_core(core, latent[:half], latent[half:])


def one_each(*tail):
    return pl.BlockSpec((1, *tail), lambda i: (i,) + (0,) * len(tail))


def kept(value):
    return pl.BlockSpec(value.shape, lambda i: (0,) * value.ndim, pipeline_mode=pl.Buffered(1))


def attention(core, x_own, x_other, gain, latent_gain, head_w, small_w, kv_w, cosine, sine, doc):
    near, half, width = x_own.shape
    rows = 2 * half
    rank, kv_cols = kv_w.shape
    heads = kv_cols // (DN + DV)
    f32, bf16 = jnp.float32, jnp.bfloat16
    shapes = [
        ((rows, width), bf16),
        ((rows, rank), bf16),
        ((rows, heads * (DN + DR)), bf16),
        ((rows, kv_cols), bf16),
        ((rows, LANES), bf16),
        ((rows, LANES), f32),
        ((rows, heads * DV), bf16),
        ((rows, rank + LANES), f32),
        ((half, width), bf16),
        ((half, width), bf16),
    ]
    return pl.pallas_call(
        functools.partial(attention_kernel, heads, rank),
        grid=(near,),
        in_specs=[
            pl.BlockSpec(memory_space=pltpu.SMEM),
            *[one_each(half, width)] * 2,
            *[kept(a) for a in (gain, latent_gain, head_w, small_w, kv_w)],
            *[one_each(rows, LANES)] * 2,
            one_each(rows, 1),
            one_each(1, rows),
        ],
        out_specs=[one_each(*shape) for shape, _ in shapes],
        out_shape=[jax.ShapeDtypeStruct((near, *shape), kind) for shape, kind in shapes],
        compiler_params=pltpu.CompilerParams(vmem_limit_bytes=58 * 1024 * 1024),
        cost_estimate=pl.CostEstimate(
            flops=2 * near * rows * width * (rank + 3 * heads * DN),
            bytes_accessed=4 * near * rows * width,
            transcendentals=0,
        ),
    )(
        core,
        x_own,
        x_other,
        gain,
        latent_gain,
        head_w,
        small_w,
        kv_w,
        cosine,
        sine,
        doc[:, :, None],
        doc[:, None, :],
    )


def attention_backward(core, d_own, d_other, kept_rows, head_w, kv_w, cosine, sine, doc):
    near, half, width = d_own.shape
    rows = 2 * half
    rank, kv_cols = kv_w.shape
    heads = kv_cols // (DN + DV)
    head_cols = heads * (DN + DR + DV)
    f32, bf16 = jnp.float32, jnp.bfloat16
    sds = jax.ShapeDtypeStruct
    return pl.pallas_call(
        functools.partial(attention_backward_kernel, heads),
        grid=(near,),
        in_specs=[
            pl.BlockSpec(memory_space=pltpu.SMEM),
            *[one_each(half, width)] * 2,
            *[one_each(*v.shape[1:]) for v in kept_rows],
            *[kept(a) for a in (head_w, kv_w)],
            *[one_each(rows, LANES)] * 2,
            one_each(rows, 1),
            one_each(1, rows),
        ],
        out_specs=[
            pl.BlockSpec((width, head_cols), lambda i: (0, 0)),
            pl.BlockSpec((rank, kv_cols), lambda i: (0, 0)),
            *[one_each(half, width)] * 2,
            *[one_each(half, rank + LANES)] * 2,
        ],
        out_shape=[
            sds((width, head_cols), bf16),
            sds((rank, kv_cols), bf16),
            *[sds((near, half, width), bf16)] * 2,
            *[sds((near, half, rank + LANES), bf16)] * 2,
        ],
        scratch_shapes=[
            pltpu.VMEM((width, head_cols), f32),
            pltpu.VMEM((rank, kv_cols), f32),
        ],
        compiler_params=pltpu.CompilerParams(vmem_limit_bytes=58 * 1024 * 1024),
        cost_estimate=pl.CostEstimate(
            flops=near * rows * width * heads * DN,
            bytes_accessed=2 * near * rows * width,
            transcendentals=0,
        ),
    )(
        core,
        d_own,
        d_other,
        *kept_rows,
        head_w,
        kv_w,
        cosine,
        sine,
        doc[:, :, None],
        doc[:, None, :],
    )


def product_kernel(*refs):
    *operands, out_ref = refs
    count = len(operands) // 2
    total = 0.0
    for left_ref, right_ref in zip(operands[:count], operands[count:]):
        total += dot_tn(left_ref[0], right_ref[...])
    out_ref[0] = total


def column_products(lefts, rights, tile=512):
    count, _, height = lefts[0].shape
    width = rights[0].shape[1]
    return pl.pallas_call(
        product_kernel,
        grid=(width // tile, count),
        in_specs=[
            *[pl.BlockSpec((1, v.shape[1], height), lambda j, i: (i, 0, 0)) for v in lefts],
            *[pl.BlockSpec((v.shape[0], tile), lambda j, i: (0, j)) for v in rights],
        ],
        out_specs=pl.BlockSpec((1, height, tile), lambda j, i: (i, 0, j)),
        out_shape=jax.ShapeDtypeStruct((count, height, width), jnp.float32),
        compiler_params=pltpu.CompilerParams(vmem_limit_bytes=58 * 1024 * 1024),
        cost_estimate=pl.CostEstimate(flops=width, bytes_accessed=width, transcendentals=0),
    )(*lefts, *rights)


def output_kernel(act, sact_own, sact_other, meta_own, meta_other, down_w, sdown_w, own_out, other_out):
    f32, bf16 = jnp.float32, jnp.bfloat16
    count, half, _ = meta_own.shape
    lane = lax.broadcasted_iota(jnp.int32, (2 * half, LANES), 1).astype(f32)
    out = dot_nn(act[...], down_w[...]).astype(bf16)
    for i in range(count):
        meta = jnp.concatenate([meta_own[i], meta_other[i]], axis=0)
        pick = (meta[:, :1] == lane).astype(bf16)
        sact = jnp.concatenate([sact_own[i], sact_other[i]], axis=0)
        here = slice(i * LANES, (i + 1) * LANES)
        rows = (dot_nn(pick, out[here]) + dot_nn(sact, sdown_w[...])).astype(bf16)
        own_out[i], other_out[i] = rows[:half], rows[half:]


def outputs(act, sact_own, sact_other, meta_own, meta_other, down_w, sdown_w, per_step=4):
    groups, half, _ = meta_own.shape
    hidden, width = down_w.shape
    lead, flat, whole = block_specs(per_step)
    return pl.pallas_call(
        output_kernel,
        grid=(groups // per_step,),
        in_specs=[
            flat(hidden),
            *[lead(half, LANES)] * 4,
            *[whole(a) for a in (down_w, sdown_w)],
        ],
        out_specs=[lead(half, width)] * 2,
        out_shape=[jax.ShapeDtypeStruct((groups, half, width), jnp.bfloat16)] * 2,
        compiler_params=pltpu.CompilerParams(vmem_limit_bytes=58 * 1024 * 1024),
        cost_estimate=pl.CostEstimate(
            flops=groups * half * LANES * width,
            bytes_accessed=groups * half * width,
            transcendentals=0,
        ),
    )(act, sact_own, sact_other, meta_own, meta_other, down_w, sdown_w)


def token_plan(
    inputs,
    attn_gain,
    w_query,
    w_latent,
    latent_gain,
    w_kv,
    w_out,
    ffn_gain,
    w_router,
    shared_gate_up,
    shared_down,
    expert_gate_up,
    expert_down,
    lengths,
    routes,
    cotangent,
):
    f32, bf16 = jnp.float32, jnp.bfloat16
    core, me = lax.axis_index("tensor"), lax.axis_index("expert")
    groups = lax.axis_size("expert")
    deep, place, z = groups // PLANE, me % PLANE, me // PLANE
    tok_rows, width = inputs.shape
    half = tok_rows // 2
    own_at, other_at = core * half, (1 - core) * half
    expert_count = w_router.shape[1]
    route_count = routes.shape[1]
    capacity = tok_rows * route_count * 4 // (3 * expert_count)
    shared_cols = shared_gate_up.shape[2] // groups
    latent_cols, rank_width = w_latent.shape[1], latent_gain.shape[0] * groups
    block_rows = w_query.shape[0]
    kv_rows = w_kv.shape[0]

    query_cols = w_query.shape[1] // PLANE
    out_cols = w_out.shape[0] // PLANE
    small = jnp.concatenate(
        [
            w_latent,
            w_latent[:, rank_width:],
            w_router,
            attn_gain[:, None],
            ffn_gain[:, None],
            jnp.pad(latent_gain, (0, block_rows - kv_rows))[:, None],
        ],
        axis=1,
    )
    small_cols = small.shape[1]
    route_half = take_rows(routes, own_at, half).astype(bf16).reshape(block_rows // 2, -1)
    length_col = jnp.pad(lengths[0].astype(bf16), (0, block_rows // 2 - lengths.shape[1]))[:, None]
    route_cols = route_half.shape[1] + 1
    small_half = jnp.concatenate(
        [
            take_rows(small, core * (block_rows // 2), block_rows // 2),
            route_half,
            length_col,
            jnp.zeros((block_rows // 2, -(small_cols + route_cols) % (2 * LANES)), bf16),
        ],
        axis=1,
    )
    packed_cols = small_half.shape[1] // 2
    small_packed = jnp.concatenate([small_half[:, :packed_cols], small_half[:, packed_cols:]])
    kv_cols = w_kv.shape[1] // PLANE
    kv_parts = block_rows // kv_rows
    kv_piece = kv_cols // kv_parts
    w_out_t = w_out.T

    local_heads = query_cols // (DN + DR)

    def by_parts(block):
        heads = [block[:, h * (DN + DR) : (h + 1) * (DN + DR)] for h in range(local_heads)]
        return [h[:, :DN] for h in heads] + [h[:, DN:] for h in heads]

    def quarter(index):
        kv_here = take_rows(w_kv, index * kv_cols, kv_cols, axis=1)
        kv_here = [kv_here[:, p * kv_piece : (p + 1) * kv_piece] for p in range(kv_parts)]
        return jnp.concatenate(
            [
                *by_parts(take_rows(w_query, index * query_cols, query_cols, axis=1)),
                take_rows(w_out_t, index * out_cols, out_cols, axis=1),
                jnp.concatenate(kv_here, axis=0),
            ],
            axis=1,
        )

    near_w = [quarter(place)] + [to_partner(quarter(place ^ r), r) for r in range(1, PLANE)]
    small_line = deep_join(small_packed, deep_pieces(small_packed), z)
    near_w, small_line = tie(near_w, small_line)
    plane_w = jnp.stack(by_place(near_w, place))
    small_sent, x_sent, plane_w = tie(
        small_line.swapaxes(0, 1), take_rows(inputs, own_at, half), plane_w
    )
    small_sent = jnp.stack([small_sent, to_partner(small_sent, 1)])
    small_sent = jnp.concatenate([small_sent, to_partner(small_sent, 2)], axis=0)
    x_sent = jnp.stack([x_sent, to_partner(x_sent, 2)])
    x_came = to_partner(x_sent, 1)
    x_near_own = jnp.stack([x_sent[0], x_came[0], x_sent[1], x_came[1]])
    x_near_other = swap_cores(x_near_own)
    deep_w = deep_hops(plane_w)
    small_parts = [small_sent[r].swapaxes(0, 1) for r in range(PLANE)]
    small_own = jnp.stack(by_place(small_parts, place), axis=1)
    small_own = small_own.reshape(groups, block_rows, packed_cols)
    small_own = jnp.concatenate(
        [small_own[:, : block_rows // 2], small_own[:, block_rows // 2 :]], axis=2
    )
    small_other = swap_cores(small_own)
    small_all = in_order(core, small_own, small_other, axis=1)
    small_all, x_near_other, deep_w = tie(small_all, x_near_other, deep_w)
    head_w = deep_join(plane_w, join_hops(deep_w), z)
    length_at = small_cols + route_cols - 1
    lengths_near = take_rows(small_own, z * PLANE, PLANE)[:, : lengths.shape[1], length_at]
    lengths_near = lengths_near.astype(jnp.int32)
    lengths_near = jnp.stack(by_place([lengths_near[r] for r in range(PLANE)], place))
    shared_rows = jnp.concatenate(
        [shared_gate_up[0].T, shared_gate_up[1].T, shared_down], axis=0
    ).reshape(3, groups, shared_cols, block_rows)
    shared_rows = shared_rows.swapaxes(0, 1).reshape(groups, 3 * shared_cols, block_rows)
    dy_sent, head_w = tie(take_rows(cotangent, own_at, half), head_w)
    dy_own_rows = take_rows(cotangent, own_at, half)
    dy_gather = RowGather(dy_sent)
    dy_came = dy_gather.along()
    head_w = head_w.reshape(groups, block_rows, -1)
    flat_head = head_w.reshape(groups * block_rows, -1)
    at = query_cols + out_cols
    kv_w = head_w[:, :, at : at + kv_piece].reshape(groups, kv_parts, kv_rows, kv_piece)
    kv_w = kv_w.transpose(0, 2, 1, 3).reshape(groups * kv_rows, kv_cols)

    block_index = jnp.arange(groups)
    block_chip = (z - block_index % deep) % deep * PLANE + (place ^ (block_index // deep))
    in_blocks = (block_chip[:, None] == block_index[None, :]).astype(bf16)

    def routes_of(came):
        came = came[:, :, small_cols : small_cols + route_half.shape[1]].reshape(groups, -1)
        came = jnp.dot(in_blocks, came, preferred_element_type=f32)
        return came.astype(jnp.int32).reshape(groups, half, route_count)

    routes_own, routes_other = routes_of(small_own), routes_of(small_other)
    flat_small = small_all.reshape(groups * block_rows, -1)
    latent_w = flat_small[:, :latent_cols]
    at = rank_width + LANES
    router_w = flat_small[:, at : at + expert_count]
    at += expert_count
    gain_one, gain_two = flat_small[:, at], flat_small[:, at + 1]
    latent_g = small_all[:, :kv_rows, at + 2].reshape(-1)

    near_rows = PLANE * tok_rows
    relative, doc = jax.vmap(lambda one: doc_places(one, tok_rows))(lengths_near)
    cosine, sine_tab = rope_tables(relative.reshape(-1), DR)
    cosine, sine_tab = [v.reshape(PLANE, tok_rows, -1) for v in (cosine, sine_tab)]
    rope = (
        jnp.concatenate([cosine] * 4, axis=-1),
        jnp.concatenate([-sine_tab, sine_tab] * 2, axis=-1),
        doc.astype(f32),
    )
    core_index = core.reshape(1).astype(jnp.int32)
    *kept_rows, latent, part_own, part_other = attention(
        core_index,
        x_near_own,
        x_near_other,
        gain_one.astype(f32)[None],
        latent_g.astype(f32)[None],
        flat_head,
        flat_small,
        kv_w,
        *rope,
    )
    normed_b = kept_rows[0].reshape(near_rows, width)

    def sum_cores(own, other):
        return add_wide(own, swap_cores(other)).astype(bf16)

    def sum_plane(both):
        return plane_scatter([both[r] for r in range(PLANE)])

    part_own, part_other, dy_came = tie(part_own, part_other, dy_came)
    attn_own = sum_plane(sum_cores(part_own, part_other))
    x_own = take_rows(inputs, own_at, half).astype(f32)
    hidden = x_own + attn_own
    hnormed, scale_two = rms_forward(hidden, gain_two.astype(f32))
    hnormed_b = hnormed.astype(bf16)
    normed_cols = jnp.concatenate(
        [
            take_rows(normed_b, (k * PLANE + place) * block_rows, block_rows, axis=1)
            for k in range(deep)
        ],
        axis=1,
    )
    hnormed_b, normed_cols, shared_rows, routes_own, routes_other = tie(
        hnormed_b, normed_cols, shared_rows, routes_own, routes_other
    )
    dy_line = jnp.stack(dy_came)
    def membership(named):
        one_hot = named[..., None] == jnp.arange(expert_count, dtype=jnp.int32)
        return jnp.any(named == me, axis=-1), jnp.any(one_hot, axis=2)

    member_own, hot_own = membership(routes_own)
    member_other, hot_other = membership(routes_other)
    lower = (
        jnp.arange(half, dtype=jnp.int32)[:, None] <= jnp.arange(half, dtype=jnp.int32)[None, :]
    ).astype(bf16)

    def running(mask):
        counts = jnp.dot(mask.astype(bf16), lower, preferred_element_type=f32)
        return counts.astype(jnp.int32)

    count_own, count_other = running(member_own), running(member_other)
    place_own = jnp.where(member_own, count_own - 1, -1)
    place_other = jnp.where(member_other, count_own[:, -1:] + count_other - 1, -1)

    def metadata(slot, hot):
        return jnp.concatenate(
            [
                slot[..., None].astype(f32),
                jnp.zeros((groups, half, shared_cols - 1), f32),
                hot.astype(f32),
                jnp.zeros((groups, half, LANES - shared_cols - expert_count), f32),
            ],
            axis=-1,
        )

    meta_own, meta_other = metadata(place_own, hot_own), metadata(place_other, hot_other)
    hn_gather = RowGather(hnormed_b)
    shared_w = lax.all_to_all(shared_rows, "expert", split_axis=0, concat_axis=0, tiled=True)
    hn_came, dy_beside, dy_line_other, shared_w, meta_own, meta_other = tie(
        hn_gather.along(),
        dy_gather.beside(dy_line),
        swap_cores(dy_line),
        shared_w,
        meta_own,
        meta_other,
    )
    shared_w = shared_w.swapaxes(0, 1).reshape(3 * shared_cols, groups * block_rows)
    first_w = jnp.concatenate(
        [
            shared_w[:shared_cols],
            router_w.T,
            jnp.zeros((LANES - shared_cols - expert_count, width), bf16),
            shared_w[shared_cols : 2 * shared_cols],
            jnp.zeros((LANES - shared_cols, width), bf16),
        ],
        axis=0,
    )
    sdown_rows = jnp.pad(shared_w[2 * shared_cols :], ((0, LANES - shared_cols), (0, 0)))
    gate_up_w, down_w = jnp.swapaxes(expert_gate_up[0], 1, 2), expert_down[0]

    def run_experts(which, hn_part, hn_part_other):
        at, to = which[0] * deep, (which[-1] + 1) * deep
        return experts(
            me.reshape(1).astype(jnp.int32),
            hn_part,
            hn_part_other,
            *dy_parts[which],
            meta_own[at:to],
            meta_other[at:to],
            gate_up_w,
            down_w,
            first_w,
            sdown_rows,
            shared_cols,
            expert_count,
        )

    parts = ((0,), (1, 2), (3,))
    dy_parts = {parts[0]: (dy_line, dy_line_other)}
    hn_line, dy_beside = tie(jnp.stack(hn_came), dy_beside)
    dy_near = jnp.concatenate(dy_beside, axis=0)
    hn_beside, dy_beside, done_line, *dy_parts[parts[1]] = tie(
        hn_gather.beside(hn_line),
        dy_beside,
        run_experts(parts[0], hn_line, swap_cores(hn_line)),
        dy_near,
        swap_cores(dy_near),
    )
    d_line_came = swap_cores(done_line[5])
    hn_near = jnp.concatenate(hn_beside, axis=0)
    hn_far, dy_far, done_near = tie(
        hn_gather.far(hn_beside),
        dy_gather.far(dy_beside),
        run_experts(parts[1], hn_near, swap_cores(hn_near)),
    )
    dy_far = jnp.concatenate(dy_far, axis=1)
    dy_parts[parts[2]] = dy_far, swap_cores(dy_far)
    d_near_came = swap_cores(done_near[5])
    hn_far = jnp.concatenate(hn_far, axis=1)
    done_far = run_experts(parts[2], hn_far, swap_cores(hn_far))
    done = (done_line, done_near, done_far)
    slot_rows, slot_dy, slot_act, d_gate_up = [[v[i] for v in done] for i in range(4)]
    shared_grads = add_wide(*[v[8] for v in done])

    def by_flips(line, near, far):
        return [line, near[:deep], near[deep:], far]

    d_rows_own = by_flips(*[v[4] for v in done])
    d_rows_came = by_flips(d_line_came, d_near_came, swap_cores(done_far[5]))

    def two_parts(value):
        return value[..., 0] + value[..., 1]

    dgate_own, dgate_other = [
        jnp.concatenate([two_parts(v[i]) for v in done], axis=0) for i in (9, 10)
    ]
    dgate_sent = dgate_own + swap_cores(dgate_other)
    dgate_high = dgate_sent.astype(bf16)
    dgate_low = (dgate_sent - dgate_high.astype(f32)).astype(bf16)
    d_rows_came, dgate_high, dgate_low = tie(d_rows_came, dgate_high, dgate_low)
    d_sum = RowSum(d_rows_own, d_rows_came)
    sends, shared_grads, slot_act = tie(d_sum.sends(), shared_grads, slot_act)
    came = d_sum.move(sends)
    gate_rows = jnp.stack([contract_rows(in_blocks, v).reshape(-1) for v in (dgate_high, dgate_low)])
    grads_sent = jnp.concatenate([shared_grads, gate_rows], axis=0).astype(bf16)
    grads_sent = grads_sent.reshape(-1, groups, block_rows)
    grads_came = lax.all_to_all(grads_sent, "expert", split_axis=1, concat_axis=1, tiled=True)
    out_done = [
        outputs(
            act,
            v[6],
            v[7],
            meta_own[p[0] * deep : (p[-1] + 1) * deep],
            meta_other[p[0] * deep : (p[-1] + 1) * deep],
            down_w,
            sdown_rows,
        )
        for act, v, p in zip(slot_act, done, parts)
    ]
    edown_grad = column_products([v[None] for v in slot_act], slot_dy)[0]
    came, out_done, edown_grad, grads_came = tie(came, out_done, edown_grad, grads_came)
    dgate = add_wide(grads_came[3 * shared_cols], grads_came[3 * shared_cols + 1]).T
    sends, slot_rows, out_done = tie(d_sum.sends_again(came), slot_rows, out_done)
    came_again = d_sum.move_again(sends)
    egu_grad = column_products(d_gate_up, slot_rows).swapaxes(1, 2)
    out_own = by_flips(*[v[0] for v in out_done])
    out_came = by_flips(*[swap_cores(v[1]) for v in out_done])
    out_sum = RowSum(out_own, out_came)
    out_sends = out_sum.sends()
    came_again, egu_grad, out_sends = tie(came_again, egu_grad, out_sends)
    z_sends, out_sends, dgate = tie(
        line_sends(d_sum.line(came, came_again)), out_sends, dgate
    )
    z_came = line_move(z_sends)
    out_first = out_sum.move(out_sends)
    hot_mine = take_rows(
        jnp.any(routes[..., None] == jnp.arange(expert_count, dtype=jnp.int32), axis=1), own_at, half
    )
    sig = jax.nn.sigmoid(jnp.dot(hnormed_b, router_w, preferred_element_type=f32))
    chosen = jnp.where(hot_mine, sig, 0.0)
    chosen_sum = jnp.sum(chosen, axis=1, keepdims=True)
    dgate = jnp.where(hot_mine, dgate, 0.0)
    inner = jnp.sum(dgate * chosen, axis=1, keepdims=True)
    d_chosen = ROUTE_SCALE * (dgate / chosen_sum - inner / (chosen_sum * chosen_sum))
    d_logits = (jnp.where(hot_mine, d_chosen, 0.0) * sig * (1.0 - sig)).astype(bf16)
    router_grad = contract_rows(d_logits, hnormed_b)
    z_came, d_logits, router_grad = tie(z_came, d_logits, router_grad)
    d_hn = add_wide(*z_came)
    d_hn = d_hn + contract_cols(d_logits, router_w)
    d_hidden_norm, gain_two_grad = rms_backward(hidden, scale_two, gain_two.astype(f32), d_hn)
    d_hidden = dy_own_rows.astype(f32) + d_hidden_norm
    d_parts, out_first = tie(plane_gather(d_hidden.astype(bf16)), out_first)
    d_near_own = jnp.stack(d_parts)
    d_near_other = swap_cores(d_near_own)
    out_sends, d_near_other = tie(out_sum.sends_again(out_first), d_near_other)
    out_second = out_sum.move_again(out_sends)

    (
        head_grad,
        kv_grad,
        normed_part_own,
        normed_part_other,
        latent_part_own,
        latent_part_other,
    ) = attention_backward(
        core_index, d_near_own, d_near_other, kept_rows, flat_head, kv_w, *rope
    )
    kv_grad = kv_grad.reshape(groups, kv_rows, kv_parts, kv_piece).transpose(0, 2, 1, 3)
    head_grad = jnp.concatenate([head_grad, kv_grad.reshape(-1, kv_piece)], axis=1)
    head_blocks = head_grad.reshape(deep, -1, head_grad.shape[1])
    head_hops = HopSum(lambda t: at_index(head_blocks, 0, t))
    came, latent_both, normed_both, out_second = tie(
        head_hops.hop(1),
        sum_cores(latent_part_own, latent_part_other),
        sum_cores(normed_part_own, normed_part_other),
        out_second,
    )
    out_line = out_sum.line(out_first, out_second)
    came, grad_both, out_line = tie(head_hops.hop(2, came), sum_plane(latent_both), out_line)
    grad_rope = grad_both[:, rank_width : rank_width + DR] + grad_both[:, rank_width + DR :]
    latent_own = take_rows(latent[0], own_at, half)
    cosine_own = take_rows(cosine[0], own_at, half)
    sine_own = take_rows(sine_tab[0], own_at, half)
    _, scale_kv = rms_forward(latent_own[:, :rank_width], latent_g.astype(f32))
    grad_c, latent_gain_grad = rms_backward(
        latent_own[:, :rank_width], scale_kv, latent_g.astype(f32), grad_both[:, :rank_width]
    )
    grad_latent = jnp.concatenate(
        [grad_c, unrotate(grad_rope, cosine_own, sine_own)], axis=-1
    ).astype(bf16)
    out_hops = HopSum(lambda t: at_index(out_line, 0, (z - t) % deep))
    came, latent_parts, grad_normed, out_z = tie(
        head_hops.hop(3, came), plane_gather(grad_latent), sum_plane(normed_both), out_hops.hop(1)
    )
    latent_near_own = jnp.stack(latent_parts)
    latent_near = in_order(core, latent_near_own, swap_cores(latent_near_own), axis=1)
    head_sums = head_hops.total(came).astype(bf16).reshape(PLANE, block_rows, -1)
    out_z, latent_near, head_shared, grads_came, grad_normed, grad_latent = tie(
        out_hops.hop(2, out_z),
        latent_near,
        share_columns(head_sums, place),
        grads_came,
        grad_normed,
        grad_latent,
    )
    out_z = out_hops.hop(3, out_z)
    latent_cut = latent_cols // 2
    latent_near = latent_near.reshape(near_rows, latent_cols)
    latent_blocks = contract_rows(
        normed_cols,
        take_rows(latent_near, core * latent_cut, latent_cut, axis=1),
    )
    latent_half = deep_scatter(latent_blocks.astype(bf16).reshape(deep, -1, latent_cut), z)
    w_latent_grad = in_order(core, latent_half, swap_cores(latent_half), axis=1)


    def by_heads(block):
        rotary = local_heads * DN
        return [
            part
            for h in range(local_heads)
            for part in (
                block[:, h * DN : (h + 1) * DN],
                block[:, rotary + h * DR : rotary + (h + 1) * DR],
            )
        ]

    at_kv = query_cols + out_cols
    w_query_grad = jnp.concatenate([v for p in head_shared for v in by_heads(p)], axis=1)
    w_query_grad = w_query_grad.astype(f32)
    w_kv_grad = jnp.concatenate(
        [
            p[q * kv_rows : (q + 1) * kv_rows, at_kv:]
            for p in head_shared
            for q in range(kv_parts)
        ],
        axis=1,
    ).astype(f32)
    w_out_grad = jnp.concatenate([p[:, query_cols:at_kv] for p in head_shared], axis=1)
    w_out_grad = w_out_grad.astype(f32).T
    sgu_out = grads_came[: 2 * shared_cols].astype(f32)
    sgu_out = sgu_out.reshape(2, shared_cols, groups, block_rows)
    sgu_out = sgu_out.transpose(0, 3, 2, 1).reshape(2, block_rows, -1)
    sdown_out = grads_came[2 * shared_cols : 3 * shared_cols].astype(f32).swapaxes(0, 1).reshape(-1, block_rows)
    grad_normed = grad_normed + contract_cols(grad_latent, latent_w)
    moe_own = out_hops.total(out_z)
    mixed_own = (hidden + moe_own).astype(bf16)
    mixed = in_order(core, mixed_own, swap_cores(mixed_own))

    _, scale_own = rms_forward(x_own, gain_one.astype(f32))
    grad_x_norm, gain_one_grad = rms_backward(x_own, scale_own, gain_one.astype(f32), grad_normed)
    input_own = d_hidden + grad_x_norm
    input_grad = in_order(core, input_own, swap_cores(input_own))

    gain_lanes = jnp.pad(
        latent_gain_grad.reshape(groups, kv_rows), ((0, 0), (0, block_rows - kv_rows))
    )
    vectors = jnp.concatenate(
        [
            router_grad,
            gain_one_grad[None],
            gain_two_grad[None],
            gain_lanes.reshape(1, -1),
        ],
        axis=0,
    ).reshape(-1, groups, block_rows)
    arrived = lax.all_to_all(vectors, "expert", split_axis=1, concat_axis=1, tiled=True)
    sums = jnp.sum(arrived, axis=1)
    sums = sums + swap_cores(sums)
    return (
        mixed,
        input_grad,
        sums[expert_count],
        w_query_grad,
        w_latent_grad,
        sums[expert_count + 2, :kv_rows],
        w_kv_grad,
        w_out_grad,
        sums[expert_count + 1],
        sums[:expert_count].T,
        sgu_out,
        sdown_out,
        egu_grad[None],
        edown_grad[None],
    )


def solution(mesh):
    groups = mesh.shape["expert"]
    plan = token_plan if groups <= 16 else weight_plan
    return jax.shard_map(
        plan,
        mesh=mesh,
        in_specs=(
            P("expert", None),
            P("expert"),
            P("expert", "tensor"),
            P("expert", None),
            P("expert"),
            P("expert", "tensor"),
            P("tensor", "expert"),
            P("expert"),
            P("expert", None),
            P(None, "expert", "tensor"),
            P("tensor", "expert"),
            P("expert", None, None, "tensor"),
            P("expert", "tensor", None),
            P("expert", None),
            P("expert", None),
            P("expert", None),
        ),
        out_specs=(
            P("expert", None),
            P("expert", None),
            P("expert"),
            P("expert", "tensor"),
            P("expert", None),
            P("expert"),
            P("expert", "tensor"),
            P("tensor", "expert"),
            P("expert"),
            P("expert", None),
            P(None, "expert", "tensor"),
            P("tensor", "expert"),
            P("expert", None, None, "tensor"),
            P("expert", "tensor", None),
        ),
        check_vma=False,
    )
```
